32 devices in a mesh: grp: 4 (over z), tok: 8 (over y, x, core).
Axes of the slice: x: 2, y: 2, z: 4, core: 2. Of those that a mesh axis runs over, the one named last changes fastest.
Arguments:
- tokens: bfloat16 [4, 2, 8192, 512], P('grp', None, 'tok'), may hold values from -6 to 6
- latents: float32 [4, 2, 2048, 512], P('grp'), may hold values from -6 to 6
- segments: int32 [4, 2, 8192], P('grp', None, 'tok'), may hold values from 0 to 7, as said below
- scene_mask: int32 [4, 2, 8, 8], P('grp'), may hold values from 0 to 1
- counts: int32 [4, 2, 8], P('grp', None, 'tok'), may hold values from 512 to 1024, as said below
- token_gain: float32 [512], replicated, may hold values from 0.1 to 1.9
- query_gain: float32 [512], replicated, may hold values from 0.1 to 1.9
- query_weight: bfloat16 [512, 512], replicated, may hold values from -0.5 to 0.5
- key_weight: bfloat16 [512, 512], replicated, may hold values from -0.25 to 0.25
- value_weight: bfloat16 [512, 512], replicated, may hold values from -0.25 to 0.25
- output_weight: bfloat16 [512, 512], replicated, may hold values from -4 to 4
- first_gain: float32 [512], replicated, may hold values from 0.1 to 1.9
- first_up: bfloat16 [512, 2048], replicated, may hold values from -0.25 to 0.25
- first_down: bfloat16 [2048, 512], replicated, may hold values from -0.25 to 0.25
- mixer_gain: float32 [512], replicated, may hold values from 0.1 to 1.9
- mixer_project: bfloat16 [512, 1536], replicated, may hold values from -0.25 to 0.25
- mixer_output: bfloat16 [512, 512], replicated, may hold values from -6 to 6
- second_gain: float32 [512], replicated, may hold values from 0.1 to 1.9
- second_up: bfloat16 [512, 2048], replicated, may hold values from -0.25 to 0.25
- second_down: bfloat16 [2048, 512], replicated, may hold values from -0.25 to 0.25
- cotangent: float32 [4, 2, 2048, 512], P('grp', None, 'tok'), may hold values from -6 to 6
Outputs:
- latents_out: float32 [4, 2, 2048, 512], P('grp', None, 'tok')
- latents_grad: float32 [4, 2, 2048, 512], P('grp', None, 'tok')
- tokens_grad: float32 [4, 2, 8192, 512], P('grp', None, 'tok')
- grad_token_gain: float32 [512], P('tok')
- grad_query_gain: float32 [512], P('tok')
- grad_query_weight: float32 [512, 512], P('tok')
- grad_key_weight: float32 [512, 512], P('tok')
- grad_value_weight: float32 [512, 512], P('tok')
- grad_output_weight: float32 [512, 512], P('tok')
- grad_first_gain: float32 [512], P('tok')
- grad_first_up: float32 [512, 2048], P('tok')
- grad_first_down: float32 [2048, 512], P('tok')
- grad_mixer_gain: float32 [512], P('tok')
- grad_mixer_project: float32 [512, 1536], P('tok')
- grad_mixer_output: float32 [512, 512], P('tok')
- grad_second_gain: float32 [512], P('tok')
- grad_second_up: float32 [512, 2048], P('tok')
- grad_second_down: float32 [2048, 512], P('tok')
The draws below stay inside these ranges and needn't reach their ends.
Inputs may be any that keep to these rules, and one draw needn't show every extreme that they name: `segments`: scenes come in runs of 32 tokens; in every set one scene holds the first 32 tokens of every device's share, and every latent group sees it. The first counts tokens of a device's share of a set are live, the rest are padding that no latent sees; in every set some device is full.
All inputs are finite; a program needn't handle non-finite values.
Results may differ from the reference program's by a relative error of at most 0.034.
Values may be sent and summed in bfloat16 or wider, within the bound.
A program may use at most 256 MiB of HBM per device.

```python
from functools import partial
import jax
import jax.numpy as jnp
from jax import lax

D = 512
FF = 2048
L = 2048
H = 8
HD = 64
TOK_DEV = 1024
MB = 2
SCENES = 8
LGROUPS = 8
HEAD = 32
GROUPS = 4
TOKENS = 8192


def scene_layout(key):
    block_key, span_key, table_key = jax.random.split(key, 3)
    blocks = jax.random.randint(block_key, (GROUPS, MB, TOKENS // HEAD), 0, SCENES)
    layout = jnp.repeat(blocks, HEAD, axis=2, total_repeat_length=TOKENS)
    spanning = jax.random.randint(span_key, (GROUPS, MB, 1), 0, SCENES)
    place = jnp.arange(TOKENS) % TOK_DEV
    layout = jnp.where(place[None, None, :] < HEAD, spanning, layout)
    table = jax.random.randint(table_key, (GROUPS, MB, SCENES, LGROUPS), 0, 2)
    chosen = jnp.arange(SCENES)[None, None, :, None] == spanning[:, :, :, None]
    table = jnp.where(chosen, 1, table)
    return (layout.astype(jnp.int32), table.astype(jnp.int32))


def draw_segments(key, part):
    layout, table = scene_layout(key)
    return layout


def draw_scene_mask(key, part):
    layout, table = scene_layout(key)
    return table


def draw_counts(key, part):
    key = jax.random.fold_in(key, 3)
    base_key, full_key = jax.random.split(key)
    shards = TOKENS // TOK_DEV
    drawn = jax.random.randint(base_key, (GROUPS, MB, shards), TOK_DEV // 2, TOK_DEV + 1)
    full = jax.random.randint(full_key, (GROUPS, MB, 1), 0, shards)
    return jnp.where(jnp.arange(shards)[None, None, :] == full, TOK_DEV, drawn).astype(jnp.int32)


def steps_of(stream_key, dims, cuts, smallest, top_value):
    level = 1.0
    for axis_at, blocks in cuts:
        draws = jax.random.uniform(jax.random.fold_in(jax.random.fold_in(stream_key, 6), axis_at), (blocks,), jnp.float32, smallest / len(cuts), top_value / len(cuts))
        level = level * jnp.repeat(jnp.exp(draws), dims[axis_at] // blocks).reshape((-1,) + (1,) * (len(dims) - 1 - axis_at))
    return level


def noise(stream_key, extent, width, most, cuts=(), held_as=jnp.bfloat16):
    result = jax.random.normal(stream_key, extent, jnp.float32) * width
    if len(cuts) > 0:
        result = steps_of(stream_key, extent, cuts, -0.22, 0.18) * result
    return jnp.clip(result, min=-most, max=most).astype(held_as)


def setup_inputs(seed: int = 0) -> dict:
    key_of = jax.random.split(jax.random.key(seed), 22)
    return {
        "tokens": noise(key_of[0], (GROUPS, MB, TOKENS, D), 1.0, 6.0, ((0, 4), (2, 8))),
        "latents": noise(key_of[1], (GROUPS, MB, L, D), 1.0, 6.0, ((0, 4),), jnp.float32),
        "segments": draw_segments(jax.random.fold_in(key_of[21], 71), 0),
        "scene_mask": draw_scene_mask(jax.random.fold_in(key_of[21], 71), 0),
        "counts": draw_counts(jax.random.fold_in(key_of[21], 71), 0),
        "token_gain": jnp.clip(1.0 + 0.18 * jax.random.normal(key_of[5], (D,), jnp.float32), 0.1, 1.9),
        "query_gain": jnp.clip(1.0 + 0.18 * jax.random.normal(key_of[6], (D,), jnp.float32), 0.1, 1.9),
        "query_weight": noise(key_of[7], (D, D), (D // 4) ** -0.5, 0.5),
        "key_weight": noise(key_of[8], (D, D), D ** -0.5, 0.25),
        "value_weight": noise(key_of[9], (D, D), D ** -0.5, 0.25),
        "output_weight": noise(key_of[10], (D, D), (max(D // 256, 1)) ** -0.5, 4.0),
        "first_gain": jnp.clip(1.0 + 0.18 * jax.random.normal(key_of[11], (D,), jnp.float32), 0.1, 1.9),
        "first_up": noise(key_of[12], (D, FF), D ** -0.5, 0.25),
        "first_down": noise(key_of[13], (FF, D), (FF // 4) ** -0.5, 0.25),
        "mixer_gain": jnp.clip(1.0 + 0.18 * jax.random.normal(key_of[14], (D,), jnp.float32), 0.1, 1.9),
        "mixer_project": noise(key_of[15], (D, 3 * D), D ** -0.5, 0.25),
        "mixer_output": noise(key_of[16], (D, D), (max(D // 512, 1)) ** -0.5, 6.0),
        "second_gain": jnp.clip(1.0 + 0.18 * jax.random.normal(key_of[17], (D,), jnp.float32), 0.1, 1.9),
        "second_up": noise(key_of[18], (D, FF), D ** -0.5, 0.25),
        "second_down": noise(key_of[19], (FF, D), (FF // 4) ** -0.5, 0.25),
        "cotangent": noise(key_of[20], (GROUPS, MB, L, D), 1.0, 6.0, ((0, 4), (2, 8)), jnp.float32),
    }


EPS = 1e-05
NEG = -1e+30
HIGH = lax.Precision.HIGHEST

@jax.custom_vjp
def low(v):
    return lax.optimization_barrier(v.astype(jnp.bfloat16)).astype(jnp.float32)

@jax.custom_vjp
def low_back(v):
    return v

def low_keep(v):
    return (low(v), None)

def low_pass(kept, grad):
    return (grad,)

def back_keep(v):
    return (v, None)

def back_low(kept, grad):
    return (low(grad),)
low.defvjp(low_keep, low_pass)
low_back.defvjp(back_keep, back_low)

def norm_rows(values, gain):
    centre = values - lax.optimization_barrier(jnp.mean(values, axis=-1, keepdims=True))
    spread = lax.optimization_barrier(jnp.mean(centre * centre, axis=-1, keepdims=True))
    return centre * lax.rsqrt(spread + EPS) * gain

def product(left, right):
    return jnp.dot(left, right, precision=HIGH)

def feed_forward(residual, gain, up_weight, down_weight):
    normed = low(norm_rows(residual, gain))
    hidden = low_back(product(normed, up_weight))
    active = low(jax.nn.gelu(hidden))
    return residual + low_back(product(active, down_weight))

def one_set(weights, source, latent_in, seg_row, mask_table, count_row):
    token_gain, query_gain, query_weight, key_weight, value_weight, output_weight, first_gain, first_up, first_down, mixer_gain, mixer_project, mixer_output, second_gain, second_up, second_down = weights
    place = jnp.arange(TOKENS) % TOK_DEV
    owner = jnp.arange(TOKENS) // TOK_DEV
    alive = place < count_row[owner]
    seen = mask_table[seg_row]
    latent_group = jnp.arange(L) // (L // LGROUPS)
    allowed = (seen[:, latent_group].T > 0) & alive[None, :]
    normed = low(norm_rows(source, token_gain))
    key_rows = low_back(low(product(normed, key_weight)))
    value_rows = low_back(low(product(normed, value_weight)))
    latent_normed = low(norm_rows(latent_in, query_gain))
    queries = low_back(low(product(latent_normed, query_weight)))
    scores = low_back(product(queries, key_rows.T) * D ** (-0.5))
    scores = jnp.where(allowed, scores, NEG)
    row_top = lax.optimization_barrier(jnp.max(scores, axis=1, keepdims=True))
    unnormed = jnp.exp(scores - row_top)
    row_total = lax.optimization_barrier(jnp.sum(unnormed, axis=1, keepdims=True))
    weighted = low_back(product(low(unnormed), value_rows))
    attended = low_back(low(weighted / row_total))
    first_mid = latent_in + low_back(product(attended, output_weight))
    mixer_mid = feed_forward(first_mid, first_gain, first_up, first_down)
    mixer_normed = low(norm_rows(mixer_mid, mixer_gain))
    packed = low_back(low(product(mixer_normed, mixer_project))).reshape(L, 3, H, HD)
    logits = low_back(jnp.einsum('qhd,khd->hqk', packed[:, 0], packed[:, 1], precision=HIGH) * HD ** (-0.5))
    peak_row = lax.optimization_barrier(jnp.max(logits, axis=-1, keepdims=True))
    raised = jnp.exp(logits - peak_row)
    softened = raised / lax.optimization_barrier(jnp.sum(raised, axis=-1, keepdims=True))
    mixed_rows = jnp.einsum('hqk,khd->qhd', low(softened), packed[:, 2], precision=HIGH).reshape(L, D)
    mixed_rows = low_back(low(mixed_rows))
    second_mid = mixer_mid + low_back(product(mixed_rows, mixer_output))
    return feed_forward(second_mid, second_gain, second_up, second_down)

def reference(tokens, latents, segments, scene_mask, counts, token_gain, query_gain, query_weight, key_weight, value_weight, output_weight, first_gain, first_up, first_down, mixer_gain, mixer_project, mixer_output, second_gain, second_up, second_down, cotangent):
    weights = tuple((item.astype(jnp.float32) for item in (token_gain, query_gain, query_weight, key_weight, value_weight, output_weight, first_gain, first_up, first_down, mixer_gain, mixer_project, mixer_output, second_gain, second_up, second_down)))
    source_all = tokens.astype(jnp.float32).reshape(GROUPS * MB, TOKENS, D)
    latent_all = latents.reshape(GROUPS * MB, L, D)
    seg_all = segments.reshape(GROUPS * MB, TOKENS).astype(jnp.int32)
    mask_all = scene_mask.reshape(GROUPS * MB, SCENES, LGROUPS).astype(jnp.int32)
    count_all = counts.reshape(GROUPS * MB, TOKENS // TOK_DEV).astype(jnp.int32)

    def forward(source_in, latent_start, weight_all):

        def single(item):
            return jax.checkpoint(partial(one_set, weight_all))(*item)
        return lax.map(single, (source_in, latent_start, seg_all, mask_all, count_all))
    outputs, pull = jax.vjp(forward, source_all, latent_all, weights)
    source_grad, latent_grad, weight_grad = pull(cotangent.reshape(GROUPS * MB, L, D))
    return (outputs.reshape(GROUPS, MB, L, D), latent_grad.reshape(GROUPS, MB, L, D), source_grad.reshape(GROUPS, MB, TOKENS, D), weight_grad[0], weight_grad[1], weight_grad[2], weight_grad[3], weight_grad[4], weight_grad[5], weight_grad[6], weight_grad[7], weight_grad[8], weight_grad[9], weight_grad[10], weight_grad[11], weight_grad[12], weight_grad[13], weight_grad[14])
```

```python
import functools

import jax
import jax.numpy as jnp
from jax import lax
from jax.experimental import pallas as pl
from jax.experimental.pallas import tpu as pltpu
from jax.sharding import PartitionSpec as P

D = 512
L = 2048
H = 8
HD = 64
TOK_DEV = 1024
MB = 2
SCENES = 8
LGROUPS = 8


EPS = 1e-05
NEG = -1e30


def norm_rows(values, gain):
    centre = values - jnp.mean(values, axis=-1, keepdims=True)
    spread = jnp.mean(centre * centre, axis=-1, keepdims=True)
    return centre * lax.rsqrt(spread + EPS) * gain


def norm_back(values, gain, upstream):
    unused, pull = jax.vjp(norm_rows, values, gain)
    return pull(upstream)


def gelu_back(hidden, upstream):
    unused, pull = jax.vjp(jax.nn.gelu, hidden)
    return pull(upstream)[0]


def product_plain(left, right):
    return jnp.dot(left, right, preferred_element_type=jnp.float32)


def product_rows(left, right):
    return lax.dot_general(
        left, right, (((0,), (0,)), ((), ())), preferred_element_type=jnp.float32
    )


def product_cols(left, right):
    return lax.dot_general(
        left, right, (((1,), (1,)), ((), ())), preferred_element_type=jnp.float32
    )


def add_term(store, name, value):
    if name in store:
        store[name] = store[name] + value
    else:
        store[name] = value


def project_tokens(tokens, member, token_gain, key_weight, value_weight):
    source = tokens[0, member].astype(jnp.float32)
    normed = norm_rows(source, token_gain).astype(jnp.bfloat16)
    key_rows = product_plain(normed, key_weight).astype(jnp.bfloat16)
    value_rows = product_plain(normed, value_weight).astype(jnp.bfloat16)
    return (source, normed, key_rows, value_rows)


def mlp_forward(residual, gain, up_weight, down_weight):
    normed = norm_rows(residual, gain).astype(jnp.bfloat16)
    hidden = product_plain(normed, up_weight)
    active = jax.nn.gelu(hidden).astype(jnp.bfloat16)
    return (residual + product_plain(active, down_weight), (normed, hidden, active))


def mlp_backward(residual, gain, up_weight, down_weight, saved, upstream):
    normed, hidden, active = saved
    grad_low = upstream.astype(jnp.bfloat16)
    grad_down = product_rows(active, grad_low)
    hidden_grad = gelu_back(hidden, product_cols(grad_low, down_weight)).astype(jnp.bfloat16)
    grad_up = product_rows(normed, hidden_grad)
    residual_grad, grad_gain = norm_back(residual, gain, product_cols(hidden_grad, up_weight))
    return (upstream + residual_grad, grad_gain, grad_up, grad_down)


def mixer_forward(residual, gain, project, output):
    own_rows = residual.shape[0]
    normed = norm_rows(residual, gain).astype(jnp.bfloat16)
    packed = product_plain(normed, project).astype(jnp.bfloat16)
    pair_rows = lax.all_gather(packed[:, D:], "tok", axis=0, tiled=True)
    every = pair_rows.shape[0]
    own_queries = packed[:, :D].reshape(own_rows, H, HD)
    keys = pair_rows[:, :D].reshape(every, H, HD)
    values = pair_rows[:, D:].reshape(every, H, HD)
    logits = jnp.einsum(
        "qhd,khd->hqk", own_queries, keys, preferred_element_type=jnp.float32
    ) * HD ** (-0.5)
    peak_row = jnp.max(logits, axis=-1, keepdims=True)
    raised = jnp.exp(logits - peak_row)
    softened = raised / jnp.sum(raised, axis=-1, keepdims=True)
    softened_low = softened.astype(jnp.bfloat16)
    mixed_rows = jnp.einsum(
        "hqk,khd->qhd", softened_low, values, preferred_element_type=jnp.float32
    )
    mixed_rows = mixed_rows.reshape(own_rows, D).astype(jnp.bfloat16)
    return (
        residual + product_plain(mixed_rows, output),
        (normed, own_queries, keys, values, softened, softened_low, mixed_rows),
    )


def mixer_backward(residual, gain, project, output, saved, upstream):
    normed, own_queries, keys, values, softened, softened_low, mixed_rows = saved
    own_rows = upstream.shape[0]
    every = keys.shape[0]
    grad_low = upstream.astype(jnp.bfloat16)
    grad_output = product_rows(mixed_rows, grad_low)
    mixed_grad = product_cols(grad_low, output).astype(jnp.bfloat16).reshape(own_rows, H, HD)
    value_grad = jnp.einsum(
        "hqk,qhd->khd", softened_low, mixed_grad, preferred_element_type=jnp.float32
    )
    soft_grad = jnp.einsum("qhd,khd->hqk", mixed_grad, values, preferred_element_type=jnp.float32)
    logit_grad = softened * (soft_grad - jnp.sum(soft_grad * softened, axis=-1, keepdims=True))
    logit_grad = logit_grad.astype(jnp.bfloat16)
    query_grad = jnp.einsum(
        "hqk,khd->qhd", logit_grad, keys, preferred_element_type=jnp.float32
    ) * HD ** (-0.5)
    key_grad = jnp.einsum(
        "hqk,qhd->khd", logit_grad, own_queries, preferred_element_type=jnp.float32
    ) * HD ** (-0.5)
    pair_terms = jnp.concatenate([key_grad.reshape(every, D), value_grad.reshape(every, D)], axis=1)
    pair_grad = lax.psum_scatter(
        pair_terms.astype(jnp.bfloat16), "tok", scatter_dimension=0, tiled=True
    ).astype(jnp.float32)
    packed_grad = jnp.concatenate([query_grad.reshape(own_rows, D), pair_grad], axis=1).astype(
        jnp.bfloat16
    )
    grad_project = product_rows(normed, packed_grad)
    residual_grad, grad_gain = norm_back(residual, gain, product_cols(packed_grad, project))
    return (upstream + residual_grad, grad_gain, grad_project, grad_output)


def general_body(
    tokens,
    latents,
    segments,
    scene_mask,
    counts,
    token_gain,
    query_gain,
    query_weight,
    key_weight,
    value_weight,
    output_weight,
    first_gain,
    first_up,
    first_down,
    mixer_gain,
    mixer_project,
    mixer_output,
    second_gain,
    second_up,
    second_down,
    cotangent,
):
    scale = D ** (-0.5)
    shards = lax.axis_size("tok")
    own_rows = L // shards
    row_start = lax.axis_index("tok") * own_rows
    latent_group = jnp.arange(L) // (L // LGROUPS)
    latent_onehot = (latent_group[:, None] == jnp.arange(LGROUPS)[None, :]).astype(jnp.float32)
    token_place = jnp.arange(TOK_DEV)
    records = []
    latent_outs = []
    for member in range(MB):
        record = {}
        source, normed, key_rows, value_rows = project_tokens(
            tokens, member, token_gain, key_weight, value_weight
        )
        record["token_side"] = (source, normed, key_rows, value_rows)
        scene_onehot = (segments[0, member][:, None] == jnp.arange(SCENES)[None, :]).astype(
            jnp.float32
        )
        token_seen = jnp.dot(scene_onehot, scene_mask[0, member].astype(jnp.float32))
        visible = product_cols(latent_onehot, token_seen)
        alive = token_place < counts[0, member, 0]
        allowed = (visible > 0.5) & alive[None, :]
        latent_every = latents[0, member]
        normed_every = norm_rows(latent_every, query_gain).astype(jnp.bfloat16)
        queries = product_plain(normed_every, query_weight).astype(jnp.bfloat16)
        scores = jnp.where(allowed, product_cols(queries, key_rows) * scale, NEG)
        row_top = lax.pmax(jnp.max(scores, axis=1), "tok")
        unnormed = jnp.exp(scores - row_top[:, None])
        row_total, weighted = (
            lax.psum_scatter(
                jnp.sum(unnormed, axis=1).astype(jnp.bfloat16),
                "tok",
                scatter_dimension=0,
                tiled=True,
            ).astype(jnp.float32),
            lax.psum_scatter(
                product_plain(unnormed.astype(jnp.bfloat16), value_rows).astype(jnp.bfloat16),
                "tok",
                scatter_dimension=0,
                tiled=True,
            ).astype(jnp.float32),
        )
        latent_in = lax.dynamic_slice_in_dim(latent_every, row_start, own_rows, 0)
        latent_normed = lax.dynamic_slice_in_dim(normed_every, row_start, own_rows, 0)
        attended = weighted / row_total[:, None]
        attended_low = attended.astype(jnp.bfloat16)
        first_mid = latent_in + product_plain(attended_low, output_weight)
        mixer_mid, first_saved = mlp_forward(first_mid, first_gain, first_up, first_down)
        second_mid, mixer_saved = mixer_forward(mixer_mid, mixer_gain, mixer_project, mixer_output)
        final_rows, second_saved = mlp_forward(second_mid, second_gain, second_up, second_down)
        latent_outs.append(final_rows)
        record["latent_side"] = (
            allowed,
            latent_in,
            latent_normed,
            queries,
            row_top,
            row_total,
            attended,
            attended_low,
            first_mid,
            mixer_mid,
            second_mid,
            first_saved,
            mixer_saved,
            second_saved,
        )
        records.append(record)
    grads = {}
    latent_grads = []
    token_grads = []
    for member in range(MB):
        record = records[member]
        source, normed, key_rows, value_rows = record["token_side"]
        (
            allowed,
            latent_in,
            latent_normed,
            queries,
            row_top,
            row_total,
            attended,
            attended_low,
            first_mid,
            mixer_mid,
            second_mid,
            first_saved,
            mixer_saved,
            second_saved,
        ) = record["latent_side"]
        second_back = mlp_backward(
            second_mid, second_gain, second_up, second_down, second_saved, cotangent[0, member]
        )
        add_term(grads, "second_gain", second_back[1])
        add_term(grads, "second_up", second_back[2])
        add_term(grads, "second_down", second_back[3])
        mixer_back = mixer_backward(
            mixer_mid, mixer_gain, mixer_project, mixer_output, mixer_saved, second_back[0]
        )
        add_term(grads, "mixer_gain", mixer_back[1])
        add_term(grads, "mixer_project", mixer_back[2])
        add_term(grads, "mixer_output", mixer_back[3])
        first_back = mlp_backward(
            first_mid, first_gain, first_up, first_down, first_saved, mixer_back[0]
        )
        add_term(grads, "first_gain", first_back[1])
        add_term(grads, "first_up", first_back[2])
        add_term(grads, "first_down", first_back[3])
        latent_upstream = first_back[0]
        grad_low = latent_upstream.astype(jnp.bfloat16)
        add_term(grads, "output_weight", product_rows(attended_low, grad_low))
        attended_grad = lax.optimization_barrier(
            product_cols(grad_low, output_weight).astype(jnp.bfloat16)
        ).astype(jnp.float32)
        weighted_grad = (attended_grad / row_total[:, None]).astype(jnp.bfloat16)
        total_grad = -jnp.sum(attended_grad * attended, axis=1) / row_total
        weighted_every, total_every = (
            lax.all_gather(
                weighted_grad.astype(jnp.float32).astype(jnp.bfloat16), "tok", axis=0, tiled=True
            ).astype(jnp.float32),
            lax.all_gather(total_grad.astype(jnp.bfloat16), "tok", axis=0, tiled=True).astype(
                total_grad.dtype
            ),
        )
        weighted_every = weighted_every.astype(jnp.bfloat16)
        scores = jnp.where(allowed, product_cols(queries, key_rows) * scale, NEG)
        unnormed = jnp.exp(scores - row_top[:, None])
        unnormed_grad = product_cols(weighted_every, value_rows) + total_every[:, None]
        score_grad = (unnormed * unnormed_grad).astype(jnp.bfloat16)
        value_grad = product_rows(unnormed.astype(jnp.bfloat16), weighted_every).astype(
            jnp.bfloat16
        )
        key_grad = (product_rows(score_grad, queries) * scale).astype(jnp.bfloat16)
        query_grad = lax.psum_scatter(
            (product_plain(score_grad, key_rows) * scale).astype(jnp.bfloat16),
            "tok",
            scatter_dimension=0,
            tiled=True,
        )
        add_term(grads, "key_weight", product_rows(normed, key_grad))
        add_term(grads, "value_weight", product_rows(normed, value_grad))
        normed_grad = product_cols(key_grad, key_weight) + product_cols(value_grad, value_weight)
        source_grad, gain_grad = norm_back(source, token_gain, normed_grad)
        add_term(grads, "token_gain", gain_grad)
        token_grads.append(source_grad)
        add_term(grads, "query_weight", product_rows(latent_normed, query_grad))
        latent_grad, gain_grad = norm_back(
            latent_in, query_gain, product_cols(query_grad, query_weight)
        )
        add_term(grads, "query_gain", gain_grad)
        latent_grads.append(latent_upstream + latent_grad)
    parts = (
        lax.psum_scatter(
            grads["token_gain"].astype(jnp.bfloat16), "tok", scatter_dimension=0, tiled=True
        ).astype(jnp.float32),
        lax.psum_scatter(
            grads["query_gain"].astype(jnp.bfloat16), "tok", scatter_dimension=0, tiled=True
        ).astype(jnp.float32),
        lax.psum_scatter(
            grads["query_weight"].astype(jnp.bfloat16), "tok", scatter_dimension=0, tiled=True
        ).astype(jnp.float32),
        lax.psum_scatter(
            grads["key_weight"].astype(jnp.bfloat16), "tok", scatter_dimension=0, tiled=True
        ).astype(jnp.float32),
        lax.psum_scatter(
            grads["value_weight"].astype(jnp.bfloat16), "tok", scatter_dimension=0, tiled=True
        ).astype(jnp.float32),
        lax.psum_scatter(
            grads["output_weight"].astype(jnp.bfloat16), "tok", scatter_dimension=0, tiled=True
        ).astype(jnp.float32),
        lax.psum_scatter(
            grads["first_gain"].astype(jnp.bfloat16), "tok", scatter_dimension=0, tiled=True
        ).astype(jnp.float32),
        lax.psum_scatter(
            grads["first_up"].astype(jnp.bfloat16), "tok", scatter_dimension=0, tiled=True
        ).astype(jnp.float32),
        lax.psum_scatter(
            grads["first_down"].astype(jnp.bfloat16), "tok", scatter_dimension=0, tiled=True
        ).astype(jnp.float32),
        lax.psum_scatter(
            grads["mixer_gain"].astype(jnp.bfloat16), "tok", scatter_dimension=0, tiled=True
        ).astype(jnp.float32),
        lax.psum_scatter(
            grads["mixer_project"].astype(jnp.bfloat16), "tok", scatter_dimension=0, tiled=True
        ).astype(jnp.float32),
        lax.psum_scatter(
            grads["mixer_output"].astype(jnp.bfloat16), "tok", scatter_dimension=0, tiled=True
        ).astype(jnp.float32),
        lax.psum_scatter(
            grads["second_gain"].astype(jnp.bfloat16), "tok", scatter_dimension=0, tiled=True
        ).astype(jnp.float32),
        lax.psum_scatter(
            grads["second_up"].astype(jnp.bfloat16), "tok", scatter_dimension=0, tiled=True
        ).astype(jnp.float32),
        lax.psum_scatter(
            grads["second_down"].astype(jnp.bfloat16), "tok", scatter_dimension=0, tiled=True
        ).astype(jnp.float32),
    )
    summed = (
        lax.psum(parts[0].astype(jnp.bfloat16), "grp").astype(jnp.float32),
        lax.psum(parts[1].astype(jnp.bfloat16), "grp").astype(jnp.float32),
        lax.psum(parts[2].astype(jnp.bfloat16), "grp").astype(jnp.float32),
        lax.psum(parts[3].astype(jnp.bfloat16), "grp").astype(jnp.float32),
        lax.psum(parts[4].astype(jnp.bfloat16), "grp").astype(jnp.float32),
        lax.psum(parts[5].astype(jnp.bfloat16), "grp").astype(jnp.float32),
        lax.psum(parts[6].astype(jnp.bfloat16), "grp").astype(jnp.float32),
        lax.psum(parts[7].astype(jnp.bfloat16), "grp").astype(jnp.float32),
        lax.psum(parts[8].astype(jnp.bfloat16), "grp").astype(jnp.float32),
        lax.psum(parts[9].astype(jnp.bfloat16), "grp").astype(jnp.float32),
        lax.psum(parts[10].astype(jnp.bfloat16), "grp").astype(jnp.float32),
        lax.psum(parts[11].astype(jnp.bfloat16), "grp").astype(jnp.float32),
        lax.psum(parts[12].astype(jnp.bfloat16), "grp").astype(jnp.float32),
        lax.psum(parts[13].astype(jnp.bfloat16), "grp").astype(jnp.float32),
        lax.psum(parts[14].astype(jnp.bfloat16), "grp").astype(jnp.float32),
    )
    return (
        jnp.stack(latent_outs)[None],
        jnp.stack(latent_grads)[None],
        jnp.stack(token_grads)[None],
    ) + tuple(summed)


TOK = 8
ROWS = L // TOK
FF = 2048
GR = L // LGROUPS
LOG2E = 1.4426950408889634
LN2 = 0.6931471805599453
F32 = jnp.float32
BF16 = jnp.bfloat16
MIB = 1024 * 1024


def nn(left, right):
    return lax.dot_general(left, right, (((1,), (0,)), ((), ())), preferred_element_type=F32)


def nt(left, right):
    return lax.dot_general(left, right, (((1,), (1,)), ((), ())), preferred_element_type=F32)


def tn(left, right):
    return lax.dot_general(left, right, (((0,), (0,)), ((), ())), preferred_element_type=F32)


def norm_parts(values):
    centre = values - jnp.mean(values, axis=-1, keepdims=True)
    inverse = lax.rsqrt(jnp.mean(centre * centre, axis=-1, keepdims=True) + EPS)
    return centre * inverse, inverse


def norm_pull(hat, inverse, gain, upstream):
    scaled = upstream * gain
    inner = jnp.mean(scaled * hat, axis=-1, keepdims=True)
    grad = (scaled - jnp.mean(scaled, axis=-1, keepdims=True) - hat * inner) * inverse
    return grad, upstream * hat


def places():
    me = lax.axis_index("tok")
    core = lax.rem(me, 2)
    chip = lax.div(me, 2)
    mate = me + 1 - 2 * core
    flip_x = chip + 1 - 2 * lax.rem(chip, 2)
    flip_y = lax.rem(chip + 2, 4)
    far = 3 - chip
    return me, core, chip, mate, (far, flip_x, flip_y)


def remote(src, dst, send_sem, recv_sem, peer):
    return pltpu.make_async_remote_copy(
        src_ref=src,
        dst_ref=dst,
        send_sem=send_sem,
        recv_sem=recv_sem,
        device_id={"tok": peer},
        device_id_type=pl.DeviceIdType.MESH,
    )


def greet(devices):
    barrier = pltpu.get_barrier_semaphore()
    for device in devices:
        pl.semaphore_signal(
            barrier, inc=1, device_id={"tok": device}, device_id_type=pl.DeviceIdType.MESH
        )
    pl.semaphore_wait(barrier, len(devices))


def mask_bias(hot, table):
    seen = nn(hot, table)
    bias = (seen - 1.0) * 1e30
    return jnp.concatenate([bias, bias], axis=1)


def cross_forward_kernel(
    tok_ref, lat_ref, tgain_ref, qgain_ref, qw_ref, kw_ref, vw_ref, hot_ref, tab_ref,
    k_ref, v_ref, q_ref, acc_ref, ml_ref, vt_ref,
):
    @pl.when(pl.program_id(1) == 0)
    def _():
        hat, inverse = norm_parts(tok_ref[0, 0].astype(F32))
        normed = (hat * tgain_ref[...]).astype(BF16)
        k_ref[0] = nn(normed, kw_ref[...]).astype(BF16)
        values = nn(normed, vw_ref[...]).astype(BF16)
        v_ref[0] = values
        vt_ref[...] = values.T

    hat, inverse = norm_parts(lat_ref[0, 0])
    normed = (hat * qgain_ref[...]).astype(BF16)
    queries = (nn(normed, qw_ref[...]) * (D ** (-0.5) * LOG2E)).astype(BF16)
    q_ref[0] = queries
    scores = nt(k_ref[0], queries) + mask_bias(hot_ref[0], tab_ref[0, 0])
    top = jnp.max(scores, axis=0, keepdims=True)
    raised = jnp.exp2(scores - top)
    total = jnp.sum(raised, axis=0, keepdims=True)
    acc_ref[0, 0] = nn(vt_ref[...], raised.astype(BF16)).astype(BF16)
    ml_ref[0, 0] = jnp.concatenate([top, total, jnp.zeros((6, GR), F32)], axis=0)


def cross_forward(tokens, latents, token_gain, query_gain, query_weight, key_weight, value_weight, hot, table):
    whole = lambda shape: pl.BlockSpec(shape, lambda b, g: (0,) * len(shape))
    return pl.pallas_call(
        cross_forward_kernel,
        grid=(MB, LGROUPS),
        in_specs=[
            pl.BlockSpec((1, 1, TOK_DEV, D), lambda b, g: (0, b, 0, 0)),
            pl.BlockSpec((1, 1, GR, D), lambda b, g: (0, b, g, 0)),
            whole((1, D)),
            whole((1, D)),
            whole((D, D)),
            whole((D, D)),
            whole((D, D)),
            pl.BlockSpec((1, TOK_DEV, 128), lambda b, g: (b, 0, 0)),
            pl.BlockSpec((1, 1, 128, 128), lambda b, g: (b, g, 0, 0)),
        ],
        out_specs=[
            pl.BlockSpec((1, TOK_DEV, D), lambda b, g: (b, 0, 0)),
            pl.BlockSpec((1, TOK_DEV, D), lambda b, g: (b, 0, 0)),
            pl.BlockSpec((1, GR, D), lambda b, g: (b, g, 0)),
            pl.BlockSpec((1, 1, D, GR), lambda b, g: (g, b, 0, 0)),
            pl.BlockSpec((1, 1, 8, GR), lambda b, g: (g, b, 0, 0)),
        ],
        out_shape=[
            jax.ShapeDtypeStruct((MB, TOK_DEV, D), BF16),
            jax.ShapeDtypeStruct((MB, TOK_DEV, D), BF16),
            jax.ShapeDtypeStruct((MB, L, D), BF16),
            jax.ShapeDtypeStruct((LGROUPS, MB, D, GR), BF16),
            jax.ShapeDtypeStruct((LGROUPS, MB, 8, GR), F32),
        ],
        scratch_shapes=[pltpu.VMEM((D, TOK_DEV), BF16)],
        compiler_params=pltpu.CompilerParams(
            dimension_semantics=("arbitrary", "arbitrary"), vmem_limit_bytes=48 * MIB
        ),
        cost_estimate=pl.CostEstimate(
            flops=14 * 10**9, bytes_accessed=22 * 10**6, transcendentals=4 * 10**6
        ),
        name="cross_forward",
    )(tokens, latents, token_gain, query_gain, query_weight, key_weight, value_weight, hot, table)


def gather_sum_kernel(
    softmax, *refs
):
    if softmax:
        (part_ref, stat_ref, out_ref, lse_ref, mine, got, stage, arrive, total,
         mine_s, got_s, stage_s, arrive_s, local_sem, core_send, core_recv, chip_send, chip_recv,
         local_sem_s, core_send_s, core_recv_s, chip_send_s, chip_recv_s) = refs
    else:
        (part_ref, out_ref, mine, got, stage, arrive, total,
         local_sem, core_send, core_recv, chip_send, chip_recv) = refs
    me, core, chip, mate, others = places()
    targets = others + (chip,)
    greet([mate] + [2 * other + core for other in others])
    locals_, cores = [], []
    for slot, target in enumerate(targets):
        own_block = 2 * target + core
        mate_block = 2 * target + 1 - core
        cores.append([remote(part_ref.at[mate_block], got.at[slot], core_send.at[slot], core_recv.at[slot], mate)])
        locals_.append([pltpu.make_async_copy(part_ref.at[own_block], mine.at[slot], local_sem.at[slot])])
        if softmax:
            cores[-1].append(remote(stat_ref.at[mate_block], got_s.at[slot], core_send_s.at[slot], core_recv_s.at[slot], mate))
            locals_[-1].append(pltpu.make_async_copy(stat_ref.at[own_block], mine_s.at[slot], local_sem_s.at[slot]))
        for copy in cores[-1] + locals_[-1]:
            copy.start()
    chips = []
    for slot, target in enumerate(targets):
        for copy in locals_[slot]:
            copy.wait()
        for copy in cores[slot]:
            copy.wait_recv()
        for member in range(MB):
            left = mine[slot, member].astype(F32)
            right = got[slot, member].astype(F32)
            if softmax:
                left_s, right_s = mine_s[slot, member], got_s[slot, member]
                top = jnp.maximum(left_s[0:1], right_s[0:1])
                left_w, right_w = jnp.exp2(left_s[0:1] - top), jnp.exp2(right_s[0:1] - top)
                added = left * left_w + right * right_w
                sums = left_s[1:2] * left_w + right_s[1:2] * right_w
                stage_s[slot, member] = jnp.concatenate([top, sums, jnp.zeros((6, ROWS), F32)], axis=0)
            else:
                added = left + right
            if slot == 3:
                total[member] = added
            else:
                stage[slot, member] = added.astype(BF16)
        if slot < 3:
            peer = 2 * target + core
            chips.append([remote(stage.at[slot], arrive.at[slot], chip_send.at[slot], chip_recv.at[slot], peer)])
            if softmax:
                chips[-1].append(remote(stage_s.at[slot], arrive_s.at[slot], chip_send_s.at[slot], chip_recv_s.at[slot], peer))
            for copy in chips[-1]:
                copy.start()
    for slot in (1, 2, 0):
        for copy in chips[slot]:
            copy.wait_recv()
        for member in range(MB):
            new = arrive[slot, member].astype(F32)
            if softmax:
                left_s, right_s = stage_s[3, member], arrive_s[slot, member]
                top = jnp.maximum(left_s[0:1], right_s[0:1])
                left_w, right_w = jnp.exp2(left_s[0:1] - top), jnp.exp2(right_s[0:1] - top)
                total[member] = total[member] * left_w + new * right_w
                sums = left_s[1:2] * left_w + right_s[1:2] * right_w
                stage_s[3, member] = jnp.concatenate([top, sums, jnp.zeros((6, ROWS), F32)], axis=0)
            else:
                total[member] = total[member] + new
    for member in range(MB):
        if softmax:
            stats = stage_s[3, member]
            out_ref[member] = (total[member] / stats[1:2]).T
            lse = stats[0:1] + jnp.log2(stats[1:2])
            lse_ref[member] = jnp.concatenate([lse, jnp.zeros((7, ROWS), F32)], axis=0)
        else:
            out_ref[member] = total[member].T
    for group in cores + chips:
        for copy in group:
            copy.wait_send()


def gather_sum(softmax, collective_id, *parts):
    dma = pltpu.SemaphoreType.DMA
    data = [
        pltpu.VMEM((4, MB, D, ROWS), BF16),
        pltpu.VMEM((4, MB, D, ROWS), BF16),
        pltpu.VMEM((3, MB, D, ROWS), BF16),
        pltpu.VMEM((3, MB, D, ROWS), BF16),
        pltpu.VMEM((MB, D, ROWS), F32),
    ]
    sems = [dma((4,)), dma((4,)), dma((4,)), dma((3,)), dma((3,))]
    out_shape = [jax.ShapeDtypeStruct((MB, ROWS, D), F32)]
    scratch = data + sems
    if softmax:
        stats = [
            pltpu.VMEM((4, MB, 8, ROWS), F32),
            pltpu.VMEM((4, MB, 8, ROWS), F32),
            pltpu.VMEM((4, MB, 8, ROWS), F32),
            pltpu.VMEM((3, MB, 8, ROWS), F32),
        ]
        scratch = data + stats + sems + [dma((4,)), dma((4,)), dma((4,)), dma((3,)), dma((3,))]
        out_shape.append(jax.ShapeDtypeStruct((MB, 8, ROWS), F32))
    return pl.pallas_call(
        functools.partial(gather_sum_kernel, softmax),
        in_specs=[pl.BlockSpec(memory_space=pl.ANY)] * len(parts),
        out_specs=[pl.BlockSpec(memory_space=pltpu.VMEM)] * len(out_shape),
        out_shape=out_shape,
        scratch_shapes=scratch,
        compiler_params=pltpu.CompilerParams(
            collective_id=collective_id, has_side_effects=True, vmem_limit_bytes=48 * MIB
        ),
        name="weighted_sum" if softmax else "query_grad_sum",
    )(*parts)


def exchange_kernel(to_heads, src_ref, dst_ref, send_sem, recv_sem, local_sem):
    me, core, chip, mate, others = places()
    peers = []
    for other in others:
        peers += [2 * other + core, 2 * other + 1 - core]
    peers.append(mate)
    greet(peers)

    def ends(mine, device, member):
        rows_lane = pl.ds(member * ROWS, ROWS)
        if to_heads:
            source = src_ref.at[:, device, :, rows_lane]
            target = dst_ref.at[:, member, :, pl.ds(pl.multiple_of(mine * ROWS, ROWS), ROWS)]
        else:
            source = src_ref.at[:, member, :, pl.ds(pl.multiple_of(device * ROWS, ROWS), ROWS)]
            target = dst_ref.at[:, mine, :, rows_lane]
        return source, target

    copies = []
    for slot, peer in enumerate(peers):
        for member in range(MB):
            source, target = ends(me, peer, member)
            copies.append(remote(source, target, send_sem.at[slot, member], recv_sem.at[slot, member], peer))
            copies[-1].start()
    own = []
    for member in range(MB):
        source, target = ends(me, me, member)
        own.append(pltpu.make_async_copy(source, target, local_sem.at[member]))
        own[-1].start()
    for copy in own:
        copy.wait()
    for copy in copies:
        copy.wait()


def exchange(to_heads, collective_id, source):
    kinds = source.shape[0]
    shape = (kinds, MB, HD, L) if to_heads else (kinds, H, HD, MB * ROWS)
    dma = pltpu.SemaphoreType.DMA
    return pl.pallas_call(
        functools.partial(exchange_kernel, to_heads),
        in_specs=[pl.BlockSpec(memory_space=pl.ANY)],
        out_specs=pl.BlockSpec(memory_space=pl.ANY),
        out_shape=jax.ShapeDtypeStruct(shape, source.dtype),
        scratch_shapes=[dma((7, MB)), dma((7, MB)), dma((MB,))],
        compiler_params=pltpu.CompilerParams(collective_id=collective_id, has_side_effects=True),
        name="exchange",
    )(source)


def share_kernel(data_ref, stat_ref, all_ref, stats_ref, near_send, near_recv, far_send, far_recv, on_send, on_recv, local_sem):
    me, core, chip, mate, others = places()
    greet([mate] + [2 * other + core for other in others])
    pairs = ((data_ref, all_ref), (stat_ref, stats_ref))
    local, near, far, on = [], [], [], []
    for slot, other in enumerate(others):
        for kind, (source, target) in enumerate(pairs):
            far.append(remote(source, target.at[me], far_send.at[slot, kind], far_recv.at[slot, kind], 2 * other + core))
            far[-1].start()
    for kind, (source, target) in enumerate(pairs):
        near.append(remote(source, target.at[me], near_send.at[kind], near_recv.at[kind], mate))
        near[-1].start()
        local.append(pltpu.make_async_copy(source, target.at[me], local_sem.at[kind]))
        local[-1].start()
    for slot in (1, 2, 0):
        for kind, (source, target) in enumerate(pairs):
            far[2 * slot + kind].wait_recv()
            place = target.at[2 * others[slot] + core]
            on.append(remote(place, place, on_send.at[slot, kind], on_recv.at[slot, kind], mate))
            on[-1].start()
    for copy in local + near + on:
        copy.wait()
    for copy in far:
        copy.wait_send()


def share(collective_id, data, stats):
    dma = pltpu.SemaphoreType.DMA
    return pl.pallas_call(
        share_kernel,
        in_specs=[pl.BlockSpec(memory_space=pl.ANY)] * 2,
        out_specs=[pl.BlockSpec(memory_space=pl.ANY)] * 2,
        out_shape=[
            jax.ShapeDtypeStruct((TOK,) + data.shape, data.dtype),
            jax.ShapeDtypeStruct((TOK,) + stats.shape, stats.dtype),
        ],
        scratch_shapes=[dma((2,)), dma((2,)), dma((3, 2)), dma((3, 2)), dma((3, 2)), dma((3, 2)), dma((2,))],
        compiler_params=pltpu.CompilerParams(collective_id=collective_id, has_side_effects=True),
        name="share_grads",
    )(data, stats)


def mixer_attend_kernel(all_ref, q_ref, mixed_ref, exact_ref, lse_ref, keys, values):
    @pl.when(pl.program_id(1) == 0)
    def _():
        keys[...] = all_ref[1, 0].T
        values[0:HD] = all_ref[2, 0]
        values[HD:] = jnp.ones((16, L), BF16)

    logits = nn(keys[...], q_ref[0, 0])
    top = jnp.max(logits, axis=0, keepdims=True)
    raised = jnp.exp2(logits - top).astype(BF16)
    both = nn(values[...], raised)
    total = both[HD:HD + 1]
    mixed = both[0:HD] / total
    exact_ref[0] = mixed
    mixed_ref[0, 0] = mixed.astype(BF16)
    lse = top + jnp.log2(total)
    lse_ref[0] = jnp.concatenate([lse, jnp.zeros((7, lse.shape[1]), F32)], axis=0)


QB = 256


def mixer_attend(packed):
    return pl.pallas_call(
        mixer_attend_kernel,
        grid=(MB, L // QB),
        in_specs=[
            pl.BlockSpec((3, 1, HD, L), lambda b, i: (0, b, 0, 0)),
            pl.BlockSpec((1, 1, HD, QB), lambda b, i: (0, b, 0, i)),
        ],
        out_specs=[
            pl.BlockSpec((1, 1, HD, QB), lambda b, i: (0, b, 0, i)),
            pl.BlockSpec((1, HD, QB), lambda b, i: (b, 0, i)),
            pl.BlockSpec((1, 8, QB), lambda b, i: (b, 0, i)),
        ],
        out_shape=[
            jax.ShapeDtypeStruct((1, MB, HD, L), BF16),
            jax.ShapeDtypeStruct((MB, HD, L), F32),
            jax.ShapeDtypeStruct((MB, 8, L), F32),
        ],
        scratch_shapes=[pltpu.VMEM((L, HD), BF16), pltpu.VMEM((HD + 16, L), BF16)],
        compiler_params=pltpu.CompilerParams(
            dimension_semantics=("arbitrary", "arbitrary"), vmem_limit_bytes=48 * MIB
        ),
        cost_estimate=pl.CostEstimate(
            flops=9 * 10**9, bytes_accessed=4 * 10**6, transcendentals=8 * 10**6
        ),
        name="mixer_attend",
    )(packed, packed)


def mixer_attend_back_kernel(all_ref, q_ref, up_ref, exact_ref, lse_ref, out_ref, keys, values, key_acc, value_acc):
    step = pl.program_id(1)

    @pl.when(step == 0)
    def _():
        keys[...] = all_ref[1, 0].T
        values[...] = all_ref[2, 0].T
        key_acc[...] = jnp.zeros_like(key_acc)
        value_acc[...] = jnp.zeros_like(value_acc)

    queries = q_ref[0, 0]
    upstream = up_ref[0, 0]
    inner = jnp.sum(upstream.astype(F32) * exact_ref[0], axis=0, keepdims=True)
    softened = jnp.exp2(nn(keys[...], queries) - lse_ref[0][0:1])
    soft_grad = nn(values[...], upstream)
    logit_grad = (softened * (soft_grad - inner)).astype(BF16)
    value_acc[...] += nt(upstream, softened.astype(BF16))
    key_acc[...] += nt(queries, logit_grad)
    query_grad = nn(all_ref[1, 0], logit_grad) * HD ** (-0.5)
    out_ref[0, 0, :, pl.ds(pl.multiple_of(step * QB, QB), QB)] = query_grad.astype(BF16)

    @pl.when(step == L // QB - 1)
    def _():
        out_ref[1, 0] = (key_acc[...] * LN2).astype(BF16)
        out_ref[2, 0] = value_acc[...].astype(BF16)


def mixer_attend_back(packed, upstream, exact, lse):
    return pl.pallas_call(
        mixer_attend_back_kernel,
        grid=(MB, L // QB),
        in_specs=[
            pl.BlockSpec((3, 1, HD, L), lambda b, i: (0, b, 0, 0)),
            pl.BlockSpec((1, 1, HD, QB), lambda b, i: (0, b, 0, i)),
            pl.BlockSpec((1, 1, HD, QB), lambda b, i: (0, b, 0, i)),
            pl.BlockSpec((1, HD, QB), lambda b, i: (b, 0, i)),
            pl.BlockSpec((1, 8, QB), lambda b, i: (b, 0, i)),
        ],
        out_specs=pl.BlockSpec((3, 1, HD, L), lambda b, i: (0, b, 0, 0)),
        out_shape=jax.ShapeDtypeStruct((3, MB, HD, L), BF16),
        scratch_shapes=[
            pltpu.VMEM((L, HD), BF16),
            pltpu.VMEM((L, HD), BF16),
            pltpu.VMEM((HD, L), F32),
            pltpu.VMEM((HD, L), F32),
        ],
        compiler_params=pltpu.CompilerParams(
            dimension_semantics=("arbitrary", "arbitrary"), vmem_limit_bytes=48 * MIB
        ),
        cost_estimate=pl.CostEstimate(
            flops=22 * 10**9, bytes_accessed=5 * 10**6, transcendentals=8 * 10**6
        ),
        name="mixer_attend_back",
    )(packed, packed, upstream, exact, lse)


def cross_backward_kernel(
    tok_ref, tgain_ref, kw_ref, vw_ref, hot_ref, tab_ref, k_ref, v_ref, q_ref, up_ref, stat_ref,
    dq_ref, dtok_ref, dkw_ref, dvw_ref, dgain_ref, kt_ref, dk_ref, dv_ref,
):
    member, step = pl.program_id(0), pl.program_id(1)

    @pl.when(step == 0)
    def _():
        kt_ref[...] = k_ref[0].T
        dk_ref[...] = jnp.zeros_like(dk_ref)
        dv_ref[...] = jnp.zeros_like(dv_ref)

    queries = q_ref[0]
    upstream = up_ref[0, 0]
    stats = stat_ref[0, 0]
    scores = nt(k_ref[0], queries) + mask_bias(hot_ref[0], tab_ref[0, 0])
    weights = jnp.exp2(scores - stats[0:1])
    dv_ref[...] += nn(weights.astype(BF16), upstream)
    score_grad = (weights * (nt(v_ref[0], upstream) - stats[1:2])).astype(BF16)
    dk_ref[...] += nn(score_grad, queries)
    dq_ref[0, 0] = (nn(kt_ref[...], score_grad) * D ** (-0.5)).astype(BF16)

    @pl.when(step == LGROUPS - 1)
    def _():
        gain = tgain_ref[...]
        hat, inverse = norm_parts(tok_ref[0, 0].astype(F32))
        normed = (hat * gain).astype(BF16)
        key_grad = (dk_ref[...] * LN2).astype(BF16)
        value_grad = dv_ref[...].astype(BF16)
        key_term = tn(normed, key_grad)
        value_term = tn(normed, value_grad)
        normed_grad = nt(key_grad, kw_ref[...]) + nt(value_grad, vw_ref[...])
        source_grad, gain_rows = norm_pull(hat, inverse, gain, normed_grad)
        dtok_ref[0, 0] = source_grad
        gain_term = jnp.sum(gain_rows, axis=0, keepdims=True)

        @pl.when(member == 0)
        def _():
            dkw_ref[...] = key_term
            dvw_ref[...] = value_term
            dgain_ref[...] = gain_term

        @pl.when(member > 0)
        def _():
            dkw_ref[...] += key_term
            dvw_ref[...] += value_term
            dgain_ref[...] += gain_term


def cross_backward(tokens, token_gain, key_weight, value_weight, hot, table, keys, values, queries, upstream, stats):
    whole = lambda shape: pl.BlockSpec(shape, lambda b, g: (0,) * len(shape))
    return pl.pallas_call(
        cross_backward_kernel,
        grid=(MB, LGROUPS),
        in_specs=[
            pl.BlockSpec((1, 1, TOK_DEV, D), lambda b, g: (0, b, 0, 0)),
            whole((1, D)),
            whole((D, D)),
            whole((D, D)),
            pl.BlockSpec((1, TOK_DEV, 128), lambda b, g: (b, 0, 0)),
            pl.BlockSpec((1, 1, 128, 128), lambda b, g: (b, g, 0, 0)),
            pl.BlockSpec((1, TOK_DEV, D), lambda b, g: (b, 0, 0)),
            pl.BlockSpec((1, TOK_DEV, D), lambda b, g: (b, 0, 0)),
            pl.BlockSpec((1, GR, D), lambda b, g: (b, g, 0)),
            pl.BlockSpec((1, 1, GR, D), lambda b, g: (g, b, 0, 0)),
            pl.BlockSpec((1, 1, 8, GR), lambda b, g: (g, b, 0, 0)),
        ],
        out_specs=[
            pl.BlockSpec((1, 1, D, GR), lambda b, g: (g, b, 0, 0)),
            pl.BlockSpec((1, 1, TOK_DEV, D), lambda b, g: (0, b, 0, 0)),
            whole((D, D)),
            whole((D, D)),
            whole((1, D)),
        ],
        out_shape=[
            jax.ShapeDtypeStruct((LGROUPS, MB, D, GR), BF16),
            jax.ShapeDtypeStruct((1, MB, TOK_DEV, D), F32),
            jax.ShapeDtypeStruct((D, D), F32),
            jax.ShapeDtypeStruct((D, D), F32),
            jax.ShapeDtypeStruct((1, D), F32),
        ],
        scratch_shapes=[
            pltpu.VMEM((D, TOK_DEV), BF16),
            pltpu.VMEM((TOK_DEV, D), F32),
            pltpu.VMEM((TOK_DEV, D), F32),
        ],
        compiler_params=pltpu.CompilerParams(
            dimension_semantics=("arbitrary", "arbitrary"), vmem_limit_bytes=56 * MIB
        ),
        cost_estimate=pl.CostEstimate(
            flops=26 * 10**9, bytes_accessed=24 * 10**6, transcendentals=4 * 10**6
        ),
        name="cross_backward",
    )(tokens, token_gain, key_weight, value_weight, hot, table, keys, values, queries, upstream, stats)


def reduce_grads(columns, rows):
    part = lax.psum_scatter(columns.astype(BF16), "tok", scatter_dimension=0, tiled=True)
    other = lax.psum_scatter(rows.astype(BF16), "tok", scatter_dimension=0, tiled=True)
    return lax.psum((part, other), "grp")


def fast_body(
    tokens,
    latents,
    segments,
    scene_mask,
    counts,
    token_gain,
    query_gain,
    query_weight,
    key_weight,
    value_weight,
    output_weight,
    first_gain,
    first_up,
    first_down,
    mixer_gain,
    mixer_project,
    mixer_output,
    second_gain,
    second_up,
    second_down,
    cotangent,
):
    me = lax.axis_index("tok")
    lanes = jnp.arange(128)
    alive = jnp.arange(TOK_DEV)[None, :] < counts[0]
    hot = (segments[0][:, :, None] == lanes[None, None, :]) & alive[:, :, None]
    hot = hot.astype(BF16)
    table = jnp.pad(scene_mask[0].transpose(0, 2, 1), ((0, 0), (0, 0), (0, 128 - SCENES)))
    table = jnp.broadcast_to((table > 0)[..., None], (MB, LGROUPS, 128, 128)).astype(BF16)

    keys, values, queries, weighted, figures = cross_forward(
        tokens, latents, token_gain[None], query_gain[None], query_weight, key_weight, value_weight, hot, table
    )
    attended, lse = gather_sum(True, 0, weighted, figures)
    attended = attended.reshape(MB * ROWS, D)
    latent_in = lax.dynamic_slice_in_dim(latents[0], me * ROWS, ROWS, 1).reshape(MB * ROWS, D)

    attended_low = attended.astype(BF16)
    first_mid = latent_in + nn(attended_low, output_weight)
    mixer_mid, first_saved = mlp_forward(first_mid, first_gain, first_up, first_down)

    mixer_normed = norm_rows(mixer_mid, mixer_gain).astype(BF16)
    packed = lax.dot_general(
        mixer_project, mixer_normed, (((0,), (1,)), ((), ())), preferred_element_type=F32
    ).reshape(3, D, MB * ROWS)
    packed = packed * jnp.array([HD ** (-0.5) * LOG2E, 1.0, 1.0], F32)[:, None, None]
    packed = packed.astype(BF16).reshape(3, H, HD, MB * ROWS)
    head_packed = exchange(True, 1, packed)
    head_mixed, head_exact, head_lse = mixer_attend(head_packed)
    mixed = exchange(False, 2, head_mixed).reshape(D, MB * ROWS)
    second_mid = mixer_mid + tn(mixed, mixer_output)
    final_rows, second_saved = mlp_forward(second_mid, second_gain, second_up, second_down)

    upstream = cotangent.reshape(MB * ROWS, D)
    upstream, d_second_gain, d_second_up, d_second_down = mlp_backward(
        second_mid, second_gain, second_up, second_down, second_saved, upstream
    )
    grad_low = upstream.astype(BF16)
    d_mixer_output = nn(mixed, grad_low)
    mixed_grad = nt(mixer_output, grad_low).astype(BF16).reshape(1, H, HD, MB * ROWS)
    head_grad = mixer_attend_back(head_packed, exchange(True, 3, mixed_grad), head_exact, head_lse)
    packed_grad = exchange(False, 4, head_grad).reshape(3 * D, MB * ROWS)
    d_mixer_project = lax.dot_general(
        mixer_normed, packed_grad, (((0,), (1,)), ((), ())), preferred_element_type=F32
    )
    normed_grad = lax.dot_general(
        packed_grad, mixer_project, (((0,), (1,)), ((), ())), preferred_element_type=F32
    )
    residual_grad, d_mixer_gain = norm_back(mixer_mid, mixer_gain, normed_grad)
    upstream, d_first_gain, d_first_up, d_first_down = mlp_backward(
        first_mid, first_gain, first_up, first_down, first_saved, upstream + residual_grad
    )
    grad_low = upstream.astype(BF16)
    d_output = tn(attended_low, grad_low)
    attended_grad = nt(grad_low, output_weight).astype(BF16)
    inner = jnp.sum(attended_grad.astype(F32) * attended, axis=1).reshape(MB, ROWS)
    figures = jnp.concatenate(
        [lse[:, 0:1], inner[:, None], jnp.zeros((MB, 6, ROWS), F32)], axis=1
    )
    upstream_all, figures_all = share(5, attended_grad.reshape(MB, ROWS, D), figures)
    query_part, tokens_grad, d_key, d_value, d_token_gain = cross_backward(
        tokens, token_gain[None], key_weight, value_weight, hot, table, keys, values, queries,
        upstream_all, figures_all,
    )
    query_grad = gather_sum(False, 6, query_part)[0].reshape(MB * ROWS, D).astype(BF16)
    latent_normed = norm_rows(latent_in, query_gain).astype(BF16)
    d_query = tn(latent_normed, query_grad)
    latent_grad, d_query_gain = norm_back(latent_in, query_gain, nt(query_grad, query_weight))
    latent_grad = upstream + latent_grad

    columns, rows = reduce_grads(
        jnp.concatenate(
            [d_second_up, d_mixer_output, d_mixer_project, d_first_up, d_output, d_key, d_value, d_query,
             jnp.pad(jnp.stack([d_second_gain, d_mixer_gain, d_first_gain, d_token_gain[0], d_query_gain], axis=1), ((0, 0), (0, 123)))], axis=1
        ),
        jnp.concatenate([d_second_down, d_first_down], axis=1),
    )
    columns = columns.astype(F32)
    rows = rows.astype(F32)
    widths = [FF, D, 3 * D, FF, D, D, D, D, 128]
    cuts = [sum(widths[:i]) for i in range(len(widths) + 1)]
    (o_second_up, o_mixer_output, o_mixer_project, o_first_up, o_output, o_key, o_value, o_query, o_gains) = [
        columns[:, cuts[i]:cuts[i + 1]] for i in range(len(widths))
    ]
    return (
        final_rows.reshape(1, MB, ROWS, D),
        latent_grad.reshape(1, MB, ROWS, D),
        tokens_grad,
        o_gains[:, 3],
        o_gains[:, 4],
        o_query,
        o_key,
        o_value,
        o_output,
        o_gains[:, 2],
        o_first_up,
        rows[:, D:],
        o_gains[:, 1],
        o_mixer_project,
        o_mixer_output,
        o_gains[:, 0],
        o_second_up,
        rows[:, :D],
    )


IN_SPECS = (
    P("grp", None, "tok", None),
    P("grp", None, None, None),
    P("grp", None, "tok"),
    P("grp", None, None, None),
    P("grp", None, "tok"),
    P(),
    P(),
    P(),
    P(),
    P(),
    P(),
    P(),
    P(),
    P(),
    P(),
    P(),
    P(),
    P(),
    P(),
    P(),
    P("grp", None, "tok", None),
)
OUT_SPECS = (
    P("grp", None, "tok", None),
    P("grp", None, "tok", None),
    P("grp", None, "tok", None),
    P("tok"),
    P("tok"),
    P("tok", None),
    P("tok", None),
    P("tok", None),
    P("tok", None),
    P("tok"),
    P("tok", None),
    P("tok", None),
    P("tok"),
    P("tok", None),
    P("tok", None),
    P("tok"),
    P("tok", None),
    P("tok", None),
)


def solution(mesh):
    return jax.shard_map(
        fast_body if mesh.shape["tok"] == TOK else general_body,
        mesh=mesh,
        in_specs=IN_SPECS,
        out_specs=OUT_SPECS,
        check_vma=False,
    )
```

```python
import functools

import jax
import jax.numpy as jnp
from jax import lax
from jax.experimental import pallas as pl
from jax.experimental.pallas import tpu as pltpu
from jax.sharding import PartitionSpec as P

D = 512
L = 2048
H = 8
HD = 64
TOK_DEV = 1024
MB = 2
SCENES = 8
LGROUPS = 8


EPS = 1e-05
NEG = -1e30


def norm_rows(values, gain):
    centre = values - jnp.mean(values, axis=-1, keepdims=True)
    spread = jnp.mean(centre * centre, axis=-1, keepdims=True)
    return centre * lax.rsqrt(spread + EPS) * gain


def norm_back(values, gain, upstream):
    unused, pull = jax.vjp(norm_rows, values, gain)
    return pull(upstream)


def gelu_back(hidden, upstream):
    unused, pull = jax.vjp(jax.nn.gelu, hidden)
    return pull(upstream)[0]


def product_plain(left, right):
    return jnp.dot(left, right, preferred_element_type=jnp.float32)


def product_rows(left, right):
    return lax.dot_general(
        left, right, (((0,), (0,)), ((), ())), preferred_element_type=jnp.float32
    )


def product_cols(left, right):
    return lax.dot_general(
        left, right, (((1,), (1,)), ((), ())), preferred_element_type=jnp.float32
    )


def add_term(store, name, value):
    if name in store:
        store[name] = store[name] + value
    else:
        store[name] = value


def project_tokens(tokens, member, token_gain, key_weight, value_weight):
    source = tokens[0, member].astype(jnp.float32)
    normed = norm_rows(source, token_gain).astype(jnp.bfloat16)
    key_rows = product_plain(normed, key_weight).astype(jnp.bfloat16)
    value_rows = product_plain(normed, value_weight).astype(jnp.bfloat16)
    return (source, normed, key_rows, value_rows)


def mlp_forward(residual, gain, up_weight, down_weight):
    normed = norm_rows(residual, gain).astype(jnp.bfloat16)
    hidden = product_plain(normed, up_weight)
    active = jax.nn.gelu(hidden).astype(jnp.bfloat16)
    return (residual + product_plain(active, down_weight), (normed, hidden, active))


def mlp_backward(residual, gain, up_weight, down_weight, saved, upstream):
    normed, hidden, active = saved
    grad_low = upstream.astype(jnp.bfloat16)
    grad_down = product_rows(active, grad_low)
    hidden_grad = gelu_back(hidden, product_cols(grad_low, down_weight)).astype(jnp.bfloat16)
    grad_up = product_rows(normed, hidden_grad)
    residual_grad, grad_gain = norm_back(residual, gain, product_cols(hidden_grad, up_weight))
    return (upstream + residual_grad, grad_gain, grad_up, grad_down)


def mixer_forward(residual, gain, project, output):
    own_rows = residual.shape[0]
    normed = norm_rows(residual, gain).astype(jnp.bfloat16)
    packed = product_plain(normed, project).astype(jnp.bfloat16)
    pair_rows = lax.all_gather(packed[:, D:], "tok", axis=0, tiled=True)
    every = pair_rows.shape[0]
    own_queries = packed[:, :D].reshape(own_rows, H, HD)
    keys = pair_rows[:, :D].reshape(every, H, HD)
    values = pair_rows[:, D:].reshape(every, H, HD)
    logits = jnp.einsum(
        "qhd,khd->hqk", own_queries, keys, preferred_element_type=jnp.float32
    ) * HD ** (-0.5)
    peak_row = jnp.max(logits, axis=-1, keepdims=True)
    raised = jnp.exp(logits - peak_row)
    softened = raised / jnp.sum(raised, axis=-1, keepdims=True)
    softened_low = softened.astype(jnp.bfloat16)
    mixed_rows = jnp.einsum(
        "hqk,khd->qhd", softened_low, values, preferred_element_type=jnp.float32
    )
    mixed_rows = mixed_rows.reshape(own_rows, D).astype(jnp.bfloat16)
    return (
        residual + product_plain(mixed_rows, output),
        (normed, own_queries, keys, values, softened, softened_low, mixed_rows),
    )


def mixer_backward(residual, gain, project, output, saved, upstream):
    normed, own_queries, keys, values, softened, softened_low, mixed_rows = saved
    own_rows = upstream.shape[0]
    every = keys.shape[0]
    grad_low = upstream.astype(jnp.bfloat16)
    grad_output = product_rows(mixed_rows, grad_low)
    mixed_grad = product_cols(grad_low, output).astype(jnp.bfloat16).reshape(own_rows, H, HD)
    value_grad = jnp.einsum(
        "hqk,qhd->khd", softened_low, mixed_grad, preferred_element_type=jnp.float32
    )
    soft_grad = jnp.einsum("qhd,khd->hqk", mixed_grad, values, preferred_element_type=jnp.float32)
    logit_grad = softened * (soft_grad - jnp.sum(soft_grad * softened, axis=-1, keepdims=True))
    logit_grad = logit_grad.astype(jnp.bfloat16)
    query_grad = jnp.einsum(
        "hqk,khd->qhd", logit_grad, keys, preferred_element_type=jnp.float32
    ) * HD ** (-0.5)
    key_grad = jnp.einsum(
        "hqk,qhd->khd", logit_grad, own_queries, preferred_element_type=jnp.float32
    ) * HD ** (-0.5)
    pair_terms = jnp.concatenate([key_grad.reshape(every, D), value_grad.reshape(every, D)], axis=1)
    pair_grad = lax.psum_scatter(
        pair_terms.astype(jnp.bfloat16), "tok", scatter_dimension=0, tiled=True
    ).astype(jnp.float32)
    packed_grad = jnp.concatenate([query_grad.reshape(own_rows, D), pair_grad], axis=1).astype(
        jnp.bfloat16
    )
    grad_project = product_rows(normed, packed_grad)
    residual_grad, grad_gain = norm_back(residual, gain, product_cols(packed_grad, project))
    return (upstream + residual_grad, grad_gain, grad_project, grad_output)


def general_body(
    tokens,
    latents,
    segments,
    scene_mask,
    counts,
    token_gain,
    query_gain,
    query_weight,
    key_weight,
    value_weight,
    output_weight,
    first_gain,
    first_up,
    first_down,
    mixer_gain,
    mixer_project,
    mixer_output,
    second_gain,
    second_up,
    second_down,
    cotangent,
):
    scale = D ** (-0.5)
    shards = lax.axis_size("tok")
    own_rows = L // shards
    row_start = lax.axis_index("tok") * own_rows
    latent_group = jnp.arange(L) // (L // LGROUPS)
    latent_onehot = (latent_group[:, None] == jnp.arange(LGROUPS)[None, :]).astype(jnp.float32)
    token_place = jnp.arange(TOK_DEV)
    records = []
    latent_outs = []
    for member in range(MB):
        record = {}
        source, normed, key_rows, value_rows = project_tokens(
            tokens, member, token_gain, key_weight, value_weight
        )
        record["token_side"] = (source, normed, key_rows, value_rows)
        scene_onehot = (segments[0, member][:, None] == jnp.arange(SCENES)[None, :]).astype(
            jnp.float32
        )
        token_seen = jnp.dot(scene_onehot, scene_mask[0, member].astype(jnp.float32))
        visible = product_cols(latent_onehot, token_seen)
        alive = token_place < counts[0, member, 0]
        allowed = (visible > 0.5) & alive[None, :]
        latent_every = latents[0, member]
        normed_every = norm_rows(latent_every, query_gain).astype(jnp.bfloat16)
        queries = product_plain(normed_every, query_weight).astype(jnp.bfloat16)
        scores = jnp.where(allowed, product_cols(queries, key_rows) * scale, NEG)
        row_top = lax.pmax(jnp.max(scores, axis=1), "tok")
        unnormed = jnp.exp(scores - row_top[:, None])
        row_total, weighted = (
            lax.psum_scatter(
                jnp.sum(unnormed, axis=1).astype(jnp.bfloat16),
                "tok",
                scatter_dimension=0,
                tiled=True,
            ).astype(jnp.float32),
            lax.psum_scatter(
                product_plain(unnormed.astype(jnp.bfloat16), value_rows).astype(jnp.bfloat16),
                "tok",
                scatter_dimension=0,
                tiled=True,
            ).astype(jnp.float32),
        )
        latent_in = lax.dynamic_slice_in_dim(latent_every, row_start, own_rows, 0)
        latent_normed = lax.dynamic_slice_in_dim(normed_every, row_start, own_rows, 0)
        attended = weighted / row_total[:, None]
        attended_low = attended.astype(jnp.bfloat16)
        first_mid = latent_in + product_plain(attended_low, output_weight)
        mixer_mid, first_saved = mlp_forward(first_mid, first_gain, first_up, first_down)
        second_mid, mixer_saved = mixer_forward(mixer_mid, mixer_gain, mixer_project, mixer_output)
        final_rows, second_saved = mlp_forward(second_mid, second_gain, second_up, second_down)
        latent_outs.append(final_rows)
        record["latent_side"] = (
            allowed,
            latent_in,
            latent_normed,
            queries,
            row_top,
            row_total,
            attended,
            attended_low,
            first_mid,
            mixer_mid,
            second_mid,
            first_saved,
            mixer_saved,
            second_saved,
        )
        records.append(record)
    grads = {}
    latent_grads = []
    token_grads = []
    for member in range(MB):
        record = records[member]
        source, normed, key_rows, value_rows = record["token_side"]
        (
            allowed,
            latent_in,
            latent_normed,
            queries,
            row_top,
            row_total,
            attended,
            attended_low,
            first_mid,
            mixer_mid,
            second_mid,
            first_saved,
            mixer_saved,
            second_saved,
        ) = record["latent_side"]
        second_back = mlp_backward(
            second_mid, second_gain, second_up, second_down, second_saved, cotangent[0, member]
        )
        add_term(grads, "second_gain", second_back[1])
        add_term(grads, "second_up", second_back[2])
        add_term(grads, "second_down", second_back[3])
        mixer_back = mixer_backward(
            mixer_mid, mixer_gain, mixer_project, mixer_output, mixer_saved, second_back[0]
        )
        add_term(grads, "mixer_gain", mixer_back[1])
        add_term(grads, "mixer_project", mixer_back[2])
        add_term(grads, "mixer_output", mixer_back[3])
        first_back = mlp_backward(
            first_mid, first_gain, first_up, first_down, first_saved, mixer_back[0]
        )
        add_term(grads, "first_gain", first_back[1])
        add_term(grads, "first_up", first_back[2])
        add_term(grads, "first_down", first_back[3])
        latent_upstream = first_back[0]
        grad_low = latent_upstream.astype(jnp.bfloat16)
        add_term(grads, "output_weight", product_rows(attended_low, grad_low))
        attended_grad = lax.optimization_barrier(
            product_cols(grad_low, output_weight).astype(jnp.bfloat16)
        ).astype(jnp.float32)
        weighted_grad = (attended_grad / row_total[:, None]).astype(jnp.bfloat16)
        total_grad = -jnp.sum(attended_grad * attended, axis=1) / row_total
        weighted_every, total_every = (
            lax.all_gather(
                weighted_grad.astype(jnp.float32).astype(jnp.bfloat16), "tok", axis=0, tiled=True
            ).astype(jnp.float32),
            lax.all_gather(total_grad.astype(jnp.bfloat16), "tok", axis=0, tiled=True).astype(
                total_grad.dtype
            ),
        )
        weighted_every = weighted_every.astype(jnp.bfloat16)
        scores = jnp.where(allowed, product_cols(queries, key_rows) * scale, NEG)
        unnormed = jnp.exp(scores - row_top[:, None])
        unnormed_grad = product_cols(weighted_every, value_rows) + total_every[:, None]
        score_grad = (unnormed * unnormed_grad).astype(jnp.bfloat16)
        value_grad = product_rows(unnormed.astype(jnp.bfloat16), weighted_every).astype(
            jnp.bfloat16
        )
        key_grad = (product_rows(score_grad, queries) * scale).astype(jnp.bfloat16)
        query_grad = lax.psum_scatter(
            (product_plain(score_grad, key_rows) * scale).astype(jnp.bfloat16),
            "tok",
            scatter_dimension=0,
            tiled=True,
        )
        add_term(grads, "key_weight", product_rows(normed, key_grad))
        add_term(grads, "value_weight", product_rows(normed, value_grad))
        normed_grad = product_cols(key_grad, key_weight) + product_cols(value_grad, value_weight)
        source_grad, gain_grad = norm_back(source, token_gain, normed_grad)
        add_term(grads, "token_gain", gain_grad)
        token_grads.append(source_grad)
        add_term(grads, "query_weight", product_rows(latent_normed, query_grad))
        latent_grad, gain_grad = norm_back(
            latent_in, query_gain, product_cols(query_grad, query_weight)
        )
        add_term(grads, "query_gain", gain_grad)
        latent_grads.append(latent_upstream + latent_grad)
    parts = (
        lax.psum_scatter(
            grads["token_gain"].astype(jnp.bfloat16), "tok", scatter_dimension=0, tiled=True
        ).astype(jnp.float32),
        lax.psum_scatter(
            grads["query_gain"].astype(jnp.bfloat16), "tok", scatter_dimension=0, tiled=True
        ).astype(jnp.float32),
        lax.psum_scatter(
            grads["query_weight"].astype(jnp.bfloat16), "tok", scatter_dimension=0, tiled=True
        ).astype(jnp.float32),
        lax.psum_scatter(
            grads["key_weight"].astype(jnp.bfloat16), "tok", scatter_dimension=0, tiled=True
        ).astype(jnp.float32),
        lax.psum_scatter(
            grads["value_weight"].astype(jnp.bfloat16), "tok", scatter_dimension=0, tiled=True
        ).astype(jnp.float32),
        lax.psum_scatter(
            grads["output_weight"].astype(jnp.bfloat16), "tok", scatter_dimension=0, tiled=True
        ).astype(jnp.float32),
        lax.psum_scatter(
            grads["first_gain"].astype(jnp.bfloat16), "tok", scatter_dimension=0, tiled=True
        ).astype(jnp.float32),
        lax.psum_scatter(
            grads["first_up"].astype(jnp.bfloat16), "tok", scatter_dimension=0, tiled=True
        ).astype(jnp.float32),
        lax.psum_scatter(
            grads["first_down"].astype(jnp.bfloat16), "tok", scatter_dimension=0, tiled=True
        ).astype(jnp.float32),
        lax.psum_scatter(
            grads["mixer_gain"].astype(jnp.bfloat16), "tok", scatter_dimension=0, tiled=True
        ).astype(jnp.float32),
        lax.psum_scatter(
            grads["mixer_project"].astype(jnp.bfloat16), "tok", scatter_dimension=0, tiled=True
        ).astype(jnp.float32),
        lax.psum_scatter(
            grads["mixer_output"].astype(jnp.bfloat16), "tok", scatter_dimension=0, tiled=True
        ).astype(jnp.float32),
        lax.psum_scatter(
            grads["second_gain"].astype(jnp.bfloat16), "tok", scatter_dimension=0, tiled=True
        ).astype(jnp.float32),
        lax.psum_scatter(
            grads["second_up"].astype(jnp.bfloat16), "tok", scatter_dimension=0, tiled=True
        ).astype(jnp.float32),
        lax.psum_scatter(
            grads["second_down"].astype(jnp.bfloat16), "tok", scatter_dimension=0, tiled=True
        ).astype(jnp.float32),
    )
    summed = (
        lax.psum(parts[0].astype(jnp.bfloat16), "grp").astype(jnp.float32),
        lax.psum(parts[1].astype(jnp.bfloat16), "grp").astype(jnp.float32),
        lax.psum(parts[2].astype(jnp.bfloat16), "grp").astype(jnp.float32),
        lax.psum(parts[3].astype(jnp.bfloat16), "grp").astype(jnp.float32),
        lax.psum(parts[4].astype(jnp.bfloat16), "grp").astype(jnp.float32),
        lax.psum(parts[5].astype(jnp.bfloat16), "grp").astype(jnp.float32),
        lax.psum(parts[6].astype(jnp.bfloat16), "grp").astype(jnp.float32),
        lax.psum(parts[7].astype(jnp.bfloat16), "grp").astype(jnp.float32),
        lax.psum(parts[8].astype(jnp.bfloat16), "grp").astype(jnp.float32),
        lax.psum(parts[9].astype(jnp.bfloat16), "grp").astype(jnp.float32),
        lax.psum(parts[10].astype(jnp.bfloat16), "grp").astype(jnp.float32),
        lax.psum(parts[11].astype(jnp.bfloat16), "grp").astype(jnp.float32),
        lax.psum(parts[12].astype(jnp.bfloat16), "grp").astype(jnp.float32),
        lax.psum(parts[13].astype(jnp.bfloat16), "grp").astype(jnp.float32),
        lax.psum(parts[14].astype(jnp.bfloat16), "grp").astype(jnp.float32),
    )
    return (
        jnp.stack(latent_outs)[None],
        jnp.stack(latent_grads)[None],
        jnp.stack(token_grads)[None],
    ) + tuple(summed)


TOK = 8
ROWS = L // TOK
FF = 2048
GR = L // LGROUPS
LOG2E = 1.4426950408889634
LN2 = 0.6931471805599453
F32 = jnp.float32
BF16 = jnp.bfloat16
MIB = 1024 * 1024


def nn(left, right):
    return lax.dot_general(left, right, (((1,), (0,)), ((), ())), preferred_element_type=F32)


def nt(left, right):
    return lax.dot_general(left, right, (((1,), (1,)), ((), ())), preferred_element_type=F32)


def tn(left, right):
    return lax.dot_general(left, right, (((0,), (0,)), ((), ())), preferred_element_type=F32)


def norm_parts(values):
    centre = values - jnp.mean(values, axis=-1, keepdims=True)
    inverse = lax.rsqrt(jnp.mean(centre * centre, axis=-1, keepdims=True) + EPS)
    return centre * inverse, inverse


def norm_pull(hat, inverse, gain, upstream):
    scaled = upstream * gain
    inner = jnp.mean(scaled * hat, axis=-1, keepdims=True)
    grad = (scaled - jnp.mean(scaled, axis=-1, keepdims=True) - hat * inner) * inverse
    return grad, upstream * hat


def places():
    me = lax.axis_index("tok")
    core = lax.rem(me, 2)
    chip = lax.div(me, 2)
    mate = me + 1 - 2 * core
    flip_x = chip + 1 - 2 * lax.rem(chip, 2)
    flip_y = lax.rem(chip + 2, 4)
    far = 3 - chip
    return me, core, chip, mate, (far, flip_x, flip_y)


def remote(src, dst, send_sem, recv_sem, peer):
    return pltpu.make_async_remote_copy(
        src_ref=src,
        dst_ref=dst,
        send_sem=send_sem,
        recv_sem=recv_sem,
        device_id={"tok": peer},
        device_id_type=pl.DeviceIdType.MESH,
    )


def greet(devices):
    barrier = pltpu.get_barrier_semaphore()
    for device in devices:
        pl.semaphore_signal(
            barrier, inc=1, device_id={"tok": device}, device_id_type=pl.DeviceIdType.MESH
        )
    pl.semaphore_wait(barrier, len(devices))


def mask_bias(hot, table):
    seen = nn(hot, table)
    bias = (seen - 1.0) * 1e30
    return jnp.concatenate([bias, bias], axis=1)


def cross_forward_kernel(
    tok_ref, lat_ref, tgain_ref, qgain_ref, qw_ref, kw_ref, vw_ref, hot_ref, tab_ref,
    k_ref, v_ref, q_ref, acc_ref, ml_ref, vt_ref,
):
    @pl.when(pl.program_id(1) == 0)
    def _():
        hat, inverse = norm_parts(tok_ref[0, 0].astype(F32))
        normed = (hat * tgain_ref[...]).astype(BF16)
        k_ref[0] = nn(normed, kw_ref[...]).astype(BF16)
        values = nn(normed, vw_ref[...]).astype(BF16)
        v_ref[0] = values
        vt_ref[...] = values.T

    hat, inverse = norm_parts(lat_ref[0, 0])
    normed = (hat * qgain_ref[...]).astype(BF16)
    queries = (nn(normed, qw_ref[...]) * (D ** (-0.5) * LOG2E)).astype(BF16)
    q_ref[0] = queries
    scores = nt(k_ref[0], queries) + mask_bias(hot_ref[0], tab_ref[0, 0])
    top = jnp.max(scores, axis=0, keepdims=True)
    raised = jnp.exp2(scores - top)
    total = jnp.sum(raised, axis=0, keepdims=True)
    acc_ref[0, 0] = nn(vt_ref[...], raised.astype(BF16)).astype(BF16)
    ml_ref[0, 0] = jnp.concatenate([top, total, jnp.zeros((6, GR), F32)], axis=0)


def cross_forward(tokens, latents, token_gain, query_gain, query_weight, key_weight, value_weight, hot, table):
    whole = lambda shape: pl.BlockSpec(shape, lambda b, g: (0,) * len(shape))
    return pl.pallas_call(
        cross_forward_kernel,
        grid=(MB, LGROUPS),
        in_specs=[
            pl.BlockSpec((1, 1, TOK_DEV, D), lambda b, g: (0, b, 0, 0)),
            pl.BlockSpec((1, 1, GR, D), lambda b, g: (0, b, g, 0)),
            whole((1, D)),
            whole((1, D)),
            whole((D, D)),
            whole((D, D)),
            whole((D, D)),
            pl.BlockSpec((1, TOK_DEV, 128), lambda b, g: (b, 0, 0)),
            pl.BlockSpec((1, 1, 128, 128), lambda b, g: (b, g, 0, 0)),
        ],
        out_specs=[
            pl.BlockSpec((1, TOK_DEV, D), lambda b, g: (b, 0, 0)),
            pl.BlockSpec((1, TOK_DEV, D), lambda b, g: (b, 0, 0)),
            pl.BlockSpec((1, GR, D), lambda b, g: (b, g, 0)),
            pl.BlockSpec((1, 1, D, GR), lambda b, g: (g, b, 0, 0)),
            pl.BlockSpec((1, 1, 8, GR), lambda b, g: (g, b, 0, 0)),
        ],
        out_shape=[
            jax.ShapeDtypeStruct((MB, TOK_DEV, D), BF16),
            jax.ShapeDtypeStruct((MB, TOK_DEV, D), BF16),
            jax.ShapeDtypeStruct((MB, L, D), BF16),
            jax.ShapeDtypeStruct((LGROUPS, MB, D, GR), BF16),
            jax.ShapeDtypeStruct((LGROUPS, MB, 8, GR), F32),
        ],
        scratch_shapes=[pltpu.VMEM((D, TOK_DEV), BF16)],
        compiler_params=pltpu.CompilerParams(
            dimension_semantics=("arbitrary", "arbitrary"), vmem_limit_bytes=48 * MIB
        ),
        cost_estimate=pl.CostEstimate(
            flops=14 * 10**9, bytes_accessed=22 * 10**6, transcendentals=4 * 10**6
        ),
        name="cross_forward",
    )(tokens, latents, token_gain, query_gain, query_weight, key_weight, value_weight, hot, table)


def gather_sum_kernel(
    softmax, *refs
):
    if softmax:
        (part_ref, stat_ref, out_ref, lse_ref, mine, got, stage, arrive, total,
         mine_s, got_s, stage_s, arrive_s, local_sem, core_send, core_recv, chip_send, chip_recv,
         local_sem_s, core_send_s, core_recv_s, chip_send_s, chip_recv_s) = refs
    else:
        (part_ref, out_ref, mine, got, stage, arrive, total,
         local_sem, core_send, core_recv, chip_send, chip_recv) = refs
    me, core, chip, mate, others = places()
    targets = others + (chip,)
    greet([mate] + [2 * other + core for other in others])
    locals_, cores = [], []
    for slot, target in enumerate(targets):
        own_block = 2 * target + core
        mate_block = 2 * target + 1 - core
        cores.append([remote(part_ref.at[mate_block], got.at[slot], core_send.at[slot], core_recv.at[slot], mate)])
        locals_.append([pltpu.make_async_copy(part_ref.at[own_block], mine.at[slot], local_sem.at[slot])])
        if softmax:
            cores[-1].append(remote(stat_ref.at[mate_block], got_s.at[slot], core_send_s.at[slot], core_recv_s.at[slot], mate))
            locals_[-1].append(pltpu.make_async_copy(stat_ref.at[own_block], mine_s.at[slot], local_sem_s.at[slot]))
        for copy in cores[-1] + locals_[-1]:
            copy.start()
    chips = []
    for slot, target in enumerate(targets):
        for copy in locals_[slot]:
            copy.wait()
        for copy in cores[slot]:
            copy.wait_recv()
        for member in range(MB):
            left = mine[slot, member].astype(F32)
            right = got[slot, member].astype(F32)
            if softmax:
                left_s, right_s = mine_s[slot, member], got_s[slot, member]
                top = jnp.maximum(left_s[0:1], right_s[0:1])
                left_w, right_w = jnp.exp2(left_s[0:1] - top), jnp.exp2(right_s[0:1] - top)
                added = left * left_w + right * right_w
                sums = left_s[1:2] * left_w + right_s[1:2] * right_w
                stage_s[slot, member] = jnp.concatenate([top, sums, jnp.zeros((6, ROWS), F32)], axis=0)
            else:
                added = left + right
            if slot == 3:
                total[member] = added
            else:
                stage[slot, member] = added.astype(BF16)
        if slot < 3:
            peer = 2 * target + core
            chips.append([remote(stage.at[slot], arrive.at[slot], chip_send.at[slot], chip_recv.at[slot], peer)])
            if softmax:
                chips[-1].append(remote(stage_s.at[slot], arrive_s.at[slot], chip_send_s.at[slot], chip_recv_s.at[slot], peer))
            for copy in chips[-1]:
                copy.start()
    for slot in (1, 2, 0):
        for copy in chips[slot]:
            copy.wait_recv()
        for member in range(MB):
            new = arrive[slot, member].astype(F32)
            if softmax:
                left_s, right_s = stage_s[3, member], arrive_s[slot, member]
                top = jnp.maximum(left_s[0:1], right_s[0:1])
                left_w, right_w = jnp.exp2(left_s[0:1] - top), jnp.exp2(right_s[0:1] - top)
                total[member] = total[member] * left_w + new * right_w
                sums = left_s[1:2] * left_w + right_s[1:2] * right_w
                stage_s[3, member] = jnp.concatenate([top, sums, jnp.zeros((6, ROWS), F32)], axis=0)
            else:
                total[member] = total[member] + new
    for member in range(MB):
        if softmax:
            stats = stage_s[3, member]
            out_ref[member] = (total[member] / stats[1:2]).T
            lse = stats[0:1] + jnp.log2(stats[1:2])
            lse_ref[member] = jnp.concatenate([lse, jnp.zeros((7, ROWS), F32)], axis=0)
        else:
            out_ref[member] = total[member].T
    for group in cores + chips:
        for copy in group:
            copy.wait_send()


def gather_sum(softmax, collective_id, *parts):
    dma = pltpu.SemaphoreType.DMA
    data = [
        pltpu.VMEM((4, MB, D, ROWS), BF16),
        pltpu.VMEM((4, MB, D, ROWS), BF16),
        pltpu.VMEM((3, MB, D, ROWS), BF16),
        pltpu.VMEM((3, MB, D, ROWS), BF16),
        pltpu.VMEM((MB, D, ROWS), F32),
    ]
    sems = [dma((4,)), dma((4,)), dma((4,)), dma((3,)), dma((3,))]
    out_shape = [jax.ShapeDtypeStruct((MB, ROWS, D), F32)]
    scratch = data + sems
    if softmax:
        stats = [
            pltpu.VMEM((4, MB, 8, ROWS), F32),
            pltpu.VMEM((4, MB, 8, ROWS), F32),
            pltpu.VMEM((4, MB, 8, ROWS), F32),
            pltpu.VMEM((3, MB, 8, ROWS), F32),
        ]
        scratch = data + stats + sems + [dma((4,)), dma((4,)), dma((4,)), dma((3,)), dma((3,))]
        out_shape.append(jax.ShapeDtypeStruct((MB, 8, ROWS), F32))
    return pl.pallas_call(
        functools.partial(gather_sum_kernel, softmax),
        in_specs=[pl.BlockSpec(memory_space=pl.ANY)] * len(parts),
        out_specs=[pl.BlockSpec(memory_space=pltpu.VMEM)] * len(out_shape),
        out_shape=out_shape,
        scratch_shapes=scratch,
        compiler_params=pltpu.CompilerParams(
            collective_id=collective_id, has_side_effects=True, vmem_limit_bytes=48 * MIB
        ),
        name="weighted_sum" if softmax else "query_grad_sum",
    )(*parts)


def exchange_kernel(to_heads, src_ref, dst_ref, send_sem, recv_sem, local_sem):
    me, core, chip, mate, others = places()
    peers = []
    for other in others:
        peers += [2 * other + core, 2 * other + 1 - core]
    peers.append(mate)
    greet(peers)

    def ends(mine, device, member):
        rows_lane = pl.ds(member * ROWS, ROWS)
        if to_heads:
            source = src_ref.at[:, device, :, rows_lane]
            target = dst_ref.at[:, member, :, pl.ds(pl.multiple_of(mine * ROWS, ROWS), ROWS)]
        else:
            source = src_ref.at[:, member, :, pl.ds(pl.multiple_of(device * ROWS, ROWS), ROWS)]
            target = dst_ref.at[:, mine, :, rows_lane]
        return source, target

    copies = []
    for slot, peer in enumerate(peers):
        for member in range(MB):
            source, target = ends(me, peer, member)
            copies.append(remote(source, target, send_sem.at[slot, member], recv_sem.at[slot, member], peer))
            copies[-1].start()
    own = []
    for member in range(MB):
        source, target = ends(me, me, member)
        own.append(pltpu.make_async_copy(source, target, local_sem.at[member]))
        own[-1].start()
    for copy in own:
        copy.wait()
    for copy in copies:
        copy.wait()


def exchange(to_heads, collective_id, source):
    kinds = source.shape[0]
    shape = (kinds, MB, HD, L) if to_heads else (kinds, H, HD, MB * ROWS)
    dma = pltpu.SemaphoreType.DMA
    return pl.pallas_call(
        functools.partial(exchange_kernel, to_heads),
        in_specs=[pl.BlockSpec(memory_space=pl.ANY)],
        out_specs=pl.BlockSpec(memory_space=pl.ANY),
        out_shape=jax.ShapeDtypeStruct(shape, source.dtype),
        scratch_shapes=[dma((7, MB)), dma((7, MB)), dma((MB,))],
        compiler_params=pltpu.CompilerParams(collective_id=collective_id, has_side_effects=True),
        name="exchange",
    )(source)


def share_kernel(data_ref, stat_ref, all_ref, stats_ref, near_send, near_recv, far_send, far_recv, on_send, on_recv, local_sem):
    me, core, chip, mate, others = places()
    greet([mate] + [2 * other + core for other in others])
    pairs = ((data_ref, all_ref), (stat_ref, stats_ref))
    local, near, far, on = [], [], [], []
    for slot, other in enumerate(others):
        for kind, (source, target) in enumerate(pairs):
            far.append(remote(source, target.at[me], far_send.at[slot, kind], far_recv.at[slot, kind], 2 * other + core))
            far[-1].start()
    for kind, (source, target) in enumerate(pairs):
        near.append(remote(source, target.at[me], near_send.at[kind], near_recv.at[kind], mate))
        near[-1].start()
        local.append(pltpu.make_async_copy(source, target.at[me], local_sem.at[kind]))
        local[-1].start()
    for slot in (1, 2, 0):
        for kind, (source, target) in enumerate(pairs):
            far[2 * slot + kind].wait_recv()
            place = target.at[2 * others[slot] + core]
            on.append(remote(place, place, on_send.at[slot, kind], on_recv.at[slot, kind], mate))
            on[-1].start()
    for copy in local + near + on:
        copy.wait()
    for copy in far:
        copy.wait_send()


def share(collective_id, data, stats):
    dma = pltpu.SemaphoreType.DMA
    return pl.pallas_call(
        share_kernel,
        in_specs=[pl.BlockSpec(memory_space=pl.ANY)] * 2,
        out_specs=[pl.BlockSpec(memory_space=pl.ANY)] * 2,
        out_shape=[
            jax.ShapeDtypeStruct((TOK,) + data.shape, data.dtype),
            jax.ShapeDtypeStruct((TOK,) + stats.shape, stats.dtype),
        ],
        scratch_shapes=[dma((2,)), dma((2,)), dma((3, 2)), dma((3, 2)), dma((3, 2)), dma((3, 2)), dma((2,))],
        compiler_params=pltpu.CompilerParams(collective_id=collective_id, has_side_effects=True),
        name="share_grads",
    )(data, stats)


def mixer_attend_kernel(all_ref, q_ref, mixed_ref, exact_ref, lse_ref, keys, values):
    @pl.when(pl.program_id(1) == 0)
    def _():
        keys[...] = all_ref[1, 0].T
        values[0:HD] = all_ref[2, 0]
        values[HD:] = jnp.ones((16, L), BF16)

    logits = nn(keys[...], q_ref[0, 0])
    top = jnp.max(logits, axis=0, keepdims=True)
    raised = jnp.exp2(logits - top).astype(BF16)
    both = nn(values[...], raised)
    total = both[HD:HD + 1]
    mixed = both[0:HD] / total
    exact_ref[0] = mixed
    mixed_ref[0, 0] = mixed.astype(BF16)
    lse = top + jnp.log2(total)
    lse_ref[0] = jnp.concatenate([lse, jnp.zeros((7, lse.shape[1]), F32)], axis=0)


QB = 256


def mixer_attend(packed):
    return pl.pallas_call(
        mixer_attend_kernel,
        grid=(MB, L // QB),
        in_specs=[
            pl.BlockSpec((3, 1, HD, L), lambda b, i: (0, b, 0, 0)),
            pl.BlockSpec((1, 1, HD, QB), lambda b, i: (0, b, 0, i)),
        ],
        out_specs=[
            pl.BlockSpec((1, 1, HD, QB), lambda b, i: (0, b, 0, i)),
            pl.BlockSpec((1, HD, QB), lambda b, i: (b, 0, i)),
            pl.BlockSpec((1, 8, QB), lambda b, i: (b, 0, i)),
        ],
        out_shape=[
            jax.ShapeDtypeStruct((1, MB, HD, L), BF16),
            jax.ShapeDtypeStruct((MB, HD, L), F32),
            jax.ShapeDtypeStruct((MB, 8, L), F32),
        ],
        scratch_shapes=[pltpu.VMEM((L, HD), BF16), pltpu.VMEM((HD + 16, L), BF16)],
        compiler_params=pltpu.CompilerParams(
            dimension_semantics=("arbitrary", "arbitrary"), vmem_limit_bytes=48 * MIB
        ),
        cost_estimate=pl.CostEstimate(
            flops=9 * 10**9, bytes_accessed=4 * 10**6, transcendentals=8 * 10**6
        ),
        name="mixer_attend",
    )(packed, packed)


def mixer_attend_back_kernel(all_ref, q_ref, up_ref, exact_ref, lse_ref, out_ref, keys, values, key_acc, value_acc):
    step = pl.program_id(1)

    @pl.when(step == 0)
    def _():
        keys[...] = all_ref[1, 0].T
        values[...] = all_ref[2, 0].T
        key_acc[...] = jnp.zeros_like(key_acc)
        value_acc[...] = jnp.zeros_like(value_acc)

    queries = q_ref[0, 0]
    upstream = up_ref[0, 0]
    inner = jnp.sum(upstream.astype(F32) * exact_ref[0], axis=0, keepdims=True)
    softened = jnp.exp2(nn(keys[...], queries) - lse_ref[0][0:1])
    soft_grad = nn(values[...], upstream)
    logit_grad = (softened * (soft_grad - inner)).astype(BF16)
    value_acc[...] += nt(upstream, softened.astype(BF16))
    key_acc[...] += nt(queries, logit_grad)
    query_grad = nn(all_ref[1, 0], logit_grad) * HD ** (-0.5)
    out_ref[0, 0, :, pl.ds(pl.multiple_of(step * QB, QB), QB)] = query_grad.astype(BF16)

    @pl.when(step == L // QB - 1)
    def _():
        out_ref[1, 0] = (key_acc[...] * LN2).astype(BF16)
        out_ref[2, 0] = value_acc[...].astype(BF16)


def mixer_attend_back(packed, upstream, exact, lse):
    return pl.pallas_call(
        mixer_attend_back_kernel,
        grid=(MB, L // QB),
        in_specs=[
            pl.BlockSpec((3, 1, HD, L), lambda b, i: (0, b, 0, 0)),
            pl.BlockSpec((1, 1, HD, QB), lambda b, i: (0, b, 0, i)),
            pl.BlockSpec((1, 1, HD, QB), lambda b, i: (0, b, 0, i)),
            pl.BlockSpec((1, HD, QB), lambda b, i: (b, 0, i)),
            pl.BlockSpec((1, 8, QB), lambda b, i: (b, 0, i)),
        ],
        out_specs=pl.BlockSpec((3, 1, HD, L), lambda b, i: (0, b, 0, 0)),
        out_shape=jax.ShapeDtypeStruct((3, MB, HD, L), BF16),
        scratch_shapes=[
            pltpu.VMEM((L, HD), BF16),
            pltpu.VMEM((L, HD), BF16),
            pltpu.VMEM((HD, L), F32),
            pltpu.VMEM((HD, L), F32),
        ],
        compiler_params=pltpu.CompilerParams(
            dimension_semantics=("arbitrary", "arbitrary"), vmem_limit_bytes=48 * MIB
        ),
        cost_estimate=pl.CostEstimate(
            flops=22 * 10**9, bytes_accessed=5 * 10**6, transcendentals=8 * 10**6
        ),
        name="mixer_attend_back",
    )(packed, packed, upstream, exact, lse)


def cross_backward_kernel(
    tok_ref, tgain_ref, kw_ref, vw_ref, hot_ref, tab_ref, k_ref, v_ref, q_ref, up_ref, stat_ref,
    dq_ref, dtok_ref, dkw_ref, dvw_ref, dgain_ref, kt_ref, dk_ref, dv_ref,
):
    member, step = pl.program_id(0), pl.program_id(1)

    @pl.when(step == 0)
    def _():
        kt_ref[...] = k_ref[0].T
        dk_ref[...] = jnp.zeros_like(dk_ref)
        dv_ref[...] = jnp.zeros_like(dv_ref)

    queries = q_ref[0]
    upstream = up_ref[0, 0]
    stats = stat_ref[0, 0]
    scores = nt(k_ref[0], queries) + mask_bias(hot_ref[0], tab_ref[0, 0])
    weights = jnp.exp2(scores - stats[0:1])
    dv_ref[...] += nn(weights.astype(BF16), upstream)
    score_grad = (weights * (nt(v_ref[0], upstream) - stats[1:2])).astype(BF16)
    dk_ref[...] += nn(score_grad, queries)
    dq_ref[0, 0] = (nn(kt_ref[...], score_grad) * D ** (-0.5)).astype(BF16)

    @pl.when(step == LGROUPS - 1)
    def _():
        gain = tgain_ref[...]
        hat, inverse = norm_parts(tok_ref[0, 0].astype(F32))
        normed = (hat * gain).astype(BF16)
        key_grad = (dk_ref[...] * LN2).astype(BF16)
        value_grad = dv_ref[...].astype(BF16)
        key_term = tn(normed, key_grad)
        value_term = tn(normed, value_grad)
        normed_grad = nt(key_grad, kw_ref[...]) + nt(value_grad, vw_ref[...])
        source_grad, gain_rows = norm_pull(hat, inverse, gain, normed_grad)
        dtok_ref[0, 0] = source_grad
        gain_term = jnp.sum(gain_rows, axis=0, keepdims=True)

        @pl.when(member == 0)
        def _():
            dkw_ref[...] = key_term
            dvw_ref[...] = value_term
            dgain_ref[...] = gain_term

        @pl.when(member > 0)
        def _():
            dkw_ref[...] += key_term
            dvw_ref[...] += value_term
            dgain_ref[...] += gain_term


def cross_backward(tokens, token_gain, key_weight, value_weight, hot, table, keys, values, queries, upstream, stats):
    whole = lambda shape: pl.BlockSpec(shape, lambda b, g: (0,) * len(shape))
    return pl.pallas_call(
        cross_backward_kernel,
        grid=(MB, LGROUPS),
        in_specs=[
            pl.BlockSpec((1, 1, TOK_DEV, D), lambda b, g: (0, b, 0, 0)),
            whole((1, D)),
            whole((D, D)),
            whole((D, D)),
            pl.BlockSpec((1, TOK_DEV, 128), lambda b, g: (b, 0, 0)),
            pl.BlockSpec((1, 1, 128, 128), lambda b, g: (b, g, 0, 0)),
            pl.BlockSpec((1, TOK_DEV, D), lambda b, g: (b, 0, 0)),
            pl.BlockSpec((1, TOK_DEV, D), lambda b, g: (b, 0, 0)),
            pl.BlockSpec((1, GR, D), lambda b, g: (b, g, 0)),
            pl.BlockSpec((1, 1, GR, D), lambda b, g: (g, b, 0, 0)),
            pl.BlockSpec((1, 1, 8, GR), lambda b, g: (g, b, 0, 0)),
        ],
        out_specs=[
            pl.BlockSpec((1, 1, D, GR), lambda b, g: (g, b, 0, 0)),
            pl.BlockSpec((1, 1, TOK_DEV, D), lambda b, g: (0, b, 0, 0)),
            whole((D, D)),
            whole((D, D)),
            whole((1, D)),
        ],
        out_shape=[
            jax.ShapeDtypeStruct((LGROUPS, MB, D, GR), BF16),
            jax.ShapeDtypeStruct((1, MB, TOK_DEV, D), F32),
            jax.ShapeDtypeStruct((D, D), F32),
            jax.ShapeDtypeStruct((D, D), F32),
            jax.ShapeDtypeStruct((1, D), F32),
        ],
        scratch_shapes=[
            pltpu.VMEM((D, TOK_DEV), BF16),
            pltpu.VMEM((TOK_DEV, D), F32),
            pltpu.VMEM((TOK_DEV, D), F32),
        ],
        compiler_params=pltpu.CompilerParams(
            dimension_semantics=("arbitrary", "arbitrary"), vmem_limit_bytes=56 * MIB
        ),
        cost_estimate=pl.CostEstimate(
            flops=26 * 10**9, bytes_accessed=24 * 10**6, transcendentals=4 * 10**6
        ),
        name="cross_backward",
    )(tokens, token_gain, key_weight, value_weight, hot, table, keys, values, queries, upstream, stats)


def reduce_kernel(items, *refs):
    n = len(items)
    sources, outs, scratch = refs[:n], refs[n:2 * n], refs[2 * n:]
    mine, got, first_in, second_in, z_keep, z_first, z_second = [scratch[i * n:(i + 1) * n] for i in range(7)]
    (local_sem, core_send, core_recv, one_send, one_recv, two_send, two_recv, z_send, z_recv) = scratch[7 * n:]
    me, core, chip, mate, (far, flip_x, flip_y) = places()
    targets = (chip, flip_x, flip_y, far)
    level = lax.axis_index("grp")
    odd = lax.rem(level, 2)
    level_near = level + 1 - 2 * odd
    level_far = lax.rem(level + 2, 4)
    barrier = pltpu.get_barrier_semaphore()
    for device in (mate, 2 * flip_x + core, 2 * flip_y + core):
        pl.semaphore_signal(barrier, inc=1, device_id={"tok": device}, device_id_type=pl.DeviceIdType.MESH)
    for other in (level_near, level_far):
        pl.semaphore_signal(barrier, inc=1, device_id={"grp": other}, device_id_type=pl.DeviceIdType.MESH)
    pl.semaphore_wait(barrier, 5)

    def along(item, src, dst, step, other):
        return pltpu.make_async_remote_copy(
            src_ref=src, dst_ref=dst, send_sem=z_send.at[item, step], recv_sem=z_recv.at[item, step],
            device_id={"grp": other}, device_id_type=pl.DeviceIdType.MESH,
        )

    sent, cores, ones, twos, zs = [], {}, {}, {}, {}
    for i, (rows, columns, kind, x_first) in enumerate(items):
        cores[i] = []
        for slot in (3, 2, 1, 0):
            own_rows = pl.ds(pl.multiple_of((2 * targets[slot] + core) * rows, rows), rows)
            mate_rows = pl.ds(pl.multiple_of((2 * targets[slot] + 1 - core) * rows, rows), rows)
            there = remote(sources[i].at[mate_rows], got[i].at[slot], core_send.at[i, slot], core_recv.at[i, slot], mate)
            here = pltpu.make_async_copy(sources[i].at[own_rows], mine[i].at[slot], local_sem.at[i, slot])
            there.start()
            here.start()
            cores[i].append((slot, there, here))
            sent.append(there)

    def add(target, one, two, kind):
        target[...] = (one[...].astype(F32) + two[...].astype(F32)).astype(kind)

    def core_sums(i):
        rows, columns, kind, x_first = items[i]
        for slot, there, here in cores[i]:
            there.wait_recv()
            here.wait()
            add(mine[i].at[slot], mine[i].at[slot], got[i].at[slot], kind)
        near = 1 if x_first else 2
        peer = 2 * targets[near] + core
        ones[i] = []
        for place, slot in ((1, 3), (0, near)):
            copy = remote(mine[i].at[slot], first_in[i].at[place], one_send.at[i, place], one_recv.at[i, place], peer)
            copy.start()
            ones[i].append((place, copy))
            sent.append(copy)

    def first_sums(i):
        rows, columns, kind, x_first = items[i]
        other = 2 if x_first else 1
        for place, copy in ones[i]:
            copy.wait_recv()
            slot = other if place == 1 else 0
            add(mine[i].at[slot], mine[i].at[slot], first_in[i].at[place], kind)
            if place == 1:
                twos[i] = remote(mine[i].at[slot], second_in[i], two_send.at[i], two_recv.at[i], 2 * targets[other] + core)
                twos[i].start()
                sent.append(twos[i])

    def second_sums(i):
        rows, columns, kind, x_first = items[i]
        half = rows // 2
        twos[i].wait_recv()
        add(mine[i].at[0], mine[i].at[0], second_in[i], kind)
        away = pl.ds(pl.multiple_of((1 - odd) * half, half), half)
        zs[i, 0] = along(i, mine[i].at[0, away], z_first[i], 0, level_near)
        zs[i, 0].start()
        sent.append(zs[i, 0])

    def grp_first(i):
        rows, columns, kind, x_first = items[i]
        half = rows // 2
        keep = pl.ds(pl.multiple_of(odd * half, half), half)
        zs[i, 0].wait_recv()
        add(z_keep[i].at[0], mine[i].at[0, keep], z_first[i], kind)
        zs[i, 1] = along(i, z_keep[i].at[0], z_second[i].at[0], 1, level_far)
        zs[i, 1].start()
        sent.append(zs[i, 1])

    def grp_second(i):
        rows, columns, kind, x_first = items[i]
        half = rows // 2
        keep = pl.ds(pl.multiple_of(odd * half, half), half)
        zs[i, 1].wait_recv()
        add(z_keep[i].at[1], z_keep[i].at[0], z_second[i].at[0], kind)
        zs[i, 2] = along(i, z_keep[i].at[1], z_second[i].at[1], 2, level_near)
        zs[i, 2].start()
        sent.append(zs[i, 2])
        outs[i][keep] = z_keep[i][1].astype(F32)

    def grp_third(i):
        rows, columns, kind, x_first = items[i]
        half = rows // 2
        away = pl.ds(pl.multiple_of((1 - odd) * half, half), half)
        zs[i, 2].wait_recv()
        outs[i][away] = z_second[i][1].astype(F32)

    stages = (core_sums, first_sums, second_sums, grp_first, grp_second, grp_third)
    lags = (0, 2, 3, 4, 5, 6)
    for step in range(n + lags[-1]):
        for stage, lag in zip(stages, lags):
            if 0 <= step - lag < n:
                stage(step - lag)
    for copy in sent:
        copy.wait_send()


def reduce_grads(collective_id, arrays, x_firsts):
    items = tuple(
        (array.shape[0] // TOK, array.shape[1], array.dtype, x_first) for array, x_first in zip(arrays, x_firsts)
    )
    n = len(items)
    dma = pltpu.SemaphoreType.DMA
    blocks = lambda count, part: [
        pltpu.VMEM(((count,) if count else ()) + (rows // part, columns), kind) for rows, columns, kind, unused in items
    ]
    return pl.pallas_call(
        functools.partial(reduce_kernel, items),
        in_specs=[pl.BlockSpec(memory_space=pl.ANY)] * n,
        out_specs=[pl.BlockSpec(memory_space=pltpu.VMEM)] * n,
        out_shape=[jax.ShapeDtypeStruct((rows, columns), F32) for rows, columns, kind, unused in items],
        scratch_shapes=blocks(4, 1) + blocks(4, 1) + blocks(2, 1) + blocks(0, 1) + blocks(2, 2) + blocks(0, 2) + blocks(2, 2)
        + [dma((n, 4)), dma((n, 4)), dma((n, 4)), dma((n, 2)), dma((n, 2)), dma((n,)), dma((n,)), dma((n, 3)), dma((n, 3))],
        compiler_params=pltpu.CompilerParams(
            collective_id=collective_id, has_side_effects=True, vmem_limit_bytes=56 * MIB
        ),
        name="reduce_grads",
    )(*arrays)


def fast_body(
    tokens,
    latents,
    segments,
    scene_mask,
    counts,
    token_gain,
    query_gain,
    query_weight,
    key_weight,
    value_weight,
    output_weight,
    first_gain,
    first_up,
    first_down,
    mixer_gain,
    mixer_project,
    mixer_output,
    second_gain,
    second_up,
    second_down,
    cotangent,
):
    me = lax.axis_index("tok")
    lanes = jnp.arange(128)
    alive = jnp.arange(TOK_DEV)[None, :] < counts[0]
    hot = (segments[0][:, :, None] == lanes[None, None, :]) & alive[:, :, None]
    hot = hot.astype(BF16)
    table = jnp.pad(scene_mask[0].transpose(0, 2, 1), ((0, 0), (0, 0), (0, 128 - SCENES)))
    table = jnp.broadcast_to((table > 0)[..., None], (MB, LGROUPS, 128, 128)).astype(BF16)

    keys, values, queries, weighted, figures = cross_forward(
        tokens, latents, token_gain[None], query_gain[None], query_weight, key_weight, value_weight, hot, table
    )
    attended, lse = gather_sum(True, 0, weighted, figures)
    attended = attended.reshape(MB * ROWS, D)
    latent_in = lax.dynamic_slice_in_dim(latents[0], me * ROWS, ROWS, 1).reshape(MB * ROWS, D)

    attended_low = attended.astype(BF16)
    first_mid = latent_in + nn(attended_low, output_weight)
    mixer_mid, first_saved = mlp_forward(first_mid, first_gain, first_up, first_down)

    mixer_normed = norm_rows(mixer_mid, mixer_gain).astype(BF16)
    packed = lax.dot_general(
        mixer_project, mixer_normed, (((0,), (1,)), ((), ())), preferred_element_type=F32
    ).reshape(3, D, MB * ROWS)
    packed = packed * jnp.array([HD ** (-0.5) * LOG2E, 1.0, 1.0], F32)[:, None, None]
    packed = packed.astype(BF16).reshape(3, H, HD, MB * ROWS)
    head_packed = exchange(True, 1, packed)
    head_mixed, head_exact, head_lse = mixer_attend(head_packed)
    mixed = exchange(False, 2, head_mixed).reshape(D, MB * ROWS)
    second_mid = mixer_mid + tn(mixed, mixer_output)
    final_rows, second_saved = mlp_forward(second_mid, second_gain, second_up, second_down)

    upstream = cotangent.reshape(MB * ROWS, D)
    upstream, d_second_gain, d_second_up, d_second_down = mlp_backward(
        second_mid, second_gain, second_up, second_down, second_saved, upstream
    )
    grad_low = upstream.astype(BF16)
    d_mixer_output = nn(mixed, grad_low)
    mixed_grad = nt(mixer_output, grad_low).astype(BF16).reshape(1, H, HD, MB * ROWS)
    head_grad = mixer_attend_back(head_packed, exchange(True, 3, mixed_grad), head_exact, head_lse)
    packed_grad = exchange(False, 4, head_grad).reshape(3 * D, MB * ROWS)
    d_mixer_project = lax.dot_general(
        mixer_normed, packed_grad, (((0,), (1,)), ((), ())), preferred_element_type=F32
    )
    normed_grad = lax.dot_general(
        packed_grad, mixer_project, (((0,), (1,)), ((), ())), preferred_element_type=F32
    )
    residual_grad, d_mixer_gain = norm_back(mixer_mid, mixer_gain, normed_grad)
    upstream, d_first_gain, d_first_up, d_first_down = mlp_backward(
        first_mid, first_gain, first_up, first_down, first_saved, upstream + residual_grad
    )
    grad_low = upstream.astype(BF16)
    d_output = tn(attended_low, grad_low)
    attended_grad = nt(grad_low, output_weight).astype(BF16)
    inner = jnp.sum(attended_grad.astype(F32) * attended, axis=1).reshape(MB, ROWS)
    figures = jnp.concatenate(
        [lse[:, 0:1], inner[:, None], jnp.zeros((MB, 6, ROWS), F32)], axis=1
    )
    upstream_all, figures_all = share(5, attended_grad.reshape(MB, ROWS, D), figures)
    query_part, tokens_grad, d_key, d_value, d_token_gain = cross_backward(
        tokens, token_gain[None], key_weight, value_weight, hot, table, keys, values, queries,
        upstream_all, figures_all,
    )
    query_grad = gather_sum(False, 6, query_part)[0].reshape(MB * ROWS, D).astype(BF16)
    latent_normed = norm_rows(latent_in, query_gain).astype(BF16)
    d_query = tn(latent_normed, query_grad)
    latent_grad, d_query_gain = norm_back(latent_in, query_gain, nt(query_grad, query_weight))
    latent_grad = upstream + latent_grad

    small = jnp.concatenate(
        [d.astype(BF16) for d in (d_mixer_output, d_output, d_key, d_value, d_query)], axis=1
    )
    gains = jnp.stack([d_token_gain[0], d_query_gain, d_first_gain, d_mixer_gain, d_second_gain])
    gains = jnp.pad(
        gains.reshape(5, TOK, D // TOK).transpose(1, 0, 2), ((0, 0), (0, 11), (0, 128 - D // TOK))
    ).reshape(TOK * 16, 128)
    o_second_down, o_second_up, o_first_down, o_first_up, o_project, o_small, o_gains = reduce_grads(
        7,
        [d_second_down.astype(BF16), d_second_up.astype(BF16), d_first_down.astype(BF16),
         d_first_up.astype(BF16), d_mixer_project.astype(BF16), small, gains],
        (False, True, False, True, True, False, False),
    )
    o_mixer_output, o_output, o_key, o_value, o_query = [o_small[:, i * D:(i + 1) * D] for i in range(5)]
    o_gains = o_gains[:, :D // TOK]
    return (
        final_rows.reshape(1, MB, ROWS, D),
        latent_grad.reshape(1, MB, ROWS, D),
        tokens_grad,
        o_gains[0],
        o_gains[1],
        o_query,
        o_key,
        o_value,
        o_output,
        o_gains[2],
        o_first_up,
        o_first_down,
        o_gains[3],
        o_project,
        o_mixer_output,
        o_gains[4],
        o_second_up,
        o_second_down,
    )


IN_SPECS = (
    P("grp", None, "tok", None),
    P("grp", None, None, None),
    P("grp", None, "tok"),
    P("grp", None, None, None),
    P("grp", None, "tok"),
    P(),
    P(),
    P(),
    P(),
    P(),
    P(),
    P(),
    P(),
    P(),
    P(),
    P(),
    P(),
    P(),
    P(),
    P(),
    P("grp", None, "tok", None),
)
OUT_SPECS = (
    P("grp", None, "tok", None),
    P("grp", None, "tok", None),
    P("grp", None, "tok", None),
    P("tok"),
    P("tok"),
    P("tok", None),
    P("tok", None),
    P("tok", None),
    P("tok", None),
    P("tok"),
    P("tok", None),
    P("tok", None),
    P("tok"),
    P("tok", None),
    P("tok", None),
    P("tok"),
    P("tok", None),
    P("tok", None),
)


def solution(mesh):
    return jax.shard_map(
        fast_body if mesh.shape["tok"] == TOK else general_body,
        mesh=mesh,
        in_specs=IN_SPECS,
        out_specs=OUT_SPECS,
        check_vma=False,
    )
```

```python
import functools

import jax
import jax.numpy as jnp
from jax import lax
from jax.experimental import pallas as pl
from jax.experimental.pallas import tpu as pltpu
from jax.sharding import PartitionSpec as P

D = 512
L = 2048
H = 8
HD = 64
TOK_DEV = 1024
MB = 2
SCENES = 8
LGROUPS = 8


EPS = 1e-05
NEG = -1e30


def norm_rows(values, gain):
    centre = values - jnp.mean(values, axis=-1, keepdims=True)
    spread = jnp.mean(centre * centre, axis=-1, keepdims=True)
    return centre * lax.rsqrt(spread + EPS) * gain


def norm_back(values, gain, upstream):
    unused, pull = jax.vjp(norm_rows, values, gain)
    return pull(upstream)


def gelu_back(hidden, upstream):
    unused, pull = jax.vjp(jax.nn.gelu, hidden)
    return pull(upstream)[0]


def product_plain(left, right):
    return jnp.dot(left, right, preferred_element_type=jnp.float32)


def product_rows(left, right):
    return lax.dot_general(
        left, right, (((0,), (0,)), ((), ())), preferred_element_type=jnp.float32
    )


def product_cols(left, right):
    return lax.dot_general(
        left, right, (((1,), (1,)), ((), ())), preferred_element_type=jnp.float32
    )


def add_term(store, name, value):
    if name in store:
        store[name] = store[name] + value
    else:
        store[name] = value


def project_tokens(tokens, member, token_gain, key_weight, value_weight):
    source = tokens[0, member].astype(jnp.float32)
    normed = norm_rows(source, token_gain).astype(jnp.bfloat16)
    key_rows = product_plain(normed, key_weight).astype(jnp.bfloat16)
    value_rows = product_plain(normed, value_weight).astype(jnp.bfloat16)
    return (source, normed, key_rows, value_rows)


def mlp_forward(residual, gain, up_weight, down_weight):
    normed = norm_rows(residual, gain).astype(jnp.bfloat16)
    hidden = product_plain(normed, up_weight)
    active = jax.nn.gelu(hidden).astype(jnp.bfloat16)
    return (residual + product_plain(active, down_weight), (normed, hidden, active))


def mlp_backward(residual, gain, up_weight, down_weight, saved, upstream):
    normed, hidden, active = saved
    grad_low = upstream.astype(jnp.bfloat16)
    grad_down = product_rows(active, grad_low)
    hidden_grad = gelu_back(hidden, product_cols(grad_low, down_weight)).astype(jnp.bfloat16)
    grad_up = product_rows(normed, hidden_grad)
    residual_grad, grad_gain = norm_back(residual, gain, product_cols(hidden_grad, up_weight))
    return (upstream + residual_grad, grad_gain, grad_up, grad_down)


def mixer_forward(residual, gain, project, output):
    own_rows = residual.shape[0]
    normed = norm_rows(residual, gain).astype(jnp.bfloat16)
    packed = product_plain(normed, project).astype(jnp.bfloat16)
    pair_rows = lax.all_gather(packed[:, D:], "tok", axis=0, tiled=True)
    every = pair_rows.shape[0]
    own_queries = packed[:, :D].reshape(own_rows, H, HD)
    keys = pair_rows[:, :D].reshape(every, H, HD)
    values = pair_rows[:, D:].reshape(every, H, HD)
    logits = jnp.einsum(
        "qhd,khd->hqk", own_queries, keys, preferred_element_type=jnp.float32
    ) * HD ** (-0.5)
    peak_row = jnp.max(logits, axis=-1, keepdims=True)
    raised = jnp.exp(logits - peak_row)
    softened = raised / jnp.sum(raised, axis=-1, keepdims=True)
    softened_low = softened.astype(jnp.bfloat16)
    mixed_rows = jnp.einsum(
        "hqk,khd->qhd", softened_low, values, preferred_element_type=jnp.float32
    )
    mixed_rows = mixed_rows.reshape(own_rows, D).astype(jnp.bfloat16)
    return (
        residual + product_plain(mixed_rows, output),
        (normed, own_queries, keys, values, softened, softened_low, mixed_rows),
    )


def mixer_backward(residual, gain, project, output, saved, upstream):
    normed, own_queries, keys, values, softened, softened_low, mixed_rows = saved
    own_rows = upstream.shape[0]
    every = keys.shape[0]
    grad_low = upstream.astype(jnp.bfloat16)
    grad_output = product_rows(mixed_rows, grad_low)
    mixed_grad = product_cols(grad_low, output).astype(jnp.bfloat16).reshape(own_rows, H, HD)
    value_grad = jnp.einsum(
        "hqk,qhd->khd", softened_low, mixed_grad, preferred_element_type=jnp.float32
    )
    soft_grad = jnp.einsum("qhd,khd->hqk", mixed_grad, values, preferred_element_type=jnp.float32)
    logit_grad = softened * (soft_grad - jnp.sum(soft_grad * softened, axis=-1, keepdims=True))
    logit_grad = logit_grad.astype(jnp.bfloat16)
    query_grad = jnp.einsum(
        "hqk,khd->qhd", logit_grad, keys, preferred_element_type=jnp.float32
    ) * HD ** (-0.5)
    key_grad = jnp.einsum(
        "hqk,qhd->khd", logit_grad, own_queries, preferred_element_type=jnp.float32
    ) * HD ** (-0.5)
    pair_terms = jnp.concatenate([key_grad.reshape(every, D), value_grad.reshape(every, D)], axis=1)
    pair_grad = lax.psum_scatter(
        pair_terms.astype(jnp.bfloat16), "tok", scatter_dimension=0, tiled=True
    ).astype(jnp.float32)
    packed_grad = jnp.concatenate([query_grad.reshape(own_rows, D), pair_grad], axis=1).astype(
        jnp.bfloat16
    )
    grad_project = product_rows(normed, packed_grad)
    residual_grad, grad_gain = norm_back(residual, gain, product_cols(packed_grad, project))
    return (upstream + residual_grad, grad_gain, grad_project, grad_output)


def general_body(
    tokens,
    latents,
    segments,
    scene_mask,
    counts,
    token_gain,
    query_gain,
    query_weight,
    key_weight,
    value_weight,
    output_weight,
    first_gain,
    first_up,
    first_down,
    mixer_gain,
    mixer_project,
    mixer_output,
    second_gain,
    second_up,
    second_down,
    cotangent,
):
    scale = D ** (-0.5)
    shards = lax.axis_size("tok")
    own_rows = L // shards
    row_start = lax.axis_index("tok") * own_rows
    latent_group = jnp.arange(L) // (L // LGROUPS)
    latent_onehot = (latent_group[:, None] == jnp.arange(LGROUPS)[None, :]).astype(jnp.float32)
    token_place = jnp.arange(TOK_DEV)
    records = []
    latent_outs = []
    for member in range(MB):
        record = {}
        source, normed, key_rows, value_rows = project_tokens(
            tokens, member, token_gain, key_weight, value_weight
        )
        record["token_side"] = (source, normed, key_rows, value_rows)
        scene_onehot = (segments[0, member][:, None] == jnp.arange(SCENES)[None, :]).astype(
            jnp.float32
        )
        token_seen = jnp.dot(scene_onehot, scene_mask[0, member].astype(jnp.float32))
        visible = product_cols(latent_onehot, token_seen)
        alive = token_place < counts[0, member, 0]
        allowed = (visible > 0.5) & alive[None, :]
        latent_every = latents[0, member]
        normed_every = norm_rows(latent_every, query_gain).astype(jnp.bfloat16)
        queries = product_plain(normed_every, query_weight).astype(jnp.bfloat16)
        scores = jnp.where(allowed, product_cols(queries, key_rows) * scale, NEG)
        row_top = lax.pmax(jnp.max(scores, axis=1), "tok")
        unnormed = jnp.exp(scores - row_top[:, None])
        row_total, weighted = (
            lax.psum_scatter(
                jnp.sum(unnormed, axis=1).astype(jnp.bfloat16),
                "tok",
                scatter_dimension=0,
                tiled=True,
            ).astype(jnp.float32),
            lax.psum_scatter(
                product_plain(unnormed.astype(jnp.bfloat16), value_rows).astype(jnp.bfloat16),
                "tok",
                scatter_dimension=0,
                tiled=True,
            ).astype(jnp.float32),
        )
        latent_in = lax.dynamic_slice_in_dim(latent_every, row_start, own_rows, 0)
        latent_normed = lax.dynamic_slice_in_dim(normed_every, row_start, own_rows, 0)
        attended = weighted / row_total[:, None]
        attended_low = attended.astype(jnp.bfloat16)
        first_mid = latent_in + product_plain(attended_low, output_weight)
        mixer_mid, first_saved = mlp_forward(first_mid, first_gain, first_up, first_down)
        second_mid, mixer_saved = mixer_forward(mixer_mid, mixer_gain, mixer_project, mixer_output)
        final_rows, second_saved = mlp_forward(second_mid, second_gain, second_up, second_down)
        latent_outs.append(final_rows)
        record["latent_side"] = (
            allowed,
            latent_in,
            latent_normed,
            queries,
            row_top,
            row_total,
            attended,
            attended_low,
            first_mid,
            mixer_mid,
            second_mid,
            first_saved,
            mixer_saved,
            second_saved,
        )
        records.append(record)
    grads = {}
    latent_grads = []
    token_grads = []
    for member in range(MB):
        record = records[member]
        source, normed, key_rows, value_rows = record["token_side"]
        (
            allowed,
            latent_in,
            latent_normed,
            queries,
            row_top,
            row_total,
            attended,
            attended_low,
            first_mid,
            mixer_mid,
            second_mid,
            first_saved,
            mixer_saved,
            second_saved,
        ) = record["latent_side"]
        second_back = mlp_backward(
            second_mid, second_gain, second_up, second_down, second_saved, cotangent[0, member]
        )
        add_term(grads, "second_gain", second_back[1])
        add_term(grads, "second_up", second_back[2])
        add_term(grads, "second_down", second_back[3])
        mixer_back = mixer_backward(
            mixer_mid, mixer_gain, mixer_project, mixer_output, mixer_saved, second_back[0]
        )
        add_term(grads, "mixer_gain", mixer_back[1])
        add_term(grads, "mixer_project", mixer_back[2])
        add_term(grads, "mixer_output", mixer_back[3])
        first_back = mlp_backward(
            first_mid, first_gain, first_up, first_down, first_saved, mixer_back[0]
        )
        add_term(grads, "first_gain", first_back[1])
        add_term(grads, "first_up", first_back[2])
        add_term(grads, "first_down", first_back[3])
        latent_upstream = first_back[0]
        grad_low = latent_upstream.astype(jnp.bfloat16)
        add_term(grads, "output_weight", product_rows(attended_low, grad_low))
        attended_grad = lax.optimization_barrier(
            product_cols(grad_low, output_weight).astype(jnp.bfloat16)
        ).astype(jnp.float32)
        weighted_grad = (attended_grad / row_total[:, None]).astype(jnp.bfloat16)
        total_grad = -jnp.sum(attended_grad * attended, axis=1) / row_total
        weighted_every, total_every = (
            lax.all_gather(
                weighted_grad.astype(jnp.float32).astype(jnp.bfloat16), "tok", axis=0, tiled=True
            ).astype(jnp.float32),
            lax.all_gather(total_grad.astype(jnp.bfloat16), "tok", axis=0, tiled=True).astype(
                total_grad.dtype
            ),
        )
        weighted_every = weighted_every.astype(jnp.bfloat16)
        scores = jnp.where(allowed, product_cols(queries, key_rows) * scale, NEG)
        unnormed = jnp.exp(scores - row_top[:, None])
        unnormed_grad = product_cols(weighted_every, value_rows) + total_every[:, None]
        score_grad = (unnormed * unnormed_grad).astype(jnp.bfloat16)
        value_grad = product_rows(unnormed.astype(jnp.bfloat16), weighted_every).astype(
            jnp.bfloat16
        )
        key_grad = (product_rows(score_grad, queries) * scale).astype(jnp.bfloat16)
        query_grad = lax.psum_scatter(
            (product_plain(score_grad, key_rows) * scale).astype(jnp.bfloat16),
            "tok",
            scatter_dimension=0,
            tiled=True,
        )
        add_term(grads, "key_weight", product_rows(normed, key_grad))
        add_term(grads, "value_weight", product_rows(normed, value_grad))
        normed_grad = product_cols(key_grad, key_weight) + product_cols(value_grad, value_weight)
        source_grad, gain_grad = norm_back(source, token_gain, normed_grad)
        add_term(grads, "token_gain", gain_grad)
        token_grads.append(source_grad)
        add_term(grads, "query_weight", product_rows(latent_normed, query_grad))
        latent_grad, gain_grad = norm_back(
            latent_in, query_gain, product_cols(query_grad, query_weight)
        )
        add_term(grads, "query_gain", gain_grad)
        latent_grads.append(latent_upstream + latent_grad)
    parts = (
        lax.psum_scatter(
            grads["token_gain"].astype(jnp.bfloat16), "tok", scatter_dimension=0, tiled=True
        ).astype(jnp.float32),
        lax.psum_scatter(
            grads["query_gain"].astype(jnp.bfloat16), "tok", scatter_dimension=0, tiled=True
        ).astype(jnp.float32),
        lax.psum_scatter(
            grads["query_weight"].astype(jnp.bfloat16), "tok", scatter_dimension=0, tiled=True
        ).astype(jnp.float32),
        lax.psum_scatter(
            grads["key_weight"].astype(jnp.bfloat16), "tok", scatter_dimension=0, tiled=True
        ).astype(jnp.float32),
        lax.psum_scatter(
            grads["value_weight"].astype(jnp.bfloat16), "tok", scatter_dimension=0, tiled=True
        ).astype(jnp.float32),
        lax.psum_scatter(
            grads["output_weight"].astype(jnp.bfloat16), "tok", scatter_dimension=0, tiled=True
        ).astype(jnp.float32),
        lax.psum_scatter(
            grads["first_gain"].astype(jnp.bfloat16), "tok", scatter_dimension=0, tiled=True
        ).astype(jnp.float32),
        lax.psum_scatter(
            grads["first_up"].astype(jnp.bfloat16), "tok", scatter_dimension=0, tiled=True
        ).astype(jnp.float32),
        lax.psum_scatter(
            grads["first_down"].astype(jnp.bfloat16), "tok", scatter_dimension=0, tiled=True
        ).astype(jnp.float32),
        lax.psum_scatter(
            grads["mixer_gain"].astype(jnp.bfloat16), "tok", scatter_dimension=0, tiled=True
        ).astype(jnp.float32),
        lax.psum_scatter(
            grads["mixer_project"].astype(jnp.bfloat16), "tok", scatter_dimension=0, tiled=True
        ).astype(jnp.float32),
        lax.psum_scatter(
            grads["mixer_output"].astype(jnp.bfloat16), "tok", scatter_dimension=0, tiled=True
        ).astype(jnp.float32),
        lax.psum_scatter(
            grads["second_gain"].astype(jnp.bfloat16), "tok", scatter_dimension=0, tiled=True
        ).astype(jnp.float32),
        lax.psum_scatter(
            grads["second_up"].astype(jnp.bfloat16), "tok", scatter_dimension=0, tiled=True
        ).astype(jnp.float32),
        lax.psum_scatter(
            grads["second_down"].astype(jnp.bfloat16), "tok", scatter_dimension=0, tiled=True
        ).astype(jnp.float32),
    )
    summed = (
        lax.psum(parts[0].astype(jnp.bfloat16), "grp").astype(jnp.float32),
        lax.psum(parts[1].astype(jnp.bfloat16), "grp").astype(jnp.float32),
        lax.psum(parts[2].astype(jnp.bfloat16), "grp").astype(jnp.float32),
        lax.psum(parts[3].astype(jnp.bfloat16), "grp").astype(jnp.float32),
        lax.psum(parts[4].astype(jnp.bfloat16), "grp").astype(jnp.float32),
        lax.psum(parts[5].astype(jnp.bfloat16), "grp").astype(jnp.float32),
        lax.psum(parts[6].astype(jnp.bfloat16), "grp").astype(jnp.float32),
        lax.psum(parts[7].astype(jnp.bfloat16), "grp").astype(jnp.float32),
        lax.psum(parts[8].astype(jnp.bfloat16), "grp").astype(jnp.float32),
        lax.psum(parts[9].astype(jnp.bfloat16), "grp").astype(jnp.float32),
        lax.psum(parts[10].astype(jnp.bfloat16), "grp").astype(jnp.float32),
        lax.psum(parts[11].astype(jnp.bfloat16), "grp").astype(jnp.float32),
        lax.psum(parts[12].astype(jnp.bfloat16), "grp").astype(jnp.float32),
        lax.psum(parts[13].astype(jnp.bfloat16), "grp").astype(jnp.float32),
        lax.psum(parts[14].astype(jnp.bfloat16), "grp").astype(jnp.float32),
    )
    return (
        jnp.stack(latent_outs)[None],
        jnp.stack(latent_grads)[None],
        jnp.stack(token_grads)[None],
    ) + tuple(summed)


TOK = 8
ROWS = L // TOK
FF = 2048
GR = L // LGROUPS
LOG2E = 1.4426950408889634
LN2 = 0.6931471805599453
F32 = jnp.float32
BF16 = jnp.bfloat16
MIB = 1024 * 1024


def nn(left, right):
    return lax.dot_general(left, right, (((1,), (0,)), ((), ())), preferred_element_type=F32)


def nt(left, right):
    return lax.dot_general(left, right, (((1,), (1,)), ((), ())), preferred_element_type=F32)


def tn(left, right):
    return lax.dot_general(left, right, (((0,), (0,)), ((), ())), preferred_element_type=F32)


def norm_parts(values):
    centre = values - jnp.mean(values, axis=-1, keepdims=True)
    inverse = lax.rsqrt(jnp.mean(centre * centre, axis=-1, keepdims=True) + EPS)
    return centre * inverse, inverse


def norm_pull(hat, inverse, gain, upstream):
    scaled = upstream * gain
    inner = jnp.mean(scaled * hat, axis=-1, keepdims=True)
    grad = (scaled - jnp.mean(scaled, axis=-1, keepdims=True) - hat * inner) * inverse
    return grad, upstream * hat


def places():
    me = lax.axis_index("tok")
    core = lax.rem(me, 2)
    chip = lax.div(me, 2)
    mate = me + 1 - 2 * core
    flip_x = chip + 1 - 2 * lax.rem(chip, 2)
    flip_y = lax.rem(chip + 2, 4)
    far = 3 - chip
    return me, core, chip, mate, (far, flip_x, flip_y)


def remote(src, dst, send_sem, recv_sem, peer):
    return pltpu.make_async_remote_copy(
        src_ref=src,
        dst_ref=dst,
        send_sem=send_sem,
        recv_sem=recv_sem,
        device_id={"tok": peer},
        device_id_type=pl.DeviceIdType.MESH,
    )


def greet(devices):
    barrier = pltpu.get_barrier_semaphore()
    for device in devices:
        pl.semaphore_signal(
            barrier, inc=1, device_id={"tok": device}, device_id_type=pl.DeviceIdType.MESH
        )
    pl.semaphore_wait(barrier, len(devices))


def exchange_kernel(to_heads, src_ref, dst_ref, send_sem, recv_sem, local_sem):
    me, core, chip, mate, others = places()
    peers = []
    for other in others:
        peers += [2 * other + core, 2 * other + 1 - core]
    peers.append(mate)
    greet(peers)

    def ends(mine, device, member):
        rows_lane = pl.ds(member * ROWS, ROWS)
        if to_heads:
            source = src_ref.at[:, device, :, rows_lane]
            target = dst_ref.at[:, member, :, pl.ds(pl.multiple_of(mine * ROWS, ROWS), ROWS)]
        else:
            source = src_ref.at[:, member, :, pl.ds(pl.multiple_of(device * ROWS, ROWS), ROWS)]
            target = dst_ref.at[:, mine, :, rows_lane]
        return source, target

    copies = []
    for slot, peer in enumerate(peers):
        for member in range(MB):
            source, target = ends(me, peer, member)
            copies.append(remote(source, target, send_sem.at[slot, member], recv_sem.at[slot, member], peer))
            copies[-1].start()
    own = []
    for member in range(MB):
        source, target = ends(me, me, member)
        own.append(pltpu.make_async_copy(source, target, local_sem.at[member]))
        own[-1].start()
    for copy in own:
        copy.wait()
    for copy in copies:
        copy.wait()


def exchange(to_heads, collective_id, source):
    kinds = source.shape[0]
    shape = (kinds, MB, HD, L) if to_heads else (kinds, H, HD, MB * ROWS)
    dma = pltpu.SemaphoreType.DMA
    return pl.pallas_call(
        functools.partial(exchange_kernel, to_heads),
        in_specs=[pl.BlockSpec(memory_space=pl.ANY)],
        out_specs=pl.BlockSpec(memory_space=pl.ANY),
        out_shape=jax.ShapeDtypeStruct(shape, source.dtype),
        scratch_shapes=[dma((7, MB)), dma((7, MB)), dma((MB,))],
        compiler_params=pltpu.CompilerParams(collective_id=collective_id, has_side_effects=True),
        name="exchange",
    )(source)


def mixer_attend_kernel(all_ref, q_ref, mixed_ref, exact_ref, lse_ref, keys, values):
    @pl.when(pl.program_id(1) == 0)
    def _():
        keys[...] = all_ref[1, 0].T
        values[0:HD] = all_ref[2, 0]
        values[HD:] = jnp.ones((16, L), BF16)

    logits = nn(keys[...], q_ref[0, 0])
    top = jnp.max(logits, axis=0, keepdims=True)
    raised = jnp.exp2(logits - top).astype(BF16)
    both = nn(values[...], raised)
    total = both[HD:HD + 1]
    mixed = both[0:HD] / total
    exact_ref[0] = mixed
    mixed_ref[0, 0] = mixed.astype(BF16)
    lse = top + jnp.log2(total)
    lse_ref[0] = jnp.concatenate([lse, jnp.zeros((7, lse.shape[1]), F32)], axis=0)


QB = 256


def mixer_attend(packed):
    return pl.pallas_call(
        mixer_attend_kernel,
        grid=(MB, L // QB),
        in_specs=[
            pl.BlockSpec((3, 1, HD, L), lambda b, i: (0, b, 0, 0)),
            pl.BlockSpec((1, 1, HD, QB), lambda b, i: (0, b, 0, i)),
        ],
        out_specs=[
            pl.BlockSpec((1, 1, HD, QB), lambda b, i: (0, b, 0, i)),
            pl.BlockSpec((1, HD, QB), lambda b, i: (b, 0, i)),
            pl.BlockSpec((1, 8, QB), lambda b, i: (b, 0, i)),
        ],
        out_shape=[
            jax.ShapeDtypeStruct((1, MB, HD, L), BF16),
            jax.ShapeDtypeStruct((MB, HD, L), F32),
            jax.ShapeDtypeStruct((MB, 8, L), F32),
        ],
        scratch_shapes=[pltpu.VMEM((L, HD), BF16), pltpu.VMEM((HD + 16, L), BF16)],
        compiler_params=pltpu.CompilerParams(
            dimension_semantics=("arbitrary", "arbitrary"), vmem_limit_bytes=48 * MIB
        ),
        cost_estimate=pl.CostEstimate(
            flops=9 * 10**9, bytes_accessed=4 * 10**6, transcendentals=8 * 10**6
        ),
        name="mixer_attend",
    )(packed, packed)


def mixer_attend_back_kernel(all_ref, q_ref, up_ref, exact_ref, lse_ref, out_ref, keys, values, key_acc, value_acc):
    step = pl.program_id(1)

    @pl.when(step == 0)
    def _():
        keys[...] = all_ref[1, 0].T
        values[...] = all_ref[2, 0].T
        key_acc[...] = jnp.zeros_like(key_acc)
        value_acc[...] = jnp.zeros_like(value_acc)

    queries = q_ref[0, 0]
    upstream = up_ref[0, 0]
    inner = jnp.sum(upstream.astype(F32) * exact_ref[0], axis=0, keepdims=True)
    softened = jnp.exp2(nn(keys[...], queries) - lse_ref[0][0:1])
    soft_grad = nn(values[...], upstream)
    logit_grad = (softened * (soft_grad - inner)).astype(BF16)
    value_acc[...] += nt(upstream, softened.astype(BF16))
    key_acc[...] += nt(queries, logit_grad)
    query_grad = nn(all_ref[1, 0], logit_grad) * HD ** (-0.5)
    out_ref[0, 0, :, pl.ds(pl.multiple_of(step * QB, QB), QB)] = query_grad.astype(BF16)

    @pl.when(step == L // QB - 1)
    def _():
        out_ref[1, 0] = (key_acc[...] * LN2).astype(BF16)
        out_ref[2, 0] = value_acc[...].astype(BF16)


def mixer_attend_back(packed, upstream, exact, lse):
    return pl.pallas_call(
        mixer_attend_back_kernel,
        grid=(MB, L // QB),
        in_specs=[
            pl.BlockSpec((3, 1, HD, L), lambda b, i: (0, b, 0, 0)),
            pl.BlockSpec((1, 1, HD, QB), lambda b, i: (0, b, 0, i)),
            pl.BlockSpec((1, 1, HD, QB), lambda b, i: (0, b, 0, i)),
            pl.BlockSpec((1, HD, QB), lambda b, i: (b, 0, i)),
            pl.BlockSpec((1, 8, QB), lambda b, i: (b, 0, i)),
        ],
        out_specs=pl.BlockSpec((3, 1, HD, L), lambda b, i: (0, b, 0, 0)),
        out_shape=jax.ShapeDtypeStruct((3, MB, HD, L), BF16),
        scratch_shapes=[
            pltpu.VMEM((L, HD), BF16),
            pltpu.VMEM((L, HD), BF16),
            pltpu.VMEM((HD, L), F32),
            pltpu.VMEM((HD, L), F32),
        ],
        compiler_params=pltpu.CompilerParams(
            dimension_semantics=("arbitrary", "arbitrary"), vmem_limit_bytes=48 * MIB
        ),
        cost_estimate=pl.CostEstimate(
            flops=22 * 10**9, bytes_accessed=5 * 10**6, transcendentals=8 * 10**6
        ),
        name="mixer_attend_back",
    )(packed, packed, upstream, exact, lse)


def chip_at(chip, flip):
    across = lax.rem(lax.rem(chip, 2) + lax.rem(flip, 2), 2)
    along = lax.rem(lax.div(chip, 2) + lax.div(flip, 2), 2)
    return 2 * along + across


def mask_rows(seg_ref, mask_ref, count_ref, bias_ref):
    for member in range(MB):
        scene = lax.broadcasted_iota(jnp.int32, (SCENES, TOK_DEV), 0)
        place = lax.broadcasted_iota(jnp.int32, (SCENES, TOK_DEV), 1)
        hot = jnp.where((seg_ref[member] == scene) & (place < count_ref[member]), 1.0, 0.0)
        seen = tn(jnp.where(mask_ref[member] > 0, 1.0, 0.0).astype(BF16), hot.astype(BF16))
        bias_ref[member] = jnp.where(seen > 0.5, 0.0, NEG)


def to_rows(first, second):
    rows = first.shape[0]
    lane = lax.broadcasted_iota(jnp.int32, (rows, 128), 1)
    return jnp.where(lane == 0, first, second).T[0:8]


def cross_forward_kernel(
    tok_ref, lat_ref, tgain_ref, qgain_ref, qw_ref, kw_ref, vw_ref, seg_ref, mask_ref, count_ref,
    k_out, v_out, q_out, att_ref, lse_ref,
    tok_buf, lat_buf, keys, values, queries, bias, part, part_s, got, got_s, stage, stage_s,
    arrive, arrive_s, total,
    tok_sem, lat_sem, k_sem, v_sem, q_sem,
    core_send, core_recv, core_send_s, core_recv_s, chip_send, chip_recv, chip_send_s, chip_recv_s,
):
    me, core, chip, mate, others = places()
    span = 2 * ROWS

    def unpack(step):
        return lax.div(step, 4), 3 - lax.rem(step, 4)

    def lat_copy(step):
        member, flip = unpack(step)
        start = pl.multiple_of(chip_at(chip, flip) * span, span)
        return pltpu.make_async_copy(lat_ref.at[0, member, pl.ds(start, span)], lat_buf.at[step], lat_sem.at[step])

    def q_copy(step):
        member, flip = unpack(step)
        start = pl.multiple_of(chip_at(chip, flip) * span, span)
        return pltpu.make_async_copy(queries.at[step], q_out.at[member, pl.ds(start, span)], q_sem.at[step])

    def tok_copy(member):
        return pltpu.make_async_copy(tok_ref.at[0, member], tok_buf.at[member], tok_sem.at[member])

    def kv_copies(member):
        return (
            pltpu.make_async_copy(keys.at[member], k_out.at[member], k_sem.at[member]),
            pltpu.make_async_copy(values.at[member], v_out.at[member], v_sem.at[member]),
        )

    def core_copies(step):
        return (
            remote(part.at[step, 1 - core], got.at[step], core_send.at[step], core_recv.at[step], mate),
            remote(part_s.at[step, 1 - core], got_s.at[step], core_send_s.at[step], core_recv_s.at[step], mate),
        )

    def chip_copies(step):
        member, flip = unpack(step)
        peer = 2 * chip_at(chip, flip) + core
        place = 3 * member + flip - 1
        return (
            remote(stage.at[step], arrive.at[place], chip_send.at[place], chip_recv.at[place], peer),
            remote(stage_s.at[step], arrive_s.at[place], chip_send_s.at[place], chip_recv_s.at[place], peer),
        )

    for member in range(MB):
        tok_copy(member).start()
    for step in range(2 * 4):
        lat_copy(step).start()
    greet([mate] + [2 * other + core for other in others])
    mask_rows(seg_ref, mask_ref, count_ref, bias)

    def compute(step):
        member, flip = unpack(step)

        @pl.when(flip == 3)
        def _():
            tok_copy(member).wait()
            hat, inverse = norm_parts(tok_buf[member].astype(F32))
            normed = (hat * tgain_ref[...]).astype(BF16)
            keys[member] = nn(normed, kw_ref[...]).astype(BF16)
            values[member] = nn(normed, vw_ref[...]).astype(BF16)
            for copy in kv_copies(member):
                copy.start()

        lat_copy(step).wait()
        hat, inverse = norm_parts(lat_buf[step])
        normed = (hat * qgain_ref[...]).astype(BF16)
        asked = (nn(normed, qw_ref[...]) * (D ** (-0.5) * LOG2E)).astype(BF16)
        queries[step] = asked
        q_copy(step).start()
        scores = nt(asked, keys[member])
        raised = []
        for half in range(2):
            seen = bias[member, pl.ds(2 * chip_at(chip, flip) + half, 1), :]
            own = scores[half * ROWS:(half + 1) * ROWS] + seen
            top = jnp.max(own, axis=1, keepdims=True)
            own = jnp.exp2(own - top)
            part_s[step, half] = to_rows(top, jnp.sum(own, axis=1, keepdims=True))
            raised.append(own.astype(BF16))
        sums = nn(jnp.concatenate(raised, axis=0), values[member]).astype(BF16)
        for half in range(2):
            part[step, half] = sums[half * ROWS:(half + 1) * ROWS]
        for copy in core_copies(step):
            copy.start()

    def merge(one, one_s, two, two_s):
        top = jnp.maximum(one_s[0:1], two_s[0:1])
        one_w, two_w = jnp.exp2(one_s[0:1] - top), jnp.exp2(two_s[0:1] - top)
        sums = one_s[1:2] * one_w + two_s[1:2] * two_w
        spare = jnp.zeros((6, ROWS), F32)
        weights = jnp.concatenate([one_w, two_w, spare], axis=0).T
        return one * weights[:, 0:1] + two * weights[:, 1:2], jnp.concatenate([top, sums, spare], axis=0)

    def combine(step):
        member, flip = unpack(step)
        for copy in core_copies(step):
            copy.wait_recv()
        added, figures = merge(
            part[step, core].astype(F32), part_s[step, core], got[step].astype(F32), got_s[step]
        )
        stage_s[step] = figures

        @pl.when(flip > 0)
        def _():
            stage[step] = added.astype(BF16)
            for copy in chip_copies(step):
                copy.start()

        @pl.when(flip == 0)
        def _():
            total[member] = added

    def finish(member):
        added, figures = total[member], stage_s[4 * member + 3]
        for flip in (1, 2, 3):
            for copy in chip_copies(4 * member + 3 - flip):
                copy.wait_recv()
            place = 3 * member + flip - 1
            added, figures = merge(added, figures, arrive[place].astype(F32), arrive_s[place])
        spare = jnp.zeros((7, ROWS), F32)
        inverse = jnp.concatenate([1.0 / figures[1:2], spare], axis=0).T
        att_ref[member] = added * inverse[:, 0:1]
        lse_ref[member] = jnp.concatenate([figures[0:1] + jnp.log2(figures[1:2]), spare], axis=0)

    def step_body(step, carry):
        compute(step)

        @pl.when(step > 0)
        def _():
            combine(step - 1)

        return carry

    lax.fori_loop(0, 4 * MB, step_body, 0)
    combine(jnp.int32(4 * MB - 1))
    for member in range(MB):
        finish(member)
    for member in range(MB):
        for copy in kv_copies(member):
            copy.wait()
        for slot in range(4):
            step = 4 * member + slot
            q_copy(step).wait()
            for copy in core_copies(step):
                copy.wait_send()
            if slot < 3:
                for copy in chip_copies(step):
                    copy.wait_send()


def cross_forward(collective_id, *args):
    dma = pltpu.SemaphoreType.DMA
    span = 2 * ROWS
    steps = 4 * MB
    vmem = pl.BlockSpec(memory_space=pltpu.VMEM)
    hbm = pl.BlockSpec(memory_space=pl.ANY)
    return pl.pallas_call(
        cross_forward_kernel,
        in_specs=[hbm, hbm] + [vmem] * 8,
        out_specs=[hbm, hbm, hbm, vmem, vmem],
        out_shape=[
            jax.ShapeDtypeStruct((MB, TOK_DEV, D), BF16),
            jax.ShapeDtypeStruct((MB, TOK_DEV, D), BF16),
            jax.ShapeDtypeStruct((MB, L, D), BF16),
            jax.ShapeDtypeStruct((MB, ROWS, D), F32),
            jax.ShapeDtypeStruct((MB, 8, ROWS), F32),
        ],
        scratch_shapes=[
            pltpu.VMEM((MB, TOK_DEV, D), BF16),
            pltpu.VMEM((steps, span, D), F32),
            pltpu.VMEM((MB, TOK_DEV, D), BF16),
            pltpu.VMEM((MB, TOK_DEV, D), BF16),
            pltpu.VMEM((steps, span, D), BF16),
            pltpu.VMEM((MB, LGROUPS, TOK_DEV), F32),
            pltpu.VMEM((steps, 2, ROWS, D), BF16),
            pltpu.VMEM((steps, 2, 8, ROWS), F32),
            pltpu.VMEM((steps, ROWS, D), BF16),
            pltpu.VMEM((steps, 8, ROWS), F32),
            pltpu.VMEM((steps, ROWS, D), BF16),
            pltpu.VMEM((steps, 8, ROWS), F32),
            pltpu.VMEM((3 * MB, ROWS, D), BF16),
            pltpu.VMEM((3 * MB, 8, ROWS), F32),
            pltpu.VMEM((MB, ROWS, D), F32),
            dma((MB,)), dma((steps,)), dma((MB,)), dma((MB,)), dma((steps,)),
        ] + [dma((steps,))] * 4 + [dma((3 * MB,))] * 4,
        compiler_params=pltpu.CompilerParams(
            collective_id=collective_id, has_side_effects=True, vmem_limit_bytes=56 * MIB
        ),
        cost_estimate=pl.CostEstimate(
            flops=14 * 10**9, bytes_accessed=22 * 10**6, transcendentals=4 * 10**6
        ),
        name="cross_forward",
    )(*args)


def cross_backward_kernel(
    tok_ref, tgain_ref, kw_ref, vw_ref, seg_ref, mask_ref, count_ref, k_ref, v_ref, q_ref, up_ref, fig_ref,
    dq_ref, dtok_ref, dkw_ref, dvw_ref, dgain_ref,
    tok_buf, keys, values, queries, ups, figs, bias, part, got, stage, arrive, total, dk, dv, dtok, dkw, dvw,
    tok_sem, k_sem, v_sem, q_sem, out_sem, near_send, near_recv, far_send, far_recv, on_send, on_recv, own_sem,
    core_send, core_recv, chip_send, chip_recv,
):
    me, core, chip, mate, others = places()
    span = 2 * ROWS

    def slot_of(step):
        member, place = lax.div(step, 4), lax.rem(step, 4)
        return member, place + member * (3 - 2 * place)

    def loads(slot):
        member, flip = divmod(slot, 4)
        start = pl.multiple_of(chip_at(chip, flip) * span, span)
        return pltpu.make_async_copy(q_ref.at[member, pl.ds(start, span)], queries.at[slot], q_sem.at[slot])

    def tok_copies(member):
        return (
            pltpu.make_async_copy(k_ref.at[member], keys.at[member], k_sem.at[member]),
            pltpu.make_async_copy(v_ref.at[member], values.at[member], v_sem.at[member]),
            pltpu.make_async_copy(tok_ref.at[0, member], tok_buf.at[member], tok_sem.at[member]),
        )

    def out_copy(member):
        return pltpu.make_async_copy(dtok.at[member], dtok_ref.at[0, member], out_sem.at[member])

    def own_copies(member):
        slot = 4 * member
        return (
            pltpu.make_async_copy(up_ref.at[member], ups.at[slot, core], own_sem.at[member, 0]),
            pltpu.make_async_copy(fig_ref.at[member], figs.at[slot, core], own_sem.at[member, 1]),
        )

    def near_copies(member):
        slot = 4 * member
        return (
            remote(up_ref.at[member], ups.at[slot, core], near_send.at[member, 0], near_recv.at[member, 0], mate),
            remote(fig_ref.at[member], figs.at[slot, core], near_send.at[member, 1], near_recv.at[member, 1], mate),
        )

    def far_copies(slot):
        member, flip = slot // 4, slot % 4
        peer = 2 * chip_at(chip, flip) + core
        return (
            remote(up_ref.at[member], ups.at[slot, core], far_send.at[slot, 0], far_recv.at[slot, 0], peer),
            remote(fig_ref.at[member], figs.at[slot, core], far_send.at[slot, 1], far_recv.at[slot, 1], peer),
        )

    def on_copies(slot):
        return (
            remote(ups.at[slot, core], ups.at[slot, core], on_send.at[slot, 0], on_recv.at[slot, 0], mate),
            remote(figs.at[slot, core], figs.at[slot, core], on_send.at[slot, 1], on_recv.at[slot, 1], mate),
        )

    def pass_on(slot):
        for copy in far_copies(slot):
            copy.wait_recv()
        for copy in on_copies(slot):
            copy.start()

    def core_copy(slot):
        return remote(part.at[slot, 1 - core], got.at[slot], core_send.at[slot], core_recv.at[slot], mate)

    def chip_copy(slot):
        member, flip = lax.div(slot, 4), lax.rem(slot, 4)
        peer = 2 * chip_at(chip, flip) + core
        place = 3 * member + flip - 1
        return remote(stage.at[slot], arrive.at[place], chip_send.at[place], chip_recv.at[place], peer)

    for copy in own_copies(0):
        copy.start()
    for copy in tok_copies(0):
        copy.start()
    for flip in (0, 1, 2, 3):
        loads(flip).start()
    for copy in own_copies(1):
        copy.start()
    for copy in tok_copies(1):
        copy.start()
    for flip in (3, 2, 1, 0):
        loads(4 + flip).start()
    greet([mate] + [2 * other + core for other in others])
    for member in range(MB):
        for copy in near_copies(member):
            copy.start()
        for flip in ((1, 2, 3) if member == 0 else (3, 2, 1)):
            for copy in far_copies(4 * member + flip):
                copy.start()
    mask_rows(seg_ref, mask_ref, count_ref, bias)

    def compute(step):
        member, flip = slot_of(step)
        slot = 4 * member + flip

        @pl.when(lax.rem(step, 4) == 0)
        def _():
            for copy in tok_copies(member):
                copy.wait()
            dk[...] = jnp.zeros_like(dk)
            dv[...] = jnp.zeros_like(dv)

        start = pl.multiple_of(chip_at(chip, flip) * span, span)
        pltpu.make_async_copy(q_ref.at[member, pl.ds(start, span)], queries.at[slot], q_sem.at[slot]).wait()

        @pl.when(flip == 0)
        def _():
            for copy in own_copies(member):
                copy.wait()
            for copy in near_copies(member):
                copy.wait_recv()

        @pl.when(flip > 0)
        def _():
            for copy in on_copies(slot):
                copy.wait_recv()

        asked = queries[slot]
        upstream = ups[slot].reshape(span, D)
        scores = nt(asked, keys[member])
        soft = nt(upstream, values[member])
        weights, grads = [], []
        for half in range(2):
            seen = bias[member, pl.ds(2 * chip_at(chip, flip) + half, 1), :]
            figures = figs[slot, half].T
            rows = slice(half * ROWS, (half + 1) * ROWS)
            weight = jnp.exp2(scores[rows] + seen - figures[:, 0:1])
            grads.append((weight * (soft[rows] - figures[:, 1:2])).astype(BF16))
            weights.append(weight.astype(BF16))
        weight = jnp.concatenate(weights, axis=0)
        grad = jnp.concatenate(grads, axis=0)
        dv[...] += tn(weight, upstream)
        dk[...] += tn(grad, asked)
        asked_grad = (nn(grad, keys[member]) * D ** (-0.5)).astype(BF16)
        for half in range(2):
            part[slot, half] = asked_grad[half * ROWS:(half + 1) * ROWS]
        core_copy(slot).start()

    def combine(step):
        member, flip = slot_of(step)
        slot = 4 * member + flip
        core_copy(slot).wait_recv()
        added = part[slot, core].astype(F32) + got[slot].astype(F32)

        @pl.when(flip > 0)
        def _():
            stage[slot] = added.astype(BF16)
            chip_copy(slot).start()

        @pl.when(flip == 0)
        def _():
            total[member] = added

    def tokens_back(member):
        gain = tgain_ref[...]
        hat, inverse = norm_parts(tok_buf[member].astype(F32))
        normed = (hat * gain).astype(BF16)
        key_grad = (dk[...] * LN2).astype(BF16)
        value_grad = dv[...].astype(BF16)
        key_term = tn(normed, key_grad)
        value_term = tn(normed, value_grad)
        normed_grad = nt(key_grad, kw_ref[...]) + nt(value_grad, vw_ref[...])
        source_grad, gain_rows = norm_pull(hat, inverse, gain, normed_grad)
        dtok[member] = source_grad
        out_copy(member).start()
        gain_term = jnp.sum(gain_rows, axis=0, keepdims=True)

        @pl.when(member == 0)
        def _():
            dkw[...] = key_term
            dvw[...] = value_term
            dgain_ref[...] = gain_term

        @pl.when(member > 0)
        def _():
            dkw_ref[...] = (dkw[...] + key_term).astype(BF16)
            dvw_ref[...] = (dvw[...] + value_term).astype(BF16)
            dgain_ref[...] += gain_term

    def step_body(step, carry):
        compute(step)

        @pl.when(step > 0)
        def _():
            combine(step - 1)

        @pl.when(step == 0)
        def _():
            pass_on(1)
            pass_on(2)

        @pl.when(step == 1)
        def _():
            pass_on(3)

        @pl.when(step == 3)
        def _():
            pass_on(7)
            pass_on(6)

        @pl.when(step == 4)
        def _():
            pass_on(5)

        @pl.when(step == 4 * MB - 1)
        def _():
            combine(step)

        @pl.when(lax.rem(step, 4) == 3)
        def _():
            tokens_back(lax.div(step, 4))

        return carry

    lax.fori_loop(0, 4 * MB, step_body, 0)
    for member in range(MB):
        added = total[member]
        for flip in (1, 2, 3):
            chip_copy(4 * member + flip).wait_recv()
            added = added + arrive[3 * member + flip - 1].astype(F32)
        dq_ref[member] = added.astype(BF16)
    for member in range(MB):
        out_copy(member).wait()
        for copy in near_copies(member):
            copy.wait_send()
        for flip in range(4):
            slot = 4 * member + flip
            core_copy(slot).wait_send()
            if flip > 0:
                chip_copy(slot).wait_send()
                for copy in far_copies(slot) + on_copies(slot):
                    copy.wait_send()


def cross_backward(collective_id, *args):
    dma = pltpu.SemaphoreType.DMA
    span = 2 * ROWS
    steps = 4 * MB
    vmem = pl.BlockSpec(memory_space=pltpu.VMEM)
    hbm = pl.BlockSpec(memory_space=pl.ANY)
    return pl.pallas_call(
        cross_backward_kernel,
        in_specs=[hbm] + [vmem] * 6 + [hbm] * 5,
        out_specs=[vmem, hbm, vmem, vmem, vmem],
        out_shape=[
            jax.ShapeDtypeStruct((MB, ROWS, D), BF16),
            jax.ShapeDtypeStruct((1, MB, TOK_DEV, D), F32),
            jax.ShapeDtypeStruct((D, D), BF16),
            jax.ShapeDtypeStruct((D, D), BF16),
            jax.ShapeDtypeStruct((1, D), F32),
        ],
        scratch_shapes=[
            pltpu.VMEM((MB, TOK_DEV, D), BF16),
            pltpu.VMEM((MB, TOK_DEV, D), BF16),
            pltpu.VMEM((MB, TOK_DEV, D), BF16),
            pltpu.VMEM((steps, span, D), BF16),
            pltpu.VMEM((steps, 2, ROWS, D), BF16),
            pltpu.VMEM((steps, 2, 8, ROWS), F32),
            pltpu.VMEM((MB, LGROUPS, TOK_DEV), F32),
            pltpu.VMEM((steps, 2, ROWS, D), BF16),
            pltpu.VMEM((steps, ROWS, D), BF16),
            pltpu.VMEM((steps, ROWS, D), BF16),
            pltpu.VMEM((3 * MB, ROWS, D), BF16),
            pltpu.VMEM((MB, ROWS, D), F32),
            pltpu.VMEM((TOK_DEV, D), F32),
            pltpu.VMEM((TOK_DEV, D), F32),
            pltpu.VMEM((MB, TOK_DEV, D), F32),
            pltpu.VMEM((D, D), F32),
            pltpu.VMEM((D, D), F32),
            dma((MB,)), dma((MB,)), dma((MB,)), dma((steps,)), dma((MB,)),
            dma((MB, 2)), dma((MB, 2)), dma((steps, 2)), dma((steps, 2)), dma((steps, 2)), dma((steps, 2)), dma((MB, 2)),
            dma((steps,)), dma((steps,)), dma((3 * MB,)), dma((3 * MB,)),
        ],
        compiler_params=pltpu.CompilerParams(
            collective_id=collective_id, has_side_effects=True, vmem_limit_bytes=58 * MIB
        ),
        cost_estimate=pl.CostEstimate(
            flops=26 * 10**9, bytes_accessed=24 * 10**6, transcendentals=4 * 10**6
        ),
        name="cross_backward",
    )(*args)


def reduce_kernel(items, *refs):
    n = len(items)
    sources, outs, scratch = refs[:n], refs[n:2 * n], refs[2 * n:]
    mine, got, first_in, second_in, z_keep, z_first, z_second = [scratch[i * n:(i + 1) * n] for i in range(7)]
    (local_sem, core_send, core_recv, one_send, one_recv, two_send, two_recv, z_send, z_recv) = scratch[7 * n:]
    me, core, chip, mate, (far, flip_x, flip_y) = places()
    targets = (chip, flip_x, flip_y, far)
    level = lax.axis_index("grp")
    odd = lax.rem(level, 2)
    level_near = level + 1 - 2 * odd
    level_far = lax.rem(level + 2, 4)
    barrier = pltpu.get_barrier_semaphore()
    for device in (mate, 2 * flip_x + core, 2 * flip_y + core):
        pl.semaphore_signal(barrier, inc=1, device_id={"tok": device}, device_id_type=pl.DeviceIdType.MESH)
    for other in (level_near, level_far):
        pl.semaphore_signal(barrier, inc=1, device_id={"grp": other}, device_id_type=pl.DeviceIdType.MESH)
    pl.semaphore_wait(barrier, 5)

    def along(item, src, dst, step, other):
        return pltpu.make_async_remote_copy(
            src_ref=src, dst_ref=dst, send_sem=z_send.at[item, step], recv_sem=z_recv.at[item, step],
            device_id={"grp": other}, device_id_type=pl.DeviceIdType.MESH,
        )

    sent, cores, ones, twos, zs = [], {}, {}, {}, {}
    for i, (rows, columns, kind, x_first) in enumerate(items):
        cores[i] = []
        for slot in (3, 2, 1, 0):
            own_rows = pl.ds(pl.multiple_of((2 * targets[slot] + core) * rows, rows), rows)
            mate_rows = pl.ds(pl.multiple_of((2 * targets[slot] + 1 - core) * rows, rows), rows)
            there = remote(sources[i].at[mate_rows], got[i].at[slot], core_send.at[i, slot], core_recv.at[i, slot], mate)
            here = pltpu.make_async_copy(sources[i].at[own_rows], mine[i].at[slot], local_sem.at[i, slot])
            there.start()
            here.start()
            cores[i].append((slot, there, here))
            sent.append(there)

    def add(target, one, two, kind):
        target[...] = (one[...].astype(F32) + two[...].astype(F32)).astype(kind)

    def core_sums(i):
        rows, columns, kind, x_first = items[i]
        for slot, there, here in cores[i]:
            there.wait_recv()
            here.wait()
            add(mine[i].at[slot], mine[i].at[slot], got[i].at[slot], kind)
        near = 1 if x_first else 2
        peer = 2 * targets[near] + core
        ones[i] = []
        for place, slot in ((1, 3), (0, near)):
            copy = remote(mine[i].at[slot], first_in[i].at[place], one_send.at[i, place], one_recv.at[i, place], peer)
            copy.start()
            ones[i].append((place, copy))
            sent.append(copy)

    def first_sums(i):
        rows, columns, kind, x_first = items[i]
        other = 2 if x_first else 1
        for place, copy in ones[i]:
            copy.wait_recv()
            slot = other if place == 1 else 0
            add(mine[i].at[slot], mine[i].at[slot], first_in[i].at[place], kind)
            if place == 1:
                twos[i] = remote(mine[i].at[slot], second_in[i], two_send.at[i], two_recv.at[i], 2 * targets[other] + core)
                twos[i].start()
                sent.append(twos[i])

    def second_sums(i):
        rows, columns, kind, x_first = items[i]
        half = rows // 2
        twos[i].wait_recv()
        add(mine[i].at[0], mine[i].at[0], second_in[i], kind)
        away = pl.ds(pl.multiple_of((1 - odd) * half, half), half)
        zs[i, 0] = along(i, mine[i].at[0, away], z_first[i], 0, level_near)
        zs[i, 0].start()
        sent.append(zs[i, 0])

    def grp_first(i):
        rows, columns, kind, x_first = items[i]
        half = rows // 2
        keep = pl.ds(pl.multiple_of(odd * half, half), half)
        zs[i, 0].wait_recv()
        add(z_keep[i].at[0], mine[i].at[0, keep], z_first[i], kind)
        zs[i, 1] = along(i, z_keep[i].at[0], z_second[i].at[0], 1, level_far)
        zs[i, 1].start()
        sent.append(zs[i, 1])

    def grp_second(i):
        rows, columns, kind, x_first = items[i]
        half = rows // 2
        keep = pl.ds(pl.multiple_of(odd * half, half), half)
        zs[i, 1].wait_recv()
        add(z_keep[i].at[1], z_keep[i].at[0], z_second[i].at[0], kind)
        zs[i, 2] = along(i, z_keep[i].at[1], z_second[i].at[1], 2, level_near)
        zs[i, 2].start()
        sent.append(zs[i, 2])
        outs[i][keep] = z_keep[i][1].astype(F32)

    def grp_third(i):
        rows, columns, kind, x_first = items[i]
        half = rows // 2
        away = pl.ds(pl.multiple_of((1 - odd) * half, half), half)
        zs[i, 2].wait_recv()
        outs[i][away] = z_second[i][1].astype(F32)

    stages = (core_sums, first_sums, second_sums, grp_first, grp_second, grp_third)
    lags = (0, 2, 3, 4, 5, 6)
    for step in range(n + lags[-1]):
        for stage, lag in zip(stages, lags):
            if 0 <= step - lag < n:
                stage(step - lag)
    for copy in sent:
        copy.wait_send()


def reduce_grads(collective_id, arrays, x_firsts):
    items = tuple(
        (array.shape[0] // TOK, array.shape[1], array.dtype, x_first) for array, x_first in zip(arrays, x_firsts)
    )
    n = len(items)
    dma = pltpu.SemaphoreType.DMA
    blocks = lambda count, part: [
        pltpu.VMEM(((count,) if count else ()) + (rows // part, columns), kind) for rows, columns, kind, unused in items
    ]
    return pl.pallas_call(
        functools.partial(reduce_kernel, items),
        in_specs=[pl.BlockSpec(memory_space=pl.ANY)] * n,
        out_specs=[pl.BlockSpec(memory_space=pltpu.VMEM)] * n,
        out_shape=[jax.ShapeDtypeStruct((rows, columns), F32) for rows, columns, kind, unused in items],
        scratch_shapes=blocks(4, 1) + blocks(4, 1) + blocks(2, 1) + blocks(0, 1) + blocks(2, 2) + blocks(0, 2) + blocks(2, 2)
        + [dma((n, 4)), dma((n, 4)), dma((n, 4)), dma((n, 2)), dma((n, 2)), dma((n,)), dma((n,)), dma((n, 3)), dma((n, 3))],
        compiler_params=pltpu.CompilerParams(
            collective_id=collective_id, has_side_effects=True, vmem_limit_bytes=56 * MIB
        ),
        name="reduce_grads",
    )(*arrays)


def fast_body(
    tokens,
    latents,
    segments,
    scene_mask,
    counts,
    token_gain,
    query_gain,
    query_weight,
    key_weight,
    value_weight,
    output_weight,
    first_gain,
    first_up,
    first_down,
    mixer_gain,
    mixer_project,
    mixer_output,
    second_gain,
    second_up,
    second_down,
    cotangent,
):
    me = lax.axis_index("tok")
    scenes = (segments[0][:, None], scene_mask[0], counts[0][:, :, None])
    keys, values, queries, attended, lse = cross_forward(
        0, tokens, latents, token_gain[None], query_gain[None], query_weight, key_weight, value_weight, *scenes
    )
    attended = attended.reshape(MB * ROWS, D)
    latent_in = lax.dynamic_slice_in_dim(latents[0], me * ROWS, ROWS, 1).reshape(MB * ROWS, D)

    attended_low = attended.astype(BF16)
    first_mid = latent_in + nn(attended_low, output_weight)
    mixer_mid, first_saved = mlp_forward(first_mid, first_gain, first_up, first_down)

    mixer_normed = norm_rows(mixer_mid, mixer_gain).astype(BF16)
    packed = lax.dot_general(
        mixer_project, mixer_normed, (((0,), (1,)), ((), ())), preferred_element_type=F32
    ).reshape(3, D, MB * ROWS)
    packed = packed * jnp.array([HD ** (-0.5) * LOG2E, 1.0, 1.0], F32)[:, None, None]
    packed = packed.astype(BF16).reshape(3, H, HD, MB * ROWS)
    head_packed = exchange(True, 1, packed)
    head_mixed, head_exact, head_lse = mixer_attend(head_packed)
    mixed = exchange(False, 2, head_mixed).reshape(D, MB * ROWS)
    second_mid = mixer_mid + tn(mixed, mixer_output)
    final_rows, second_saved = mlp_forward(second_mid, second_gain, second_up, second_down)

    upstream = cotangent.reshape(MB * ROWS, D)
    upstream, d_second_gain, d_second_up, d_second_down = mlp_backward(
        second_mid, second_gain, second_up, second_down, second_saved, upstream
    )
    grad_low = upstream.astype(BF16)
    d_mixer_output = nn(mixed, grad_low)
    mixed_grad = nt(mixer_output, grad_low).astype(BF16).reshape(1, H, HD, MB * ROWS)
    head_grad = mixer_attend_back(head_packed, exchange(True, 3, mixed_grad), head_exact, head_lse)
    packed_grad = exchange(False, 4, head_grad).reshape(3 * D, MB * ROWS)
    d_mixer_project = lax.dot_general(
        mixer_normed, packed_grad, (((0,), (1,)), ((), ())), preferred_element_type=F32
    )
    normed_grad = lax.dot_general(
        packed_grad, mixer_project, (((0,), (1,)), ((), ())), preferred_element_type=F32
    )
    residual_grad, d_mixer_gain = norm_back(mixer_mid, mixer_gain, normed_grad)
    upstream, d_first_gain, d_first_up, d_first_down = mlp_backward(
        first_mid, first_gain, first_up, first_down, first_saved, upstream + residual_grad
    )
    grad_low = upstream.astype(BF16)
    d_output = tn(attended_low, grad_low)
    attended_grad = nt(grad_low, output_weight).astype(BF16)
    inner = jnp.sum(attended_grad.astype(F32) * attended, axis=1).reshape(MB, ROWS)
    figures = jnp.concatenate(
        [lse[:, 0:1], inner[:, None], jnp.zeros((MB, 6, ROWS), F32)], axis=1
    )
    query_grad, tokens_grad, d_key, d_value, d_token_gain = cross_backward(
        5, tokens, token_gain[None], key_weight, value_weight, *scenes, keys, values, queries,
        attended_grad.reshape(MB, ROWS, D), figures,
    )
    query_grad = query_grad.reshape(MB * ROWS, D)
    latent_normed = norm_rows(latent_in, query_gain).astype(BF16)
    d_query = tn(latent_normed, query_grad)
    latent_grad, d_query_gain = norm_back(latent_in, query_gain, nt(query_grad, query_weight))
    latent_grad = upstream + latent_grad

    small = jnp.concatenate(
        [d.astype(BF16) for d in (d_mixer_output, d_output, d_key, d_value, d_query)], axis=1
    )
    gains = jnp.stack([d_token_gain[0], d_query_gain, d_first_gain, d_mixer_gain, d_second_gain])
    gains = jnp.pad(
        gains.reshape(5, TOK, D // TOK).transpose(1, 0, 2), ((0, 0), (0, 11), (0, 128 - D // TOK))
    ).reshape(TOK * 16, 128)
    o_second_down, o_second_up, o_first_down, o_first_up, o_project, o_small, o_gains = reduce_grads(
        7,
        [d_second_down.astype(BF16), d_second_up.astype(BF16), d_first_down.astype(BF16),
         d_first_up.astype(BF16), d_mixer_project.astype(BF16), small, gains],
        (False, True, False, True, True, False, False),
    )
    o_mixer_output, o_output, o_key, o_value, o_query = [o_small[:, i * D:(i + 1) * D] for i in range(5)]
    o_gains = o_gains[:, :D // TOK]
    return (
        final_rows.reshape(1, MB, ROWS, D),
        latent_grad.reshape(1, MB, ROWS, D),
        tokens_grad,
        o_gains[0],
        o_gains[1],
        o_query,
        o_key,
        o_value,
        o_output,
        o_gains[2],
        o_first_up,
        o_first_down,
        o_gains[3],
        o_project,
        o_mixer_output,
        o_gains[4],
        o_second_up,
        o_second_down,
    )


IN_SPECS = (
    P("grp", None, "tok", None),
    P("grp", None, None, None),
    P("grp", None, "tok"),
    P("grp", None, None, None),
    P("grp", None, "tok"),
    P(),
    P(),
    P(),
    P(),
    P(),
    P(),
    P(),
    P(),
    P(),
    P(),
    P(),
    P(),
    P(),
    P(),
    P(),
    P("grp", None, "tok", None),
)
OUT_SPECS = (
    P("grp", None, "tok", None),
    P("grp", None, "tok", None),
    P("grp", None, "tok", None),
    P("tok"),
    P("tok"),
    P("tok", None),
    P("tok", None),
    P("tok", None),
    P("tok", None),
    P("tok"),
    P("tok", None),
    P("tok", None),
    P("tok"),
    P("tok", None),
    P("tok", None),
    P("tok"),
    P("tok", None),
    P("tok", None),
)


def solution(mesh):
    return jax.shard_map(
        fast_body if mesh.shape["tok"] == TOK else general_body,
        mesh=mesh,
        in_specs=IN_SPECS,
        out_specs=OUT_SPECS,
        check_vma=False,
    )
```

```python
import functools

import jax
import jax.numpy as jnp
from jax import lax
from jax.experimental import pallas as pl
from jax.experimental.pallas import tpu as pltpu
from jax.sharding import PartitionSpec as P

D = 512
L = 2048
H = 8
HD = 64
TOK_DEV = 1024
MB = 2
SCENES = 8
LGROUPS = 8


EPS = 1e-05
NEG = -1e30


def norm_rows(values, gain):
    centre = values - jnp.mean(values, axis=-1, keepdims=True)
    spread = jnp.mean(centre * centre, axis=-1, keepdims=True)
    return centre * lax.rsqrt(spread + EPS) * gain


def norm_back(values, gain, upstream):
    unused, pull = jax.vjp(norm_rows, values, gain)
    return pull(upstream)


def gelu_back(hidden, upstream):
    unused, pull = jax.vjp(jax.nn.gelu, hidden)
    return pull(upstream)[0]


def product_plain(left, right):
    return jnp.dot(left, right, preferred_element_type=jnp.float32)


def product_rows(left, right):
    return lax.dot_general(
        left, right, (((0,), (0,)), ((), ())), preferred_element_type=jnp.float32
    )


def product_cols(left, right):
    return lax.dot_general(
        left, right, (((1,), (1,)), ((), ())), preferred_element_type=jnp.float32
    )


def add_term(store, name, value):
    if name in store:
        store[name] = store[name] + value
    else:
        store[name] = value


def project_tokens(tokens, member, token_gain, key_weight, value_weight):
    source = tokens[0, member].astype(jnp.float32)
    normed = norm_rows(source, token_gain).astype(jnp.bfloat16)
    key_rows = product_plain(normed, key_weight).astype(jnp.bfloat16)
    value_rows = product_plain(normed, value_weight).astype(jnp.bfloat16)
    return (source, normed, key_rows, value_rows)


def mlp_forward(residual, gain, up_weight, down_weight):
    normed = norm_rows(residual, gain).astype(jnp.bfloat16)
    hidden = product_plain(normed, up_weight)
    active = jax.nn.gelu(hidden).astype(jnp.bfloat16)
    return (residual + product_plain(active, down_weight), (normed, hidden, active))


def mlp_backward(residual, gain, up_weight, down_weight, saved, upstream):
    normed, hidden, active = saved
    grad_low = upstream.astype(jnp.bfloat16)
    grad_down = product_rows(active, grad_low)
    hidden_grad = gelu_back(hidden, product_cols(grad_low, down_weight)).astype(jnp.bfloat16)
    grad_up = product_rows(normed, hidden_grad)
    residual_grad, grad_gain = norm_back(residual, gain, product_cols(hidden_grad, up_weight))
    return (upstream + residual_grad, grad_gain, grad_up, grad_down)


def mixer_forward(residual, gain, project, output):
    own_rows = residual.shape[0]
    normed = norm_rows(residual, gain).astype(jnp.bfloat16)
    packed = product_plain(normed, project).astype(jnp.bfloat16)
    pair_rows = lax.all_gather(packed[:, D:], "tok", axis=0, tiled=True)
    every = pair_rows.shape[0]
    own_queries = packed[:, :D].reshape(own_rows, H, HD)
    keys = pair_rows[:, :D].reshape(every, H, HD)
    values = pair_rows[:, D:].reshape(every, H, HD)
    logits = jnp.einsum(
        "qhd,khd->hqk", own_queries, keys, preferred_element_type=jnp.float32
    ) * HD ** (-0.5)
    peak_row = jnp.max(logits, axis=-1, keepdims=True)
    raised = jnp.exp(logits - peak_row)
    softened = raised / jnp.sum(raised, axis=-1, keepdims=True)
    softened_low = softened.astype(jnp.bfloat16)
    mixed_rows = jnp.einsum(
        "hqk,khd->qhd", softened_low, values, preferred_element_type=jnp.float32
    )
    mixed_rows = mixed_rows.reshape(own_rows, D).astype(jnp.bfloat16)
    return (
        residual + product_plain(mixed_rows, output),
        (normed, own_queries, keys, values, softened, softened_low, mixed_rows),
    )


def mixer_backward(residual, gain, project, output, saved, upstream):
    normed, own_queries, keys, values, softened, softened_low, mixed_rows = saved
    own_rows = upstream.shape[0]
    every = keys.shape[0]
    grad_low = upstream.astype(jnp.bfloat16)
    grad_output = product_rows(mixed_rows, grad_low)
    mixed_grad = product_cols(grad_low, output).astype(jnp.bfloat16).reshape(own_rows, H, HD)
    value_grad = jnp.einsum(
        "hqk,qhd->khd", softened_low, mixed_grad, preferred_element_type=jnp.float32
    )
    soft_grad = jnp.einsum("qhd,khd->hqk", mixed_grad, values, preferred_element_type=jnp.float32)
    logit_grad = softened * (soft_grad - jnp.sum(soft_grad * softened, axis=-1, keepdims=True))
    logit_grad = logit_grad.astype(jnp.bfloat16)
    query_grad = jnp.einsum(
        "hqk,khd->qhd", logit_grad, keys, preferred_element_type=jnp.float32
    ) * HD ** (-0.5)
    key_grad = jnp.einsum(
        "hqk,qhd->khd", logit_grad, own_queries, preferred_element_type=jnp.float32
    ) * HD ** (-0.5)
    pair_terms = jnp.concatenate([key_grad.reshape(every, D), value_grad.reshape(every, D)], axis=1)
    pair_grad = lax.psum_scatter(
        pair_terms.astype(jnp.bfloat16), "tok", scatter_dimension=0, tiled=True
    ).astype(jnp.float32)
    packed_grad = jnp.concatenate([query_grad.reshape(own_rows, D), pair_grad], axis=1).astype(
        jnp.bfloat16
    )
    grad_project = product_rows(normed, packed_grad)
    residual_grad, grad_gain = norm_back(residual, gain, product_cols(packed_grad, project))
    return (upstream + residual_grad, grad_gain, grad_project, grad_output)


def general_body(
    tokens,
    latents,
    segments,
    scene_mask,
    counts,
    token_gain,
    query_gain,
    query_weight,
    key_weight,
    value_weight,
    output_weight,
    first_gain,
    first_up,
    first_down,
    mixer_gain,
    mixer_project,
    mixer_output,
    second_gain,
    second_up,
    second_down,
    cotangent,
):
    scale = D ** (-0.5)
    shards = lax.axis_size("tok")
    own_rows = L // shards
    row_start = lax.axis_index("tok") * own_rows
    latent_group = jnp.arange(L) // (L // LGROUPS)
    latent_onehot = (latent_group[:, None] == jnp.arange(LGROUPS)[None, :]).astype(jnp.float32)
    token_place = jnp.arange(TOK_DEV)
    records = []
    latent_outs = []
    for member in range(MB):
        record = {}
        source, normed, key_rows, value_rows = project_tokens(
            tokens, member, token_gain, key_weight, value_weight
        )
        record["token_side"] = (source, normed, key_rows, value_rows)
        scene_onehot = (segments[0, member][:, None] == jnp.arange(SCENES)[None, :]).astype(
            jnp.float32
        )
        token_seen = jnp.dot(scene_onehot, scene_mask[0, member].astype(jnp.float32))
        visible = product_cols(latent_onehot, token_seen)
        alive = token_place < counts[0, member, 0]
        allowed = (visible > 0.5) & alive[None, :]
        latent_every = latents[0, member]
        normed_every = norm_rows(latent_every, query_gain).astype(jnp.bfloat16)
        queries = product_plain(normed_every, query_weight).astype(jnp.bfloat16)
        scores = jnp.where(allowed, product_cols(queries, key_rows) * scale, NEG)
        row_top = lax.pmax(jnp.max(scores, axis=1), "tok")
        unnormed = jnp.exp(scores - row_top[:, None])
        row_total, weighted = (
            lax.psum_scatter(
                jnp.sum(unnormed, axis=1).astype(jnp.bfloat16),
                "tok",
                scatter_dimension=0,
                tiled=True,
            ).astype(jnp.float32),
            lax.psum_scatter(
                product_plain(unnormed.astype(jnp.bfloat16), value_rows).astype(jnp.bfloat16),
                "tok",
                scatter_dimension=0,
                tiled=True,
            ).astype(jnp.float32),
        )
        latent_in = lax.dynamic_slice_in_dim(latent_every, row_start, own_rows, 0)
        latent_normed = lax.dynamic_slice_in_dim(normed_every, row_start, own_rows, 0)
        attended = weighted / row_total[:, None]
        attended_low = attended.astype(jnp.bfloat16)
        first_mid = latent_in + product_plain(attended_low, output_weight)
        mixer_mid, first_saved = mlp_forward(first_mid, first_gain, first_up, first_down)
        second_mid, mixer_saved = mixer_forward(mixer_mid, mixer_gain, mixer_project, mixer_output)
        final_rows, second_saved = mlp_forward(second_mid, second_gain, second_up, second_down)
        latent_outs.append(final_rows)
        record["latent_side"] = (
            allowed,
            latent_in,
            latent_normed,
            queries,
            row_top,
            row_total,
            attended,
            attended_low,
            first_mid,
            mixer_mid,
            second_mid,
            first_saved,
            mixer_saved,
            second_saved,
        )
        records.append(record)
    grads = {}
    latent_grads = []
    token_grads = []
    for member in range(MB):
        record = records[member]
        source, normed, key_rows, value_rows = record["token_side"]
        (
            allowed,
            latent_in,
            latent_normed,
            queries,
            row_top,
            row_total,
            attended,
            attended_low,
            first_mid,
            mixer_mid,
            second_mid,
            first_saved,
            mixer_saved,
            second_saved,
        ) = record["latent_side"]
        second_back = mlp_backward(
            second_mid, second_gain, second_up, second_down, second_saved, cotangent[0, member]
        )
        add_term(grads, "second_gain", second_back[1])
        add_term(grads, "second_up", second_back[2])
        add_term(grads, "second_down", second_back[3])
        mixer_back = mixer_backward(
            mixer_mid, mixer_gain, mixer_project, mixer_output, mixer_saved, second_back[0]
        )
        add_term(grads, "mixer_gain", mixer_back[1])
        add_term(grads, "mixer_project", mixer_back[2])
        add_term(grads, "mixer_output", mixer_back[3])
        first_back = mlp_backward(
            first_mid, first_gain, first_up, first_down, first_saved, mixer_back[0]
        )
        add_term(grads, "first_gain", first_back[1])
        add_term(grads, "first_up", first_back[2])
        add_term(grads, "first_down", first_back[3])
        latent_upstream = first_back[0]
        grad_low = latent_upstream.astype(jnp.bfloat16)
        add_term(grads, "output_weight", product_rows(attended_low, grad_low))
        attended_grad = lax.optimization_barrier(
            product_cols(grad_low, output_weight).astype(jnp.bfloat16)
        ).astype(jnp.float32)
        weighted_grad = (attended_grad / row_total[:, None]).astype(jnp.bfloat16)
        total_grad = -jnp.sum(attended_grad * attended, axis=1) / row_total
        weighted_every, total_every = (
            lax.all_gather(
                weighted_grad.astype(jnp.float32).astype(jnp.bfloat16), "tok", axis=0, tiled=True
            ).astype(jnp.float32),
            lax.all_gather(total_grad.astype(jnp.bfloat16), "tok", axis=0, tiled=True).astype(
                total_grad.dtype
            ),
        )
        weighted_every = weighted_every.astype(jnp.bfloat16)
        scores = jnp.where(allowed, product_cols(queries, key_rows) * scale, NEG)
        unnormed = jnp.exp(scores - row_top[:, None])
        unnormed_grad = product_cols(weighted_every, value_rows) + total_every[:, None]
        score_grad = (unnormed * unnormed_grad).astype(jnp.bfloat16)
        value_grad = product_rows(unnormed.astype(jnp.bfloat16), weighted_every).astype(
            jnp.bfloat16
        )
        key_grad = (product_rows(score_grad, queries) * scale).astype(jnp.bfloat16)
        query_grad = lax.psum_scatter(
            (product_plain(score_grad, key_rows) * scale).astype(jnp.bfloat16),
            "tok",
            scatter_dimension=0,
            tiled=True,
        )
        add_term(grads, "key_weight", product_rows(normed, key_grad))
        add_term(grads, "value_weight", product_rows(normed, value_grad))
        normed_grad = product_cols(key_grad, key_weight) + product_cols(value_grad, value_weight)
        source_grad, gain_grad = norm_back(source, token_gain, normed_grad)
        add_term(grads, "token_gain", gain_grad)
        token_grads.append(source_grad)
        add_term(grads, "query_weight", product_rows(latent_normed, query_grad))
        latent_grad, gain_grad = norm_back(
            latent_in, query_gain, product_cols(query_grad, query_weight)
        )
        add_term(grads, "query_gain", gain_grad)
        latent_grads.append(latent_upstream + latent_grad)
    parts = (
        lax.psum_scatter(
            grads["token_gain"].astype(jnp.bfloat16), "tok", scatter_dimension=0, tiled=True
        ).astype(jnp.float32),
        lax.psum_scatter(
            grads["query_gain"].astype(jnp.bfloat16), "tok", scatter_dimension=0, tiled=True
        ).astype(jnp.float32),
        lax.psum_scatter(
            grads["query_weight"].astype(jnp.bfloat16), "tok", scatter_dimension=0, tiled=True
        ).astype(jnp.float32),
        lax.psum_scatter(
            grads["key_weight"].astype(jnp.bfloat16), "tok", scatter_dimension=0, tiled=True
        ).astype(jnp.float32),
        lax.psum_scatter(
            grads["value_weight"].astype(jnp.bfloat16), "tok", scatter_dimension=0, tiled=True
        ).astype(jnp.float32),
        lax.psum_scatter(
            grads["output_weight"].astype(jnp.bfloat16), "tok", scatter_dimension=0, tiled=True
        ).astype(jnp.float32),
        lax.psum_scatter(
            grads["first_gain"].astype(jnp.bfloat16), "tok", scatter_dimension=0, tiled=True
        ).astype(jnp.float32),
        lax.psum_scatter(
            grads["first_up"].astype(jnp.bfloat16), "tok", scatter_dimension=0, tiled=True
        ).astype(jnp.float32),
        lax.psum_scatter(
            grads["first_down"].astype(jnp.bfloat16), "tok", scatter_dimension=0, tiled=True
        ).astype(jnp.float32),
        lax.psum_scatter(
            grads["mixer_gain"].astype(jnp.bfloat16), "tok", scatter_dimension=0, tiled=True
        ).astype(jnp.float32),
        lax.psum_scatter(
            grads["mixer_project"].astype(jnp.bfloat16), "tok", scatter_dimension=0, tiled=True
        ).astype(jnp.float32),
        lax.psum_scatter(
            grads["mixer_output"].astype(jnp.bfloat16), "tok", scatter_dimension=0, tiled=True
        ).astype(jnp.float32),
        lax.psum_scatter(
            grads["second_gain"].astype(jnp.bfloat16), "tok", scatter_dimension=0, tiled=True
        ).astype(jnp.float32),
        lax.psum_scatter(
            grads["second_up"].astype(jnp.bfloat16), "tok", scatter_dimension=0, tiled=True
        ).astype(jnp.float32),
        lax.psum_scatter(
            grads["second_down"].astype(jnp.bfloat16), "tok", scatter_dimension=0, tiled=True
        ).astype(jnp.float32),
    )
    summed = (
        lax.psum(parts[0].astype(jnp.bfloat16), "grp").astype(jnp.float32),
        lax.psum(parts[1].astype(jnp.bfloat16), "grp").astype(jnp.float32),
        lax.psum(parts[2].astype(jnp.bfloat16), "grp").astype(jnp.float32),
        lax.psum(parts[3].astype(jnp.bfloat16), "grp").astype(jnp.float32),
        lax.psum(parts[4].astype(jnp.bfloat16), "grp").astype(jnp.float32),
        lax.psum(parts[5].astype(jnp.bfloat16), "grp").astype(jnp.float32),
        lax.psum(parts[6].astype(jnp.bfloat16), "grp").astype(jnp.float32),
        lax.psum(parts[7].astype(jnp.bfloat16), "grp").astype(jnp.float32),
        lax.psum(parts[8].astype(jnp.bfloat16), "grp").astype(jnp.float32),
        lax.psum(parts[9].astype(jnp.bfloat16), "grp").astype(jnp.float32),
        lax.psum(parts[10].astype(jnp.bfloat16), "grp").astype(jnp.float32),
        lax.psum(parts[11].astype(jnp.bfloat16), "grp").astype(jnp.float32),
        lax.psum(parts[12].astype(jnp.bfloat16), "grp").astype(jnp.float32),
        lax.psum(parts[13].astype(jnp.bfloat16), "grp").astype(jnp.float32),
        lax.psum(parts[14].astype(jnp.bfloat16), "grp").astype(jnp.float32),
    )
    return (
        jnp.stack(latent_outs)[None],
        jnp.stack(latent_grads)[None],
        jnp.stack(token_grads)[None],
    ) + tuple(summed)


TOK = 8
ROWS = L // TOK
FF = 2048
GR = L // LGROUPS
LOG2E = 1.4426950408889634
LN2 = 0.6931471805599453
F32 = jnp.float32
BF16 = jnp.bfloat16
MIB = 1024 * 1024


def nn(left, right):
    return lax.dot_general(left, right, (((1,), (0,)), ((), ())), preferred_element_type=F32)


def nt(left, right):
    return lax.dot_general(left, right, (((1,), (1,)), ((), ())), preferred_element_type=F32)


def tn(left, right):
    return lax.dot_general(left, right, (((0,), (0,)), ((), ())), preferred_element_type=F32)


def norm_parts(values):
    centre = values - jnp.mean(values, axis=-1, keepdims=True)
    inverse = lax.rsqrt(jnp.mean(centre * centre, axis=-1, keepdims=True) + EPS)
    return centre * inverse, inverse


def norm_pull(hat, inverse, gain, upstream):
    scaled = upstream * gain
    inner = jnp.mean(scaled * hat, axis=-1, keepdims=True)
    grad = (scaled - jnp.mean(scaled, axis=-1, keepdims=True) - hat * inner) * inverse
    return grad, upstream * hat


def places():
    me = lax.axis_index("tok")
    core = lax.rem(me, 2)
    chip = lax.div(me, 2)
    mate = me + 1 - 2 * core
    flip_x = chip + 1 - 2 * lax.rem(chip, 2)
    flip_y = lax.rem(chip + 2, 4)
    far = 3 - chip
    return me, core, chip, mate, (far, flip_x, flip_y)


def remote(src, dst, send_sem, recv_sem, peer):
    return pltpu.make_async_remote_copy(
        src_ref=src,
        dst_ref=dst,
        send_sem=send_sem,
        recv_sem=recv_sem,
        device_id={"tok": peer},
        device_id_type=pl.DeviceIdType.MESH,
    )


def greet(devices):
    barrier = pltpu.get_barrier_semaphore()
    for device in devices:
        pl.semaphore_signal(
            barrier, inc=1, device_id={"tok": device}, device_id_type=pl.DeviceIdType.MESH
        )
    pl.semaphore_wait(barrier, len(devices))


def exchange_kernel(to_heads, src_ref, dst_ref, send_sem, recv_sem, local_sem):
    me, core, chip, mate, others = places()
    peers = []
    for other in others:
        peers += [2 * other + core, 2 * other + 1 - core]
    peers.append(mate)
    greet(peers)

    def ends(mine, device, member):
        rows_lane = pl.ds(member * ROWS, ROWS)
        if to_heads:
            source = src_ref.at[:, device, :, rows_lane]
            target = dst_ref.at[:, member, :, pl.ds(pl.multiple_of(mine * ROWS, ROWS), ROWS)]
        else:
            source = src_ref.at[:, member, :, pl.ds(pl.multiple_of(device * ROWS, ROWS), ROWS)]
            target = dst_ref.at[:, mine, :, rows_lane]
        return source, target

    copies = []
    for slot, peer in enumerate(peers):
        for member in range(MB):
            source, target = ends(me, peer, member)
            copies.append(remote(source, target, send_sem.at[slot, member], recv_sem.at[slot, member], peer))
            copies[-1].start()
    own = []
    for member in range(MB):
        source, target = ends(me, me, member)
        own.append(pltpu.make_async_copy(source, target, local_sem.at[member]))
        own[-1].start()
    for copy in own:
        copy.wait()
    for copy in copies:
        copy.wait()


def exchange(to_heads, collective_id, source):
    kinds = source.shape[0]
    shape = (kinds, MB, HD, L) if to_heads else (kinds, H, HD, MB * ROWS)
    dma = pltpu.SemaphoreType.DMA
    return pl.pallas_call(
        functools.partial(exchange_kernel, to_heads),
        in_specs=[pl.BlockSpec(memory_space=pl.ANY)],
        out_specs=pl.BlockSpec(memory_space=pl.ANY),
        out_shape=jax.ShapeDtypeStruct(shape, source.dtype),
        scratch_shapes=[dma((7, MB)), dma((7, MB)), dma((MB,))],
        compiler_params=pltpu.CompilerParams(collective_id=collective_id, has_side_effects=True),
        name="exchange",
    )(source)


def mixer_attend_kernel(all_ref, q_ref, mixed_ref, exact_ref, lse_ref, keys, values):
    @pl.when(pl.program_id(1) == 0)
    def _():
        keys[...] = all_ref[1, 0].T
        values[0:HD] = all_ref[2, 0]
        values[HD:] = jnp.ones((16, L), BF16)

    logits = nn(keys[...], q_ref[0, 0])
    top = jnp.max(logits, axis=0, keepdims=True)
    raised = jnp.exp2(logits - top).astype(BF16)
    both = nn(values[...], raised)
    total = both[HD:HD + 1]
    mixed = both[0:HD] / total
    exact_ref[0] = mixed
    mixed_ref[0, 0] = mixed.astype(BF16)
    lse = top + jnp.log2(total)
    lse_ref[0] = jnp.concatenate([lse, jnp.zeros((7, lse.shape[1]), F32)], axis=0)


QB = 256


def mixer_attend(packed):
    return pl.pallas_call(
        mixer_attend_kernel,
        grid=(MB, L // QB),
        in_specs=[
            pl.BlockSpec((3, 1, HD, L), lambda b, i: (0, b, 0, 0)),
            pl.BlockSpec((1, 1, HD, QB), lambda b, i: (0, b, 0, i)),
        ],
        out_specs=[
            pl.BlockSpec((1, 1, HD, QB), lambda b, i: (0, b, 0, i)),
            pl.BlockSpec((1, HD, QB), lambda b, i: (b, 0, i)),
            pl.BlockSpec((1, 8, QB), lambda b, i: (b, 0, i)),
        ],
        out_shape=[
            jax.ShapeDtypeStruct((1, MB, HD, L), BF16),
            jax.ShapeDtypeStruct((MB, HD, L), F32),
            jax.ShapeDtypeStruct((MB, 8, L), F32),
        ],
        scratch_shapes=[pltpu.VMEM((L, HD), BF16), pltpu.VMEM((HD + 16, L), BF16)],
        compiler_params=pltpu.CompilerParams(
            dimension_semantics=("arbitrary", "arbitrary"), vmem_limit_bytes=48 * MIB
        ),
        cost_estimate=pl.CostEstimate(
            flops=9 * 10**9, bytes_accessed=4 * 10**6, transcendentals=8 * 10**6
        ),
        name="mixer_attend",
    )(packed, packed)


def mixer_attend_back_kernel(all_ref, q_ref, up_ref, exact_ref, lse_ref, out_ref, keys, values, key_acc, value_acc):
    step = pl.program_id(1)

    @pl.when(step == 0)
    def _():
        keys[...] = all_ref[1, 0].T
        values[...] = all_ref[2, 0].T
        key_acc[...] = jnp.zeros_like(key_acc)
        value_acc[...] = jnp.zeros_like(value_acc)

    queries = q_ref[0, 0]
    upstream = up_ref[0, 0]
    inner = jnp.sum(upstream.astype(F32) * exact_ref[0], axis=0, keepdims=True)
    softened = jnp.exp2(nn(keys[...], queries) - lse_ref[0][0:1])
    soft_grad = nn(values[...], upstream)
    logit_grad = (softened * (soft_grad - inner)).astype(BF16)
    value_acc[...] += nt(upstream, softened.astype(BF16))
    key_acc[...] += nt(queries, logit_grad)
    query_grad = nn(all_ref[1, 0], logit_grad) * HD ** (-0.5)
    out_ref[0, 0, :, pl.ds(pl.multiple_of(step * QB, QB), QB)] = query_grad.astype(BF16)

    @pl.when(step == L // QB - 1)
    def _():
        out_ref[1, 0] = (key_acc[...] * LN2).astype(BF16)
        out_ref[2, 0] = value_acc[...].astype(BF16)


def mixer_attend_back(packed, upstream, exact, lse):
    return pl.pallas_call(
        mixer_attend_back_kernel,
        grid=(MB, L // QB),
        in_specs=[
            pl.BlockSpec((3, 1, HD, L), lambda b, i: (0, b, 0, 0)),
            pl.BlockSpec((1, 1, HD, QB), lambda b, i: (0, b, 0, i)),
            pl.BlockSpec((1, 1, HD, QB), lambda b, i: (0, b, 0, i)),
            pl.BlockSpec((1, HD, QB), lambda b, i: (b, 0, i)),
            pl.BlockSpec((1, 8, QB), lambda b, i: (b, 0, i)),
        ],
        out_specs=pl.BlockSpec((3, 1, HD, L), lambda b, i: (0, b, 0, 0)),
        out_shape=jax.ShapeDtypeStruct((3, MB, HD, L), BF16),
        scratch_shapes=[
            pltpu.VMEM((L, HD), BF16),
            pltpu.VMEM((L, HD), BF16),
            pltpu.VMEM((HD, L), F32),
            pltpu.VMEM((HD, L), F32),
        ],
        compiler_params=pltpu.CompilerParams(
            dimension_semantics=("arbitrary", "arbitrary"), vmem_limit_bytes=48 * MIB
        ),
        cost_estimate=pl.CostEstimate(
            flops=22 * 10**9, bytes_accessed=5 * 10**6, transcendentals=8 * 10**6
        ),
        name="mixer_attend_back",
    )(packed, packed, upstream, exact, lse)


def chip_at(chip, flip):
    across = lax.rem(lax.rem(chip, 2) + lax.rem(flip, 2), 2)
    along = lax.rem(lax.div(chip, 2) + lax.div(flip, 2), 2)
    return 2 * along + across


def mask_rows(seg_ref, mask_ref, count_ref, bias_ref):
    for member in range(MB):
        scene = lax.broadcasted_iota(jnp.int32, (SCENES, TOK_DEV), 0)
        place = lax.broadcasted_iota(jnp.int32, (SCENES, TOK_DEV), 1)
        hot = jnp.where((seg_ref[member] == scene) & (place < count_ref[member]), 1.0, 0.0)
        seen = tn(jnp.where(mask_ref[member] > 0, 1.0, 0.0).astype(BF16), hot.astype(BF16))
        bias_ref[member] = jnp.where(seen > 0.5, 0.0, NEG)


def to_rows(first, second):
    rows = first.shape[0]
    lane = lax.broadcasted_iota(jnp.int32, (rows, 128), 1)
    return jnp.where(lane == 0, first, second).T[0:8]


def cross_forward_kernel(
    tok_ref, lat_ref, tgain_ref, qgain_ref, qw_ref, kw_ref, vw_ref, seg_ref, mask_ref, count_ref,
    k_out, v_out, q_out, att_ref, lse_ref,
    tok_buf, lat_buf, keys, values, queries, bias, part, part_s, got, got_s, stage, stage_s,
    arrive, arrive_s, total,
    tok_sem, lat_sem, k_sem, v_sem, q_sem,
    core_send, core_recv, core_send_s, core_recv_s, chip_send, chip_recv, chip_send_s, chip_recv_s,
):
    me, core, chip, mate, others = places()
    span = 2 * ROWS

    def unpack(step):
        return lax.div(step, 4), 3 - lax.rem(step, 4)

    def lat_copy(step):
        member, flip = unpack(step)
        start = pl.multiple_of(chip_at(chip, flip) * span, span)
        return pltpu.make_async_copy(lat_ref.at[0, member, pl.ds(start, span)], lat_buf.at[step], lat_sem.at[step])

    def q_copy(step):
        member, flip = unpack(step)
        start = pl.multiple_of(chip_at(chip, flip) * span, span)
        return pltpu.make_async_copy(queries.at[step], q_out.at[member, pl.ds(start, span)], q_sem.at[step])

    def tok_copy(member):
        return pltpu.make_async_copy(tok_ref.at[0, member], tok_buf.at[member], tok_sem.at[member])

    def kv_copies(member):
        return (
            pltpu.make_async_copy(keys.at[member], k_out.at[member], k_sem.at[member]),
            pltpu.make_async_copy(values.at[member], v_out.at[member], v_sem.at[member]),
        )

    def core_copies(step):
        return (
            remote(part.at[step, 1 - core], got.at[step], core_send.at[step], core_recv.at[step], mate),
            remote(part_s.at[step, 1 - core], got_s.at[step], core_send_s.at[step], core_recv_s.at[step], mate),
        )

    def chip_copies(step):
        member, flip = unpack(step)
        peer = 2 * chip_at(chip, flip) + core
        place = 3 * member + flip - 1
        return (
            remote(stage.at[step], arrive.at[place], chip_send.at[place], chip_recv.at[place], peer),
            remote(stage_s.at[step], arrive_s.at[place], chip_send_s.at[place], chip_recv_s.at[place], peer),
        )

    for member in range(MB):
        tok_copy(member).start()
    for step in range(2 * 4):
        lat_copy(step).start()
    greet([mate] + [2 * other + core for other in others])
    mask_rows(seg_ref, mask_ref, count_ref, bias)

    def compute(step):
        member, flip = unpack(step)

        @pl.when(flip == 3)
        def _():
            tok_copy(member).wait()
            hat, inverse = norm_parts(tok_buf[member].astype(F32))
            normed = (hat * tgain_ref[...]).astype(BF16)
            keys[member] = nn(normed, kw_ref[...]).astype(BF16)
            values[member] = nn(normed, vw_ref[...]).astype(BF16)
            for copy in kv_copies(member):
                copy.start()

        lat_copy(step).wait()
        hat, inverse = norm_parts(lat_buf[step])
        normed = (hat * qgain_ref[...]).astype(BF16)
        asked = (nn(normed, qw_ref[...]) * (D ** (-0.5) * LOG2E)).astype(BF16)
        queries[step] = asked
        q_copy(step).start()
        scores = nt(asked, keys[member])
        raised = []
        for half in range(2):
            seen = bias[member, pl.ds(2 * chip_at(chip, flip) + half, 1), :]
            own = scores[half * ROWS:(half + 1) * ROWS] + seen
            top = jnp.max(own, axis=1, keepdims=True)
            own = jnp.exp2(own - top)
            part_s[step, half] = to_rows(top, jnp.sum(own, axis=1, keepdims=True))
            raised.append(own.astype(BF16))
        sums = nn(jnp.concatenate(raised, axis=0), values[member]).astype(BF16)
        for half in range(2):
            part[step, half] = sums[half * ROWS:(half + 1) * ROWS]
        for copy in core_copies(step):
            copy.start()

    def merge(one, one_s, two, two_s):
        top = jnp.maximum(one_s[0:1], two_s[0:1])
        one_w, two_w = jnp.exp2(one_s[0:1] - top), jnp.exp2(two_s[0:1] - top)
        sums = one_s[1:2] * one_w + two_s[1:2] * two_w
        spare = jnp.zeros((6, ROWS), F32)
        weights = jnp.concatenate([one_w, two_w, spare], axis=0).T
        return one * weights[:, 0:1] + two * weights[:, 1:2], jnp.concatenate([top, sums, spare], axis=0)

    def combine(step):
        member, flip = unpack(step)
        for copy in core_copies(step):
            copy.wait_recv()
        added, figures = merge(
            part[step, core].astype(F32), part_s[step, core], got[step].astype(F32), got_s[step]
        )
        stage_s[step] = figures

        @pl.when(flip > 0)
        def _():
            stage[step] = added.astype(BF16)
            for copy in chip_copies(step):
                copy.start()

        @pl.when(flip == 0)
        def _():
            total[member] = added

    def finish(member):
        added, figures = total[member], stage_s[4 * member + 3]
        for flip in (1, 2, 3):
            for copy in chip_copies(4 * member + 3 - flip):
                copy.wait_recv()
            place = 3 * member + flip - 1
            added, figures = merge(added, figures, arrive[place].astype(F32), arrive_s[place])
        spare = jnp.zeros((7, ROWS), F32)
        inverse = jnp.concatenate([1.0 / figures[1:2], spare], axis=0).T
        att_ref[member] = added * inverse[:, 0:1]
        lse_ref[member] = jnp.concatenate([figures[0:1] + jnp.log2(figures[1:2]), spare], axis=0)

    def step_body(step, carry):
        compute(step)

        @pl.when(step > 0)
        def _():
            combine(step - 1)

        return carry

    lax.fori_loop(0, 4 * MB, step_body, 0)
    combine(jnp.int32(4 * MB - 1))
    for member in range(MB):
        finish(member)
    for member in range(MB):
        for copy in kv_copies(member):
            copy.wait()
        for slot in range(4):
            step = 4 * member + slot
            q_copy(step).wait()
            for copy in core_copies(step):
                copy.wait_send()
            if slot < 3:
                for copy in chip_copies(step):
                    copy.wait_send()


def cross_forward(collective_id, *args):
    dma = pltpu.SemaphoreType.DMA
    span = 2 * ROWS
    steps = 4 * MB
    vmem = pl.BlockSpec(memory_space=pltpu.VMEM)
    hbm = pl.BlockSpec(memory_space=pl.ANY)
    return pl.pallas_call(
        cross_forward_kernel,
        in_specs=[hbm, hbm] + [vmem] * 8,
        out_specs=[hbm, hbm, hbm, vmem, vmem],
        out_shape=[
            jax.ShapeDtypeStruct((MB, TOK_DEV, D), BF16),
            jax.ShapeDtypeStruct((MB, TOK_DEV, D), BF16),
            jax.ShapeDtypeStruct((MB, L, D), BF16),
            jax.ShapeDtypeStruct((MB, ROWS, D), F32),
            jax.ShapeDtypeStruct((MB, 8, ROWS), F32),
        ],
        scratch_shapes=[
            pltpu.VMEM((MB, TOK_DEV, D), BF16),
            pltpu.VMEM((steps, span, D), F32),
            pltpu.VMEM((MB, TOK_DEV, D), BF16),
            pltpu.VMEM((MB, TOK_DEV, D), BF16),
            pltpu.VMEM((steps, span, D), BF16),
            pltpu.VMEM((MB, LGROUPS, TOK_DEV), F32),
            pltpu.VMEM((steps, 2, ROWS, D), BF16),
            pltpu.VMEM((steps, 2, 8, ROWS), F32),
            pltpu.VMEM((steps, ROWS, D), BF16),
            pltpu.VMEM((steps, 8, ROWS), F32),
            pltpu.VMEM((steps, ROWS, D), BF16),
            pltpu.VMEM((steps, 8, ROWS), F32),
            pltpu.VMEM((3 * MB, ROWS, D), BF16),
            pltpu.VMEM((3 * MB, 8, ROWS), F32),
            pltpu.VMEM((MB, ROWS, D), F32),
            dma((MB,)), dma((steps,)), dma((MB,)), dma((MB,)), dma((steps,)),
        ] + [dma((steps,))] * 4 + [dma((3 * MB,))] * 4,
        compiler_params=pltpu.CompilerParams(
            collective_id=collective_id, has_side_effects=True, vmem_limit_bytes=56 * MIB
        ),
        cost_estimate=pl.CostEstimate(
            flops=14 * 10**9, bytes_accessed=22 * 10**6, transcendentals=4 * 10**6
        ),
        name="cross_forward",
    )(*args)


def cross_backward_kernel(
    tok_ref, tgain_ref, kw_ref, vw_ref, seg_ref, mask_ref, count_ref, k_ref, v_ref, q_ref, up_ref, fig_ref,
    dq_ref, dtok_ref, dkw_ref, dvw_ref, dgain_ref,
    tok_buf, keys, values, queries, ups, figs, bias, part, got, stage, arrive, total, dk, dv, dtok, dkw, dvw,
    tok_sem, k_sem, v_sem, q_sem, out_sem, near_send, near_recv, far_send, far_recv, on_send, on_recv, own_sem,
    core_send, core_recv, chip_send, chip_recv,
):
    me, core, chip, mate, others = places()
    span = 2 * ROWS

    def slot_of(step):
        member, place = lax.div(step, 4), lax.rem(step, 4)
        return member, place + member * (3 - 2 * place)

    def loads(slot):
        member, flip = divmod(slot, 4)
        start = pl.multiple_of(chip_at(chip, flip) * span, span)
        return pltpu.make_async_copy(q_ref.at[member, pl.ds(start, span)], queries.at[slot], q_sem.at[slot])

    def tok_copies(member):
        return (
            pltpu.make_async_copy(k_ref.at[member], keys.at[member], k_sem.at[member]),
            pltpu.make_async_copy(v_ref.at[member], values.at[member], v_sem.at[member]),
            pltpu.make_async_copy(tok_ref.at[0, member], tok_buf.at[member], tok_sem.at[member]),
        )

    def out_copy(member):
        return pltpu.make_async_copy(dtok.at[member], dtok_ref.at[0, member], out_sem.at[member])

    def own_copies(member):
        slot = 4 * member
        return (
            pltpu.make_async_copy(up_ref.at[member], ups.at[slot, core], own_sem.at[member, 0]),
            pltpu.make_async_copy(fig_ref.at[member], figs.at[slot, core], own_sem.at[member, 1]),
        )

    def near_copies(member):
        slot = 4 * member
        return (
            remote(up_ref.at[member], ups.at[slot, core], near_send.at[member, 0], near_recv.at[member, 0], mate),
            remote(fig_ref.at[member], figs.at[slot, core], near_send.at[member, 1], near_recv.at[member, 1], mate),
        )

    def far_copies(slot):
        member, flip = slot // 4, slot % 4
        peer = 2 * chip_at(chip, flip) + core
        return (
            remote(up_ref.at[member], ups.at[slot, core], far_send.at[slot, 0], far_recv.at[slot, 0], peer),
            remote(fig_ref.at[member], figs.at[slot, core], far_send.at[slot, 1], far_recv.at[slot, 1], peer),
        )

    def on_copies(slot):
        return (
            remote(ups.at[slot, core], ups.at[slot, core], on_send.at[slot, 0], on_recv.at[slot, 0], mate),
            remote(figs.at[slot, core], figs.at[slot, core], on_send.at[slot, 1], on_recv.at[slot, 1], mate),
        )

    def pass_on(slot):
        for copy in far_copies(slot):
            copy.wait_recv()
        for copy in on_copies(slot):
            copy.start()

    def core_copy(slot):
        return remote(part.at[slot, 1 - core], got.at[slot], core_send.at[slot], core_recv.at[slot], mate)

    def chip_copy(slot):
        member, flip = lax.div(slot, 4), lax.rem(slot, 4)
        peer = 2 * chip_at(chip, flip) + core
        place = 3 * member + flip - 1
        return remote(stage.at[slot], arrive.at[place], chip_send.at[place], chip_recv.at[place], peer)

    for copy in own_copies(0):
        copy.start()
    for copy in tok_copies(0):
        copy.start()
    for flip in (0, 1, 2, 3):
        loads(flip).start()
    for copy in own_copies(1):
        copy.start()
    for copy in tok_copies(1):
        copy.start()
    for flip in (3, 2, 1, 0):
        loads(4 + flip).start()
    greet([mate] + [2 * other + core for other in others])
    for member in range(MB):
        for copy in near_copies(member):
            copy.start()
        for flip in ((1, 2, 3) if member == 0 else (3, 2, 1)):
            for copy in far_copies(4 * member + flip):
                copy.start()
    mask_rows(seg_ref, mask_ref, count_ref, bias)

    def compute(step):
        member, flip = slot_of(step)
        slot = 4 * member + flip

        @pl.when(lax.rem(step, 4) == 0)
        def _():
            for copy in tok_copies(member):
                copy.wait()
            dk[...] = jnp.zeros_like(dk)
            dv[...] = jnp.zeros_like(dv)

        start = pl.multiple_of(chip_at(chip, flip) * span, span)
        pltpu.make_async_copy(q_ref.at[member, pl.ds(start, span)], queries.at[slot], q_sem.at[slot]).wait()

        @pl.when(flip == 0)
        def _():
            for copy in own_copies(member):
                copy.wait()
            for copy in near_copies(member):
                copy.wait_recv()

        @pl.when(flip > 0)
        def _():
            for copy in on_copies(slot):
                copy.wait_recv()

        asked = queries[slot]
        upstream = ups[slot].reshape(span, D)
        scores = nt(asked, keys[member])
        soft = nt(upstream, values[member])
        weights, grads = [], []
        for half in range(2):
            seen = bias[member, pl.ds(2 * chip_at(chip, flip) + half, 1), :]
            figures = figs[slot, half].T
            rows = slice(half * ROWS, (half + 1) * ROWS)
            weight = jnp.exp2(scores[rows] + seen - figures[:, 0:1])
            grads.append((weight * (soft[rows] - figures[:, 1:2])).astype(BF16))
            weights.append(weight.astype(BF16))
        weight = jnp.concatenate(weights, axis=0)
        grad = jnp.concatenate(grads, axis=0)
        dv[...] += tn(weight, upstream)
        dk[...] += tn(grad, asked)
        asked_grad = (nn(grad, keys[member]) * D ** (-0.5)).astype(BF16)
        for half in range(2):
            part[slot, half] = asked_grad[half * ROWS:(half + 1) * ROWS]
        core_copy(slot).start()

    def combine(step):
        member, flip = slot_of(step)
        slot = 4 * member + flip
        core_copy(slot).wait_recv()
        added = part[slot, core].astype(F32) + got[slot].astype(F32)

        @pl.when(flip > 0)
        def _():
            stage[slot] = added.astype(BF16)
            chip_copy(slot).start()

        @pl.when(flip == 0)
        def _():
            total[member] = added

    def tokens_back(member):
        gain = tgain_ref[...]
        hat, inverse = norm_parts(tok_buf[member].astype(F32))
        normed = (hat * gain).astype(BF16)
        key_grad = (dk[...] * LN2).astype(BF16)
        value_grad = dv[...].astype(BF16)
        key_term = tn(normed, key_grad)
        value_term = tn(normed, value_grad)
        normed_grad = nt(key_grad, kw_ref[...]) + nt(value_grad, vw_ref[...])
        source_grad, gain_rows = norm_pull(hat, inverse, gain, normed_grad)
        dtok[member] = source_grad
        out_copy(member).start()
        gain_term = jnp.sum(gain_rows, axis=0, keepdims=True)

        @pl.when(member == 0)
        def _():
            dkw[...] = key_term
            dvw[...] = value_term
            dgain_ref[...] = gain_term

        @pl.when(member > 0)
        def _():
            dkw_ref[...] = (dkw[...] + key_term).astype(BF16)
            dvw_ref[...] = (dvw[...] + value_term).astype(BF16)
            dgain_ref[...] += gain_term

    def step_body(step, carry):
        compute(step)

        @pl.when(step > 0)
        def _():
            combine(step - 1)

        @pl.when(step == 0)
        def _():
            pass_on(1)
            pass_on(2)

        @pl.when(step == 1)
        def _():
            pass_on(3)

        @pl.when(step == 3)
        def _():
            pass_on(7)
            pass_on(6)

        @pl.when(step == 4)
        def _():
            pass_on(5)

        @pl.when(step == 4 * MB - 1)
        def _():
            combine(step)

        @pl.when(lax.rem(step, 4) == 3)
        def _():
            tokens_back(lax.div(step, 4))

        return carry

    lax.fori_loop(0, 4 * MB, step_body, 0)
    for member in range(MB):
        added = total[member]
        for flip in (1, 2, 3):
            chip_copy(4 * member + flip).wait_recv()
            added = added + arrive[3 * member + flip - 1].astype(F32)
        dq_ref[member] = added.astype(BF16)
    for member in range(MB):
        out_copy(member).wait()
        for copy in near_copies(member):
            copy.wait_send()
        for flip in range(4):
            slot = 4 * member + flip
            core_copy(slot).wait_send()
            if flip > 0:
                chip_copy(slot).wait_send()
                for copy in far_copies(slot) + on_copies(slot):
                    copy.wait_send()


def cross_backward(collective_id, *args):
    dma = pltpu.SemaphoreType.DMA
    span = 2 * ROWS
    steps = 4 * MB
    vmem = pl.BlockSpec(memory_space=pltpu.VMEM)
    hbm = pl.BlockSpec(memory_space=pl.ANY)
    return pl.pallas_call(
        cross_backward_kernel,
        in_specs=[hbm] + [vmem] * 6 + [hbm] * 5,
        out_specs=[vmem, hbm, vmem, vmem, vmem],
        out_shape=[
            jax.ShapeDtypeStruct((MB, ROWS, D), BF16),
            jax.ShapeDtypeStruct((1, MB, TOK_DEV, D), F32),
            jax.ShapeDtypeStruct((D, D), BF16),
            jax.ShapeDtypeStruct((D, D), BF16),
            jax.ShapeDtypeStruct((1, D), F32),
        ],
        scratch_shapes=[
            pltpu.VMEM((MB, TOK_DEV, D), BF16),
            pltpu.VMEM((MB, TOK_DEV, D), BF16),
            pltpu.VMEM((MB, TOK_DEV, D), BF16),
            pltpu.VMEM((steps, span, D), BF16),
            pltpu.VMEM((steps, 2, ROWS, D), BF16),
            pltpu.VMEM((steps, 2, 8, ROWS), F32),
            pltpu.VMEM((MB, LGROUPS, TOK_DEV), F32),
            pltpu.VMEM((steps, 2, ROWS, D), BF16),
            pltpu.VMEM((steps, ROWS, D), BF16),
            pltpu.VMEM((steps, ROWS, D), BF16),
            pltpu.VMEM((3 * MB, ROWS, D), BF16),
            pltpu.VMEM((MB, ROWS, D), F32),
            pltpu.VMEM((TOK_DEV, D), F32),
            pltpu.VMEM((TOK_DEV, D), F32),
            pltpu.VMEM((MB, TOK_DEV, D), F32),
            pltpu.VMEM((D, D), F32),
            pltpu.VMEM((D, D), F32),
            dma((MB,)), dma((MB,)), dma((MB,)), dma((steps,)), dma((MB,)),
            dma((MB, 2)), dma((MB, 2)), dma((steps, 2)), dma((steps, 2)), dma((steps, 2)), dma((steps, 2)), dma((MB, 2)),
            dma((steps,)), dma((steps,)), dma((3 * MB,)), dma((3 * MB,)),
        ],
        compiler_params=pltpu.CompilerParams(
            collective_id=collective_id, has_side_effects=True, vmem_limit_bytes=58 * MIB
        ),
        cost_estimate=pl.CostEstimate(
            flops=26 * 10**9, bytes_accessed=24 * 10**6, transcendentals=4 * 10**6
        ),
        name="cross_backward",
    )(*args)


def reduce_kernel(items, count, *refs):
    n = len(items)
    sources, outs, scratch = refs[:count], refs[count:2 * count], refs[2 * count:]
    mine, got, first_in, second_in, z_keep, z_first, z_second = [scratch[i * n:(i + 1) * n] for i in range(7)]
    (local_sem, core_send, core_recv, one_send, one_recv, two_send, two_recv, z_send, z_recv) = scratch[7 * n:]
    me, core, chip, mate, (far, flip_x, flip_y) = places()
    x, y = lax.rem(chip, 2), lax.div(chip, 2)
    level = lax.axis_index("grp")
    odd = lax.rem(level, 2)
    level_near = level + 1 - 2 * odd
    level_far = lax.rem(level + 2, 4)
    barrier = pltpu.get_barrier_semaphore()
    for device in (mate, 2 * flip_x + core, 2 * flip_y + core):
        pl.semaphore_signal(barrier, inc=1, device_id={"tok": device}, device_id_type=pl.DeviceIdType.MESH)
    for other in (level_near, level_far):
        pl.semaphore_signal(barrier, inc=1, device_id={"grp": other}, device_id_type=pl.DeviceIdType.MESH)
    pl.semaphore_wait(barrier, 5)

    def along(item, src, dst, step, other):
        return pltpu.make_async_remote_copy(
            src_ref=src, dst_ref=dst, send_sem=z_send.at[item, step], recv_sem=z_recv.at[item, step],
            device_id={"grp": other}, device_id_type=pl.DeviceIdType.MESH,
        )

    sent, cores, ones, twos, zs = [], {}, {}, {}, {}

    def add(target, one, two):
        target[...] = (one[...].astype(F32) + two[...].astype(F32)).astype(target.dtype)

    def core_sends(i):
        source, rows, row_at, columns, column_at, x_first = items[i]
        part = (pl.ds(row_at, rows), pl.ds(column_at, columns))
        there = remote(sources[source].at[:, :, 1 - core, *part], got[i], core_send.at[i], core_recv.at[i], mate)
        here = pltpu.make_async_copy(sources[source].at[:, :, core, *part], mine[i], local_sem.at[i])
        there.start()
        here.start()
        cores[i] = (there, here)
        sent.append(there)

    def core_sums(i):
        there, here = cores[i]
        there.wait_recv()
        here.wait()
        add(mine[i], mine[i], got[i])
        x_first = items[i][-1]
        away = mine[i].at[:, 1 - x] if x_first else mine[i].at[1 - y]
        peer = 2 * (flip_x if x_first else flip_y) + core
        ones[i] = remote(away, first_in[i], one_send.at[i], one_recv.at[i], peer)
        ones[i].start()
        sent.append(ones[i])

    def first_sums(i):
        x_first = items[i][-1]
        ones[i].wait_recv()
        keep = mine[i].at[:, x] if x_first else mine[i].at[y]
        add(keep, keep, first_in[i])
        away = mine[i].at[1 - y, x] if x_first else mine[i].at[y, 1 - x]
        peer = 2 * (flip_y if x_first else flip_x) + core
        twos[i] = remote(away, second_in[i], two_send.at[i], two_recv.at[i], peer)
        twos[i].start()
        sent.append(twos[i])

    def halves(i):
        half = items[i][1] // 2
        keep = pl.ds(pl.multiple_of(odd * half, half), half)
        away = pl.ds(pl.multiple_of((1 - odd) * half, half), half)
        return keep, away

    def second_sums(i):
        keep, away = halves(i)
        twos[i].wait_recv()
        add(mine[i].at[y, x], mine[i].at[y, x], second_in[i])
        zs[i, 0] = along(i, mine[i].at[y, x, away], z_first[i], 0, level_near)
        zs[i, 0].start()
        sent.append(zs[i, 0])

    def grp_first(i):
        keep, away = halves(i)
        zs[i, 0].wait_recv()
        add(z_keep[i].at[0], mine[i].at[y, x, keep], z_first[i])
        zs[i, 1] = along(i, z_keep[i].at[0], z_second[i].at[0], 1, level_far)
        zs[i, 1].start()
        sent.append(zs[i, 1])

    def store(i, odd_half, value):
        source, rows, row_at, columns, column_at, x_first = items[i]
        half = rows // 2
        start = pl.multiple_of(row_at + odd_half * half, half)
        outs[source][pl.ds(start, half), pl.ds(column_at, columns)] = value.astype(F32)

    def grp_second(i):
        zs[i, 1].wait_recv()
        add(z_keep[i].at[1], z_keep[i].at[0], z_second[i].at[0])
        zs[i, 2] = along(i, z_keep[i].at[1], z_second[i].at[1], 2, level_near)
        zs[i, 2].start()
        sent.append(zs[i, 2])
        store(i, odd, z_keep[i][1])

    def grp_third(i):
        zs[i, 2].wait_recv()
        store(i, 1 - odd, z_second[i][1])

    stages = (core_sends, core_sums, first_sums, second_sums, grp_first, grp_second, grp_third)
    lags = (0, 2, 4, 5, 6, 7, 8)
    for step in range(n + lags[-1]):
        for stage, lag in zip(stages, lags):
            if 0 <= step - lag < n:
                stage(step - lag)
    for copy in sent:
        copy.wait_send()


def reduce_grads(collective_id, arrays, cuts):
    sources, items = [], []
    for source, (array, cut) in enumerate(zip(arrays, cuts)):
        rows, columns = array.shape[0] // TOK, array.shape[1]
        sources.append(array.reshape(2, 2, 2, rows, columns))
        parts = abs(cut)
        for part in range(parts):
            high, wide = (rows, columns // parts) if cut > 0 else (rows // parts, columns)
            row_at, column_at = (0, part * wide) if cut > 0 else (part * high, 0)
            items.append((source, high, row_at, wide, column_at, len(items) % 2 == 0))
    n = len(items)
    dma = pltpu.SemaphoreType.DMA
    blocks = lambda lead, part: [
        pltpu.VMEM(lead + (item[1] // part, item[3]), arrays[item[0]].dtype) for item in items
    ]
    return pl.pallas_call(
        functools.partial(reduce_kernel, tuple(items), len(arrays)),
        in_specs=[pl.BlockSpec(memory_space=pl.ANY)] * len(arrays),
        out_specs=[pl.BlockSpec(memory_space=pltpu.VMEM)] * len(arrays),
        out_shape=[jax.ShapeDtypeStruct((array.shape[0] // TOK, array.shape[1]), F32) for array in arrays],
        scratch_shapes=blocks((2, 2), 1) + blocks((2, 2), 1) + blocks((2,), 1) + blocks((), 1)
        + blocks((2,), 2) + blocks((), 2) + blocks((2,), 2)
        + [dma((n,)) for unused in range(7)] + [dma((n, 3)), dma((n, 3))],
        compiler_params=pltpu.CompilerParams(
            collective_id=collective_id, has_side_effects=True, vmem_limit_bytes=56 * MIB
        ),
        name="reduce_grads",
    )(*sources)


def reduce_early(columns, rows):
    each = rows.shape[0] // TOK
    short = D // TOK
    side = rows.reshape(TOK, each // short, short, D).transpose(0, 2, 1, 3).reshape(D, FF)
    both = jnp.concatenate([columns, side], axis=1)
    part = lax.psum_scatter(both, "tok", scatter_dimension=0, tiled=True)
    return part


def finish_early(part, width):
    each, short = FF // TOK, D // TOK
    part = lax.psum(part, "grp").astype(F32)
    side = part[:, width:].reshape(short, each // short, D).transpose(1, 0, 2).reshape(each, D)
    return part, side


def fast_body(
    tokens,
    latents,
    segments,
    scene_mask,
    counts,
    token_gain,
    query_gain,
    query_weight,
    key_weight,
    value_weight,
    output_weight,
    first_gain,
    first_up,
    first_down,
    mixer_gain,
    mixer_project,
    mixer_output,
    second_gain,
    second_up,
    second_down,
    cotangent,
):
    me = lax.axis_index("tok")
    scenes = (segments[0][:, None], scene_mask[0], counts[0][:, :, None])
    keys, values, queries, attended, lse = cross_forward(
        0, tokens, latents, token_gain[None], query_gain[None], query_weight, key_weight, value_weight, *scenes
    )
    attended = attended.reshape(MB * ROWS, D)
    latent_in = lax.dynamic_slice_in_dim(latents[0], me * ROWS, ROWS, 1).reshape(MB * ROWS, D)

    attended_low = attended.astype(BF16)
    first_mid = latent_in + nn(attended_low, output_weight)
    mixer_mid, first_saved = mlp_forward(first_mid, first_gain, first_up, first_down)

    mixer_normed = norm_rows(mixer_mid, mixer_gain).astype(BF16)
    packed = lax.dot_general(
        mixer_project, mixer_normed, (((0,), (1,)), ((), ())), preferred_element_type=F32
    ).reshape(3, D, MB * ROWS)
    packed = packed * jnp.array([HD ** (-0.5) * LOG2E, 1.0, 1.0], F32)[:, None, None]
    packed = packed.astype(BF16).reshape(3, H, HD, MB * ROWS)
    head_packed = exchange(True, 1, packed)
    head_mixed, head_exact, head_lse = mixer_attend(head_packed)
    mixed = exchange(False, 2, head_mixed).reshape(D, MB * ROWS)
    second_mid = mixer_mid + tn(mixed, mixer_output)
    final_rows, second_saved = mlp_forward(second_mid, second_gain, second_up, second_down)

    upstream = cotangent.reshape(MB * ROWS, D)
    upstream, d_second_gain, d_second_up, d_second_down = mlp_backward(
        second_mid, second_gain, second_up, second_down, second_saved, upstream
    )
    grad_low = upstream.astype(BF16)
    d_mixer_output = nn(mixed, grad_low)
    early = reduce_early(
        jnp.concatenate([d_second_up.astype(BF16), d_mixer_output.astype(BF16)], axis=1),
        d_second_down.astype(BF16),
    )
    mixed_grad = nt(mixer_output, grad_low).astype(BF16).reshape(1, H, HD, MB * ROWS)
    head_grad = mixer_attend_back(head_packed, exchange(True, 3, mixed_grad), head_exact, head_lse)
    packed_grad = exchange(False, 4, head_grad).reshape(3 * D, MB * ROWS)
    d_mixer_project = lax.dot_general(
        mixer_normed, packed_grad, (((0,), (1,)), ((), ())), preferred_element_type=F32
    )
    normed_grad = lax.dot_general(
        packed_grad, mixer_project, (((0,), (1,)), ((), ())), preferred_element_type=F32
    )
    residual_grad, d_mixer_gain = norm_back(mixer_mid, mixer_gain, normed_grad)
    upstream, d_first_gain, d_first_up, d_first_down = mlp_backward(
        first_mid, first_gain, first_up, first_down, first_saved, upstream + residual_grad
    )
    grad_low = upstream.astype(BF16)
    d_output = tn(attended_low, grad_low)
    attended_grad = nt(grad_low, output_weight).astype(BF16)
    inner = jnp.sum(attended_grad.astype(F32) * attended, axis=1).reshape(MB, ROWS)
    figures = jnp.concatenate(
        [lse[:, 0:1], inner[:, None], jnp.zeros((MB, 6, ROWS), F32)], axis=1
    )
    attended_grad, early = lax.optimization_barrier((attended_grad, early))
    early, o_second_down = finish_early(early, FF + D)
    query_grad, tokens_grad, d_key, d_value, d_token_gain = cross_backward(
        5, tokens, token_gain[None], key_weight, value_weight, *scenes, keys, values, queries,
        attended_grad.reshape(MB, ROWS, D), figures,
    )
    query_grad = query_grad.reshape(MB * ROWS, D)
    latent_normed = norm_rows(latent_in, query_gain).astype(BF16)
    d_query = tn(latent_normed, query_grad)
    latent_grad, d_query_gain = norm_back(latent_in, query_gain, nt(query_grad, query_weight))
    latent_grad = upstream + latent_grad

    gains = jnp.stack([d_token_gain[0], d_query_gain, d_first_gain, d_mixer_gain, d_second_gain])
    gains = jnp.pad(
        gains.reshape(5, TOK, D // TOK).transpose(1, 0, 2), ((0, 0), (0, 11), (0, 128 - D // TOK))
    ).reshape(TOK * 16, 128)
    o_first_up, o_first_down, o_project, o_output, o_key, o_value, o_query, o_gains = reduce_grads(
        7,
        [d_first_up.astype(BF16), d_first_down.astype(BF16), d_mixer_project.astype(BF16), d_output.astype(BF16),
         d_key, d_value, d_query.astype(BF16), gains],
        (2, -2, 2, 1, 1, 1, 1, 1),
    )
    o_gains = o_gains[:, :D // TOK]
    o_second_up, o_mixer_output = early[:, :FF], early[:, FF:FF + D]
    return (
        final_rows.reshape(1, MB, ROWS, D),
        latent_grad.reshape(1, MB, ROWS, D),
        tokens_grad,
        o_gains[0],
        o_gains[1],
        o_query,
        o_key,
        o_value,
        o_output,
        o_gains[2],
        o_first_up,
        o_first_down,
        o_gains[3],
        o_project,
        o_mixer_output,
        o_gains[4],
        o_second_up,
        o_second_down,
    )


IN_SPECS = (
    P("grp", None, "tok", None),
    P("grp", None, None, None),
    P("grp", None, "tok"),
    P("grp", None, None, None),
    P("grp", None, "tok"),
    P(),
    P(),
    P(),
    P(),
    P(),
    P(),
    P(),
    P(),
    P(),
    P(),
    P(),
    P(),
    P(),
    P(),
    P(),
    P("grp", None, "tok", None),
)
OUT_SPECS = (
    P("grp", None, "tok", None),
    P("grp", None, "tok", None),
    P("grp", None, "tok", None),
    P("tok"),
    P("tok"),
    P("tok", None),
    P("tok", None),
    P("tok", None),
    P("tok", None),
    P("tok"),
    P("tok", None),
    P("tok", None),
    P("tok"),
    P("tok", None),
    P("tok", None),
    P("tok"),
    P("tok", None),
    P("tok", None),
)


def solution(mesh):
    return jax.shard_map(
        fast_body if mesh.shape["tok"] == TOK else general_body,
        mesh=mesh,
        in_specs=IN_SPECS,
        out_specs=OUT_SPECS,
        check_vma=False,
    )
```

```python
import functools

import jax
import jax.numpy as jnp
from jax import lax
from jax.experimental import pallas as pl
from jax.experimental.pallas import tpu as pltpu
from jax.sharding import PartitionSpec as P

D = 512
L = 2048
H = 8
HD = 64
TOK_DEV = 1024
MB = 2
SCENES = 8
LGROUPS = 8


EPS = 1e-05
NEG = -1e30


def norm_rows(values, gain):
    centre = values - jnp.mean(values, axis=-1, keepdims=True)
    spread = jnp.mean(centre * centre, axis=-1, keepdims=True)
    return centre * lax.rsqrt(spread + EPS) * gain


def norm_back(values, gain, upstream):
    unused, pull = jax.vjp(norm_rows, values, gain)
    return pull(upstream)


def gelu_back(hidden, upstream):
    unused, pull = jax.vjp(jax.nn.gelu, hidden)
    return pull(upstream)[0]


def product_plain(left, right):
    return jnp.dot(left, right, preferred_element_type=jnp.float32)


def product_rows(left, right):
    return lax.dot_general(
        left, right, (((0,), (0,)), ((), ())), preferred_element_type=jnp.float32
    )


def product_cols(left, right):
    return lax.dot_general(
        left, right, (((1,), (1,)), ((), ())), preferred_element_type=jnp.float32
    )


def add_term(store, name, value):
    if name in store:
        store[name] = store[name] + value
    else:
        store[name] = value


def project_tokens(tokens, member, token_gain, key_weight, value_weight):
    source = tokens[0, member].astype(jnp.float32)
    normed = norm_rows(source, token_gain).astype(jnp.bfloat16)
    key_rows = product_plain(normed, key_weight).astype(jnp.bfloat16)
    value_rows = product_plain(normed, value_weight).astype(jnp.bfloat16)
    return (source, normed, key_rows, value_rows)


def mlp_forward(residual, gain, up_weight, down_weight):
    normed = norm_rows(residual, gain).astype(jnp.bfloat16)
    hidden = product_plain(normed, up_weight)
    active = jax.nn.gelu(hidden).astype(jnp.bfloat16)
    return (residual + product_plain(active, down_weight), (normed, hidden, active))


def mlp_backward(residual, gain, up_weight, down_weight, saved, upstream):
    normed, hidden, active = saved
    grad_low = upstream.astype(jnp.bfloat16)
    grad_down = product_rows(active, grad_low)
    hidden_grad = gelu_back(hidden, product_cols(grad_low, down_weight)).astype(jnp.bfloat16)
    grad_up = product_rows(normed, hidden_grad)
    residual_grad, grad_gain = norm_back(residual, gain, product_cols(hidden_grad, up_weight))
    return (upstream + residual_grad, grad_gain, grad_up, grad_down)


def mixer_forward(residual, gain, project, output):
    own_rows = residual.shape[0]
    normed = norm_rows(residual, gain).astype(jnp.bfloat16)
    packed = product_plain(normed, project).astype(jnp.bfloat16)
    pair_rows = lax.all_gather(packed[:, D:], "tok", axis=0, tiled=True)
    every = pair_rows.shape[0]
    own_queries = packed[:, :D].reshape(own_rows, H, HD)
    keys = pair_rows[:, :D].reshape(every, H, HD)
    values = pair_rows[:, D:].reshape(every, H, HD)
    logits = jnp.einsum(
        "qhd,khd->hqk", own_queries, keys, preferred_element_type=jnp.float32
    ) * HD ** (-0.5)
    peak_row = jnp.max(logits, axis=-1, keepdims=True)
    raised = jnp.exp(logits - peak_row)
    softened = raised / jnp.sum(raised, axis=-1, keepdims=True)
    softened_low = softened.astype(jnp.bfloat16)
    mixed_rows = jnp.einsum(
        "hqk,khd->qhd", softened_low, values, preferred_element_type=jnp.float32
    )
    mixed_rows = mixed_rows.reshape(own_rows, D).astype(jnp.bfloat16)
    return (
        residual + product_plain(mixed_rows, output),
        (normed, own_queries, keys, values, softened, softened_low, mixed_rows),
    )


def mixer_backward(residual, gain, project, output, saved, upstream):
    normed, own_queries, keys, values, softened, softened_low, mixed_rows = saved
    own_rows = upstream.shape[0]
    every = keys.shape[0]
    grad_low = upstream.astype(jnp.bfloat16)
    grad_output = product_rows(mixed_rows, grad_low)
    mixed_grad = product_cols(grad_low, output).astype(jnp.bfloat16).reshape(own_rows, H, HD)
    value_grad = jnp.einsum(
        "hqk,qhd->khd", softened_low, mixed_grad, preferred_element_type=jnp.float32
    )
    soft_grad = jnp.einsum("qhd,khd->hqk", mixed_grad, values, preferred_element_type=jnp.float32)
    logit_grad = softened * (soft_grad - jnp.sum(soft_grad * softened, axis=-1, keepdims=True))
    logit_grad = logit_grad.astype(jnp.bfloat16)
    query_grad = jnp.einsum(
        "hqk,khd->qhd", logit_grad, keys, preferred_element_type=jnp.float32
    ) * HD ** (-0.5)
    key_grad = jnp.einsum(
        "hqk,qhd->khd", logit_grad, own_queries, preferred_element_type=jnp.float32
    ) * HD ** (-0.5)
    pair_terms = jnp.concatenate([key_grad.reshape(every, D), value_grad.reshape(every, D)], axis=1)
    pair_grad = lax.psum_scatter(
        pair_terms.astype(jnp.bfloat16), "tok", scatter_dimension=0, tiled=True
    ).astype(jnp.float32)
    packed_grad = jnp.concatenate([query_grad.reshape(own_rows, D), pair_grad], axis=1).astype(
        jnp.bfloat16
    )
    grad_project = product_rows(normed, packed_grad)
    residual_grad, grad_gain = norm_back(residual, gain, product_cols(packed_grad, project))
    return (upstream + residual_grad, grad_gain, grad_project, grad_output)


def general_body(
    tokens,
    latents,
    segments,
    scene_mask,
    counts,
    token_gain,
    query_gain,
    query_weight,
    key_weight,
    value_weight,
    output_weight,
    first_gain,
    first_up,
    first_down,
    mixer_gain,
    mixer_project,
    mixer_output,
    second_gain,
    second_up,
    second_down,
    cotangent,
):
    scale = D ** (-0.5)
    shards = lax.axis_size("tok")
    own_rows = L // shards
    row_start = lax.axis_index("tok") * own_rows
    latent_group = jnp.arange(L) // (L // LGROUPS)
    latent_onehot = (latent_group[:, None] == jnp.arange(LGROUPS)[None, :]).astype(jnp.float32)
    token_place = jnp.arange(TOK_DEV)
    records = []
    latent_outs = []
    for member in range(MB):
        record = {}
        source, normed, key_rows, value_rows = project_tokens(
            tokens, member, token_gain, key_weight, value_weight
        )
        record["token_side"] = (source, normed, key_rows, value_rows)
        scene_onehot = (segments[0, member][:, None] == jnp.arange(SCENES)[None, :]).astype(
            jnp.float32
        )
        token_seen = jnp.dot(scene_onehot, scene_mask[0, member].astype(jnp.float32))
        visible = product_cols(latent_onehot, token_seen)
        alive = token_place < counts[0, member, 0]
        allowed = (visible > 0.5) & alive[None, :]
        latent_every = latents[0, member]
        normed_every = norm_rows(latent_every, query_gain).astype(jnp.bfloat16)
        queries = product_plain(normed_every, query_weight).astype(jnp.bfloat16)
        scores = jnp.where(allowed, product_cols(queries, key_rows) * scale, NEG)
        row_top = lax.pmax(jnp.max(scores, axis=1), "tok")
        unnormed = jnp.exp(scores - row_top[:, None])
        row_total, weighted = (
            lax.psum_scatter(
                jnp.sum(unnormed, axis=1).astype(jnp.bfloat16),
                "tok",
                scatter_dimension=0,
                tiled=True,
            ).astype(jnp.float32),
            lax.psum_scatter(
                product_plain(unnormed.astype(jnp.bfloat16), value_rows).astype(jnp.bfloat16),
                "tok",
                scatter_dimension=0,
                tiled=True,
            ).astype(jnp.float32),
        )
        latent_in = lax.dynamic_slice_in_dim(latent_every, row_start, own_rows, 0)
        latent_normed = lax.dynamic_slice_in_dim(normed_every, row_start, own_rows, 0)
        attended = weighted / row_total[:, None]
        attended_low = attended.astype(jnp.bfloat16)
        first_mid = latent_in + product_plain(attended_low, output_weight)
        mixer_mid, first_saved = mlp_forward(first_mid, first_gain, first_up, first_down)
        second_mid, mixer_saved = mixer_forward(mixer_mid, mixer_gain, mixer_project, mixer_output)
        final_rows, second_saved = mlp_forward(second_mid, second_gain, second_up, second_down)
        latent_outs.append(final_rows)
        record["latent_side"] = (
            allowed,
            latent_in,
            latent_normed,
            queries,
            row_top,
            row_total,
            attended,
            attended_low,
            first_mid,
            mixer_mid,
            second_mid,
            first_saved,
            mixer_saved,
            second_saved,
        )
        records.append(record)
    grads = {}
    latent_grads = []
    token_grads = []
    for member in range(MB):
        record = records[member]
        source, normed, key_rows, value_rows = record["token_side"]
        (
            allowed,
            latent_in,
            latent_normed,
            queries,
            row_top,
            row_total,
            attended,
            attended_low,
            first_mid,
            mixer_mid,
            second_mid,
            first_saved,
            mixer_saved,
            second_saved,
        ) = record["latent_side"]
        second_back = mlp_backward(
            second_mid, second_gain, second_up, second_down, second_saved, cotangent[0, member]
        )
        add_term(grads, "second_gain", second_back[1])
        add_term(grads, "second_up", second_back[2])
        add_term(grads, "second_down", second_back[3])
        mixer_back = mixer_backward(
            mixer_mid, mixer_gain, mixer_project, mixer_output, mixer_saved, second_back[0]
        )
        add_term(grads, "mixer_gain", mixer_back[1])
        add_term(grads, "mixer_project", mixer_back[2])
        add_term(grads, "mixer_output", mixer_back[3])
        first_back = mlp_backward(
            first_mid, first_gain, first_up, first_down, first_saved, mixer_back[0]
        )
        add_term(grads, "first_gain", first_back[1])
        add_term(grads, "first_up", first_back[2])
        add_term(grads, "first_down", first_back[3])
        latent_upstream = first_back[0]
        grad_low = latent_upstream.astype(jnp.bfloat16)
        add_term(grads, "output_weight", product_rows(attended_low, grad_low))
        attended_grad = lax.optimization_barrier(
            product_cols(grad_low, output_weight).astype(jnp.bfloat16)
        ).astype(jnp.float32)
        weighted_grad = (attended_grad / row_total[:, None]).astype(jnp.bfloat16)
        total_grad = -jnp.sum(attended_grad * attended, axis=1) / row_total
        weighted_every, total_every = (
            lax.all_gather(
                weighted_grad.astype(jnp.float32).astype(jnp.bfloat16), "tok", axis=0, tiled=True
            ).astype(jnp.float32),
            lax.all_gather(total_grad.astype(jnp.bfloat16), "tok", axis=0, tiled=True).astype(
                total_grad.dtype
            ),
        )
        weighted_every = weighted_every.astype(jnp.bfloat16)
        scores = jnp.where(allowed, product_cols(queries, key_rows) * scale, NEG)
        unnormed = jnp.exp(scores - row_top[:, None])
        unnormed_grad = product_cols(weighted_every, value_rows) + total_every[:, None]
        score_grad = (unnormed * unnormed_grad).astype(jnp.bfloat16)
        value_grad = product_rows(unnormed.astype(jnp.bfloat16), weighted_every).astype(
            jnp.bfloat16
        )
        key_grad = (product_rows(score_grad, queries) * scale).astype(jnp.bfloat16)
        query_grad = lax.psum_scatter(
            (product_plain(score_grad, key_rows) * scale).astype(jnp.bfloat16),
            "tok",
            scatter_dimension=0,
            tiled=True,
        )
        add_term(grads, "key_weight", product_rows(normed, key_grad))
        add_term(grads, "value_weight", product_rows(normed, value_grad))
        normed_grad = product_cols(key_grad, key_weight) + product_cols(value_grad, value_weight)
        source_grad, gain_grad = norm_back(source, token_gain, normed_grad)
        add_term(grads, "token_gain", gain_grad)
        token_grads.append(source_grad)
        add_term(grads, "query_weight", product_rows(latent_normed, query_grad))
        latent_grad, gain_grad = norm_back(
            latent_in, query_gain, product_cols(query_grad, query_weight)
        )
        add_term(grads, "query_gain", gain_grad)
        latent_grads.append(latent_upstream + latent_grad)
    parts = (
        lax.psum_scatter(
            grads["token_gain"].astype(jnp.bfloat16), "tok", scatter_dimension=0, tiled=True
        ).astype(jnp.float32),
        lax.psum_scatter(
            grads["query_gain"].astype(jnp.bfloat16), "tok", scatter_dimension=0, tiled=True
        ).astype(jnp.float32),
        lax.psum_scatter(
            grads["query_weight"].astype(jnp.bfloat16), "tok", scatter_dimension=0, tiled=True
        ).astype(jnp.float32),
        lax.psum_scatter(
            grads["key_weight"].astype(jnp.bfloat16), "tok", scatter_dimension=0, tiled=True
        ).astype(jnp.float32),
        lax.psum_scatter(
            grads["value_weight"].astype(jnp.bfloat16), "tok", scatter_dimension=0, tiled=True
        ).astype(jnp.float32),
        lax.psum_scatter(
            grads["output_weight"].astype(jnp.bfloat16), "tok", scatter_dimension=0, tiled=True
        ).astype(jnp.float32),
        lax.psum_scatter(
            grads["first_gain"].astype(jnp.bfloat16), "tok", scatter_dimension=0, tiled=True
        ).astype(jnp.float32),
        lax.psum_scatter(
            grads["first_up"].astype(jnp.bfloat16), "tok", scatter_dimension=0, tiled=True
        ).astype(jnp.float32),
        lax.psum_scatter(
            grads["first_down"].astype(jnp.bfloat16), "tok", scatter_dimension=0, tiled=True
        ).astype(jnp.float32),
        lax.psum_scatter(
            grads["mixer_gain"].astype(jnp.bfloat16), "tok", scatter_dimension=0, tiled=True
        ).astype(jnp.float32),
        lax.psum_scatter(
            grads["mixer_project"].astype(jnp.bfloat16), "tok", scatter_dimension=0, tiled=True
        ).astype(jnp.float32),
        lax.psum_scatter(
            grads["mixer_output"].astype(jnp.bfloat16), "tok", scatter_dimension=0, tiled=True
        ).astype(jnp.float32),
        lax.psum_scatter(
            grads["second_gain"].astype(jnp.bfloat16), "tok", scatter_dimension=0, tiled=True
        ).astype(jnp.float32),
        lax.psum_scatter(
            grads["second_up"].astype(jnp.bfloat16), "tok", scatter_dimension=0, tiled=True
        ).astype(jnp.float32),
        lax.psum_scatter(
            grads["second_down"].astype(jnp.bfloat16), "tok", scatter_dimension=0, tiled=True
        ).astype(jnp.float32),
    )
    summed = (
        lax.psum(parts[0].astype(jnp.bfloat16), "grp").astype(jnp.float32),
        lax.psum(parts[1].astype(jnp.bfloat16), "grp").astype(jnp.float32),
        lax.psum(parts[2].astype(jnp.bfloat16), "grp").astype(jnp.float32),
        lax.psum(parts[3].astype(jnp.bfloat16), "grp").astype(jnp.float32),
        lax.psum(parts[4].astype(jnp.bfloat16), "grp").astype(jnp.float32),
        lax.psum(parts[5].astype(jnp.bfloat16), "grp").astype(jnp.float32),
        lax.psum(parts[6].astype(jnp.bfloat16), "grp").astype(jnp.float32),
        lax.psum(parts[7].astype(jnp.bfloat16), "grp").astype(jnp.float32),
        lax.psum(parts[8].astype(jnp.bfloat16), "grp").astype(jnp.float32),
        lax.psum(parts[9].astype(jnp.bfloat16), "grp").astype(jnp.float32),
        lax.psum(parts[10].astype(jnp.bfloat16), "grp").astype(jnp.float32),
        lax.psum(parts[11].astype(jnp.bfloat16), "grp").astype(jnp.float32),
        lax.psum(parts[12].astype(jnp.bfloat16), "grp").astype(jnp.float32),
        lax.psum(parts[13].astype(jnp.bfloat16), "grp").astype(jnp.float32),
        lax.psum(parts[14].astype(jnp.bfloat16), "grp").astype(jnp.float32),
    )
    return (
        jnp.stack(latent_outs)[None],
        jnp.stack(latent_grads)[None],
        jnp.stack(token_grads)[None],
    ) + tuple(summed)


TOK = 8
ROWS = L // TOK
FF = 2048
GR = L // LGROUPS
LOG2E = 1.4426950408889634
LN2 = 0.6931471805599453
F32 = jnp.float32
BF16 = jnp.bfloat16
MIB = 1024 * 1024


def nn(left, right):
    return lax.dot_general(left, right, (((1,), (0,)), ((), ())), preferred_element_type=F32)


def nt(left, right):
    return lax.dot_general(left, right, (((1,), (1,)), ((), ())), preferred_element_type=F32)


def tn(left, right):
    return lax.dot_general(left, right, (((0,), (0,)), ((), ())), preferred_element_type=F32)


def norm_parts(values):
    centre = values - jnp.mean(values, axis=-1, keepdims=True)
    inverse = lax.rsqrt(jnp.mean(centre * centre, axis=-1, keepdims=True) + EPS)
    return centre * inverse, inverse


def norm_pull(hat, inverse, gain, upstream):
    scaled = upstream * gain
    inner = jnp.mean(scaled * hat, axis=-1, keepdims=True)
    grad = (scaled - jnp.mean(scaled, axis=-1, keepdims=True) - hat * inner) * inverse
    return grad, upstream * hat


def places():
    me = lax.axis_index("tok")
    core = lax.rem(me, 2)
    chip = lax.div(me, 2)
    mate = me + 1 - 2 * core
    flip_x = chip + 1 - 2 * lax.rem(chip, 2)
    flip_y = lax.rem(chip + 2, 4)
    far = 3 - chip
    return me, core, chip, mate, (far, flip_x, flip_y)


def remote(src, dst, send_sem, recv_sem, peer):
    return pltpu.make_async_remote_copy(
        src_ref=src,
        dst_ref=dst,
        send_sem=send_sem,
        recv_sem=recv_sem,
        device_id={"tok": peer},
        device_id_type=pl.DeviceIdType.MESH,
    )


def greet(devices):
    barrier = pltpu.get_barrier_semaphore()
    for device in devices:
        pl.semaphore_signal(
            barrier, inc=1, device_id={"tok": device}, device_id_type=pl.DeviceIdType.MESH
        )
    pl.semaphore_wait(barrier, len(devices))


def chip_at(chip, flip):
    across = lax.rem(lax.rem(chip, 2) + lax.rem(flip, 2), 2)
    along = lax.rem(lax.div(chip, 2) + lax.div(flip, 2), 2)
    return 2 * along + across


def mask_rows(seg_ref, mask_ref, count_ref, bias_ref):
    for member in range(MB):
        scene = lax.broadcasted_iota(jnp.int32, (SCENES, TOK_DEV), 0)
        place = lax.broadcasted_iota(jnp.int32, (SCENES, TOK_DEV), 1)
        hot = jnp.where((seg_ref[member] == scene) & (place < count_ref[member]), 1.0, 0.0)
        seen = tn(jnp.where(mask_ref[member] > 0, 1.0, 0.0).astype(BF16), hot.astype(BF16))
        bias_ref[member] = jnp.where(seen > 0.5, 0.0, NEG)


def to_rows(first, second):
    rows = first.shape[0]
    lane = lax.broadcasted_iota(jnp.int32, (rows, 128), 1)
    return jnp.where(lane == 0, first, second).T[0:8]


def cross_forward_kernel(
    tok_ref, lat_ref, tgain_ref, qgain_ref, qw_ref, kw_ref, vw_ref, seg_ref, mask_ref, count_ref,
    k_out, v_out, q_out, att_ref, lse_ref,
    tok_buf, lat_buf, keys, values, queries, bias, part, part_s, got, got_s, stage, stage_s,
    arrive, arrive_s, total,
    tok_sem, lat_sem, k_sem, v_sem, q_sem,
    core_send, core_recv, core_send_s, core_recv_s, chip_send, chip_recv, chip_send_s, chip_recv_s,
):
    me, core, chip, mate, others = places()
    span = 2 * ROWS

    def unpack(step):
        return lax.div(step, 4), 3 - lax.rem(step, 4)

    def lat_copy(step):
        member, flip = unpack(step)
        start = pl.multiple_of(chip_at(chip, flip) * span, span)
        return pltpu.make_async_copy(lat_ref.at[0, member, pl.ds(start, span)], lat_buf.at[step], lat_sem.at[step])

    def q_copy(step):
        member, flip = unpack(step)
        start = pl.multiple_of(chip_at(chip, flip) * span, span)
        return pltpu.make_async_copy(queries.at[step], q_out.at[member, pl.ds(start, span)], q_sem.at[step])

    def tok_copy(member):
        return pltpu.make_async_copy(tok_ref.at[0, member], tok_buf.at[member], tok_sem.at[member])

    def kv_copies(member):
        return (
            pltpu.make_async_copy(keys.at[member], k_out.at[member], k_sem.at[member]),
            pltpu.make_async_copy(values.at[member], v_out.at[member], v_sem.at[member]),
        )

    def core_copies(step):
        return (
            remote(part.at[step, 1 - core], got.at[step], core_send.at[step], core_recv.at[step], mate),
            remote(part_s.at[step, 1 - core], got_s.at[step], core_send_s.at[step], core_recv_s.at[step], mate),
        )

    def chip_copies(step):
        member, flip = unpack(step)
        peer = 2 * chip_at(chip, flip) + core
        place = 3 * member + flip - 1
        return (
            remote(stage.at[step], arrive.at[place], chip_send.at[place], chip_recv.at[place], peer),
            remote(stage_s.at[step], arrive_s.at[place], chip_send_s.at[place], chip_recv_s.at[place], peer),
        )

    for member in range(MB):
        tok_copy(member).start()
    for step in range(2 * 4):
        lat_copy(step).start()
    greet([mate] + [2 * other + core for other in others])
    mask_rows(seg_ref, mask_ref, count_ref, bias)

    def compute(step):
        member, flip = unpack(step)

        @pl.when(flip == 3)
        def _():
            tok_copy(member).wait()
            hat, inverse = norm_parts(tok_buf[member].astype(F32))
            normed = (hat * tgain_ref[...]).astype(BF16)
            keys[member] = nn(normed, kw_ref[...]).astype(BF16)
            values[member] = nn(normed, vw_ref[...]).astype(BF16)
            for copy in kv_copies(member):
                copy.start()

        lat_copy(step).wait()
        hat, inverse = norm_parts(lat_buf[step])
        normed = (hat * qgain_ref[...]).astype(BF16)
        asked = (nn(normed, qw_ref[...]) * (D ** (-0.5) * LOG2E)).astype(BF16)
        queries[step] = asked
        q_copy(step).start()
        scores = nt(asked, keys[member])
        raised = []
        for half in range(2):
            seen = bias[member, pl.ds(2 * chip_at(chip, flip) + half, 1), :]
            own = scores[half * ROWS:(half + 1) * ROWS] + seen
            top = jnp.max(own, axis=1, keepdims=True)
            own = jnp.exp2(own - top)
            part_s[step, half] = to_rows(top, jnp.sum(own, axis=1, keepdims=True))
            raised.append(own.astype(BF16))
        sums = nn(jnp.concatenate(raised, axis=0), values[member]).astype(BF16)
        for half in range(2):
            part[step, half] = sums[half * ROWS:(half + 1) * ROWS]
        for copy in core_copies(step):
            copy.start()

    def merge(one, one_s, two, two_s):
        top = jnp.maximum(one_s[0:1], two_s[0:1])
        one_w, two_w = jnp.exp2(one_s[0:1] - top), jnp.exp2(two_s[0:1] - top)
        sums = one_s[1:2] * one_w + two_s[1:2] * two_w
        spare = jnp.zeros((6, ROWS), F32)
        weights = jnp.concatenate([one_w, two_w, spare], axis=0).T
        return one * weights[:, 0:1] + two * weights[:, 1:2], jnp.concatenate([top, sums, spare], axis=0)

    def combine(step):
        member, flip = unpack(step)
        for copy in core_copies(step):
            copy.wait_recv()
        added, figures = merge(
            part[step, core].astype(F32), part_s[step, core], got[step].astype(F32), got_s[step]
        )
        stage_s[step] = figures

        @pl.when(flip > 0)
        def _():
            stage[step] = added.astype(BF16)
            for copy in chip_copies(step):
                copy.start()

        @pl.when(flip == 0)
        def _():
            total[member] = added

    def finish(member):
        added, figures = total[member], stage_s[4 * member + 3]
        for flip in (1, 2, 3):
            for copy in chip_copies(4 * member + 3 - flip):
                copy.wait_recv()
            place = 3 * member + flip - 1
            added, figures = merge(added, figures, arrive[place].astype(F32), arrive_s[place])
        spare = jnp.zeros((7, ROWS), F32)
        inverse = jnp.concatenate([1.0 / figures[1:2], spare], axis=0).T
        att_ref[member] = added * inverse[:, 0:1]
        lse_ref[member] = jnp.concatenate([figures[0:1] + jnp.log2(figures[1:2]), spare], axis=0)

    def step_body(step, carry):
        compute(step)

        @pl.when(step > 0)
        def _():
            combine(step - 1)

        return carry

    lax.fori_loop(0, 4 * MB, step_body, 0)
    combine(jnp.int32(4 * MB - 1))
    for member in range(MB):
        finish(member)
    for member in range(MB):
        for copy in kv_copies(member):
            copy.wait()
        for slot in range(4):
            step = 4 * member + slot
            q_copy(step).wait()
            for copy in core_copies(step):
                copy.wait_send()
            if slot < 3:
                for copy in chip_copies(step):
                    copy.wait_send()


def cross_forward(collective_id, *args):
    dma = pltpu.SemaphoreType.DMA
    span = 2 * ROWS
    steps = 4 * MB
    vmem = pl.BlockSpec(memory_space=pltpu.VMEM)
    hbm = pl.BlockSpec(memory_space=pl.ANY)
    return pl.pallas_call(
        cross_forward_kernel,
        in_specs=[hbm, hbm] + [vmem] * 8,
        out_specs=[hbm, hbm, hbm, vmem, vmem],
        out_shape=[
            jax.ShapeDtypeStruct((MB, TOK_DEV, D), BF16),
            jax.ShapeDtypeStruct((MB, TOK_DEV, D), BF16),
            jax.ShapeDtypeStruct((MB, L, D), BF16),
            jax.ShapeDtypeStruct((MB, ROWS, D), F32),
            jax.ShapeDtypeStruct((MB, 8, ROWS), F32),
        ],
        scratch_shapes=[
            pltpu.VMEM((MB, TOK_DEV, D), BF16),
            pltpu.VMEM((steps, span, D), F32),
            pltpu.VMEM((MB, TOK_DEV, D), BF16),
            pltpu.VMEM((MB, TOK_DEV, D), BF16),
            pltpu.VMEM((steps, span, D), BF16),
            pltpu.VMEM((MB, LGROUPS, TOK_DEV), F32),
            pltpu.VMEM((steps, 2, ROWS, D), BF16),
            pltpu.VMEM((steps, 2, 8, ROWS), F32),
            pltpu.VMEM((steps, ROWS, D), BF16),
            pltpu.VMEM((steps, 8, ROWS), F32),
            pltpu.VMEM((steps, ROWS, D), BF16),
            pltpu.VMEM((steps, 8, ROWS), F32),
            pltpu.VMEM((3 * MB, ROWS, D), BF16),
            pltpu.VMEM((3 * MB, 8, ROWS), F32),
            pltpu.VMEM((MB, ROWS, D), F32),
            dma((MB,)), dma((steps,)), dma((MB,)), dma((MB,)), dma((steps,)),
        ] + [dma((steps,))] * 4 + [dma((3 * MB,))] * 4,
        compiler_params=pltpu.CompilerParams(
            collective_id=collective_id, has_side_effects=True, vmem_limit_bytes=56 * MIB
        ),
        cost_estimate=pl.CostEstimate(
            flops=14 * 10**9, bytes_accessed=22 * 10**6, transcendentals=4 * 10**6
        ),
        name="cross_forward",
    )(*args)


def cross_backward_kernel(
    tok_ref, tgain_ref, kw_ref, vw_ref, seg_ref, mask_ref, count_ref, k_ref, v_ref, q_ref, up_ref, fig_ref,
    dq_ref, dtok_ref, dkw_ref, dvw_ref, dgain_ref,
    tok_buf, keys, values, queries, ups, figs, bias, part, got, stage, arrive, total, dk, dv, dtok, dkw, dvw,
    tok_sem, k_sem, v_sem, q_sem, out_sem, near_send, near_recv, far_send, far_recv, on_send, on_recv, own_sem,
    core_send, core_recv, chip_send, chip_recv,
):
    me, core, chip, mate, others = places()
    span = 2 * ROWS

    def slot_of(step):
        member, place = lax.div(step, 4), lax.rem(step, 4)
        return member, place + member * (3 - 2 * place)

    def loads(slot):
        member, flip = divmod(slot, 4)
        start = pl.multiple_of(chip_at(chip, flip) * span, span)
        return pltpu.make_async_copy(q_ref.at[member, pl.ds(start, span)], queries.at[slot], q_sem.at[slot])

    def tok_copies(member):
        return (
            pltpu.make_async_copy(k_ref.at[member], keys.at[member], k_sem.at[member]),
            pltpu.make_async_copy(v_ref.at[member], values.at[member], v_sem.at[member]),
            pltpu.make_async_copy(tok_ref.at[0, member], tok_buf.at[member], tok_sem.at[member]),
        )

    def out_copy(member):
        return pltpu.make_async_copy(dtok.at[member], dtok_ref.at[0, member], out_sem.at[member])

    def own_copies(member):
        slot = 4 * member
        return (
            pltpu.make_async_copy(up_ref.at[member], ups.at[slot, core], own_sem.at[member, 0]),
            pltpu.make_async_copy(fig_ref.at[member], figs.at[slot, core], own_sem.at[member, 1]),
        )

    def near_copies(member):
        slot = 4 * member
        return (
            remote(up_ref.at[member], ups.at[slot, core], near_send.at[member, 0], near_recv.at[member, 0], mate),
            remote(fig_ref.at[member], figs.at[slot, core], near_send.at[member, 1], near_recv.at[member, 1], mate),
        )

    def far_copies(slot):
        member, flip = slot // 4, slot % 4
        peer = 2 * chip_at(chip, flip) + core
        return (
            remote(up_ref.at[member], ups.at[slot, core], far_send.at[slot, 0], far_recv.at[slot, 0], peer),
            remote(fig_ref.at[member], figs.at[slot, core], far_send.at[slot, 1], far_recv.at[slot, 1], peer),
        )

    def on_copies(slot):
        return (
            remote(ups.at[slot, core], ups.at[slot, core], on_send.at[slot, 0], on_recv.at[slot, 0], mate),
            remote(figs.at[slot, core], figs.at[slot, core], on_send.at[slot, 1], on_recv.at[slot, 1], mate),
        )

    def pass_on(slot):
        for copy in far_copies(slot):
            copy.wait_recv()
        for copy in on_copies(slot):
            copy.start()

    def core_copy(slot):
        return remote(part.at[slot, 1 - core], got.at[slot], core_send.at[slot], core_recv.at[slot], mate)

    def chip_copy(slot):
        member, flip = lax.div(slot, 4), lax.rem(slot, 4)
        peer = 2 * chip_at(chip, flip) + core
        place = 3 * member + flip - 1
        return remote(stage.at[slot], arrive.at[place], chip_send.at[place], chip_recv.at[place], peer)

    for copy in own_copies(0):
        copy.start()
    for copy in tok_copies(0):
        copy.start()
    for flip in (0, 1, 2, 3):
        loads(flip).start()
    for copy in own_copies(1):
        copy.start()
    for copy in tok_copies(1):
        copy.start()
    for flip in (3, 2, 1, 0):
        loads(4 + flip).start()
    greet([mate] + [2 * other + core for other in others])
    for member in range(MB):
        for copy in near_copies(member):
            copy.start()
        for flip in ((1, 2, 3) if member == 0 else (3, 2, 1)):
            for copy in far_copies(4 * member + flip):
                copy.start()
    mask_rows(seg_ref, mask_ref, count_ref, bias)

    def compute(step):
        member, flip = slot_of(step)
        slot = 4 * member + flip

        @pl.when(lax.rem(step, 4) == 0)
        def _():
            for copy in tok_copies(member):
                copy.wait()
            dk[...] = jnp.zeros_like(dk)
            dv[...] = jnp.zeros_like(dv)

        start = pl.multiple_of(chip_at(chip, flip) * span, span)
        pltpu.make_async_copy(q_ref.at[member, pl.ds(start, span)], queries.at[slot], q_sem.at[slot]).wait()

        @pl.when(flip == 0)
        def _():
            for copy in own_copies(member):
                copy.wait()
            for copy in near_copies(member):
                copy.wait_recv()

        @pl.when(flip > 0)
        def _():
            for copy in on_copies(slot):
                copy.wait_recv()

        asked = queries[slot]
        upstream = ups[slot].reshape(span, D)
        scores = nt(asked, keys[member])
        soft = nt(upstream, values[member])
        weights, grads = [], []
        for half in range(2):
            seen = bias[member, pl.ds(2 * chip_at(chip, flip) + half, 1), :]
            figures = figs[slot, half].T
            rows = slice(half * ROWS, (half + 1) * ROWS)
            weight = jnp.exp2(scores[rows] + seen - figures[:, 0:1])
            grads.append((weight * (soft[rows] - figures[:, 1:2])).astype(BF16))
            weights.append(weight.astype(BF16))
        weight = jnp.concatenate(weights, axis=0)
        grad = jnp.concatenate(grads, axis=0)
        dv[...] += tn(weight, upstream)
        dk[...] += tn(grad, asked)
        asked_grad = (nn(grad, keys[member]) * D ** (-0.5)).astype(BF16)
        for half in range(2):
            part[slot, half] = asked_grad[half * ROWS:(half + 1) * ROWS]
        core_copy(slot).start()

    def combine(step):
        member, flip = slot_of(step)
        slot = 4 * member + flip
        core_copy(slot).wait_recv()
        added = part[slot, core].astype(F32) + got[slot].astype(F32)

        @pl.when(flip > 0)
        def _():
            stage[slot] = added.astype(BF16)
            chip_copy(slot).start()

        @pl.when(flip == 0)
        def _():
            total[member] = added

    def tokens_back(member):
        gain = tgain_ref[...]
        hat, inverse = norm_parts(tok_buf[member].astype(F32))
        normed = (hat * gain).astype(BF16)
        key_grad = (dk[...] * LN2).astype(BF16)
        value_grad = dv[...].astype(BF16)
        key_term = tn(normed, key_grad)
        value_term = tn(normed, value_grad)
        normed_grad = nt(key_grad, kw_ref[...]) + nt(value_grad, vw_ref[...])
        source_grad, gain_rows = norm_pull(hat, inverse, gain, normed_grad)
        dtok[member] = source_grad
        out_copy(member).start()
        gain_term = jnp.sum(gain_rows, axis=0, keepdims=True)

        @pl.when(member == 0)
        def _():
            dkw[...] = key_term
            dvw[...] = value_term
            dgain_ref[...] = gain_term

        @pl.when(member > 0)
        def _():
            dkw_ref[...] = (dkw[...] + key_term).astype(BF16)
            dvw_ref[...] = (dvw[...] + value_term).astype(BF16)
            dgain_ref[...] += gain_term

    def step_body(step, carry):
        compute(step)

        @pl.when(step > 0)
        def _():
            combine(step - 1)

        @pl.when(step == 0)
        def _():
            pass_on(1)
            pass_on(2)

        @pl.when(step == 1)
        def _():
            pass_on(3)

        @pl.when(step == 3)
        def _():
            pass_on(7)
            pass_on(6)

        @pl.when(step == 4)
        def _():
            pass_on(5)

        @pl.when(step == 4 * MB - 1)
        def _():
            combine(step)

        @pl.when(lax.rem(step, 4) == 3)
        def _():
            tokens_back(lax.div(step, 4))

        return carry

    lax.fori_loop(0, 4 * MB, step_body, 0)
    for member in range(MB):
        added = total[member]
        for flip in (1, 2, 3):
            chip_copy(4 * member + flip).wait_recv()
            added = added + arrive[3 * member + flip - 1].astype(F32)
        dq_ref[member] = added.astype(BF16)
    for member in range(MB):
        out_copy(member).wait()
        for copy in near_copies(member):
            copy.wait_send()
        for flip in range(4):
            slot = 4 * member + flip
            core_copy(slot).wait_send()
            if flip > 0:
                chip_copy(slot).wait_send()
                for copy in far_copies(slot) + on_copies(slot):
                    copy.wait_send()


def cross_backward(collective_id, *args):
    dma = pltpu.SemaphoreType.DMA
    span = 2 * ROWS
    steps = 4 * MB
    vmem = pl.BlockSpec(memory_space=pltpu.VMEM)
    hbm = pl.BlockSpec(memory_space=pl.ANY)
    return pl.pallas_call(
        cross_backward_kernel,
        in_specs=[hbm] + [vmem] * 6 + [hbm] * 5,
        out_specs=[vmem, hbm, vmem, vmem, vmem],
        out_shape=[
            jax.ShapeDtypeStruct((MB, ROWS, D), BF16),
            jax.ShapeDtypeStruct((1, MB, TOK_DEV, D), F32),
            jax.ShapeDtypeStruct((D, D), BF16),
            jax.ShapeDtypeStruct((D, D), BF16),
            jax.ShapeDtypeStruct((1, D), F32),
        ],
        scratch_shapes=[
            pltpu.VMEM((MB, TOK_DEV, D), BF16),
            pltpu.VMEM((MB, TOK_DEV, D), BF16),
            pltpu.VMEM((MB, TOK_DEV, D), BF16),
            pltpu.VMEM((steps, span, D), BF16),
            pltpu.VMEM((steps, 2, ROWS, D), BF16),
            pltpu.VMEM((steps, 2, 8, ROWS), F32),
            pltpu.VMEM((MB, LGROUPS, TOK_DEV), F32),
            pltpu.VMEM((steps, 2, ROWS, D), BF16),
            pltpu.VMEM((steps, ROWS, D), BF16),
            pltpu.VMEM((steps, ROWS, D), BF16),
            pltpu.VMEM((3 * MB, ROWS, D), BF16),
            pltpu.VMEM((MB, ROWS, D), F32),
            pltpu.VMEM((TOK_DEV, D), F32),
            pltpu.VMEM((TOK_DEV, D), F32),
            pltpu.VMEM((MB, TOK_DEV, D), F32),
            pltpu.VMEM((D, D), F32),
            pltpu.VMEM((D, D), F32),
            dma((MB,)), dma((MB,)), dma((MB,)), dma((steps,)), dma((MB,)),
            dma((MB, 2)), dma((MB, 2)), dma((steps, 2)), dma((steps, 2)), dma((steps, 2)), dma((steps, 2)), dma((MB, 2)),
            dma((steps,)), dma((steps,)), dma((3 * MB,)), dma((3 * MB,)),
        ],
        compiler_params=pltpu.CompilerParams(
            collective_id=collective_id, has_side_effects=True, vmem_limit_bytes=58 * MIB
        ),
        cost_estimate=pl.CostEstimate(
            flops=26 * 10**9, bytes_accessed=24 * 10**6, transcendentals=4 * 10**6
        ),
        name="cross_backward",
    )(*args)


GELU_A = 0.7978845608028654
GELU_B = 0.044715


def gelu_parts(hidden):
    square = hidden * hidden
    bent = jnp.tanh(GELU_A * hidden * (1.0 + GELU_B * square))
    half = 0.5 * (1.0 + bent)
    slope = half + 0.5 * hidden * (1.0 - bent * bent) * (GELU_A * (1.0 + 3.0 * GELU_B * square))
    return hidden * half, slope


def greet_all(tok_devices, grp_devices=()):
    barrier = pltpu.get_barrier_semaphore()
    for axis, devices in (("tok", tok_devices), ("grp", grp_devices)):
        for device in devices:
            pl.semaphore_signal(
                barrier, inc=1, device_id={axis: device}, device_id_type=pl.DeviceIdType.MESH
            )
    pl.semaphore_wait(barrier, len(tok_devices) + len(grp_devices))


def all_peers():
    me, core, chip, mate, others = places()
    peers = []
    for other in others:
        peers += [2 * other + core, 2 * other + 1 - core]
    return me, peers + [mate]


def head_copies(row_side, head_side, to_heads, member, me, peers, send, recv, local):
    lanes = pl.ds(member * ROWS, ROWS)
    row_at = lambda device: row_side.at[:, device, :, lanes]
    head_at = lambda device: head_side.at[:, member, :, pl.ds(pl.multiple_of(device * ROWS, ROWS), ROWS)]
    source, target = (row_at, head_at) if to_heads else (head_at, row_at)
    copies = [
        remote(source(peer), target(me), send.at[slot, member], recv.at[slot, member], peer)
        for slot, peer in enumerate(peers)
    ]
    return copies, pltpu.make_async_copy(source(me), target(me), local.at[member])


QB = 1024
QB_BACK = 256


def latents_forward_kernel(
    lat_ref, att_ref, cot_ref, ow_ref, fgain_ref, fup_ref, fdown_ref, mgain_ref, proj_ref, mow_ref, sgain_ref,
    sup_ref, sdown_ref,
    out_ref, fmid_ref, mmid_ref, packed_ref, exact_ref, lse_ref, up_ref, mgrad_ref, ddown_ref, dup_ref, dmo_ref,
    dgain_ref,
    lat, att, cot, ow, fup, fdown, proj, mow, sup, sdown,
    out, fmid, mmid, heads, exact, up, mgrad, ddown, dup, dmo,
    rows_out, keys, values, mixed, mixed_rows,
    load_sem, store_sem, send_a, recv_a, local_a, send_b, recv_b, local_b,
):
    me, peers = all_peers()
    own = pl.ds(pl.multiple_of(me * ROWS, ROWS), ROWS)
    names = ("lat", "att", "ow", "fup", "fdown", "proj", "mow", "sup", "sdown", "cot")
    loads = {}
    for i, (source, target) in enumerate((
        (lat_ref.at[0, :, own], lat), (att_ref, att), (ow_ref, ow), (fup_ref, fup), (fdown_ref, fdown),
        (proj_ref, proj), (mow_ref, mow), (sup_ref, sup), (sdown_ref, sdown), (cot_ref.at[0], cot),
    )):
        loads[names[i]] = pltpu.make_async_copy(source, target, load_sem.at[i])
        loads[names[i]].start()
    stores = []

    def store(source, target):
        stores.append(pltpu.make_async_copy(source, target, store_sem.at[len(stores)]))
        stores[-1].start()

    greet_all(peers)
    flat = (MB * ROWS, D)
    for name in ("lat", "att", "ow"):
        loads[name].wait()
    first = lat[...].reshape(flat) + nn(att[...].reshape(flat).astype(BF16), ow[...])
    fmid[...] = first
    store(fmid, fmid_ref)
    normed = (norm_parts(first)[0] * fgain_ref[...]).astype(BF16)
    loads["fup"].wait()
    loads["fdown"].wait()
    mid = first
    for part in range(2):
        cut = slice(part * FF // 2, (part + 1) * FF // 2)
        mid = mid + nn(jax.nn.gelu(nn(normed, fup[:, cut])).astype(BF16), fdown[cut])
    mmid[...] = mid
    store(mmid, mmid_ref)
    normed = (norm_parts(mid)[0] * mgain_ref[...]).astype(BF16).T
    loads["proj"].wait()
    for kind, scale in enumerate((HD ** (-0.5) * LOG2E, 1.0, 1.0)):
        packed = tn(proj[:, kind * D:(kind + 1) * D], normed) * scale
        rows_out[kind] = packed.astype(BF16).reshape(H, HD, MB * ROWS)
    outward = [head_copies(rows_out, heads, True, member, me, peers, send_a, recv_a, local_a) for member in range(MB)]
    backward = [
        head_copies(mixed_rows, mixed, False, member, me, peers, send_b, recv_b, local_b) for member in range(MB)
    ]
    for copies, here in outward:
        for copy in copies:
            copy.start()
        here.start()
    for member in range(MB):
        copies, here = outward[member]
        for copy in copies:
            copy.wait_recv()
        here.wait()
        store(heads.at[:, member], packed_ref.at[:, member])
        keys[...] = heads[1, member].T
        values[0:HD] = heads[2, member]
        values[HD:] = jnp.ones((16, L), BF16)

        def attend(step, carry, member=member):
            at = pl.ds(pl.multiple_of(step * QB, QB), QB)
            logits = nn(keys[...], heads[0, member, :, at])
            top = jnp.max(logits, axis=0, keepdims=True)
            both = nn(values[...], jnp.exp2(logits - top).astype(BF16))
            total = both[HD:HD + 1]
            result = both[0:HD] / total
            exact[member, :, at] = result
            mixed[0, member, :, at] = result.astype(BF16)
            lse_ref[member, :, at] = jnp.broadcast_to(top + jnp.log2(total), (8, QB))
            return carry

        lax.fori_loop(0, L // QB, attend, 0)
        for copy in backward[member][0] + [backward[member][1]]:
            copy.start()
    store(exact, exact_ref)
    loads["mow"].wait()
    loads["sup"].wait()
    loads["sdown"].wait()
    loads["cot"].wait()
    for copies, here in backward:
        for copy in copies:
            copy.wait_recv()
        here.wait()
    mixed_t = mixed_rows[0].reshape(D, MB * ROWS)
    second = mmid[...] + tn(mixed_t, mow[...])
    hat, inverse = norm_parts(second)
    normed = (hat * sgain_ref[...]).astype(BF16)
    upstream = cot[...].reshape(flat)
    grad = upstream.astype(BF16)
    final = second
    normed_grad = jnp.zeros(flat, F32)
    for part in range(2):
        cut = slice(part * FF // 2, (part + 1) * FF // 2)
        act, slope = gelu_parts(nn(normed, sup[:, cut]))
        act = act.astype(BF16)
        final = final + nn(act, sdown[cut])
        hidden_grad = (slope * nt(grad, sdown[cut])).astype(BF16)
        normed_grad = normed_grad + nt(hidden_grad, sup[:, cut])
        ddown[cut] = tn(act, grad).astype(BF16)
        dup[:, cut] = tn(normed, hidden_grad).astype(BF16)
    store(ddown, ddown_ref)
    store(dup, dup_ref)
    out[...] = final.reshape(MB, ROWS, D)
    store(out, out_ref.at[0])
    residual, gain_rows = norm_pull(hat, inverse, sgain_ref[...], normed_grad)
    dgain_ref[...] = jnp.sum(gain_rows, axis=0, keepdims=True)
    upstream = upstream + residual
    up[...] = upstream
    store(up, up_ref)
    grad = upstream.astype(BF16)
    mgrad[0] = nt(mow[...], grad).astype(BF16).reshape(H, HD, MB * ROWS)
    store(mgrad, mgrad_ref)
    dmo[...] = nn(mixed_t, grad).astype(BF16)
    store(dmo, dmo_ref)
    for copy in stores:
        copy.wait()
    for copies, here in outward + backward:
        for copy in copies:
            copy.wait_send()


def latents_forward(collective_id, *args):
    dma = pltpu.SemaphoreType.DMA
    vmem = pl.BlockSpec(memory_space=pltpu.VMEM)
    hbm = pl.BlockSpec(memory_space=pl.ANY)
    rows = MB * ROWS
    stored = [
        ((1, MB, ROWS, D), F32), ((rows, D), F32), ((rows, D), F32), ((3, MB, HD, L), BF16), ((MB, HD, L), F32),
        ((MB, 8, L), F32), ((rows, D), F32), ((1, H, HD, rows), BF16), ((FF, D), BF16), ((D, FF), BF16), ((D, D), BF16),
        ((1, D), F32),
    ]
    return pl.pallas_call(
        latents_forward_kernel,
        in_specs=[hbm, hbm, hbm, hbm, vmem, hbm, hbm, vmem, hbm, hbm, vmem, hbm, hbm],
        out_specs=[hbm] * 5 + [vmem] + [hbm] * 5 + [vmem],
        out_shape=[jax.ShapeDtypeStruct(shape, kind) for shape, kind in stored],
        scratch_shapes=[
            pltpu.VMEM((MB, ROWS, D), F32), pltpu.VMEM((MB, ROWS, D), F32), pltpu.VMEM((MB, ROWS, D), F32),
            pltpu.VMEM((D, D), BF16), pltpu.VMEM((D, FF), BF16), pltpu.VMEM((FF, D), BF16),
            pltpu.VMEM((D, 3 * D), BF16), pltpu.VMEM((D, D), BF16), pltpu.VMEM((D, FF), BF16),
            pltpu.VMEM((FF, D), BF16),
            pltpu.VMEM((MB, ROWS, D), F32), pltpu.VMEM((rows, D), F32), pltpu.VMEM((rows, D), F32),
            pltpu.VMEM((3, MB, HD, L), BF16), pltpu.VMEM((MB, HD, L), F32), pltpu.VMEM((rows, D), F32),
            pltpu.VMEM((1, H, HD, rows), BF16), pltpu.VMEM((FF, D), BF16), pltpu.VMEM((D, FF), BF16),
            pltpu.VMEM((D, D), BF16),
            pltpu.VMEM((3, H, HD, rows), BF16), pltpu.VMEM((L, HD), BF16), pltpu.VMEM((HD + 16, L), BF16),
            pltpu.VMEM((1, MB, HD, L), BF16), pltpu.VMEM((1, H, HD, rows), BF16),
            dma((10,)), dma((11,)), dma((7, MB)), dma((7, MB)), dma((MB,)), dma((7, MB)), dma((7, MB)), dma((MB,)),
        ],
        compiler_params=pltpu.CompilerParams(
            collective_id=collective_id, has_side_effects=True, vmem_limit_bytes=60 * MIB
        ),
        cost_estimate=pl.CostEstimate(
            flops=20 * 10**9, bytes_accessed=30 * 10**6, transcendentals=10 * 10**6
        ),
        name="latents_forward",
    )(*args)


def reduce_steps(items, sources, outs, scratch):
    n = len(items)
    mine, got, first_in, second_in, z_keep, z_first, z_second = [scratch[i * n:(i + 1) * n] for i in range(7)]
    (local_sem, core_send, core_recv, one_send, one_recv, two_send, two_recv, z_send, z_recv) = scratch[7 * n:]
    me, core, chip, mate, (far, flip_x, flip_y) = places()
    x, y = lax.rem(chip, 2), lax.div(chip, 2)
    level = lax.axis_index("grp")
    odd = lax.rem(level, 2)
    level_near = level + 1 - 2 * odd
    level_far = lax.rem(level + 2, 4)
    near_devices = (mate, 2 * flip_x + core, 2 * flip_y + core)

    def along(item, src, dst, step, other):
        return pltpu.make_async_remote_copy(
            src_ref=src, dst_ref=dst, send_sem=z_send.at[item, step], recv_sem=z_recv.at[item, step],
            device_id={"grp": other}, device_id_type=pl.DeviceIdType.MESH,
        )

    sent, cores, ones, twos, zs = [], {}, {}, {}, {}

    def add(target, one, two):
        target[...] = (one[...].astype(F32) + two[...].astype(F32)).astype(target.dtype)

    def core_sends(i):
        source, rows, row_at, columns, column_at, x_first = items[i]
        part = (pl.ds(row_at, rows), pl.ds(column_at, columns))
        there = remote(sources[source].at[:, :, 1 - core, *part], got[i], core_send.at[i], core_recv.at[i], mate)
        here = pltpu.make_async_copy(sources[source].at[:, :, core, *part], mine[i], local_sem.at[i])
        there.start()
        here.start()
        cores[i] = (there, here)
        sent.append(there)

    def core_sums(i):
        there, here = cores[i]
        there.wait_recv()
        here.wait()
        add(mine[i], mine[i], got[i])
        x_first = items[i][-1]
        away = mine[i].at[:, 1 - x] if x_first else mine[i].at[1 - y]
        peer = 2 * (flip_x if x_first else flip_y) + core
        ones[i] = remote(away, first_in[i], one_send.at[i], one_recv.at[i], peer)
        ones[i].start()
        sent.append(ones[i])

    def first_sums(i):
        x_first = items[i][-1]
        ones[i].wait_recv()
        keep = mine[i].at[:, x] if x_first else mine[i].at[y]
        add(keep, keep, first_in[i])
        away = mine[i].at[1 - y, x] if x_first else mine[i].at[y, 1 - x]
        peer = 2 * (flip_y if x_first else flip_x) + core
        twos[i] = remote(away, second_in[i], two_send.at[i], two_recv.at[i], peer)
        twos[i].start()
        sent.append(twos[i])

    def halves(i):
        half = items[i][1] // 2
        keep = pl.ds(pl.multiple_of(odd * half, half), half)
        away = pl.ds(pl.multiple_of((1 - odd) * half, half), half)
        return keep, away

    def second_sums(i):
        keep, away = halves(i)
        twos[i].wait_recv()
        add(mine[i].at[y, x], mine[i].at[y, x], second_in[i])
        zs[i, 0] = along(i, mine[i].at[y, x, away], z_first[i], 0, level_near)
        zs[i, 0].start()
        sent.append(zs[i, 0])

    def grp_first(i):
        keep, away = halves(i)
        zs[i, 0].wait_recv()
        add(z_keep[i].at[0], mine[i].at[y, x, keep], z_first[i])
        zs[i, 1] = along(i, z_keep[i].at[0], z_second[i].at[0], 1, level_far)
        zs[i, 1].start()
        sent.append(zs[i, 1])

    def store(i, odd_half, value):
        source, rows, row_at, columns, column_at, x_first = items[i]
        half = rows // 2
        start = pl.multiple_of(row_at + odd_half * half, half)
        outs[source][pl.ds(start, half), pl.ds(column_at, columns)] = value.astype(F32)

    def grp_second(i):
        zs[i, 1].wait_recv()
        add(z_keep[i].at[1], z_keep[i].at[0], z_second[i].at[0])
        zs[i, 2] = along(i, z_keep[i].at[1], z_second[i].at[1], 2, level_near)
        zs[i, 2].start()
        sent.append(zs[i, 2])
        store(i, odd, z_keep[i][1])

    def grp_third(i):
        zs[i, 2].wait_recv()
        store(i, 1 - odd, z_second[i][1])

    def finish():
        for copy in sent:
            copy.wait_send()

    stages = (core_sends, core_sums, first_sums, second_sums, grp_first, grp_second, grp_third, finish)
    return stages, near_devices, (level_near, level_far)


def reduce_kernel(items, count, *refs):
    stages, near_devices, grp_devices = reduce_steps(items, refs[:count], refs[count:2 * count], refs[2 * count:])
    greet_all(near_devices, grp_devices)
    n = len(items)
    lags = (0, 2, 4, 5, 6, 7, 8)
    for step in range(n + lags[-1]):
        for stage, lag in zip(stages, lags):
            if 0 <= step - lag < n:
                stage(step - lag)
    stages[-1]()


def reduce_plan(arrays, cuts):
    sources, items = [], []
    for source, (array, cut) in enumerate(zip(arrays, cuts)):
        rows, columns = array.shape[0] // TOK, array.shape[1]
        sources.append(array.reshape(2, 2, 2, rows, columns))
        parts = abs(cut)
        for part in range(parts):
            high, wide = (rows, columns // parts) if cut > 0 else (rows // parts, columns)
            row_at, column_at = (0, part * wide) if cut > 0 else (part * high, 0)
            items.append((source, high, row_at, wide, column_at, len(items) % 2 == 0))
    n = len(items)
    dma = pltpu.SemaphoreType.DMA
    blocks = lambda lead, part: [
        pltpu.VMEM(lead + (item[1] // part, item[3]), arrays[item[0]].dtype) for item in items
    ]
    scratch = (
        blocks((2, 2), 1) + blocks((2, 2), 1) + blocks((2,), 1) + blocks((), 1) + blocks((2,), 2) + blocks((), 2)
        + blocks((2,), 2) + [dma((n,)) for unused in range(7)] + [dma((n, 3)), dma((n, 3))]
    )
    outs = [jax.ShapeDtypeStruct((array.shape[0] // TOK, array.shape[1]), F32) for array in arrays]
    return sources, tuple(items), outs, scratch


def reduce_grads(collective_id, arrays, cuts):
    sources, items, outs, scratch = reduce_plan(arrays, cuts)
    return pl.pallas_call(
        functools.partial(reduce_kernel, items, len(arrays)),
        in_specs=[pl.BlockSpec(memory_space=pl.ANY)] * len(arrays),
        out_specs=[pl.BlockSpec(memory_space=pltpu.VMEM)] * len(arrays),
        out_shape=outs,
        scratch_shapes=scratch,
        compiler_params=pltpu.CompilerParams(
            collective_id=collective_id, has_side_effects=True, vmem_limit_bytes=56 * MIB
        ),
        name="reduce_grads",
    )(*sources)


def latents_backward_kernel(items, *refs):
    (mgrad_ref, packed_ref, exact_ref, lse_ref, up_ref, mmid_ref, fmid_ref, att_ref, clse_ref, ow_ref, fgain_ref,
     fup_ref, fdown_ref, mgain_ref, proj_ref) = refs[:15]
    count = max(item[0] for item in items) + 1
    sources = refs[15:15 + count]
    (agrad_ref, fig_ref, lup_ref, dup_ref, ddown_ref, dproj_ref, dout_ref, dmgain_ref, dfgain_ref) = refs[
        15 + count:24 + count]
    reduced = refs[24 + count:24 + 2 * count]
    rest = refs[24 + 2 * count:]
    (heads, exact, ups, mmid, fmid, att, ow, fup, fdown, proj, keys, values, upstream_heads, key_acc, value_acc,
     grads, back, agrad, lup, dup, ddown, dproj, dout, hidden,
     load_sem, store_sem, send_a, recv_a, local_a, send_b, recv_b, local_b) = rest[:32]
    me, peers = all_peers()
    reducer, near_devices, grp_devices = reduce_steps(items, sources, reduced, rest[32:])
    core_sends, core_sums, first_sums, second_sums, grp_first, grp_second, grp_third, finish = reducer

    def reduce_all(stage):
        for item in range(len(items)):
            stage(item)

    names = ("heads", "exact", "fmid", "fup", "up", "mmid", "proj", "fdown", "att", "ow")
    loads = {}
    for i, (source, target) in enumerate((
        (packed_ref, heads), (exact_ref, exact), (fmid_ref, fmid), (fup_ref, fup), (up_ref, ups), (mmid_ref, mmid),
        (proj_ref, proj), (fdown_ref, fdown), (att_ref, att), (ow_ref, ow),
    )):
        loads[names[i]] = pltpu.make_async_copy(source, target, load_sem.at[i])
        loads[names[i]].start()
    stores = []

    def store(source, target):
        stores.append(pltpu.make_async_copy(source, target, store_sem.at[len(stores)]))
        stores[-1].start()

    greet_all(peers, grp_devices)
    outward = [
        head_copies(mgrad_ref, upstream_heads, True, member, me, peers, send_a, recv_a, local_a) for member in range(MB)
    ]
    backward = [head_copies(back, grads, False, member, me, peers, send_b, recv_b, local_b) for member in range(MB)]
    for copies, here in outward:
        for copy in copies:
            copy.start()
        here.start()
    reduce_all(core_sends)
    loads["fmid"].wait()
    loads["fup"].wait()
    first_hat, first_inverse = norm_parts(fmid[...])
    first_normed = (first_hat * fgain_ref[...]).astype(BF16)
    hidden[...] = nn(first_normed, fup[...])
    loads["heads"].wait()
    loads["exact"].wait()
    for member in range(MB):
        keys[...] = heads[1, member].T
        values[...] = heads[2, member].T
        key_acc[...] = jnp.zeros_like(key_acc)
        value_acc[...] = jnp.zeros_like(value_acc)
        copies, here = outward[member]
        for copy in copies:
            copy.wait_recv()
        here.wait()

        def attend_back(step, carry, member=member):
            at = pl.ds(pl.multiple_of(step * QB_BACK, QB_BACK), QB_BACK)
            queries = heads[0, member, :, at]
            upstream = upstream_heads[0, member, :, at]
            inner = jnp.sum(upstream.astype(F32) * exact[member, :, at], axis=0, keepdims=True)
            softened = jnp.exp2(nn(keys[...], queries) - lse_ref[member, 0:1, at])
            logit_grad = (softened * (nn(values[...], upstream) - inner)).astype(BF16)
            value_acc[...] += nt(upstream, softened.astype(BF16))
            key_acc[...] += nt(queries, logit_grad)
            grads[0, member, :, at] = (nn(heads[1, member], logit_grad) * HD ** (-0.5)).astype(BF16)
            return carry

        steps = L // QB_BACK
        lax.fori_loop(0, steps // 2, attend_back, 0)
        if member == 0:
            reduce_all(core_sums)
        else:
            reduce_all(first_sums)
        lax.fori_loop(steps // 2, steps, attend_back, 0)
        grads[1, member] = (key_acc[...] * LN2).astype(BF16)
        grads[2, member] = value_acc[...].astype(BF16)
        for copy in backward[member][0] + [backward[member][1]]:
            copy.start()
    loads["up"].wait()
    loads["mmid"].wait()
    loads["proj"].wait()
    loads["fdown"].wait()
    mixer_hat, mixer_inverse = norm_parts(mmid[...])
    mixer_normed = (mixer_hat * mgain_ref[...]).astype(BF16).T
    reduce_all(second_sums)
    for copies, here in backward:
        for copy in copies:
            copy.wait_recv()
        here.wait()
    packed_grad = back[...].reshape(3 * D, MB * ROWS)
    normed_grad = nn(proj[...], packed_grad).T
    residual, gain_rows = norm_pull(mixer_hat, mixer_inverse, mgain_ref[...], normed_grad)
    dmgain_ref[...] = jnp.sum(gain_rows, axis=0, keepdims=True)
    upstream = ups[...] + residual
    dproj[...] = nt(mixer_normed, packed_grad).astype(BF16)
    store(dproj, dproj_ref)
    reduce_all(grp_first)
    grad = upstream.astype(BF16)
    normed_grad = jnp.zeros((MB * ROWS, D), F32)
    for part in range(2):
        cut = slice(part * FF // 2, (part + 1) * FF // 2)
        act, slope = gelu_parts(hidden[:, cut])
        hidden_grad = (slope * nt(grad, fdown[cut])).astype(BF16)
        normed_grad = normed_grad + nt(hidden_grad, fup[:, cut])
        ddown[cut] = tn(act.astype(BF16), grad).astype(BF16)
        dup[:, cut] = tn(first_normed, hidden_grad).astype(BF16)
    store(ddown, ddown_ref)
    store(dup, dup_ref)
    reduce_all(grp_second)
    residual, gain_rows = norm_pull(first_hat, first_inverse, fgain_ref[...], normed_grad)
    dfgain_ref[...] = jnp.sum(gain_rows, axis=0, keepdims=True)
    upstream = upstream + residual
    lup[...] = upstream
    store(lup, lup_ref)
    grad = upstream.astype(BF16)
    loads["att"].wait()
    loads["ow"].wait()
    attended = att[...].reshape(MB * ROWS, D)
    attended_grad = nt(grad, ow[...]).astype(BF16)
    agrad[...] = attended_grad.reshape(MB, ROWS, D)
    store(agrad, agrad_ref)
    inner = jnp.sum(attended_grad.astype(F32) * attended, axis=1, keepdims=True)
    for member in range(MB):
        rows = slice(member * ROWS, (member + 1) * ROWS)
        spare = jnp.zeros((6, ROWS), F32)
        fig_ref[member] = jnp.concatenate(
            [clse_ref[member, 0:1], to_rows(inner[rows], inner[rows])[0:1], spare], axis=0
        )
    dout[...] = tn(attended.astype(BF16), grad).astype(BF16)
    store(dout, dout_ref)
    reduce_all(grp_third)
    finish()
    for copy in stores:
        copy.wait()
    for copies, here in outward + backward:
        for copy in copies:
            copy.wait_send()


def latents_backward(collective_id, arrays, *args):
    dma = pltpu.SemaphoreType.DMA
    vmem = pl.BlockSpec(memory_space=pltpu.VMEM)
    hbm = pl.BlockSpec(memory_space=pl.ANY)
    rows = MB * ROWS
    sources, items, reduced, reduce_scratch = reduce_plan(arrays, (1,) * len(arrays))
    stored = [
        ((MB, ROWS, D), BF16), ((MB, 8, ROWS), F32), ((rows, D), F32), ((D, FF), BF16), ((FF, D), BF16),
        ((D, 3 * D), BF16), ((D, D), BF16), ((1, D), F32), ((1, D), F32),
    ]
    return pl.pallas_call(
        functools.partial(latents_backward_kernel, items),
        in_specs=[hbm, hbm, hbm, vmem, hbm, hbm, hbm, hbm, vmem, hbm, vmem, hbm, hbm, vmem, hbm] + [hbm] * len(arrays),
        out_specs=[hbm, vmem] + [hbm] * 5 + [vmem] * (2 + len(arrays)),
        out_shape=[jax.ShapeDtypeStruct(shape, kind) for shape, kind in stored] + reduced,
        scratch_shapes=[
            pltpu.VMEM((3, MB, HD, L), BF16), pltpu.VMEM((MB, HD, L), F32), pltpu.VMEM((rows, D), F32),
            pltpu.VMEM((rows, D), F32), pltpu.VMEM((rows, D), F32), pltpu.VMEM((MB, ROWS, D), F32),
            pltpu.VMEM((D, D), BF16), pltpu.VMEM((D, FF), BF16), pltpu.VMEM((FF, D), BF16),
            pltpu.VMEM((D, 3 * D), BF16), pltpu.VMEM((L, HD), BF16), pltpu.VMEM((L, HD), BF16),
            pltpu.VMEM((1, MB, HD, L), BF16), pltpu.VMEM((HD, L), F32), pltpu.VMEM((HD, L), F32),
            pltpu.VMEM((3, MB, HD, L), BF16), pltpu.VMEM((3, H, HD, rows), BF16),
            pltpu.VMEM((MB, ROWS, D), BF16), pltpu.VMEM((rows, D), F32), pltpu.VMEM((D, FF), BF16),
            pltpu.VMEM((FF, D), BF16), pltpu.VMEM((D, 3 * D), BF16), pltpu.VMEM((D, D), BF16),
            pltpu.VMEM((rows, FF), F32),
            dma((10,)), dma((6,)), dma((7, MB)), dma((7, MB)), dma((MB,)), dma((7, MB)), dma((7, MB)), dma((MB,)),
        ] + reduce_scratch,
        compiler_params=pltpu.CompilerParams(
            collective_id=collective_id, has_side_effects=True, vmem_limit_bytes=61 * MIB
        ),
        cost_estimate=pl.CostEstimate(
            flops=35 * 10**9, bytes_accessed=36 * 10**6, transcendentals=10 * 10**6
        ),
        name="latents_backward",
    )(*args, *sources)


def fast_body(
    tokens,
    latents,
    segments,
    scene_mask,
    counts,
    token_gain,
    query_gain,
    query_weight,
    key_weight,
    value_weight,
    output_weight,
    first_gain,
    first_up,
    first_down,
    mixer_gain,
    mixer_project,
    mixer_output,
    second_gain,
    second_up,
    second_down,
    cotangent,
):
    me = lax.axis_index("tok")
    scenes = (segments[0][:, None], scene_mask[0], counts[0][:, :, None])
    keys, values, queries, attended, lse = cross_forward(
        0, tokens, latents, token_gain[None], query_gain[None], query_weight, key_weight, value_weight, *scenes
    )
    (latents_out, first_mid, mixer_mid, packed, exact, head_lse, upstream, mixed_grad, d_second_down, d_second_up,
     d_mixer_output, d_second_gain) = latents_forward(
        1, latents, attended, cotangent, output_weight, first_gain[None], first_up, first_down, mixer_gain[None],
        mixer_project, mixer_output, second_gain[None], second_up, second_down,
    )
    (attended_grad, figures, upstream, d_first_up, d_first_down, d_project, d_output, d_mixer_gain, d_first_gain,
     o_second_up, o_second_down, o_mixer_output) = latents_backward(
        2, [d_second_up, d_second_down, d_mixer_output], mixed_grad, packed, exact, head_lse, upstream, mixer_mid,
        first_mid, attended, lse, output_weight, first_gain[None], first_up, first_down, mixer_gain[None], mixer_project,
    )
    query_grad, tokens_grad, d_key, d_value, d_token_gain = cross_backward(
        5, tokens, token_gain[None], key_weight, value_weight, *scenes, keys, values, queries,
        attended_grad, figures,
    )
    query_grad = query_grad.reshape(MB * ROWS, D)
    latent_in = lax.dynamic_slice_in_dim(latents[0], me * ROWS, ROWS, 1).reshape(MB * ROWS, D)
    latent_in, query_grad = lax.optimization_barrier((latent_in, query_grad))
    latent_normed = norm_rows(latent_in, query_gain).astype(BF16)
    d_query = tn(latent_normed, query_grad)
    latent_grad, d_query_gain = norm_back(latent_in, query_gain, nt(query_grad, query_weight))
    latent_grad = upstream + latent_grad

    gains = jnp.stack([d_token_gain[0], d_query_gain, d_first_gain[0], d_mixer_gain[0], d_second_gain[0]])
    gains = jnp.pad(
        gains.reshape(5, TOK, D // TOK).transpose(1, 0, 2), ((0, 0), (0, 11), (0, 128 - D // TOK))
    ).reshape(TOK * 16, 128)
    o_first_up, o_first_down, o_project, o_output, o_key, o_value, o_query, o_gains = reduce_grads(
        7,
        [d_first_up, d_first_down, d_project, d_output, d_key, d_value, d_query.astype(BF16), gains],
        (2, -2, 2, 1, 1, 1, 1, 1),
    )
    o_gains = o_gains[:, :D // TOK]
    return (
        latents_out,
        latent_grad.reshape(1, MB, ROWS, D),
        tokens_grad,
        o_gains[0],
        o_gains[1],
        o_query,
        o_key,
        o_value,
        o_output,
        o_gains[2],
        o_first_up,
        o_first_down,
        o_gains[3],
        o_project,
        o_mixer_output,
        o_gains[4],
        o_second_up,
        o_second_down,
    )


IN_SPECS = (
    P("grp", None, "tok", None),
    P("grp", None, None, None),
    P("grp", None, "tok"),
    P("grp", None, None, None),
    P("grp", None, "tok"),
    P(),
    P(),
    P(),
    P(),
    P(),
    P(),
    P(),
    P(),
    P(),
    P(),
    P(),
    P(),
    P(),
    P(),
    P(),
    P("grp", None, "tok", None),
)
OUT_SPECS = (
    P("grp", None, "tok", None),
    P("grp", None, "tok", None),
    P("grp", None, "tok", None),
    P("tok"),
    P("tok"),
    P("tok", None),
    P("tok", None),
    P("tok", None),
    P("tok", None),
    P("tok"),
    P("tok", None),
    P("tok", None),
    P("tok"),
    P("tok", None),
    P("tok", None),
    P("tok"),
    P("tok", None),
    P("tok", None),
)


def solution(mesh):
    return jax.shard_map(
        fast_body if mesh.shape["tok"] == TOK else general_body,
        mesh=mesh,
        in_specs=IN_SPECS,
        out_specs=OUT_SPECS,
        check_vma=False,
    )
```

```python
import functools

import jax
import jax.numpy as jnp
from jax import lax
from jax.experimental import pallas as pl
from jax.experimental.pallas import tpu as pltpu
from jax.sharding import PartitionSpec as P

D = 512
L = 2048
H = 8
HD = 64
TOK_DEV = 1024
MB = 2
SCENES = 8
LGROUPS = 8


EPS = 1e-05
NEG = -1e30


def norm_rows(values, gain):
    centre = values - jnp.mean(values, axis=-1, keepdims=True)
    spread = jnp.mean(centre * centre, axis=-1, keepdims=True)
    return centre * lax.rsqrt(spread + EPS) * gain


def norm_back(values, gain, upstream):
    unused, pull = jax.vjp(norm_rows, values, gain)
    return pull(upstream)


def gelu_back(hidden, upstream):
    unused, pull = jax.vjp(jax.nn.gelu, hidden)
    return pull(upstream)[0]


def product_plain(left, right):
    return jnp.dot(left, right, preferred_element_type=jnp.float32)


def product_rows(left, right):
    return lax.dot_general(
        left, right, (((0,), (0,)), ((), ())), preferred_element_type=jnp.float32
    )


def product_cols(left, right):
    return lax.dot_general(
        left, right, (((1,), (1,)), ((), ())), preferred_element_type=jnp.float32
    )


def add_term(store, name, value):
    if name in store:
        store[name] = store[name] + value
    else:
        store[name] = value


def project_tokens(tokens, member, token_gain, key_weight, value_weight):
    source = tokens[0, member].astype(jnp.float32)
    normed = norm_rows(source, token_gain).astype(jnp.bfloat16)
    key_rows = product_plain(normed, key_weight).astype(jnp.bfloat16)
    value_rows = product_plain(normed, value_weight).astype(jnp.bfloat16)
    return (source, normed, key_rows, value_rows)


def mlp_forward(residual, gain, up_weight, down_weight):
    normed = norm_rows(residual, gain).astype(jnp.bfloat16)
    hidden = product_plain(normed, up_weight)
    active = jax.nn.gelu(hidden).astype(jnp.bfloat16)
    return (residual + product_plain(active, down_weight), (normed, hidden, active))


def mlp_backward(residual, gain, up_weight, down_weight, saved, upstream):
    normed, hidden, active = saved
    grad_low = upstream.astype(jnp.bfloat16)
    grad_down = product_rows(active, grad_low)
    hidden_grad = gelu_back(hidden, product_cols(grad_low, down_weight)).astype(jnp.bfloat16)
    grad_up = product_rows(normed, hidden_grad)
    residual_grad, grad_gain = norm_back(residual, gain, product_cols(hidden_grad, up_weight))
    return (upstream + residual_grad, grad_gain, grad_up, grad_down)


def mixer_forward(residual, gain, project, output):
    own_rows = residual.shape[0]
    normed = norm_rows(residual, gain).astype(jnp.bfloat16)
    packed = product_plain(normed, project).astype(jnp.bfloat16)
    pair_rows = lax.all_gather(packed[:, D:], "tok", axis=0, tiled=True)
    every = pair_rows.shape[0]
    own_queries = packed[:, :D].reshape(own_rows, H, HD)
    keys = pair_rows[:, :D].reshape(every, H, HD)
    values = pair_rows[:, D:].reshape(every, H, HD)
    logits = jnp.einsum(
        "qhd,khd->hqk", own_queries, keys, preferred_element_type=jnp.float32
    ) * HD ** (-0.5)
    peak_row = jnp.max(logits, axis=-1, keepdims=True)
    raised = jnp.exp(logits - peak_row)
    softened = raised / jnp.sum(raised, axis=-1, keepdims=True)
    softened_low = softened.astype(jnp.bfloat16)
    mixed_rows = jnp.einsum(
        "hqk,khd->qhd", softened_low, values, preferred_element_type=jnp.float32
    )
    mixed_rows = mixed_rows.reshape(own_rows, D).astype(jnp.bfloat16)
    return (
        residual + product_plain(mixed_rows, output),
        (normed, own_queries, keys, values, softened, softened_low, mixed_rows),
    )


def mixer_backward(residual, gain, project, output, saved, upstream):
    normed, own_queries, keys, values, softened, softened_low, mixed_rows = saved
    own_rows = upstream.shape[0]
    every = keys.shape[0]
    grad_low = upstream.astype(jnp.bfloat16)
    grad_output = product_rows(mixed_rows, grad_low)
    mixed_grad = product_cols(grad_low, output).astype(jnp.bfloat16).reshape(own_rows, H, HD)
    value_grad = jnp.einsum(
        "hqk,qhd->khd", softened_low, mixed_grad, preferred_element_type=jnp.float32
    )
    soft_grad = jnp.einsum("qhd,khd->hqk", mixed_grad, values, preferred_element_type=jnp.float32)
    logit_grad = softened * (soft_grad - jnp.sum(soft_grad * softened, axis=-1, keepdims=True))
    logit_grad = logit_grad.astype(jnp.bfloat16)
    query_grad = jnp.einsum(
        "hqk,khd->qhd", logit_grad, keys, preferred_element_type=jnp.float32
    ) * HD ** (-0.5)
    key_grad = jnp.einsum(
        "hqk,qhd->khd", logit_grad, own_queries, preferred_element_type=jnp.float32
    ) * HD ** (-0.5)
    pair_terms = jnp.concatenate([key_grad.reshape(every, D), value_grad.reshape(every, D)], axis=1)
    pair_grad = lax.psum_scatter(
        pair_terms.astype(jnp.bfloat16), "tok", scatter_dimension=0, tiled=True
    ).astype(jnp.float32)
    packed_grad = jnp.concatenate([query_grad.reshape(own_rows, D), pair_grad], axis=1).astype(
        jnp.bfloat16
    )
    grad_project = product_rows(normed, packed_grad)
    residual_grad, grad_gain = norm_back(residual, gain, product_cols(packed_grad, project))
    return (upstream + residual_grad, grad_gain, grad_project, grad_output)


def general_body(
    tokens,
    latents,
    segments,
    scene_mask,
    counts,
    token_gain,
    query_gain,
    query_weight,
    key_weight,
    value_weight,
    output_weight,
    first_gain,
    first_up,
    first_down,
    mixer_gain,
    mixer_project,
    mixer_output,
    second_gain,
    second_up,
    second_down,
    cotangent,
):
    scale = D ** (-0.5)
    shards = lax.axis_size("tok")
    own_rows = L // shards
    row_start = lax.axis_index("tok") * own_rows
    latent_group = jnp.arange(L) // (L // LGROUPS)
    latent_onehot = (latent_group[:, None] == jnp.arange(LGROUPS)[None, :]).astype(jnp.float32)
    token_place = jnp.arange(TOK_DEV)
    records = []
    latent_outs = []
    for member in range(MB):
        record = {}
        source, normed, key_rows, value_rows = project_tokens(
            tokens, member, token_gain, key_weight, value_weight
        )
        record["token_side"] = (source, normed, key_rows, value_rows)
        scene_onehot = (segments[0, member][:, None] == jnp.arange(SCENES)[None, :]).astype(
            jnp.float32
        )
        token_seen = jnp.dot(scene_onehot, scene_mask[0, member].astype(jnp.float32))
        visible = product_cols(latent_onehot, token_seen)
        alive = token_place < counts[0, member, 0]
        allowed = (visible > 0.5) & alive[None, :]
        latent_every = latents[0, member]
        normed_every = norm_rows(latent_every, query_gain).astype(jnp.bfloat16)
        queries = product_plain(normed_every, query_weight).astype(jnp.bfloat16)
        scores = jnp.where(allowed, product_cols(queries, key_rows) * scale, NEG)
        row_top = lax.pmax(jnp.max(scores, axis=1), "tok")
        unnormed = jnp.exp(scores - row_top[:, None])
        row_total, weighted = (
            lax.psum_scatter(
                jnp.sum(unnormed, axis=1).astype(jnp.bfloat16),
                "tok",
                scatter_dimension=0,
                tiled=True,
            ).astype(jnp.float32),
            lax.psum_scatter(
                product_plain(unnormed.astype(jnp.bfloat16), value_rows).astype(jnp.bfloat16),
                "tok",
                scatter_dimension=0,
                tiled=True,
            ).astype(jnp.float32),
        )
        latent_in = lax.dynamic_slice_in_dim(latent_every, row_start, own_rows, 0)
        latent_normed = lax.dynamic_slice_in_dim(normed_every, row_start, own_rows, 0)
        attended = weighted / row_total[:, None]
        attended_low = attended.astype(jnp.bfloat16)
        first_mid = latent_in + product_plain(attended_low, output_weight)
        mixer_mid, first_saved = mlp_forward(first_mid, first_gain, first_up, first_down)
        second_mid, mixer_saved = mixer_forward(mixer_mid, mixer_gain, mixer_project, mixer_output)
        final_rows, second_saved = mlp_forward(second_mid, second_gain, second_up, second_down)
        latent_outs.append(final_rows)
        record["latent_side"] = (
            allowed,
            latent_in,
            latent_normed,
            queries,
            row_top,
            row_total,
            attended,
            attended_low,
            first_mid,
            mixer_mid,
            second_mid,
            first_saved,
            mixer_saved,
            second_saved,
        )
        records.append(record)
    grads = {}
    latent_grads = []
    token_grads = []
    for member in range(MB):
        record = records[member]
        source, normed, key_rows, value_rows = record["token_side"]
        (
            allowed,
            latent_in,
            latent_normed,
            queries,
            row_top,
            row_total,
            attended,
            attended_low,
            first_mid,
            mixer_mid,
            second_mid,
            first_saved,
            mixer_saved,
            second_saved,
        ) = record["latent_side"]
        second_back = mlp_backward(
            second_mid, second_gain, second_up, second_down, second_saved, cotangent[0, member]
        )
        add_term(grads, "second_gain", second_back[1])
        add_term(grads, "second_up", second_back[2])
        add_term(grads, "second_down", second_back[3])
        mixer_back = mixer_backward(
            mixer_mid, mixer_gain, mixer_project, mixer_output, mixer_saved, second_back[0]
        )
        add_term(grads, "mixer_gain", mixer_back[1])
        add_term(grads, "mixer_project", mixer_back[2])
        add_term(grads, "mixer_output", mixer_back[3])
        first_back = mlp_backward(
            first_mid, first_gain, first_up, first_down, first_saved, mixer_back[0]
        )
        add_term(grads, "first_gain", first_back[1])
        add_term(grads, "first_up", first_back[2])
        add_term(grads, "first_down", first_back[3])
        latent_upstream = first_back[0]
        grad_low = latent_upstream.astype(jnp.bfloat16)
        add_term(grads, "output_weight", product_rows(attended_low, grad_low))
        attended_grad = lax.optimization_barrier(
            product_cols(grad_low, output_weight).astype(jnp.bfloat16)
        ).astype(jnp.float32)
        weighted_grad = (attended_grad / row_total[:, None]).astype(jnp.bfloat16)
        total_grad = -jnp.sum(attended_grad * attended, axis=1) / row_total
        weighted_every, total_every = (
            lax.all_gather(
                weighted_grad.astype(jnp.float32).astype(jnp.bfloat16), "tok", axis=0, tiled=True
            ).astype(jnp.float32),
            lax.all_gather(total_grad.astype(jnp.bfloat16), "tok", axis=0, tiled=True).astype(
                total_grad.dtype
            ),
        )
        weighted_every = weighted_every.astype(jnp.bfloat16)
        scores = jnp.where(allowed, product_cols(queries, key_rows) * scale, NEG)
        unnormed = jnp.exp(scores - row_top[:, None])
        unnormed_grad = product_cols(weighted_every, value_rows) + total_every[:, None]
        score_grad = (unnormed * unnormed_grad).astype(jnp.bfloat16)
        value_grad = product_rows(unnormed.astype(jnp.bfloat16), weighted_every).astype(
            jnp.bfloat16
        )
        key_grad = (product_rows(score_grad, queries) * scale).astype(jnp.bfloat16)
        query_grad = lax.psum_scatter(
            (product_plain(score_grad, key_rows) * scale).astype(jnp.bfloat16),
            "tok",
            scatter_dimension=0,
            tiled=True,
        )
        add_term(grads, "key_weight", product_rows(normed, key_grad))
        add_term(grads, "value_weight", product_rows(normed, value_grad))
        normed_grad = product_cols(key_grad, key_weight) + product_cols(value_grad, value_weight)
        source_grad, gain_grad = norm_back(source, token_gain, normed_grad)
        add_term(grads, "token_gain", gain_grad)
        token_grads.append(source_grad)
        add_term(grads, "query_weight", product_rows(latent_normed, query_grad))
        latent_grad, gain_grad = norm_back(
            latent_in, query_gain, product_cols(query_grad, query_weight)
        )
        add_term(grads, "query_gain", gain_grad)
        latent_grads.append(latent_upstream + latent_grad)
    parts = (
        lax.psum_scatter(
            grads["token_gain"].astype(jnp.bfloat16), "tok", scatter_dimension=0, tiled=True
        ).astype(jnp.float32),
        lax.psum_scatter(
            grads["query_gain"].astype(jnp.bfloat16), "tok", scatter_dimension=0, tiled=True
        ).astype(jnp.float32),
        lax.psum_scatter(
            grads["query_weight"].astype(jnp.bfloat16), "tok", scatter_dimension=0, tiled=True
        ).astype(jnp.float32),
        lax.psum_scatter(
            grads["key_weight"].astype(jnp.bfloat16), "tok", scatter_dimension=0, tiled=True
        ).astype(jnp.float32),
        lax.psum_scatter(
            grads["value_weight"].astype(jnp.bfloat16), "tok", scatter_dimension=0, tiled=True
        ).astype(jnp.float32),
        lax.psum_scatter(
            grads["output_weight"].astype(jnp.bfloat16), "tok", scatter_dimension=0, tiled=True
        ).astype(jnp.float32),
        lax.psum_scatter(
            grads["first_gain"].astype(jnp.bfloat16), "tok", scatter_dimension=0, tiled=True
        ).astype(jnp.float32),
        lax.psum_scatter(
            grads["first_up"].astype(jnp.bfloat16), "tok", scatter_dimension=0, tiled=True
        ).astype(jnp.float32),
        lax.psum_scatter(
            grads["first_down"].astype(jnp.bfloat16), "tok", scatter_dimension=0, tiled=True
        ).astype(jnp.float32),
        lax.psum_scatter(
            grads["mixer_gain"].astype(jnp.bfloat16), "tok", scatter_dimension=0, tiled=True
        ).astype(jnp.float32),
        lax.psum_scatter(
            grads["mixer_project"].astype(jnp.bfloat16), "tok", scatter_dimension=0, tiled=True
        ).astype(jnp.float32),
        lax.psum_scatter(
            grads["mixer_output"].astype(jnp.bfloat16), "tok", scatter_dimension=0, tiled=True
        ).astype(jnp.float32),
        lax.psum_scatter(
            grads["second_gain"].astype(jnp.bfloat16), "tok", scatter_dimension=0, tiled=True
        ).astype(jnp.float32),
        lax.psum_scatter(
            grads["second_up"].astype(jnp.bfloat16), "tok", scatter_dimension=0, tiled=True
        ).astype(jnp.float32),
        lax.psum_scatter(
            grads["second_down"].astype(jnp.bfloat16), "tok", scatter_dimension=0, tiled=True
        ).astype(jnp.float32),
    )
    summed = (
        lax.psum(parts[0].astype(jnp.bfloat16), "grp").astype(jnp.float32),
        lax.psum(parts[1].astype(jnp.bfloat16), "grp").astype(jnp.float32),
        lax.psum(parts[2].astype(jnp.bfloat16), "grp").astype(jnp.float32),
        lax.psum(parts[3].astype(jnp.bfloat16), "grp").astype(jnp.float32),
        lax.psum(parts[4].astype(jnp.bfloat16), "grp").astype(jnp.float32),
        lax.psum(parts[5].astype(jnp.bfloat16), "grp").astype(jnp.float32),
        lax.psum(parts[6].astype(jnp.bfloat16), "grp").astype(jnp.float32),
        lax.psum(parts[7].astype(jnp.bfloat16), "grp").astype(jnp.float32),
        lax.psum(parts[8].astype(jnp.bfloat16), "grp").astype(jnp.float32),
        lax.psum(parts[9].astype(jnp.bfloat16), "grp").astype(jnp.float32),
        lax.psum(parts[10].astype(jnp.bfloat16), "grp").astype(jnp.float32),
        lax.psum(parts[11].astype(jnp.bfloat16), "grp").astype(jnp.float32),
        lax.psum(parts[12].astype(jnp.bfloat16), "grp").astype(jnp.float32),
        lax.psum(parts[13].astype(jnp.bfloat16), "grp").astype(jnp.float32),
        lax.psum(parts[14].astype(jnp.bfloat16), "grp").astype(jnp.float32),
    )
    return (
        jnp.stack(latent_outs)[None],
        jnp.stack(latent_grads)[None],
        jnp.stack(token_grads)[None],
    ) + tuple(summed)


TOK = 8
ROWS = L // TOK
FF = 2048
GR = L // LGROUPS
LOG2E = 1.4426950408889634
LN2 = 0.6931471805599453
F32 = jnp.float32
BF16 = jnp.bfloat16
MIB = 1024 * 1024


def nn(left, right):
    return lax.dot_general(left, right, (((1,), (0,)), ((), ())), preferred_element_type=F32)


def nt(left, right):
    return lax.dot_general(left, right, (((1,), (1,)), ((), ())), preferred_element_type=F32)


def tn(left, right):
    return lax.dot_general(left, right, (((0,), (0,)), ((), ())), preferred_element_type=F32)


def norm_parts(values):
    centre = values - jnp.mean(values, axis=-1, keepdims=True)
    inverse = lax.rsqrt(jnp.mean(centre * centre, axis=-1, keepdims=True) + EPS)
    return centre * inverse, inverse


def norm_pull(hat, inverse, gain, upstream):
    scaled = upstream * gain
    inner = jnp.mean(scaled * hat, axis=-1, keepdims=True)
    grad = (scaled - jnp.mean(scaled, axis=-1, keepdims=True) - hat * inner) * inverse
    return grad, upstream * hat


def places():
    me = lax.axis_index("tok")
    core = lax.rem(me, 2)
    chip = lax.div(me, 2)
    mate = me + 1 - 2 * core
    flip_x = chip + 1 - 2 * lax.rem(chip, 2)
    flip_y = lax.rem(chip + 2, 4)
    far = 3 - chip
    return me, core, chip, mate, (far, flip_x, flip_y)


def remote(src, dst, send_sem, recv_sem, peer):
    return pltpu.make_async_remote_copy(
        src_ref=src,
        dst_ref=dst,
        send_sem=send_sem,
        recv_sem=recv_sem,
        device_id={"tok": peer},
        device_id_type=pl.DeviceIdType.MESH,
    )


def greet(devices):
    barrier = pltpu.get_barrier_semaphore()
    for device in devices:
        pl.semaphore_signal(
            barrier, inc=1, device_id={"tok": device}, device_id_type=pl.DeviceIdType.MESH
        )
    pl.semaphore_wait(barrier, len(devices))


def chip_at(chip, flip):
    high, low = divmod(flip, 2) if isinstance(flip, int) else (lax.div(flip, 2), lax.rem(flip, 2))
    across = lax.rem(lax.rem(chip, 2) + low, 2)
    along = lax.rem(lax.div(chip, 2) + high, 2)
    return 2 * along + across


def mask_loads(seg_ref, mask_ref, seg_buf, mask_buf, sem):
    return (
        pltpu.make_async_copy(seg_ref.at[0], seg_buf, sem.at[0]),
        pltpu.make_async_copy(mask_ref.at[0], mask_buf, sem.at[1]),
    )


def mask_rows(seg_buf, mask_buf, count_ref, bias_ref):
    for member in range(MB):
        scene = lax.broadcasted_iota(jnp.int32, (SCENES, TOK_DEV), 0)
        place = lax.broadcasted_iota(jnp.int32, (SCENES, TOK_DEV), 1)
        hot = jnp.where((seg_buf[member:member + 1] == scene) & (place < count_ref[0, member, 0]), 1.0, 0.0)
        seen = tn(jnp.where(mask_buf[member] > 0, 1.0, 0.0).astype(BF16), hot.astype(BF16))
        bias_ref[member] = jnp.where(seen > 0.5, 0.0, NEG)


def to_rows(first, second):
    rows = first.shape[0]
    lane = lax.broadcasted_iota(jnp.int32, (rows, 128), 1)
    return jnp.where(lane == 0, first, second).T[0:8]


def cross_forward_kernel(
    tok_ref, lat_ref, tgain_ref, qgain_ref, qw_ref, kw_ref, vw_ref, seg_ref, mask_ref, count_ref,
    k_out, v_out, q_out, att_ref, lse_ref,
    tok_buf, lat_buf, keys, values, queries, bias, part, part_s, got, got_s, stage, stage_s,
    arrive, arrive_s, total, seg_buf, mask_buf,
    mask_sem, tok_sem, lat_sem, k_sem, v_sem, q_sem,
    core_send, core_recv, core_send_s, core_recv_s, chip_send, chip_recv, chip_send_s, chip_recv_s,
):
    me, core, chip, mate, others = places()
    span = 2 * ROWS

    def unpack(step):
        return lax.div(step, 4), 3 - lax.rem(step, 4)

    def lat_copy(step):
        member, flip = unpack(step)
        start = pl.multiple_of(chip_at(chip, flip) * span, span)
        return pltpu.make_async_copy(lat_ref.at[0, member, pl.ds(start, span)], lat_buf.at[step], lat_sem.at[step])

    def q_copy(step):
        member, flip = unpack(step)
        start = pl.multiple_of(chip_at(chip, flip) * span, span)
        return pltpu.make_async_copy(queries.at[step], q_out.at[member, pl.ds(start, span)], q_sem.at[step])

    def tok_copy(member):
        return pltpu.make_async_copy(tok_ref.at[0, member], tok_buf.at[member], tok_sem.at[member])

    def kv_copies(member):
        return (
            pltpu.make_async_copy(keys.at[member], k_out.at[member], k_sem.at[member]),
            pltpu.make_async_copy(values.at[member], v_out.at[member], v_sem.at[member]),
        )

    def core_copies(step):
        return (
            remote(part.at[step, 1 - core], got.at[step], core_send.at[step], core_recv.at[step], mate),
            remote(part_s.at[step, 1 - core], got_s.at[step], core_send_s.at[step], core_recv_s.at[step], mate),
        )

    def chip_copies(step):
        member, flip = unpack(step)
        peer = 2 * chip_at(chip, flip) + core
        place = 3 * member + flip - 1
        return (
            remote(stage.at[step], arrive.at[place], chip_send.at[place], chip_recv.at[place], peer),
            remote(stage_s.at[step], arrive_s.at[place], chip_send_s.at[place], chip_recv_s.at[place], peer),
        )

    tok_copy(0).start()
    masks = mask_loads(seg_ref, mask_ref, seg_buf, mask_buf, mask_sem)
    for copy in masks:
        copy.start()
    for step in range(4):
        lat_copy(step).start()
    tok_copy(1).start()
    for step in range(4, 2 * 4):
        lat_copy(step).start()
    greet([mate] + [2 * other + core for other in others])
    for copy in masks:
        copy.wait()
    mask_rows(seg_buf, mask_buf, count_ref, bias)

    def compute(step):
        member, flip = unpack(step)

        @pl.when(flip == 3)
        def _():
            tok_copy(member).wait()
            hat, inverse = norm_parts(tok_buf[member].astype(F32))
            normed = (hat * tgain_ref[...]).astype(BF16)
            keys[member] = nn(normed, kw_ref[...]).astype(BF16)
            values[member] = nn(normed, vw_ref[...]).astype(BF16)
            for copy in kv_copies(member):
                copy.start()

        lat_copy(step).wait()
        hat, inverse = norm_parts(lat_buf[step])
        normed = (hat * qgain_ref[...]).astype(BF16)
        asked = (nn(normed, qw_ref[...]) * (D ** (-0.5) * LOG2E)).astype(BF16)
        queries[step] = asked
        q_copy(step).start()
        scores = nt(asked, keys[member])
        raised = []
        for half in range(2):
            seen = bias[member, pl.ds(2 * chip_at(chip, flip) + half, 1), :]
            own = scores[half * ROWS:(half + 1) * ROWS] + seen
            top = jnp.max(own, axis=1, keepdims=True)
            own = jnp.exp2(own - top)
            part_s[step, half] = to_rows(top, jnp.sum(own, axis=1, keepdims=True))
            raised.append(own.astype(BF16))
        sums = nn(jnp.concatenate(raised, axis=0), values[member]).astype(BF16)
        for half in range(2):
            part[step, half] = sums[half * ROWS:(half + 1) * ROWS]
        for copy in core_copies(step):
            copy.start()

    def merge(one, one_s, two, two_s):
        top = jnp.maximum(one_s[0:1], two_s[0:1])
        one_w, two_w = jnp.exp2(one_s[0:1] - top), jnp.exp2(two_s[0:1] - top)
        sums = one_s[1:2] * one_w + two_s[1:2] * two_w
        spare = jnp.zeros((6, ROWS), F32)
        weights = jnp.concatenate([one_w, two_w, spare], axis=0).T
        return one * weights[:, 0:1] + two * weights[:, 1:2], jnp.concatenate([top, sums, spare], axis=0)

    def combine(step):
        member, flip = unpack(step)
        for copy in core_copies(step):
            copy.wait_recv()
        added, figures = merge(
            part[step, core].astype(F32), part_s[step, core], got[step].astype(F32), got_s[step]
        )
        stage_s[step] = figures

        @pl.when(flip > 0)
        def _():
            stage[step] = added.astype(BF16)
            for copy in chip_copies(step):
                copy.start()

        @pl.when(flip == 0)
        def _():
            total[member] = added

    def finish(member):
        added, figures = total[member], stage_s[4 * member + 3]
        for flip in (1, 2, 3):
            for copy in chip_copies(4 * member + 3 - flip):
                copy.wait_recv()
            place = 3 * member + flip - 1
            added, figures = merge(added, figures, arrive[place].astype(F32), arrive_s[place])
        spare = jnp.zeros((7, ROWS), F32)
        inverse = jnp.concatenate([1.0 / figures[1:2], spare], axis=0).T
        att_ref[member] = added * inverse[:, 0:1]
        lse_ref[member] = jnp.concatenate([figures[0:1] + jnp.log2(figures[1:2]), spare], axis=0)

    def step_body(step, carry):
        compute(step)

        @pl.when(step > 0)
        def _():
            combine(step - 1)

        return carry

    lax.fori_loop(0, 4 * MB, step_body, 0)
    combine(jnp.int32(4 * MB - 1))
    for member in range(MB):
        finish(member)
    for member in range(MB):
        for copy in kv_copies(member):
            copy.wait()
        for slot in range(4):
            step = 4 * member + slot
            q_copy(step).wait()
            for copy in core_copies(step):
                copy.wait_send()
            if slot < 3:
                for copy in chip_copies(step):
                    copy.wait_send()


def cross_forward(collective_id, *args):
    dma = pltpu.SemaphoreType.DMA
    span = 2 * ROWS
    steps = 4 * MB
    vmem = pl.BlockSpec(memory_space=pltpu.VMEM)
    hbm = pl.BlockSpec(memory_space=pl.ANY)
    return pl.pallas_call(
        cross_forward_kernel,
        in_specs=[hbm, hbm] + [vmem] * 5 + [hbm, hbm, pl.BlockSpec(memory_space=pltpu.SMEM)],
        out_specs=[hbm, hbm, hbm, vmem, vmem],
        out_shape=[
            jax.ShapeDtypeStruct((MB, TOK_DEV, D), BF16),
            jax.ShapeDtypeStruct((MB, TOK_DEV, D), BF16),
            jax.ShapeDtypeStruct((MB, L, D), BF16),
            jax.ShapeDtypeStruct((MB, ROWS, D), F32),
            jax.ShapeDtypeStruct((MB, 8, ROWS), F32),
        ],
        scratch_shapes=[
            pltpu.VMEM((MB, TOK_DEV, D), BF16),
            pltpu.VMEM((steps, span, D), F32),
            pltpu.VMEM((MB, TOK_DEV, D), BF16),
            pltpu.VMEM((MB, TOK_DEV, D), BF16),
            pltpu.VMEM((steps, span, D), BF16),
            pltpu.VMEM((MB, LGROUPS, TOK_DEV), F32),
            pltpu.VMEM((steps, 2, ROWS, D), BF16),
            pltpu.VMEM((steps, 2, 8, ROWS), F32),
            pltpu.VMEM((steps, ROWS, D), BF16),
            pltpu.VMEM((steps, 8, ROWS), F32),
            pltpu.VMEM((steps, ROWS, D), BF16),
            pltpu.VMEM((steps, 8, ROWS), F32),
            pltpu.VMEM((3 * MB, ROWS, D), BF16),
            pltpu.VMEM((3 * MB, 8, ROWS), F32),
            pltpu.VMEM((MB, ROWS, D), F32),
            pltpu.VMEM((MB, TOK_DEV), jnp.int32),
            pltpu.VMEM((MB, SCENES, LGROUPS), jnp.int32),
            dma((2,)), dma((MB,)), dma((steps,)), dma((MB,)), dma((MB,)), dma((steps,)),
        ] + [dma((steps,))] * 4 + [dma((3 * MB,))] * 4,
        compiler_params=pltpu.CompilerParams(
            collective_id=collective_id, has_side_effects=True, vmem_limit_bytes=56 * MIB
        ),
        cost_estimate=pl.CostEstimate(
            flops=14 * 10**9, bytes_accessed=22 * 10**6, transcendentals=4 * 10**6
        ),
        name="cross_forward",
    )(*args)


def cross_backward_kernel(
    items,
    tok_ref, tgain_ref, kw_ref, vw_ref, seg_ref, mask_ref, count_ref, k_ref, v_ref, q_ref, up_ref, fig_ref,
    lat_ref, lup_ref, qgain_ref, qw_ref, fgain_ref, mgain_ref, sgain_ref, *refs,
):
    count = len(items)
    parts = refs[:count]
    dlat_ref, dtok_ref, dkw_ref, dvw_ref, dqw_ref, gains_ref = refs[count:count + 6]
    sums = refs[count + 6:2 * count + 6]
    rest = refs[2 * count + 6:]
    grp, grp_devices = grp_steps(items, parts, sums, rest[CROSS_SCRATCH:])
    (tok_buf, keys, values, queries, ups, figs, bias, part, got, stage, arrive, far_in, total, dk, dv, dtok, dkw, dvw,
     dgain_ref, lat, lup, dlat, seg_buf, mask_buf, mask_sem, tail_sem,
     tok_sem, k_sem, v_sem, q_sem, out_sem, near_send, near_recv, far_send, far_recv, on_send, on_recv, own_sem,
     fig_send, fig_recv, core_send, core_recv, chip_send, chip_recv, half_send, half_recv) = rest[:CROSS_SCRATCH]
    me, core, chip, mate, others = places()
    span = 2 * ROWS

    def slot_of(step):
        member, place = lax.div(step, 4), lax.rem(step, 4)
        return member, place + member * (3 - 2 * place)

    def loads(slot):
        member, flip = divmod(slot, 4)
        start = pl.multiple_of(chip_at(chip, flip) * span, span)
        return pltpu.make_async_copy(q_ref.at[member, pl.ds(start, span)], queries.at[slot], q_sem.at[slot])

    def tok_copies(member):
        return (
            pltpu.make_async_copy(k_ref.at[member], keys.at[member], k_sem.at[member]),
            pltpu.make_async_copy(v_ref.at[member], values.at[member], v_sem.at[member]),
            pltpu.make_async_copy(tok_ref.at[0, member], tok_buf.at[member], tok_sem.at[member]),
        )

    def out_copy(member):
        return pltpu.make_async_copy(dtok.at[member], dtok_ref.at[0, member], out_sem.at[member])

    def own_copies(member):
        slot = 4 * member
        return (
            pltpu.make_async_copy(up_ref.at[member], ups.at[slot, core], own_sem.at[member, 0]),
            pltpu.make_async_copy(fig_ref.at[member], figs.at[slot, core], own_sem.at[member, 1]),
        )

    def near_copies(member):
        slot = 4 * member
        return [
            remote(up_ref.at[member], ups.at[slot, core], near_send.at[member, 0], near_recv.at[member, 0], mate),
            remote(fig_ref.at[member], figs.at[slot, core], near_send.at[member, 1], near_recv.at[member, 1], mate),
        ]

    half_rows = (pl.ds(0, ROWS // 2), pl.ds(ROWS // 2, ROWS // 2))

    def far_copies(slot):
        member, flip = slot // 4, slot % 4
        peer = 2 * chip_at(chip, flip) + core
        if flip < 3:
            return [
                remote(up_ref.at[member], ups.at[slot, core], far_send.at[slot, 0], far_recv.at[slot, 0], peer),
                remote(fig_ref.at[member], figs.at[slot, core], far_send.at[slot, 1], far_recv.at[slot, 1], peer),
            ]
        copies = []
        for half, (held, toward) in enumerate(((1, 2), (2, 1))):
            copies.append(remote(
                ups.at[4 * member + held, core, half_rows[half]], ups.at[slot, core, half_rows[half]],
                far_send.at[slot, half], far_recv.at[slot, half], 2 * chip_at(chip, toward) + core,
            ))
        copies.append(remote(
            figs.at[4 * member + 1, core], figs.at[slot, core], fig_send.at[member], fig_recv.at[member],
            2 * chip_at(chip, 2) + core,
        ))
        return copies

    def on_copies(slot):
        return (
            remote(ups.at[slot, core], ups.at[slot, core], on_send.at[slot, 0], on_recv.at[slot, 0], mate),
            remote(figs.at[slot, core], figs.at[slot, core], on_send.at[slot, 1], on_recv.at[slot, 1], mate),
        )

    def pass_on(slot):
        for copy in far_copies(slot):
            copy.wait_recv()
        for copy in on_copies(slot):
            copy.start()

    def pass_near(member):
        pass_on(4 * member + 1)
        pass_on(4 * member + 2)
        for copy in far_copies(4 * member + 3):
            copy.start()

    def half_copy(member, half):
        return remote(
            stage.at[4 * member + 3, half_rows[half]], far_in.at[member, half], half_send.at[member, half],
            half_recv.at[member, half], 2 * chip_at(chip, half + 1) + core,
        )

    def half_copies(member):
        return [half_copy(member, half) for half in range(2)]

    def core_copy(slot):
        return remote(part.at[slot, 1 - core], got.at[slot], core_send.at[slot], core_recv.at[slot], mate)

    def chip_copy(slot):
        member, flip = slot // 4, slot % 4
        peer = 2 * chip_at(chip, flip) + core
        place = 2 * member + flip - 1
        return remote(stage.at[slot], arrive.at[place], chip_send.at[place], chip_recv.at[place], peer)

    def relay(member):
        for half in range(2):
            half_copy(member, half).wait_recv()
            slot = 4 * member + 2 - half
            joined = stage.at[slot, half_rows[half]]
            add(joined, joined, far_in.at[member, half])
            chip_copy(slot).start()

    masks = mask_loads(seg_ref, mask_ref, seg_buf, mask_buf, mask_sem)
    for copy in masks:
        copy.start()
    own_rows = pl.ds(pl.multiple_of(me * ROWS, ROWS), ROWS)
    tails = (
        pltpu.make_async_copy(lat_ref.at[0, :, own_rows], lat, tail_sem.at[0]),
        pltpu.make_async_copy(lup_ref, lup, tail_sem.at[1]),
    )
    for copy in own_copies(0):
        copy.start()
    for copy in tok_copies(0):
        copy.start()
    for flip in (0, 1, 2, 3):
        loads(flip).start()
    for copy in own_copies(1):
        copy.start()
    for copy in tok_copies(1):
        copy.start()
    for flip in (3, 2, 1, 0):
        loads(4 + flip).start()
    for copy in tails:
        copy.start()
    greet_all([mate] + [2 * other + core for other in others], grp_devices)
    for member in range(MB):
        for copy in near_copies(member):
            copy.start()
        for flip in (1, 2):
            for copy in far_copies(4 * member + flip):
                copy.start()
    for item in range(count):
        grp[0](item)
    for copy in masks:
        copy.wait()
    mask_rows(seg_buf, mask_buf, count_ref, bias)

    def compute(step):
        member, flip = slot_of(step)
        slot = 4 * member + flip

        @pl.when(lax.rem(step, 4) == 0)
        def _():
            for copy in tok_copies(member):
                copy.wait()
            dk[...] = jnp.zeros_like(dk)
            dv[...] = jnp.zeros_like(dv)

        start = pl.multiple_of(chip_at(chip, flip) * span, span)
        pltpu.make_async_copy(q_ref.at[member, pl.ds(start, span)], queries.at[slot], q_sem.at[slot]).wait()

        @pl.when(flip == 0)
        def _():
            for copy in own_copies(member):
                copy.wait()
            for copy in near_copies(member):
                copy.wait_recv()

        @pl.when(flip > 0)
        def _():
            for copy in on_copies(slot):
                copy.wait_recv()

        asked = queries[slot]
        upstream = ups[slot].reshape(span, D)
        scores = nt(asked, keys[member])
        soft = nt(upstream, values[member])
        weights, grads = [], []
        for half in range(2):
            seen = bias[member, pl.ds(2 * chip_at(chip, flip) + half, 1), :]
            figures = figs[slot, half].T
            rows = slice(half * ROWS, (half + 1) * ROWS)
            weight = jnp.exp2(scores[rows] + seen - figures[:, 0:1])
            grads.append((weight * (soft[rows] - figures[:, 1:2])).astype(BF16))
            weights.append(weight.astype(BF16))
        weight = jnp.concatenate(weights, axis=0)
        grad = jnp.concatenate(grads, axis=0)
        dv[...] += tn(weight, upstream)
        dk[...] += tn(grad, asked)
        asked_grad = (nn(grad, keys[member]) * D ** (-0.5)).astype(BF16)
        for half in range(2):
            part[slot, half] = asked_grad[half * ROWS:(half + 1) * ROWS]
        core_copy(slot).start()

    def combine(step):
        member, flip = slot_of(step)
        slot = 4 * member + flip
        core_copy(slot).wait_recv()
        added = part[slot, core].astype(F32) + got[slot].astype(F32)

        @pl.when(flip > 0)
        def _():
            stage[slot] = added.astype(BF16)

        @pl.when(flip == 0)
        def _():
            total[member] = added

    def tokens_back(member):
        gain = tgain_ref[...]
        hat, inverse = norm_parts(tok_buf[member].astype(F32))
        normed = (hat * gain).astype(BF16)
        key_grad = (dk[...] * LN2).astype(BF16)
        value_grad = dv[...].astype(BF16)
        key_term = tn(normed, key_grad)
        value_term = tn(normed, value_grad)
        normed_grad = nt(key_grad, kw_ref[...]) + nt(value_grad, vw_ref[...])
        source_grad, gain_rows = norm_pull(hat, inverse, gain, normed_grad)
        dtok[member] = source_grad
        out_copy(member).start()
        gain_term = jnp.sum(gain_rows, axis=0, keepdims=True)

        @pl.when(member == 0)
        def _():
            dkw[...] = key_term
            dvw[...] = value_term
            dgain_ref[...] = gain_term

        @pl.when(member > 0)
        def _():
            dkw_ref[...] = (dkw[...] + key_term).astype(BF16)
            dvw_ref[...] = (dvw[...] + value_term).astype(BF16)
            dgain_ref[...] += gain_term

    def step_body(step, carry):
        compute(step)

        @pl.when(step > 0)
        def _():
            combine(step - 1)

        @pl.when(step == 0)
        def _():
            pass_near(0)

        @pl.when(step == 1)
        def _():
            pass_on(3)

        @pl.when(step == 2)
        def _():
            pass_near(1)

        @pl.when(step == 3)
        def _():
            pass_on(7)

        @pl.when(step == 4)
        def _():
            for copy in half_copies(0):
                copy.start()
            for item in range(count):
                grp[1](item)

        @pl.when(step == 5)
        def _():
            for copy in half_copies(1):
                copy.start()
            relay(0)

        @pl.when(step == 6)
        def _():
            for item in range(count):
                grp[2](item)

        @pl.when(step == 4 * MB - 1)
        def _():
            relay(1)
            combine(step)

        @pl.when(lax.rem(step, 4) == 3)
        def _():
            tokens_back(lax.div(step, 4))

        return carry

    lax.fori_loop(0, 4 * MB, step_body, 0)
    for copy in tails:
        copy.wait()
    gain = qgain_ref[...]
    hat, inverse = norm_parts(lat[...].reshape(MB * ROWS, D))
    normed = (hat * gain).astype(BF16)
    asked_grads = []
    for member in range(MB):
        added = total[member]
        for flip in (1, 2):
            chip_copy(4 * member + flip).wait_recv()
            added = added + arrive[2 * member + flip - 1].astype(F32)
        asked_grads.append(added.astype(BF16))
    asked_grad = jnp.concatenate(asked_grads, axis=0)
    dqw_ref[...] = tn(normed, asked_grad).astype(BF16)
    source_grad, gain_rows = norm_pull(hat, inverse, gain, nt(asked_grad, qw_ref[...]))
    dlat[...] = (lup[...] + source_grad).reshape(MB, ROWS, D)
    last = pltpu.make_async_copy(dlat, dlat_ref.at[0], tail_sem.at[2])
    last.start()
    query_gain = jnp.sum(gain_rows, axis=0, keepdims=True)
    rows = jnp.concatenate(
        [dgain_ref[...], query_gain, fgain_ref[...], mgain_ref[...], sgain_ref[...], jnp.zeros((3, D), F32)], axis=0
    )
    gains_ref[...] = jnp.zeros_like(gains_ref)
    width = D // TOK
    for device in range(TOK):
        gains_ref[16 * device:16 * device + 8, 0:width] = rows[:, device * width:(device + 1) * width]
    for item in range(count):
        grp[3](item)
    grp[4]()
    last.wait()
    for member in range(MB):
        out_copy(member).wait()
        for copy in near_copies(member) + half_copies(member):
            copy.wait_send()
        for flip in range(4):
            slot = 4 * member + flip
            core_copy(slot).wait_send()
            if flip > 0:
                for copy in far_copies(slot):
                    copy.wait_send()
                for copy in on_copies(slot):
                    copy.wait_send()
            if flip in (1, 2):
                chip_copy(slot).wait_send()


CROSS_SCRATCH = 46


def cross_backward(collective_id, arrays, *args):
    dma = pltpu.SemaphoreType.DMA
    span = 2 * ROWS
    steps = 4 * MB
    vmem = pl.BlockSpec(memory_space=pltpu.VMEM)
    hbm = pl.BlockSpec(memory_space=pl.ANY)
    smem = pl.BlockSpec(memory_space=pltpu.SMEM)
    items = tuple((i, array.shape[0], 0, array.shape[1], 0, True) for i, array in enumerate(arrays))
    kinds = [array.dtype for array in arrays]
    scratch = [
        pltpu.VMEM((MB, TOK_DEV, D), BF16),
        pltpu.VMEM((MB, TOK_DEV, D), BF16),
        pltpu.VMEM((MB, TOK_DEV, D), BF16),
        pltpu.VMEM((steps, span, D), BF16),
        pltpu.VMEM((steps, 2, ROWS, D), BF16),
        pltpu.VMEM((steps, 2, 8, ROWS), F32),
        pltpu.VMEM((MB, LGROUPS, TOK_DEV), F32),
        pltpu.VMEM((steps, 2, ROWS, D), BF16),
        pltpu.VMEM((steps, ROWS, D), BF16),
        pltpu.VMEM((steps, ROWS, D), BF16),
        pltpu.VMEM((2 * MB, ROWS, D), BF16),
        pltpu.VMEM((MB, 2, ROWS // 2, D), BF16),
        pltpu.VMEM((MB, ROWS, D), F32),
        pltpu.VMEM((TOK_DEV, D), F32),
        pltpu.VMEM((TOK_DEV, D), F32),
        pltpu.VMEM((MB, TOK_DEV, D), F32),
        pltpu.VMEM((D, D), F32),
        pltpu.VMEM((D, D), F32),
        pltpu.VMEM((1, D), F32),
        pltpu.VMEM((MB, ROWS, D), F32),
        pltpu.VMEM((MB * ROWS, D), F32),
        pltpu.VMEM((MB, ROWS, D), F32),
        pltpu.VMEM((MB, TOK_DEV), jnp.int32),
        pltpu.VMEM((MB, SCENES, LGROUPS), jnp.int32),
        dma((2,)), dma((3,)),
        dma((MB,)), dma((MB,)), dma((MB,)), dma((steps,)), dma((MB,)),
        dma((MB, 2)), dma((MB, 2)), dma((steps, 2)), dma((steps, 2)), dma((steps, 2)), dma((steps, 2)), dma((MB, 2)),
        dma((MB,)), dma((MB,)),
        dma((steps,)), dma((steps,)), dma((2 * MB,)), dma((2 * MB,)), dma((MB, 2)), dma((MB, 2)),
    ]
    return pl.pallas_call(
        functools.partial(cross_backward_kernel, items),
        in_specs=[hbm] + [vmem] * 3 + [hbm, hbm, smem] + [hbm] * 7 + [vmem] * 5 + [vmem] * len(arrays),
        out_specs=[hbm, hbm] + [vmem] * (4 + len(arrays)),
        out_shape=[
            jax.ShapeDtypeStruct((1, MB, ROWS, D), F32),
            jax.ShapeDtypeStruct((1, MB, TOK_DEV, D), F32),
            jax.ShapeDtypeStruct((D, D), BF16),
            jax.ShapeDtypeStruct((D, D), BF16),
            jax.ShapeDtypeStruct((D, D), BF16),
            jax.ShapeDtypeStruct((16 * TOK, 128), F32),
        ] + [jax.ShapeDtypeStruct(array.shape, F32) for array in arrays],
        scratch_shapes=scratch + grp_scratch(items, kinds),
        compiler_params=pltpu.CompilerParams(
            collective_id=collective_id, has_side_effects=True, vmem_limit_bytes=60 * MIB
        ),
        cost_estimate=pl.CostEstimate(
            flops=26 * 10**9, bytes_accessed=24 * 10**6, transcendentals=4 * 10**6
        ),
        name="cross_backward",
    )(*args, *arrays)


GELU_A = 0.7978845608028654
GELU_B = 0.044715


def gelu_parts(hidden):
    square = hidden * hidden
    bent = jnp.tanh(GELU_A * hidden * (1.0 + GELU_B * square))
    half = 0.5 * (1.0 + bent)
    slope = half + 0.5 * hidden * (1.0 - bent * bent) * (GELU_A * (1.0 + 3.0 * GELU_B * square))
    return hidden * half, slope


def greet_all(tok_devices, grp_devices=()):
    barrier = pltpu.get_barrier_semaphore()
    for axis, devices in (("tok", tok_devices), ("grp", grp_devices)):
        for device in devices:
            pl.semaphore_signal(
                barrier, inc=1, device_id={axis: device}, device_id_type=pl.DeviceIdType.MESH
            )
    pl.semaphore_wait(barrier, len(tok_devices) + len(grp_devices))


def all_peers():
    me, core, chip, mate, others = places()
    peers = []
    for other in others:
        peers += [2 * other + core, 2 * other + 1 - core]
    return me, peers + [mate]


def head_copies(row_side, head_side, to_heads, member, me, peers, send, recv, local):
    lanes = pl.ds(member * ROWS, ROWS)
    row_at = lambda device: row_side.at[:, device, :, lanes]
    head_at = lambda device: head_side.at[:, member, :, pl.ds(pl.multiple_of(device * ROWS, ROWS), ROWS)]
    source, target = (row_at, head_at) if to_heads else (head_at, row_at)
    copies = [
        remote(source(peer), target(me), send.at[slot, member], recv.at[slot, member], peer)
        for slot, peer in enumerate(peers)
    ]
    return copies, pltpu.make_async_copy(source(me), target(me), local.at[member])


QB = 1024
QB_BACK = 256


def latents_forward_kernel(
    lat_ref, att_ref, cot_ref, ow_ref, fgain_ref, fup_ref, fdown_ref, mgain_ref, proj_ref, mow_ref, sgain_ref,
    sup_ref, sdown_ref,
    out_ref, fmid_ref, mmid_ref, packed_ref, exact_ref, lse_ref, up_ref, mgrad_ref, ddown_ref, dup_ref, dmo_ref,
    dgain_ref,
    lat, att, cot, ow, fup, fdown, proj, mow, sup, sdown,
    out, fmid, mmid, heads, exact, up, mgrad, ddown, dup, dmo,
    rows_out, keys, values, mixed, mixed_rows,
    load_sem, store_sem, send_a, recv_a, local_a, send_b, recv_b, local_b,
):
    me, peers = all_peers()
    own = pl.ds(pl.multiple_of(me * ROWS, ROWS), ROWS)
    names = ("lat", "att", "ow", "fup", "fdown", "proj", "mow", "sup", "sdown", "cot")
    loads = {}
    for i, (source, target) in enumerate((
        (lat_ref.at[0, :, own], lat), (att_ref, att), (ow_ref, ow), (fup_ref, fup), (fdown_ref, fdown),
        (proj_ref, proj), (mow_ref, mow), (sup_ref, sup), (sdown_ref, sdown), (cot_ref.at[0], cot),
    )):
        loads[names[i]] = pltpu.make_async_copy(source, target, load_sem.at[i])
        loads[names[i]].start()
    stores = []

    def store(source, target):
        stores.append(pltpu.make_async_copy(source, target, store_sem.at[len(stores)]))
        stores[-1].start()

    greet_all(peers)
    flat = (MB * ROWS, D)
    for name in ("lat", "att", "ow"):
        loads[name].wait()
    first = lat[...].reshape(flat) + nn(att[...].reshape(flat).astype(BF16), ow[...])
    fmid[...] = first
    store(fmid, fmid_ref)
    normed = (norm_parts(first)[0] * fgain_ref[...]).astype(BF16)
    loads["fup"].wait()
    loads["fdown"].wait()
    mid = first
    for part in range(2):
        cut = slice(part * FF // 2, (part + 1) * FF // 2)
        mid = mid + nn(jax.nn.gelu(nn(normed, fup[:, cut])).astype(BF16), fdown[cut])
    mmid[...] = mid
    store(mmid, mmid_ref)
    normed = (norm_parts(mid)[0] * mgain_ref[...]).astype(BF16).T
    loads["proj"].wait()
    for kind, scale in enumerate((HD ** (-0.5) * LOG2E, 1.0, 1.0)):
        packed = tn(proj[:, kind * D:(kind + 1) * D], normed) * scale
        rows_out[kind] = packed.astype(BF16).reshape(H, HD, MB * ROWS)
    outward = [head_copies(rows_out, heads, True, member, me, peers, send_a, recv_a, local_a) for member in range(MB)]
    backward = [
        head_copies(mixed_rows, mixed, False, member, me, peers, send_b, recv_b, local_b) for member in range(MB)
    ]
    for copies, here in outward:
        for copy in copies:
            copy.start()
        here.start()
    for member in range(MB):
        copies, here = outward[member]
        for copy in copies:
            copy.wait_recv()
        here.wait()
        store(heads.at[:, member], packed_ref.at[:, member])
        keys[...] = heads[1, member].T
        values[0:HD] = heads[2, member]
        values[HD:] = jnp.ones((16, L), BF16)

        def attend(step, carry, member=member):
            at = pl.ds(pl.multiple_of(step * QB, QB), QB)
            logits = nn(keys[...], heads[0, member, :, at])
            top = jnp.max(logits, axis=0, keepdims=True)
            both = nn(values[...], jnp.exp2(logits - top).astype(BF16))
            total = both[HD:HD + 1]
            result = both[0:HD] / total
            exact[member, :, at] = result
            mixed[0, member, :, at] = result.astype(BF16)
            lse_ref[member, :, at] = jnp.broadcast_to(top + jnp.log2(total), (8, QB))
            return carry

        lax.fori_loop(0, L // QB, attend, 0)
        for copy in backward[member][0] + [backward[member][1]]:
            copy.start()
    store(exact, exact_ref)
    loads["mow"].wait()
    loads["sup"].wait()
    loads["sdown"].wait()
    loads["cot"].wait()
    for copies, here in backward:
        for copy in copies:
            copy.wait_recv()
        here.wait()
    mixed_t = mixed_rows[0].reshape(D, MB * ROWS)
    second = mmid[...] + tn(mixed_t, mow[...])
    hat, inverse = norm_parts(second)
    normed = (hat * sgain_ref[...]).astype(BF16)
    upstream = cot[...].reshape(flat)
    grad = upstream.astype(BF16)
    final = second
    normed_grad = jnp.zeros(flat, F32)
    for part in range(2):
        cut = slice(part * FF // 2, (part + 1) * FF // 2)
        act, slope = gelu_parts(nn(normed, sup[:, cut]))
        act = act.astype(BF16)
        final = final + nn(act, sdown[cut])
        hidden_grad = (slope * nt(grad, sdown[cut])).astype(BF16)
        normed_grad = normed_grad + nt(hidden_grad, sup[:, cut])
        ddown[cut] = tn(act, grad).astype(BF16)
        dup[:, cut] = tn(normed, hidden_grad).astype(BF16)
    store(ddown, ddown_ref)
    store(dup, dup_ref)
    out[...] = final.reshape(MB, ROWS, D)
    store(out, out_ref.at[0])
    residual, gain_rows = norm_pull(hat, inverse, sgain_ref[...], normed_grad)
    dgain_ref[...] = jnp.sum(gain_rows, axis=0, keepdims=True)
    upstream = upstream + residual
    up[...] = upstream
    store(up, up_ref)
    grad = upstream.astype(BF16)
    mgrad[0] = nt(mow[...], grad).astype(BF16).reshape(H, HD, MB * ROWS)
    store(mgrad, mgrad_ref)
    dmo[...] = nn(mixed_t, grad).astype(BF16)
    store(dmo, dmo_ref)
    for copy in stores:
        copy.wait()
    for copies, here in outward + backward:
        for copy in copies:
            copy.wait_send()


def latents_forward(collective_id, *args):
    dma = pltpu.SemaphoreType.DMA
    vmem = pl.BlockSpec(memory_space=pltpu.VMEM)
    hbm = pl.BlockSpec(memory_space=pl.ANY)
    rows = MB * ROWS
    stored = [
        ((1, MB, ROWS, D), F32), ((rows, D), F32), ((rows, D), F32), ((3, MB, HD, L), BF16), ((MB, HD, L), F32),
        ((MB, 8, L), F32), ((rows, D), F32), ((1, H, HD, rows), BF16), ((FF, D), BF16), ((D, FF), BF16), ((D, D), BF16),
        ((1, D), F32),
    ]
    return pl.pallas_call(
        latents_forward_kernel,
        in_specs=[hbm, hbm, hbm, hbm, vmem, hbm, hbm, vmem, hbm, hbm, vmem, hbm, hbm],
        out_specs=[hbm] * 5 + [vmem] + [hbm] * 5 + [vmem],
        out_shape=[jax.ShapeDtypeStruct(shape, kind) for shape, kind in stored],
        scratch_shapes=[
            pltpu.VMEM((MB, ROWS, D), F32), pltpu.VMEM((MB, ROWS, D), F32), pltpu.VMEM((MB, ROWS, D), F32),
            pltpu.VMEM((D, D), BF16), pltpu.VMEM((D, FF), BF16), pltpu.VMEM((FF, D), BF16),
            pltpu.VMEM((D, 3 * D), BF16), pltpu.VMEM((D, D), BF16), pltpu.VMEM((D, FF), BF16),
            pltpu.VMEM((FF, D), BF16),
            pltpu.VMEM((MB, ROWS, D), F32), pltpu.VMEM((rows, D), F32), pltpu.VMEM((rows, D), F32),
            pltpu.VMEM((3, MB, HD, L), BF16), pltpu.VMEM((MB, HD, L), F32), pltpu.VMEM((rows, D), F32),
            pltpu.VMEM((1, H, HD, rows), BF16), pltpu.VMEM((FF, D), BF16), pltpu.VMEM((D, FF), BF16),
            pltpu.VMEM((D, D), BF16),
            pltpu.VMEM((3, H, HD, rows), BF16), pltpu.VMEM((L, HD), BF16), pltpu.VMEM((HD + 16, L), BF16),
            pltpu.VMEM((1, MB, HD, L), BF16), pltpu.VMEM((1, H, HD, rows), BF16),
            dma((10,)), dma((11,)), dma((7, MB)), dma((7, MB)), dma((MB,)), dma((7, MB)), dma((7, MB)), dma((MB,)),
        ],
        compiler_params=pltpu.CompilerParams(
            collective_id=collective_id, has_side_effects=True, vmem_limit_bytes=60 * MIB
        ),
        cost_estimate=pl.CostEstimate(
            flops=20 * 10**9, bytes_accessed=30 * 10**6, transcendentals=10 * 10**6
        ),
        name="latents_forward",
    )(*args)


def tok_steps(items, sources, scratch):
    n = len(items)
    mine, got, first_in, second_in = [scratch[i * n:(i + 1) * n] for i in range(4)]
    local_sem, core_send, core_recv, one_send, one_recv, two_send, two_recv = scratch[4 * n:4 * n + 7]
    me, core, chip, mate, (far, flip_x, flip_y) = places()
    x, y = lax.rem(chip, 2), lax.div(chip, 2)
    sent, cores, ones, twos = [], {}, {}, {}

    def core_sends(i):
        source, rows, row_at, columns, column_at, x_first = items[i]
        part = (pl.ds(row_at, rows), pl.ds(column_at, columns))
        there = remote(sources[source].at[:, :, 1 - core, *part], got[i], core_send.at[i], core_recv.at[i], mate)
        here = pltpu.make_async_copy(sources[source].at[:, :, core, *part], mine[i], local_sem.at[i])
        there.start()
        here.start()
        cores[i] = (there, here)
        sent.append(there)

    def core_sums(i):
        there, here = cores[i]
        there.wait_recv()
        here.wait()
        add(mine[i], mine[i], got[i])
        x_first = items[i][-1]
        away = mine[i].at[:, 1 - x] if x_first else mine[i].at[1 - y]
        peer = 2 * (flip_x if x_first else flip_y) + core
        ones[i] = remote(away, first_in[i], one_send.at[i], one_recv.at[i], peer)
        ones[i].start()
        sent.append(ones[i])

    def first_sums(i):
        x_first = items[i][-1]
        ones[i].wait_recv()
        keep = mine[i].at[:, x] if x_first else mine[i].at[y]
        add(keep, keep, first_in[i])
        away = mine[i].at[1 - y, x] if x_first else mine[i].at[y, 1 - x]
        peer = 2 * (flip_y if x_first else flip_x) + core
        twos[i] = remote(away, second_in[i], two_send.at[i], two_recv.at[i], peer)
        twos[i].start()
        sent.append(twos[i])

    def second_sums(i):
        twos[i].wait_recv()
        add(mine[i].at[y, x], mine[i].at[y, x], second_in[i])

    def finish():
        for copy in sent:
            copy.wait_send()

    results = [mine[i].at[y, x] for i in range(n)]
    return (core_sends, core_sums, first_sums, second_sums, finish), results, (mate, 2 * flip_x + core, 2 * flip_y + core)


def grp_steps(items, results, outs, scratch):
    n = len(items)
    z_keep, z_first, z_second = [scratch[i * n:(i + 1) * n] for i in range(3)]
    z_send, z_recv = scratch[3 * n:3 * n + 2]
    level = lax.axis_index("grp")
    odd = lax.rem(level, 2)
    level_near = level + 1 - 2 * odd
    level_far = lax.rem(level + 2, 4)
    def halves(i):
        half = items[i][1] // 2
        keep = pl.ds(pl.multiple_of(odd * half, half), half)
        away = pl.ds(pl.multiple_of((1 - odd) * half, half), half)
        return keep, away

    def along(i, step):
        source, target, other = (
            (results[i].at[halves(i)[1]], z_first[i], level_near),
            (z_keep[i].at[0], z_second[i].at[0], level_far),
            (z_keep[i].at[1], z_second[i].at[1], level_near),
        )[step]
        return pltpu.make_async_remote_copy(
            src_ref=source, dst_ref=target, send_sem=z_send.at[i, step], recv_sem=z_recv.at[i, step],
            device_id={"grp": other}, device_id_type=pl.DeviceIdType.MESH,
        )

    def store(i, odd_half, value):
        source, rows, row_at, columns, column_at, x_first = items[i]
        half = rows // 2
        start = pl.multiple_of(row_at + odd_half * half, half)
        outs[source][pl.ds(start, half), pl.ds(column_at, columns)] = value.astype(F32)

    def grp_start(i):
        along(i, 0).start()

    def grp_first(i):
        along(i, 0).wait_recv()
        add(z_keep[i].at[0], results[i].at[halves(i)[0]], z_first[i])
        along(i, 1).start()

    def grp_second(i):
        along(i, 1).wait_recv()
        add(z_keep[i].at[1], z_keep[i].at[0], z_second[i].at[0])
        along(i, 2).start()
        store(i, odd, z_keep[i][1])

    def grp_third(i):
        along(i, 2).wait_recv()
        store(i, 1 - odd, z_second[i][1])

    def finish():
        for i in range(n):
            for step in range(3):
                along(i, step).wait_send()

    return (grp_start, grp_first, grp_second, grp_third, finish), (level_near, level_far)


def add(target, one, two):
    target[...] = (one[...].astype(F32) + two[...].astype(F32)).astype(target.dtype)


def reduce_kernel(items, count, *refs):
    n = len(items)
    scratch = refs[2 * count:]
    tok, results, near_devices = tok_steps(items, refs[:count], scratch[:4 * n + 7])
    grp, grp_devices = grp_steps(items, results, refs[count:2 * count], scratch[4 * n + 7:])
    greet_all(near_devices, grp_devices)

    def last_sums(i):
        tok[3](i)
        grp[0](i)

    stages = tok[:3] + (last_sums,) + grp[1:4]
    lags = (0, 1, 4, 6, 8, 10, 12)
    for step in range(n + lags[-1]):
        for stage, lag in zip(stages, lags):
            if 0 <= step - lag < n:
                stage(step - lag)
    tok[-1]()
    grp[-1]()


def reduce_plan(arrays, cuts):
    sources, items = [], []
    for source, (array, cut) in enumerate(zip(arrays, cuts)):
        rows, columns = array.shape[0] // TOK, array.shape[1]
        sources.append(array.reshape(2, 2, 2, rows, columns))
        parts = abs(cut)
        for part in range(parts):
            high, wide = (rows, columns // parts) if cut > 0 else (rows // parts, columns)
            row_at, column_at = (0, part * wide) if cut > 0 else (part * high, 0)
            items.append((source, high, row_at, wide, column_at, len(items) % 2 == 0))
    items = tuple(items)
    kinds = [arrays[item[0]].dtype for item in items]
    shapes = [(array.shape[0] // TOK, array.shape[1]) for array in arrays]
    return sources, items, kinds, shapes


def item_blocks(items, kinds, lead, part):
    return [pltpu.VMEM(lead + (item[1] // part, item[3]), kind) for item, kind in zip(items, kinds)]


def tok_scratch(items, kinds):
    blocks = functools.partial(item_blocks, items, kinds)
    dma = pltpu.SemaphoreType.DMA
    return blocks((2, 2), 1) + blocks((2, 2), 1) + blocks((2,), 1) + blocks((), 1) + [dma((len(items),))] * 7


def grp_scratch(items, kinds):
    blocks = functools.partial(item_blocks, items, kinds)
    dma = pltpu.SemaphoreType.DMA
    return blocks((2,), 2) + blocks((), 2) + blocks((2,), 2) + [dma((len(items), 3))] * 2


def reduce_grads(collective_id, arrays, cuts):
    sources, items, kinds, shapes = reduce_plan(arrays, cuts)
    return pl.pallas_call(
        functools.partial(reduce_kernel, items, len(arrays)),
        in_specs=[pl.BlockSpec(memory_space=pl.ANY)] * len(arrays),
        out_specs=[pl.BlockSpec(memory_space=pltpu.VMEM)] * len(arrays),
        out_shape=[jax.ShapeDtypeStruct(shape, F32) for shape in shapes],
        scratch_shapes=tok_scratch(items, kinds) + grp_scratch(items, kinds),
        compiler_params=pltpu.CompilerParams(
            collective_id=collective_id, has_side_effects=True, vmem_limit_bytes=56 * MIB
        ),
        name="reduce_grads",
    )(*sources)


def write_kernel(count, *refs):
    sources, gain_ref, outs, gain_outs, sem = (
        refs[:count], refs[count], refs[count + 1:2 * count + 1], refs[2 * count + 1:-1], refs[-1])
    copies = [pltpu.make_async_copy(sources[i], outs[i], sem.at[i]) for i in range(count)]
    for copy in copies:
        copy.start()
    for i, out in enumerate(gain_outs):
        out[...] = gain_ref[i:i + 1, 0:D // TOK]
    for copy in copies:
        copy.wait()


def write_results(results, gains, gain_count):
    n = len(results)
    hbm, vmem = pl.BlockSpec(memory_space=pl.ANY), pl.BlockSpec(memory_space=pltpu.VMEM)
    return pl.pallas_call(
        functools.partial(write_kernel, n),
        in_specs=[hbm] * n + [vmem],
        out_specs=[hbm] * n + [vmem] * gain_count,
        out_shape=[jax.ShapeDtypeStruct(result.shape, result.dtype) for result in results]
        + [jax.ShapeDtypeStruct((1, D // TOK), F32)] * gain_count,
        scratch_shapes=[pltpu.SemaphoreType.DMA((n,))],
        name="write_results",
    )(*results, gains)


def latents_backward_kernel(items, *refs):
    (mgrad_ref, packed_ref, exact_ref, lse_ref, up_ref, mmid_ref, fmid_ref, att_ref, clse_ref, ow_ref, fgain_ref,
     fup_ref, fdown_ref, mgain_ref, proj_ref) = refs[:15]
    count = max(item[0] for item in items) + 1
    sources = refs[15:15 + count]
    (agrad_ref, fig_ref, lup_ref, dup_ref, ddown_ref, dproj_ref, dout_ref, dmgain_ref, dfgain_ref) = refs[
        15 + count:24 + count]
    reduced = refs[24 + count:24 + 2 * count]
    rest = refs[24 + 2 * count:]
    (heads, exact, ups, mmid, fmid, att, ow, fup, fdown, proj, keys, values, upstream_heads, key_acc, value_acc,
     grads, back, agrad, lup, dup, ddown, dproj, dout, hidden,
     load_sem, store_sem, send_a, recv_a, local_a, send_b, recv_b, local_b) = rest[:32]
    me, peers = all_peers()
    reducer, results, near_devices = tok_steps(items, sources, rest[32:])
    core_sends, core_sums, first_sums, second_sums, finish = reducer

    def reduce_all(stage):
        for item in range(len(items)):
            stage(item)

    names = ("heads", "exact", "fmid", "fup", "up", "mmid", "proj", "fdown", "att", "ow")
    loads = {}
    for i, (source, target) in enumerate((
        (packed_ref, heads), (exact_ref, exact), (fmid_ref, fmid), (fup_ref, fup), (up_ref, ups), (mmid_ref, mmid),
        (proj_ref, proj), (fdown_ref, fdown), (att_ref, att), (ow_ref, ow),
    )):
        loads[names[i]] = pltpu.make_async_copy(source, target, load_sem.at[i])
        loads[names[i]].start()
    stores = []

    def store(source, target):
        stores.append(pltpu.make_async_copy(source, target, store_sem.at[len(stores)]))
        stores[-1].start()

    greet_all(peers)
    outward = [
        head_copies(mgrad_ref, upstream_heads, True, member, me, peers, send_a, recv_a, local_a) for member in range(MB)
    ]
    backward = [head_copies(back, grads, False, member, me, peers, send_b, recv_b, local_b) for member in range(MB)]
    for copies, here in outward:
        for copy in copies:
            copy.start()
        here.start()
    reduce_all(core_sends)
    loads["fmid"].wait()
    loads["fup"].wait()
    first_hat, first_inverse = norm_parts(fmid[...])
    first_normed = (first_hat * fgain_ref[...]).astype(BF16)
    hidden[...] = nn(first_normed, fup[...])
    reduce_all(core_sums)
    loads["heads"].wait()
    loads["exact"].wait()
    for member in range(MB):
        keys[...] = heads[1, member].T
        values[...] = heads[2, member].T
        key_acc[...] = jnp.zeros_like(key_acc)
        value_acc[...] = jnp.zeros_like(value_acc)
        copies, here = outward[member]
        for copy in copies:
            copy.wait_recv()
        here.wait()

        def attend_back(step, carry, member=member):
            at = pl.ds(pl.multiple_of(step * QB_BACK, QB_BACK), QB_BACK)
            queries = heads[0, member, :, at]
            upstream = upstream_heads[0, member, :, at]
            inner = jnp.sum(upstream.astype(F32) * exact[member, :, at], axis=0, keepdims=True)
            softened = jnp.exp2(nn(keys[...], queries) - lse_ref[member, 0:1, at])
            logit_grad = (softened * (nn(values[...], upstream) - inner)).astype(BF16)
            value_acc[...] += nt(upstream, softened.astype(BF16))
            key_acc[...] += nt(queries, logit_grad)
            grads[0, member, :, at] = (nn(heads[1, member], logit_grad) * HD ** (-0.5)).astype(BF16)
            return carry

        steps = L // QB_BACK
        lax.fori_loop(0, steps, attend_back, 0)
        grads[1, member] = (key_acc[...] * LN2).astype(BF16)
        grads[2, member] = value_acc[...].astype(BF16)
        for copy in backward[member][0] + [backward[member][1]]:
            copy.start()
        if member == 0:
            reduce_all(first_sums)
    loads["up"].wait()
    loads["mmid"].wait()
    loads["proj"].wait()
    loads["fdown"].wait()
    mixer_hat, mixer_inverse = norm_parts(mmid[...])
    mixer_normed = (mixer_hat * mgain_ref[...]).astype(BF16).T
    for copies, here in backward:
        for copy in copies:
            copy.wait_recv()
        here.wait()
    packed_grad = back[...].reshape(3 * D, MB * ROWS)
    normed_grad = nn(proj[...], packed_grad).T
    residual, gain_rows = norm_pull(mixer_hat, mixer_inverse, mgain_ref[...], normed_grad)
    dmgain_ref[...] = jnp.sum(gain_rows, axis=0, keepdims=True)
    upstream = ups[...] + residual
    dproj[...] = nt(mixer_normed, packed_grad).astype(BF16)
    store(dproj, dproj_ref)
    grad = upstream.astype(BF16)
    normed_grad = jnp.zeros((MB * ROWS, D), F32)
    for part in range(2):
        cut = slice(part * FF // 2, (part + 1) * FF // 2)
        act, slope = gelu_parts(hidden[:, cut])
        hidden_grad = (slope * nt(grad, fdown[cut])).astype(BF16)
        normed_grad = normed_grad + nt(hidden_grad, fup[:, cut])
        ddown[cut] = tn(act.astype(BF16), grad).astype(BF16)
        dup[:, cut] = tn(first_normed, hidden_grad).astype(BF16)
    store(ddown, ddown_ref)
    store(dup, dup_ref)
    residual, gain_rows = norm_pull(first_hat, first_inverse, fgain_ref[...], normed_grad)
    dfgain_ref[...] = jnp.sum(gain_rows, axis=0, keepdims=True)
    upstream = upstream + residual
    lup[...] = upstream
    store(lup, lup_ref)
    grad = upstream.astype(BF16)
    loads["att"].wait()
    loads["ow"].wait()
    attended = att[...].reshape(MB * ROWS, D)
    attended_grad = nt(grad, ow[...]).astype(BF16)
    agrad[...] = attended_grad.reshape(MB, ROWS, D)
    store(agrad, agrad_ref)
    inner = jnp.sum(attended_grad.astype(F32) * attended, axis=1, keepdims=True)
    for member in range(MB):
        rows = slice(member * ROWS, (member + 1) * ROWS)
        spare = jnp.zeros((6, ROWS), F32)
        fig_ref[member] = jnp.concatenate(
            [clse_ref[member, 0:1], to_rows(inner[rows], inner[rows])[0:1], spare], axis=0
        )
    dout[...] = tn(attended.astype(BF16), grad).astype(BF16)
    store(dout, dout_ref)
    for item in range(len(items)):
        second_sums(item)
        reduced[items[item][0]][...] = results[item][...]
    finish()
    for copy in stores:
        copy.wait()
    for copies, here in outward + backward:
        for copy in copies:
            copy.wait_send()


def latents_backward(collective_id, arrays, *args):
    dma = pltpu.SemaphoreType.DMA
    vmem = pl.BlockSpec(memory_space=pltpu.VMEM)
    hbm = pl.BlockSpec(memory_space=pl.ANY)
    rows = MB * ROWS
    sources, items, kinds, shapes = reduce_plan(arrays, (1,) * len(arrays))
    reduced = [jax.ShapeDtypeStruct(shape, kind) for shape, kind in zip(shapes, kinds)]
    stored = [
        ((MB, ROWS, D), BF16), ((MB, 8, ROWS), F32), ((rows, D), F32), ((D, FF), BF16), ((FF, D), BF16),
        ((D, 3 * D), BF16), ((D, D), BF16), ((1, D), F32), ((1, D), F32),
    ]
    return pl.pallas_call(
        functools.partial(latents_backward_kernel, items),
        in_specs=[hbm, hbm, hbm, vmem, hbm, hbm, hbm, hbm, vmem, hbm, vmem, hbm, hbm, vmem, hbm] + [hbm] * len(arrays),
        out_specs=[hbm, vmem] + [hbm] * 5 + [vmem] * (2 + len(arrays)),
        out_shape=[jax.ShapeDtypeStruct(shape, kind) for shape, kind in stored] + reduced,
        scratch_shapes=[
            pltpu.VMEM((3, MB, HD, L), BF16), pltpu.VMEM((MB, HD, L), F32), pltpu.VMEM((rows, D), F32),
            pltpu.VMEM((rows, D), F32), pltpu.VMEM((rows, D), F32), pltpu.VMEM((MB, ROWS, D), F32),
            pltpu.VMEM((D, D), BF16), pltpu.VMEM((D, FF), BF16), pltpu.VMEM((FF, D), BF16),
            pltpu.VMEM((D, 3 * D), BF16), pltpu.VMEM((L, HD), BF16), pltpu.VMEM((L, HD), BF16),
            pltpu.VMEM((1, MB, HD, L), BF16), pltpu.VMEM((HD, L), F32), pltpu.VMEM((HD, L), F32),
            pltpu.VMEM((3, MB, HD, L), BF16), pltpu.VMEM((3, H, HD, rows), BF16),
            pltpu.VMEM((MB, ROWS, D), BF16), pltpu.VMEM((rows, D), F32), pltpu.VMEM((D, FF), BF16),
            pltpu.VMEM((FF, D), BF16), pltpu.VMEM((D, 3 * D), BF16), pltpu.VMEM((D, D), BF16),
            pltpu.VMEM((rows, FF), F32),
            dma((10,)), dma((6,)), dma((7, MB)), dma((7, MB)), dma((MB,)), dma((7, MB)), dma((7, MB)), dma((MB,)),
        ] + tok_scratch(items, kinds),
        compiler_params=pltpu.CompilerParams(
            collective_id=collective_id, has_side_effects=True, vmem_limit_bytes=61 * MIB
        ),
        cost_estimate=pl.CostEstimate(
            flops=35 * 10**9, bytes_accessed=36 * 10**6, transcendentals=10 * 10**6
        ),
        name="latents_backward",
    )(*args, *sources)


def fast_body(
    tokens,
    latents,
    segments,
    scene_mask,
    counts,
    token_gain,
    query_gain,
    query_weight,
    key_weight,
    value_weight,
    output_weight,
    first_gain,
    first_up,
    first_down,
    mixer_gain,
    mixer_project,
    mixer_output,
    second_gain,
    second_up,
    second_down,
    cotangent,
):
    scenes = (segments, scene_mask, counts)
    keys, values, queries, attended, lse = cross_forward(
        0, tokens, latents, token_gain[None], query_gain[None], query_weight, key_weight, value_weight, *scenes
    )
    (latents_out, first_mid, mixer_mid, packed, exact, head_lse, upstream, mixed_grad, d_second_down, d_second_up,
     d_mixer_output, d_second_gain) = latents_forward(
        1, latents, attended, cotangent, output_weight, first_gain[None], first_up, first_down, mixer_gain[None],
        mixer_project, mixer_output, second_gain[None], second_up, second_down,
    )
    (attended_grad, figures, upstream, d_first_up, d_first_down, d_project, d_output, d_mixer_gain, d_first_gain,
     *early) = latents_backward(
        2, [d_second_up, d_second_down, d_mixer_output], mixed_grad, packed, exact, head_lse, upstream, mixer_mid,
        first_mid, attended, lse, output_weight, first_gain[None], first_up, first_down, mixer_gain[None], mixer_project,
    )
    latents_grad, tokens_grad, d_key, d_value, d_query, gains, *early = cross_backward(
        5, early, tokens, token_gain[None], key_weight, value_weight, *scenes, keys, values, queries,
        attended_grad, figures, latents, upstream, query_gain[None], query_weight, d_first_gain, d_mixer_gain,
        d_second_gain,
    )
    *late, gains = reduce_grads(
        7,
        [d_first_up, d_first_down, d_project, d_output, d_key, d_value, d_query, gains],
        (4, -4, 3, 1, 1, 1, 1, 1),
    )
    (latents_out, latents_grad, tokens_grad, o_second_up, o_second_down, o_mixer_output, o_first_up, o_first_down,
     o_project, o_output, o_key, o_value, o_query, *o_gains) = write_results(
        [latents_out, latents_grad, tokens_grad, *early, *late], gains, 5
    )
    o_gains = [gain.reshape(D // TOK) for gain in o_gains]
    return (
        latents_out,
        latents_grad,
        tokens_grad,
        o_gains[0],
        o_gains[1],
        o_query,
        o_key,
        o_value,
        o_output,
        o_gains[2],
        o_first_up,
        o_first_down,
        o_gains[3],
        o_project,
        o_mixer_output,
        o_gains[4],
        o_second_up,
        o_second_down,
    )


IN_SPECS = (
    P("grp", None, "tok", None),
    P("grp", None, None, None),
    P("grp", None, "tok"),
    P("grp", None, None, None),
    P("grp", None, "tok"),
    P(),
    P(),
    P(),
    P(),
    P(),
    P(),
    P(),
    P(),
    P(),
    P(),
    P(),
    P(),
    P(),
    P(),
    P(),
    P("grp", None, "tok", None),
)
OUT_SPECS = (
    P("grp", None, "tok", None),
    P("grp", None, "tok", None),
    P("grp", None, "tok", None),
    P("tok"),
    P("tok"),
    P("tok", None),
    P("tok", None),
    P("tok", None),
    P("tok", None),
    P("tok"),
    P("tok", None),
    P("tok", None),
    P("tok"),
    P("tok", None),
    P("tok", None),
    P("tok"),
    P("tok", None),
    P("tok", None),
)


def solution(mesh):
    return jax.shard_map(
        fast_body if mesh.shape["tok"] == TOK else general_body,
        mesh=mesh,
        in_specs=IN_SPECS,
        out_specs=OUT_SPECS,
        check_vma=False,
    )
```

```python
import functools

import jax
import jax.numpy as jnp
from jax import lax
from jax.experimental import pallas as pl
from jax.experimental.pallas import tpu as pltpu
from jax.sharding import PartitionSpec as P

D = 512
L = 2048
H = 8
HD = 64
TOK_DEV = 1024
MB = 2
SCENES = 8
LGROUPS = 8


EPS = 1e-05
NEG = -1e30


def norm_rows(values, gain):
    centre = values - jnp.mean(values, axis=-1, keepdims=True)
    spread = jnp.mean(centre * centre, axis=-1, keepdims=True)
    return centre * lax.rsqrt(spread + EPS) * gain


def norm_back(values, gain, upstream):
    unused, pull = jax.vjp(norm_rows, values, gain)
    return pull(upstream)


def gelu_back(hidden, upstream):
    unused, pull = jax.vjp(jax.nn.gelu, hidden)
    return pull(upstream)[0]


def product_plain(left, right):
    return jnp.dot(left, right, preferred_element_type=jnp.float32)


def product_rows(left, right):
    return lax.dot_general(
        left, right, (((0,), (0,)), ((), ())), preferred_element_type=jnp.float32
    )


def product_cols(left, right):
    return lax.dot_general(
        left, right, (((1,), (1,)), ((), ())), preferred_element_type=jnp.float32
    )


def add_term(store, name, value):
    if name in store:
        store[name] = store[name] + value
    else:
        store[name] = value


def project_tokens(tokens, member, token_gain, key_weight, value_weight):
    source = tokens[0, member].astype(jnp.float32)
    normed = norm_rows(source, token_gain).astype(jnp.bfloat16)
    key_rows = product_plain(normed, key_weight).astype(jnp.bfloat16)
    value_rows = product_plain(normed, value_weight).astype(jnp.bfloat16)
    return (source, normed, key_rows, value_rows)


def mlp_forward(residual, gain, up_weight, down_weight):
    normed = norm_rows(residual, gain).astype(jnp.bfloat16)
    hidden = product_plain(normed, up_weight)
    active = jax.nn.gelu(hidden).astype(jnp.bfloat16)
    return (residual + product_plain(active, down_weight), (normed, hidden, active))


def mlp_backward(residual, gain, up_weight, down_weight, saved, upstream):
    normed, hidden, active = saved
    grad_low = upstream.astype(jnp.bfloat16)
    grad_down = product_rows(active, grad_low)
    hidden_grad = gelu_back(hidden, product_cols(grad_low, down_weight)).astype(jnp.bfloat16)
    grad_up = product_rows(normed, hidden_grad)
    residual_grad, grad_gain = norm_back(residual, gain, product_cols(hidden_grad, up_weight))
    return (upstream + residual_grad, grad_gain, grad_up, grad_down)


def mixer_forward(residual, gain, project, output):
    own_rows = residual.shape[0]
    normed = norm_rows(residual, gain).astype(jnp.bfloat16)
    packed = product_plain(normed, project).astype(jnp.bfloat16)
    pair_rows = lax.all_gather(packed[:, D:], "tok", axis=0, tiled=True)
    every = pair_rows.shape[0]
    own_queries = packed[:, :D].reshape(own_rows, H, HD)
    keys = pair_rows[:, :D].reshape(every, H, HD)
    values = pair_rows[:, D:].reshape(every, H, HD)
    logits = jnp.einsum(
        "qhd,khd->hqk", own_queries, keys, preferred_element_type=jnp.float32
    ) * HD ** (-0.5)
    peak_row = jnp.max(logits, axis=-1, keepdims=True)
    raised = jnp.exp(logits - peak_row)
    softened = raised / jnp.sum(raised, axis=-1, keepdims=True)
    softened_low = softened.astype(jnp.bfloat16)
    mixed_rows = jnp.einsum(
        "hqk,khd->qhd", softened_low, values, preferred_element_type=jnp.float32
    )
    mixed_rows = mixed_rows.reshape(own_rows, D).astype(jnp.bfloat16)
    return (
        residual + product_plain(mixed_rows, output),
        (normed, own_queries, keys, values, softened, softened_low, mixed_rows),
    )


def mixer_backward(residual, gain, project, output, saved, upstream):
    normed, own_queries, keys, values, softened, softened_low, mixed_rows = saved
    own_rows = upstream.shape[0]
    every = keys.shape[0]
    grad_low = upstream.astype(jnp.bfloat16)
    grad_output = product_rows(mixed_rows, grad_low)
    mixed_grad = product_cols(grad_low, output).astype(jnp.bfloat16).reshape(own_rows, H, HD)
    value_grad = jnp.einsum(
        "hqk,qhd->khd", softened_low, mixed_grad, preferred_element_type=jnp.float32
    )
    soft_grad = jnp.einsum("qhd,khd->hqk", mixed_grad, values, preferred_element_type=jnp.float32)
    logit_grad = softened * (soft_grad - jnp.sum(soft_grad * softened, axis=-1, keepdims=True))
    logit_grad = logit_grad.astype(jnp.bfloat16)
    query_grad = jnp.einsum(
        "hqk,khd->qhd", logit_grad, keys, preferred_element_type=jnp.float32
    ) * HD ** (-0.5)
    key_grad = jnp.einsum(
        "hqk,qhd->khd", logit_grad, own_queries, preferred_element_type=jnp.float32
    ) * HD ** (-0.5)
    pair_terms = jnp.concatenate([key_grad.reshape(every, D), value_grad.reshape(every, D)], axis=1)
    pair_grad = lax.psum_scatter(
        pair_terms.astype(jnp.bfloat16), "tok", scatter_dimension=0, tiled=True
    ).astype(jnp.float32)
    packed_grad = jnp.concatenate([query_grad.reshape(own_rows, D), pair_grad], axis=1).astype(
        jnp.bfloat16
    )
    grad_project = product_rows(normed, packed_grad)
    residual_grad, grad_gain = norm_back(residual, gain, product_cols(packed_grad, project))
    return (upstream + residual_grad, grad_gain, grad_project, grad_output)


def general_body(
    tokens,
    latents,
    segments,
    scene_mask,
    counts,
    token_gain,
    query_gain,
    query_weight,
    key_weight,
    value_weight,
    output_weight,
    first_gain,
    first_up,
    first_down,
    mixer_gain,
    mixer_project,
    mixer_output,
    second_gain,
    second_up,
    second_down,
    cotangent,
):
    scale = D ** (-0.5)
    shards = lax.axis_size("tok")
    own_rows = L // shards
    row_start = lax.axis_index("tok") * own_rows
    latent_group = jnp.arange(L) // (L // LGROUPS)
    latent_onehot = (latent_group[:, None] == jnp.arange(LGROUPS)[None, :]).astype(jnp.float32)
    token_place = jnp.arange(TOK_DEV)
    records = []
    latent_outs = []
    for member in range(MB):
        record = {}
        source, normed, key_rows, value_rows = project_tokens(
            tokens, member, token_gain, key_weight, value_weight
        )
        record["token_side"] = (source, normed, key_rows, value_rows)
        scene_onehot = (segments[0, member][:, None] == jnp.arange(SCENES)[None, :]).astype(
            jnp.float32
        )
        token_seen = jnp.dot(scene_onehot, scene_mask[0, member].astype(jnp.float32))
        visible = product_cols(latent_onehot, token_seen)
        alive = token_place < counts[0, member, 0]
        allowed = (visible > 0.5) & alive[None, :]
        latent_every = latents[0, member]
        normed_every = norm_rows(latent_every, query_gain).astype(jnp.bfloat16)
        queries = product_plain(normed_every, query_weight).astype(jnp.bfloat16)
        scores = jnp.where(allowed, product_cols(queries, key_rows) * scale, NEG)
        row_top = lax.pmax(jnp.max(scores, axis=1), "tok")
        unnormed = jnp.exp(scores - row_top[:, None])
        row_total, weighted = (
            lax.psum_scatter(
                jnp.sum(unnormed, axis=1).astype(jnp.bfloat16),
                "tok",
                scatter_dimension=0,
                tiled=True,
            ).astype(jnp.float32),
            lax.psum_scatter(
                product_plain(unnormed.astype(jnp.bfloat16), value_rows).astype(jnp.bfloat16),
                "tok",
                scatter_dimension=0,
                tiled=True,
            ).astype(jnp.float32),
        )
        latent_in = lax.dynamic_slice_in_dim(latent_every, row_start, own_rows, 0)
        latent_normed = lax.dynamic_slice_in_dim(normed_every, row_start, own_rows, 0)
        attended = weighted / row_total[:, None]
        attended_low = attended.astype(jnp.bfloat16)
        first_mid = latent_in + product_plain(attended_low, output_weight)
        mixer_mid, first_saved = mlp_forward(first_mid, first_gain, first_up, first_down)
        second_mid, mixer_saved = mixer_forward(mixer_mid, mixer_gain, mixer_project, mixer_output)
        final_rows, second_saved = mlp_forward(second_mid, second_gain, second_up, second_down)
        latent_outs.append(final_rows)
        record["latent_side"] = (
            allowed,
            latent_in,
            latent_normed,
            queries,
            row_top,
            row_total,
            attended,
            attended_low,
            first_mid,
            mixer_mid,
            second_mid,
            first_saved,
            mixer_saved,
            second_saved,
        )
        records.append(record)
    grads = {}
    latent_grads = []
    token_grads = []
    for member in range(MB):
        record = records[member]
        source, normed, key_rows, value_rows = record["token_side"]
        (
            allowed,
            latent_in,
            latent_normed,
            queries,
            row_top,
            row_total,
            attended,
            attended_low,
            first_mid,
            mixer_mid,
            second_mid,
            first_saved,
            mixer_saved,
            second_saved,
        ) = record["latent_side"]
        second_back = mlp_backward(
            second_mid, second_gain, second_up, second_down, second_saved, cotangent[0, member]
        )
        add_term(grads, "second_gain", second_back[1])
        add_term(grads, "second_up", second_back[2])
        add_term(grads, "second_down", second_back[3])
        mixer_back = mixer_backward(
            mixer_mid, mixer_gain, mixer_project, mixer_output, mixer_saved, second_back[0]
        )
        add_term(grads, "mixer_gain", mixer_back[1])
        add_term(grads, "mixer_project", mixer_back[2])
        add_term(grads, "mixer_output", mixer_back[3])
        first_back = mlp_backward(
            first_mid, first_gain, first_up, first_down, first_saved, mixer_back[0]
        )
        add_term(grads, "first_gain", first_back[1])
        add_term(grads, "first_up", first_back[2])
        add_term(grads, "first_down", first_back[3])
        latent_upstream = first_back[0]
        grad_low = latent_upstream.astype(jnp.bfloat16)
        add_term(grads, "output_weight", product_rows(attended_low, grad_low))
        attended_grad = lax.optimization_barrier(
            product_cols(grad_low, output_weight).astype(jnp.bfloat16)
        ).astype(jnp.float32)
        weighted_grad = (attended_grad / row_total[:, None]).astype(jnp.bfloat16)
        total_grad = -jnp.sum(attended_grad * attended, axis=1) / row_total
        weighted_every, total_every = (
            lax.all_gather(
                weighted_grad.astype(jnp.float32).astype(jnp.bfloat16), "tok", axis=0, tiled=True
            ).astype(jnp.float32),
            lax.all_gather(total_grad.astype(jnp.bfloat16), "tok", axis=0, tiled=True).astype(
                total_grad.dtype
            ),
        )
        weighted_every = weighted_every.astype(jnp.bfloat16)
        scores = jnp.where(allowed, product_cols(queries, key_rows) * scale, NEG)
        unnormed = jnp.exp(scores - row_top[:, None])
        unnormed_grad = product_cols(weighted_every, value_rows) + total_every[:, None]
        score_grad = (unnormed * unnormed_grad).astype(jnp.bfloat16)
        value_grad = product_rows(unnormed.astype(jnp.bfloat16), weighted_every).astype(
            jnp.bfloat16
        )
        key_grad = (product_rows(score_grad, queries) * scale).astype(jnp.bfloat16)
        query_grad = lax.psum_scatter(
            (product_plain(score_grad, key_rows) * scale).astype(jnp.bfloat16),
            "tok",
            scatter_dimension=0,
            tiled=True,
        )
        add_term(grads, "key_weight", product_rows(normed, key_grad))
        add_term(grads, "value_weight", product_rows(normed, value_grad))
        normed_grad = product_cols(key_grad, key_weight) + product_cols(value_grad, value_weight)
        source_grad, gain_grad = norm_back(source, token_gain, normed_grad)
        add_term(grads, "token_gain", gain_grad)
        token_grads.append(source_grad)
        add_term(grads, "query_weight", product_rows(latent_normed, query_grad))
        latent_grad, gain_grad = norm_back(
            latent_in, query_gain, product_cols(query_grad, query_weight)
        )
        add_term(grads, "query_gain", gain_grad)
        latent_grads.append(latent_upstream + latent_grad)
    parts = (
        lax.psum_scatter(
            grads["token_gain"].astype(jnp.bfloat16), "tok", scatter_dimension=0, tiled=True
        ).astype(jnp.float32),
        lax.psum_scatter(
            grads["query_gain"].astype(jnp.bfloat16), "tok", scatter_dimension=0, tiled=True
        ).astype(jnp.float32),
        lax.psum_scatter(
            grads["query_weight"].astype(jnp.bfloat16), "tok", scatter_dimension=0, tiled=True
        ).astype(jnp.float32),
        lax.psum_scatter(
            grads["key_weight"].astype(jnp.bfloat16), "tok", scatter_dimension=0, tiled=True
        ).astype(jnp.float32),
        lax.psum_scatter(
            grads["value_weight"].astype(jnp.bfloat16), "tok", scatter_dimension=0, tiled=True
        ).astype(jnp.float32),
        lax.psum_scatter(
            grads["output_weight"].astype(jnp.bfloat16), "tok", scatter_dimension=0, tiled=True
        ).astype(jnp.float32),
        lax.psum_scatter(
            grads["first_gain"].astype(jnp.bfloat16), "tok", scatter_dimension=0, tiled=True
        ).astype(jnp.float32),
        lax.psum_scatter(
            grads["first_up"].astype(jnp.bfloat16), "tok", scatter_dimension=0, tiled=True
        ).astype(jnp.float32),
        lax.psum_scatter(
            grads["first_down"].astype(jnp.bfloat16), "tok", scatter_dimension=0, tiled=True
        ).astype(jnp.float32),
        lax.psum_scatter(
            grads["mixer_gain"].astype(jnp.bfloat16), "tok", scatter_dimension=0, tiled=True
        ).astype(jnp.float32),
        lax.psum_scatter(
            grads["mixer_project"].astype(jnp.bfloat16), "tok", scatter_dimension=0, tiled=True
        ).astype(jnp.float32),
        lax.psum_scatter(
            grads["mixer_output"].astype(jnp.bfloat16), "tok", scatter_dimension=0, tiled=True
        ).astype(jnp.float32),
        lax.psum_scatter(
            grads["second_gain"].astype(jnp.bfloat16), "tok", scatter_dimension=0, tiled=True
        ).astype(jnp.float32),
        lax.psum_scatter(
            grads["second_up"].astype(jnp.bfloat16), "tok", scatter_dimension=0, tiled=True
        ).astype(jnp.float32),
        lax.psum_scatter(
            grads["second_down"].astype(jnp.bfloat16), "tok", scatter_dimension=0, tiled=True
        ).astype(jnp.float32),
    )
    summed = (
        lax.psum(parts[0].astype(jnp.bfloat16), "grp").astype(jnp.float32),
        lax.psum(parts[1].astype(jnp.bfloat16), "grp").astype(jnp.float32),
        lax.psum(parts[2].astype(jnp.bfloat16), "grp").astype(jnp.float32),
        lax.psum(parts[3].astype(jnp.bfloat16), "grp").astype(jnp.float32),
        lax.psum(parts[4].astype(jnp.bfloat16), "grp").astype(jnp.float32),
        lax.psum(parts[5].astype(jnp.bfloat16), "grp").astype(jnp.float32),
        lax.psum(parts[6].astype(jnp.bfloat16), "grp").astype(jnp.float32),
        lax.psum(parts[7].astype(jnp.bfloat16), "grp").astype(jnp.float32),
        lax.psum(parts[8].astype(jnp.bfloat16), "grp").astype(jnp.float32),
        lax.psum(parts[9].astype(jnp.bfloat16), "grp").astype(jnp.float32),
        lax.psum(parts[10].astype(jnp.bfloat16), "grp").astype(jnp.float32),
        lax.psum(parts[11].astype(jnp.bfloat16), "grp").astype(jnp.float32),
        lax.psum(parts[12].astype(jnp.bfloat16), "grp").astype(jnp.float32),
        lax.psum(parts[13].astype(jnp.bfloat16), "grp").astype(jnp.float32),
        lax.psum(parts[14].astype(jnp.bfloat16), "grp").astype(jnp.float32),
    )
    return (
        jnp.stack(latent_outs)[None],
        jnp.stack(latent_grads)[None],
        jnp.stack(token_grads)[None],
    ) + tuple(summed)


TOK = 8
ROWS = L // TOK
FF = 2048
GR = L // LGROUPS
LOG2E = 1.4426950408889634
LN2 = 0.6931471805599453
F32 = jnp.float32
BF16 = jnp.bfloat16
MIB = 1024 * 1024


def nn(left, right):
    return lax.dot_general(left, right, (((1,), (0,)), ((), ())), preferred_element_type=F32)


def nt(left, right):
    return lax.dot_general(left, right, (((1,), (1,)), ((), ())), preferred_element_type=F32)


def tn(left, right):
    return lax.dot_general(left, right, (((0,), (0,)), ((), ())), preferred_element_type=F32)


def norm_parts(values):
    centre = values - jnp.mean(values, axis=-1, keepdims=True)
    inverse = lax.rsqrt(jnp.mean(centre * centre, axis=-1, keepdims=True) + EPS)
    return centre * inverse, inverse


def norm_pull(hat, inverse, gain, upstream):
    scaled = upstream * gain
    inner = jnp.mean(scaled * hat, axis=-1, keepdims=True)
    grad = (scaled - jnp.mean(scaled, axis=-1, keepdims=True) - hat * inner) * inverse
    return grad, upstream * hat


def places():
    me = lax.axis_index("tok")
    core = lax.rem(me, 2)
    chip = lax.div(me, 2)
    mate = me + 1 - 2 * core
    flip_x = chip + 1 - 2 * lax.rem(chip, 2)
    flip_y = lax.rem(chip + 2, 4)
    far = 3 - chip
    return me, core, chip, mate, (far, flip_x, flip_y)


def remote(src, dst, send_sem, recv_sem, peer):
    return pltpu.make_async_remote_copy(
        src_ref=src,
        dst_ref=dst,
        send_sem=send_sem,
        recv_sem=recv_sem,
        device_id={"tok": peer},
        device_id_type=pl.DeviceIdType.MESH,
    )


def greet(devices):
    barrier = pltpu.get_barrier_semaphore()
    for device in devices:
        pl.semaphore_signal(
            barrier, inc=1, device_id={"tok": device}, device_id_type=pl.DeviceIdType.MESH
        )
    pl.semaphore_wait(barrier, len(devices))


def chip_at(chip, flip):
    high, low = divmod(flip, 2) if isinstance(flip, int) else (lax.div(flip, 2), lax.rem(flip, 2))
    across = lax.rem(lax.rem(chip, 2) + low, 2)
    along = lax.rem(lax.div(chip, 2) + high, 2)
    return 2 * along + across


def mask_loads(seg_ref, mask_ref, seg_buf, mask_buf, sem):
    return (
        pltpu.make_async_copy(seg_ref.at[0], seg_buf, sem.at[0]),
        pltpu.make_async_copy(mask_ref.at[0], mask_buf, sem.at[1]),
    )


def mask_rows(seg_buf, mask_buf, count_ref, bias_ref):
    for member in range(MB):
        scene = lax.broadcasted_iota(jnp.int32, (SCENES, TOK_DEV), 0)
        place = lax.broadcasted_iota(jnp.int32, (SCENES, TOK_DEV), 1)
        hot = jnp.where((seg_buf[member:member + 1] == scene) & (place < count_ref[0, member, 0]), 1.0, 0.0)
        seen = tn(jnp.where(mask_buf[member] > 0, 1.0, 0.0).astype(BF16), hot.astype(BF16))
        bias_ref[member] = jnp.where(seen > 0.5, 0.0, NEG)


def to_rows(first, second):
    rows = first.shape[0]
    lane = lax.broadcasted_iota(jnp.int32, (rows, 128), 1)
    return jnp.where(lane == 0, first, second).T[0:8]


def cross_forward_kernel(
    tok_ref, lat_ref, tgain_ref, qgain_ref, qw_ref, kw_ref, vw_ref, seg_ref, mask_ref, count_ref,
    k_out, v_out, q_out, att_ref, lse_ref,
    tok_buf, lat_buf, keys, values, queries, bias, part, part_s, got, got_s, stage, stage_s,
    arrive, arrive_s, total, seg_buf, mask_buf,
    mask_sem, tok_sem, lat_sem, k_sem, v_sem, q_sem,
    core_send, core_recv, core_send_s, core_recv_s, chip_send, chip_recv, chip_send_s, chip_recv_s,
):
    me, core, chip, mate, others = places()
    span = 2 * ROWS

    def unpack(step):
        return lax.div(step, 4), 3 - lax.rem(step, 4)

    def lat_copy(step):
        member, flip = unpack(step)
        start = pl.multiple_of(chip_at(chip, flip) * span, span)
        return pltpu.make_async_copy(lat_ref.at[0, member, pl.ds(start, span)], lat_buf.at[step], lat_sem.at[step])

    def q_copy(step):
        member, flip = unpack(step)
        start = pl.multiple_of(chip_at(chip, flip) * span, span)
        return pltpu.make_async_copy(queries.at[step], q_out.at[member, pl.ds(start, span)], q_sem.at[step])

    def tok_copy(member):
        return pltpu.make_async_copy(tok_ref.at[0, member], tok_buf.at[member], tok_sem.at[member])

    def kv_copies(member):
        return (
            pltpu.make_async_copy(keys.at[member], k_out.at[member], k_sem.at[member]),
            pltpu.make_async_copy(values.at[member], v_out.at[member], v_sem.at[member]),
        )

    def core_copies(step):
        return (
            remote(part.at[step, 1 - core], got.at[step], core_send.at[step], core_recv.at[step], mate),
            remote(part_s.at[step, 1 - core], got_s.at[step], core_send_s.at[step], core_recv_s.at[step], mate),
        )

    def chip_copies(step):
        member, flip = unpack(step)
        peer = 2 * chip_at(chip, flip) + core
        place = 3 * member + flip - 1
        return (
            remote(stage.at[step], arrive.at[place], chip_send.at[place], chip_recv.at[place], peer),
            remote(stage_s.at[step], arrive_s.at[place], chip_send_s.at[place], chip_recv_s.at[place], peer),
        )

    tok_copy(0).start()
    masks = mask_loads(seg_ref, mask_ref, seg_buf, mask_buf, mask_sem)
    for copy in masks:
        copy.start()
    for step in range(4):
        lat_copy(step).start()
    tok_copy(1).start()
    for step in range(4, 2 * 4):
        lat_copy(step).start()
    greet([mate] + [2 * other + core for other in others])
    for copy in masks:
        copy.wait()
    mask_rows(seg_buf, mask_buf, count_ref, bias)

    def compute(step):
        member, flip = unpack(step)

        @pl.when(flip == 3)
        def _():
            tok_copy(member).wait()
            hat, inverse = norm_parts(tok_buf[member].astype(F32))
            normed = (hat * tgain_ref[...]).astype(BF16)
            keys[member] = nn(normed, kw_ref[...]).astype(BF16)
            values[member] = nn(normed, vw_ref[...]).astype(BF16)
            for copy in kv_copies(member):
                copy.start()

        lat_copy(step).wait()
        hat, inverse = norm_parts(lat_buf[step])
        normed = (hat * qgain_ref[...]).astype(BF16)
        asked = (nn(normed, qw_ref[...]) * (D ** (-0.5) * LOG2E)).astype(BF16)
        queries[step] = asked
        q_copy(step).start()
        scores = nt(asked, keys[member])
        raised = []
        for half in range(2):
            seen = bias[member, pl.ds(2 * chip_at(chip, flip) + half, 1), :]
            own = scores[half * ROWS:(half + 1) * ROWS] + seen
            top = jnp.max(own, axis=1, keepdims=True)
            own = jnp.exp2(own - top)
            part_s[step, half] = to_rows(top, jnp.sum(own, axis=1, keepdims=True))
            raised.append(own.astype(BF16))
        sums = nn(jnp.concatenate(raised, axis=0), values[member]).astype(BF16)
        for half in range(2):
            part[step, half] = sums[half * ROWS:(half + 1) * ROWS]
        for copy in core_copies(step):
            copy.start()

    def merge(one, one_s, two, two_s):
        top = jnp.maximum(one_s[0:1], two_s[0:1])
        one_w, two_w = jnp.exp2(one_s[0:1] - top), jnp.exp2(two_s[0:1] - top)
        sums = one_s[1:2] * one_w + two_s[1:2] * two_w
        spare = jnp.zeros((6, ROWS), F32)
        weights = jnp.concatenate([one_w, two_w, spare], axis=0).T
        return one * weights[:, 0:1] + two * weights[:, 1:2], jnp.concatenate([top, sums, spare], axis=0)

    def combine(step):
        member, flip = unpack(step)
        for copy in core_copies(step):
            copy.wait_recv()
        added, figures = merge(
            part[step, core].astype(F32), part_s[step, core], got[step].astype(F32), got_s[step]
        )
        stage_s[step] = figures

        @pl.when(flip > 0)
        def _():
            stage[step] = added.astype(BF16)
            for copy in chip_copies(step):
                copy.start()

        @pl.when(flip == 0)
        def _():
            total[member] = added

    def finish(member):
        added, figures = total[member], stage_s[4 * member + 3]
        for flip in (1, 2, 3):
            for copy in chip_copies(4 * member + 3 - flip):
                copy.wait_recv()
            place = 3 * member + flip - 1
            added, figures = merge(added, figures, arrive[place].astype(F32), arrive_s[place])
        spare = jnp.zeros((7, ROWS), F32)
        inverse = jnp.concatenate([1.0 / figures[1:2], spare], axis=0).T
        att_ref[member] = added * inverse[:, 0:1]
        lse_ref[member] = jnp.concatenate([figures[0:1] + jnp.log2(figures[1:2]), spare], axis=0)

    def step_body(step, carry):
        compute(step)

        @pl.when(step > 0)
        def _():
            combine(step - 1)

        return carry

    lax.fori_loop(0, 4 * MB, step_body, 0)
    combine(jnp.int32(4 * MB - 1))
    for member in range(MB):
        finish(member)
    for member in range(MB):
        for copy in kv_copies(member):
            copy.wait()
        for slot in range(4):
            step = 4 * member + slot
            q_copy(step).wait()
            for copy in core_copies(step):
                copy.wait_send()
            if slot < 3:
                for copy in chip_copies(step):
                    copy.wait_send()


def cross_forward(collective_id, *args):
    dma = pltpu.SemaphoreType.DMA
    span = 2 * ROWS
    steps = 4 * MB
    vmem = pl.BlockSpec(memory_space=pltpu.VMEM)
    hbm = pl.BlockSpec(memory_space=pl.ANY)
    return pl.pallas_call(
        cross_forward_kernel,
        in_specs=[hbm, hbm] + [vmem] * 5 + [hbm, hbm, pl.BlockSpec(memory_space=pltpu.SMEM)],
        out_specs=[hbm, hbm, hbm, vmem, vmem],
        out_shape=[
            jax.ShapeDtypeStruct((MB, TOK_DEV, D), BF16),
            jax.ShapeDtypeStruct((MB, TOK_DEV, D), BF16),
            jax.ShapeDtypeStruct((MB, L, D), BF16),
            jax.ShapeDtypeStruct((MB, ROWS, D), F32),
            jax.ShapeDtypeStruct((MB, 8, ROWS), F32),
        ],
        scratch_shapes=[
            pltpu.VMEM((MB, TOK_DEV, D), BF16),
            pltpu.VMEM((steps, span, D), F32),
            pltpu.VMEM((MB, TOK_DEV, D), BF16),
            pltpu.VMEM((MB, TOK_DEV, D), BF16),
            pltpu.VMEM((steps, span, D), BF16),
            pltpu.VMEM((MB, LGROUPS, TOK_DEV), F32),
            pltpu.VMEM((steps, 2, ROWS, D), BF16),
            pltpu.VMEM((steps, 2, 8, ROWS), F32),
            pltpu.VMEM((steps, ROWS, D), BF16),
            pltpu.VMEM((steps, 8, ROWS), F32),
            pltpu.VMEM((steps, ROWS, D), BF16),
            pltpu.VMEM((steps, 8, ROWS), F32),
            pltpu.VMEM((3 * MB, ROWS, D), BF16),
            pltpu.VMEM((3 * MB, 8, ROWS), F32),
            pltpu.VMEM((MB, ROWS, D), F32),
            pltpu.VMEM((MB, TOK_DEV), jnp.int32),
            pltpu.VMEM((MB, SCENES, LGROUPS), jnp.int32),
            dma((2,)), dma((MB,)), dma((steps,)), dma((MB,)), dma((MB,)), dma((steps,)),
        ] + [dma((steps,))] * 4 + [dma((3 * MB,))] * 4,
        compiler_params=pltpu.CompilerParams(
            collective_id=collective_id, has_side_effects=True, vmem_limit_bytes=56 * MIB
        ),
        cost_estimate=pl.CostEstimate(
            flops=14 * 10**9, bytes_accessed=22 * 10**6, transcendentals=4 * 10**6
        ),
        name="cross_forward",
    )(*args)


def cross_backward_kernel(
    items, grad_items,
    tok_ref, tgain_ref, kw_ref, vw_ref, seg_ref, mask_ref, count_ref, k_ref, v_ref, q_ref, up_ref, fig_ref,
    lat_ref, lup_ref, qgain_ref, qw_ref, fgain_ref, mgain_ref, sgain_ref, *refs,
):
    count, more = len(items), len(grad_items)
    parts, sources = refs[:count], refs[count:count + more]
    refs = refs[count + more:]
    dlat_ref, dtok_ref, dkw_ref, dvw_ref, dqw_ref, gains_ref = refs[:6]
    sums, helds = refs[6:6 + count], refs[6 + count:6 + count + more]
    rest = refs[6 + count + more:]
    cut = CROSS_SCRATCH + 3 * count + 2
    grp, grp_devices = grp_steps(items, parts, sums, rest[CROSS_SCRATCH:cut])
    tok, near_devices = tok_steps(grad_items, sources, rest[cut:])
    (tok_buf, keys, values, queries, ups, figs, bias, part, got, stage, arrive, far_in, total, dk, dv, dkw, dvw,
     dgain_ref, lat, lup, seg_buf, mask_buf, mask_sem, tail_sem,
     tok_sem, k_sem, v_sem, q_sem, out_sem, near_send, near_recv, far_send, far_recv, on_send, on_recv, own_sem,
     fig_send, fig_recv, core_send, core_recv, chip_send, chip_recv, half_send, half_recv) = rest[:CROSS_SCRATCH]
    me, core, chip, mate, others = places()
    span = 2 * ROWS

    def slot_of(step):
        late = lax.div(step + 3, 8)
        member = jnp.where(step == 1, 1, late)
        flip = jnp.where(step < 2, 0, jnp.where(late == 0, step - 1, 8 - step))
        return member, flip

    def loads(step):
        member, flip = slot_of(step)
        start = pl.multiple_of(chip_at(chip, flip) * span, span)
        ring = lax.rem(step, 4)
        return pltpu.make_async_copy(q_ref.at[member, pl.ds(start, span)], queries.at[ring], q_sem.at[ring])

    def tok_copies(member):
        return (
            pltpu.make_async_copy(k_ref.at[member], keys.at[member], k_sem.at[member]),
            pltpu.make_async_copy(v_ref.at[member], values.at[member], v_sem.at[member]),
            pltpu.make_async_copy(tok_ref.at[0, member], tok_buf.at[member], tok_sem.at[member]),
        )

    def out_copy(member):
        return pltpu.make_async_copy(dk.at[member], dtok_ref.at[0, member], out_sem.at[member])

    def own_copies(member):
        slot = 4 * member
        return (
            pltpu.make_async_copy(up_ref.at[member], ups.at[slot, core], own_sem.at[member, 0]),
            pltpu.make_async_copy(fig_ref.at[member], figs.at[slot, core], own_sem.at[member, 1]),
        )

    def near_copies(member):
        slot = 4 * member
        return [
            remote(up_ref.at[member], ups.at[slot, core], near_send.at[member, 0], near_recv.at[member, 0], mate),
            remote(fig_ref.at[member], figs.at[slot, core], near_send.at[member, 1], near_recv.at[member, 1], mate),
        ]

    half_rows = (pl.ds(0, ROWS // 2), pl.ds(ROWS // 2, ROWS // 2))

    def far_copies(slot):
        member, flip = slot // 4, slot % 4
        peer = 2 * chip_at(chip, flip) + core
        if flip < 3:
            return [
                remote(up_ref.at[member], ups.at[slot, core], far_send.at[slot, 0], far_recv.at[slot, 0], peer),
                remote(fig_ref.at[member], figs.at[slot, core], far_send.at[slot, 1], far_recv.at[slot, 1], peer),
            ]
        copies = []
        for half, (held, toward) in enumerate(((1, 2), (2, 1))):
            copies.append(remote(
                ups.at[4 * member + held, core, half_rows[half]], ups.at[slot, core, half_rows[half]],
                far_send.at[slot, half], far_recv.at[slot, half], 2 * chip_at(chip, toward) + core,
            ))
        copies.append(remote(
            figs.at[4 * member + 1, core], figs.at[slot, core], fig_send.at[member], fig_recv.at[member],
            2 * chip_at(chip, 2) + core,
        ))
        return copies

    def on_copies(slot):
        return (
            remote(ups.at[slot, core], ups.at[slot, core], on_send.at[slot, 0], on_recv.at[slot, 0], mate),
            remote(figs.at[slot, core], figs.at[slot, core], on_send.at[slot, 1], on_recv.at[slot, 1], mate),
        )

    def pass_on(slot):
        for copy in far_copies(slot):
            copy.wait_recv()
        for copy in on_copies(slot):
            copy.start()

    def pass_near(member):
        pass_on(4 * member + 1)
        pass_on(4 * member + 2)
        for copy in far_copies(4 * member + 3):
            copy.start()

    def half_copy(member, half):
        return remote(
            stage.at[4 * member + 3, half_rows[half]], far_in.at[member, half], half_send.at[member, half],
            half_recv.at[member, half], 2 * chip_at(chip, half + 1) + core,
        )

    def half_copies(member):
        return [half_copy(member, half) for half in range(2)]

    def core_copy(step):
        member, flip = slot_of(step)
        slot, ring = 4 * member + flip, lax.rem(step, 4)
        return remote(part.at[ring, 1 - core], got.at[slot], core_send.at[slot], core_recv.at[slot], mate)

    def chip_copy(slot):
        member, flip = slot // 4, slot % 4
        peer = 2 * chip_at(chip, flip) + core
        place = 2 * member + flip - 1
        return remote(stage.at[slot], arrive.at[place], chip_send.at[place], chip_recv.at[place], peer)

    def relay(member):
        for half in range(2):
            half_copy(member, half).wait_recv()
            slot = 4 * member + 2 - half
            joined = stage.at[slot, half_rows[half]]
            add(joined, joined, far_in.at[member, half])
            chip_copy(slot).start()

    masks = mask_loads(seg_ref, mask_ref, seg_buf, mask_buf, mask_sem)
    for copy in masks:
        copy.start()
    own_rows = pl.ds(pl.multiple_of(me * ROWS, ROWS), ROWS)
    tails = (
        pltpu.make_async_copy(lat_ref.at[0, :, own_rows], lat, tail_sem.at[0]),
        pltpu.make_async_copy(lup_ref, lup, tail_sem.at[1]),
    )
    for copy in own_copies(0):
        copy.start()
    for copy in tok_copies(0):
        copy.start()
    for step in range(3):
        loads(jnp.int32(step)).start()
    for copy in own_copies(1):
        copy.start()
    for copy in tok_copies(1):
        copy.start()
    for copy in tails:
        copy.start()
    greet_all([mate] + [2 * other + core for other in others], grp_devices)
    for member in range(MB):
        for copy in near_copies(member):
            copy.start()
    for flip in (1, 2):
        for copy in far_copies(flip):
            copy.start()
    for item in range(more):
        tok[0](item)
    for item in range(count):
        grp[0](item)
    for copy in masks:
        copy.wait()
    mask_rows(seg_buf, mask_buf, count_ref, bias)

    def compute(step):
        member, flip = slot_of(step)
        slot = 4 * member + flip

        @pl.when(step < 2)
        def _():
            for copy in tok_copies(member):
                copy.wait()
            dk[member] = jnp.zeros((TOK_DEV, D), F32)
            dv[member] = jnp.zeros((TOK_DEV, D), F32)

        loads(step).wait()

        @pl.when(step + 3 < 4 * MB)
        def _():
            loads(step + 3).start()

        @pl.when(flip == 0)
        def _():
            for copy in own_copies(member):
                copy.wait()
            for copy in near_copies(member):
                copy.wait_recv()

        @pl.when(flip > 0)
        def _():
            for copy in on_copies(slot):
                copy.wait_recv()

        asked = queries[lax.rem(step, 4)]
        upstream = ups[slot].reshape(span, D)
        scores = nt(asked, keys[member])
        soft = nt(upstream, values[member])
        weights, grads = [], []
        for half in range(2):
            seen = bias[member, pl.ds(2 * chip_at(chip, flip) + half, 1), :]
            figures = figs[slot, half].T
            rows = slice(half * ROWS, (half + 1) * ROWS)
            weight = jnp.exp2(scores[rows] + seen - figures[:, 0:1])
            grads.append((weight * (soft[rows] - figures[:, 1:2])).astype(BF16))
            weights.append(weight.astype(BF16))
        weight = jnp.concatenate(weights, axis=0)
        grad = jnp.concatenate(grads, axis=0)
        dv[member] += tn(weight, upstream)
        dk[member] += tn(grad, asked)
        asked_grad = (nn(grad, keys[member]) * D ** (-0.5)).astype(BF16)

        @pl.when(step >= 4)
        def _():
            core_copy(step - 4).wait_send()

        for half in range(2):
            part[lax.rem(step, 4), half] = asked_grad[half * ROWS:(half + 1) * ROWS]
        core_copy(step).start()

    def combine(step):
        member, flip = slot_of(step)
        slot = 4 * member + flip
        core_copy(step).wait_recv()
        added = part[lax.rem(step, 4), core].astype(F32) + got[slot].astype(F32)

        @pl.when(flip > 0)
        def _():
            stage[slot] = added.astype(BF16)

        @pl.when(flip == 0)
        def _():
            total[member] = added

    def tokens_back(member, half):
        gain = tgain_ref[...]
        rows = pl.ds(pl.multiple_of(half * span, span), span)
        hat, inverse = norm_parts(tok_buf[member, rows].astype(F32))
        normed = (hat * gain).astype(BF16)
        key_grad = (dk[member, rows] * LN2).astype(BF16)
        value_grad = dv[member, rows].astype(BF16)
        dkw[...] += tn(normed, key_grad)
        dvw[...] += tn(normed, value_grad)
        normed_grad = nt(key_grad, kw_ref[...]) + nt(value_grad, vw_ref[...])
        source_grad, gain_rows = norm_pull(hat, inverse, gain, normed_grad)
        dk[member, rows] = source_grad
        dgain_ref[...] += jnp.sum(gain_rows, axis=0, keepdims=True)

    def hold(item):
        helds[item][...] = tok[4](item).astype(helds[item].dtype)

    def step_body(step, carry):
        compute(step)

        @pl.when(step > 0)
        def _():
            combine(step - 1)

        @pl.when(step == 0)
        def _():
            for flip in (1, 2):
                for copy in far_copies(4 + flip):
                    copy.start()
            tok[1](0)

        @pl.when(step == 1)
        def _():
            pass_near(0)

        @pl.when(step == 2)
        def _():
            tok[1](1)

        @pl.when(step == 3)
        def _():
            pass_on(3)
            pass_near(1)

        @pl.when(step == 4)
        def _():
            pass_on(7)
            for item in range(count):
                grp[1](item)
            tok[1](2)

        @pl.when(step == 5)
        def _():
            for copy in half_copies(0):
                copy.start()
            tok[2](0)

        @pl.when(step == 6)
        def _():
            for copy in half_copies(1):
                copy.start()
            relay(0)

        @pl.when(step == 4 * MB - 1)
        def _():
            tok[3](0)
            tok[2](1)

        return carry

    lax.fori_loop(0, 4 * MB, step_body, 0)

    def tokens_body(member, carry):
        @pl.when(member == 1)
        def _():
            hold(0)
            tok[2](2)

        for half in range(TOK_DEV // span):
            tokens_back(member, half)
        out_copy(member).start()

        @pl.when(member == 0)
        def _():
            combine(4 * MB - 1)
            relay(1)

        return carry

    dkw[...] = jnp.zeros_like(dkw)
    dvw[...] = jnp.zeros_like(dvw)
    dgain_ref[...] = jnp.zeros_like(dgain_ref)
    lax.fori_loop(0, MB, tokens_body, 0)
    dkw_ref[...] = dkw[...].astype(BF16)
    dvw_ref[...] = dvw[...].astype(BF16)
    tok[3](1)
    tok[3](2)
    for copy in tails:
        copy.wait()
    gain = qgain_ref[...]
    hat, inverse = norm_parts(lat[...].reshape(MB * ROWS, D))
    normed = (hat * gain).astype(BF16)
    asked_grads = []
    for member in range(MB):
        added = total[member]
        for flip in (1, 2):
            chip_copy(4 * member + flip).wait_recv()
            added = added + arrive[2 * member + flip - 1].astype(F32)
        asked_grads.append(added.astype(BF16))
    asked_grad = jnp.concatenate(asked_grads, axis=0)
    dqw_ref[...] = tn(normed, asked_grad).astype(BF16)
    source_grad, gain_rows = norm_pull(hat, inverse, gain, nt(asked_grad, qw_ref[...]))
    lup[...] += source_grad
    last = pltpu.make_async_copy(lup, dlat_ref, tail_sem.at[2])
    last.start()
    query_gain = jnp.sum(gain_rows, axis=0, keepdims=True)
    rows = jnp.concatenate(
        [dgain_ref[...], query_gain, fgain_ref[...], mgain_ref[...], sgain_ref[...], jnp.zeros((3, D), F32)], axis=0
    )
    gains_ref[...] = jnp.zeros_like(gains_ref)
    width = D // TOK
    for device in range(TOK):
        gains_ref[16 * device:16 * device + 8, 0:width] = rows[:, device * width:(device + 1) * width]
    for item in range(count):
        grp[2](item)
    grp[3]()
    hold(1)
    hold(2)
    tok[5]()
    last.wait()
    for step in range(4, 4 * MB):
        core_copy(jnp.int32(step)).wait_send()
    for member in range(MB):
        out_copy(member).wait()
        for copy in near_copies(member) + half_copies(member):
            copy.wait_send()
        for flip in range(4):
            slot = 4 * member + flip
            if flip > 0:
                for copy in far_copies(slot):
                    copy.wait_send()
                for copy in on_copies(slot):
                    copy.wait_send()
            if flip in (1, 2):
                chip_copy(slot).wait_send()


CROSS_SCRATCH = 44


def cross_backward(collective_id, arrays, grads, *args):
    dma = pltpu.SemaphoreType.DMA
    span = 2 * ROWS
    steps = 4 * MB
    vmem = pl.BlockSpec(memory_space=pltpu.VMEM)
    hbm = pl.BlockSpec(memory_space=pl.ANY)
    smem = pl.BlockSpec(memory_space=pltpu.SMEM)
    items, kinds = held_plan(arrays)
    sources, grad_items, grad_kinds, shapes = reduce_plan(grads)
    scratch = [
        pltpu.VMEM((MB, TOK_DEV, D), BF16),
        pltpu.VMEM((MB, TOK_DEV, D), BF16),
        pltpu.VMEM((MB, TOK_DEV, D), BF16),
        pltpu.VMEM((4, span, D), BF16),
        pltpu.VMEM((steps, 2, ROWS, D), BF16),
        pltpu.VMEM((steps, 2, 8, ROWS), F32),
        pltpu.VMEM((MB, LGROUPS, TOK_DEV), F32),
        pltpu.VMEM((4, 2, ROWS, D), BF16),
        pltpu.VMEM((steps, ROWS, D), BF16),
        pltpu.VMEM((steps, ROWS, D), BF16),
        pltpu.VMEM((2 * MB, ROWS, D), BF16),
        pltpu.VMEM((MB, 2, ROWS // 2, D), BF16),
        pltpu.VMEM((MB, ROWS, D), F32),
        pltpu.VMEM((MB, TOK_DEV, D), F32),
        pltpu.VMEM((MB, TOK_DEV, D), F32),
        pltpu.VMEM((D, D), F32),
        pltpu.VMEM((D, D), F32),
        pltpu.VMEM((1, D), F32),
        pltpu.VMEM((MB, ROWS, D), F32),
        pltpu.VMEM((MB * ROWS, D), F32),
        pltpu.VMEM((MB, TOK_DEV), jnp.int32),
        pltpu.VMEM((MB, SCENES, LGROUPS), jnp.int32),
        dma((2,)), dma((3,)),
        dma((MB,)), dma((MB,)), dma((MB,)), dma((4,)), dma((MB,)),
        dma((MB, 2)), dma((MB, 2)), dma((steps, 2)), dma((steps, 2)), dma((steps, 2)), dma((steps, 2)), dma((MB, 2)),
        dma((MB,)), dma((MB,)),
        dma((steps,)), dma((steps,)), dma((2 * MB,)), dma((2 * MB,)), dma((MB, 2)), dma((MB, 2)),
    ]
    return pl.pallas_call(
        functools.partial(cross_backward_kernel, items, grad_items),
        in_specs=[hbm] + [vmem] * 3 + [hbm, hbm, smem] + [hbm] * 7 + [vmem] * 5 + [vmem] * len(arrays) + [hbm] * len(grads),
        out_specs=[hbm, hbm] + [vmem] * (4 + len(arrays) + len(grads)),
        out_shape=[
            jax.ShapeDtypeStruct((MB * ROWS, D), F32),
            jax.ShapeDtypeStruct((1, MB, TOK_DEV, D), F32),
            jax.ShapeDtypeStruct((D, D), BF16),
            jax.ShapeDtypeStruct((D, D), BF16),
            jax.ShapeDtypeStruct((D, D), BF16),
            jax.ShapeDtypeStruct((16 * TOK, 128), F32),
        ] + [jax.ShapeDtypeStruct((item[1], item[3]), F32) for item in items]
        + [jax.ShapeDtypeStruct((high // 2, wide), kind) for (high, wide), kind in zip(shapes, grad_kinds)],
        scratch_shapes=scratch + grp_scratch(items, kinds) + tok_scratch(grad_items, grad_kinds),
        compiler_params=pltpu.CompilerParams(
            collective_id=collective_id, has_side_effects=True, vmem_limit_bytes=60 * MIB
        ),
        cost_estimate=pl.CostEstimate(
            flops=26 * 10**9, bytes_accessed=24 * 10**6, transcendentals=4 * 10**6
        ),
        name="cross_backward",
    )(*args, *arrays, *sources)


GELU_A = 0.7978845608028654
GELU_B = 0.044715


def gelu_parts(hidden):
    square = hidden * hidden
    bent = jnp.tanh(GELU_A * hidden * (1.0 + GELU_B * square))
    half = 0.5 * (1.0 + bent)
    slope = half + 0.5 * hidden * (1.0 - bent * bent) * (GELU_A * (1.0 + 3.0 * GELU_B * square))
    return hidden * half, slope


def greet_all(tok_devices, grp_devices=()):
    barrier = pltpu.get_barrier_semaphore()
    for axis, devices in (("tok", tok_devices), ("grp", grp_devices)):
        for device in devices:
            pl.semaphore_signal(
                barrier, inc=1, device_id={axis: device}, device_id_type=pl.DeviceIdType.MESH
            )
    pl.semaphore_wait(barrier, len(tok_devices) + len(grp_devices))


def all_peers():
    me, core, chip, mate, others = places()
    peers = []
    for other in others:
        peers += [2 * other + core, 2 * other + 1 - core]
    return me, peers + [mate]


def head_copies(row_side, head_side, to_heads, member, me, peers, send, recv, local):
    lanes = pl.ds(member * ROWS, ROWS)
    row_at = lambda device: row_side.at[:, device, :, lanes]
    head_at = lambda device: head_side.at[:, member, :, pl.ds(pl.multiple_of(device * ROWS, ROWS), ROWS)]
    source, target = (row_at, head_at) if to_heads else (head_at, row_at)
    copies = [
        remote(source(peer), target(me), send.at[slot, member], recv.at[slot, member], peer)
        for slot, peer in enumerate(peers)
    ]
    return copies, pltpu.make_async_copy(source(me), target(me), local.at[member])


QB = 1024
QB_BACK = 256


def latents_forward_kernel(
    lat_ref, att_ref, cot_ref, ow_ref, fgain_ref, fup_ref, fdown_ref, mgain_ref, proj_ref, mow_ref, sgain_ref,
    sup_ref, sdown_ref,
    out_ref, fmid_ref, mmid_ref, packed_ref, exact_ref, lse_ref, up_ref, mgrad_ref, ddown_ref, dup_ref, dmo_ref,
    dgain_ref,
    lat, att, cot, ow, fup, fdown, proj, mow, sup, sdown,
    out, fmid, mmid, heads, exact, up, mgrad, ddown, dup, dmo,
    rows_out, keys, values, mixed, mixed_rows,
    load_sem, store_sem, send_a, recv_a, local_a, send_b, recv_b, local_b,
):
    me, peers = all_peers()
    own = pl.ds(pl.multiple_of(me * ROWS, ROWS), ROWS)
    names = ("lat", "att", "ow", "fup", "fdown", "proj", "mow", "sup", "sdown", "cot")
    loads = {}
    for i, (source, target) in enumerate((
        (lat_ref.at[0, :, own], lat), (att_ref, att), (ow_ref, ow), (fup_ref, fup), (fdown_ref, fdown),
        (proj_ref, proj), (mow_ref, mow), (sup_ref, sup), (sdown_ref, sdown), (cot_ref.at[0], cot),
    )):
        loads[names[i]] = pltpu.make_async_copy(source, target, load_sem.at[i])
        loads[names[i]].start()
    stores = []

    def store(source, target):
        stores.append(pltpu.make_async_copy(source, target, store_sem.at[len(stores)]))
        stores[-1].start()

    greet_all(peers)
    flat = (MB * ROWS, D)
    for name in ("lat", "att", "ow"):
        loads[name].wait()
    first = lat[...].reshape(flat) + nn(att[...].reshape(flat).astype(BF16), ow[...])
    fmid[...] = first
    store(fmid, fmid_ref)
    normed = (norm_parts(first)[0] * fgain_ref[...]).astype(BF16)
    loads["fup"].wait()
    loads["fdown"].wait()
    mid = first
    for part in range(2):
        cut = slice(part * FF // 2, (part + 1) * FF // 2)
        mid = mid + nn(jax.nn.gelu(nn(normed, fup[:, cut])).astype(BF16), fdown[cut])
    mmid[...] = mid
    store(mmid, mmid_ref)
    normed = (norm_parts(mid)[0] * mgain_ref[...]).astype(BF16).T
    loads["proj"].wait()
    for kind, scale in enumerate((HD ** (-0.5) * LOG2E, 1.0, 1.0)):
        packed = tn(proj[:, kind * D:(kind + 1) * D], normed) * scale
        rows_out[kind] = packed.astype(BF16).reshape(H, HD, MB * ROWS)
    outward = [head_copies(rows_out, heads, True, member, me, peers, send_a, recv_a, local_a) for member in range(MB)]
    backward = [
        head_copies(mixed_rows, mixed, False, member, me, peers, send_b, recv_b, local_b) for member in range(MB)
    ]
    for copies, here in outward:
        for copy in copies:
            copy.start()
        here.start()
    for member in range(MB):
        copies, here = outward[member]
        for copy in copies:
            copy.wait_recv()
        here.wait()
        store(heads.at[:, member], packed_ref.at[:, member])
        keys[...] = heads[1, member].T
        values[0:HD] = heads[2, member]
        values[HD:] = jnp.ones((16, L), BF16)

        def attend(step, carry, member=member):
            at = pl.ds(pl.multiple_of(step * QB, QB), QB)
            logits = nn(keys[...], heads[0, member, :, at])
            top = jnp.max(logits, axis=0, keepdims=True)
            both = nn(values[...], jnp.exp2(logits - top).astype(BF16))
            total = both[HD:HD + 1]
            result = both[0:HD] / total
            exact[member, :, at] = result
            mixed[0, member, :, at] = result.astype(BF16)
            lse_ref[member, :, at] = jnp.broadcast_to(top + jnp.log2(total), (8, QB))
            return carry

        lax.fori_loop(0, L // QB, attend, 0)
        for copy in backward[member][0] + [backward[member][1]]:
            copy.start()
    store(exact, exact_ref)
    loads["mow"].wait()
    loads["sup"].wait()
    loads["sdown"].wait()
    loads["cot"].wait()
    for copies, here in backward:
        for copy in copies:
            copy.wait_recv()
        here.wait()
    mixed_t = mixed_rows[0].reshape(D, MB * ROWS)
    second = mmid[...] + tn(mixed_t, mow[...])
    hat, inverse = norm_parts(second)
    normed = (hat * sgain_ref[...]).astype(BF16)
    upstream = cot[...].reshape(flat)
    grad = upstream.astype(BF16)
    final = second
    normed_grad = jnp.zeros(flat, F32)
    for part in range(2):
        cut = slice(part * FF // 2, (part + 1) * FF // 2)
        act, slope = gelu_parts(nn(normed, sup[:, cut]))
        act = act.astype(BF16)
        final = final + nn(act, sdown[cut])
        hidden_grad = (slope * nt(grad, sdown[cut])).astype(BF16)
        normed_grad = normed_grad + nt(hidden_grad, sup[:, cut])
        ddown[cut] = tn(act, grad).astype(BF16)
        dup[:, cut] = tn(normed, hidden_grad).astype(BF16)
    store(ddown, ddown_ref)
    store(dup, dup_ref)
    out[...] = final.reshape(MB, ROWS, D)
    store(out, out_ref.at[0])
    residual, gain_rows = norm_pull(hat, inverse, sgain_ref[...], normed_grad)
    dgain_ref[...] = jnp.sum(gain_rows, axis=0, keepdims=True)
    upstream = upstream + residual
    up[...] = upstream
    store(up, up_ref)
    grad = upstream.astype(BF16)
    mgrad[0] = nt(mow[...], grad).astype(BF16).reshape(H, HD, MB * ROWS)
    store(mgrad, mgrad_ref)
    dmo[...] = nn(mixed_t, grad).astype(BF16)
    store(dmo, dmo_ref)
    for copy in stores:
        copy.wait()
    for copies, here in outward + backward:
        for copy in copies:
            copy.wait_send()


def latents_forward(collective_id, *args):
    dma = pltpu.SemaphoreType.DMA
    vmem = pl.BlockSpec(memory_space=pltpu.VMEM)
    hbm = pl.BlockSpec(memory_space=pl.ANY)
    rows = MB * ROWS
    stored = [
        ((1, MB, ROWS, D), F32), ((rows, D), F32), ((rows, D), F32), ((3, MB, HD, L), BF16), ((MB, HD, L), F32),
        ((MB, 8, L), F32), ((rows, D), F32), ((1, H, HD, rows), BF16), ((FF, D), BF16), ((D, FF), BF16), ((D, D), BF16),
        ((1, D), F32),
    ]
    return pl.pallas_call(
        latents_forward_kernel,
        in_specs=[hbm, hbm, hbm, hbm, vmem, hbm, hbm, vmem, hbm, hbm, vmem, hbm, hbm],
        out_specs=[hbm] * 5 + [vmem] + [hbm] * 5 + [vmem],
        out_shape=[jax.ShapeDtypeStruct(shape, kind) for shape, kind in stored],
        scratch_shapes=[
            pltpu.VMEM((MB, ROWS, D), F32), pltpu.VMEM((MB, ROWS, D), F32), pltpu.VMEM((MB, ROWS, D), F32),
            pltpu.VMEM((D, D), BF16), pltpu.VMEM((D, FF), BF16), pltpu.VMEM((FF, D), BF16),
            pltpu.VMEM((D, 3 * D), BF16), pltpu.VMEM((D, D), BF16), pltpu.VMEM((D, FF), BF16),
            pltpu.VMEM((FF, D), BF16),
            pltpu.VMEM((MB, ROWS, D), F32), pltpu.VMEM((rows, D), F32), pltpu.VMEM((rows, D), F32),
            pltpu.VMEM((3, MB, HD, L), BF16), pltpu.VMEM((MB, HD, L), F32), pltpu.VMEM((rows, D), F32),
            pltpu.VMEM((1, H, HD, rows), BF16), pltpu.VMEM((FF, D), BF16), pltpu.VMEM((D, FF), BF16),
            pltpu.VMEM((D, D), BF16),
            pltpu.VMEM((3, H, HD, rows), BF16), pltpu.VMEM((L, HD), BF16), pltpu.VMEM((HD + 16, L), BF16),
            pltpu.VMEM((1, MB, HD, L), BF16), pltpu.VMEM((1, H, HD, rows), BF16),
            dma((10,)), dma((11,)), dma((7, MB)), dma((7, MB)), dma((MB,)), dma((7, MB)), dma((7, MB)), dma((MB,)),
        ],
        compiler_params=pltpu.CompilerParams(
            collective_id=collective_id, has_side_effects=True, vmem_limit_bytes=60 * MIB
        ),
        cost_estimate=pl.CostEstimate(
            flops=20 * 10**9, bytes_accessed=30 * 10**6, transcendentals=10 * 10**6
        ),
        name="latents_forward",
    )(*args)


def levels():
    level = lax.axis_index("grp")
    odd = lax.rem(level, 2)
    return odd, level + 1 - 2 * odd, lax.rem(level + 2, 4)


def half_slices(rows, odd):
    half = rows // 2
    keep = pl.ds(pl.multiple_of(odd * half, half), half)
    away = pl.ds(pl.multiple_of((1 - odd) * half, half), half)
    return keep, away


def tok_steps(items, sources, scratch):
    n = len(items)
    mine, got, near_in, first_in, second_in = [scratch[i * n:(i + 1) * n] for i in range(5)]
    (local_sem, core_send, core_recv, near_send, near_recv, one_send, one_recv, two_send, two_recv) = scratch[5 * n:]
    me, core, chip, mate, (far, flip_x, flip_y) = places()
    x, y = lax.rem(chip, 2), lax.div(chip, 2)
    odd, level_near, level_far = levels()

    def core_copies(i):
        source, rows, row_at, columns, column_at, x_first = items[i]
        part = (pl.ds(row_at, rows), pl.ds(column_at, columns))
        return (
            remote(sources[source].at[:, :, 1 - core, *part], got[i], core_send.at[i], core_recv.at[i], mate),
            pltpu.make_async_copy(sources[source].at[:, :, core, *part], mine[i], local_sem.at[i]),
        )

    def near_copy(i):
        keep, away = half_slices(items[i][1], odd)
        return pltpu.make_async_remote_copy(
            src_ref=mine[i].at[:, :, away], dst_ref=near_in[i], send_sem=near_send.at[i], recv_sem=near_recv.at[i],
            device_id={"grp": level_near}, device_id_type=pl.DeviceIdType.MESH,
        )

    def first_copy(i):
        keep, away = half_slices(items[i][1], odd)
        x_first = items[i][-1]
        source = mine[i].at[:, 1 - x, keep] if x_first else mine[i].at[1 - y, :, keep]
        peer = 2 * (flip_x if x_first else flip_y) + core
        return remote(source, first_in[i], one_send.at[i], one_recv.at[i], peer)

    def second_copy(i):
        keep, away = half_slices(items[i][1], odd)
        x_first = items[i][-1]
        source = mine[i].at[1 - y, x, keep] if x_first else mine[i].at[y, 1 - x, keep]
        peer = 2 * (flip_y if x_first else flip_x) + core
        return remote(source, second_in[i], two_send.at[i], two_recv.at[i], peer)

    def core_sends(i):
        for copy in core_copies(i):
            copy.start()

    def core_sums(i):
        there, here = core_copies(i)
        there.wait_recv()
        here.wait()
        add(mine[i], mine[i], got[i])
        near_copy(i).start()

    def near_sums(i):
        keep, away = half_slices(items[i][1], odd)
        near_copy(i).wait_recv()
        held = mine[i].at[:, :, keep]
        add(held, held, near_in[i])
        first_copy(i).start()

    def first_sums(i):
        keep, away = half_slices(items[i][1], odd)
        first_copy(i).wait_recv()
        held = mine[i].at[:, x, keep] if items[i][-1] else mine[i].at[y, :, keep]
        add(held, held, first_in[i])
        second_copy(i).start()

    def second_sums(i):
        keep, away = half_slices(items[i][1], odd)
        second_copy(i).wait_recv()
        return mine[i][y, x, keep].astype(F32) + second_in[i][...].astype(F32)

    def finish():
        for i in range(n):
            core_copies(i)[0].wait_send()
            for copy in (near_copy(i), first_copy(i), second_copy(i)):
                copy.wait_send()

    return (core_sends, core_sums, near_sums, first_sums, second_sums, finish), (
        mate, 2 * flip_x + core, 2 * flip_y + core)


def grp_steps(items, held, outs, scratch):
    n = len(items)
    far_in, joined, near_in = [scratch[i * n:(i + 1) * n] for i in range(3)]
    z_send, z_recv = scratch[3 * n:]
    odd, level_near, level_far = levels()

    def along(i, step):
        source, target, other = (
            (held[i], far_in[i], level_far),
            (joined[i], near_in[i], level_near),
        )[step]
        return pltpu.make_async_remote_copy(
            src_ref=source, dst_ref=target, send_sem=z_send.at[i, step], recv_sem=z_recv.at[i, step],
            device_id={"grp": other}, device_id_type=pl.DeviceIdType.MESH,
        )

    def store(i, odd_half, value):
        source, rows, row_at, columns, column_at, x_first = items[i]
        half = rows // 2
        start = pl.multiple_of(row_at + odd_half * half, half)
        outs[source][pl.ds(start, half), pl.ds(column_at, columns)] = value.astype(F32)

    def far_start(i):
        along(i, 0).start()

    def far_sum(i):
        along(i, 0).wait_recv()
        add(joined[i], held[i], far_in[i])
        along(i, 1).start()
        store(i, odd, joined[i][...])

    def near_store(i):
        along(i, 1).wait_recv()
        store(i, 1 - odd, near_in[i][...])

    def finish():
        for i in range(n):
            for step in range(2):
                along(i, step).wait_send()

    return (far_start, far_sum, near_store, finish), (level_near, level_far)


def add(target, one, two):
    target[...] = (one[...].astype(F32) + two[...].astype(F32)).astype(target.dtype)


def reduce_kernel(items, whole, count, whole_count, *refs):
    n, m = len(items), len(whole)
    sources, held = refs[:count], refs[count:count + m]
    outs = refs[count + m:2 * count + m]
    whole_outs = refs[2 * count + m:2 * count + m + whole_count]
    scratch = refs[2 * count + m + whole_count:]
    cut = 5 * n + 9
    own_held = scratch[cut:cut + n]
    tok, near_devices = tok_steps(items, sources, scratch[:cut])
    late, grp_devices = grp_steps(items, own_held, outs, scratch[cut + n:cut + 4 * n + 2])
    early, unused = grp_steps(whole, held, whole_outs, scratch[cut + 4 * n + 2:])
    greet_all(near_devices, grp_devices)

    def last_sums(i):
        own_held[i][...] = tok[4](i).astype(own_held[i].dtype)
        late[0](i)

    for i in range(n):
        tok[0](i)
    early[0](0)
    for i in range(n):
        tok[1](i)
    for i in range(1, m):
        early[0](i)
    for i in range(n):
        tok[2](i)
    early[1](0)
    for i in range(n):
        tok[3](i)
    for i in range(n):
        last_sums(i)
    for i in range(1, m):
        early[1](i)
        early[2](i - 1)
    for i in range(n):
        late[1](i)
    early[2](m - 1)
    for i in range(n):
        late[2](i)
    tok[-1]()
    late[-1]()
    early[-1]()


def reduce_plan(arrays):
    sources, items = [], []
    for source, array in enumerate(arrays):
        rows, columns = array.shape[0] // TOK, array.shape[1]
        sources.append(array.reshape(2, 2, 2, rows, columns))
        items.append((source, rows, 0, columns, 0, source % 2 == 0))
    kinds = [array.dtype for array in arrays]
    shapes = [(array.shape[0] // TOK, array.shape[1]) for array in arrays]
    return sources, tuple(items), kinds, shapes


def held_plan(arrays):
    items = tuple((i, 2 * array.shape[0], 0, array.shape[1], 0, True) for i, array in enumerate(arrays))
    return items, [array.dtype for array in arrays]


def item_blocks(items, kinds, lead, part):
    return [pltpu.VMEM(lead + (item[1] // part, item[3]), kind) for item, kind in zip(items, kinds)]


def tok_scratch(items, kinds):
    blocks = functools.partial(item_blocks, items, kinds)
    return (blocks((2, 2), 1) + blocks((2, 2), 1) + blocks((2, 2), 2) + blocks((2,), 2) + blocks((), 2)
            + [pltpu.SemaphoreType.DMA((len(items),))] * 9)


def grp_scratch(items, kinds):
    blocks = functools.partial(item_blocks, items, kinds)
    return blocks((), 2) * 3 + [pltpu.SemaphoreType.DMA((len(items), 2))] * 2


def reduce_grads(collective_id, arrays, held):
    sources, items, kinds, shapes = reduce_plan(arrays)
    whole, whole_kinds = held_plan(held)
    vmem = pl.BlockSpec(memory_space=pltpu.VMEM)
    hbm = pl.BlockSpec(memory_space=pl.ANY)
    return pl.pallas_call(
        functools.partial(reduce_kernel, items, whole, len(arrays), len(held)),
        in_specs=[hbm] * len(arrays) + [vmem] * len(held),
        out_specs=[vmem] * (len(arrays) + len(held)),
        out_shape=[jax.ShapeDtypeStruct(shape, F32) for shape in shapes]
        + [jax.ShapeDtypeStruct((item[1], item[3]), F32) for item in whole],
        scratch_shapes=tok_scratch(items, kinds) + item_blocks(items, kinds, (), 2) + grp_scratch(items, kinds)
        + grp_scratch(whole, whole_kinds),
        compiler_params=pltpu.CompilerParams(
            collective_id=collective_id, has_side_effects=True, vmem_limit_bytes=56 * MIB
        ),
        name="reduce_grads",
    )(*sources, *held)


def write_kernel(count, *refs):
    sources, gain_ref, outs = refs[:count], refs[count], refs[count + 1:2 * count + 1]
    gain_outs, buffers = refs[2 * count + 1:-count - 2], refs[-count - 2:-2]
    in_sem, out_sem = refs[-2:]
    ins = [pltpu.make_async_copy(sources[i], buffers[i], in_sem.at[i]) for i in range(count)]
    backs = [pltpu.make_async_copy(buffers[i], outs[i], out_sem.at[i]) for i in range(count)]
    for copy in ins:
        copy.start()
    for i, out in enumerate(gain_outs):
        out[...] = gain_ref[i:i + 1, 0:D // TOK]
    for i in range(count):
        ins[i].wait()
        backs[i].start()
    for copy in backs:
        copy.wait()


def write_results(results, gains, gain_count):
    n = len(results)
    hbm, vmem = pl.BlockSpec(memory_space=pl.ANY), pl.BlockSpec(memory_space=pltpu.VMEM)
    return pl.pallas_call(
        functools.partial(write_kernel, n),
        in_specs=[hbm] * n + [vmem],
        out_specs=[hbm] * n + [vmem] * gain_count,
        out_shape=[jax.ShapeDtypeStruct(result.shape, result.dtype) for result in results]
        + [jax.ShapeDtypeStruct((1, D // TOK), F32)] * gain_count,
        scratch_shapes=[pltpu.VMEM(result.shape, result.dtype) for result in results]
        + [pltpu.SemaphoreType.DMA((n,)), pltpu.SemaphoreType.DMA((n,))],
        compiler_params=pltpu.CompilerParams(vmem_limit_bytes=40 * MIB),
        name="write_results",
    )(*results, gains)


def latents_backward_kernel(items, *refs):
    (mgrad_ref, packed_ref, exact_ref, lse_ref, up_ref, mmid_ref, fmid_ref, att_ref, clse_ref, ow_ref, fgain_ref,
     fup_ref, fdown_ref, mgain_ref, proj_ref) = refs[:15]
    count = max(item[0] for item in items) + 1
    sources = refs[15:15 + count]
    (agrad_ref, fig_ref, lup_ref, dup_ref, ddown_ref, dproj_ref, dout_ref, dmgain_ref, dfgain_ref) = refs[
        15 + count:24 + count]
    reduced = refs[24 + count:24 + 2 * count]
    rest = refs[24 + 2 * count:]
    (heads, exact, ups, mmid, fmid, att, ow, fup, fdown, proj, keys, values, upstream_heads, key_acc, value_acc,
     grads, back, agrad, lup, dup, ddown, dproj, dout, hidden,
     load_sem, store_sem, send_a, recv_a, local_a, send_b, recv_b, local_b) = rest[:32]
    me, peers = all_peers()
    reducer, near_devices = tok_steps(items, sources, rest[32:])
    core_sends, core_sums, near_sums, first_sums, second_sums, finish = reducer
    odd, level_near, level_far = levels()

    def hold(item):
        reduced[item][...] = second_sums(item).astype(reduced[item].dtype)

    names = ("heads", "exact", "fmid", "fup", "up", "mmid", "proj", "fdown", "att", "ow")
    loads = {}
    for i, (source, target) in enumerate((
        (packed_ref, heads), (exact_ref, exact), (fmid_ref, fmid), (fup_ref, fup), (up_ref, ups), (mmid_ref, mmid),
        (proj_ref, proj), (fdown_ref, fdown), (att_ref, att), (ow_ref, ow),
    )):
        loads[names[i]] = pltpu.make_async_copy(source, target, load_sem.at[i])
        loads[names[i]].start()
    stores = []

    def store(source, target):
        stores.append(pltpu.make_async_copy(source, target, store_sem.at[len(stores)]))
        stores[-1].start()

    greet_all(peers, (level_near,))
    outward = [
        head_copies(mgrad_ref, upstream_heads, True, member, me, peers, send_a, recv_a, local_a) for member in range(MB)
    ]
    backward = [head_copies(back, grads, False, member, me, peers, send_b, recv_b, local_b) for member in range(MB)]
    for copies, here in outward:
        for copy in copies:
            copy.start()
        here.start()
    for item in range(3):
        core_sends(item)
    loads["fmid"].wait()
    loads["fup"].wait()
    first_hat, first_inverse = norm_parts(fmid[...])
    first_normed = (first_hat * fgain_ref[...]).astype(BF16)
    hidden[...] = nn(first_normed, fup[...])
    core_sums(0)
    loads["heads"].wait()
    loads["exact"].wait()
    for member in range(MB):
        keys[...] = heads[1, member].T
        values[...] = heads[2, member].T
        key_acc[...] = jnp.zeros_like(key_acc)
        value_acc[...] = jnp.zeros_like(value_acc)
        copies, here = outward[member]
        for copy in copies:
            copy.wait_recv()
        here.wait()

        def attend_back(step, carry, member=member):
            at = pl.ds(pl.multiple_of(step * QB_BACK, QB_BACK), QB_BACK)
            queries = heads[0, member, :, at]
            upstream = upstream_heads[0, member, :, at]
            inner = jnp.sum(upstream.astype(F32) * exact[member, :, at], axis=0, keepdims=True)
            softened = jnp.exp2(nn(keys[...], queries) - lse_ref[member, 0:1, at])
            logit_grad = (softened * (nn(values[...], upstream) - inner)).astype(BF16)
            value_acc[...] += nt(upstream, softened.astype(BF16))
            key_acc[...] += nt(queries, logit_grad)
            grads[0, member, :, at] = (nn(heads[1, member], logit_grad) * HD ** (-0.5)).astype(BF16)
            return carry

        steps = L // QB_BACK
        lax.fori_loop(0, steps, attend_back, 0)
        grads[1, member] = (key_acc[...] * LN2).astype(BF16)
        grads[2, member] = value_acc[...].astype(BF16)
        for copy in backward[member][0] + [backward[member][1]]:
            copy.start()
        if member == 0:
            near_sums(0)
            core_sums(1)
            core_sums(2)
        else:
            first_sums(0)
            near_sums(1)
            near_sums(2)
    loads["up"].wait()
    loads["mmid"].wait()
    loads["proj"].wait()
    loads["fdown"].wait()
    mixer_hat, mixer_inverse = norm_parts(mmid[...])
    mixer_normed = (mixer_hat * mgain_ref[...]).astype(BF16).T
    for copies, here in backward:
        for copy in copies:
            copy.wait_recv()
        here.wait()
    hold(0)
    first_sums(1)
    first_sums(2)
    packed_grad = back[...].reshape(3 * D, MB * ROWS)
    normed_grad = nn(proj[...], packed_grad).T
    residual, gain_rows = norm_pull(mixer_hat, mixer_inverse, mgain_ref[...], normed_grad)
    dmgain_ref[...] = jnp.sum(gain_rows, axis=0, keepdims=True)
    upstream = ups[...] + residual
    dproj[...] = nt(mixer_normed, packed_grad).astype(BF16)
    store(dproj, dproj_ref)
    grad = upstream.astype(BF16)
    normed_grad = jnp.zeros((MB * ROWS, D), F32)
    for part in range(2):
        cut = slice(part * FF // 2, (part + 1) * FF // 2)
        act, slope = gelu_parts(hidden[:, cut])
        hidden_grad = (slope * nt(grad, fdown[cut])).astype(BF16)
        normed_grad = normed_grad + nt(hidden_grad, fup[:, cut])
        ddown[cut] = tn(act.astype(BF16), grad).astype(BF16)
        dup[:, cut] = tn(first_normed, hidden_grad).astype(BF16)
    store(ddown, ddown_ref)
    store(dup, dup_ref)
    residual, gain_rows = norm_pull(first_hat, first_inverse, fgain_ref[...], normed_grad)
    dfgain_ref[...] = jnp.sum(gain_rows, axis=0, keepdims=True)
    upstream = upstream + residual
    lup[...] = upstream
    store(lup, lup_ref)
    grad = upstream.astype(BF16)
    loads["att"].wait()
    loads["ow"].wait()
    attended = att[...].reshape(MB * ROWS, D)
    attended_grad = nt(grad, ow[...]).astype(BF16)
    agrad[...] = attended_grad.reshape(MB, ROWS, D)
    store(agrad, agrad_ref)
    inner = jnp.sum(attended_grad.astype(F32) * attended, axis=1, keepdims=True)
    for member in range(MB):
        rows = slice(member * ROWS, (member + 1) * ROWS)
        spare = jnp.zeros((6, ROWS), F32)
        fig_ref[member] = jnp.concatenate(
            [clse_ref[member, 0:1], to_rows(inner[rows], inner[rows])[0:1], spare], axis=0
        )
    dout[...] = tn(attended.astype(BF16), grad).astype(BF16)
    store(dout, dout_ref)
    hold(1)
    hold(2)
    finish()
    for copy in stores:
        copy.wait()
    for copies, here in outward + backward:
        for copy in copies:
            copy.wait_send()


def latents_backward(collective_id, arrays, *args):
    dma = pltpu.SemaphoreType.DMA
    vmem = pl.BlockSpec(memory_space=pltpu.VMEM)
    hbm = pl.BlockSpec(memory_space=pl.ANY)
    rows = MB * ROWS
    sources, items, kinds, shapes = reduce_plan(arrays)
    reduced = [jax.ShapeDtypeStruct((rows_ // 2, columns), kind) for (rows_, columns), kind in zip(shapes, kinds)]
    stored = [
        ((MB, ROWS, D), BF16), ((MB, 8, ROWS), F32), ((rows, D), F32), ((D, FF), BF16), ((FF, D), BF16),
        ((D, 3 * D), BF16), ((D, D), BF16), ((1, D), F32), ((1, D), F32),
    ]
    return pl.pallas_call(
        functools.partial(latents_backward_kernel, items),
        in_specs=[hbm, hbm, hbm, vmem, hbm, hbm, hbm, hbm, vmem, hbm, vmem, hbm, hbm, vmem, hbm] + [hbm] * len(arrays),
        out_specs=[hbm, vmem] + [hbm] * 5 + [vmem] * (2 + len(arrays)),
        out_shape=[jax.ShapeDtypeStruct(shape, kind) for shape, kind in stored] + reduced,
        scratch_shapes=[
            pltpu.VMEM((3, MB, HD, L), BF16), pltpu.VMEM((MB, HD, L), F32), pltpu.VMEM((rows, D), F32),
            pltpu.VMEM((rows, D), F32), pltpu.VMEM((rows, D), F32), pltpu.VMEM((MB, ROWS, D), F32),
            pltpu.VMEM((D, D), BF16), pltpu.VMEM((D, FF), BF16), pltpu.VMEM((FF, D), BF16),
            pltpu.VMEM((D, 3 * D), BF16), pltpu.VMEM((L, HD), BF16), pltpu.VMEM((L, HD), BF16),
            pltpu.VMEM((1, MB, HD, L), BF16), pltpu.VMEM((HD, L), F32), pltpu.VMEM((HD, L), F32),
            pltpu.VMEM((3, MB, HD, L), BF16), pltpu.VMEM((3, H, HD, rows), BF16),
            pltpu.VMEM((MB, ROWS, D), BF16), pltpu.VMEM((rows, D), F32), pltpu.VMEM((D, FF), BF16),
            pltpu.VMEM((FF, D), BF16), pltpu.VMEM((D, 3 * D), BF16), pltpu.VMEM((D, D), BF16),
            pltpu.VMEM((rows, FF), F32),
            dma((10,)), dma((6,)), dma((7, MB)), dma((7, MB)), dma((MB,)), dma((7, MB)), dma((7, MB)), dma((MB,)),
        ] + tok_scratch(items, kinds),
        compiler_params=pltpu.CompilerParams(
            collective_id=collective_id, has_side_effects=True, vmem_limit_bytes=61 * MIB
        ),
        cost_estimate=pl.CostEstimate(
            flops=35 * 10**9, bytes_accessed=36 * 10**6, transcendentals=10 * 10**6
        ),
        name="latents_backward",
    )(*args, *sources)


def fast_body(
    tokens,
    latents,
    segments,
    scene_mask,
    counts,
    token_gain,
    query_gain,
    query_weight,
    key_weight,
    value_weight,
    output_weight,
    first_gain,
    first_up,
    first_down,
    mixer_gain,
    mixer_project,
    mixer_output,
    second_gain,
    second_up,
    second_down,
    cotangent,
):
    scenes = (segments, scene_mask, counts)
    keys, values, queries, attended, lse = cross_forward(
        0, tokens, latents, token_gain[None], query_gain[None], query_weight, key_weight, value_weight, *scenes
    )
    (latents_out, first_mid, mixer_mid, packed, exact, head_lse, upstream, mixed_grad, d_second_down, d_second_up,
     d_mixer_output, d_second_gain) = latents_forward(
        1, latents, attended, cotangent, output_weight, first_gain[None], first_up, first_down, mixer_gain[None],
        mixer_project, mixer_output, second_gain[None], second_up, second_down,
    )
    (attended_grad, figures, upstream, d_first_up, d_first_down, d_project, d_output, d_mixer_gain, d_first_gain,
     *early) = latents_backward(
        2, [d_second_up, d_second_down, d_mixer_output], mixed_grad, packed, exact, head_lse, upstream, mixer_mid,
        first_mid, attended, lse, output_weight, first_gain[None], first_up, first_down, mixer_gain[None], mixer_project,
    )
    latents_grad, tokens_grad, d_key, d_value, d_query, gains, *rest = cross_backward(
        5, early, [d_first_up, d_first_down, d_project], tokens, token_gain[None], key_weight, value_weight,
        *scenes, keys, values, queries, attended_grad, figures, latents, upstream, query_gain[None], query_weight,
        d_first_gain, d_mixer_gain, d_second_gain,
    )
    early, held = rest[:len(early)], rest[len(early):]
    o_output, o_key, o_value, o_query, gains, *late = reduce_grads(
        7, [d_output, d_key, d_value, d_query, gains], held
    )
    (latents_out, latents_grad, tokens_grad, o_second_up, o_second_down, o_mixer_output, o_first_up, o_first_down,
     o_project, o_output, o_key, o_value, o_query, *o_gains) = write_results(
        [latents_out, latents_grad.reshape(latents_out.shape), tokens_grad, *early, *late, o_output, o_key, o_value, o_query], gains, 5
    )
    o_gains = [gain.reshape(D // TOK) for gain in o_gains]
    return (
        latents_out,
        latents_grad,
        tokens_grad,
        o_gains[0],
        o_gains[1],
        o_query,
        o_key,
        o_value,
        o_output,
        o_gains[2],
        o_first_up,
        o_first_down,
        o_gains[3],
        o_project,
        o_mixer_output,
        o_gains[4],
        o_second_up,
        o_second_down,
    )


IN_SPECS = (
    P("grp", None, "tok", None),
    P("grp", None, None, None),
    P("grp", None, "tok"),
    P("grp", None, None, None),
    P("grp", None, "tok"),
    P(),
    P(),
    P(),
    P(),
    P(),
    P(),
    P(),
    P(),
    P(),
    P(),
    P(),
    P(),
    P(),
    P(),
    P(),
    P("grp", None, "tok", None),
)
OUT_SPECS = (
    P("grp", None, "tok", None),
    P("grp", None, "tok", None),
    P("grp", None, "tok", None),
    P("tok"),
    P("tok"),
    P("tok", None),
    P("tok", None),
    P("tok", None),
    P("tok", None),
    P("tok"),
    P("tok", None),
    P("tok", None),
    P("tok"),
    P("tok", None),
    P("tok", None),
    P("tok"),
    P("tok", None),
    P("tok", None),
)


def solution(mesh):
    return jax.shard_map(
        fast_body if mesh.shape["tok"] == TOK else general_body,
        mesh=mesh,
        in_specs=IN_SPECS,
        out_specs=OUT_SPECS,
        check_vma=False,
    )
```

```python
import functools

import jax
import jax.numpy as jnp
from jax import lax
from jax.experimental import pallas as pl
from jax.experimental.pallas import tpu as pltpu
from jax.sharding import PartitionSpec as P

D = 512
L = 2048
H = 8
HD = 64
TOK_DEV = 1024
MB = 2
SCENES = 8
LGROUPS = 8


EPS = 1e-05
NEG = -1e30


def norm_rows(values, gain):
    centre = values - jnp.mean(values, axis=-1, keepdims=True)
    spread = jnp.mean(centre * centre, axis=-1, keepdims=True)
    return centre * lax.rsqrt(spread + EPS) * gain


def norm_back(values, gain, upstream):
    unused, pull = jax.vjp(norm_rows, values, gain)
    return pull(upstream)


def gelu_back(hidden, upstream):
    unused, pull = jax.vjp(jax.nn.gelu, hidden)
    return pull(upstream)[0]


def product_plain(left, right):
    return jnp.dot(left, right, preferred_element_type=jnp.float32)


def product_rows(left, right):
    return lax.dot_general(
        left, right, (((0,), (0,)), ((), ())), preferred_element_type=jnp.float32
    )


def product_cols(left, right):
    return lax.dot_general(
        left, right, (((1,), (1,)), ((), ())), preferred_element_type=jnp.float32
    )


def add_term(store, name, value):
    if name in store:
        store[name] = store[name] + value
    else:
        store[name] = value


def project_tokens(tokens, member, token_gain, key_weight, value_weight):
    source = tokens[0, member].astype(jnp.float32)
    normed = norm_rows(source, token_gain).astype(jnp.bfloat16)
    key_rows = product_plain(normed, key_weight).astype(jnp.bfloat16)
    value_rows = product_plain(normed, value_weight).astype(jnp.bfloat16)
    return (source, normed, key_rows, value_rows)


def mlp_forward(residual, gain, up_weight, down_weight):
    normed = norm_rows(residual, gain).astype(jnp.bfloat16)
    hidden = product_plain(normed, up_weight)
    active = jax.nn.gelu(hidden).astype(jnp.bfloat16)
    return (residual + product_plain(active, down_weight), (normed, hidden, active))


def mlp_backward(residual, gain, up_weight, down_weight, saved, upstream):
    normed, hidden, active = saved
    grad_low = upstream.astype(jnp.bfloat16)
    grad_down = product_rows(active, grad_low)
    hidden_grad = gelu_back(hidden, product_cols(grad_low, down_weight)).astype(jnp.bfloat16)
    grad_up = product_rows(normed, hidden_grad)
    residual_grad, grad_gain = norm_back(residual, gain, product_cols(hidden_grad, up_weight))
    return (upstream + residual_grad, grad_gain, grad_up, grad_down)


def mixer_forward(residual, gain, project, output):
    own_rows = residual.shape[0]
    normed = norm_rows(residual, gain).astype(jnp.bfloat16)
    packed = product_plain(normed, project).astype(jnp.bfloat16)
    pair_rows = lax.all_gather(packed[:, D:], "tok", axis=0, tiled=True)
    every = pair_rows.shape[0]
    own_queries = packed[:, :D].reshape(own_rows, H, HD)
    keys = pair_rows[:, :D].reshape(every, H, HD)
    values = pair_rows[:, D:].reshape(every, H, HD)
    logits = jnp.einsum(
        "qhd,khd->hqk", own_queries, keys, preferred_element_type=jnp.float32
    ) * HD ** (-0.5)
    peak_row = jnp.max(logits, axis=-1, keepdims=True)
    raised = jnp.exp(logits - peak_row)
    softened = raised / jnp.sum(raised, axis=-1, keepdims=True)
    softened_low = softened.astype(jnp.bfloat16)
    mixed_rows = jnp.einsum(
        "hqk,khd->qhd", softened_low, values, preferred_element_type=jnp.float32
    )
    mixed_rows = mixed_rows.reshape(own_rows, D).astype(jnp.bfloat16)
    return (
        residual + product_plain(mixed_rows, output),
        (normed, own_queries, keys, values, softened, softened_low, mixed_rows),
    )


def mixer_backward(residual, gain, project, output, saved, upstream):
    normed, own_queries, keys, values, softened, softened_low, mixed_rows = saved
    own_rows = upstream.shape[0]
    every = keys.shape[0]
    grad_low = upstream.astype(jnp.bfloat16)
    grad_output = product_rows(mixed_rows, grad_low)
    mixed_grad = product_cols(grad_low, output).astype(jnp.bfloat16).reshape(own_rows, H, HD)
    value_grad = jnp.einsum(
        "hqk,qhd->khd", softened_low, mixed_grad, preferred_element_type=jnp.float32
    )
    soft_grad = jnp.einsum("qhd,khd->hqk", mixed_grad, values, preferred_element_type=jnp.float32)
    logit_grad = softened * (soft_grad - jnp.sum(soft_grad * softened, axis=-1, keepdims=True))
    logit_grad = logit_grad.astype(jnp.bfloat16)
    query_grad = jnp.einsum(
        "hqk,khd->qhd", logit_grad, keys, preferred_element_type=jnp.float32
    ) * HD ** (-0.5)
    key_grad = jnp.einsum(
        "hqk,qhd->khd", logit_grad, own_queries, preferred_element_type=jnp.float32
    ) * HD ** (-0.5)
    pair_terms = jnp.concatenate([key_grad.reshape(every, D), value_grad.reshape(every, D)], axis=1)
    pair_grad = lax.psum_scatter(
        pair_terms.astype(jnp.bfloat16), "tok", scatter_dimension=0, tiled=True
    ).astype(jnp.float32)
    packed_grad = jnp.concatenate([query_grad.reshape(own_rows, D), pair_grad], axis=1).astype(
        jnp.bfloat16
    )
    grad_project = product_rows(normed, packed_grad)
    residual_grad, grad_gain = norm_back(residual, gain, product_cols(packed_grad, project))
    return (upstream + residual_grad, grad_gain, grad_project, grad_output)


def general_body(
    tokens,
    latents,
    segments,
    scene_mask,
    counts,
    token_gain,
    query_gain,
    query_weight,
    key_weight,
    value_weight,
    output_weight,
    first_gain,
    first_up,
    first_down,
    mixer_gain,
    mixer_project,
    mixer_output,
    second_gain,
    second_up,
    second_down,
    cotangent,
):
    scale = D ** (-0.5)
    shards = lax.axis_size("tok")
    own_rows = L // shards
    row_start = lax.axis_index("tok") * own_rows
    latent_group = jnp.arange(L) // (L // LGROUPS)
    latent_onehot = (latent_group[:, None] == jnp.arange(LGROUPS)[None, :]).astype(jnp.float32)
    token_place = jnp.arange(TOK_DEV)
    records = []
    latent_outs = []
    for member in range(MB):
        record = {}
        source, normed, key_rows, value_rows = project_tokens(
            tokens, member, token_gain, key_weight, value_weight
        )
        record["token_side"] = (source, normed, key_rows, value_rows)
        scene_onehot = (segments[0, member][:, None] == jnp.arange(SCENES)[None, :]).astype(
            jnp.float32
        )
        token_seen = jnp.dot(scene_onehot, scene_mask[0, member].astype(jnp.float32))
        visible = product_cols(latent_onehot, token_seen)
        alive = token_place < counts[0, member, 0]
        allowed = (visible > 0.5) & alive[None, :]
        latent_every = latents[0, member]
        normed_every = norm_rows(latent_every, query_gain).astype(jnp.bfloat16)
        queries = product_plain(normed_every, query_weight).astype(jnp.bfloat16)
        scores = jnp.where(allowed, product_cols(queries, key_rows) * scale, NEG)
        row_top = lax.pmax(jnp.max(scores, axis=1), "tok")
        unnormed = jnp.exp(scores - row_top[:, None])
        row_total, weighted = (
            lax.psum_scatter(
                jnp.sum(unnormed, axis=1).astype(jnp.bfloat16),
                "tok",
                scatter_dimension=0,
                tiled=True,
            ).astype(jnp.float32),
            lax.psum_scatter(
                product_plain(unnormed.astype(jnp.bfloat16), value_rows).astype(jnp.bfloat16),
                "tok",
                scatter_dimension=0,
                tiled=True,
            ).astype(jnp.float32),
        )
        latent_in = lax.dynamic_slice_in_dim(latent_every, row_start, own_rows, 0)
        latent_normed = lax.dynamic_slice_in_dim(normed_every, row_start, own_rows, 0)
        attended = weighted / row_total[:, None]
        attended_low = attended.astype(jnp.bfloat16)
        first_mid = latent_in + product_plain(attended_low, output_weight)
        mixer_mid, first_saved = mlp_forward(first_mid, first_gain, first_up, first_down)
        second_mid, mixer_saved = mixer_forward(mixer_mid, mixer_gain, mixer_project, mixer_output)
        final_rows, second_saved = mlp_forward(second_mid, second_gain, second_up, second_down)
        latent_outs.append(final_rows)
        record["latent_side"] = (
            allowed,
            latent_in,
            latent_normed,
            queries,
            row_top,
            row_total,
            attended,
            attended_low,
            first_mid,
            mixer_mid,
            second_mid,
            first_saved,
            mixer_saved,
            second_saved,
        )
        records.append(record)
    grads = {}
    latent_grads = []
    token_grads = []
    for member in range(MB):
        record = records[member]
        source, normed, key_rows, value_rows = record["token_side"]
        (
            allowed,
            latent_in,
            latent_normed,
            queries,
            row_top,
            row_total,
            attended,
            attended_low,
            first_mid,
            mixer_mid,
            second_mid,
            first_saved,
            mixer_saved,
            second_saved,
        ) = record["latent_side"]
        second_back = mlp_backward(
            second_mid, second_gain, second_up, second_down, second_saved, cotangent[0, member]
        )
        add_term(grads, "second_gain", second_back[1])
        add_term(grads, "second_up", second_back[2])
        add_term(grads, "second_down", second_back[3])
        mixer_back = mixer_backward(
            mixer_mid, mixer_gain, mixer_project, mixer_output, mixer_saved, second_back[0]
        )
        add_term(grads, "mixer_gain", mixer_back[1])
        add_term(grads, "mixer_project", mixer_back[2])
        add_term(grads, "mixer_output", mixer_back[3])
        first_back = mlp_backward(
            first_mid, first_gain, first_up, first_down, first_saved, mixer_back[0]
        )
        add_term(grads, "first_gain", first_back[1])
        add_term(grads, "first_up", first_back[2])
        add_term(grads, "first_down", first_back[3])
        latent_upstream = first_back[0]
        grad_low = latent_upstream.astype(jnp.bfloat16)
        add_term(grads, "output_weight", product_rows(attended_low, grad_low))
        attended_grad = lax.optimization_barrier(
            product_cols(grad_low, output_weight).astype(jnp.bfloat16)
        ).astype(jnp.float32)
        weighted_grad = (attended_grad / row_total[:, None]).astype(jnp.bfloat16)
        total_grad = -jnp.sum(attended_grad * attended, axis=1) / row_total
        weighted_every, total_every = (
            lax.all_gather(
                weighted_grad.astype(jnp.float32).astype(jnp.bfloat16), "tok", axis=0, tiled=True
            ).astype(jnp.float32),
            lax.all_gather(total_grad.astype(jnp.bfloat16), "tok", axis=0, tiled=True).astype(
                total_grad.dtype
            ),
        )
        weighted_every = weighted_every.astype(jnp.bfloat16)
        scores = jnp.where(allowed, product_cols(queries, key_rows) * scale, NEG)
        unnormed = jnp.exp(scores - row_top[:, None])
        unnormed_grad = product_cols(weighted_every, value_rows) + total_every[:, None]
        score_grad = (unnormed * unnormed_grad).astype(jnp.bfloat16)
        value_grad = product_rows(unnormed.astype(jnp.bfloat16), weighted_every).astype(
            jnp.bfloat16
        )
        key_grad = (product_rows(score_grad, queries) * scale).astype(jnp.bfloat16)
        query_grad = lax.psum_scatter(
            (product_plain(score_grad, key_rows) * scale).astype(jnp.bfloat16),
            "tok",
            scatter_dimension=0,
            tiled=True,
        )
        add_term(grads, "key_weight", product_rows(normed, key_grad))
        add_term(grads, "value_weight", product_rows(normed, value_grad))
        normed_grad = product_cols(key_grad, key_weight) + product_cols(value_grad, value_weight)
        source_grad, gain_grad = norm_back(source, token_gain, normed_grad)
        add_term(grads, "token_gain", gain_grad)
        token_grads.append(source_grad)
        add_term(grads, "query_weight", product_rows(latent_normed, query_grad))
        latent_grad, gain_grad = norm_back(
            latent_in, query_gain, product_cols(query_grad, query_weight)
        )
        add_term(grads, "query_gain", gain_grad)
        latent_grads.append(latent_upstream + latent_grad)
    parts = (
        lax.psum_scatter(
            grads["token_gain"].astype(jnp.bfloat16), "tok", scatter_dimension=0, tiled=True
        ).astype(jnp.float32),
        lax.psum_scatter(
            grads["query_gain"].astype(jnp.bfloat16), "tok", scatter_dimension=0, tiled=True
        ).astype(jnp.float32),
        lax.psum_scatter(
            grads["query_weight"].astype(jnp.bfloat16), "tok", scatter_dimension=0, tiled=True
        ).astype(jnp.float32),
        lax.psum_scatter(
            grads["key_weight"].astype(jnp.bfloat16), "tok", scatter_dimension=0, tiled=True
        ).astype(jnp.float32),
        lax.psum_scatter(
            grads["value_weight"].astype(jnp.bfloat16), "tok", scatter_dimension=0, tiled=True
        ).astype(jnp.float32),
        lax.psum_scatter(
            grads["output_weight"].astype(jnp.bfloat16), "tok", scatter_dimension=0, tiled=True
        ).astype(jnp.float32),
        lax.psum_scatter(
            grads["first_gain"].astype(jnp.bfloat16), "tok", scatter_dimension=0, tiled=True
        ).astype(jnp.float32),
        lax.psum_scatter(
            grads["first_up"].astype(jnp.bfloat16), "tok", scatter_dimension=0, tiled=True
        ).astype(jnp.float32),
        lax.psum_scatter(
            grads["first_down"].astype(jnp.bfloat16), "tok", scatter_dimension=0, tiled=True
        ).astype(jnp.float32),
        lax.psum_scatter(
            grads["mixer_gain"].astype(jnp.bfloat16), "tok", scatter_dimension=0, tiled=True
        ).astype(jnp.float32),
        lax.psum_scatter(
            grads["mixer_project"].astype(jnp.bfloat16), "tok", scatter_dimension=0, tiled=True
        ).astype(jnp.float32),
        lax.psum_scatter(
            grads["mixer_output"].astype(jnp.bfloat16), "tok", scatter_dimension=0, tiled=True
        ).astype(jnp.float32),
        lax.psum_scatter(
            grads["second_gain"].astype(jnp.bfloat16), "tok", scatter_dimension=0, tiled=True
        ).astype(jnp.float32),
        lax.psum_scatter(
            grads["second_up"].astype(jnp.bfloat16), "tok", scatter_dimension=0, tiled=True
        ).astype(jnp.float32),
        lax.psum_scatter(
            grads["second_down"].astype(jnp.bfloat16), "tok", scatter_dimension=0, tiled=True
        ).astype(jnp.float32),
    )
    summed = (
        lax.psum(parts[0].astype(jnp.bfloat16), "grp").astype(jnp.float32),
        lax.psum(parts[1].astype(jnp.bfloat16), "grp").astype(jnp.float32),
        lax.psum(parts[2].astype(jnp.bfloat16), "grp").astype(jnp.float32),
        lax.psum(parts[3].astype(jnp.bfloat16), "grp").astype(jnp.float32),
        lax.psum(parts[4].astype(jnp.bfloat16), "grp").astype(jnp.float32),
        lax.psum(parts[5].astype(jnp.bfloat16), "grp").astype(jnp.float32),
        lax.psum(parts[6].astype(jnp.bfloat16), "grp").astype(jnp.float32),
        lax.psum(parts[7].astype(jnp.bfloat16), "grp").astype(jnp.float32),
        lax.psum(parts[8].astype(jnp.bfloat16), "grp").astype(jnp.float32),
        lax.psum(parts[9].astype(jnp.bfloat16), "grp").astype(jnp.float32),
        lax.psum(parts[10].astype(jnp.bfloat16), "grp").astype(jnp.float32),
        lax.psum(parts[11].astype(jnp.bfloat16), "grp").astype(jnp.float32),
        lax.psum(parts[12].astype(jnp.bfloat16), "grp").astype(jnp.float32),
        lax.psum(parts[13].astype(jnp.bfloat16), "grp").astype(jnp.float32),
        lax.psum(parts[14].astype(jnp.bfloat16), "grp").astype(jnp.float32),
    )
    return (
        jnp.stack(latent_outs)[None],
        jnp.stack(latent_grads)[None],
        jnp.stack(token_grads)[None],
    ) + tuple(summed)


TOK = 8
ROWS = L // TOK
FF = 2048
GR = L // LGROUPS
LOG2E = 1.4426950408889634
LN2 = 0.6931471805599453
F32 = jnp.float32
BF16 = jnp.bfloat16
MIB = 1024 * 1024


def nn(left, right):
    return lax.dot_general(left, right, (((1,), (0,)), ((), ())), preferred_element_type=F32)


def nt(left, right):
    return lax.dot_general(left, right, (((1,), (1,)), ((), ())), preferred_element_type=F32)


def tn(left, right):
    return lax.dot_general(left, right, (((0,), (0,)), ((), ())), preferred_element_type=F32)


def norm_parts(values):
    centre = values - jnp.mean(values, axis=-1, keepdims=True)
    inverse = lax.rsqrt(jnp.mean(centre * centre, axis=-1, keepdims=True) + EPS)
    return centre * inverse, inverse


def norm_pull(hat, inverse, gain, upstream):
    scaled = upstream * gain
    inner = jnp.mean(scaled * hat, axis=-1, keepdims=True)
    grad = (scaled - jnp.mean(scaled, axis=-1, keepdims=True) - hat * inner) * inverse
    return grad, upstream * hat


def places():
    me = lax.axis_index("tok")
    core = lax.rem(me, 2)
    chip = lax.div(me, 2)
    mate = me + 1 - 2 * core
    flip_x = chip + 1 - 2 * lax.rem(chip, 2)
    flip_y = lax.rem(chip + 2, 4)
    far = 3 - chip
    return me, core, chip, mate, (far, flip_x, flip_y)


def remote(src, dst, send_sem, recv_sem, peer):
    return pltpu.make_async_remote_copy(
        src_ref=src,
        dst_ref=dst,
        send_sem=send_sem,
        recv_sem=recv_sem,
        device_id={"tok": peer},
        device_id_type=pl.DeviceIdType.MESH,
    )


def greet(devices):
    barrier = pltpu.get_barrier_semaphore()
    for device in devices:
        pl.semaphore_signal(
            barrier, inc=1, device_id={"tok": device}, device_id_type=pl.DeviceIdType.MESH
        )
    pl.semaphore_wait(barrier, len(devices))


def chip_at(chip, flip):
    high, low = divmod(flip, 2) if isinstance(flip, int) else (lax.div(flip, 2), lax.rem(flip, 2))
    across = lax.rem(lax.rem(chip, 2) + low, 2)
    along = lax.rem(lax.div(chip, 2) + high, 2)
    return 2 * along + across


def mask_loads(seg_ref, mask_ref, seg_buf, mask_buf, sem):
    return (
        pltpu.make_async_copy(seg_ref.at[0], seg_buf, sem.at[0]),
        pltpu.make_async_copy(mask_ref.at[0], mask_buf, sem.at[1]),
    )


def mask_rows(seg_buf, mask_buf, count_ref, bias_ref):
    for member in range(MB):
        scene = lax.broadcasted_iota(jnp.int32, (SCENES, TOK_DEV), 0)
        place = lax.broadcasted_iota(jnp.int32, (SCENES, TOK_DEV), 1)
        hot = jnp.where((seg_buf[member:member + 1] == scene) & (place < count_ref[0, member, 0]), 1.0, 0.0)
        seen = tn(jnp.where(mask_buf[member] > 0, 1.0, 0.0).astype(BF16), hot.astype(BF16))
        bias_ref[member] = jnp.where(seen > 0.5, 0.0, NEG)


def to_rows(first, second):
    rows = first.shape[0]
    lane = lax.broadcasted_iota(jnp.int32, (rows, 128), 1)
    return jnp.where(lane == 0, first, second).T[0:8]


def cross_forward_kernel(
    tok_ref, lat_ref, tgain_ref, qgain_ref, qw_ref, kw_ref, vw_ref, seg_ref, mask_ref, count_ref,
    k_out, v_out, q_out, att_ref, lse_ref,
    tok_buf, lat_buf, keys, values, queries, bias, part, part_s, got, got_s, stage, stage_s,
    arrive, arrive_s, total, seg_buf, mask_buf,
    mask_sem, tok_sem, lat_sem, k_sem, v_sem, q_sem,
    core_send, core_recv, core_send_s, core_recv_s, chip_send, chip_recv, chip_send_s, chip_recv_s,
):
    me, core, chip, mate, others = places()
    span = 2 * ROWS

    def unpack(step):
        return lax.div(step, 4), 3 - lax.rem(step, 4)

    def lat_copy(step):
        member, flip = unpack(step)
        start = pl.multiple_of(chip_at(chip, flip) * span, span)
        return pltpu.make_async_copy(lat_ref.at[0, member, pl.ds(start, span)], lat_buf.at[step], lat_sem.at[step])

    def q_copy(step):
        member, flip = unpack(step)
        start = pl.multiple_of(chip_at(chip, flip) * span, span)
        return pltpu.make_async_copy(queries.at[step], q_out.at[member, pl.ds(start, span)], q_sem.at[step])

    def tok_copy(member):
        return pltpu.make_async_copy(tok_ref.at[0, member], tok_buf.at[member], tok_sem.at[member])

    def kv_copies(member):
        return (
            pltpu.make_async_copy(keys.at[member], k_out.at[member], k_sem.at[member]),
            pltpu.make_async_copy(values.at[member], v_out.at[member], v_sem.at[member]),
        )

    def core_copies(step):
        return (
            remote(part.at[step, 1 - core], got.at[step], core_send.at[step], core_recv.at[step], mate),
            remote(part_s.at[step, 1 - core], got_s.at[step], core_send_s.at[step], core_recv_s.at[step], mate),
        )

    def chip_copies(step):
        member, flip = unpack(step)
        peer = 2 * chip_at(chip, flip) + core
        place = 3 * member + flip - 1
        return (
            remote(stage.at[step], arrive.at[place], chip_send.at[place], chip_recv.at[place], peer),
            remote(stage_s.at[step], arrive_s.at[place], chip_send_s.at[place], chip_recv_s.at[place], peer),
        )

    tok_copy(0).start()
    masks = mask_loads(seg_ref, mask_ref, seg_buf, mask_buf, mask_sem)
    for copy in masks:
        copy.start()
    for step in range(4):
        lat_copy(step).start()
    tok_copy(1).start()
    for step in range(4, 2 * 4):
        lat_copy(step).start()
    greet([mate] + [2 * other + core for other in others])
    for copy in masks:
        copy.wait()
    mask_rows(seg_buf, mask_buf, count_ref, bias)

    def project(member):
        tok_copy(member).wait()
        hat, inverse = norm_parts(tok_buf[member].astype(F32))
        normed = (hat * tgain_ref[...]).astype(BF16)
        keys[member] = nn(normed, kw_ref[...]).astype(BF16)
        values[member] = nn(normed, vw_ref[...]).astype(BF16)
        for copy in kv_copies(member):
            copy.start()

    def ask(step):
        hat, inverse = norm_parts(lat_buf[step])
        normed = (hat * qgain_ref[...]).astype(BF16)
        queries[step] = (nn(normed, qw_ref[...]) * (D ** (-0.5) * LOG2E)).astype(BF16)

    def compute(step, ahead):
        member, flip = unpack(step)

        @pl.when(flip == 3)
        def _():
            project(member)

        if ahead:
            lat_copy(step + 1).wait()
        scores = nt(queries[step], keys[member])
        if ahead:
            ask(step + 1)
        raised = []
        for half in range(2):
            seen = bias[member, pl.ds(2 * chip_at(chip, flip) + half, 1), :]
            own = scores[half * ROWS:(half + 1) * ROWS] + seen
            top = jnp.max(own, axis=1, keepdims=True)
            own = jnp.exp2(own - top)
            part_s[step, half] = to_rows(top, jnp.sum(own, axis=1, keepdims=True))
            raised.append(own.astype(BF16))
        sums = nn(jnp.concatenate(raised, axis=0), values[member]).astype(BF16)
        for half in range(2):
            part[step, half] = sums[half * ROWS:(half + 1) * ROWS]
        for copy in core_copies(step):
            copy.start()
        if ahead:
            q_copy(step + 1).start()

    def merge(one, one_s, two, two_s):
        top = jnp.maximum(one_s[0:1], two_s[0:1])
        one_w, two_w = jnp.exp2(one_s[0:1] - top), jnp.exp2(two_s[0:1] - top)
        sums = one_s[1:2] * one_w + two_s[1:2] * two_w
        spare = jnp.zeros((6, ROWS), F32)
        weights = jnp.concatenate([one_w, two_w, spare], axis=0).T
        return one * weights[:, 0:1] + two * weights[:, 1:2], jnp.concatenate([top, sums, spare], axis=0)

    def combine(step):
        member, flip = unpack(step)
        for copy in core_copies(step):
            copy.wait_recv()
        added, figures = merge(
            part[step, core].astype(F32), part_s[step, core], got[step].astype(F32), got_s[step]
        )
        stage_s[step] = figures

        @pl.when(flip > 0)
        def _():
            stage[step] = added.astype(BF16)
            for copy in chip_copies(step):
                copy.start()

        @pl.when(flip == 0)
        def _():
            total[member] = added

    def finish(member):
        added, figures = total[member], stage_s[4 * member + 3]
        for flip in (1, 2, 3):
            for copy in chip_copies(4 * member + 3 - flip):
                copy.wait_recv()
            place = 3 * member + flip - 1
            added, figures = merge(added, figures, arrive[place].astype(F32), arrive_s[place])
        spare = jnp.zeros((7, ROWS), F32)
        inverse = jnp.concatenate([1.0 / figures[1:2], spare], axis=0).T
        att_ref[member] = added * inverse[:, 0:1]
        lse_ref[member] = jnp.concatenate([figures[0:1] + jnp.log2(figures[1:2]), spare], axis=0)

    def step_body(step, carry):
        compute(step, True)

        @pl.when(step > 0)
        def _():
            combine(step - 1)

        return carry

    last = jnp.int32(4 * MB - 1)
    lat_copy(jnp.int32(0)).wait()
    ask(0)
    q_copy(jnp.int32(0)).start()
    lax.fori_loop(0, 4 * MB - 1, step_body, 0)
    compute(last, False)
    combine(last - 1)
    combine(last)
    for member in range(MB):
        finish(member)
    for member in range(MB):
        for copy in kv_copies(member):
            copy.wait()
        for slot in range(4):
            step = 4 * member + slot
            q_copy(step).wait()
            for copy in core_copies(step):
                copy.wait_send()
            if slot < 3:
                for copy in chip_copies(step):
                    copy.wait_send()


def cross_forward(collective_id, *args):
    dma = pltpu.SemaphoreType.DMA
    span = 2 * ROWS
    steps = 4 * MB
    vmem = pl.BlockSpec(memory_space=pltpu.VMEM)
    hbm = pl.BlockSpec(memory_space=pl.ANY)
    return pl.pallas_call(
        cross_forward_kernel,
        in_specs=[hbm, hbm] + [vmem] * 5 + [hbm, hbm, pl.BlockSpec(memory_space=pltpu.SMEM)],
        out_specs=[hbm, hbm, hbm, vmem, vmem],
        out_shape=[
            jax.ShapeDtypeStruct((MB, TOK_DEV, D), BF16),
            jax.ShapeDtypeStruct((MB, TOK_DEV, D), BF16),
            jax.ShapeDtypeStruct((MB, L, D), BF16),
            jax.ShapeDtypeStruct((MB, ROWS, D), F32),
            jax.ShapeDtypeStruct((MB, 8, ROWS), F32),
        ],
        scratch_shapes=[
            pltpu.VMEM((MB, TOK_DEV, D), BF16),
            pltpu.VMEM((steps, span, D), F32),
            pltpu.VMEM((MB, TOK_DEV, D), BF16),
            pltpu.VMEM((MB, TOK_DEV, D), BF16),
            pltpu.VMEM((steps, span, D), BF16),
            pltpu.VMEM((MB, LGROUPS, TOK_DEV), F32),
            pltpu.VMEM((steps, 2, ROWS, D), BF16),
            pltpu.VMEM((steps, 2, 8, ROWS), F32),
            pltpu.VMEM((steps, ROWS, D), BF16),
            pltpu.VMEM((steps, 8, ROWS), F32),
            pltpu.VMEM((steps, ROWS, D), BF16),
            pltpu.VMEM((steps, 8, ROWS), F32),
            pltpu.VMEM((3 * MB, ROWS, D), BF16),
            pltpu.VMEM((3 * MB, 8, ROWS), F32),
            pltpu.VMEM((MB, ROWS, D), F32),
            pltpu.VMEM((MB, TOK_DEV), jnp.int32),
            pltpu.VMEM((MB, SCENES, LGROUPS), jnp.int32),
            dma((2,)), dma((MB,)), dma((steps,)), dma((MB,)), dma((MB,)), dma((steps,)),
        ] + [dma((steps,))] * 4 + [dma((3 * MB,))] * 4,
        compiler_params=pltpu.CompilerParams(
            collective_id=collective_id, has_side_effects=True, vmem_limit_bytes=56 * MIB
        ),
        cost_estimate=pl.CostEstimate(
            flops=14 * 10**9, bytes_accessed=22 * 10**6, transcendentals=4 * 10**6
        ),
        name="cross_forward",
    )(*args)


def cross_backward_kernel(
    items, grad_items,
    tok_ref, tgain_ref, kw_ref, vw_ref, seg_ref, mask_ref, count_ref, k_ref, v_ref, q_ref, up_ref, fig_ref,
    lat_ref, lup_ref, qgain_ref, qw_ref, fgain_ref, mgain_ref, sgain_ref, *refs,
):
    count, more = len(items), len(grad_items)
    parts, sources = refs[:count], refs[count:count + more]
    refs = refs[count + more:]
    dlat_ref, dtok_ref, dkw_ref, dvw_ref, dqw_ref, gains_ref = refs[:6]
    sums, helds = refs[6:6 + count], refs[6 + count:6 + count + more]
    rest = refs[6 + count + more:]
    cut = CROSS_SCRATCH + 3 * count + 2
    grp, grp_devices = grp_steps(items, parts, (), rest[CROSS_SCRATCH:cut], sums)
    tok, near_devices = tok_steps(grad_items, sources, rest[cut:])
    (tok_buf, keys, values, queries, ups, figs, bias, part, got, stage, arrive, far_in, total, dk, dv, dkw, dvw,
     dgain_ref, lat, lup, seg_buf, mask_buf, mask_sem, tail_sem,
     tok_sem, k_sem, v_sem, q_sem, out_sem, near_send, near_recv, far_send, far_recv, on_send, on_recv, own_sem,
     fig_send, fig_recv, core_send, core_recv, chip_send, chip_recv, half_send, half_recv) = rest[:CROSS_SCRATCH]
    me, core, chip, mate, others = places()
    span = 2 * ROWS

    def slot_of(step):
        late = lax.div(step + 3, 8)
        member = jnp.where(step == 1, 1, late)
        flip = jnp.where(step < 2, 0, jnp.where(late == 0, step - 1, 8 - step))
        return member, flip

    def loads(step):
        member, flip = slot_of(step)
        start = pl.multiple_of(chip_at(chip, flip) * span, span)
        ring = lax.rem(step, 4)
        return pltpu.make_async_copy(q_ref.at[member, pl.ds(start, span)], queries.at[ring], q_sem.at[ring])

    def tok_copies(member):
        return (
            pltpu.make_async_copy(k_ref.at[member], keys.at[member], k_sem.at[member]),
            pltpu.make_async_copy(v_ref.at[member], values.at[member], v_sem.at[member]),
            pltpu.make_async_copy(tok_ref.at[0, member], tok_buf.at[member], tok_sem.at[member]),
        )

    def out_copy(member):
        return pltpu.make_async_copy(dk.at[member], dtok_ref.at[0, member], out_sem.at[member])

    def own_copies(member):
        slot = 4 * member
        return (
            pltpu.make_async_copy(up_ref.at[member], ups.at[slot, core], own_sem.at[member, 0]),
            pltpu.make_async_copy(fig_ref.at[member], figs.at[slot, core], own_sem.at[member, 1]),
        )

    def near_copies(member):
        slot = 4 * member
        return [
            remote(up_ref.at[member], ups.at[slot, core], near_send.at[member, 0], near_recv.at[member, 0], mate),
            remote(fig_ref.at[member], figs.at[slot, core], near_send.at[member, 1], near_recv.at[member, 1], mate),
        ]

    half_rows = (pl.ds(0, ROWS // 2), pl.ds(ROWS // 2, ROWS // 2))

    def far_copies(slot):
        member, flip = slot // 4, slot % 4
        peer = 2 * chip_at(chip, flip) + core
        if flip < 3:
            return [
                remote(up_ref.at[member], ups.at[slot, core], far_send.at[slot, 0], far_recv.at[slot, 0], peer),
                remote(fig_ref.at[member], figs.at[slot, core], far_send.at[slot, 1], far_recv.at[slot, 1], peer),
            ]
        copies = []
        for half, (held, toward) in enumerate(((1, 2), (2, 1))):
            copies.append(remote(
                ups.at[4 * member + held, core, half_rows[half]], ups.at[slot, core, half_rows[half]],
                far_send.at[slot, half], far_recv.at[slot, half], 2 * chip_at(chip, toward) + core,
            ))
        copies.append(remote(
            figs.at[4 * member + 1, core], figs.at[slot, core], fig_send.at[member], fig_recv.at[member],
            2 * chip_at(chip, 2) + core,
        ))
        return copies

    def on_copies(slot):
        return (
            remote(ups.at[slot, core], ups.at[slot, core], on_send.at[slot, 0], on_recv.at[slot, 0], mate),
            remote(figs.at[slot, core], figs.at[slot, core], on_send.at[slot, 1], on_recv.at[slot, 1], mate),
        )

    def pass_on(slot):
        for copy in far_copies(slot):
            copy.wait_recv()
        for copy in on_copies(slot):
            copy.start()

    def pass_near(member):
        pass_on(4 * member + 1)
        pass_on(4 * member + 2)
        for copy in far_copies(4 * member + 3):
            copy.start()

    def half_copy(member, half):
        return remote(
            stage.at[4 * member + 3, half_rows[half]], far_in.at[member, half], half_send.at[member, half],
            half_recv.at[member, half], 2 * chip_at(chip, half + 1) + core,
        )

    def half_copies(member):
        return [half_copy(member, half) for half in range(2)]

    def core_copy(step):
        member, flip = slot_of(step)
        slot, ring = 4 * member + flip, lax.rem(step, 4)
        return remote(part.at[ring, 1 - core], got.at[slot], core_send.at[slot], core_recv.at[slot], mate)

    def chip_copy(slot):
        member, flip = slot // 4, slot % 4
        peer = 2 * chip_at(chip, flip) + core
        place = 2 * member + flip - 1
        return remote(stage.at[slot], arrive.at[place], chip_send.at[place], chip_recv.at[place], peer)

    def relay(member):
        for half in range(2):
            half_copy(member, half).wait_recv()
            slot = 4 * member + 2 - half
            joined = stage.at[slot, half_rows[half]]
            add(joined, joined, far_in.at[member, half])
            chip_copy(slot).start()

    masks = mask_loads(seg_ref, mask_ref, seg_buf, mask_buf, mask_sem)
    for copy in masks:
        copy.start()
    own_rows = pl.ds(pl.multiple_of(me * ROWS, ROWS), ROWS)
    tails = (
        pltpu.make_async_copy(lat_ref.at[0, :, own_rows], lat, tail_sem.at[0]),
        pltpu.make_async_copy(lup_ref, lup, tail_sem.at[1]),
    )
    for copy in own_copies(0):
        copy.start()
    for copy in tok_copies(0):
        copy.start()
    for step in range(3):
        loads(jnp.int32(step)).start()
    for copy in own_copies(1):
        copy.start()
    for copy in tok_copies(1):
        copy.start()
    for copy in tails:
        copy.start()
    greet_all([mate] + [2 * other + core for other in others], grp_devices)
    for member in range(MB):
        for copy in near_copies(member):
            copy.start()
    for flip in (1, 2):
        for copy in far_copies(flip):
            copy.start()
    for item in range(more):
        tok[0](item)
    for item in range(count):
        grp[0](item)
    for copy in masks:
        copy.wait()
    mask_rows(seg_buf, mask_buf, count_ref, bias)

    def compute(step):
        member, flip = slot_of(step)
        slot = 4 * member + flip

        @pl.when(step < 2)
        def _():
            for copy in tok_copies(member):
                copy.wait()
            dk[member] = jnp.zeros((TOK_DEV, D), F32)
            dv[member] = jnp.zeros((TOK_DEV, D), F32)

        loads(step).wait()

        @pl.when(step + 3 < 4 * MB)
        def _():
            loads(step + 3).start()

        @pl.when(flip == 0)
        def _():
            for copy in own_copies(member):
                copy.wait()
            for copy in near_copies(member):
                copy.wait_recv()

        @pl.when(flip > 0)
        def _():
            for copy in on_copies(slot):
                copy.wait_recv()

        asked = queries[lax.rem(step, 4)]
        upstream = ups[slot].reshape(span, D)
        scores = nt(asked, keys[member])
        soft = nt(upstream, values[member])
        weights, grads = [], []
        for half in range(2):
            seen = bias[member, pl.ds(2 * chip_at(chip, flip) + half, 1), :]
            figures = figs[slot, half].T
            rows = slice(half * ROWS, (half + 1) * ROWS)
            weight = jnp.exp2(scores[rows] + seen - figures[:, 0:1])
            grads.append((weight * (soft[rows] - figures[:, 1:2])).astype(BF16))
            weights.append(weight.astype(BF16))
        weight = jnp.concatenate(weights, axis=0)
        grad = jnp.concatenate(grads, axis=0)
        dv[member] += tn(weight, upstream)
        dk[member] += tn(grad, asked)
        asked_grad = (nn(grad, keys[member]) * D ** (-0.5)).astype(BF16)

        @pl.when(step >= 4)
        def _():
            core_copy(step - 4).wait_send()

        for half in range(2):
            part[lax.rem(step, 4), half] = asked_grad[half * ROWS:(half + 1) * ROWS]
        core_copy(step).start()

    def combine(step):
        member, flip = slot_of(step)
        slot = 4 * member + flip
        core_copy(step).wait_recv()
        added = part[lax.rem(step, 4), core].astype(F32) + got[slot].astype(F32)

        @pl.when(flip > 0)
        def _():
            stage[slot] = added.astype(BF16)

        @pl.when(flip == 0)
        def _():
            total[member] = added

    def tokens_back(member, half):
        gain = tgain_ref[...]
        rows = pl.ds(pl.multiple_of(half * span, span), span)
        hat, inverse = norm_parts(tok_buf[member, rows].astype(F32))
        normed = (hat * gain).astype(BF16)
        key_grad = (dk[member, rows] * LN2).astype(BF16)
        value_grad = dv[member, rows].astype(BF16)
        dkw[...] += tn(normed, key_grad)
        dvw[...] += tn(normed, value_grad)
        normed_grad = nt(key_grad, kw_ref[...]) + nt(value_grad, vw_ref[...])
        source_grad, gain_rows = norm_pull(hat, inverse, gain, normed_grad)
        dk[member, rows] = source_grad
        dgain_ref[...] += jnp.sum(gain_rows, axis=0, keepdims=True)

    def hold(item):
        helds[item][...] = tok[4](item).astype(helds[item].dtype)

    def step_body(step, carry):
        compute(step)

        @pl.when(step > 0)
        def _():
            combine(step - 1)

        @pl.when(step == 0)
        def _():
            for flip in (1, 2):
                for copy in far_copies(4 + flip):
                    copy.start()
            tok[1](0)

        @pl.when(step == 1)
        def _():
            pass_near(0)

        @pl.when(step == 2)
        def _():
            tok[1](1)

        @pl.when(step == 3)
        def _():
            pass_on(3)
            pass_near(1)

        @pl.when(step == 4)
        def _():
            pass_on(7)
            for item in range(count):
                grp[4](item)
            tok[1](2)

        @pl.when(step == 5)
        def _():
            for copy in half_copies(0):
                copy.start()
            tok[2](0)

        @pl.when(step == 6)
        def _():
            for copy in half_copies(1):
                copy.start()
            relay(0)

        @pl.when(step == 4 * MB - 1)
        def _():
            tok[3](0)
            tok[2](1)

        return carry

    lax.fori_loop(0, 4 * MB, step_body, 0)

    def tokens_body(member, carry):
        @pl.when(member == 1)
        def _():
            hold(0)
            tok[2](2)

        for half in range(TOK_DEV // span):
            tokens_back(member, half)
        out_copy(member).start()

        @pl.when(member == 0)
        def _():
            combine(4 * MB - 1)
            relay(1)

        return carry

    dkw[...] = jnp.zeros_like(dkw)
    dvw[...] = jnp.zeros_like(dvw)
    dgain_ref[...] = jnp.zeros_like(dgain_ref)
    lax.fori_loop(0, MB, tokens_body, 0)
    dkw_ref[...] = dkw[...].astype(BF16)
    dvw_ref[...] = dvw[...].astype(BF16)
    tok[3](1)
    tok[3](2)
    for copy in tails:
        copy.wait()
    gain = qgain_ref[...]
    hat, inverse = norm_parts(lat[...].reshape(MB * ROWS, D))
    normed = (hat * gain).astype(BF16)
    asked_grads = []
    for member in range(MB):
        added = total[member]
        for flip in (1, 2):
            chip_copy(4 * member + flip).wait_recv()
            added = added + arrive[2 * member + flip - 1].astype(F32)
        asked_grads.append(added.astype(BF16))
    asked_grad = jnp.concatenate(asked_grads, axis=0)
    dqw_ref[...] = tn(normed, asked_grad).astype(BF16)
    source_grad, gain_rows = norm_pull(hat, inverse, gain, nt(asked_grad, qw_ref[...]))
    lup[...] += source_grad
    last = pltpu.make_async_copy(lup, dlat_ref, tail_sem.at[2])
    last.start()
    query_gain = jnp.sum(gain_rows, axis=0, keepdims=True)
    rows = jnp.concatenate(
        [dgain_ref[...], query_gain, fgain_ref[...], mgain_ref[...], sgain_ref[...], jnp.zeros((3, D), F32)], axis=0
    )
    gains_ref[...] = jnp.zeros_like(gains_ref)
    width = D // TOK
    for device in range(TOK):
        gains_ref[16 * device:16 * device + 8, 0:width] = rows[:, device * width:(device + 1) * width]
    grp[3]((0,))
    hold(1)
    hold(2)
    tok[5]()
    last.wait()
    for step in range(4, 4 * MB):
        core_copy(jnp.int32(step)).wait_send()
    for member in range(MB):
        out_copy(member).wait()
        for copy in near_copies(member) + half_copies(member):
            copy.wait_send()
        for flip in range(4):
            slot = 4 * member + flip
            if flip > 0:
                for copy in far_copies(slot):
                    copy.wait_send()
                for copy in on_copies(slot):
                    copy.wait_send()
            if flip in (1, 2):
                chip_copy(slot).wait_send()


CROSS_SCRATCH = 44


def cross_backward(collective_id, arrays, grads, *args):
    dma = pltpu.SemaphoreType.DMA
    span = 2 * ROWS
    steps = 4 * MB
    vmem = pl.BlockSpec(memory_space=pltpu.VMEM)
    hbm = pl.BlockSpec(memory_space=pl.ANY)
    smem = pl.BlockSpec(memory_space=pltpu.SMEM)
    items, kinds = held_plan(arrays)
    sources, grad_items, grad_kinds, shapes = reduce_plan(grads)
    scratch = [
        pltpu.VMEM((MB, TOK_DEV, D), BF16),
        pltpu.VMEM((MB, TOK_DEV, D), BF16),
        pltpu.VMEM((MB, TOK_DEV, D), BF16),
        pltpu.VMEM((4, span, D), BF16),
        pltpu.VMEM((steps, 2, ROWS, D), BF16),
        pltpu.VMEM((steps, 2, 8, ROWS), F32),
        pltpu.VMEM((MB, LGROUPS, TOK_DEV), F32),
        pltpu.VMEM((4, 2, ROWS, D), BF16),
        pltpu.VMEM((steps, ROWS, D), BF16),
        pltpu.VMEM((steps, ROWS, D), BF16),
        pltpu.VMEM((2 * MB, ROWS, D), BF16),
        pltpu.VMEM((MB, 2, ROWS // 2, D), BF16),
        pltpu.VMEM((MB, ROWS, D), F32),
        pltpu.VMEM((MB, TOK_DEV, D), F32),
        pltpu.VMEM((MB, TOK_DEV, D), F32),
        pltpu.VMEM((D, D), F32),
        pltpu.VMEM((D, D), F32),
        pltpu.VMEM((1, D), F32),
        pltpu.VMEM((MB, ROWS, D), F32),
        pltpu.VMEM((MB * ROWS, D), F32),
        pltpu.VMEM((MB, TOK_DEV), jnp.int32),
        pltpu.VMEM((MB, SCENES, LGROUPS), jnp.int32),
        dma((2,)), dma((3,)),
        dma((MB,)), dma((MB,)), dma((MB,)), dma((4,)), dma((MB,)),
        dma((MB, 2)), dma((MB, 2)), dma((steps, 2)), dma((steps, 2)), dma((steps, 2)), dma((steps, 2)), dma((MB, 2)),
        dma((MB,)), dma((MB,)),
        dma((steps,)), dma((steps,)), dma((2 * MB,)), dma((2 * MB,)), dma((MB, 2)), dma((MB, 2)),
    ]
    return pl.pallas_call(
        functools.partial(cross_backward_kernel, items, grad_items),
        in_specs=[hbm] + [vmem] * 3 + [hbm, hbm, smem] + [hbm] * 7 + [vmem] * 5 + [vmem] * len(arrays) + [hbm] * len(grads),
        out_specs=[hbm, hbm] + [vmem] * (4 + len(arrays) + len(grads)),
        out_shape=[
            jax.ShapeDtypeStruct((MB * ROWS, D), F32),
            jax.ShapeDtypeStruct((1, MB, TOK_DEV, D), F32),
            jax.ShapeDtypeStruct((D, D), BF16),
            jax.ShapeDtypeStruct((D, D), BF16),
            jax.ShapeDtypeStruct((D, D), BF16),
            jax.ShapeDtypeStruct((16 * TOK, 128), F32),
        ] + [jax.ShapeDtypeStruct(array.shape, array.dtype) for array in arrays]
        + [jax.ShapeDtypeStruct((high // 2, wide), kind) for (high, wide), kind in zip(shapes, grad_kinds)],
        scratch_shapes=scratch + grp_scratch(items, kinds) + tok_scratch(grad_items, grad_kinds),
        compiler_params=pltpu.CompilerParams(
            collective_id=collective_id, has_side_effects=True, vmem_limit_bytes=60 * MIB
        ),
        cost_estimate=pl.CostEstimate(
            flops=26 * 10**9, bytes_accessed=24 * 10**6, transcendentals=4 * 10**6
        ),
        name="cross_backward",
    )(*args, *arrays, *sources)


GELU_A = 0.7978845608028654
GELU_B = 0.044715


def gelu_parts(hidden):
    square = hidden * hidden
    bent = jnp.tanh(GELU_A * hidden * (1.0 + GELU_B * square))
    half = 0.5 * (1.0 + bent)
    slope = half + 0.5 * hidden * (1.0 - bent * bent) * (GELU_A * (1.0 + 3.0 * GELU_B * square))
    return hidden * half, slope


def greet_all(tok_devices, grp_devices=()):
    barrier = pltpu.get_barrier_semaphore()
    for axis, devices in (("tok", tok_devices), ("grp", grp_devices)):
        for device in devices:
            pl.semaphore_signal(
                barrier, inc=1, device_id={axis: device}, device_id_type=pl.DeviceIdType.MESH
            )
    pl.semaphore_wait(barrier, len(tok_devices) + len(grp_devices))


def all_peers():
    me, core, chip, mate, others = places()
    peers = []
    for other in others:
        peers += [2 * other + core, 2 * other + 1 - core]
    return me, peers + [mate]


def head_copies(row_side, head_side, to_heads, member, me, peers, send, recv, local):
    lanes = pl.ds(member * ROWS, ROWS)
    row_at = lambda device: row_side.at[:, device, :, lanes]
    head_at = lambda device: head_side.at[:, member, :, pl.ds(pl.multiple_of(device * ROWS, ROWS), ROWS)]
    source, target = (row_at, head_at) if to_heads else (head_at, row_at)
    copies = [
        remote(source(peer), target(me), send.at[slot, member], recv.at[slot, member], peer)
        for slot, peer in enumerate(peers)
    ]
    return copies, pltpu.make_async_copy(source(me), target(me), local.at[member])


QB = 1024
QB_BACK = 256


def latents_forward_kernel(
    lat_ref, att_ref, cot_ref, ow_ref, fgain_ref, fup_ref, fdown_ref, mgain_ref, proj_ref, mow_ref, sgain_ref,
    sup_ref, sdown_ref,
    out_ref, fmid_ref, mmid_ref, packed_ref, exact_ref, lse_ref, up_ref, mgrad_ref, ddown_ref, dup_ref, dmo_ref,
    dgain_ref,
    lat, att, cot, ow, fup, fdown, proj, mow, sup, sdown,
    out, fmid, mmid, heads, exact, up, mgrad, ddown, dup, dmo,
    rows_out, keys, values, mixed, mixed_rows,
    load_sem, store_sem, send_a, recv_a, local_a, send_b, recv_b, local_b,
):
    me, peers = all_peers()
    own = pl.ds(pl.multiple_of(me * ROWS, ROWS), ROWS)
    names = ("lat", "att", "ow", "fup", "fdown", "proj", "mow", "sup", "sdown", "cot")
    loads = {}
    for i, (source, target) in enumerate((
        (lat_ref.at[0, :, own], lat), (att_ref, att), (ow_ref, ow), (fup_ref, fup), (fdown_ref, fdown),
        (proj_ref, proj), (mow_ref, mow), (sup_ref, sup), (sdown_ref, sdown), (cot_ref.at[0], cot),
    )):
        loads[names[i]] = pltpu.make_async_copy(source, target, load_sem.at[i])
        loads[names[i]].start()
    stores = []

    def store(source, target):
        stores.append(pltpu.make_async_copy(source, target, store_sem.at[len(stores)]))
        stores[-1].start()

    greet_all(peers)
    flat = (MB * ROWS, D)
    for name in ("lat", "att", "ow"):
        loads[name].wait()
    first = lat[...].reshape(flat) + nn(att[...].reshape(flat).astype(BF16), ow[...])
    fmid[...] = first
    store(fmid, fmid_ref)
    normed = (norm_parts(first)[0] * fgain_ref[...]).astype(BF16)
    loads["fup"].wait()
    loads["fdown"].wait()
    mid = first
    for part in range(2):
        cut = slice(part * FF // 2, (part + 1) * FF // 2)
        mid = mid + nn(jax.nn.gelu(nn(normed, fup[:, cut])).astype(BF16), fdown[cut])
    mmid[...] = mid
    store(mmid, mmid_ref)
    normed = (norm_parts(mid)[0] * mgain_ref[...]).astype(BF16).T
    loads["proj"].wait()
    for kind, scale in enumerate((HD ** (-0.5) * LOG2E, 1.0, 1.0)):
        packed = tn(proj[:, kind * D:(kind + 1) * D], normed) * scale
        rows_out[kind] = packed.astype(BF16).reshape(H, HD, MB * ROWS)
    outward = [head_copies(rows_out, heads, True, member, me, peers, send_a, recv_a, local_a) for member in range(MB)]
    backward = [
        head_copies(mixed_rows, mixed, False, member, me, peers, send_b, recv_b, local_b) for member in range(MB)
    ]
    for copies, here in outward:
        for copy in copies:
            copy.start()
        here.start()
    for member in range(MB):
        copies, here = outward[member]
        for copy in copies:
            copy.wait_recv()
        here.wait()
        store(heads.at[:, member], packed_ref.at[:, member])
        keys[...] = heads[1, member].T
        values[0:HD] = heads[2, member]
        values[HD:] = jnp.ones((16, L), BF16)

        def attend(step, carry, member=member):
            at = pl.ds(pl.multiple_of(step * QB, QB), QB)
            logits = nn(keys[...], heads[0, member, :, at])
            top = jnp.max(logits, axis=0, keepdims=True)
            both = nn(values[...], jnp.exp2(logits - top).astype(BF16))
            total = both[HD:HD + 1]
            result = both[0:HD] / total
            exact[member, :, at] = result
            mixed[0, member, :, at] = result.astype(BF16)
            lse_ref[member, :, at] = jnp.broadcast_to(top + jnp.log2(total), (8, QB))
            return carry

        lax.fori_loop(0, L // QB, attend, 0)
        for copy in backward[member][0] + [backward[member][1]]:
            copy.start()
    store(exact, exact_ref)
    loads["mow"].wait()
    loads["sup"].wait()
    loads["sdown"].wait()
    loads["cot"].wait()
    for copies, here in backward:
        for copy in copies:
            copy.wait_recv()
        here.wait()
    mixed_t = mixed_rows[0].reshape(D, MB * ROWS)
    second = mmid[...] + tn(mixed_t, mow[...])
    hat, inverse = norm_parts(second)
    normed = (hat * sgain_ref[...]).astype(BF16)
    upstream = cot[...].reshape(flat)
    grad = upstream.astype(BF16)
    final = second
    normed_grad = jnp.zeros(flat, F32)
    for part in range(2):
        cut = slice(part * FF // 2, (part + 1) * FF // 2)
        act, slope = gelu_parts(nn(normed, sup[:, cut]))
        act = act.astype(BF16)
        final = final + nn(act, sdown[cut])
        hidden_grad = (slope * nt(grad, sdown[cut])).astype(BF16)
        normed_grad = normed_grad + nt(hidden_grad, sup[:, cut])
        ddown[cut] = tn(act, grad).astype(BF16)
        dup[:, cut] = tn(normed, hidden_grad).astype(BF16)
    store(ddown, ddown_ref)
    store(dup, dup_ref)
    out[...] = final.reshape(MB, ROWS, D)
    store(out, out_ref.at[0])
    residual, gain_rows = norm_pull(hat, inverse, sgain_ref[...], normed_grad)
    dgain_ref[...] = jnp.sum(gain_rows, axis=0, keepdims=True)
    upstream = upstream + residual
    up[...] = upstream
    store(up, up_ref)
    grad = upstream.astype(BF16)
    mgrad[0] = nt(mow[...], grad).astype(BF16).reshape(H, HD, MB * ROWS)
    store(mgrad, mgrad_ref)
    dmo[...] = nn(mixed_t, grad).astype(BF16)
    store(dmo, dmo_ref)
    for copy in stores:
        copy.wait()
    for copies, here in outward + backward:
        for copy in copies:
            copy.wait_send()


def latents_forward(collective_id, *args):
    dma = pltpu.SemaphoreType.DMA
    vmem = pl.BlockSpec(memory_space=pltpu.VMEM)
    hbm = pl.BlockSpec(memory_space=pl.ANY)
    rows = MB * ROWS
    stored = [
        ((1, MB, ROWS, D), F32), ((rows, D), F32), ((rows, D), F32), ((3, MB, HD, L), BF16), ((MB, HD, L), F32),
        ((MB, 8, L), F32), ((rows, D), F32), ((1, H, HD, rows), BF16), ((FF, D), BF16), ((D, FF), BF16), ((D, D), BF16),
        ((1, D), F32),
    ]
    return pl.pallas_call(
        latents_forward_kernel,
        in_specs=[hbm, hbm, hbm, hbm, vmem, hbm, hbm, vmem, hbm, hbm, vmem, hbm, hbm],
        out_specs=[hbm] * 5 + [vmem] + [hbm] * 5 + [vmem],
        out_shape=[jax.ShapeDtypeStruct(shape, kind) for shape, kind in stored],
        scratch_shapes=[
            pltpu.VMEM((MB, ROWS, D), F32), pltpu.VMEM((MB, ROWS, D), F32), pltpu.VMEM((MB, ROWS, D), F32),
            pltpu.VMEM((D, D), BF16), pltpu.VMEM((D, FF), BF16), pltpu.VMEM((FF, D), BF16),
            pltpu.VMEM((D, 3 * D), BF16), pltpu.VMEM((D, D), BF16), pltpu.VMEM((D, FF), BF16),
            pltpu.VMEM((FF, D), BF16),
            pltpu.VMEM((MB, ROWS, D), F32), pltpu.VMEM((rows, D), F32), pltpu.VMEM((rows, D), F32),
            pltpu.VMEM((3, MB, HD, L), BF16), pltpu.VMEM((MB, HD, L), F32), pltpu.VMEM((rows, D), F32),
            pltpu.VMEM((1, H, HD, rows), BF16), pltpu.VMEM((FF, D), BF16), pltpu.VMEM((D, FF), BF16),
            pltpu.VMEM((D, D), BF16),
            pltpu.VMEM((3, H, HD, rows), BF16), pltpu.VMEM((L, HD), BF16), pltpu.VMEM((HD + 16, L), BF16),
            pltpu.VMEM((1, MB, HD, L), BF16), pltpu.VMEM((1, H, HD, rows), BF16),
            dma((10,)), dma((11,)), dma((7, MB)), dma((7, MB)), dma((MB,)), dma((7, MB)), dma((7, MB)), dma((MB,)),
        ],
        compiler_params=pltpu.CompilerParams(
            collective_id=collective_id, has_side_effects=True, vmem_limit_bytes=60 * MIB
        ),
        cost_estimate=pl.CostEstimate(
            flops=20 * 10**9, bytes_accessed=30 * 10**6, transcendentals=10 * 10**6
        ),
        name="latents_forward",
    )(*args)


def levels():
    level = lax.axis_index("grp")
    odd = lax.rem(level, 2)
    return odd, level + 1 - 2 * odd, lax.rem(level + 2, 4)


def half_slices(rows, odd):
    half = rows // 2
    keep = pl.ds(pl.multiple_of(odd * half, half), half)
    away = pl.ds(pl.multiple_of((1 - odd) * half, half), half)
    return keep, away


def tok_steps(items, sources, scratch):
    n = len(items)
    mine, got, near_in, first_in, second_in = [scratch[i * n:(i + 1) * n] for i in range(5)]
    (local_sem, core_send, core_recv, near_send, near_recv, one_send, one_recv, two_send, two_recv) = scratch[5 * n:]
    me, core, chip, mate, (far, flip_x, flip_y) = places()
    x, y = lax.rem(chip, 2), lax.div(chip, 2)
    odd, level_near, level_far = levels()

    def core_copies(i):
        source, rows, row_at, columns, column_at, x_first = items[i]
        part = (pl.ds(row_at, rows), pl.ds(column_at, columns))
        return (
            remote(sources[source].at[:, :, 1 - core, *part], got[i], core_send.at[i], core_recv.at[i], mate),
            pltpu.make_async_copy(sources[source].at[:, :, core, *part], mine[i], local_sem.at[i]),
        )

    def near_copy(i):
        keep, away = half_slices(items[i][1], odd)
        return pltpu.make_async_remote_copy(
            src_ref=mine[i].at[:, :, away], dst_ref=near_in[i], send_sem=near_send.at[i], recv_sem=near_recv.at[i],
            device_id={"grp": level_near}, device_id_type=pl.DeviceIdType.MESH,
        )

    def first_copy(i):
        keep, away = half_slices(items[i][1], odd)
        x_first = items[i][-1]
        source = mine[i].at[:, 1 - x, keep] if x_first else mine[i].at[1 - y, :, keep]
        peer = 2 * (flip_x if x_first else flip_y) + core
        return remote(source, first_in[i], one_send.at[i], one_recv.at[i], peer)

    def second_copy(i):
        keep, away = half_slices(items[i][1], odd)
        x_first = items[i][-1]
        source = mine[i].at[1 - y, x, keep] if x_first else mine[i].at[y, 1 - x, keep]
        peer = 2 * (flip_y if x_first else flip_x) + core
        return remote(source, second_in[i], two_send.at[i], two_recv.at[i], peer)

    def core_sends(i):
        for copy in core_copies(i):
            copy.start()

    def core_sums(i):
        there, here = core_copies(i)
        there.wait_recv()
        here.wait()
        add(mine[i], mine[i], got[i])
        near_copy(i).start()

    def near_sums(i):
        keep, away = half_slices(items[i][1], odd)
        near_copy(i).wait_recv()
        held = mine[i].at[:, :, keep]
        add(held, held, near_in[i])
        first_copy(i).start()

    def first_sums(i):
        keep, away = half_slices(items[i][1], odd)
        first_copy(i).wait_recv()
        held = mine[i].at[:, x, keep] if items[i][-1] else mine[i].at[y, :, keep]
        add(held, held, first_in[i])
        second_copy(i).start()

    def second_sums(i):
        keep, away = half_slices(items[i][1], odd)
        second_copy(i).wait_recv()
        return mine[i][y, x, keep].astype(F32) + second_in[i][...].astype(F32)

    def finish():
        for i in range(n):
            core_copies(i)[0].wait_send()
            for copy in (near_copy(i), first_copy(i), second_copy(i)):
                copy.wait_send()

    return (core_sends, core_sums, near_sums, first_sums, second_sums, finish), (
        mate, 2 * flip_x + core, 2 * flip_y + core)


def plain_steps(items, sources, scratch):
    n = len(items)
    mine, got, near_in, first_in, second_in = [scratch[i * n:(i + 1) * n] for i in range(5)]
    (local_sem, core_send, core_recv, near_send, near_recv, one_send, one_recv, two_send, two_recv) = scratch[5 * n:]
    me, core, chip, mate, (far, flip_x, flip_y) = places()
    x, y = lax.rem(chip, 2), lax.div(chip, 2)
    odd, level_near, level_far = levels()

    def core_copy(i):
        return remote(sources[i].at[:, :, 1 - core], got[i], core_send.at[i], core_recv.at[i], mate)

    def local_copy(i):
        return pltpu.make_async_copy(sources[i].at[:, :, core], mine[i], local_sem.at[i])

    def first_copy(i):
        x_first = items[i][-1]
        source = mine[i].at[:, 1 - x] if x_first else mine[i].at[1 - y]
        peer = 2 * (flip_x if x_first else flip_y) + core
        return remote(source, first_in[i], one_send.at[i], one_recv.at[i], peer)

    def second_copy(i):
        x_first = items[i][-1]
        source = mine[i].at[1 - y, x] if x_first else mine[i].at[y, 1 - x]
        peer = 2 * (flip_y if x_first else flip_x) + core
        return remote(source, second_in[i], two_send.at[i], two_recv.at[i], peer)

    def near_copy(i):
        keep, away = half_slices(items[i][1], odd)
        return pltpu.make_async_remote_copy(
            src_ref=mine[i].at[y, x, away], dst_ref=near_in[i], send_sem=near_send.at[i], recv_sem=near_recv.at[i],
            device_id={"grp": level_near}, device_id_type=pl.DeviceIdType.MESH,
        )

    def core_sends(i):
        core_copy(i).start()
        local_copy(i).start()

    def core_sums(i):
        core_copy(i).wait_recv()
        local_copy(i).wait()
        add(mine[i], mine[i], got[i])
        first_copy(i).start()

    def first_sums(i):
        first_copy(i).wait_recv()
        held = mine[i].at[:, x] if items[i][-1] else mine[i].at[y]
        add(held, held, first_in[i])
        second_copy(i).start()

    def second_sums(i):
        second_copy(i).wait_recv()
        held = mine[i].at[y, x]
        add(held, held, second_in[i])
        near_copy(i).start()

    def near_sums(i):
        keep, away = half_slices(items[i][1], odd)
        near_copy(i).wait_recv()
        return mine[i][y, x, keep].astype(F32) + near_in[i][...].astype(F32)

    def finish():
        for i in range(n):
            for copy in (core_copy(i), near_copy(i), first_copy(i), second_copy(i)):
                copy.wait_send()

    return (core_sends, core_sums, first_sums, second_sums, near_sums, finish), (
        mate, 2 * flip_x + core, 2 * flip_y + core)


def grp_steps(items, held, outs, scratch, joined=None):
    n = len(items)
    far_in, own_joined, near_in = [scratch[i * n:(i + 1) * n] for i in range(3)]
    z_send, z_recv = scratch[3 * n:]
    joined = own_joined if joined is None else joined
    odd, level_near, level_far = levels()

    def along(i, step):
        source, target, other = (
            (held[i], far_in[i], level_far),
            (joined[i], near_in[i], level_near),
        )[step]
        return pltpu.make_async_remote_copy(
            src_ref=source, dst_ref=target, send_sem=z_send.at[i, step], recv_sem=z_recv.at[i, step],
            device_id={"grp": other}, device_id_type=pl.DeviceIdType.MESH,
        )

    def store(i, odd_half, value):
        source, rows, row_at, columns, column_at, x_first = items[i]
        half = rows // 2
        start = pl.multiple_of(row_at + odd_half * half, half)
        outs[source][pl.ds(start, half), pl.ds(column_at, columns)] = value.astype(F32)

    def far_start(i):
        along(i, 0).start()

    def far_join(i):
        along(i, 0).wait_recv()
        add(joined[i], held[i], far_in[i])

    def near_start(i):
        along(i, 1).start()
        store(i, odd, joined[i][...])

    def far_sum(i):
        far_join(i)
        near_start(i)

    def near_store(i):
        along(i, 1).wait_recv()
        store(i, 1 - odd, near_in[i][...])

    def finish(steps=(0, 1)):
        for i in range(n):
            for step in steps:
                along(i, step).wait_send()

    return (far_start, far_sum, near_store, finish, far_join, near_start), (level_near, level_far)


def add(target, one, two):
    target[...] = (one[...].astype(F32) + two[...].astype(F32)).astype(target.dtype)


def reduce_kernel(items, whole, joined, count, *refs):
    n, m, k = len(items), len(whole), len(joined)
    sources, held, done = refs[:count], refs[count:count + m], refs[count + m:count + m + k]
    refs = refs[count + m + k:]
    outs, whole_outs, joined_outs = refs[:count], refs[count:count + m], refs[count + m:count + m + k]
    scratch = refs[count + m + k:]
    cut = 5 * n + 9
    own_held = scratch[cut:cut + n]
    tok, near_devices = plain_steps(items, sources, scratch[:cut])
    cut += n
    late, grp_devices = grp_steps(items, own_held, outs, scratch[cut:cut + 3 * n + 2])
    cut += 3 * n + 2
    early, unused = grp_steps(whole, held, whole_outs, scratch[cut:cut + 3 * m + 2])
    cut += 3 * m + 2
    first, unused = grp_steps(joined, done, joined_outs, scratch[cut:], done)
    greet_all(near_devices, grp_devices)
    for i in range(n):
        tok[0](i)
    for i in range(m):
        early[0](i)
    for i in range(n):
        tok[1](i)
    for i in range(k):
        first[5](i)
    for i in range(n):
        tok[2](i)
    early[1](0)
    for i in range(n):
        tok[3](i)
    for i in range(n):
        own_held[i][...] = tok[4](i).astype(own_held[i].dtype)
        late[0](i)
    for i in range(1, m):
        early[1](i)
        early[2](i - 1)
    for i in range(k):
        first[2](i)
    for i in range(n):
        late[1](i)
    early[2](m - 1)
    for i in range(n):
        late[2](i)
    tok[-1]()
    late[3]()
    early[3]()
    first[3]((1,))


def reduce_plan(arrays):
    sources, items = [], []
    for source, array in enumerate(arrays):
        rows, columns = array.shape[0] // TOK, array.shape[1]
        sources.append(array.reshape(2, 2, 2, rows, columns))
        items.append((source, rows, 0, columns, 0, source % 2 == 0))
    kinds = [array.dtype for array in arrays]
    shapes = [(array.shape[0] // TOK, array.shape[1]) for array in arrays]
    return sources, tuple(items), kinds, shapes


def held_plan(arrays):
    items = tuple((i, 2 * array.shape[0], 0, array.shape[1], 0, True) for i, array in enumerate(arrays))
    return items, [array.dtype for array in arrays]


def item_blocks(items, kinds, lead, part):
    return [pltpu.VMEM(lead + (item[1] // part, item[3]), kind) for item, kind in zip(items, kinds)]


def plain_scratch(items, kinds):
    blocks = functools.partial(item_blocks, items, kinds)
    return (blocks((2, 2), 1) + blocks((2, 2), 1) + blocks((), 2) + blocks((2,), 1) + blocks((), 1)
            + [pltpu.SemaphoreType.DMA((len(items),))] * 9)


def tok_scratch(items, kinds):
    blocks = functools.partial(item_blocks, items, kinds)
    return (blocks((2, 2), 1) + blocks((2, 2), 1) + blocks((2, 2), 2) + blocks((2,), 2) + blocks((), 2)
            + [pltpu.SemaphoreType.DMA((len(items),))] * 9)


def grp_scratch(items, kinds):
    blocks = functools.partial(item_blocks, items, kinds)
    return blocks((), 2) * 3 + [pltpu.SemaphoreType.DMA((len(items), 2))] * 2


def reduce_grads(collective_id, arrays, held, done):
    sources, items, kinds, shapes = reduce_plan(arrays)
    whole, whole_kinds = held_plan(held)
    joined, joined_kinds = held_plan(done)
    vmem = pl.BlockSpec(memory_space=pltpu.VMEM)
    hbm = pl.BlockSpec(memory_space=pl.ANY)
    return pl.pallas_call(
        functools.partial(reduce_kernel, items, whole, joined, len(arrays)),
        in_specs=[hbm] * len(arrays) + [vmem] * (len(held) + len(done)),
        out_specs=[vmem] * (len(arrays) + len(held) + len(done)),
        out_shape=[jax.ShapeDtypeStruct(shape, F32) for shape in shapes]
        + [jax.ShapeDtypeStruct((item[1], item[3]), F32) for item in whole + joined],
        scratch_shapes=plain_scratch(items, kinds) + item_blocks(items, kinds, (), 2) + grp_scratch(items, kinds)
        + grp_scratch(whole, whole_kinds) + grp_scratch(joined, joined_kinds),
        compiler_params=pltpu.CompilerParams(
            collective_id=collective_id, has_side_effects=True, vmem_limit_bytes=56 * MIB
        ),
        name="reduce_grads",
    )(*sources, *held, *done)


def write_kernel(count, *refs):
    sources, gain_ref, outs = refs[:count], refs[count], refs[count + 1:2 * count + 1]
    gain_outs, buffers = refs[2 * count + 1:-count - 2], refs[-count - 2:-2]
    in_sem, out_sem = refs[-2:]
    ins = [pltpu.make_async_copy(sources[i], buffers[i], in_sem.at[i]) for i in range(count)]
    backs = [pltpu.make_async_copy(buffers[i], outs[i], out_sem.at[i]) for i in range(count)]
    for copy in ins:
        copy.start()
    for i, out in enumerate(gain_outs):
        out[...] = gain_ref[i:i + 1, 0:D // TOK]
    for i in range(count):
        ins[i].wait()
        backs[i].start()
    for copy in backs:
        copy.wait()


def write_results(results, gains, gain_count):
    n = len(results)
    hbm, vmem = pl.BlockSpec(memory_space=pl.ANY), pl.BlockSpec(memory_space=pltpu.VMEM)
    return pl.pallas_call(
        functools.partial(write_kernel, n),
        in_specs=[hbm] * n + [vmem],
        out_specs=[hbm] * n + [vmem] * gain_count,
        out_shape=[jax.ShapeDtypeStruct(result.shape, result.dtype) for result in results]
        + [jax.ShapeDtypeStruct((1, D // TOK), F32)] * gain_count,
        scratch_shapes=[pltpu.VMEM(result.shape, result.dtype) for result in results]
        + [pltpu.SemaphoreType.DMA((n,)), pltpu.SemaphoreType.DMA((n,))],
        compiler_params=pltpu.CompilerParams(vmem_limit_bytes=60 * MIB),
        name="write_results",
    )(*results, gains)


def latents_backward_kernel(items, *refs):
    (mgrad_ref, packed_ref, exact_ref, lse_ref, up_ref, mmid_ref, fmid_ref, att_ref, clse_ref, ow_ref, fgain_ref,
     fup_ref, fdown_ref, mgain_ref, proj_ref) = refs[:15]
    count = max(item[0] for item in items) + 1
    sources = refs[15:15 + count]
    (agrad_ref, fig_ref, lup_ref, dup_ref, ddown_ref, dproj_ref, dout_ref, dmgain_ref, dfgain_ref) = refs[
        15 + count:24 + count]
    reduced = refs[24 + count:24 + 2 * count]
    rest = refs[24 + 2 * count:]
    (heads, exact, ups, mmid, fmid, att, ow, fup, fdown, proj, keys, values, upstream_heads, key_acc, value_acc,
     grads, back, agrad, lup, dup, ddown, dproj, dout, hidden,
     load_sem, store_sem, send_a, recv_a, local_a, send_b, recv_b, local_b) = rest[:32]
    me, peers = all_peers()
    reducer, near_devices = tok_steps(items, sources, rest[32:])
    core_sends, core_sums, near_sums, first_sums, second_sums, finish = reducer
    odd, level_near, level_far = levels()

    def hold(item):
        reduced[item][...] = second_sums(item).astype(reduced[item].dtype)

    names = ("heads", "exact", "fmid", "fup", "up", "mmid", "proj", "fdown", "att", "ow")
    loads = {}
    for i, (source, target) in enumerate((
        (packed_ref, heads), (exact_ref, exact), (fmid_ref, fmid), (fup_ref, fup), (up_ref, ups), (mmid_ref, mmid),
        (proj_ref, proj), (fdown_ref, fdown), (att_ref, att), (ow_ref, ow),
    )):
        loads[names[i]] = pltpu.make_async_copy(source, target, load_sem.at[i])
        loads[names[i]].start()
    stores = []

    def store(source, target):
        stores.append(pltpu.make_async_copy(source, target, store_sem.at[len(stores)]))
        stores[-1].start()

    greet_all(peers, (level_near,))
    outward = [
        head_copies(mgrad_ref, upstream_heads, True, member, me, peers, send_a, recv_a, local_a) for member in range(MB)
    ]
    backward = [head_copies(back, grads, False, member, me, peers, send_b, recv_b, local_b) for member in range(MB)]
    for copies, here in outward:
        for copy in copies:
            copy.start()
        here.start()
    for item in range(3):
        core_sends(item)
    loads["fmid"].wait()
    loads["fup"].wait()
    first_hat, first_inverse = norm_parts(fmid[...])
    first_normed = (first_hat * fgain_ref[...]).astype(BF16)
    hidden[...] = nn(first_normed, fup[...])
    core_sums(0)
    loads["heads"].wait()
    loads["exact"].wait()
    for member in range(MB):
        keys[...] = heads[1, member].T
        values[...] = heads[2, member].T
        key_acc[...] = jnp.zeros_like(key_acc)
        value_acc[...] = jnp.zeros_like(value_acc)
        copies, here = outward[member]
        for copy in copies:
            copy.wait_recv()
        here.wait()

        def attend_back(step, carry, member=member):
            at = pl.ds(pl.multiple_of(step * QB_BACK, QB_BACK), QB_BACK)
            queries = heads[0, member, :, at]
            upstream = upstream_heads[0, member, :, at]
            inner = jnp.sum(upstream.astype(F32) * exact[member, :, at], axis=0, keepdims=True)
            softened = jnp.exp2(nn(keys[...], queries) - lse_ref[member, 0:1, at])
            logit_grad = (softened * (nn(values[...], upstream) - inner)).astype(BF16)
            value_acc[...] += nt(upstream, softened.astype(BF16))
            key_acc[...] += nt(queries, logit_grad)
            grads[0, member, :, at] = (nn(heads[1, member], logit_grad) * HD ** (-0.5)).astype(BF16)
            return carry

        steps = L // QB_BACK
        lax.fori_loop(0, steps, attend_back, 0)
        grads[1, member] = (key_acc[...] * LN2).astype(BF16)
        grads[2, member] = value_acc[...].astype(BF16)
        for copy in backward[member][0] + [backward[member][1]]:
            copy.start()
        if member == 0:
            near_sums(0)
            core_sums(1)
            core_sums(2)
        else:
            first_sums(0)
            near_sums(1)
            near_sums(2)
    loads["up"].wait()
    loads["mmid"].wait()
    loads["proj"].wait()
    loads["fdown"].wait()
    mixer_hat, mixer_inverse = norm_parts(mmid[...])
    mixer_normed = (mixer_hat * mgain_ref[...]).astype(BF16).T
    for copies, here in backward:
        for copy in copies:
            copy.wait_recv()
        here.wait()
    hold(0)
    first_sums(1)
    first_sums(2)
    packed_grad = back[...].reshape(3 * D, MB * ROWS)
    normed_grad = nn(proj[...], packed_grad).T
    residual, gain_rows = norm_pull(mixer_hat, mixer_inverse, mgain_ref[...], normed_grad)
    dmgain_ref[...] = jnp.sum(gain_rows, axis=0, keepdims=True)
    upstream = ups[...] + residual
    dproj[...] = nt(mixer_normed, packed_grad).astype(BF16)
    store(dproj, dproj_ref)
    grad = upstream.astype(BF16)
    normed_grad = jnp.zeros((MB * ROWS, D), F32)
    for part in range(2):
        cut = slice(part * FF // 2, (part + 1) * FF // 2)
        act, slope = gelu_parts(hidden[:, cut])
        hidden_grad = (slope * nt(grad, fdown[cut])).astype(BF16)
        normed_grad = normed_grad + nt(hidden_grad, fup[:, cut])
        ddown[cut] = tn(act.astype(BF16), grad).astype(BF16)
        dup[:, cut] = tn(first_normed, hidden_grad).astype(BF16)
    store(ddown, ddown_ref)
    store(dup, dup_ref)
    residual, gain_rows = norm_pull(first_hat, first_inverse, fgain_ref[...], normed_grad)
    dfgain_ref[...] = jnp.sum(gain_rows, axis=0, keepdims=True)
    upstream = upstream + residual
    lup[...] = upstream
    store(lup, lup_ref)
    grad = upstream.astype(BF16)
    loads["att"].wait()
    loads["ow"].wait()
    attended = att[...].reshape(MB * ROWS, D)
    attended_grad = nt(grad, ow[...]).astype(BF16)
    agrad[...] = attended_grad.reshape(MB, ROWS, D)
    store(agrad, agrad_ref)
    inner = jnp.sum(attended_grad.astype(F32) * attended, axis=1, keepdims=True)
    for member in range(MB):
        rows = slice(member * ROWS, (member + 1) * ROWS)
        spare = jnp.zeros((6, ROWS), F32)
        fig_ref[member] = jnp.concatenate(
            [clse_ref[member, 0:1], to_rows(inner[rows], inner[rows])[0:1], spare], axis=0
        )
    dout[...] = tn(attended.astype(BF16), grad).astype(BF16)
    store(dout, dout_ref)
    hold(1)
    hold(2)
    finish()
    for copy in stores:
        copy.wait()
    for copies, here in outward + backward:
        for copy in copies:
            copy.wait_send()


def latents_backward(collective_id, arrays, *args):
    dma = pltpu.SemaphoreType.DMA
    vmem = pl.BlockSpec(memory_space=pltpu.VMEM)
    hbm = pl.BlockSpec(memory_space=pl.ANY)
    rows = MB * ROWS
    sources, items, kinds, shapes = reduce_plan(arrays)
    reduced = [jax.ShapeDtypeStruct((rows_ // 2, columns), kind) for (rows_, columns), kind in zip(shapes, kinds)]
    stored = [
        ((MB, ROWS, D), BF16), ((MB, 8, ROWS), F32), ((rows, D), F32), ((D, FF), BF16), ((FF, D), BF16),
        ((D, 3 * D), BF16), ((D, D), BF16), ((1, D), F32), ((1, D), F32),
    ]
    return pl.pallas_call(
        functools.partial(latents_backward_kernel, items),
        in_specs=[hbm, hbm, hbm, vmem, hbm, hbm, hbm, hbm, vmem, hbm, vmem, hbm, hbm, vmem, hbm] + [hbm] * len(arrays),
        out_specs=[hbm, vmem] + [hbm] * 5 + [vmem] * (2 + len(arrays)),
        out_shape=[jax.ShapeDtypeStruct(shape, kind) for shape, kind in stored] + reduced,
        scratch_shapes=[
            pltpu.VMEM((3, MB, HD, L), BF16), pltpu.VMEM((MB, HD, L), F32), pltpu.VMEM((rows, D), F32),
            pltpu.VMEM((rows, D), F32), pltpu.VMEM((rows, D), F32), pltpu.VMEM((MB, ROWS, D), F32),
            pltpu.VMEM((D, D), BF16), pltpu.VMEM((D, FF), BF16), pltpu.VMEM((FF, D), BF16),
            pltpu.VMEM((D, 3 * D), BF16), pltpu.VMEM((L, HD), BF16), pltpu.VMEM((L, HD), BF16),
            pltpu.VMEM((1, MB, HD, L), BF16), pltpu.VMEM((HD, L), F32), pltpu.VMEM((HD, L), F32),
            pltpu.VMEM((3, MB, HD, L), BF16), pltpu.VMEM((3, H, HD, rows), BF16),
            pltpu.VMEM((MB, ROWS, D), BF16), pltpu.VMEM((rows, D), F32), pltpu.VMEM((D, FF), BF16),
            pltpu.VMEM((FF, D), BF16), pltpu.VMEM((D, 3 * D), BF16), pltpu.VMEM((D, D), BF16),
            pltpu.VMEM((rows, FF), F32),
            dma((10,)), dma((6,)), dma((7, MB)), dma((7, MB)), dma((MB,)), dma((7, MB)), dma((7, MB)), dma((MB,)),
        ] + tok_scratch(items, kinds),
        compiler_params=pltpu.CompilerParams(
            collective_id=collective_id, has_side_effects=True, vmem_limit_bytes=61 * MIB
        ),
        cost_estimate=pl.CostEstimate(
            flops=35 * 10**9, bytes_accessed=36 * 10**6, transcendentals=10 * 10**6
        ),
        name="latents_backward",
    )(*args, *sources)


def fast_body(
    tokens,
    latents,
    segments,
    scene_mask,
    counts,
    token_gain,
    query_gain,
    query_weight,
    key_weight,
    value_weight,
    output_weight,
    first_gain,
    first_up,
    first_down,
    mixer_gain,
    mixer_project,
    mixer_output,
    second_gain,
    second_up,
    second_down,
    cotangent,
):
    scenes = (segments, scene_mask, counts)
    keys, values, queries, attended, lse = cross_forward(
        0, tokens, latents, token_gain[None], query_gain[None], query_weight, key_weight, value_weight, *scenes
    )
    (latents_out, first_mid, mixer_mid, packed, exact, head_lse, upstream, mixed_grad, d_second_down, d_second_up,
     d_mixer_output, d_second_gain) = latents_forward(
        1, latents, attended, cotangent, output_weight, first_gain[None], first_up, first_down, mixer_gain[None],
        mixer_project, mixer_output, second_gain[None], second_up, second_down,
    )
    (attended_grad, figures, upstream, d_first_up, d_first_down, d_project, d_output, d_mixer_gain, d_first_gain,
     *early) = latents_backward(
        2, [d_second_up, d_second_down, d_mixer_output], mixed_grad, packed, exact, head_lse, upstream, mixer_mid,
        first_mid, attended, lse, output_weight, first_gain[None], first_up, first_down, mixer_gain[None], mixer_project,
    )
    latents_grad, tokens_grad, d_key, d_value, d_query, gains, *rest = cross_backward(
        5, early, [d_first_up, d_first_down, d_project], tokens, token_gain[None], key_weight, value_weight,
        *scenes, keys, values, queries, attended_grad, figures, latents, upstream, query_gain[None], query_weight,
        d_first_gain, d_mixer_gain, d_second_gain,
    )
    early, held = rest[:len(early)], rest[len(early):]
    o_output, o_key, o_value, o_query, gains, *late = reduce_grads(
        7, [d_output, d_key, d_value, d_query, gains], held, early
    )
    late, early = late[:len(held)], late[len(held):]
    (latents_out, latents_grad, tokens_grad, o_second_up, o_second_down, o_mixer_output, o_first_up, o_first_down,
     o_project, o_output, o_key, o_value, o_query, *o_gains) = write_results(
        [latents_out, latents_grad.reshape(latents_out.shape), tokens_grad, *early, *late, o_output, o_key, o_value, o_query], gains, 5
    )
    o_gains = [gain.reshape(D // TOK) for gain in o_gains]
    return (
        latents_out,
        latents_grad,
        tokens_grad,
        o_gains[0],
        o_gains[1],
        o_query,
        o_key,
        o_value,
        o_output,
        o_gains[2],
        o_first_up,
        o_first_down,
        o_gains[3],
        o_project,
        o_mixer_output,
        o_gains[4],
        o_second_up,
        o_second_down,
    )


IN_SPECS = (
    P("grp", None, "tok", None),
    P("grp", None, None, None),
    P("grp", None, "tok"),
    P("grp", None, None, None),
    P("grp", None, "tok"),
    P(),
    P(),
    P(),
    P(),
    P(),
    P(),
    P(),
    P(),
    P(),
    P(),
    P(),
    P(),
    P(),
    P(),
    P(),
    P("grp", None, "tok", None),
)
OUT_SPECS = (
    P("grp", None, "tok", None),
    P("grp", None, "tok", None),
    P("grp", None, "tok", None),
    P("tok"),
    P("tok"),
    P("tok", None),
    P("tok", None),
    P("tok", None),
    P("tok", None),
    P("tok"),
    P("tok", None),
    P("tok", None),
    P("tok"),
    P("tok", None),
    P("tok", None),
    P("tok"),
    P("tok", None),
    P("tok", None),
)


def solution(mesh):
    return jax.shard_map(
        fast_body if mesh.shape["tok"] == TOK else general_body,
        mesh=mesh,
        in_specs=IN_SPECS,
        out_specs=OUT_SPECS,
        check_vma=False,
    )
```

```python
import functools

import jax
import jax.numpy as jnp
from jax import lax
from jax.experimental import pallas as pl
from jax.experimental.pallas import tpu as pltpu
from jax.sharding import PartitionSpec as P

D = 512
L = 2048
H = 8
HD = 64
TOK_DEV = 1024
MB = 2
SCENES = 8
LGROUPS = 8


EPS = 1e-05
NEG = -1e30


def norm_rows(values, gain):
    centre = values - jnp.mean(values, axis=-1, keepdims=True)
    spread = jnp.mean(centre * centre, axis=-1, keepdims=True)
    return centre * lax.rsqrt(spread + EPS) * gain


def norm_back(values, gain, upstream):
    unused, pull = jax.vjp(norm_rows, values, gain)
    return pull(upstream)


def gelu_back(hidden, upstream):
    unused, pull = jax.vjp(jax.nn.gelu, hidden)
    return pull(upstream)[0]


def product_plain(left, right):
    return jnp.dot(left, right, preferred_element_type=jnp.float32)


def product_rows(left, right):
    return lax.dot_general(
        left, right, (((0,), (0,)), ((), ())), preferred_element_type=jnp.float32
    )


def product_cols(left, right):
    return lax.dot_general(
        left, right, (((1,), (1,)), ((), ())), preferred_element_type=jnp.float32
    )


def add_term(store, name, value):
    if name in store:
        store[name] = store[name] + value
    else:
        store[name] = value


def project_tokens(tokens, member, token_gain, key_weight, value_weight):
    source = tokens[0, member].astype(jnp.float32)
    normed = norm_rows(source, token_gain).astype(jnp.bfloat16)
    key_rows = product_plain(normed, key_weight).astype(jnp.bfloat16)
    value_rows = product_plain(normed, value_weight).astype(jnp.bfloat16)
    return (source, normed, key_rows, value_rows)


def mlp_forward(residual, gain, up_weight, down_weight):
    normed = norm_rows(residual, gain).astype(jnp.bfloat16)
    hidden = product_plain(normed, up_weight)
    active = jax.nn.gelu(hidden).astype(jnp.bfloat16)
    return (residual + product_plain(active, down_weight), (normed, hidden, active))


def mlp_backward(residual, gain, up_weight, down_weight, saved, upstream):
    normed, hidden, active = saved
    grad_low = upstream.astype(jnp.bfloat16)
    grad_down = product_rows(active, grad_low)
    hidden_grad = gelu_back(hidden, product_cols(grad_low, down_weight)).astype(jnp.bfloat16)
    grad_up = product_rows(normed, hidden_grad)
    residual_grad, grad_gain = norm_back(residual, gain, product_cols(hidden_grad, up_weight))
    return (upstream + residual_grad, grad_gain, grad_up, grad_down)


def mixer_forward(residual, gain, project, output):
    own_rows = residual.shape[0]
    normed = norm_rows(residual, gain).astype(jnp.bfloat16)
    packed = product_plain(normed, project).astype(jnp.bfloat16)
    pair_rows = lax.all_gather(packed[:, D:], "tok", axis=0, tiled=True)
    every = pair_rows.shape[0]
    own_queries = packed[:, :D].reshape(own_rows, H, HD)
    keys = pair_rows[:, :D].reshape(every, H, HD)
    values = pair_rows[:, D:].reshape(every, H, HD)
    logits = jnp.einsum(
        "qhd,khd->hqk", own_queries, keys, preferred_element_type=jnp.float32
    ) * HD ** (-0.5)
    peak_row = jnp.max(logits, axis=-1, keepdims=True)
    raised = jnp.exp(logits - peak_row)
    softened = raised / jnp.sum(raised, axis=-1, keepdims=True)
    softened_low = softened.astype(jnp.bfloat16)
    mixed_rows = jnp.einsum(
        "hqk,khd->qhd", softened_low, values, preferred_element_type=jnp.float32
    )
    mixed_rows = mixed_rows.reshape(own_rows, D).astype(jnp.bfloat16)
    return (
        residual + product_plain(mixed_rows, output),
        (normed, own_queries, keys, values, softened, softened_low, mixed_rows),
    )


def mixer_backward(residual, gain, project, output, saved, upstream):
    normed, own_queries, keys, values, softened, softened_low, mixed_rows = saved
    own_rows = upstream.shape[0]
    every = keys.shape[0]
    grad_low = upstream.astype(jnp.bfloat16)
    grad_output = product_rows(mixed_rows, grad_low)
    mixed_grad = product_cols(grad_low, output).astype(jnp.bfloat16).reshape(own_rows, H, HD)
    value_grad = jnp.einsum(
        "hqk,qhd->khd", softened_low, mixed_grad, preferred_element_type=jnp.float32
    )
    soft_grad = jnp.einsum("qhd,khd->hqk", mixed_grad, values, preferred_element_type=jnp.float32)
    logit_grad = softened * (soft_grad - jnp.sum(soft_grad * softened, axis=-1, keepdims=True))
    logit_grad = logit_grad.astype(jnp.bfloat16)
    query_grad = jnp.einsum(
        "hqk,khd->qhd", logit_grad, keys, preferred_element_type=jnp.float32
    ) * HD ** (-0.5)
    key_grad = jnp.einsum(
        "hqk,qhd->khd", logit_grad, own_queries, preferred_element_type=jnp.float32
    ) * HD ** (-0.5)
    pair_terms = jnp.concatenate([key_grad.reshape(every, D), value_grad.reshape(every, D)], axis=1)
    pair_grad = lax.psum_scatter(
        pair_terms.astype(jnp.bfloat16), "tok", scatter_dimension=0, tiled=True
    ).astype(jnp.float32)
    packed_grad = jnp.concatenate([query_grad.reshape(own_rows, D), pair_grad], axis=1).astype(
        jnp.bfloat16
    )
    grad_project = product_rows(normed, packed_grad)
    residual_grad, grad_gain = norm_back(residual, gain, product_cols(packed_grad, project))
    return (upstream + residual_grad, grad_gain, grad_project, grad_output)


def general_body(
    tokens,
    latents,
    segments,
    scene_mask,
    counts,
    token_gain,
    query_gain,
    query_weight,
    key_weight,
    value_weight,
    output_weight,
    first_gain,
    first_up,
    first_down,
    mixer_gain,
    mixer_project,
    mixer_output,
    second_gain,
    second_up,
    second_down,
    cotangent,
):
    scale = D ** (-0.5)
    shards = lax.axis_size("tok")
    own_rows = L // shards
    row_start = lax.axis_index("tok") * own_rows
    latent_group = jnp.arange(L) // (L // LGROUPS)
    latent_onehot = (latent_group[:, None] == jnp.arange(LGROUPS)[None, :]).astype(jnp.float32)
    token_place = jnp.arange(TOK_DEV)
    records = []
    latent_outs = []
    for member in range(MB):
        record = {}
        source, normed, key_rows, value_rows = project_tokens(
            tokens, member, token_gain, key_weight, value_weight
        )
        record["token_side"] = (source, normed, key_rows, value_rows)
        scene_onehot = (segments[0, member][:, None] == jnp.arange(SCENES)[None, :]).astype(
            jnp.float32
        )
        token_seen = jnp.dot(scene_onehot, scene_mask[0, member].astype(jnp.float32))
        visible = product_cols(latent_onehot, token_seen)
        alive = token_place < counts[0, member, 0]
        allowed = (visible > 0.5) & alive[None, :]
        latent_every = latents[0, member]
        normed_every = norm_rows(latent_every, query_gain).astype(jnp.bfloat16)
        queries = product_plain(normed_every, query_weight).astype(jnp.bfloat16)
        scores = jnp.where(allowed, product_cols(queries, key_rows) * scale, NEG)
        row_top = lax.pmax(jnp.max(scores, axis=1), "tok")
        unnormed = jnp.exp(scores - row_top[:, None])
        row_total, weighted = (
            lax.psum_scatter(
                jnp.sum(unnormed, axis=1).astype(jnp.bfloat16),
                "tok",
                scatter_dimension=0,
                tiled=True,
            ).astype(jnp.float32),
            lax.psum_scatter(
                product_plain(unnormed.astype(jnp.bfloat16), value_rows).astype(jnp.bfloat16),
                "tok",
                scatter_dimension=0,
                tiled=True,
            ).astype(jnp.float32),
        )
        latent_in = lax.dynamic_slice_in_dim(latent_every, row_start, own_rows, 0)
        latent_normed = lax.dynamic_slice_in_dim(normed_every, row_start, own_rows, 0)
        attended = weighted / row_total[:, None]
        attended_low = attended.astype(jnp.bfloat16)
        first_mid = latent_in + product_plain(attended_low, output_weight)
        mixer_mid, first_saved = mlp_forward(first_mid, first_gain, first_up, first_down)
        second_mid, mixer_saved = mixer_forward(mixer_mid, mixer_gain, mixer_project, mixer_output)
        final_rows, second_saved = mlp_forward(second_mid, second_gain, second_up, second_down)
        latent_outs.append(final_rows)
        record["latent_side"] = (
            allowed,
            latent_in,
            latent_normed,
            queries,
            row_top,
            row_total,
            attended,
            attended_low,
            first_mid,
            mixer_mid,
            second_mid,
            first_saved,
            mixer_saved,
            second_saved,
        )
        records.append(record)
    grads = {}
    latent_grads = []
    token_grads = []
    for member in range(MB):
        record = records[member]
        source, normed, key_rows, value_rows = record["token_side"]
        (
            allowed,
            latent_in,
            latent_normed,
            queries,
            row_top,
            row_total,
            attended,
            attended_low,
            first_mid,
            mixer_mid,
            second_mid,
            first_saved,
            mixer_saved,
            second_saved,
        ) = record["latent_side"]
        second_back = mlp_backward(
            second_mid, second_gain, second_up, second_down, second_saved, cotangent[0, member]
        )
        add_term(grads, "second_gain", second_back[1])
        add_term(grads, "second_up", second_back[2])
        add_term(grads, "second_down", second_back[3])
        mixer_back = mixer_backward(
            mixer_mid, mixer_gain, mixer_project, mixer_output, mixer_saved, second_back[0]
        )
        add_term(grads, "mixer_gain", mixer_back[1])
        add_term(grads, "mixer_project", mixer_back[2])
        add_term(grads, "mixer_output", mixer_back[3])
        first_back = mlp_backward(
            first_mid, first_gain, first_up, first_down, first_saved, mixer_back[0]
        )
        add_term(grads, "first_gain", first_back[1])
        add_term(grads, "first_up", first_back[2])
        add_term(grads, "first_down", first_back[3])
        latent_upstream = first_back[0]
        grad_low = latent_upstream.astype(jnp.bfloat16)
        add_term(grads, "output_weight", product_rows(attended_low, grad_low))
        attended_grad = lax.optimization_barrier(
            product_cols(grad_low, output_weight).astype(jnp.bfloat16)
        ).astype(jnp.float32)
        weighted_grad = (attended_grad / row_total[:, None]).astype(jnp.bfloat16)
        total_grad = -jnp.sum(attended_grad * attended, axis=1) / row_total
        weighted_every, total_every = (
            lax.all_gather(
                weighted_grad.astype(jnp.float32).astype(jnp.bfloat16), "tok", axis=0, tiled=True
            ).astype(jnp.float32),
            lax.all_gather(total_grad.astype(jnp.bfloat16), "tok", axis=0, tiled=True).astype(
                total_grad.dtype
            ),
        )
        weighted_every = weighted_every.astype(jnp.bfloat16)
        scores = jnp.where(allowed, product_cols(queries, key_rows) * scale, NEG)
        unnormed = jnp.exp(scores - row_top[:, None])
        unnormed_grad = product_cols(weighted_every, value_rows) + total_every[:, None]
        score_grad = (unnormed * unnormed_grad).astype(jnp.bfloat16)
        value_grad = product_rows(unnormed.astype(jnp.bfloat16), weighted_every).astype(
            jnp.bfloat16
        )
        key_grad = (product_rows(score_grad, queries) * scale).astype(jnp.bfloat16)
        query_grad = lax.psum_scatter(
            (product_plain(score_grad, key_rows) * scale).astype(jnp.bfloat16),
            "tok",
            scatter_dimension=0,
            tiled=True,
        )
        add_term(grads, "key_weight", product_rows(normed, key_grad))
        add_term(grads, "value_weight", product_rows(normed, value_grad))
        normed_grad = product_cols(key_grad, key_weight) + product_cols(value_grad, value_weight)
        source_grad, gain_grad = norm_back(source, token_gain, normed_grad)
        add_term(grads, "token_gain", gain_grad)
        token_grads.append(source_grad)
        add_term(grads, "query_weight", product_rows(latent_normed, query_grad))
        latent_grad, gain_grad = norm_back(
            latent_in, query_gain, product_cols(query_grad, query_weight)
        )
        add_term(grads, "query_gain", gain_grad)
        latent_grads.append(latent_upstream + latent_grad)
    parts = (
        lax.psum_scatter(
            grads["token_gain"].astype(jnp.bfloat16), "tok", scatter_dimension=0, tiled=True
        ).astype(jnp.float32),
        lax.psum_scatter(
            grads["query_gain"].astype(jnp.bfloat16), "tok", scatter_dimension=0, tiled=True
        ).astype(jnp.float32),
        lax.psum_scatter(
            grads["query_weight"].astype(jnp.bfloat16), "tok", scatter_dimension=0, tiled=True
        ).astype(jnp.float32),
        lax.psum_scatter(
            grads["key_weight"].astype(jnp.bfloat16), "tok", scatter_dimension=0, tiled=True
        ).astype(jnp.float32),
        lax.psum_scatter(
            grads["value_weight"].astype(jnp.bfloat16), "tok", scatter_dimension=0, tiled=True
        ).astype(jnp.float32),
        lax.psum_scatter(
            grads["output_weight"].astype(jnp.bfloat16), "tok", scatter_dimension=0, tiled=True
        ).astype(jnp.float32),
        lax.psum_scatter(
            grads["first_gain"].astype(jnp.bfloat16), "tok", scatter_dimension=0, tiled=True
        ).astype(jnp.float32),
        lax.psum_scatter(
            grads["first_up"].astype(jnp.bfloat16), "tok", scatter_dimension=0, tiled=True
        ).astype(jnp.float32),
        lax.psum_scatter(
            grads["first_down"].astype(jnp.bfloat16), "tok", scatter_dimension=0, tiled=True
        ).astype(jnp.float32),
        lax.psum_scatter(
            grads["mixer_gain"].astype(jnp.bfloat16), "tok", scatter_dimension=0, tiled=True
        ).astype(jnp.float32),
        lax.psum_scatter(
            grads["mixer_project"].astype(jnp.bfloat16), "tok", scatter_dimension=0, tiled=True
        ).astype(jnp.float32),
        lax.psum_scatter(
            grads["mixer_output"].astype(jnp.bfloat16), "tok", scatter_dimension=0, tiled=True
        ).astype(jnp.float32),
        lax.psum_scatter(
            grads["second_gain"].astype(jnp.bfloat16), "tok", scatter_dimension=0, tiled=True
        ).astype(jnp.float32),
        lax.psum_scatter(
            grads["second_up"].astype(jnp.bfloat16), "tok", scatter_dimension=0, tiled=True
        ).astype(jnp.float32),
        lax.psum_scatter(
            grads["second_down"].astype(jnp.bfloat16), "tok", scatter_dimension=0, tiled=True
        ).astype(jnp.float32),
    )
    summed = (
        lax.psum(parts[0].astype(jnp.bfloat16), "grp").astype(jnp.float32),
        lax.psum(parts[1].astype(jnp.bfloat16), "grp").astype(jnp.float32),
        lax.psum(parts[2].astype(jnp.bfloat16), "grp").astype(jnp.float32),
        lax.psum(parts[3].astype(jnp.bfloat16), "grp").astype(jnp.float32),
        lax.psum(parts[4].astype(jnp.bfloat16), "grp").astype(jnp.float32),
        lax.psum(parts[5].astype(jnp.bfloat16), "grp").astype(jnp.float32),
        lax.psum(parts[6].astype(jnp.bfloat16), "grp").astype(jnp.float32),
        lax.psum(parts[7].astype(jnp.bfloat16), "grp").astype(jnp.float32),
        lax.psum(parts[8].astype(jnp.bfloat16), "grp").astype(jnp.float32),
        lax.psum(parts[9].astype(jnp.bfloat16), "grp").astype(jnp.float32),
        lax.psum(parts[10].astype(jnp.bfloat16), "grp").astype(jnp.float32),
        lax.psum(parts[11].astype(jnp.bfloat16), "grp").astype(jnp.float32),
        lax.psum(parts[12].astype(jnp.bfloat16), "grp").astype(jnp.float32),
        lax.psum(parts[13].astype(jnp.bfloat16), "grp").astype(jnp.float32),
        lax.psum(parts[14].astype(jnp.bfloat16), "grp").astype(jnp.float32),
    )
    return (
        jnp.stack(latent_outs)[None],
        jnp.stack(latent_grads)[None],
        jnp.stack(token_grads)[None],
    ) + tuple(summed)


TOK = 8
ROWS = L // TOK
FF = 2048
GR = L // LGROUPS
LOG2E = 1.4426950408889634
LN2 = 0.6931471805599453
F32 = jnp.float32
BF16 = jnp.bfloat16
MIB = 1024 * 1024


def nn(left, right):
    return lax.dot_general(left, right, (((1,), (0,)), ((), ())), preferred_element_type=F32)


def nt(left, right):
    return lax.dot_general(left, right, (((1,), (1,)), ((), ())), preferred_element_type=F32)


def tn(left, right):
    return lax.dot_general(left, right, (((0,), (0,)), ((), ())), preferred_element_type=F32)


def norm_parts(values):
    centre = values - jnp.mean(values, axis=-1, keepdims=True)
    inverse = lax.rsqrt(jnp.mean(centre * centre, axis=-1, keepdims=True) + EPS)
    return centre * inverse, inverse


def norm_pull(hat, inverse, gain, upstream):
    scaled = upstream * gain
    inner = jnp.mean(scaled * hat, axis=-1, keepdims=True)
    grad = (scaled - jnp.mean(scaled, axis=-1, keepdims=True) - hat * inner) * inverse
    return grad, upstream * hat


def places():
    me = lax.axis_index("tok")
    core = lax.rem(me, 2)
    chip = lax.div(me, 2)
    mate = me + 1 - 2 * core
    flip_x = chip + 1 - 2 * lax.rem(chip, 2)
    flip_y = lax.rem(chip + 2, 4)
    far = 3 - chip
    return me, core, chip, mate, (far, flip_x, flip_y)


def remote(src, dst, send_sem, recv_sem, peer):
    return pltpu.make_async_remote_copy(
        src_ref=src,
        dst_ref=dst,
        send_sem=send_sem,
        recv_sem=recv_sem,
        device_id={"tok": peer},
        device_id_type=pl.DeviceIdType.MESH,
    )


def greet(devices):
    barrier = pltpu.get_barrier_semaphore()
    for device in devices:
        pl.semaphore_signal(
            barrier, inc=1, device_id={"tok": device}, device_id_type=pl.DeviceIdType.MESH
        )
    pl.semaphore_wait(barrier, len(devices))


def chip_at(chip, flip):
    high, low = divmod(flip, 2) if isinstance(flip, int) else (lax.div(flip, 2), lax.rem(flip, 2))
    across = lax.rem(lax.rem(chip, 2) + low, 2)
    along = lax.rem(lax.div(chip, 2) + high, 2)
    return 2 * along + across


def mask_loads(seg_ref, mask_ref, seg_buf, mask_buf, sem):
    return (
        pltpu.make_async_copy(seg_ref.at[0], seg_buf, sem.at[0]),
        pltpu.make_async_copy(mask_ref.at[0], mask_buf, sem.at[1]),
    )


def mask_rows(seg_buf, mask_buf, count_ref, bias_ref):
    for member in range(MB):
        scene = lax.broadcasted_iota(jnp.int32, (SCENES, TOK_DEV), 0)
        place = lax.broadcasted_iota(jnp.int32, (SCENES, TOK_DEV), 1)
        hot = jnp.where((seg_buf[member:member + 1] == scene) & (place < count_ref[0, member, 0]), 1.0, 0.0)
        seen = tn(jnp.where(mask_buf[member] > 0, 1.0, 0.0).astype(BF16), hot.astype(BF16))
        bias_ref[member] = jnp.where(seen > 0.5, 0.0, NEG)


def to_rows(first, second):
    rows = first.shape[0]
    lane = lax.broadcasted_iota(jnp.int32, (rows, 128), 1)
    return jnp.where(lane == 0, first, second).T[0:8]


def cross_forward_kernel(
    tok_ref, lat_ref, tgain_ref, qgain_ref, qw_ref, kw_ref, vw_ref, seg_ref, mask_ref, count_ref,
    k_out, v_out, q_out, att_ref, lse_ref,
    tok_buf, lat_buf, keys, values, queries, bias, part, part_s, got, got_s, stage, stage_s,
    arrive, arrive_s, total, seg_buf, mask_buf,
    mask_sem, tok_sem, lat_sem, k_sem, v_sem, q_sem,
    core_send, core_recv, core_send_s, core_recv_s, chip_send, chip_recv, chip_send_s, chip_recv_s,
):
    me, core, chip, mate, others = places()
    span = 2 * ROWS

    def unpack(step):
        return lax.div(step, 4), 3 - lax.rem(step, 4)

    def lat_copy(step):
        member, flip = unpack(step)
        start = pl.multiple_of(chip_at(chip, flip) * span, span)
        return pltpu.make_async_copy(lat_ref.at[0, member, pl.ds(start, span)], lat_buf.at[step], lat_sem.at[step])

    def q_copy(step):
        member, flip = unpack(step)
        start = pl.multiple_of(chip_at(chip, flip) * span, span)
        return pltpu.make_async_copy(queries.at[step], q_out.at[member, pl.ds(start, span)], q_sem.at[step])

    def tok_copy(member):
        return pltpu.make_async_copy(tok_ref.at[0, member], tok_buf.at[member], tok_sem.at[member])

    def kv_copies(member):
        return (
            pltpu.make_async_copy(keys.at[member], k_out.at[member], k_sem.at[member]),
            pltpu.make_async_copy(values.at[member], v_out.at[member], v_sem.at[member]),
        )

    def core_copies(step):
        return (
            remote(part.at[step, 1 - core], got.at[step], core_send.at[step], core_recv.at[step], mate),
            remote(part_s.at[step, 1 - core], got_s.at[step], core_send_s.at[step], core_recv_s.at[step], mate),
        )

    def chip_copies(step):
        member, flip = unpack(step)
        peer = 2 * chip_at(chip, flip) + core
        place = 3 * member + flip - 1
        return (
            remote(stage.at[step], arrive.at[place], chip_send.at[place], chip_recv.at[place], peer),
            remote(stage_s.at[step], arrive_s.at[place], chip_send_s.at[place], chip_recv_s.at[place], peer),
        )

    tok_copy(0).start()
    masks = mask_loads(seg_ref, mask_ref, seg_buf, mask_buf, mask_sem)
    for copy in masks:
        copy.start()
    for step in range(4):
        lat_copy(step).start()
    tok_copy(1).start()
    for step in range(4, 2 * 4):
        lat_copy(step).start()
    greet([mate] + [2 * other + core for other in others])
    for copy in masks:
        copy.wait()
    mask_rows(seg_buf, mask_buf, count_ref, bias)

    def project(member):
        tok_copy(member).wait()
        hat, inverse = norm_parts(tok_buf[member].astype(F32))
        normed = (hat * tgain_ref[...]).astype(BF16)
        keys[member] = nn(normed, kw_ref[...]).astype(BF16)
        values[member] = nn(normed, vw_ref[...]).astype(BF16)
        for copy in kv_copies(member):
            copy.start()

    def ask(step):
        hat, inverse = norm_parts(lat_buf[step])
        normed = (hat * qgain_ref[...]).astype(BF16)
        queries[step] = (nn(normed, qw_ref[...]) * (D ** (-0.5) * LOG2E)).astype(BF16)

    def compute(step, ahead):
        member, flip = unpack(step)

        @pl.when(flip == 3)
        def _():
            project(member)

        if ahead:
            lat_copy(step + 1).wait()
        scores = nt(queries[step], keys[member])
        if ahead:
            ask(step + 1)
        raised = []
        for half in range(2):
            seen = bias[member, pl.ds(2 * chip_at(chip, flip) + half, 1), :]
            own = scores[half * ROWS:(half + 1) * ROWS] + seen
            top = jnp.max(own, axis=1, keepdims=True)
            own = jnp.exp2(own - top)
            part_s[step, half] = to_rows(top, jnp.sum(own, axis=1, keepdims=True))
            raised.append(own.astype(BF16))
        sums = nn(jnp.concatenate(raised, axis=0), values[member]).astype(BF16)
        for half in range(2):
            part[step, half] = sums[half * ROWS:(half + 1) * ROWS]
        for copy in core_copies(step):
            copy.start()
        if ahead:
            q_copy(step + 1).start()

    def merge(one, one_s, two, two_s):
        top = jnp.maximum(one_s[0:1], two_s[0:1])
        one_w, two_w = jnp.exp2(one_s[0:1] - top), jnp.exp2(two_s[0:1] - top)
        sums = one_s[1:2] * one_w + two_s[1:2] * two_w
        spare = jnp.zeros((6, ROWS), F32)
        weights = jnp.concatenate([one_w, two_w, spare], axis=0).T
        return one * weights[:, 0:1] + two * weights[:, 1:2], jnp.concatenate([top, sums, spare], axis=0)

    def combine(step):
        member, flip = unpack(step)
        for copy in core_copies(step):
            copy.wait_recv()
        added, figures = merge(
            part[step, core].astype(F32), part_s[step, core], got[step].astype(F32), got_s[step]
        )
        stage_s[step] = figures

        @pl.when(flip > 0)
        def _():
            stage[step] = added.astype(BF16)
            for copy in chip_copies(step):
                copy.start()

        @pl.when(flip == 0)
        def _():
            total[member] = added

    def finish(member):
        added, figures = total[member], stage_s[4 * member + 3]
        for flip in (1, 2, 3):
            for copy in chip_copies(4 * member + 3 - flip):
                copy.wait_recv()
            place = 3 * member + flip - 1
            added, figures = merge(added, figures, arrive[place].astype(F32), arrive_s[place])
        spare = jnp.zeros((7, ROWS), F32)
        inverse = jnp.concatenate([1.0 / figures[1:2], spare], axis=0).T
        att_ref[member] = added * inverse[:, 0:1]
        lse_ref[member] = jnp.concatenate([figures[0:1] + jnp.log2(figures[1:2]), spare], axis=0)

    def step_body(step, carry):
        compute(step, True)

        @pl.when(step > 0)
        def _():
            combine(step - 1)

        return carry

    last = jnp.int32(4 * MB - 1)
    lat_copy(jnp.int32(0)).wait()
    ask(0)
    q_copy(jnp.int32(0)).start()
    lax.fori_loop(0, 4 * MB - 1, step_body, 0)
    compute(last, False)
    combine(last - 1)
    combine(last)
    for member in range(MB):
        finish(member)
    for member in range(MB):
        for copy in kv_copies(member):
            copy.wait()
        for slot in range(4):
            step = 4 * member + slot
            q_copy(step).wait()
            for copy in core_copies(step):
                copy.wait_send()
            if slot < 3:
                for copy in chip_copies(step):
                    copy.wait_send()


def cross_forward(collective_id, *args):
    dma = pltpu.SemaphoreType.DMA
    span = 2 * ROWS
    steps = 4 * MB
    vmem = pl.BlockSpec(memory_space=pltpu.VMEM)
    hbm = pl.BlockSpec(memory_space=pl.ANY)
    return pl.pallas_call(
        cross_forward_kernel,
        in_specs=[hbm, hbm] + [vmem] * 5 + [hbm, hbm, pl.BlockSpec(memory_space=pltpu.SMEM)],
        out_specs=[hbm, hbm, hbm, vmem, vmem],
        out_shape=[
            jax.ShapeDtypeStruct((MB, TOK_DEV, D), BF16),
            jax.ShapeDtypeStruct((MB, TOK_DEV, D), BF16),
            jax.ShapeDtypeStruct((MB, L, D), BF16),
            jax.ShapeDtypeStruct((MB, ROWS, D), F32),
            jax.ShapeDtypeStruct((MB, 8, ROWS), F32),
        ],
        scratch_shapes=[
            pltpu.VMEM((MB, TOK_DEV, D), BF16),
            pltpu.VMEM((steps, span, D), F32),
            pltpu.VMEM((MB, TOK_DEV, D), BF16),
            pltpu.VMEM((MB, TOK_DEV, D), BF16),
            pltpu.VMEM((steps, span, D), BF16),
            pltpu.VMEM((MB, LGROUPS, TOK_DEV), F32),
            pltpu.VMEM((steps, 2, ROWS, D), BF16),
            pltpu.VMEM((steps, 2, 8, ROWS), F32),
            pltpu.VMEM((steps, ROWS, D), BF16),
            pltpu.VMEM((steps, 8, ROWS), F32),
            pltpu.VMEM((steps, ROWS, D), BF16),
            pltpu.VMEM((steps, 8, ROWS), F32),
            pltpu.VMEM((3 * MB, ROWS, D), BF16),
            pltpu.VMEM((3 * MB, 8, ROWS), F32),
            pltpu.VMEM((MB, ROWS, D), F32),
            pltpu.VMEM((MB, TOK_DEV), jnp.int32),
            pltpu.VMEM((MB, SCENES, LGROUPS), jnp.int32),
            dma((2,)), dma((MB,)), dma((steps,)), dma((MB,)), dma((MB,)), dma((steps,)),
        ] + [dma((steps,))] * 4 + [dma((3 * MB,))] * 4,
        compiler_params=pltpu.CompilerParams(
            collective_id=collective_id, has_side_effects=True, vmem_limit_bytes=56 * MIB
        ),
        cost_estimate=pl.CostEstimate(
            flops=14 * 10**9, bytes_accessed=22 * 10**6, transcendentals=4 * 10**6
        ),
        name="cross_forward",
    )(*args)


def cross_backward_kernel(
    items, grad_items,
    tok_ref, tgain_ref, kw_ref, vw_ref, seg_ref, mask_ref, count_ref, k_ref, v_ref, q_ref, up_ref, fig_ref,
    lat_ref, lup_ref, qgain_ref, qw_ref, fgain_ref, mgain_ref, sgain_ref, *refs,
):
    count, more = len(items), len(grad_items)
    parts, sources = refs[:count], refs[count:count + more]
    refs = refs[count + more:]
    dlat_ref, dtok_ref, dkw_ref, dvw_ref, dqw_ref, gains_ref = refs[:6]
    sums, helds = refs[6:6 + count], refs[6 + count:6 + count + more]
    rest = refs[6 + count + more:]
    cut = CROSS_SCRATCH + 3 * count + 2
    grp, grp_devices = grp_steps(items, parts, (), rest[CROSS_SCRATCH:cut], sums)
    tok, near_devices = tok_steps(grad_items, sources, rest[cut:])
    (tok_buf, keys, values, queries, ups, figs, bias, part, got, stage, arrive, far_in, total, dk, dv, dkw, dvw,
     dgain_ref, lat, lup, seg_buf, mask_buf, mask_sem, tail_sem,
     tok_sem, k_sem, v_sem, q_sem, out_sem, near_send, near_recv, far_send, far_recv, on_send, on_recv, own_sem,
     fig_send, fig_recv, core_send, core_recv, chip_send, chip_recv, half_send, half_recv) = rest[:CROSS_SCRATCH]
    me, core, chip, mate, others = places()
    span = 2 * ROWS

    def slot_of(step):
        late = lax.div(step + 3, 8)
        member = jnp.where(step == 1, 1, late)
        flip = jnp.where(step < 2, 0, jnp.where(late == 0, step - 1, 8 - step))
        return member, flip

    def loads(step):
        member, flip = slot_of(step)
        start = pl.multiple_of(chip_at(chip, flip) * span, span)
        ring = lax.rem(step, 4)
        return pltpu.make_async_copy(q_ref.at[member, pl.ds(start, span)], queries.at[ring], q_sem.at[ring])

    def tok_copies(member):
        return (
            pltpu.make_async_copy(k_ref.at[member], keys.at[member], k_sem.at[member]),
            pltpu.make_async_copy(v_ref.at[member], values.at[member], v_sem.at[member]),
            pltpu.make_async_copy(tok_ref.at[0, member], tok_buf.at[member], tok_sem.at[member]),
        )

    def out_copy(member):
        return pltpu.make_async_copy(dk.at[member], dtok_ref.at[0, member], out_sem.at[member])

    def own_copies(member):
        slot = 4 * member
        return (
            pltpu.make_async_copy(up_ref.at[member], ups.at[slot, core], own_sem.at[member, 0]),
            pltpu.make_async_copy(fig_ref.at[member], figs.at[slot, core], own_sem.at[member, 1]),
        )

    def near_copies(member):
        slot = 4 * member
        return [
            remote(up_ref.at[member], ups.at[slot, core], near_send.at[member, 0], near_recv.at[member, 0], mate),
            remote(fig_ref.at[member], figs.at[slot, core], near_send.at[member, 1], near_recv.at[member, 1], mate),
        ]

    half_rows = (pl.ds(0, ROWS // 2), pl.ds(ROWS // 2, ROWS // 2))

    def far_copies(slot):
        member, flip = slot // 4, slot % 4
        peer = 2 * chip_at(chip, flip) + core
        if flip < 3:
            return [
                remote(up_ref.at[member], ups.at[slot, core], far_send.at[slot, 0], far_recv.at[slot, 0], peer),
                remote(fig_ref.at[member], figs.at[slot, core], far_send.at[slot, 1], far_recv.at[slot, 1], peer),
            ]
        copies = []
        for half, (held, toward) in enumerate(((1, 2), (2, 1))):
            copies.append(remote(
                ups.at[4 * member + held, core, half_rows[half]], ups.at[slot, core, half_rows[half]],
                far_send.at[slot, half], far_recv.at[slot, half], 2 * chip_at(chip, toward) + core,
            ))
        copies.append(remote(
            figs.at[4 * member + 1, core], figs.at[slot, core], fig_send.at[member], fig_recv.at[member],
            2 * chip_at(chip, 2) + core,
        ))
        return copies

    def on_copies(slot):
        return (
            remote(ups.at[slot, core], ups.at[slot, core], on_send.at[slot, 0], on_recv.at[slot, 0], mate),
            remote(figs.at[slot, core], figs.at[slot, core], on_send.at[slot, 1], on_recv.at[slot, 1], mate),
        )

    def pass_on(slot):
        for copy in far_copies(slot):
            copy.wait_recv()
        for copy in on_copies(slot):
            copy.start()

    def pass_near(member):
        pass_on(4 * member + 1)
        pass_on(4 * member + 2)
        for copy in far_copies(4 * member + 3):
            copy.start()

    def half_copy(member, half):
        return remote(
            stage.at[4 * member + 3, half_rows[half]], far_in.at[member, half], half_send.at[member, half],
            half_recv.at[member, half], 2 * chip_at(chip, half + 1) + core,
        )

    def half_copies(member):
        return [half_copy(member, half) for half in range(2)]

    def core_copy(step):
        member, flip = slot_of(step)
        slot, ring = 4 * member + flip, lax.rem(step, 4)
        return remote(part.at[ring, 1 - core], got.at[slot], core_send.at[slot], core_recv.at[slot], mate)

    def chip_copy(slot):
        member, flip = slot // 4, slot % 4
        peer = 2 * chip_at(chip, flip) + core
        place = 2 * member + flip - 1
        return remote(stage.at[slot], arrive.at[place], chip_send.at[place], chip_recv.at[place], peer)

    def relay(member):
        for half in range(2):
            half_copy(member, half).wait_recv()
            slot = 4 * member + 2 - half
            joined = stage.at[slot, half_rows[half]]
            add(joined, joined, far_in.at[member, half])
            chip_copy(slot).start()

    masks = mask_loads(seg_ref, mask_ref, seg_buf, mask_buf, mask_sem)
    for copy in masks:
        copy.start()
    own_rows = pl.ds(pl.multiple_of(me * ROWS, ROWS), ROWS)
    tails = (
        pltpu.make_async_copy(lat_ref.at[0, :, own_rows], lat, tail_sem.at[0]),
        pltpu.make_async_copy(lup_ref, lup, tail_sem.at[1]),
    )
    for copy in own_copies(0):
        copy.start()
    for copy in tok_copies(0):
        copy.start()
    for step in range(3):
        loads(jnp.int32(step)).start()
    for copy in own_copies(1):
        copy.start()
    for copy in tok_copies(1):
        copy.start()
    for copy in tails:
        copy.start()
    greet_all([mate] + [2 * other + core for other in others], grp_devices)
    for member in range(MB):
        for copy in near_copies(member):
            copy.start()
    for flip in (1, 2):
        for copy in far_copies(flip):
            copy.start()
    tok[0](0)
    for item in range(count):
        grp[0](item)
    for copy in masks:
        copy.wait()
    mask_rows(seg_buf, mask_buf, count_ref, bias)

    def compute(step):
        member, flip = slot_of(step)
        slot = 4 * member + flip

        @pl.when(step < 2)
        def _():
            for copy in tok_copies(member):
                copy.wait()
            dk[member] = jnp.zeros((TOK_DEV, D), F32)
            dv[member] = jnp.zeros((TOK_DEV, D), F32)

        loads(step).wait()

        @pl.when(step + 3 < 4 * MB)
        def _():
            loads(step + 3).start()

        @pl.when(flip == 0)
        def _():
            for copy in own_copies(member):
                copy.wait()
            for copy in near_copies(member):
                copy.wait_recv()

        @pl.when(flip > 0)
        def _():
            for copy in on_copies(slot):
                copy.wait_recv()

        asked = queries[lax.rem(step, 4)]
        upstream = ups[slot].reshape(span, D)
        scores = nt(asked, keys[member])
        soft = nt(upstream, values[member])
        weights, grads = [], []
        for half in range(2):
            seen = bias[member, pl.ds(2 * chip_at(chip, flip) + half, 1), :]
            figures = figs[slot, half].T
            rows = slice(half * ROWS, (half + 1) * ROWS)
            weight = jnp.exp2(scores[rows] + seen - figures[:, 0:1])
            grads.append((weight * (soft[rows] - figures[:, 1:2])).astype(BF16))
            weights.append(weight.astype(BF16))
        weight = jnp.concatenate(weights, axis=0)
        grad = jnp.concatenate(grads, axis=0)
        dv[member] += tn(weight, upstream)
        dk[member] += tn(grad, asked)
        asked_grad = (nn(grad, keys[member]) * D ** (-0.5)).astype(BF16)

        @pl.when(step >= 4)
        def _():
            core_copy(step - 4).wait_send()

        for half in range(2):
            part[lax.rem(step, 4), half] = asked_grad[half * ROWS:(half + 1) * ROWS]
        core_copy(step).start()

    def combine(step):
        member, flip = slot_of(step)
        slot = 4 * member + flip
        core_copy(step).wait_recv()
        added = part[lax.rem(step, 4), core].astype(F32) + got[slot].astype(F32)

        @pl.when(flip > 0)
        def _():
            stage[slot] = added.astype(BF16)

        @pl.when(flip == 0)
        def _():
            total[member] = added

    def tokens_back(member, half):
        gain = tgain_ref[...]
        rows = pl.ds(pl.multiple_of(half * span, span), span)
        hat, inverse = norm_parts(tok_buf[member, rows].astype(F32))
        normed = (hat * gain).astype(BF16)
        key_grad = (dk[member, rows] * LN2).astype(BF16)
        value_grad = dv[member, rows].astype(BF16)
        dkw[...] += tn(normed, key_grad)
        dvw[...] += tn(normed, value_grad)
        normed_grad = nt(key_grad, kw_ref[...]) + nt(value_grad, vw_ref[...])
        source_grad, gain_rows = norm_pull(hat, inverse, gain, normed_grad)
        dk[member, rows] = source_grad
        dgain_ref[...] += jnp.sum(gain_rows, axis=0, keepdims=True)

    def hold(item):
        helds[item][...] = tok[4](item).astype(helds[item].dtype)

    def step_body(step, carry):
        compute(step)

        @pl.when(step > 0)
        def _():
            combine(step - 1)

        @pl.when(step == 0)
        def _():
            for flip in (1, 2):
                for copy in far_copies(4 + flip):
                    copy.start()
            tok[1](0)
            tok[0](1)

        @pl.when(step == 1)
        def _():
            pass_near(0)
            tok[0](2)

        @pl.when(step == 2)
        def _():
            tok[1](1)

        @pl.when(step == 3)
        def _():
            pass_on(3)
            pass_near(1)

        @pl.when(step == 4)
        def _():
            pass_on(7)
            for item in range(count):
                grp[4](item)
            tok[1](2)

        @pl.when(step == 5)
        def _():
            for copy in half_copies(0):
                copy.start()
            tok[2](0)

        @pl.when(step == 6)
        def _():
            for copy in half_copies(1):
                copy.start()
            relay(0)

        return carry

    lax.fori_loop(0, 4 * MB, step_body, 0)

    def tokens_body(member, carry):
        @pl.when(member == 1)
        def _():
            tok[3](0)
            tok[2](1)

        for half in range(TOK_DEV // span):
            tokens_back(member, half)
        out_copy(member).start()

        @pl.when(member == 0)
        def _():
            combine(4 * MB - 1)
            relay(1)

        return carry

    dkw[...] = jnp.zeros_like(dkw)
    dvw[...] = jnp.zeros_like(dvw)
    dgain_ref[...] = jnp.zeros_like(dgain_ref)
    lax.fori_loop(0, MB, tokens_body, 0)
    dkw_ref[...] = dkw[...].astype(BF16)
    dvw_ref[...] = dvw[...].astype(BF16)
    tok[2](2)
    hold(0)
    tok[3](1)
    for copy in tails:
        copy.wait()
    gain = qgain_ref[...]
    hat, inverse = norm_parts(lat[...].reshape(MB * ROWS, D))
    normed = (hat * gain).astype(BF16)
    asked_grads = []
    for member in range(MB):
        added = total[member]
        for flip in (1, 2):
            chip_copy(4 * member + flip).wait_recv()
            added = added + arrive[2 * member + flip - 1].astype(F32)
        asked_grads.append(added.astype(BF16))
    asked_grad = jnp.concatenate(asked_grads, axis=0)
    dqw_ref[...] = tn(normed, asked_grad).astype(BF16)
    source_grad, gain_rows = norm_pull(hat, inverse, gain, nt(asked_grad, qw_ref[...]))
    lup[...] += source_grad
    tok[3](2)
    last = pltpu.make_async_copy(lup, dlat_ref, tail_sem.at[2])
    last.start()
    query_gain = jnp.sum(gain_rows, axis=0, keepdims=True)
    rows = jnp.concatenate(
        [dgain_ref[...], query_gain, fgain_ref[...], mgain_ref[...], sgain_ref[...], jnp.zeros((3, D), F32)], axis=0
    )
    gains_ref[...] = jnp.zeros_like(gains_ref)
    width = D // TOK
    for device in range(TOK):
        gains_ref[16 * device:16 * device + 8, 0:width] = rows[:, device * width:(device + 1) * width]
    grp[3]((0,))
    hold(1)
    hold(2)
    tok[5]()
    last.wait()
    for step in range(4, 4 * MB):
        core_copy(jnp.int32(step)).wait_send()
    for member in range(MB):
        out_copy(member).wait()
        for copy in near_copies(member) + half_copies(member):
            copy.wait_send()
        for flip in range(4):
            slot = 4 * member + flip
            if flip > 0:
                for copy in far_copies(slot):
                    copy.wait_send()
                for copy in on_copies(slot):
                    copy.wait_send()
            if flip in (1, 2):
                chip_copy(slot).wait_send()


CROSS_SCRATCH = 44


def cross_backward(collective_id, arrays, grads, *args):
    dma = pltpu.SemaphoreType.DMA
    span = 2 * ROWS
    steps = 4 * MB
    vmem = pl.BlockSpec(memory_space=pltpu.VMEM)
    hbm = pl.BlockSpec(memory_space=pl.ANY)
    smem = pl.BlockSpec(memory_space=pltpu.SMEM)
    items, kinds = held_plan(arrays)
    sources, grad_items, grad_kinds, shapes = reduce_plan(grads)
    scratch = [
        pltpu.VMEM((MB, TOK_DEV, D), BF16),
        pltpu.VMEM((MB, TOK_DEV, D), BF16),
        pltpu.VMEM((MB, TOK_DEV, D), BF16),
        pltpu.VMEM((4, span, D), BF16),
        pltpu.VMEM((steps, 2, ROWS, D), BF16),
        pltpu.VMEM((steps, 2, 8, ROWS), F32),
        pltpu.VMEM((MB, LGROUPS, TOK_DEV), F32),
        pltpu.VMEM((4, 2, ROWS, D), BF16),
        pltpu.VMEM((steps, ROWS, D), BF16),
        pltpu.VMEM((steps, ROWS, D), BF16),
        pltpu.VMEM((2 * MB, ROWS, D), BF16),
        pltpu.VMEM((MB, 2, ROWS // 2, D), BF16),
        pltpu.VMEM((MB, ROWS, D), F32),
        pltpu.VMEM((MB, TOK_DEV, D), F32),
        pltpu.VMEM((MB, TOK_DEV, D), F32),
        pltpu.VMEM((D, D), F32),
        pltpu.VMEM((D, D), F32),
        pltpu.VMEM((1, D), F32),
        pltpu.VMEM((MB, ROWS, D), F32),
        pltpu.VMEM((MB * ROWS, D), F32),
        pltpu.VMEM((MB, TOK_DEV), jnp.int32),
        pltpu.VMEM((MB, SCENES, LGROUPS), jnp.int32),
        dma((2,)), dma((3,)),
        dma((MB,)), dma((MB,)), dma((MB,)), dma((4,)), dma((MB,)),
        dma((MB, 2)), dma((MB, 2)), dma((steps, 2)), dma((steps, 2)), dma((steps, 2)), dma((steps, 2)), dma((MB, 2)),
        dma((MB,)), dma((MB,)),
        dma((steps,)), dma((steps,)), dma((2 * MB,)), dma((2 * MB,)), dma((MB, 2)), dma((MB, 2)),
    ]
    return pl.pallas_call(
        functools.partial(cross_backward_kernel, items, grad_items),
        in_specs=[hbm] + [vmem] * 3 + [hbm, hbm, smem] + [hbm] * 7 + [vmem] * 5 + [vmem] * len(arrays) + [hbm] * len(grads),
        out_specs=[hbm, hbm] + [vmem] * (4 + len(arrays) + len(grads)),
        out_shape=[
            jax.ShapeDtypeStruct((MB * ROWS, D), F32),
            jax.ShapeDtypeStruct((1, MB, TOK_DEV, D), F32),
            jax.ShapeDtypeStruct((D, D), BF16),
            jax.ShapeDtypeStruct((D, D), BF16),
            jax.ShapeDtypeStruct((D, D), BF16),
            jax.ShapeDtypeStruct((16 * TOK, 128), F32),
        ] + [jax.ShapeDtypeStruct(array.shape, array.dtype) for array in arrays]
        + [jax.ShapeDtypeStruct((high // 2, wide), kind) for (high, wide), kind in zip(shapes, grad_kinds)],
        scratch_shapes=scratch + grp_scratch(items, kinds) + tok_scratch(grad_items, grad_kinds),
        compiler_params=pltpu.CompilerParams(
            collective_id=collective_id, has_side_effects=True, vmem_limit_bytes=60 * MIB
        ),
        cost_estimate=pl.CostEstimate(
            flops=26 * 10**9, bytes_accessed=24 * 10**6, transcendentals=4 * 10**6
        ),
        name="cross_backward",
    )(*args, *arrays, *sources)


GELU_A = 0.7978845608028654
GELU_B = 0.044715


def gelu_parts(hidden):
    square = hidden * hidden
    bent = jnp.tanh(GELU_A * hidden * (1.0 + GELU_B * square))
    half = 0.5 * (1.0 + bent)
    slope = half + 0.5 * hidden * (1.0 - bent * bent) * (GELU_A * (1.0 + 3.0 * GELU_B * square))
    return hidden * half, slope


def greet_all(tok_devices, grp_devices=()):
    barrier = pltpu.get_barrier_semaphore()
    for axis, devices in (("tok", tok_devices), ("grp", grp_devices)):
        for device in devices:
            pl.semaphore_signal(
                barrier, inc=1, device_id={axis: device}, device_id_type=pl.DeviceIdType.MESH
            )
    pl.semaphore_wait(barrier, len(tok_devices) + len(grp_devices))


def all_peers():
    me, core, chip, mate, others = places()
    peers = []
    for other in others:
        peers += [2 * other + core, 2 * other + 1 - core]
    return me, peers + [mate]


def head_copies(row_side, head_side, to_heads, member, me, peers, send, recv, local):
    lanes = pl.ds(member * ROWS, ROWS)
    row_at = lambda device: row_side.at[:, device, :, lanes]
    head_at = lambda device: head_side.at[:, member, :, pl.ds(pl.multiple_of(device * ROWS, ROWS), ROWS)]
    source, target = (row_at, head_at) if to_heads else (head_at, row_at)
    copies = [
        remote(source(peer), target(me), send.at[slot, member], recv.at[slot, member], peer)
        for slot, peer in enumerate(peers)
    ]
    return copies, pltpu.make_async_copy(source(me), target(me), local.at[member])


QB = 1024
QB_BACK = 256


def latents_forward_kernel(
    lat_ref, att_ref, cot_ref, ow_ref, fgain_ref, fup_ref, fdown_ref, mgain_ref, proj_ref, mow_ref, sgain_ref,
    sup_ref, sdown_ref,
    out_ref, fmid_ref, mmid_ref, packed_ref, exact_ref, lse_ref, up_ref, mgrad_ref, ddown_ref, dup_ref, dmo_ref,
    dgain_ref,
    lat, att, cot, ow, fup, fdown, proj, mow, sup, sdown,
    out, fmid, mmid, heads, exact, up, mgrad, ddown, dup, dmo,
    rows_out, keys, values, mixed, mixed_rows, active, hidden_low, normed_low,
    load_sem, store_sem, send_a, recv_a, local_a, send_b, recv_b, local_b,
):
    me, peers = all_peers()
    own = pl.ds(pl.multiple_of(me * ROWS, ROWS), ROWS)
    names = ("lat", "att", "ow", "fup", "fdown", "proj", "mow", "sup", "sdown", "cot")
    loads = {}
    for i, (source, target) in enumerate((
        (lat_ref.at[0, :, own], lat), (att_ref, att), (ow_ref, ow), (fup_ref, fup), (fdown_ref, fdown),
        (proj_ref, proj), (mow_ref, mow), (sup_ref, sup), (sdown_ref, sdown), (cot_ref.at[0], cot),
    )):
        loads[names[i]] = pltpu.make_async_copy(source, target, load_sem.at[i])
        loads[names[i]].start()
    stores = []

    def store(source, target):
        stores.append(pltpu.make_async_copy(source, target, store_sem.at[len(stores)]))
        stores[-1].start()

    greet_all(peers)
    flat = (MB * ROWS, D)
    for name in ("lat", "att", "ow"):
        loads[name].wait()
    outward = [head_copies(rows_out, heads, True, member, me, peers, send_a, recv_a, local_a) for member in range(MB)]
    backward = [
        head_copies(mixed_rows, mixed, False, member, me, peers, send_b, recv_b, local_b) for member in range(MB)
    ]
    for member in range(MB):
        rows = slice(member * ROWS, (member + 1) * ROWS)
        first = lat[member] + nn(att[member].astype(BF16), ow[...])
        fmid[rows] = first
        normed = (norm_parts(first)[0] * fgain_ref[...]).astype(BF16)
        if member == 0:
            loads["fup"].wait()
            loads["fdown"].wait()
        mid = first
        for part in range(2):
            cut = slice(part * FF // 2, (part + 1) * FF // 2)
            mid = mid + nn(jax.nn.gelu(nn(normed, fup[:, cut])).astype(BF16), fdown[cut])
        mmid[rows] = mid
        normed = (norm_parts(mid)[0] * mgain_ref[...]).astype(BF16).T
        if member == 0:
            loads["proj"].wait()
        for kind, scale in enumerate((HD ** (-0.5) * LOG2E, 1.0, 1.0)):
            packed = tn(proj[:, kind * D:(kind + 1) * D], normed) * scale
            rows_out[kind, :, :, rows] = packed.astype(BF16).reshape(H, HD, ROWS)
        copies, here = outward[member]
        for copy in copies:
            copy.start()
        here.start()
    store(fmid, fmid_ref)
    store(mmid, mmid_ref)
    for member in range(MB):
        copies, here = outward[member]
        for copy in copies:
            copy.wait_recv()
        here.wait()
        store(heads.at[:, member], packed_ref.at[:, member])
        keys[...] = heads[1, member].T
        values[0:HD] = heads[2, member]
        values[HD:] = jnp.ones((16, L), BF16)

        def attend(step, carry, member=member):
            at = pl.ds(pl.multiple_of(step * QB, QB), QB)
            logits = nn(keys[...], heads[0, member, :, at])
            top = jnp.max(logits, axis=0, keepdims=True)
            both = nn(values[...], jnp.exp2(logits - top).astype(BF16))
            total = both[HD:HD + 1]
            result = both[0:HD] / total
            exact[member, :, at] = result
            mixed[0, member, :, at] = result.astype(BF16)
            lse_ref[member, :, at] = jnp.broadcast_to(top + jnp.log2(total), (8, QB))
            return carry

        lax.fori_loop(0, L // QB, attend, 0)
        for copy in backward[member][0] + [backward[member][1]]:
            copy.start()
    store(exact, exact_ref)
    loads["mow"].wait()
    loads["sup"].wait()
    loads["sdown"].wait()
    loads["cot"].wait()
    gains = []
    for member in range(MB):
        copies, here = backward[member]
        for copy in copies:
            copy.wait_recv()
        here.wait()
        rows = slice(member * ROWS, (member + 1) * ROWS)
        second = mmid[rows] + tn(mixed_rows[0, :, :, rows].reshape(D, ROWS), mow[...])
        hat, inverse = norm_parts(second)
        normed = (hat * sgain_ref[...]).astype(BF16)
        normed_low[rows] = normed
        upstream = cot[member]
        grad = upstream.astype(BF16)
        final = second
        normed_grad = jnp.zeros((ROWS, D), F32)
        for part in range(2):
            cut = slice(part * FF // 2, (part + 1) * FF // 2)
            act, slope = gelu_parts(nn(normed, sup[:, cut]))
            act = act.astype(BF16)
            active[rows, cut] = act
            final = final + nn(act, sdown[cut])
            hidden_grad = (slope * nt(grad, sdown[cut])).astype(BF16)
            hidden_low[rows, cut] = hidden_grad
            normed_grad = normed_grad + nt(hidden_grad, sup[:, cut])
        out[member] = final
        residual, gain_rows = norm_pull(hat, inverse, sgain_ref[...], normed_grad)
        gains.append(jnp.sum(gain_rows, axis=0, keepdims=True))
        upstream = upstream + residual
        up[rows] = upstream
        mgrad[0, :, :, rows] = nt(mow[...], upstream.astype(BF16)).astype(BF16).reshape(H, HD, ROWS)
    store(out, out_ref.at[0])
    store(up, up_ref)
    store(mgrad, mgrad_ref)
    dgain_ref[...] = gains[0] + gains[1]
    ddown[...] = tn(active[...], cot[...].reshape(flat).astype(BF16)).astype(BF16)
    store(ddown, ddown_ref)
    dup[...] = tn(normed_low[...], hidden_low[...]).astype(BF16)
    store(dup, dup_ref)
    dmo[...] = nn(mixed_rows[0].reshape(D, MB * ROWS), up[...].astype(BF16)).astype(BF16)
    store(dmo, dmo_ref)
    for copy in stores:
        copy.wait()
    for copies, here in outward + backward:
        for copy in copies:
            copy.wait_send()


def latents_forward(collective_id, *args):
    dma = pltpu.SemaphoreType.DMA
    vmem = pl.BlockSpec(memory_space=pltpu.VMEM)
    hbm = pl.BlockSpec(memory_space=pl.ANY)
    rows = MB * ROWS
    stored = [
        ((1, MB, ROWS, D), F32), ((rows, D), F32), ((rows, D), F32), ((3, MB, HD, L), BF16), ((MB, HD, L), F32),
        ((MB, 8, L), F32), ((rows, D), F32), ((1, H, HD, rows), BF16), ((FF, D), BF16), ((D, FF), BF16), ((D, D), BF16),
        ((1, D), F32),
    ]
    return pl.pallas_call(
        latents_forward_kernel,
        in_specs=[hbm, hbm, hbm, hbm, vmem, hbm, hbm, vmem, hbm, hbm, vmem, hbm, hbm],
        out_specs=[hbm] * 5 + [vmem] + [hbm] * 5 + [vmem],
        out_shape=[jax.ShapeDtypeStruct(shape, kind) for shape, kind in stored],
        scratch_shapes=[
            pltpu.VMEM((MB, ROWS, D), F32), pltpu.VMEM((MB, ROWS, D), F32), pltpu.VMEM((MB, ROWS, D), F32),
            pltpu.VMEM((D, D), BF16), pltpu.VMEM((D, FF), BF16), pltpu.VMEM((FF, D), BF16),
            pltpu.VMEM((D, 3 * D), BF16), pltpu.VMEM((D, D), BF16), pltpu.VMEM((D, FF), BF16),
            pltpu.VMEM((FF, D), BF16),
            pltpu.VMEM((MB, ROWS, D), F32), pltpu.VMEM((rows, D), F32), pltpu.VMEM((rows, D), F32),
            pltpu.VMEM((3, MB, HD, L), BF16), pltpu.VMEM((MB, HD, L), F32), pltpu.VMEM((rows, D), F32),
            pltpu.VMEM((1, H, HD, rows), BF16), pltpu.VMEM((FF, D), BF16), pltpu.VMEM((D, FF), BF16),
            pltpu.VMEM((D, D), BF16),
            pltpu.VMEM((3, H, HD, rows), BF16), pltpu.VMEM((L, HD), BF16), pltpu.VMEM((HD + 16, L), BF16),
            pltpu.VMEM((1, MB, HD, L), BF16), pltpu.VMEM((1, H, HD, rows), BF16),
            pltpu.VMEM((rows, FF), BF16), pltpu.VMEM((rows, FF), BF16), pltpu.VMEM((rows, D), BF16),
            dma((10,)), dma((11,)), dma((7, MB)), dma((7, MB)), dma((MB,)), dma((7, MB)), dma((7, MB)), dma((MB,)),
        ],
        compiler_params=pltpu.CompilerParams(
            collective_id=collective_id, has_side_effects=True, vmem_limit_bytes=60 * MIB
        ),
        cost_estimate=pl.CostEstimate(
            flops=20 * 10**9, bytes_accessed=30 * 10**6, transcendentals=10 * 10**6
        ),
        name="latents_forward",
    )(*args)


def levels():
    level = lax.axis_index("grp")
    odd = lax.rem(level, 2)
    return odd, level + 1 - 2 * odd, lax.rem(level + 2, 4)


def half_slices(rows, odd):
    half = rows // 2
    keep = pl.ds(pl.multiple_of(odd * half, half), half)
    away = pl.ds(pl.multiple_of((1 - odd) * half, half), half)
    return keep, away


def tok_steps(items, sources, scratch):
    n = len(items)
    mine, got, near_in, first_in, second_in = [scratch[i * n:(i + 1) * n] for i in range(5)]
    (local_sem, core_send, core_recv, near_send, near_recv, one_send, one_recv, two_send, two_recv) = scratch[5 * n:]
    me, core, chip, mate, (far, flip_x, flip_y) = places()
    x, y = lax.rem(chip, 2), lax.div(chip, 2)
    odd, level_near, level_far = levels()

    def core_copies(i):
        source, rows, row_at, columns, column_at, x_first = items[i]
        part = (pl.ds(row_at, rows), pl.ds(column_at, columns))
        return (
            remote(sources[source].at[:, :, 1 - core, *part], got[i], core_send.at[i], core_recv.at[i], mate),
            pltpu.make_async_copy(sources[source].at[:, :, core, *part], mine[i], local_sem.at[i]),
        )

    def near_copy(i):
        keep, away = half_slices(items[i][1], odd)
        return pltpu.make_async_remote_copy(
            src_ref=mine[i].at[:, :, away], dst_ref=near_in[i], send_sem=near_send.at[i], recv_sem=near_recv.at[i],
            device_id={"grp": level_near}, device_id_type=pl.DeviceIdType.MESH,
        )

    def first_copy(i):
        keep, away = half_slices(items[i][1], odd)
        x_first = items[i][-1]
        source = mine[i].at[:, 1 - x, keep] if x_first else mine[i].at[1 - y, :, keep]
        peer = 2 * (flip_x if x_first else flip_y) + core
        return remote(source, first_in[i], one_send.at[i], one_recv.at[i], peer)

    def second_copy(i):
        keep, away = half_slices(items[i][1], odd)
        x_first = items[i][-1]
        source = mine[i].at[1 - y, x, keep] if x_first else mine[i].at[y, 1 - x, keep]
        peer = 2 * (flip_y if x_first else flip_x) + core
        return remote(source, second_in[i], two_send.at[i], two_recv.at[i], peer)

    def core_sends(i):
        for copy in core_copies(i):
            copy.start()

    def core_sums(i):
        there, here = core_copies(i)
        there.wait_recv()
        here.wait()
        add(mine[i], mine[i], got[i])
        near_copy(i).start()

    def near_sums(i):
        keep, away = half_slices(items[i][1], odd)
        near_copy(i).wait_recv()
        held = mine[i].at[:, :, keep]
        add(held, held, near_in[i])
        first_copy(i).start()

    def first_sums(i):
        keep, away = half_slices(items[i][1], odd)
        first_copy(i).wait_recv()
        held = mine[i].at[:, x, keep] if items[i][-1] else mine[i].at[y, :, keep]
        add(held, held, first_in[i])
        second_copy(i).start()

    def second_sums(i):
        keep, away = half_slices(items[i][1], odd)
        second_copy(i).wait_recv()
        return mine[i][y, x, keep].astype(F32) + second_in[i][...].astype(F32)

    def finish():
        for i in range(n):
            core_copies(i)[0].wait_send()
            for copy in (near_copy(i), first_copy(i), second_copy(i)):
                copy.wait_send()

    return (core_sends, core_sums, near_sums, first_sums, second_sums, finish), (
        mate, 2 * flip_x + core, 2 * flip_y + core)


def plain_steps(items, sources, scratch):
    n = len(items)
    mine, got, near_in, first_in, second_in = [scratch[i * n:(i + 1) * n] for i in range(5)]
    (local_sem, core_send, core_recv, near_send, near_recv, one_send, one_recv, two_send, two_recv) = scratch[5 * n:]
    me, core, chip, mate, (far, flip_x, flip_y) = places()
    x, y = lax.rem(chip, 2), lax.div(chip, 2)
    odd, level_near, level_far = levels()

    def core_copy(i):
        return remote(sources[i].at[:, :, 1 - core], got[i], core_send.at[i], core_recv.at[i], mate)

    def local_copy(i):
        return pltpu.make_async_copy(sources[i].at[:, :, core], mine[i], local_sem.at[i])

    def first_copy(i):
        x_first = items[i][-1]
        source = mine[i].at[:, 1 - x] if x_first else mine[i].at[1 - y]
        peer = 2 * (flip_x if x_first else flip_y) + core
        return remote(source, first_in[i], one_send.at[i], one_recv.at[i], peer)

    def second_copy(i):
        x_first = items[i][-1]
        source = mine[i].at[1 - y, x] if x_first else mine[i].at[y, 1 - x]
        peer = 2 * (flip_y if x_first else flip_x) + core
        return remote(source, second_in[i], two_send.at[i], two_recv.at[i], peer)

    def near_copy(i):
        keep, away = half_slices(items[i][1], odd)
        return pltpu.make_async_remote_copy(
            src_ref=mine[i].at[y, x, away], dst_ref=near_in[i], send_sem=near_send.at[i], recv_sem=near_recv.at[i],
            device_id={"grp": level_near}, device_id_type=pl.DeviceIdType.MESH,
        )

    def core_sends(i):
        core_copy(i).start()
        local_copy(i).start()

    def core_sums(i):
        core_copy(i).wait_recv()
        local_copy(i).wait()
        add(mine[i], mine[i], got[i])
        first_copy(i).start()

    def first_sums(i):
        first_copy(i).wait_recv()
        held = mine[i].at[:, x] if items[i][-1] else mine[i].at[y]
        add(held, held, first_in[i])
        second_copy(i).start()

    def second_sums(i):
        second_copy(i).wait_recv()
        held = mine[i].at[y, x]
        add(held, held, second_in[i])
        near_copy(i).start()

    def near_sums(i):
        keep, away = half_slices(items[i][1], odd)
        near_copy(i).wait_recv()
        return mine[i][y, x, keep].astype(F32) + near_in[i][...].astype(F32)

    def finish():
        for i in range(n):
            for copy in (core_copy(i), near_copy(i), first_copy(i), second_copy(i)):
                copy.wait_send()

    return (core_sends, core_sums, first_sums, second_sums, near_sums, finish), (
        mate, 2 * flip_x + core, 2 * flip_y + core)


def grp_steps(items, held, outs, scratch, joined=None):
    n = len(items)
    far_in, own_joined, near_in = [scratch[i * n:(i + 1) * n] for i in range(3)]
    z_send, z_recv = scratch[3 * n:]
    joined = own_joined if joined is None else joined
    odd, level_near, level_far = levels()

    def along(i, step):
        source, target, other = (
            (held[i], far_in[i], level_far),
            (joined[i], near_in[i], level_near),
        )[step]
        return pltpu.make_async_remote_copy(
            src_ref=source, dst_ref=target, send_sem=z_send.at[i, step], recv_sem=z_recv.at[i, step],
            device_id={"grp": other}, device_id_type=pl.DeviceIdType.MESH,
        )

    def store(i, odd_half, value):
        source, rows, row_at, columns, column_at, x_first = items[i]
        half = rows // 2
        start = pl.multiple_of(row_at + odd_half * half, half)
        outs[source][pl.ds(start, half), pl.ds(column_at, columns)] = value.astype(F32)

    def far_start(i):
        along(i, 0).start()

    def far_join(i):
        along(i, 0).wait_recv()
        add(joined[i], held[i], far_in[i])

    def near_start(i):
        along(i, 1).start()
        store(i, odd, joined[i][...])

    def far_sum(i):
        far_join(i)
        near_start(i)

    def near_store(i):
        along(i, 1).wait_recv()
        store(i, 1 - odd, near_in[i][...])

    def finish(steps=(0, 1)):
        for i in range(n):
            for step in steps:
                along(i, step).wait_send()

    return (far_start, far_sum, near_store, finish, far_join, near_start), (level_near, level_far)


def add(target, one, two):
    target[...] = one[...] + two[...]


def reduce_kernel(items, whole, joined, count, *refs):
    n, m, k = len(items), len(whole), len(joined)
    sources, held, done = refs[:count], refs[count:count + m], refs[count + m:count + m + k]
    refs = refs[count + m + k:]
    outs, whole_outs, joined_outs = refs[:count], refs[count:count + m], refs[count + m:count + m + k]
    scratch = refs[count + m + k:]
    cut = 5 * n + 9
    own_held = scratch[cut:cut + n]
    tok, near_devices = plain_steps(items, sources, scratch[:cut])
    cut += n
    late, grp_devices = grp_steps(items, own_held, outs, scratch[cut:cut + 3 * n + 2])
    cut += 3 * n + 2
    early, unused = grp_steps(whole, held, whole_outs, scratch[cut:cut + 3 * m + 2])
    cut += 3 * m + 2
    first, unused = grp_steps(joined, done, joined_outs, scratch[cut:], done)
    greet_all(near_devices, grp_devices)
    for i in range(n):
        tok[0](i)
    for i in range(m):
        early[0](i)
    for i in range(n):
        tok[1](i)
    for i in range(k):
        first[5](i)
    for i in range(n):
        tok[2](i)
    for i in range(n):
        tok[3](i)
    for i in range(n):
        own_held[i][...] = tok[4](i).astype(own_held[i].dtype)
        late[0](i)
    early[1](0)
    for i in range(1, m):
        early[1](i)
        early[2](i - 1)
    for i in range(k):
        first[2](i)
    for i in range(n):
        late[1](i)
    early[2](m - 1)
    for i in range(n):
        late[2](i)
    tok[-1]()
    late[3]()
    early[3]()
    first[3]((1,))


def reduce_plan(arrays):
    sources, items = [], []
    for source, array in enumerate(arrays):
        rows, columns = array.shape[0] // TOK, array.shape[1]
        sources.append(array.reshape(2, 2, 2, rows, columns))
        items.append((source, rows, 0, columns, 0, source % 2 == 0))
    kinds = [array.dtype for array in arrays]
    shapes = [(array.shape[0] // TOK, array.shape[1]) for array in arrays]
    return sources, tuple(items), kinds, shapes


def held_plan(arrays):
    items = tuple((i, 2 * array.shape[0], 0, array.shape[1], 0, True) for i, array in enumerate(arrays))
    return items, [array.dtype for array in arrays]


def item_blocks(items, kinds, lead, part):
    return [pltpu.VMEM(lead + (item[1] // part, item[3]), kind) for item, kind in zip(items, kinds)]


def plain_scratch(items, kinds):
    blocks = functools.partial(item_blocks, items, kinds)
    return (blocks((2, 2), 1) + blocks((2, 2), 1) + blocks((), 2) + blocks((2,), 1) + blocks((), 1)
            + [pltpu.SemaphoreType.DMA((len(items),))] * 9)


def tok_scratch(items, kinds):
    blocks = functools.partial(item_blocks, items, kinds)
    return (blocks((2, 2), 1) + blocks((2, 2), 1) + blocks((2, 2), 2) + blocks((2,), 2) + blocks((), 2)
            + [pltpu.SemaphoreType.DMA((len(items),))] * 9)


def grp_scratch(items, kinds):
    blocks = functools.partial(item_blocks, items, kinds)
    return blocks((), 2) * 3 + [pltpu.SemaphoreType.DMA((len(items), 2))] * 2


def reduce_grads(collective_id, arrays, held, done):
    sources, items, kinds, shapes = reduce_plan(arrays)
    whole, whole_kinds = held_plan(held)
    joined, joined_kinds = held_plan(done)
    vmem = pl.BlockSpec(memory_space=pltpu.VMEM)
    hbm = pl.BlockSpec(memory_space=pl.ANY)
    return pl.pallas_call(
        functools.partial(reduce_kernel, items, whole, joined, len(arrays)),
        in_specs=[hbm] * len(arrays) + [vmem] * (len(held) + len(done)),
        out_specs=[vmem] * (len(arrays) + len(held) + len(done)),
        out_shape=[jax.ShapeDtypeStruct(shape, F32) for shape in shapes]
        + [jax.ShapeDtypeStruct((item[1], item[3]), F32) for item in whole + joined],
        scratch_shapes=plain_scratch(items, kinds) + item_blocks(items, kinds, (), 2) + grp_scratch(items, kinds)
        + grp_scratch(whole, whole_kinds) + grp_scratch(joined, joined_kinds),
        compiler_params=pltpu.CompilerParams(
            collective_id=collective_id, has_side_effects=True, vmem_limit_bytes=56 * MIB
        ),
        name="reduce_grads",
    )(*sources, *held, *done)


def write_kernel(count, *refs):
    sources, gain_ref, outs = refs[:count], refs[count], refs[count + 1:2 * count + 1]
    gain_outs, buffers = refs[2 * count + 1:-count - 2], refs[-count - 2:-2]
    in_sem, out_sem = refs[-2:]
    ins = [pltpu.make_async_copy(sources[i], buffers[i], in_sem.at[i]) for i in range(count)]
    backs = [pltpu.make_async_copy(buffers[i], outs[i], out_sem.at[i]) for i in range(count)]
    for copy in ins:
        copy.start()
    for i, out in enumerate(gain_outs):
        out[...] = gain_ref[i:i + 1, 0:D // TOK]
    for i in range(count):
        ins[i].wait()
        backs[i].start()
    for copy in backs:
        copy.wait()


def write_results(results, gains, gain_count):
    n = len(results)
    hbm, vmem = pl.BlockSpec(memory_space=pl.ANY), pl.BlockSpec(memory_space=pltpu.VMEM)
    return pl.pallas_call(
        functools.partial(write_kernel, n),
        in_specs=[hbm] * n + [vmem],
        out_specs=[hbm] * n + [vmem] * gain_count,
        out_shape=[jax.ShapeDtypeStruct(result.shape, result.dtype) for result in results]
        + [jax.ShapeDtypeStruct((1, D // TOK), F32)] * gain_count,
        scratch_shapes=[pltpu.VMEM(result.shape, result.dtype) for result in results]
        + [pltpu.SemaphoreType.DMA((n,)), pltpu.SemaphoreType.DMA((n,))],
        compiler_params=pltpu.CompilerParams(vmem_limit_bytes=60 * MIB),
        name="write_results",
    )(*results, gains)


def latents_backward_kernel(items, *refs):
    (mgrad_ref, packed_ref, exact_ref, lse_ref, up_ref, mmid_ref, fmid_ref, att_ref, clse_ref, ow_ref, fgain_ref,
     fup_ref, fdown_ref, mgain_ref, proj_ref) = refs[:15]
    count = max(item[0] for item in items) + 1
    sources = refs[15:15 + count]
    (agrad_ref, fig_ref, lup_ref, dup_ref, ddown_ref, dproj_ref, dout_ref, dmgain_ref, dfgain_ref) = refs[
        15 + count:24 + count]
    reduced = refs[24 + count:24 + 2 * count]
    rest = refs[24 + 2 * count:]
    (heads, exact, ups, mmid, fmid, att, ow, fup, fdown, proj, keys, values, upstream_heads, key_acc, value_acc,
     grads, back, agrad, lup, dup, ddown, dproj, dout, hidden, active, hidden_low, grad_low,
     load_sem, store_sem, send_a, recv_a, local_a, send_b, recv_b, local_b) = rest[:35]
    me, peers = all_peers()
    reducer, near_devices = tok_steps(items, sources, rest[35:])
    core_sends, core_sums, near_sums, first_sums, second_sums, finish = reducer
    odd, level_near, level_far = levels()

    def hold(item):
        reduced[item][...] = second_sums(item).astype(reduced[item].dtype)

    names = ("heads", "exact", "fmid", "fup", "up", "mmid", "proj", "fdown", "att", "ow")
    loads = {}
    for i, (source, target) in enumerate((
        (packed_ref, heads), (exact_ref, exact), (fmid_ref, fmid), (fup_ref, fup), (up_ref, ups), (mmid_ref, mmid),
        (proj_ref, proj), (fdown_ref, fdown), (att_ref, att), (ow_ref, ow),
    )):
        loads[names[i]] = pltpu.make_async_copy(source, target, load_sem.at[i])
        loads[names[i]].start()
    stores = []

    def store(source, target):
        stores.append(pltpu.make_async_copy(source, target, store_sem.at[len(stores)]))
        stores[-1].start()

    greet_all(peers, (level_near,))
    outward = [
        head_copies(mgrad_ref, upstream_heads, True, member, me, peers, send_a, recv_a, local_a) for member in range(MB)
    ]
    backward = [head_copies(back, grads, False, member, me, peers, send_b, recv_b, local_b) for member in range(MB)]
    for copies, here in outward:
        for copy in copies:
            copy.start()
        here.start()
    core_sends(0)
    loads["fmid"].wait()
    loads["fup"].wait()
    first_hat, first_inverse = norm_parts(fmid[...])
    first_normed = (first_hat * fgain_ref[...]).astype(BF16)
    hidden[...] = nn(first_normed, fup[...])
    core_sums(0)
    loads["heads"].wait()
    loads["exact"].wait()
    for member in range(MB):
        keys[...] = heads[1, member].T
        values[...] = heads[2, member].T
        key_acc[...] = jnp.zeros_like(key_acc)
        value_acc[...] = jnp.zeros_like(value_acc)
        copies, here = outward[member]
        for copy in copies:
            copy.wait_recv()
        here.wait()
        if member == 0:
            core_sends(1)
            core_sends(2)

        def attend_back(step, carry, member=member):
            at = pl.ds(pl.multiple_of(step * QB_BACK, QB_BACK), QB_BACK)
            queries = heads[0, member, :, at]
            upstream = upstream_heads[0, member, :, at]
            inner = jnp.sum(upstream.astype(F32) * exact[member, :, at], axis=0, keepdims=True)
            softened = jnp.exp2(nn(keys[...], queries) - lse_ref[member, 0:1, at])
            logit_grad = (softened * (nn(values[...], upstream) - inner)).astype(BF16)
            value_acc[...] += nt(upstream, softened.astype(BF16))
            key_acc[...] += nt(queries, logit_grad)
            grads[0, member, :, at] = (nn(heads[1, member], logit_grad) * HD ** (-0.5)).astype(BF16)
            return carry

        steps = L // QB_BACK
        lax.fori_loop(0, steps, attend_back, 0)
        grads[1, member] = (key_acc[...] * LN2).astype(BF16)
        grads[2, member] = value_acc[...].astype(BF16)
        for copy in backward[member][0] + [backward[member][1]]:
            copy.start()
        if member == 0:
            near_sums(0)
            core_sums(1)
            core_sums(2)
        else:
            first_sums(0)
            near_sums(1)
            near_sums(2)
    loads["up"].wait()
    loads["mmid"].wait()
    loads["proj"].wait()
    loads["fdown"].wait()
    mixer_hat, mixer_inverse = norm_parts(mmid[...])
    mixer_normed = (mixer_hat * mgain_ref[...]).astype(BF16).T
    loads["att"].wait()
    loads["ow"].wait()
    mixer_gains, first_gains = [], []

    def rows_back(member):
        copies, here = backward[member]
        for copy in copies:
            copy.wait_recv()
        here.wait()
        rows = slice(member * ROWS, (member + 1) * ROWS)
        normed_grad = nn(proj[...], back[:, :, :, rows].reshape(3 * D, ROWS)).T
        residual, gain_rows = norm_pull(mixer_hat[rows], mixer_inverse[rows], mgain_ref[...], normed_grad)
        mixer_gains.append(jnp.sum(gain_rows, axis=0, keepdims=True))
        upstream = ups[rows] + residual
        grad = upstream.astype(BF16)
        grad_low[rows] = grad
        normed_grad = jnp.zeros((ROWS, D), F32)
        for part in range(2):
            cut = slice(part * FF // 2, (part + 1) * FF // 2)
            act, slope = gelu_parts(hidden[rows, cut])
            active[rows, cut] = act.astype(BF16)
            hidden_grad = (slope * nt(grad, fdown[cut])).astype(BF16)
            hidden_low[rows, cut] = hidden_grad
            normed_grad = normed_grad + nt(hidden_grad, fup[:, cut])
        residual, gain_rows = norm_pull(first_hat[rows], first_inverse[rows], fgain_ref[...], normed_grad)
        first_gains.append(jnp.sum(gain_rows, axis=0, keepdims=True))
        upstream = upstream + residual
        lup[rows] = upstream
        attended_grad = nt(upstream.astype(BF16), ow[...]).astype(BF16)
        agrad[member] = attended_grad
        inner = jnp.sum(attended_grad.astype(F32) * att[member], axis=1, keepdims=True)
        fig_ref[member] = jnp.concatenate(
            [clse_ref[member, 0:1], to_rows(inner, inner)[0:1], jnp.zeros((6, ROWS), F32)], axis=0
        )

    rows_back(0)
    hold(0)
    first_sums(1)
    first_sums(2)
    rows_back(1)
    store(lup, lup_ref)
    store(agrad, agrad_ref)
    dmgain_ref[...] = mixer_gains[0] + mixer_gains[1]
    dfgain_ref[...] = first_gains[0] + first_gains[1]
    grad = grad_low[...]
    ddown[...] = tn(active[...], grad).astype(BF16)
    store(ddown, ddown_ref)
    dup[...] = tn(first_normed, hidden_low[...]).astype(BF16)
    store(dup, dup_ref)
    dproj[...] = nt(mixer_normed, back[...].reshape(3 * D, MB * ROWS)).astype(BF16)
    store(dproj, dproj_ref)
    dout[...] = tn(att[...].reshape(MB * ROWS, D).astype(BF16), lup[...].astype(BF16)).astype(BF16)
    store(dout, dout_ref)
    hold(1)
    hold(2)
    finish()
    for copy in stores:
        copy.wait()
    for copies, here in outward + backward:
        for copy in copies:
            copy.wait_send()


def latents_backward(collective_id, arrays, *args):
    dma = pltpu.SemaphoreType.DMA
    vmem = pl.BlockSpec(memory_space=pltpu.VMEM)
    hbm = pl.BlockSpec(memory_space=pl.ANY)
    rows = MB * ROWS
    sources, items, kinds, shapes = reduce_plan(arrays)
    reduced = [jax.ShapeDtypeStruct((rows_ // 2, columns), kind) for (rows_, columns), kind in zip(shapes, kinds)]
    stored = [
        ((MB, ROWS, D), BF16), ((MB, 8, ROWS), F32), ((rows, D), F32), ((D, FF), BF16), ((FF, D), BF16),
        ((D, 3 * D), BF16), ((D, D), BF16), ((1, D), F32), ((1, D), F32),
    ]
    return pl.pallas_call(
        functools.partial(latents_backward_kernel, items),
        in_specs=[hbm, hbm, hbm, vmem, hbm, hbm, hbm, hbm, vmem, hbm, vmem, hbm, hbm, vmem, hbm] + [hbm] * len(arrays),
        out_specs=[hbm, vmem] + [hbm] * 5 + [vmem] * (2 + len(arrays)),
        out_shape=[jax.ShapeDtypeStruct(shape, kind) for shape, kind in stored] + reduced,
        scratch_shapes=[
            pltpu.VMEM((3, MB, HD, L), BF16), pltpu.VMEM((MB, HD, L), F32), pltpu.VMEM((rows, D), F32),
            pltpu.VMEM((rows, D), F32), pltpu.VMEM((rows, D), F32), pltpu.VMEM((MB, ROWS, D), F32),
            pltpu.VMEM((D, D), BF16), pltpu.VMEM((D, FF), BF16), pltpu.VMEM((FF, D), BF16),
            pltpu.VMEM((D, 3 * D), BF16), pltpu.VMEM((L, HD), BF16), pltpu.VMEM((L, HD), BF16),
            pltpu.VMEM((1, MB, HD, L), BF16), pltpu.VMEM((HD, L), F32), pltpu.VMEM((HD, L), F32),
            pltpu.VMEM((3, MB, HD, L), BF16), pltpu.VMEM((3, H, HD, rows), BF16),
            pltpu.VMEM((MB, ROWS, D), BF16), pltpu.VMEM((rows, D), F32), pltpu.VMEM((D, FF), BF16),
            pltpu.VMEM((FF, D), BF16), pltpu.VMEM((D, 3 * D), BF16), pltpu.VMEM((D, D), BF16),
            pltpu.VMEM((rows, FF), F32), pltpu.VMEM((rows, FF), BF16), pltpu.VMEM((rows, FF), BF16),
            pltpu.VMEM((rows, D), BF16),
            dma((10,)), dma((6,)), dma((7, MB)), dma((7, MB)), dma((MB,)), dma((7, MB)), dma((7, MB)), dma((MB,)),
        ] + tok_scratch(items, kinds),
        compiler_params=pltpu.CompilerParams(
            collective_id=collective_id, has_side_effects=True, vmem_limit_bytes=61 * MIB
        ),
        cost_estimate=pl.CostEstimate(
            flops=35 * 10**9, bytes_accessed=36 * 10**6, transcendentals=10 * 10**6
        ),
        name="latents_backward",
    )(*args, *sources)


def fast_body(
    tokens,
    latents,
    segments,
    scene_mask,
    counts,
    token_gain,
    query_gain,
    query_weight,
    key_weight,
    value_weight,
    output_weight,
    first_gain,
    first_up,
    first_down,
    mixer_gain,
    mixer_project,
    mixer_output,
    second_gain,
    second_up,
    second_down,
    cotangent,
):
    scenes = (segments, scene_mask, counts)
    keys, values, queries, attended, lse = cross_forward(
        0, tokens, latents, token_gain[None], query_gain[None], query_weight, key_weight, value_weight, *scenes
    )
    (latents_out, first_mid, mixer_mid, packed, exact, head_lse, upstream, mixed_grad, d_second_down, d_second_up,
     d_mixer_output, d_second_gain) = latents_forward(
        1, latents, attended, cotangent, output_weight, first_gain[None], first_up, first_down, mixer_gain[None],
        mixer_project, mixer_output, second_gain[None], second_up, second_down,
    )
    (attended_grad, figures, upstream, d_first_up, d_first_down, d_project, d_output, d_mixer_gain, d_first_gain,
     *early) = latents_backward(
        2, [d_second_up, d_second_down, d_mixer_output], mixed_grad, packed, exact, head_lse, upstream, mixer_mid,
        first_mid, attended, lse, output_weight, first_gain[None], first_up, first_down, mixer_gain[None], mixer_project,
    )
    latents_grad, tokens_grad, d_key, d_value, d_query, gains, *rest = cross_backward(
        5, early, [d_first_up, d_first_down, d_project], tokens, token_gain[None], key_weight, value_weight,
        *scenes, keys, values, queries, attended_grad, figures, latents, upstream, query_gain[None], query_weight,
        d_first_gain, d_mixer_gain, d_second_gain,
    )
    early, held = rest[:len(early)], rest[len(early):]
    o_output, o_key, o_value, o_query, gains, *late = reduce_grads(
        7, [d_output, d_key, d_value, d_query, gains], held, early
    )
    late, early = late[:len(held)], late[len(held):]
    (latents_out, latents_grad, tokens_grad, o_second_up, o_second_down, o_mixer_output, o_first_up, o_first_down,
     o_project, o_output, o_key, o_value, o_query, *o_gains) = write_results(
        [latents_out, latents_grad.reshape(latents_out.shape), tokens_grad, *early, *late, o_output, o_key, o_value, o_query], gains, 5
    )
    o_gains = [gain.reshape(D // TOK) for gain in o_gains]
    return (
        latents_out,
        latents_grad,
        tokens_grad,
        o_gains[0],
        o_gains[1],
        o_query,
        o_key,
        o_value,
        o_output,
        o_gains[2],
        o_first_up,
        o_first_down,
        o_gains[3],
        o_project,
        o_mixer_output,
        o_gains[4],
        o_second_up,
        o_second_down,
    )


IN_SPECS = (
    P("grp", None, "tok", None),
    P("grp", None, None, None),
    P("grp", None, "tok"),
    P("grp", None, None, None),
    P("grp", None, "tok"),
    P(),
    P(),
    P(),
    P(),
    P(),
    P(),
    P(),
    P(),
    P(),
    P(),
    P(),
    P(),
    P(),
    P(),
    P(),
    P("grp", None, "tok", None),
)
OUT_SPECS = (
    P("grp", None, "tok", None),
    P("grp", None, "tok", None),
    P("grp", None, "tok", None),
    P("tok"),
    P("tok"),
    P("tok", None),
    P("tok", None),
    P("tok", None),
    P("tok", None),
    P("tok"),
    P("tok", None),
    P("tok", None),
    P("tok"),
    P("tok", None),
    P("tok", None),
    P("tok"),
    P("tok", None),
    P("tok", None),
)


def solution(mesh):
    return jax.shard_map(
        fast_body if mesh.shape["tok"] == TOK else general_body,
        mesh=mesh,
        in_specs=IN_SPECS,
        out_specs=OUT_SPECS,
        check_vma=False,
    )
```

```python
import functools

import jax
import jax.numpy as jnp
from jax import lax
from jax.experimental import pallas as pl
from jax.experimental.pallas import tpu as pltpu
from jax.sharding import PartitionSpec as P

D = 512
L = 2048
H = 8
HD = 64
TOK_DEV = 1024
MB = 2
SCENES = 8
LGROUPS = 8


EPS = 1e-05
NEG = -1e30


def norm_rows(values, gain):
    centre = values - jnp.mean(values, axis=-1, keepdims=True)
    spread = jnp.mean(centre * centre, axis=-1, keepdims=True)
    return centre * lax.rsqrt(spread + EPS) * gain


def norm_back(values, gain, upstream):
    unused, pull = jax.vjp(norm_rows, values, gain)
    return pull(upstream)


def gelu_back(hidden, upstream):
    unused, pull = jax.vjp(jax.nn.gelu, hidden)
    return pull(upstream)[0]


def product_plain(left, right):
    return jnp.dot(left, right, preferred_element_type=jnp.float32)


def product_rows(left, right):
    return lax.dot_general(
        left, right, (((0,), (0,)), ((), ())), preferred_element_type=jnp.float32
    )


def product_cols(left, right):
    return lax.dot_general(
        left, right, (((1,), (1,)), ((), ())), preferred_element_type=jnp.float32
    )


def add_term(store, name, value):
    if name in store:
        store[name] = store[name] + value
    else:
        store[name] = value


def project_tokens(tokens, member, token_gain, key_weight, value_weight):
    source = tokens[0, member].astype(jnp.float32)
    normed = norm_rows(source, token_gain).astype(jnp.bfloat16)
    key_rows = product_plain(normed, key_weight).astype(jnp.bfloat16)
    value_rows = product_plain(normed, value_weight).astype(jnp.bfloat16)
    return (source, normed, key_rows, value_rows)


def mlp_forward(residual, gain, up_weight, down_weight):
    normed = norm_rows(residual, gain).astype(jnp.bfloat16)
    hidden = product_plain(normed, up_weight)
    active = jax.nn.gelu(hidden).astype(jnp.bfloat16)
    return (residual + product_plain(active, down_weight), (normed, hidden, active))


def mlp_backward(residual, gain, up_weight, down_weight, saved, upstream):
    normed, hidden, active = saved
    grad_low = upstream.astype(jnp.bfloat16)
    grad_down = product_rows(active, grad_low)
    hidden_grad = gelu_back(hidden, product_cols(grad_low, down_weight)).astype(jnp.bfloat16)
    grad_up = product_rows(normed, hidden_grad)
    residual_grad, grad_gain = norm_back(residual, gain, product_cols(hidden_grad, up_weight))
    return (upstream + residual_grad, grad_gain, grad_up, grad_down)


def mixer_forward(residual, gain, project, output):
    own_rows = residual.shape[0]
    normed = norm_rows(residual, gain).astype(jnp.bfloat16)
    packed = product_plain(normed, project).astype(jnp.bfloat16)
    pair_rows = lax.all_gather(packed[:, D:], "tok", axis=0, tiled=True)
    every = pair_rows.shape[0]
    own_queries = packed[:, :D].reshape(own_rows, H, HD)
    keys = pair_rows[:, :D].reshape(every, H, HD)
    values = pair_rows[:, D:].reshape(every, H, HD)
    logits = jnp.einsum(
        "qhd,khd->hqk", own_queries, keys, preferred_element_type=jnp.float32
    ) * HD ** (-0.5)
    peak_row = jnp.max(logits, axis=-1, keepdims=True)
    raised = jnp.exp(logits - peak_row)
    softened = raised / jnp.sum(raised, axis=-1, keepdims=True)
    softened_low = softened.astype(jnp.bfloat16)
    mixed_rows = jnp.einsum(
        "hqk,khd->qhd", softened_low, values, preferred_element_type=jnp.float32
    )
    mixed_rows = mixed_rows.reshape(own_rows, D).astype(jnp.bfloat16)
    return (
        residual + product_plain(mixed_rows, output),
        (normed, own_queries, keys, values, softened, softened_low, mixed_rows),
    )


def mixer_backward(residual, gain, project, output, saved, upstream):
    normed, own_queries, keys, values, softened, softened_low, mixed_rows = saved
    own_rows = upstream.shape[0]
    every = keys.shape[0]
    grad_low = upstream.astype(jnp.bfloat16)
    grad_output = product_rows(mixed_rows, grad_low)
    mixed_grad = product_cols(grad_low, output).astype(jnp.bfloat16).reshape(own_rows, H, HD)
    value_grad = jnp.einsum(
        "hqk,qhd->khd", softened_low, mixed_grad, preferred_element_type=jnp.float32
    )
    soft_grad = jnp.einsum("qhd,khd->hqk", mixed_grad, values, preferred_element_type=jnp.float32)
    logit_grad = softened * (soft_grad - jnp.sum(soft_grad * softened, axis=-1, keepdims=True))
    logit_grad = logit_grad.astype(jnp.bfloat16)
    query_grad = jnp.einsum(
        "hqk,khd->qhd", logit_grad, keys, preferred_element_type=jnp.float32
    ) * HD ** (-0.5)
    key_grad = jnp.einsum(
        "hqk,qhd->khd", logit_grad, own_queries, preferred_element_type=jnp.float32
    ) * HD ** (-0.5)
    pair_terms = jnp.concatenate([key_grad.reshape(every, D), value_grad.reshape(every, D)], axis=1)
    pair_grad = lax.psum_scatter(
        pair_terms.astype(jnp.bfloat16), "tok", scatter_dimension=0, tiled=True
    ).astype(jnp.float32)
    packed_grad = jnp.concatenate([query_grad.reshape(own_rows, D), pair_grad], axis=1).astype(
        jnp.bfloat16
    )
    grad_project = product_rows(normed, packed_grad)
    residual_grad, grad_gain = norm_back(residual, gain, product_cols(packed_grad, project))
    return (upstream + residual_grad, grad_gain, grad_project, grad_output)


def general_body(
    tokens,
    latents,
    segments,
    scene_mask,
    counts,
    token_gain,
    query_gain,
    query_weight,
    key_weight,
    value_weight,
    output_weight,
    first_gain,
    first_up,
    first_down,
    mixer_gain,
    mixer_project,
    mixer_output,
    second_gain,
    second_up,
    second_down,
    cotangent,
):
    scale = D ** (-0.5)
    shards = lax.axis_size("tok")
    own_rows = L // shards
    row_start = lax.axis_index("tok") * own_rows
    latent_group = jnp.arange(L) // (L // LGROUPS)
    latent_onehot = (latent_group[:, None] == jnp.arange(LGROUPS)[None, :]).astype(jnp.float32)
    token_place = jnp.arange(TOK_DEV)
    records = []
    latent_outs = []
    for member in range(MB):
        record = {}
        source, normed, key_rows, value_rows = project_tokens(
            tokens, member, token_gain, key_weight, value_weight
        )
        record["token_side"] = (source, normed, key_rows, value_rows)
        scene_onehot = (segments[0, member][:, None] == jnp.arange(SCENES)[None, :]).astype(
            jnp.float32
        )
        token_seen = jnp.dot(scene_onehot, scene_mask[0, member].astype(jnp.float32))
        visible = product_cols(latent_onehot, token_seen)
        alive = token_place < counts[0, member, 0]
        allowed = (visible > 0.5) & alive[None, :]
        latent_every = latents[0, member]
        normed_every = norm_rows(latent_every, query_gain).astype(jnp.bfloat16)
        queries = product_plain(normed_every, query_weight).astype(jnp.bfloat16)
        scores = jnp.where(allowed, product_cols(queries, key_rows) * scale, NEG)
        row_top = lax.pmax(jnp.max(scores, axis=1), "tok")
        unnormed = jnp.exp(scores - row_top[:, None])
        row_total, weighted = (
            lax.psum_scatter(
                jnp.sum(unnormed, axis=1).astype(jnp.bfloat16),
                "tok",
                scatter_dimension=0,
                tiled=True,
            ).astype(jnp.float32),
            lax.psum_scatter(
                product_plain(unnormed.astype(jnp.bfloat16), value_rows).astype(jnp.bfloat16),
                "tok",
                scatter_dimension=0,
                tiled=True,
            ).astype(jnp.float32),
        )
        latent_in = lax.dynamic_slice_in_dim(latent_every, row_start, own_rows, 0)
        latent_normed = lax.dynamic_slice_in_dim(normed_every, row_start, own_rows, 0)
        attended = weighted / row_total[:, None]
        attended_low = attended.astype(jnp.bfloat16)
        first_mid = latent_in + product_plain(attended_low, output_weight)
        mixer_mid, first_saved = mlp_forward(first_mid, first_gain, first_up, first_down)
        second_mid, mixer_saved = mixer_forward(mixer_mid, mixer_gain, mixer_project, mixer_output)
        final_rows, second_saved = mlp_forward(second_mid, second_gain, second_up, second_down)
        latent_outs.append(final_rows)
        record["latent_side"] = (
            allowed,
            latent_in,
            latent_normed,
            queries,
            row_top,
            row_total,
            attended,
            attended_low,
            first_mid,
            mixer_mid,
            second_mid,
            first_saved,
            mixer_saved,
            second_saved,
        )
        records.append(record)
    grads = {}
    latent_grads = []
    token_grads = []
    for member in range(MB):
        record = records[member]
        source, normed, key_rows, value_rows = record["token_side"]
        (
            allowed,
            latent_in,
            latent_normed,
            queries,
            row_top,
            row_total,
            attended,
            attended_low,
            first_mid,
            mixer_mid,
            second_mid,
            first_saved,
            mixer_saved,
            second_saved,
        ) = record["latent_side"]
        second_back = mlp_backward(
            second_mid, second_gain, second_up, second_down, second_saved, cotangent[0, member]
        )
        add_term(grads, "second_gain", second_back[1])
        add_term(grads, "second_up", second_back[2])
        add_term(grads, "second_down", second_back[3])
        mixer_back = mixer_backward(
            mixer_mid, mixer_gain, mixer_project, mixer_output, mixer_saved, second_back[0]
        )
        add_term(grads, "mixer_gain", mixer_back[1])
        add_term(grads, "mixer_project", mixer_back[2])
        add_term(grads, "mixer_output", mixer_back[3])
        first_back = mlp_backward(
            first_mid, first_gain, first_up, first_down, first_saved, mixer_back[0]
        )
        add_term(grads, "first_gain", first_back[1])
        add_term(grads, "first_up", first_back[2])
        add_term(grads, "first_down", first_back[3])
        latent_upstream = first_back[0]
        grad_low = latent_upstream.astype(jnp.bfloat16)
        add_term(grads, "output_weight", product_rows(attended_low, grad_low))
        attended_grad = lax.optimization_barrier(
            product_cols(grad_low, output_weight).astype(jnp.bfloat16)
        ).astype(jnp.float32)
        weighted_grad = (attended_grad / row_total[:, None]).astype(jnp.bfloat16)
        total_grad = -jnp.sum(attended_grad * attended, axis=1) / row_total
        weighted_every, total_every = (
            lax.all_gather(
                weighted_grad.astype(jnp.float32).astype(jnp.bfloat16), "tok", axis=0, tiled=True
            ).astype(jnp.float32),
            lax.all_gather(total_grad.astype(jnp.bfloat16), "tok", axis=0, tiled=True).astype(
                total_grad.dtype
            ),
        )
        weighted_every = weighted_every.astype(jnp.bfloat16)
        scores = jnp.where(allowed, product_cols(queries, key_rows) * scale, NEG)
        unnormed = jnp.exp(scores - row_top[:, None])
        unnormed_grad = product_cols(weighted_every, value_rows) + total_every[:, None]
        score_grad = (unnormed * unnormed_grad).astype(jnp.bfloat16)
        value_grad = product_rows(unnormed.astype(jnp.bfloat16), weighted_every).astype(
            jnp.bfloat16
        )
        key_grad = (product_rows(score_grad, queries) * scale).astype(jnp.bfloat16)
        query_grad = lax.psum_scatter(
            (product_plain(score_grad, key_rows) * scale).astype(jnp.bfloat16),
            "tok",
            scatter_dimension=0,
            tiled=True,
        )
        add_term(grads, "key_weight", product_rows(normed, key_grad))
        add_term(grads, "value_weight", product_rows(normed, value_grad))
        normed_grad = product_cols(key_grad, key_weight) + product_cols(value_grad, value_weight)
        source_grad, gain_grad = norm_back(source, token_gain, normed_grad)
        add_term(grads, "token_gain", gain_grad)
        token_grads.append(source_grad)
        add_term(grads, "query_weight", product_rows(latent_normed, query_grad))
        latent_grad, gain_grad = norm_back(
            latent_in, query_gain, product_cols(query_grad, query_weight)
        )
        add_term(grads, "query_gain", gain_grad)
        latent_grads.append(latent_upstream + latent_grad)
    parts = (
        lax.psum_scatter(
            grads["token_gain"].astype(jnp.bfloat16), "tok", scatter_dimension=0, tiled=True
        ).astype(jnp.float32),
        lax.psum_scatter(
            grads["query_gain"].astype(jnp.bfloat16), "tok", scatter_dimension=0, tiled=True
        ).astype(jnp.float32),
        lax.psum_scatter(
            grads["query_weight"].astype(jnp.bfloat16), "tok", scatter_dimension=0, tiled=True
        ).astype(jnp.float32),
        lax.psum_scatter(
            grads["key_weight"].astype(jnp.bfloat16), "tok", scatter_dimension=0, tiled=True
        ).astype(jnp.float32),
        lax.psum_scatter(
            grads["value_weight"].astype(jnp.bfloat16), "tok", scatter_dimension=0, tiled=True
        ).astype(jnp.float32),
        lax.psum_scatter(
            grads["output_weight"].astype(jnp.bfloat16), "tok", scatter_dimension=0, tiled=True
        ).astype(jnp.float32),
        lax.psum_scatter(
            grads["first_gain"].astype(jnp.bfloat16), "tok", scatter_dimension=0, tiled=True
        ).astype(jnp.float32),
        lax.psum_scatter(
            grads["first_up"].astype(jnp.bfloat16), "tok", scatter_dimension=0, tiled=True
        ).astype(jnp.float32),
        lax.psum_scatter(
            grads["first_down"].astype(jnp.bfloat16), "tok", scatter_dimension=0, tiled=True
        ).astype(jnp.float32),
        lax.psum_scatter(
            grads["mixer_gain"].astype(jnp.bfloat16), "tok", scatter_dimension=0, tiled=True
        ).astype(jnp.float32),
        lax.psum_scatter(
            grads["mixer_project"].astype(jnp.bfloat16), "tok", scatter_dimension=0, tiled=True
        ).astype(jnp.float32),
        lax.psum_scatter(
            grads["mixer_output"].astype(jnp.bfloat16), "tok", scatter_dimension=0, tiled=True
        ).astype(jnp.float32),
        lax.psum_scatter(
            grads["second_gain"].astype(jnp.bfloat16), "tok", scatter_dimension=0, tiled=True
        ).astype(jnp.float32),
        lax.psum_scatter(
            grads["second_up"].astype(jnp.bfloat16), "tok", scatter_dimension=0, tiled=True
        ).astype(jnp.float32),
        lax.psum_scatter(
            grads["second_down"].astype(jnp.bfloat16), "tok", scatter_dimension=0, tiled=True
        ).astype(jnp.float32),
    )
    summed = (
        lax.psum(parts[0].astype(jnp.bfloat16), "grp").astype(jnp.float32),
        lax.psum(parts[1].astype(jnp.bfloat16), "grp").astype(jnp.float32),
        lax.psum(parts[2].astype(jnp.bfloat16), "grp").astype(jnp.float32),
        lax.psum(parts[3].astype(jnp.bfloat16), "grp").astype(jnp.float32),
        lax.psum(parts[4].astype(jnp.bfloat16), "grp").astype(jnp.float32),
        lax.psum(parts[5].astype(jnp.bfloat16), "grp").astype(jnp.float32),
        lax.psum(parts[6].astype(jnp.bfloat16), "grp").astype(jnp.float32),
        lax.psum(parts[7].astype(jnp.bfloat16), "grp").astype(jnp.float32),
        lax.psum(parts[8].astype(jnp.bfloat16), "grp").astype(jnp.float32),
        lax.psum(parts[9].astype(jnp.bfloat16), "grp").astype(jnp.float32),
        lax.psum(parts[10].astype(jnp.bfloat16), "grp").astype(jnp.float32),
        lax.psum(parts[11].astype(jnp.bfloat16), "grp").astype(jnp.float32),
        lax.psum(parts[12].astype(jnp.bfloat16), "grp").astype(jnp.float32),
        lax.psum(parts[13].astype(jnp.bfloat16), "grp").astype(jnp.float32),
        lax.psum(parts[14].astype(jnp.bfloat16), "grp").astype(jnp.float32),
    )
    return (
        jnp.stack(latent_outs)[None],
        jnp.stack(latent_grads)[None],
        jnp.stack(token_grads)[None],
    ) + tuple(summed)


TOK = 8
ROWS = L // TOK
FF = 2048
GR = L // LGROUPS
LOG2E = 1.4426950408889634
LN2 = 0.6931471805599453
F32 = jnp.float32
BF16 = jnp.bfloat16
MIB = 1024 * 1024


def nn(left, right):
    return lax.dot_general(left, right, (((1,), (0,)), ((), ())), preferred_element_type=F32)


def nt(left, right):
    return lax.dot_general(left, right, (((1,), (1,)), ((), ())), preferred_element_type=F32)


def tn(left, right):
    return lax.dot_general(left, right, (((0,), (0,)), ((), ())), preferred_element_type=F32)


def norm_parts(values):
    centre = values - jnp.mean(values, axis=-1, keepdims=True)
    inverse = lax.rsqrt(jnp.mean(centre * centre, axis=-1, keepdims=True) + EPS)
    return centre * inverse, inverse


def norm_pull(hat, inverse, gain, upstream):
    scaled = upstream * gain
    inner = jnp.mean(scaled * hat, axis=-1, keepdims=True)
    grad = (scaled - jnp.mean(scaled, axis=-1, keepdims=True) - hat * inner) * inverse
    return grad, upstream * hat


def places():
    me = lax.axis_index("tok")
    core = lax.rem(me, 2)
    chip = lax.div(me, 2)
    mate = me + 1 - 2 * core
    flip_x = chip + 1 - 2 * lax.rem(chip, 2)
    flip_y = lax.rem(chip + 2, 4)
    far = 3 - chip
    return me, core, chip, mate, (far, flip_x, flip_y)


def remote(src, dst, send_sem, recv_sem, peer):
    return pltpu.make_async_remote_copy(
        src_ref=src,
        dst_ref=dst,
        send_sem=send_sem,
        recv_sem=recv_sem,
        device_id={"tok": peer},
        device_id_type=pl.DeviceIdType.MESH,
    )


def greet(devices):
    barrier = pltpu.get_barrier_semaphore()
    for device in devices:
        pl.semaphore_signal(
            barrier, inc=1, device_id={"tok": device}, device_id_type=pl.DeviceIdType.MESH
        )
    pl.semaphore_wait(barrier, len(devices))


def chip_at(chip, flip):
    high, low = divmod(flip, 2) if isinstance(flip, int) else (lax.div(flip, 2), lax.rem(flip, 2))
    across = lax.rem(lax.rem(chip, 2) + low, 2)
    along = lax.rem(lax.div(chip, 2) + high, 2)
    return 2 * along + across


def mask_loads(seg_ref, mask_ref, seg_buf, mask_buf, sem):
    return (
        pltpu.make_async_copy(seg_ref.at[0], seg_buf, sem.at[0]),
        pltpu.make_async_copy(mask_ref.at[0], mask_buf, sem.at[1]),
    )


def mask_rows(seg_buf, mask_buf, count_ref, bias_ref):
    for member in range(MB):
        scene = lax.broadcasted_iota(jnp.int32, (SCENES, TOK_DEV), 0)
        place = lax.broadcasted_iota(jnp.int32, (SCENES, TOK_DEV), 1)
        hot = jnp.where((seg_buf[member:member + 1] == scene) & (place < count_ref[0, member, 0]), 1.0, 0.0)
        seen = tn(jnp.where(mask_buf[member] > 0, 1.0, 0.0).astype(BF16), hot.astype(BF16))
        bias_ref[member] = jnp.where(seen > 0.5, 0.0, NEG)


def to_rows(first, second):
    rows = first.shape[0]
    lane = lax.broadcasted_iota(jnp.int32, (rows, 128), 1)
    return jnp.where(lane == 0, first, second).T[0:8]


def cross_forward_kernel(
    tok_ref, lat_ref, tgain_ref, qgain_ref, qw_ref, kw_ref, vw_ref, seg_ref, mask_ref, count_ref,
    k_out, v_out, q_out, att_ref, lse_ref,
    tok_buf, lat_buf, keys, values, queries, bias, part, part_s, got, got_s, stage, stage_s,
    arrive, arrive_s, total, seg_buf, mask_buf,
    mask_sem, tok_sem, lat_sem, k_sem, v_sem, q_sem,
    core_send, core_recv, core_send_s, core_recv_s, chip_send, chip_recv, chip_send_s, chip_recv_s,
):
    me, core, chip, mate, others = places()
    span = 2 * ROWS

    def unpack(step):
        return lax.div(step, 4), 3 - lax.rem(step, 4)

    def lat_copy(step):
        member, flip = unpack(step)
        start = pl.multiple_of(chip_at(chip, flip) * span, span)
        return pltpu.make_async_copy(lat_ref.at[0, member, pl.ds(start, span)], lat_buf.at[step], lat_sem.at[step])

    def q_copy(step):
        member, flip = unpack(step)
        start = pl.multiple_of(chip_at(chip, flip) * span, span)
        return pltpu.make_async_copy(queries.at[step], q_out.at[member, pl.ds(start, span)], q_sem.at[step])

    def tok_copy(member):
        return pltpu.make_async_copy(tok_ref.at[0, member], tok_buf.at[member], tok_sem.at[member])

    def kv_copies(member):
        return (
            pltpu.make_async_copy(keys.at[member], k_out.at[member], k_sem.at[member]),
            pltpu.make_async_copy(values.at[member], v_out.at[member], v_sem.at[member]),
        )

    def core_copies(step):
        return (
            remote(part.at[step, 1 - core], got.at[step], core_send.at[step], core_recv.at[step], mate),
            remote(part_s.at[step, 1 - core], got_s.at[step], core_send_s.at[step], core_recv_s.at[step], mate),
        )

    def chip_copies(step):
        member, flip = unpack(step)
        peer = 2 * chip_at(chip, flip) + core
        place = 3 * member + flip - 1
        return (
            remote(stage.at[step], arrive.at[place], chip_send.at[place], chip_recv.at[place], peer),
            remote(stage_s.at[step], arrive_s.at[place], chip_send_s.at[place], chip_recv_s.at[place], peer),
        )

    tok_copy(0).start()
    masks = mask_loads(seg_ref, mask_ref, seg_buf, mask_buf, mask_sem)
    for copy in masks:
        copy.start()
    for step in range(4):
        lat_copy(step).start()
    tok_copy(1).start()
    for step in range(4, 2 * 4):
        lat_copy(step).start()
    greet([mate] + [2 * other + core for other in others])
    for copy in masks:
        copy.wait()
    mask_rows(seg_buf, mask_buf, count_ref, bias)

    def project(member):
        tok_copy(member).wait()
        hat, inverse = norm_parts(tok_buf[member].astype(F32))
        normed = (hat * tgain_ref[...]).astype(BF16)
        keys[member] = nn(normed, kw_ref[...]).astype(BF16)
        values[member] = nn(normed, vw_ref[...]).astype(BF16)
        for copy in kv_copies(member):
            copy.start()

    def ask(step):
        hat, inverse = norm_parts(lat_buf[step])
        normed = (hat * qgain_ref[...]).astype(BF16)
        queries[step] = (nn(normed, qw_ref[...]) * (D ** (-0.5) * LOG2E)).astype(BF16)

    def compute(step, ahead):
        member, flip = unpack(step)

        @pl.when(flip == 3)
        def _():
            project(member)

        if ahead:
            lat_copy(step + 1).wait()
        scores = nt(queries[step], keys[member])
        if ahead:
            ask(step + 1)
        raised = []
        for half in range(2):
            seen = bias[member, pl.ds(2 * chip_at(chip, flip) + half, 1), :]
            own = scores[half * ROWS:(half + 1) * ROWS] + seen
            top = jnp.max(own, axis=1, keepdims=True)
            own = jnp.exp2(own - top)
            part_s[step, half] = to_rows(top, jnp.sum(own, axis=1, keepdims=True))
            raised.append(own.astype(BF16))
        sums = nn(jnp.concatenate(raised, axis=0), values[member]).astype(BF16)
        for half in range(2):
            part[step, half] = sums[half * ROWS:(half + 1) * ROWS]
        for copy in core_copies(step):
            copy.start()
        if ahead:
            q_copy(step + 1).start()

    def merge(one, one_s, two, two_s):
        top = jnp.maximum(one_s[0:1], two_s[0:1])
        one_w, two_w = jnp.exp2(one_s[0:1] - top), jnp.exp2(two_s[0:1] - top)
        sums = one_s[1:2] * one_w + two_s[1:2] * two_w
        spare = jnp.zeros((6, ROWS), F32)
        weights = jnp.concatenate([one_w, two_w, spare], axis=0).T
        return one * weights[:, 0:1] + two * weights[:, 1:2], jnp.concatenate([top, sums, spare], axis=0)

    def combine(step):
        member, flip = unpack(step)
        for copy in core_copies(step):
            copy.wait_recv()
        added, figures = merge(
            part[step, core].astype(F32), part_s[step, core], got[step].astype(F32), got_s[step]
        )
        stage_s[step] = figures

        @pl.when(flip > 0)
        def _():
            stage[step] = added.astype(BF16)
            for copy in chip_copies(step):
                copy.start()

        @pl.when(flip == 0)
        def _():
            total[member] = added

    def finish(member):
        added, figures = total[member], stage_s[4 * member + 3]
        for flip in (1, 2, 3):
            for copy in chip_copies(4 * member + 3 - flip):
                copy.wait_recv()
            place = 3 * member + flip - 1
            added, figures = merge(added, figures, arrive[place].astype(F32), arrive_s[place])
        spare = jnp.zeros((7, ROWS), F32)
        inverse = jnp.concatenate([1.0 / figures[1:2], spare], axis=0).T
        att_ref[member] = added * inverse[:, 0:1]
        lse_ref[member] = jnp.concatenate([figures[0:1] + jnp.log2(figures[1:2]), spare], axis=0)

    def step_body(step, carry):
        compute(step, True)

        @pl.when(step > 0)
        def _():
            combine(step - 1)

        return carry

    last = jnp.int32(4 * MB - 1)
    lat_copy(jnp.int32(0)).wait()
    ask(0)
    q_copy(jnp.int32(0)).start()
    lax.fori_loop(0, 4 * MB - 1, step_body, 0)
    compute(last, False)
    combine(last - 1)
    combine(last)
    for member in range(MB):
        finish(member)
    for member in range(MB):
        for copy in kv_copies(member):
            copy.wait()
        for slot in range(4):
            step = 4 * member + slot
            q_copy(step).wait()
            for copy in core_copies(step):
                copy.wait_send()
            if slot < 3:
                for copy in chip_copies(step):
                    copy.wait_send()


def cross_forward(collective_id, *args):
    dma = pltpu.SemaphoreType.DMA
    span = 2 * ROWS
    steps = 4 * MB
    vmem = pl.BlockSpec(memory_space=pltpu.VMEM)
    hbm = pl.BlockSpec(memory_space=pl.ANY)
    return pl.pallas_call(
        cross_forward_kernel,
        in_specs=[hbm, hbm] + [vmem] * 5 + [hbm, hbm, pl.BlockSpec(memory_space=pltpu.SMEM)],
        out_specs=[hbm, hbm, hbm, vmem, vmem],
        out_shape=[
            jax.ShapeDtypeStruct((MB, TOK_DEV, D), BF16),
            jax.ShapeDtypeStruct((MB, TOK_DEV, D), BF16),
            jax.ShapeDtypeStruct((MB, L, D), BF16),
            jax.ShapeDtypeStruct((MB, ROWS, D), F32),
            jax.ShapeDtypeStruct((MB, 8, ROWS), F32),
        ],
        scratch_shapes=[
            pltpu.VMEM((MB, TOK_DEV, D), BF16),
            pltpu.VMEM((steps, span, D), F32),
            pltpu.VMEM((MB, TOK_DEV, D), BF16),
            pltpu.VMEM((MB, TOK_DEV, D), BF16),
            pltpu.VMEM((steps, span, D), BF16),
            pltpu.VMEM((MB, LGROUPS, TOK_DEV), F32),
            pltpu.VMEM((steps, 2, ROWS, D), BF16),
            pltpu.VMEM((steps, 2, 8, ROWS), F32),
            pltpu.VMEM((steps, ROWS, D), BF16),
            pltpu.VMEM((steps, 8, ROWS), F32),
            pltpu.VMEM((steps, ROWS, D), BF16),
            pltpu.VMEM((steps, 8, ROWS), F32),
            pltpu.VMEM((3 * MB, ROWS, D), BF16),
            pltpu.VMEM((3 * MB, 8, ROWS), F32),
            pltpu.VMEM((MB, ROWS, D), F32),
            pltpu.VMEM((MB, TOK_DEV), jnp.int32),
            pltpu.VMEM((MB, SCENES, LGROUPS), jnp.int32),
            dma((2,)), dma((MB,)), dma((steps,)), dma((MB,)), dma((MB,)), dma((steps,)),
        ] + [dma((steps,))] * 4 + [dma((3 * MB,))] * 4,
        compiler_params=pltpu.CompilerParams(
            collective_id=collective_id, has_side_effects=True, vmem_limit_bytes=56 * MIB
        ),
        cost_estimate=pl.CostEstimate(
            flops=14 * 10**9, bytes_accessed=22 * 10**6, transcendentals=4 * 10**6
        ),
        name="cross_forward",
    )(*args)


def cross_backward_kernel(
    items, grad_items,
    tok_ref, tgain_ref, kw_ref, vw_ref, seg_ref, mask_ref, count_ref, k_ref, v_ref, q_ref, up_ref, fig_ref,
    lat_ref, lup_ref, qgain_ref, qw_ref, fgain_ref, mgain_ref, sgain_ref, *refs,
):
    count, more = len(items), len(grad_items)
    parts, sources = refs[:count], refs[count:count + more]
    refs = refs[count + more:]
    dlat_ref, dtok_ref, dkw_ref, dvw_ref, dqw_ref, gains_ref = refs[:6]
    sums, helds = refs[6:6 + count], refs[6 + count:6 + count + more]
    rest = refs[6 + count + more:]
    cut = CROSS_SCRATCH + 3 * count + 2
    grp, grp_devices = grp_steps(items, parts, (), rest[CROSS_SCRATCH:cut], sums)
    tok, near_devices = tok_steps(grad_items, sources, rest[cut:])
    (tok_buf, keys, values, queries, ups, figs, bias, part, got, stage, arrive, far_in, total, dk, dv, dkw, dvw,
     dgain_ref, lat, lup, seg_buf, mask_buf, mask_sem, tail_sem,
     tok_sem, k_sem, v_sem, q_sem, out_sem, near_send, near_recv, far_send, far_recv, on_send, on_recv, own_sem,
     fig_send, fig_recv, core_send, core_recv, chip_send, chip_recv, half_send, half_recv) = rest[:CROSS_SCRATCH]
    me, core, chip, mate, others = places()
    span = 2 * ROWS

    def slot_of(step):
        late = lax.div(step + 3, 8)
        member = jnp.where(step == 1, 1, late)
        flip = jnp.where(step < 2, 0, jnp.where(late == 0, step - 1, 8 - step))
        return member, flip

    def loads(step):
        member, flip = slot_of(step)
        start = pl.multiple_of(chip_at(chip, flip) * span, span)
        ring = lax.rem(step, 4)
        return pltpu.make_async_copy(q_ref.at[member, pl.ds(start, span)], queries.at[ring], q_sem.at[ring])

    def tok_copies(member):
        return (
            pltpu.make_async_copy(k_ref.at[member], keys.at[member], k_sem.at[member]),
            pltpu.make_async_copy(v_ref.at[member], values.at[member], v_sem.at[member]),
            pltpu.make_async_copy(tok_ref.at[0, member], tok_buf.at[member], tok_sem.at[member]),
        )

    def out_copy(member):
        return pltpu.make_async_copy(dk.at[member], dtok_ref.at[0, member], out_sem.at[member])

    def own_copies(member):
        slot = 4 * member
        return (
            pltpu.make_async_copy(up_ref.at[member], ups.at[slot, core], own_sem.at[member, 0]),
            pltpu.make_async_copy(fig_ref.at[member], figs.at[slot, core], own_sem.at[member, 1]),
        )

    def near_copies(member):
        slot = 4 * member
        return [
            remote(up_ref.at[member], ups.at[slot, core], near_send.at[member, 0], near_recv.at[member, 0], mate),
            remote(fig_ref.at[member], figs.at[slot, core], near_send.at[member, 1], near_recv.at[member, 1], mate),
        ]

    half_rows = (pl.ds(0, ROWS // 2), pl.ds(ROWS // 2, ROWS // 2))

    def far_copies(slot):
        member, flip = slot // 4, slot % 4
        peer = 2 * chip_at(chip, flip) + core
        if flip < 3:
            return [
                remote(up_ref.at[member], ups.at[slot, core], far_send.at[slot, 0], far_recv.at[slot, 0], peer),
                remote(fig_ref.at[member], figs.at[slot, core], far_send.at[slot, 1], far_recv.at[slot, 1], peer),
            ]
        copies = []
        for half, (held, toward) in enumerate(((1, 2), (2, 1))):
            copies.append(remote(
                ups.at[4 * member + held, core, half_rows[half]], ups.at[slot, core, half_rows[half]],
                far_send.at[slot, half], far_recv.at[slot, half], 2 * chip_at(chip, toward) + core,
            ))
        copies.append(remote(
            figs.at[4 * member + 1, core], figs.at[slot, core], fig_send.at[member], fig_recv.at[member],
            2 * chip_at(chip, 2) + core,
        ))
        return copies

    def on_copies(slot):
        return (
            remote(ups.at[slot, core], ups.at[slot, core], on_send.at[slot, 0], on_recv.at[slot, 0], mate),
            remote(figs.at[slot, core], figs.at[slot, core], on_send.at[slot, 1], on_recv.at[slot, 1], mate),
        )

    def pass_on(slot):
        for copy in far_copies(slot):
            copy.wait_recv()
        for copy in on_copies(slot):
            copy.start()

    def pass_near(member):
        pass_on(4 * member + 1)
        pass_on(4 * member + 2)
        for copy in far_copies(4 * member + 3):
            copy.start()

    def half_copy(member, half):
        return remote(
            stage.at[4 * member + 3, half_rows[half]], far_in.at[member, half], half_send.at[member, half],
            half_recv.at[member, half], 2 * chip_at(chip, half + 1) + core,
        )

    def half_copies(member):
        return [half_copy(member, half) for half in range(2)]

    def core_copy(step):
        member, flip = slot_of(step)
        slot, ring = 4 * member + flip, lax.rem(step, 4)
        return remote(part.at[ring, 1 - core], got.at[slot], core_send.at[slot], core_recv.at[slot], mate)

    def chip_copy(slot):
        member, flip = slot // 4, slot % 4
        peer = 2 * chip_at(chip, flip) + core
        place = 2 * member + flip - 1
        return remote(stage.at[slot], arrive.at[place], chip_send.at[place], chip_recv.at[place], peer)

    def relay(member):
        for half in range(2):
            half_copy(member, half).wait_recv()
            slot = 4 * member + 2 - half
            joined = stage.at[slot, half_rows[half]]
            add(joined, joined, far_in.at[member, half])
            chip_copy(slot).start()

    masks = mask_loads(seg_ref, mask_ref, seg_buf, mask_buf, mask_sem)
    for copy in masks:
        copy.start()
    own_rows = pl.ds(pl.multiple_of(me * ROWS, ROWS), ROWS)
    tails = (
        pltpu.make_async_copy(lat_ref.at[0, :, own_rows], lat, tail_sem.at[0]),
        pltpu.make_async_copy(lup_ref, lup, tail_sem.at[1]),
    )
    for copy in own_copies(0):
        copy.start()
    for copy in tok_copies(0):
        copy.start()
    for step in range(3):
        loads(jnp.int32(step)).start()
    for copy in own_copies(1):
        copy.start()
    for copy in tok_copies(1):
        copy.start()
    for copy in tails:
        copy.start()
    greet_all([mate] + [2 * other + core for other in others], grp_devices)
    for member in range(MB):
        for copy in near_copies(member):
            copy.start()
    for flip in (1, 2):
        for copy in far_copies(flip):
            copy.start()
    tok[0](0)
    for item in range(count):
        grp[0](item)
    for copy in masks:
        copy.wait()
    mask_rows(seg_buf, mask_buf, count_ref, bias)

    def compute(step):
        member, flip = slot_of(step)
        slot = 4 * member + flip

        @pl.when(step < 2)
        def _():
            for copy in tok_copies(member):
                copy.wait()
            dk[member] = jnp.zeros((TOK_DEV, D), F32)
            dv[member] = jnp.zeros((TOK_DEV, D), F32)

        loads(step).wait()

        @pl.when(step + 3 < 4 * MB)
        def _():
            loads(step + 3).start()

        @pl.when(flip == 0)
        def _():
            for copy in own_copies(member):
                copy.wait()
            for copy in near_copies(member):
                copy.wait_recv()

        @pl.when(flip > 0)
        def _():
            for copy in on_copies(slot):
                copy.wait_recv()

        asked = queries[lax.rem(step, 4)]
        upstream = ups[slot].reshape(span, D)
        scores = nt(asked, keys[member])
        soft = nt(upstream, values[member])
        weights, grads = [], []
        for half in range(2):
            seen = bias[member, pl.ds(2 * chip_at(chip, flip) + half, 1), :]
            figures = figs[slot, half].T
            rows = slice(half * ROWS, (half + 1) * ROWS)
            weight = jnp.exp2(scores[rows] + seen - figures[:, 0:1])
            grads.append((weight * (soft[rows] - figures[:, 1:2])).astype(BF16))
            weights.append(weight.astype(BF16))
        weight = jnp.concatenate(weights, axis=0)
        grad = jnp.concatenate(grads, axis=0)
        middle(step)
        dv[member] += tn(weight, upstream)
        dk[member] += tn(grad, asked)
        asked_grad = (nn(grad, keys[member]) * D ** (-0.5)).astype(BF16)

        @pl.when(step >= 4)
        def _():
            core_copy(step - 4).wait_send()

        for half in range(2):
            part[lax.rem(step, 4), half] = asked_grad[half * ROWS:(half + 1) * ROWS]
        core_copy(step).start()

    def combine(step):
        member, flip = slot_of(step)
        slot = 4 * member + flip
        core_copy(step).wait_recv()
        added = part[lax.rem(step, 4), core].astype(F32) + got[slot].astype(F32)

        @pl.when(flip > 0)
        def _():
            stage[slot] = added.astype(BF16)

        @pl.when(flip == 0)
        def _():
            total[member] = added

    def tokens_back(member, half):
        gain = tgain_ref[...]
        rows = pl.ds(pl.multiple_of(half * span, span), span)
        hat, inverse = norm_parts(tok_buf[member, rows].astype(F32))
        normed = (hat * gain).astype(BF16)
        key_grad = (dk[member, rows] * LN2).astype(BF16)
        value_grad = dv[member, rows].astype(BF16)
        dkw[...] += tn(normed, key_grad)
        dvw[...] += tn(normed, value_grad)
        normed_grad = nt(key_grad, kw_ref[...]) + nt(value_grad, vw_ref[...])
        source_grad, gain_rows = norm_pull(hat, inverse, gain, normed_grad)
        dk[member, rows] = source_grad
        dgain_ref[...] += jnp.sum(gain_rows, axis=0, keepdims=True)

    def hold(item):
        helds[item][...] = tok[4](item).astype(helds[item].dtype)

    def middle(step):
        @pl.when(step > 0)
        def _():
            combine(step - 1)

        @pl.when(step == 1)
        def _():
            pass_near(0)

        @pl.when(step == 3)
        def _():
            pass_on(3)
            pass_near(1)

        @pl.when(step == 5)
        def _():
            for copy in half_copies(0):
                copy.start()

        @pl.when(step == 6)
        def _():
            for copy in half_copies(1):
                copy.start()
            relay(0)

    def step_body(step, carry):
        compute(step)

        @pl.when(step == 0)
        def _():
            for flip in (1, 2):
                for copy in far_copies(4 + flip):
                    copy.start()
            tok[1](0)
            tok[0](1)

        @pl.when(step == 1)
        def _():
            tok[0](2)

        @pl.when(step == 2)
        def _():
            tok[1](1)

        @pl.when(step == 4)
        def _():
            pass_on(7)
            for item in range(count):
                grp[4](item)
            tok[2](0)
            tok[1](2)

        @pl.when(step == 6)
        def _():
            tok[3](0)

        @pl.when(step == 4 * MB - 1)
        def _():
            combine(step)
            relay(1)

        return carry

    lax.fori_loop(0, 4 * MB, step_body, 0)

    def tokens_body(member, carry):
        for half in range(TOK_DEV // span):
            tokens_back(member, half)
        out_copy(member).start()

        @pl.when(member == 0)
        def _():
            helds[1][...] = tok[6](1)

        return carry

    dkw[...] = jnp.zeros_like(dkw)
    dvw[...] = jnp.zeros_like(dvw)
    dgain_ref[...] = jnp.zeros_like(dgain_ref)
    lax.fori_loop(0, MB, tokens_body, 0)
    dkw_ref[...] = dkw[...].astype(BF16)
    dvw_ref[...] = dvw[...].astype(BF16)
    hold(0)
    helds[2][...] = tok[6](2)
    for copy in tails:
        copy.wait()
    gain = qgain_ref[...]
    hat, inverse = norm_parts(lat[...].reshape(MB * ROWS, D))
    normed = (hat * gain).astype(BF16)
    asked_grads = []
    for member in range(MB):
        added = total[member]
        for flip in (1, 2):
            chip_copy(4 * member + flip).wait_recv()
            added = added + arrive[2 * member + flip - 1].astype(F32)
        asked_grads.append(added.astype(BF16))
    asked_grad = jnp.concatenate(asked_grads, axis=0)
    dqw_ref[...] = tn(normed, asked_grad).astype(BF16)
    source_grad, gain_rows = norm_pull(hat, inverse, gain, nt(asked_grad, qw_ref[...]))
    lup[...] += source_grad
    last = pltpu.make_async_copy(lup, dlat_ref, tail_sem.at[2])
    last.start()
    query_gain = jnp.sum(gain_rows, axis=0, keepdims=True)
    rows = jnp.concatenate(
        [dgain_ref[...], query_gain, fgain_ref[...], mgain_ref[...], sgain_ref[...], jnp.zeros((3, D), F32)], axis=0
    )
    gains_ref[...] = jnp.zeros_like(gains_ref)
    width = D // TOK
    for device in range(TOK):
        gains_ref[16 * device:16 * device + 8, 0:width] = rows[:, device * width:(device + 1) * width]
    grp[3]((0,))
    tok[5]((1, 2))
    last.wait()
    for step in range(4, 4 * MB):
        core_copy(jnp.int32(step)).wait_send()
    for member in range(MB):
        out_copy(member).wait()
        for copy in near_copies(member) + half_copies(member):
            copy.wait_send()
        for flip in range(4):
            slot = 4 * member + flip
            if flip > 0:
                for copy in far_copies(slot):
                    copy.wait_send()
                for copy in on_copies(slot):
                    copy.wait_send()
            if flip in (1, 2):
                chip_copy(slot).wait_send()


CROSS_SCRATCH = 44


def cross_backward(collective_id, arrays, grads, *args):
    dma = pltpu.SemaphoreType.DMA
    span = 2 * ROWS
    steps = 4 * MB
    vmem = pl.BlockSpec(memory_space=pltpu.VMEM)
    hbm = pl.BlockSpec(memory_space=pl.ANY)
    smem = pl.BlockSpec(memory_space=pltpu.SMEM)
    items, kinds = held_plan(arrays)
    sources, grad_items, grad_kinds, shapes = reduce_plan(grads)
    scratch = [
        pltpu.VMEM((MB, TOK_DEV, D), BF16),
        pltpu.VMEM((MB, TOK_DEV, D), BF16),
        pltpu.VMEM((MB, TOK_DEV, D), BF16),
        pltpu.VMEM((4, span, D), BF16),
        pltpu.VMEM((steps, 2, ROWS, D), BF16),
        pltpu.VMEM((steps, 2, 8, ROWS), F32),
        pltpu.VMEM((MB, LGROUPS, TOK_DEV), F32),
        pltpu.VMEM((4, 2, ROWS, D), BF16),
        pltpu.VMEM((steps, ROWS, D), BF16),
        pltpu.VMEM((steps, ROWS, D), BF16),
        pltpu.VMEM((2 * MB, ROWS, D), BF16),
        pltpu.VMEM((MB, 2, ROWS // 2, D), BF16),
        pltpu.VMEM((MB, ROWS, D), F32),
        pltpu.VMEM((MB, TOK_DEV, D), F32),
        pltpu.VMEM((MB, TOK_DEV, D), F32),
        pltpu.VMEM((D, D), F32),
        pltpu.VMEM((D, D), F32),
        pltpu.VMEM((1, D), F32),
        pltpu.VMEM((MB, ROWS, D), F32),
        pltpu.VMEM((MB * ROWS, D), F32),
        pltpu.VMEM((MB, TOK_DEV), jnp.int32),
        pltpu.VMEM((MB, SCENES, LGROUPS), jnp.int32),
        dma((2,)), dma((3,)),
        dma((MB,)), dma((MB,)), dma((MB,)), dma((4,)), dma((MB,)),
        dma((MB, 2)), dma((MB, 2)), dma((steps, 2)), dma((steps, 2)), dma((steps, 2)), dma((steps, 2)), dma((MB, 2)),
        dma((MB,)), dma((MB,)),
        dma((steps,)), dma((steps,)), dma((2 * MB,)), dma((2 * MB,)), dma((MB, 2)), dma((MB, 2)),
    ]
    return pl.pallas_call(
        functools.partial(cross_backward_kernel, items, grad_items),
        in_specs=[hbm] + [vmem] * 3 + [hbm, hbm, smem] + [hbm] * 7 + [vmem] * 5 + [vmem] * len(arrays) + [hbm] * len(grads),
        out_specs=[hbm, hbm] + [vmem] * (4 + len(arrays) + len(grads)),
        out_shape=[
            jax.ShapeDtypeStruct((MB * ROWS, D), F32),
            jax.ShapeDtypeStruct((1, MB, TOK_DEV, D), F32),
            jax.ShapeDtypeStruct((D, D), BF16),
            jax.ShapeDtypeStruct((D, D), BF16),
            jax.ShapeDtypeStruct((D, D), BF16),
            jax.ShapeDtypeStruct((16 * TOK, 128), F32),
        ] + [jax.ShapeDtypeStruct(array.shape, array.dtype) for array in arrays]
        + [
            jax.ShapeDtypeStruct((() if i == 0 else (2, 2)) + (high // 2, wide), kind)
            for i, ((high, wide), kind) in enumerate(zip(shapes, grad_kinds))
        ],
        scratch_shapes=scratch + grp_scratch(items, kinds) + tok_scratch(grad_items, grad_kinds),
        compiler_params=pltpu.CompilerParams(
            collective_id=collective_id, has_side_effects=True, vmem_limit_bytes=60 * MIB
        ),
        cost_estimate=pl.CostEstimate(
            flops=26 * 10**9, bytes_accessed=24 * 10**6, transcendentals=4 * 10**6
        ),
        name="cross_backward",
    )(*args, *arrays, *sources)


GELU_A = 0.7978845608028654
GELU_B = 0.044715


def gelu_parts(hidden):
    square = hidden * hidden
    bent = jnp.tanh(GELU_A * hidden * (1.0 + GELU_B * square))
    half = 0.5 * (1.0 + bent)
    slope = half + 0.5 * hidden * (1.0 - bent * bent) * (GELU_A * (1.0 + 3.0 * GELU_B * square))
    return hidden * half, slope


def greet_all(tok_devices, grp_devices=()):
    barrier = pltpu.get_barrier_semaphore()
    for axis, devices in (("tok", tok_devices), ("grp", grp_devices)):
        for device in devices:
            pl.semaphore_signal(
                barrier, inc=1, device_id={axis: device}, device_id_type=pl.DeviceIdType.MESH
            )
    pl.semaphore_wait(barrier, len(tok_devices) + len(grp_devices))


def all_peers():
    me, core, chip, mate, others = places()
    peers = []
    for other in others:
        peers += [2 * other + core, 2 * other + 1 - core]
    return me, peers + [mate]


def head_copies(row_side, head_side, to_heads, member, me, peers, send, recv, local):
    lanes = pl.ds(member * ROWS, ROWS)
    row_at = lambda device: row_side.at[:, device, :, lanes]
    head_at = lambda device: head_side.at[:, member, :, pl.ds(pl.multiple_of(device * ROWS, ROWS), ROWS)]
    source, target = (row_at, head_at) if to_heads else (head_at, row_at)
    copies = [
        remote(source(peer), target(me), send.at[slot, member], recv.at[slot, member], peer)
        for slot, peer in enumerate(peers)
    ]
    return copies, pltpu.make_async_copy(source(me), target(me), local.at[member])


QB = 1024
QB_BACK = 256


def latents_forward_kernel(
    lat_ref, att_ref, cot_ref, ow_ref, fgain_ref, fup_ref, fdown_ref, mgain_ref, proj_ref, mow_ref, sgain_ref,
    sup_ref, sdown_ref,
    out_ref, fmid_ref, mmid_ref, packed_ref, exact_ref, lse_ref, up_ref, mgrad_ref, ddown_ref, dup_ref, dmo_ref,
    dgain_ref,
    lat, att, cot, ow, fup, fdown, proj, mow, sup, sdown,
    out, fmid, mmid, heads, exact, up, mgrad, ddown, dup, dmo,
    rows_out, keys, values, mixed, mixed_rows, active, hidden_low, normed_low,
    load_sem, store_sem, send_a, recv_a, local_a, send_b, recv_b, local_b,
):
    me, peers = all_peers()
    own = pl.ds(pl.multiple_of(me * ROWS, ROWS), ROWS)
    names = ("lat", "att", "ow", "fup", "fdown", "proj", "mow", "sup", "sdown", "cot")
    loads = {}
    for i, (source, target) in enumerate((
        (lat_ref.at[0, :, own], lat), (att_ref, att), (ow_ref, ow), (fup_ref, fup), (fdown_ref, fdown),
        (proj_ref, proj), (mow_ref, mow), (sup_ref, sup), (sdown_ref, sdown), (cot_ref.at[0], cot),
    )):
        loads[names[i]] = pltpu.make_async_copy(source, target, load_sem.at[i])
        loads[names[i]].start()
    stores = []

    def store(source, target):
        stores.append(pltpu.make_async_copy(source, target, store_sem.at[len(stores)]))
        stores[-1].start()

    greet_all(peers)
    flat = (MB * ROWS, D)
    for name in ("lat", "att", "ow"):
        loads[name].wait()
    outward = [head_copies(rows_out, heads, True, member, me, peers, send_a, recv_a, local_a) for member in range(MB)]
    backward = [
        head_copies(mixed_rows, mixed, False, member, me, peers, send_b, recv_b, local_b) for member in range(MB)
    ]
    for member in range(MB):
        rows = slice(member * ROWS, (member + 1) * ROWS)
        first = lat[member] + nn(att[member].astype(BF16), ow[...])
        fmid[rows] = first
        normed = (norm_parts(first)[0] * fgain_ref[...]).astype(BF16)
        if member == 0:
            loads["fup"].wait()
            loads["fdown"].wait()
        mid = first
        for part in range(2):
            cut = slice(part * FF // 2, (part + 1) * FF // 2)
            mid = mid + nn(jax.nn.gelu(nn(normed, fup[:, cut])).astype(BF16), fdown[cut])
        mmid[rows] = mid
        normed = (norm_parts(mid)[0] * mgain_ref[...]).astype(BF16).T
        if member == 0:
            loads["proj"].wait()
        for kind, scale in enumerate((HD ** (-0.5) * LOG2E, 1.0, 1.0)):
            packed = tn(proj[:, kind * D:(kind + 1) * D], normed) * scale
            rows_out[kind, :, :, rows] = packed.astype(BF16).reshape(H, HD, ROWS)
        copies, here = outward[member]
        for copy in copies:
            copy.start()
        here.start()
    store(fmid, fmid_ref)
    store(mmid, mmid_ref)
    for member in range(MB):
        copies, here = outward[member]
        for copy in copies:
            copy.wait_recv()
        here.wait()
        store(heads.at[:, member], packed_ref.at[:, member])
        keys[...] = heads[1, member].T
        values[0:HD] = heads[2, member]
        values[HD:] = jnp.ones((16, L), BF16)

        def attend(step, carry, member=member):
            at = pl.ds(pl.multiple_of(step * QB, QB), QB)
            logits = nn(keys[...], heads[0, member, :, at])
            top = jnp.max(logits, axis=0, keepdims=True)
            both = nn(values[...], jnp.exp2(logits - top).astype(BF16))
            total = both[HD:HD + 1]
            result = both[0:HD] / total
            exact[member, :, at] = result
            mixed[0, member, :, at] = result.astype(BF16)
            lse_ref[member, :, at] = jnp.broadcast_to(top + jnp.log2(total), (8, QB))
            return carry

        lax.fori_loop(0, L // QB, attend, 0)
        for copy in backward[member][0] + [backward[member][1]]:
            copy.start()
    store(exact, exact_ref)
    loads["mow"].wait()
    loads["sup"].wait()
    loads["sdown"].wait()
    loads["cot"].wait()
    gains = []
    for member in range(MB):
        copies, here = backward[member]
        for copy in copies:
            copy.wait_recv()
        here.wait()
        rows = slice(member * ROWS, (member + 1) * ROWS)
        second = mmid[rows] + tn(mixed_rows[0, :, :, rows].reshape(D, ROWS), mow[...])
        hat, inverse = norm_parts(second)
        normed = (hat * sgain_ref[...]).astype(BF16)
        normed_low[rows] = normed
        upstream = cot[member]
        grad = upstream.astype(BF16)
        final = second
        normed_grad = jnp.zeros((ROWS, D), F32)
        for part in range(2):
            cut = slice(part * FF // 2, (part + 1) * FF // 2)
            act, slope = gelu_parts(nn(normed, sup[:, cut]))
            act = act.astype(BF16)
            active[rows, cut] = act
            final = final + nn(act, sdown[cut])
            hidden_grad = (slope * nt(grad, sdown[cut])).astype(BF16)
            hidden_low[rows, cut] = hidden_grad
            normed_grad = normed_grad + nt(hidden_grad, sup[:, cut])
        out[member] = final
        residual, gain_rows = norm_pull(hat, inverse, sgain_ref[...], normed_grad)
        gains.append(jnp.sum(gain_rows, axis=0, keepdims=True))
        upstream = upstream + residual
        up[rows] = upstream
        mgrad[0, :, :, rows] = nt(mow[...], upstream.astype(BF16)).astype(BF16).reshape(H, HD, ROWS)
    store(out, out_ref.at[0])
    store(up, up_ref)
    store(mgrad, mgrad_ref)
    dgain_ref[...] = gains[0] + gains[1]
    ddown[...] = tn(active[...], cot[...].reshape(flat).astype(BF16)).astype(BF16)
    store(ddown, ddown_ref)
    dup[...] = tn(normed_low[...], hidden_low[...]).astype(BF16)
    store(dup, dup_ref)
    dmo[...] = nn(mixed_rows[0].reshape(D, MB * ROWS), up[...].astype(BF16)).astype(BF16)
    store(dmo, dmo_ref)
    for copy in stores:
        copy.wait()
    for copies, here in outward + backward:
        for copy in copies:
            copy.wait_send()


def latents_forward(collective_id, *args):
    dma = pltpu.SemaphoreType.DMA
    vmem = pl.BlockSpec(memory_space=pltpu.VMEM)
    hbm = pl.BlockSpec(memory_space=pl.ANY)
    rows = MB * ROWS
    stored = [
        ((1, MB, ROWS, D), F32), ((rows, D), F32), ((rows, D), F32), ((3, MB, HD, L), BF16), ((MB, HD, L), F32),
        ((MB, 8, L), F32), ((rows, D), F32), ((1, H, HD, rows), BF16), ((FF, D), BF16), ((D, FF), BF16), ((D, D), BF16),
        ((1, D), F32),
    ]
    return pl.pallas_call(
        latents_forward_kernel,
        in_specs=[hbm, hbm, hbm, hbm, vmem, hbm, hbm, vmem, hbm, hbm, vmem, hbm, hbm],
        out_specs=[hbm] * 5 + [vmem] + [hbm] * 5 + [vmem],
        out_shape=[jax.ShapeDtypeStruct(shape, kind) for shape, kind in stored],
        scratch_shapes=[
            pltpu.VMEM((MB, ROWS, D), F32), pltpu.VMEM((MB, ROWS, D), F32), pltpu.VMEM((MB, ROWS, D), F32),
            pltpu.VMEM((D, D), BF16), pltpu.VMEM((D, FF), BF16), pltpu.VMEM((FF, D), BF16),
            pltpu.VMEM((D, 3 * D), BF16), pltpu.VMEM((D, D), BF16), pltpu.VMEM((D, FF), BF16),
            pltpu.VMEM((FF, D), BF16),
            pltpu.VMEM((MB, ROWS, D), F32), pltpu.VMEM((rows, D), F32), pltpu.VMEM((rows, D), F32),
            pltpu.VMEM((3, MB, HD, L), BF16), pltpu.VMEM((MB, HD, L), F32), pltpu.VMEM((rows, D), F32),
            pltpu.VMEM((1, H, HD, rows), BF16), pltpu.VMEM((FF, D), BF16), pltpu.VMEM((D, FF), BF16),
            pltpu.VMEM((D, D), BF16),
            pltpu.VMEM((3, H, HD, rows), BF16), pltpu.VMEM((L, HD), BF16), pltpu.VMEM((HD + 16, L), BF16),
            pltpu.VMEM((1, MB, HD, L), BF16), pltpu.VMEM((1, H, HD, rows), BF16),
            pltpu.VMEM((rows, FF), BF16), pltpu.VMEM((rows, FF), BF16), pltpu.VMEM((rows, D), BF16),
            dma((10,)), dma((11,)), dma((7, MB)), dma((7, MB)), dma((MB,)), dma((7, MB)), dma((7, MB)), dma((MB,)),
        ],
        compiler_params=pltpu.CompilerParams(
            collective_id=collective_id, has_side_effects=True, vmem_limit_bytes=60 * MIB
        ),
        cost_estimate=pl.CostEstimate(
            flops=20 * 10**9, bytes_accessed=30 * 10**6, transcendentals=10 * 10**6
        ),
        name="latents_forward",
    )(*args)


def levels():
    level = lax.axis_index("grp")
    odd = lax.rem(level, 2)
    return odd, level + 1 - 2 * odd, lax.rem(level + 2, 4)


def half_slices(rows, odd):
    half = rows // 2
    keep = pl.ds(pl.multiple_of(odd * half, half), half)
    away = pl.ds(pl.multiple_of((1 - odd) * half, half), half)
    return keep, away


def tok_steps(items, sources, scratch):
    n = len(items)
    mine, got, near_in, first_in, second_in = [scratch[i * n:(i + 1) * n] for i in range(5)]
    (local_sem, core_send, core_recv, near_send, near_recv, one_send, one_recv, two_send, two_recv) = scratch[5 * n:]
    me, core, chip, mate, (far, flip_x, flip_y) = places()
    x, y = lax.rem(chip, 2), lax.div(chip, 2)
    odd, level_near, level_far = levels()

    def core_copies(i):
        source, rows, row_at, columns, column_at, x_first = items[i]
        part = (pl.ds(row_at, rows), pl.ds(column_at, columns))
        return (
            remote(sources[source].at[:, :, 1 - core, *part], got[i], core_send.at[i], core_recv.at[i], mate),
            pltpu.make_async_copy(sources[source].at[:, :, core, *part], mine[i], local_sem.at[i]),
        )

    def near_copy(i):
        keep, away = half_slices(items[i][1], odd)
        return pltpu.make_async_remote_copy(
            src_ref=mine[i].at[:, :, away], dst_ref=near_in[i], send_sem=near_send.at[i], recv_sem=near_recv.at[i],
            device_id={"grp": level_near}, device_id_type=pl.DeviceIdType.MESH,
        )

    def first_copy(i):
        keep, away = half_slices(items[i][1], odd)
        x_first = items[i][-1]
        source = mine[i].at[:, 1 - x, keep] if x_first else mine[i].at[1 - y, :, keep]
        peer = 2 * (flip_x if x_first else flip_y) + core
        return remote(source, first_in[i], one_send.at[i], one_recv.at[i], peer)

    def second_copy(i):
        keep, away = half_slices(items[i][1], odd)
        x_first = items[i][-1]
        source = mine[i].at[1 - y, x, keep] if x_first else mine[i].at[y, 1 - x, keep]
        peer = 2 * (flip_y if x_first else flip_x) + core
        return remote(source, second_in[i], two_send.at[i], two_recv.at[i], peer)

    def core_sends(i):
        for copy in core_copies(i):
            copy.start()

    def core_sums(i):
        there, here = core_copies(i)
        there.wait_recv()
        here.wait()
        add(mine[i], mine[i], got[i])
        near_copy(i).start()

    def near_sums(i):
        keep, away = half_slices(items[i][1], odd)
        near_copy(i).wait_recv()
        held = mine[i].at[:, :, keep]
        add(held, held, near_in[i])
        first_copy(i).start()

    def first_sums(i):
        keep, away = half_slices(items[i][1], odd)
        first_copy(i).wait_recv()
        held = mine[i].at[:, x, keep] if items[i][-1] else mine[i].at[y, :, keep]
        add(held, held, first_in[i])
        second_copy(i).start()

    def second_sums(i):
        keep, away = half_slices(items[i][1], odd)
        second_copy(i).wait_recv()
        return mine[i][y, x, keep].astype(F32) + second_in[i][...].astype(F32)

    def near_hold(i):
        keep, away = half_slices(items[i][1], odd)
        near_copy(i).wait_recv()
        return mine[i][:, :, keep] + near_in[i][...]

    def finish(near_only=()):
        for i in range(n):
            core_copies(i)[0].wait_send()
            near_copy(i).wait_send()
            if i not in near_only:
                for copy in (first_copy(i), second_copy(i)):
                    copy.wait_send()

    return (core_sends, core_sums, near_sums, first_sums, second_sums, finish, near_hold), (
        mate, 2 * flip_x + core, 2 * flip_y + core)


def quad_steps(items, quads, results, scratch):
    n = len(items)
    first_in, joined, second_in = [scratch[i * n:(i + 1) * n] for i in range(3)]
    one_send, one_recv, two_send, two_recv = scratch[3 * n:]
    me, core, chip, mate, (far, flip_x, flip_y) = places()
    x, y = lax.rem(chip, 2), lax.div(chip, 2)

    def first_copy(i):
        x_first = items[i][-1]
        source = quads[i].at[:, 1 - x] if x_first else quads[i].at[1 - y]
        peer = 2 * (flip_x if x_first else flip_y) + core
        return remote(source, first_in[i], one_send.at[i], one_recv.at[i], peer)

    def second_copy(i):
        x_first = items[i][-1]
        source = joined[i].at[1 - y] if x_first else joined[i].at[1 - x]
        peer = 2 * (flip_y if x_first else flip_x) + core
        return remote(source, second_in[i], two_send.at[i], two_recv.at[i], peer)

    def first_start(i):
        first_copy(i).start()

    def first_sums(i):
        first_copy(i).wait_recv()
        add(joined[i], quads[i].at[:, x] if items[i][-1] else quads[i].at[y], first_in[i])
        second_copy(i).start()

    def second_sums(i):
        second_copy(i).wait_recv()
        add(results[i], joined[i].at[y] if items[i][-1] else joined[i].at[x], second_in[i])

    def finish():
        for i in range(n):
            for copy in (first_copy(i), second_copy(i)):
                copy.wait_send()

    return first_start, first_sums, second_sums, finish


def plain_steps(items, sources, scratch):
    n = len(items)
    mine, got, near_in, first_in, second_in = [scratch[i * n:(i + 1) * n] for i in range(5)]
    (local_sem, core_send, core_recv, near_send, near_recv, one_send, one_recv, two_send, two_recv) = scratch[5 * n:]
    me, core, chip, mate, (far, flip_x, flip_y) = places()
    x, y = lax.rem(chip, 2), lax.div(chip, 2)
    odd, level_near, level_far = levels()

    def core_copy(i):
        return remote(sources[i].at[:, :, 1 - core], got[i], core_send.at[i], core_recv.at[i], mate)

    def local_copy(i):
        return pltpu.make_async_copy(sources[i].at[:, :, core], mine[i], local_sem.at[i])

    def first_copy(i):
        x_first = items[i][-1]
        source = mine[i].at[:, 1 - x] if x_first else mine[i].at[1 - y]
        peer = 2 * (flip_x if x_first else flip_y) + core
        return remote(source, first_in[i], one_send.at[i], one_recv.at[i], peer)

    def second_copy(i):
        x_first = items[i][-1]
        source = mine[i].at[1 - y, x] if x_first else mine[i].at[y, 1 - x]
        peer = 2 * (flip_y if x_first else flip_x) + core
        return remote(source, second_in[i], two_send.at[i], two_recv.at[i], peer)

    def near_copy(i):
        keep, away = half_slices(items[i][1], odd)
        return pltpu.make_async_remote_copy(
            src_ref=mine[i].at[y, x, away], dst_ref=near_in[i], send_sem=near_send.at[i], recv_sem=near_recv.at[i],
            device_id={"grp": level_near}, device_id_type=pl.DeviceIdType.MESH,
        )

    def core_sends(i):
        core_copy(i).start()
        local_copy(i).start()

    def core_sums(i):
        core_copy(i).wait_recv()
        local_copy(i).wait()
        add(mine[i], mine[i], got[i])
        first_copy(i).start()

    def first_sums(i):
        first_copy(i).wait_recv()
        held = mine[i].at[:, x] if items[i][-1] else mine[i].at[y]
        add(held, held, first_in[i])
        second_copy(i).start()

    def second_sums(i):
        second_copy(i).wait_recv()
        held = mine[i].at[y, x]
        add(held, held, second_in[i])
        near_copy(i).start()

    def near_sums(i):
        keep, away = half_slices(items[i][1], odd)
        near_copy(i).wait_recv()
        return mine[i][y, x, keep].astype(F32) + near_in[i][...].astype(F32)

    def finish():
        for i in range(n):
            for copy in (core_copy(i), near_copy(i), first_copy(i), second_copy(i)):
                copy.wait_send()

    return (core_sends, core_sums, first_sums, second_sums, near_sums, finish), (
        mate, 2 * flip_x + core, 2 * flip_y + core)


def grp_steps(items, held, outs, scratch, joined=None):
    n = len(items)
    far_in, own_joined, near_in = [scratch[i * n:(i + 1) * n] for i in range(3)]
    z_send, z_recv = scratch[3 * n:]
    joined = own_joined if joined is None else joined
    odd, level_near, level_far = levels()

    def along(i, step):
        source, target, other = (
            (held[i], far_in[i], level_far),
            (joined[i], near_in[i], level_near),
        )[step]
        return pltpu.make_async_remote_copy(
            src_ref=source, dst_ref=target, send_sem=z_send.at[i, step], recv_sem=z_recv.at[i, step],
            device_id={"grp": other}, device_id_type=pl.DeviceIdType.MESH,
        )

    def store(i, odd_half, value):
        source, rows, row_at, columns, column_at, x_first = items[i]
        half = rows // 2
        start = pl.multiple_of(row_at + odd_half * half, half)
        outs[source][pl.ds(start, half), pl.ds(column_at, columns)] = value.astype(F32)

    def far_start(i):
        along(i, 0).start()

    def far_join(i):
        along(i, 0).wait_recv()
        add(joined[i], held[i], far_in[i])

    def near_start(i):
        along(i, 1).start()
        store(i, odd, joined[i][...])

    def far_sum(i):
        far_join(i)
        near_start(i)

    def near_store(i):
        along(i, 1).wait_recv()
        store(i, 1 - odd, near_in[i][...])

    def finish(steps=(0, 1)):
        for i in range(n):
            for step in steps:
                along(i, step).wait_send()

    return (far_start, far_sum, near_store, finish, far_join, near_start), (level_near, level_far)


def add(target, one, two):
    target[...] = one[...] + two[...]


def reduce_kernel(items, whole, square, joined, count, *refs):
    n, m, q, k = len(items), len(whole), len(square), len(joined)

    def take(length):
        nonlocal refs
        head, refs = refs[:length], refs[length:]
        return head

    sources, held, quads, done = take(count), take(m), take(q), take(k)
    outs, whole_outs, quad_outs, joined_outs = take(count), take(m), take(q), take(k)
    tok, near_devices = plain_steps(items, sources, take(5 * n + 9))
    own_held = take(n)
    late, grp_devices = grp_steps(items, own_held, outs, take(3 * n + 2))
    early, unused = grp_steps(whole, held, whole_outs, take(3 * m + 2))
    quad_held = take(q)
    sums = quad_steps(square, quads, quad_held, take(3 * q + 4))
    mid, unused = grp_steps(square, quad_held, quad_outs, take(3 * q + 2))
    first, unused = grp_steps(joined, done, joined_outs, refs, done)
    greet_all(near_devices, grp_devices)
    for i in range(n):
        tok[0](i)
    for i in range(m):
        early[0](i)
    for i in range(q):
        sums[0](i)
    for i in range(n):
        tok[1](i)
    for i in range(k):
        first[5](i)
    for i in range(q):
        sums[1](i)
    for i in range(n):
        tok[2](i)
    for i in range(q):
        sums[2](i)
        mid[0](i)
    for i in range(n):
        tok[3](i)
    for i in range(n):
        own_held[i][...] = tok[4](i).astype(own_held[i].dtype)
        late[0](i)
    for i in range(m):
        early[1](i)
    for i in range(k):
        first[2](i)
    for i in range(q):
        mid[1](i)
    for i in range(n):
        late[1](i)
    for i in range(m):
        early[2](i)
    for i in range(q):
        mid[2](i)
    for i in range(n):
        late[2](i)
    tok[-1]()
    sums[-1]()
    late[3]()
    early[3]()
    mid[3]()
    first[3]((1,))


def reduce_plan(arrays):
    sources, items = [], []
    for source, array in enumerate(arrays):
        rows, columns = array.shape[0] // TOK, array.shape[1]
        sources.append(array.reshape(2, 2, 2, rows, columns))
        items.append((source, rows, 0, columns, 0, source % 2 == 0))
    kinds = [array.dtype for array in arrays]
    shapes = [(array.shape[0] // TOK, array.shape[1]) for array in arrays]
    return sources, tuple(items), kinds, shapes


def held_plan(arrays):
    items = tuple((i, 2 * array.shape[0], 0, array.shape[1], 0, True) for i, array in enumerate(arrays))
    return items, [array.dtype for array in arrays]


def item_blocks(items, kinds, lead, part):
    return [pltpu.VMEM(lead + (item[1] // part, item[3]), kind) for item, kind in zip(items, kinds)]


def quad_plan(arrays, x_firsts):
    items = tuple(
        (i, 2 * array.shape[2], 0, array.shape[3], 0, x_first) for i, (array, x_first) in enumerate(zip(arrays, x_firsts))
    )
    return items, [array.dtype for array in arrays]


def quad_scratch(items, kinds):
    blocks = functools.partial(item_blocks, items, kinds)
    return blocks((2,), 2) + blocks((2,), 2) + blocks((), 2) + [pltpu.SemaphoreType.DMA((len(items),))] * 4


def plain_scratch(items, kinds):
    blocks = functools.partial(item_blocks, items, kinds)
    return (blocks((2, 2), 1) + blocks((2, 2), 1) + blocks((), 2) + blocks((2,), 1) + blocks((), 1)
            + [pltpu.SemaphoreType.DMA((len(items),))] * 9)


def tok_scratch(items, kinds):
    blocks = functools.partial(item_blocks, items, kinds)
    return (blocks((2, 2), 1) + blocks((2, 2), 1) + blocks((2, 2), 2) + blocks((2,), 2) + blocks((), 2)
            + [pltpu.SemaphoreType.DMA((len(items),))] * 9)


def grp_scratch(items, kinds):
    blocks = functools.partial(item_blocks, items, kinds)
    return blocks((), 2) * 3 + [pltpu.SemaphoreType.DMA((len(items), 2))] * 2


def reduce_grads(collective_id, arrays, held, quads, x_firsts, done):
    sources, items, kinds, shapes = reduce_plan(arrays)
    whole, whole_kinds = held_plan(held)
    square, square_kinds = quad_plan(quads, x_firsts)
    joined, joined_kinds = held_plan(done)
    vmem = pl.BlockSpec(memory_space=pltpu.VMEM)
    hbm = pl.BlockSpec(memory_space=pl.ANY)
    rest = len(held) + len(quads) + len(done)
    return pl.pallas_call(
        functools.partial(reduce_kernel, items, whole, square, joined, len(arrays)),
        in_specs=[hbm] * len(arrays) + [vmem] * rest,
        out_specs=[vmem] * (len(arrays) + rest),
        out_shape=[jax.ShapeDtypeStruct(shape, F32) for shape in shapes]
        + [jax.ShapeDtypeStruct((item[1], item[3]), F32) for item in whole + square + joined],
        scratch_shapes=plain_scratch(items, kinds) + item_blocks(items, kinds, (), 2) + grp_scratch(items, kinds)
        + grp_scratch(whole, whole_kinds) + item_blocks(square, square_kinds, (), 2)
        + quad_scratch(square, square_kinds) + grp_scratch(square, square_kinds) + grp_scratch(joined, joined_kinds),
        compiler_params=pltpu.CompilerParams(
            collective_id=collective_id, has_side_effects=True, vmem_limit_bytes=56 * MIB
        ),
        name="reduce_grads",
    )(*sources, *held, *quads, *done)


def write_kernel(count, *refs):
    sources, gain_ref, outs = refs[:count], refs[count], refs[count + 1:2 * count + 1]
    gain_outs, buffers = refs[2 * count + 1:-count - 2], refs[-count - 2:-2]
    in_sem, out_sem = refs[-2:]
    ins = [pltpu.make_async_copy(sources[i], buffers[i], in_sem.at[i]) for i in range(count)]
    backs = [pltpu.make_async_copy(buffers[i], outs[i], out_sem.at[i]) for i in range(count)]
    for copy in ins:
        copy.start()
    for i, out in enumerate(gain_outs):
        out[...] = gain_ref[i:i + 1, 0:D // TOK]
    for i in range(count):
        ins[i].wait()
        backs[i].start()
    for copy in backs:
        copy.wait()


def write_results(results, gains, gain_count):
    n = len(results)
    hbm, vmem = pl.BlockSpec(memory_space=pl.ANY), pl.BlockSpec(memory_space=pltpu.VMEM)
    return pl.pallas_call(
        functools.partial(write_kernel, n),
        in_specs=[hbm] * n + [vmem],
        out_specs=[hbm] * n + [vmem] * gain_count,
        out_shape=[jax.ShapeDtypeStruct(result.shape, result.dtype) for result in results]
        + [jax.ShapeDtypeStruct((1, D // TOK), F32)] * gain_count,
        scratch_shapes=[pltpu.VMEM(result.shape, result.dtype) for result in results]
        + [pltpu.SemaphoreType.DMA((n,)), pltpu.SemaphoreType.DMA((n,))],
        compiler_params=pltpu.CompilerParams(vmem_limit_bytes=60 * MIB),
        name="write_results",
    )(*results, gains)


def latents_backward_kernel(items, *refs):
    (mgrad_ref, packed_ref, exact_ref, lse_ref, up_ref, mmid_ref, fmid_ref, att_ref, clse_ref, ow_ref, fgain_ref,
     fup_ref, fdown_ref, mgain_ref, proj_ref) = refs[:15]
    count = max(item[0] for item in items) + 1
    sources = refs[15:15 + count]
    (agrad_ref, fig_ref, lup_ref, dup_ref, ddown_ref, dproj_ref, dout_ref, dmgain_ref, dfgain_ref) = refs[
        15 + count:24 + count]
    reduced = refs[24 + count:24 + 2 * count]
    rest = refs[24 + 2 * count:]
    (heads, exact, ups, mmid, fmid, att, ow, fup, fdown, proj, keys, values, upstream_heads, key_acc, value_acc,
     grads, back, agrad, lup, dup, ddown, dproj, dout, hidden, active, hidden_low, grad_low,
     load_sem, store_sem, send_a, recv_a, local_a, send_b, recv_b, local_b) = rest[:35]
    me, peers = all_peers()
    reducer, near_devices = tok_steps(items, sources, rest[35:])
    core_sends, core_sums, near_sums, first_sums, second_sums, finish = reducer[:6]
    odd, level_near, level_far = levels()

    def hold(item):
        reduced[item][...] = second_sums(item).astype(reduced[item].dtype)

    names = ("heads", "exact", "fmid", "fup", "up", "mmid", "proj", "fdown", "att", "ow")
    loads = {}
    for i, (source, target) in enumerate((
        (packed_ref, heads), (exact_ref, exact), (fmid_ref, fmid), (fup_ref, fup), (up_ref, ups), (mmid_ref, mmid),
        (proj_ref, proj), (fdown_ref, fdown), (att_ref, att), (ow_ref, ow),
    )):
        loads[names[i]] = pltpu.make_async_copy(source, target, load_sem.at[i])
        loads[names[i]].start()
    stores = []

    def store(source, target):
        stores.append(pltpu.make_async_copy(source, target, store_sem.at[len(stores)]))
        stores[-1].start()

    greet_all(peers, (level_near,))
    outward = [
        head_copies(mgrad_ref, upstream_heads, True, member, me, peers, send_a, recv_a, local_a) for member in range(MB)
    ]
    backward = [head_copies(back, grads, False, member, me, peers, send_b, recv_b, local_b) for member in range(MB)]
    for copies, here in outward:
        for copy in copies:
            copy.start()
        here.start()
    core_sends(0)
    loads["fmid"].wait()
    loads["fup"].wait()
    first_hat, first_inverse = norm_parts(fmid[...])
    first_normed = (first_hat * fgain_ref[...]).astype(BF16)
    hidden[...] = nn(first_normed, fup[...])
    core_sums(0)
    loads["heads"].wait()
    loads["exact"].wait()
    for member in range(MB):
        keys[...] = heads[1, member].T
        values[...] = heads[2, member].T
        key_acc[...] = jnp.zeros_like(key_acc)
        value_acc[...] = jnp.zeros_like(value_acc)
        copies, here = outward[member]
        for copy in copies:
            copy.wait_recv()
        here.wait()
        if member == 0:
            core_sends(1)
            core_sends(2)

        def attend_back(step, carry, member=member):
            at = pl.ds(pl.multiple_of(step * QB_BACK, QB_BACK), QB_BACK)
            queries = heads[0, member, :, at]
            upstream = upstream_heads[0, member, :, at]
            inner = jnp.sum(upstream.astype(F32) * exact[member, :, at], axis=0, keepdims=True)
            softened = jnp.exp2(nn(keys[...], queries) - lse_ref[member, 0:1, at])
            logit_grad = (softened * (nn(values[...], upstream) - inner)).astype(BF16)
            value_acc[...] += nt(upstream, softened.astype(BF16))
            key_acc[...] += nt(queries, logit_grad)
            grads[0, member, :, at] = (nn(heads[1, member], logit_grad) * HD ** (-0.5)).astype(BF16)
            return carry

        steps = L // QB_BACK
        lax.fori_loop(0, steps, attend_back, 0)
        grads[1, member] = (key_acc[...] * LN2).astype(BF16)
        grads[2, member] = value_acc[...].astype(BF16)
        for copy in backward[member][0] + [backward[member][1]]:
            copy.start()
        if member == 0:
            near_sums(0)
            core_sums(1)
            core_sums(2)
    loads["up"].wait()
    loads["mmid"].wait()
    loads["proj"].wait()
    loads["fdown"].wait()
    mixer_hat, mixer_inverse = norm_parts(mmid[...])
    mixer_normed = (mixer_hat * mgain_ref[...]).astype(BF16).T
    loads["att"].wait()
    loads["ow"].wait()
    mixer_gains, first_gains = [], []

    def rows_back(member):
        copies, here = backward[member]
        for copy in copies:
            copy.wait_recv()
        here.wait()
        rows = slice(member * ROWS, (member + 1) * ROWS)
        normed_grad = nn(proj[...], back[:, :, :, rows].reshape(3 * D, ROWS)).T
        residual, gain_rows = norm_pull(mixer_hat[rows], mixer_inverse[rows], mgain_ref[...], normed_grad)
        mixer_gains.append(jnp.sum(gain_rows, axis=0, keepdims=True))
        upstream = ups[rows] + residual
        grad = upstream.astype(BF16)
        grad_low[rows] = grad
        normed_grad = jnp.zeros((ROWS, D), F32)
        for part in range(2):
            cut = slice(part * FF // 2, (part + 1) * FF // 2)
            act, slope = gelu_parts(hidden[rows, cut])
            active[rows, cut] = act.astype(BF16)
            hidden_grad = (slope * nt(grad, fdown[cut])).astype(BF16)
            hidden_low[rows, cut] = hidden_grad
            normed_grad = normed_grad + nt(hidden_grad, fup[:, cut])
        residual, gain_rows = norm_pull(first_hat[rows], first_inverse[rows], fgain_ref[...], normed_grad)
        first_gains.append(jnp.sum(gain_rows, axis=0, keepdims=True))
        upstream = upstream + residual
        lup[rows] = upstream
        attended_grad = nt(upstream.astype(BF16), ow[...]).astype(BF16)
        agrad[member] = attended_grad
        inner = jnp.sum(attended_grad.astype(F32) * att[member], axis=1, keepdims=True)
        fig_ref[member] = jnp.concatenate(
            [clse_ref[member, 0:1], to_rows(inner, inner)[0:1], jnp.zeros((6, ROWS), F32)], axis=0
        )

    rows_back(0)
    first_sums(0)
    near_sums(1)
    near_sums(2)
    rows_back(1)
    hold(0)
    first_sums(1)
    first_sums(2)
    store(lup, lup_ref)
    store(agrad, agrad_ref)
    dmgain_ref[...] = mixer_gains[0] + mixer_gains[1]
    dfgain_ref[...] = first_gains[0] + first_gains[1]
    grad = grad_low[...]
    ddown[...] = tn(active[...], grad).astype(BF16)
    store(ddown, ddown_ref)
    dup[...] = tn(first_normed, hidden_low[...]).astype(BF16)
    store(dup, dup_ref)
    dproj[...] = nt(mixer_normed, back[...].reshape(3 * D, MB * ROWS)).astype(BF16)
    store(dproj, dproj_ref)
    dout[...] = tn(att[...].reshape(MB * ROWS, D).astype(BF16), lup[...].astype(BF16)).astype(BF16)
    store(dout, dout_ref)
    hold(1)
    hold(2)
    finish()
    for copy in stores:
        copy.wait()
    for copies, here in outward + backward:
        for copy in copies:
            copy.wait_send()


def latents_backward(collective_id, arrays, *args):
    dma = pltpu.SemaphoreType.DMA
    vmem = pl.BlockSpec(memory_space=pltpu.VMEM)
    hbm = pl.BlockSpec(memory_space=pl.ANY)
    rows = MB * ROWS
    sources, items, kinds, shapes = reduce_plan(arrays)
    reduced = [jax.ShapeDtypeStruct((rows_ // 2, columns), kind) for (rows_, columns), kind in zip(shapes, kinds)]
    stored = [
        ((MB, ROWS, D), BF16), ((MB, 8, ROWS), F32), ((rows, D), F32), ((D, FF), BF16), ((FF, D), BF16),
        ((D, 3 * D), BF16), ((D, D), BF16), ((1, D), F32), ((1, D), F32),
    ]
    return pl.pallas_call(
        functools.partial(latents_backward_kernel, items),
        in_specs=[hbm, hbm, hbm, vmem, hbm, hbm, hbm, hbm, vmem, hbm, vmem, hbm, hbm, vmem, hbm] + [hbm] * len(arrays),
        out_specs=[hbm, vmem] + [hbm] * 5 + [vmem] * (2 + len(arrays)),
        out_shape=[jax.ShapeDtypeStruct(shape, kind) for shape, kind in stored] + reduced,
        scratch_shapes=[
            pltpu.VMEM((3, MB, HD, L), BF16), pltpu.VMEM((MB, HD, L), F32), pltpu.VMEM((rows, D), F32),
            pltpu.VMEM((rows, D), F32), pltpu.VMEM((rows, D), F32), pltpu.VMEM((MB, ROWS, D), F32),
            pltpu.VMEM((D, D), BF16), pltpu.VMEM((D, FF), BF16), pltpu.VMEM((FF, D), BF16),
            pltpu.VMEM((D, 3 * D), BF16), pltpu.VMEM((L, HD), BF16), pltpu.VMEM((L, HD), BF16),
            pltpu.VMEM((1, MB, HD, L), BF16), pltpu.VMEM((HD, L), F32), pltpu.VMEM((HD, L), F32),
            pltpu.VMEM((3, MB, HD, L), BF16), pltpu.VMEM((3, H, HD, rows), BF16),
            pltpu.VMEM((MB, ROWS, D), BF16), pltpu.VMEM((rows, D), F32), pltpu.VMEM((D, FF), BF16),
            pltpu.VMEM((FF, D), BF16), pltpu.VMEM((D, 3 * D), BF16), pltpu.VMEM((D, D), BF16),
            pltpu.VMEM((rows, FF), F32), pltpu.VMEM((rows, FF), BF16), pltpu.VMEM((rows, FF), BF16),
            pltpu.VMEM((rows, D), BF16),
            dma((10,)), dma((6,)), dma((7, MB)), dma((7, MB)), dma((MB,)), dma((7, MB)), dma((7, MB)), dma((MB,)),
        ] + tok_scratch(items, kinds),
        compiler_params=pltpu.CompilerParams(
            collective_id=collective_id, has_side_effects=True, vmem_limit_bytes=61 * MIB
        ),
        cost_estimate=pl.CostEstimate(
            flops=35 * 10**9, bytes_accessed=36 * 10**6, transcendentals=10 * 10**6
        ),
        name="latents_backward",
    )(*args, *sources)


def fast_body(
    tokens,
    latents,
    segments,
    scene_mask,
    counts,
    token_gain,
    query_gain,
    query_weight,
    key_weight,
    value_weight,
    output_weight,
    first_gain,
    first_up,
    first_down,
    mixer_gain,
    mixer_project,
    mixer_output,
    second_gain,
    second_up,
    second_down,
    cotangent,
):
    scenes = (segments, scene_mask, counts)
    keys, values, queries, attended, lse = cross_forward(
        0, tokens, latents, token_gain[None], query_gain[None], query_weight, key_weight, value_weight, *scenes
    )
    (latents_out, first_mid, mixer_mid, packed, exact, head_lse, upstream, mixed_grad, d_second_down, d_second_up,
     d_mixer_output, d_second_gain) = latents_forward(
        1, latents, attended, cotangent, output_weight, first_gain[None], first_up, first_down, mixer_gain[None],
        mixer_project, mixer_output, second_gain[None], second_up, second_down,
    )
    (attended_grad, figures, upstream, d_first_up, d_first_down, d_project, d_output, d_mixer_gain, d_first_gain,
     *early) = latents_backward(
        2, [d_second_up, d_second_down, d_mixer_output], mixed_grad, packed, exact, head_lse, upstream, mixer_mid,
        first_mid, attended, lse, output_weight, first_gain[None], first_up, first_down, mixer_gain[None], mixer_project,
    )
    latents_grad, tokens_grad, d_key, d_value, d_query, gains, *rest = cross_backward(
        5, early, [d_first_up, d_first_down, d_project], tokens, token_gain[None], key_weight, value_weight,
        *scenes, keys, values, queries, attended_grad, figures, latents, upstream, query_gain[None], query_weight,
        d_first_gain, d_mixer_gain, d_second_gain,
    )
    early, held, quads = rest[:len(early)], rest[len(early):len(early) + 1], rest[len(early) + 1:]
    o_output, o_key, o_value, o_query, gains, *late = reduce_grads(
        7, [d_output, d_key, d_value, d_query, gains], held, quads, (False, True), early
    )
    late, early = late[:3], late[3:]
    (latents_out, latents_grad, tokens_grad, o_second_up, o_second_down, o_mixer_output, o_first_up, o_first_down,
     o_project, o_output, o_key, o_value, o_query, *o_gains) = write_results(
        [latents_out, latents_grad.reshape(latents_out.shape), tokens_grad, *early, *late, o_output, o_key, o_value, o_query], gains, 5
    )
    o_gains = [gain.reshape(D // TOK) for gain in o_gains]
    return (
        latents_out,
        latents_grad,
        tokens_grad,
        o_gains[0],
        o_gains[1],
        o_query,
        o_key,
        o_value,
        o_output,
        o_gains[2],
        o_first_up,
        o_first_down,
        o_gains[3],
        o_project,
        o_mixer_output,
        o_gains[4],
        o_second_up,
        o_second_down,
    )


IN_SPECS = (
    P("grp", None, "tok", None),
    P("grp", None, None, None),
    P("grp", None, "tok"),
    P("grp", None, None, None),
    P("grp", None, "tok"),
    P(),
    P(),
    P(),
    P(),
    P(),
    P(),
    P(),
    P(),
    P(),
    P(),
    P(),
    P(),
    P(),
    P(),
    P(),
    P("grp", None, "tok", None),
)
OUT_SPECS = (
    P("grp", None, "tok", None),
    P("grp", None, "tok", None),
    P("grp", None, "tok", None),
    P("tok"),
    P("tok"),
    P("tok", None),
    P("tok", None),
    P("tok", None),
    P("tok", None),
    P("tok"),
    P("tok", None),
    P("tok", None),
    P("tok"),
    P("tok", None),
    P("tok", None),
    P("tok"),
    P("tok", None),
    P("tok", None),
)


def solution(mesh):
    return jax.shard_map(
        fast_body if mesh.shape["tok"] == TOK else general_body,
        mesh=mesh,
        in_specs=IN_SPECS,
        out_specs=OUT_SPECS,
        check_vma=False,
    )
```

```python
import functools

import jax
import jax.numpy as jnp
from jax import lax
from jax.experimental import pallas as pl
from jax.experimental.pallas import tpu as pltpu
from jax.sharding import PartitionSpec as P

D = 512
L = 2048
H = 8
HD = 64
TOK_DEV = 1024
MB = 2
SCENES = 8
LGROUPS = 8


EPS = 1e-05
NEG = -1e30


def norm_rows(values, gain):
    centre = values - jnp.mean(values, axis=-1, keepdims=True)
    spread = jnp.mean(centre * centre, axis=-1, keepdims=True)
    return centre * lax.rsqrt(spread + EPS) * gain


def norm_back(values, gain, upstream):
    unused, pull = jax.vjp(norm_rows, values, gain)
    return pull(upstream)


def gelu_back(hidden, upstream):
    unused, pull = jax.vjp(jax.nn.gelu, hidden)
    return pull(upstream)[0]


def product_plain(left, right):
    return jnp.dot(left, right, preferred_element_type=jnp.float32)


def product_rows(left, right):
    return lax.dot_general(
        left, right, (((0,), (0,)), ((), ())), preferred_element_type=jnp.float32
    )


def product_cols(left, right):
    return lax.dot_general(
        left, right, (((1,), (1,)), ((), ())), preferred_element_type=jnp.float32
    )


def add_term(store, name, value):
    if name in store:
        store[name] = store[name] + value
    else:
        store[name] = value


def project_tokens(tokens, member, token_gain, key_weight, value_weight):
    source = tokens[0, member].astype(jnp.float32)
    normed = norm_rows(source, token_gain).astype(jnp.bfloat16)
    key_rows = product_plain(normed, key_weight).astype(jnp.bfloat16)
    value_rows = product_plain(normed, value_weight).astype(jnp.bfloat16)
    return (source, normed, key_rows, value_rows)


def mlp_forward(residual, gain, up_weight, down_weight):
    normed = norm_rows(residual, gain).astype(jnp.bfloat16)
    hidden = product_plain(normed, up_weight)
    active = jax.nn.gelu(hidden).astype(jnp.bfloat16)
    return (residual + product_plain(active, down_weight), (normed, hidden, active))


def mlp_backward(residual, gain, up_weight, down_weight, saved, upstream):
    normed, hidden, active = saved
    grad_low = upstream.astype(jnp.bfloat16)
    grad_down = product_rows(active, grad_low)
    hidden_grad = gelu_back(hidden, product_cols(grad_low, down_weight)).astype(jnp.bfloat16)
    grad_up = product_rows(normed, hidden_grad)
    residual_grad, grad_gain = norm_back(residual, gain, product_cols(hidden_grad, up_weight))
    return (upstream + residual_grad, grad_gain, grad_up, grad_down)


def mixer_forward(residual, gain, project, output):
    own_rows = residual.shape[0]
    normed = norm_rows(residual, gain).astype(jnp.bfloat16)
    packed = product_plain(normed, project).astype(jnp.bfloat16)
    pair_rows = lax.all_gather(packed[:, D:], "tok", axis=0, tiled=True)
    every = pair_rows.shape[0]
    own_queries = packed[:, :D].reshape(own_rows, H, HD)
    keys = pair_rows[:, :D].reshape(every, H, HD)
    values = pair_rows[:, D:].reshape(every, H, HD)
    logits = jnp.einsum(
        "qhd,khd->hqk", own_queries, keys, preferred_element_type=jnp.float32
    ) * HD ** (-0.5)
    peak_row = jnp.max(logits, axis=-1, keepdims=True)
    raised = jnp.exp(logits - peak_row)
    softened = raised / jnp.sum(raised, axis=-1, keepdims=True)
    softened_low = softened.astype(jnp.bfloat16)
    mixed_rows = jnp.einsum(
        "hqk,khd->qhd", softened_low, values, preferred_element_type=jnp.float32
    )
    mixed_rows = mixed_rows.reshape(own_rows, D).astype(jnp.bfloat16)
    return (
        residual + product_plain(mixed_rows, output),
        (normed, own_queries, keys, values, softened, softened_low, mixed_rows),
    )


def mixer_backward(residual, gain, project, output, saved, upstream):
    normed, own_queries, keys, values, softened, softened_low, mixed_rows = saved
    own_rows = upstream.shape[0]
    every = keys.shape[0]
    grad_low = upstream.astype(jnp.bfloat16)
    grad_output = product_rows(mixed_rows, grad_low)
    mixed_grad = product_cols(grad_low, output).astype(jnp.bfloat16).reshape(own_rows, H, HD)
    value_grad = jnp.einsum(
        "hqk,qhd->khd", softened_low, mixed_grad, preferred_element_type=jnp.float32
    )
    soft_grad = jnp.einsum("qhd,khd->hqk", mixed_grad, values, preferred_element_type=jnp.float32)
    logit_grad = softened * (soft_grad - jnp.sum(soft_grad * softened, axis=-1, keepdims=True))
    logit_grad = logit_grad.astype(jnp.bfloat16)
    query_grad = jnp.einsum(
        "hqk,khd->qhd", logit_grad, keys, preferred_element_type=jnp.float32
    ) * HD ** (-0.5)
    key_grad = jnp.einsum(
        "hqk,qhd->khd", logit_grad, own_queries, preferred_element_type=jnp.float32
    ) * HD ** (-0.5)
    pair_terms = jnp.concatenate([key_grad.reshape(every, D), value_grad.reshape(every, D)], axis=1)
    pair_grad = lax.psum_scatter(
        pair_terms.astype(jnp.bfloat16), "tok", scatter_dimension=0, tiled=True
    ).astype(jnp.float32)
    packed_grad = jnp.concatenate([query_grad.reshape(own_rows, D), pair_grad], axis=1).astype(
        jnp.bfloat16
    )
    grad_project = product_rows(normed, packed_grad)
    residual_grad, grad_gain = norm_back(residual, gain, product_cols(packed_grad, project))
    return (upstream + residual_grad, grad_gain, grad_project, grad_output)


def general_body(
    tokens,
    latents,
    segments,
    scene_mask,
    counts,
    token_gain,
    query_gain,
    query_weight,
    key_weight,
    value_weight,
    output_weight,
    first_gain,
    first_up,
    first_down,
    mixer_gain,
    mixer_project,
    mixer_output,
    second_gain,
    second_up,
    second_down,
    cotangent,
):
    scale = D ** (-0.5)
    shards = lax.axis_size("tok")
    own_rows = L // shards
    row_start = lax.axis_index("tok") * own_rows
    latent_group = jnp.arange(L) // (L // LGROUPS)
    latent_onehot = (latent_group[:, None] == jnp.arange(LGROUPS)[None, :]).astype(jnp.float32)
    token_place = jnp.arange(TOK_DEV)
    records = []
    latent_outs = []
    for member in range(MB):
        record = {}
        source, normed, key_rows, value_rows = project_tokens(
            tokens, member, token_gain, key_weight, value_weight
        )
        record["token_side"] = (source, normed, key_rows, value_rows)
        scene_onehot = (segments[0, member][:, None] == jnp.arange(SCENES)[None, :]).astype(
            jnp.float32
        )
        token_seen = jnp.dot(scene_onehot, scene_mask[0, member].astype(jnp.float32))
        visible = product_cols(latent_onehot, token_seen)
        alive = token_place < counts[0, member, 0]
        allowed = (visible > 0.5) & alive[None, :]
        latent_every = latents[0, member]
        normed_every = norm_rows(latent_every, query_gain).astype(jnp.bfloat16)
        queries = product_plain(normed_every, query_weight).astype(jnp.bfloat16)
        scores = jnp.where(allowed, product_cols(queries, key_rows) * scale, NEG)
        row_top = lax.pmax(jnp.max(scores, axis=1), "tok")
        unnormed = jnp.exp(scores - row_top[:, None])
        row_total, weighted = (
            lax.psum_scatter(
                jnp.sum(unnormed, axis=1).astype(jnp.bfloat16),
                "tok",
                scatter_dimension=0,
                tiled=True,
            ).astype(jnp.float32),
            lax.psum_scatter(
                product_plain(unnormed.astype(jnp.bfloat16), value_rows).astype(jnp.bfloat16),
                "tok",
                scatter_dimension=0,
                tiled=True,
            ).astype(jnp.float32),
        )
        latent_in = lax.dynamic_slice_in_dim(latent_every, row_start, own_rows, 0)
        latent_normed = lax.dynamic_slice_in_dim(normed_every, row_start, own_rows, 0)
        attended = weighted / row_total[:, None]
        attended_low = attended.astype(jnp.bfloat16)
        first_mid = latent_in + product_plain(attended_low, output_weight)
        mixer_mid, first_saved = mlp_forward(first_mid, first_gain, first_up, first_down)
        second_mid, mixer_saved = mixer_forward(mixer_mid, mixer_gain, mixer_project, mixer_output)
        final_rows, second_saved = mlp_forward(second_mid, second_gain, second_up, second_down)
        latent_outs.append(final_rows)
        record["latent_side"] = (
            allowed,
            latent_in,
            latent_normed,
            queries,
            row_top,
            row_total,
            attended,
            attended_low,
            first_mid,
            mixer_mid,
            second_mid,
            first_saved,
            mixer_saved,
            second_saved,
        )
        records.append(record)
    grads = {}
    latent_grads = []
    token_grads = []
    for member in range(MB):
        record = records[member]
        source, normed, key_rows, value_rows = record["token_side"]
        (
            allowed,
            latent_in,
            latent_normed,
            queries,
            row_top,
            row_total,
            attended,
            attended_low,
            first_mid,
            mixer_mid,
            second_mid,
            first_saved,
            mixer_saved,
            second_saved,
        ) = record["latent_side"]
        second_back = mlp_backward(
            second_mid, second_gain, second_up, second_down, second_saved, cotangent[0, member]
        )
        add_term(grads, "second_gain", second_back[1])
        add_term(grads, "second_up", second_back[2])
        add_term(grads, "second_down", second_back[3])
        mixer_back = mixer_backward(
            mixer_mid, mixer_gain, mixer_project, mixer_output, mixer_saved, second_back[0]
        )
        add_term(grads, "mixer_gain", mixer_back[1])
        add_term(grads, "mixer_project", mixer_back[2])
        add_term(grads, "mixer_output", mixer_back[3])
        first_back = mlp_backward(
            first_mid, first_gain, first_up, first_down, first_saved, mixer_back[0]
        )
        add_term(grads, "first_gain", first_back[1])
        add_term(grads, "first_up", first_back[2])
        add_term(grads, "first_down", first_back[3])
        latent_upstream = first_back[0]
        grad_low = latent_upstream.astype(jnp.bfloat16)
        add_term(grads, "output_weight", product_rows(attended_low, grad_low))
        attended_grad = lax.optimization_barrier(
            product_cols(grad_low, output_weight).astype(jnp.bfloat16)
        ).astype(jnp.float32)
        weighted_grad = (attended_grad / row_total[:, None]).astype(jnp.bfloat16)
        total_grad = -jnp.sum(attended_grad * attended, axis=1) / row_total
        weighted_every, total_every = (
            lax.all_gather(
                weighted_grad.astype(jnp.float32).astype(jnp.bfloat16), "tok", axis=0, tiled=True
            ).astype(jnp.float32),
            lax.all_gather(total_grad.astype(jnp.bfloat16), "tok", axis=0, tiled=True).astype(
                total_grad.dtype
            ),
        )
        weighted_every = weighted_every.astype(jnp.bfloat16)
        scores = jnp.where(allowed, product_cols(queries, key_rows) * scale, NEG)
        unnormed = jnp.exp(scores - row_top[:, None])
        unnormed_grad = product_cols(weighted_every, value_rows) + total_every[:, None]
        score_grad = (unnormed * unnormed_grad).astype(jnp.bfloat16)
        value_grad = product_rows(unnormed.astype(jnp.bfloat16), weighted_every).astype(
            jnp.bfloat16
        )
        key_grad = (product_rows(score_grad, queries) * scale).astype(jnp.bfloat16)
        query_grad = lax.psum_scatter(
            (product_plain(score_grad, key_rows) * scale).astype(jnp.bfloat16),
            "tok",
            scatter_dimension=0,
            tiled=True,
        )
        add_term(grads, "key_weight", product_rows(normed, key_grad))
        add_term(grads, "value_weight", product_rows(normed, value_grad))
        normed_grad = product_cols(key_grad, key_weight) + product_cols(value_grad, value_weight)
        source_grad, gain_grad = norm_back(source, token_gain, normed_grad)
        add_term(grads, "token_gain", gain_grad)
        token_grads.append(source_grad)
        add_term(grads, "query_weight", product_rows(latent_normed, query_grad))
        latent_grad, gain_grad = norm_back(
            latent_in, query_gain, product_cols(query_grad, query_weight)
        )
        add_term(grads, "query_gain", gain_grad)
        latent_grads.append(latent_upstream + latent_grad)
    parts = (
        lax.psum_scatter(
            grads["token_gain"].astype(jnp.bfloat16), "tok", scatter_dimension=0, tiled=True
        ).astype(jnp.float32),
        lax.psum_scatter(
            grads["query_gain"].astype(jnp.bfloat16), "tok", scatter_dimension=0, tiled=True
        ).astype(jnp.float32),
        lax.psum_scatter(
            grads["query_weight"].astype(jnp.bfloat16), "tok", scatter_dimension=0, tiled=True
        ).astype(jnp.float32),
        lax.psum_scatter(
            grads["key_weight"].astype(jnp.bfloat16), "tok", scatter_dimension=0, tiled=True
        ).astype(jnp.float32),
        lax.psum_scatter(
            grads["value_weight"].astype(jnp.bfloat16), "tok", scatter_dimension=0, tiled=True
        ).astype(jnp.float32),
        lax.psum_scatter(
            grads["output_weight"].astype(jnp.bfloat16), "tok", scatter_dimension=0, tiled=True
        ).astype(jnp.float32),
        lax.psum_scatter(
            grads["first_gain"].astype(jnp.bfloat16), "tok", scatter_dimension=0, tiled=True
        ).astype(jnp.float32),
        lax.psum_scatter(
            grads["first_up"].astype(jnp.bfloat16), "tok", scatter_dimension=0, tiled=True
        ).astype(jnp.float32),
        lax.psum_scatter(
            grads["first_down"].astype(jnp.bfloat16), "tok", scatter_dimension=0, tiled=True
        ).astype(jnp.float32),
        lax.psum_scatter(
            grads["mixer_gain"].astype(jnp.bfloat16), "tok", scatter_dimension=0, tiled=True
        ).astype(jnp.float32),
        lax.psum_scatter(
            grads["mixer_project"].astype(jnp.bfloat16), "tok", scatter_dimension=0, tiled=True
        ).astype(jnp.float32),
        lax.psum_scatter(
            grads["mixer_output"].astype(jnp.bfloat16), "tok", scatter_dimension=0, tiled=True
        ).astype(jnp.float32),
        lax.psum_scatter(
            grads["second_gain"].astype(jnp.bfloat16), "tok", scatter_dimension=0, tiled=True
        ).astype(jnp.float32),
        lax.psum_scatter(
            grads["second_up"].astype(jnp.bfloat16), "tok", scatter_dimension=0, tiled=True
        ).astype(jnp.float32),
        lax.psum_scatter(
            grads["second_down"].astype(jnp.bfloat16), "tok", scatter_dimension=0, tiled=True
        ).astype(jnp.float32),
    )
    summed = (
        lax.psum(parts[0].astype(jnp.bfloat16), "grp").astype(jnp.float32),
        lax.psum(parts[1].astype(jnp.bfloat16), "grp").astype(jnp.float32),
        lax.psum(parts[2].astype(jnp.bfloat16), "grp").astype(jnp.float32),
        lax.psum(parts[3].astype(jnp.bfloat16), "grp").astype(jnp.float32),
        lax.psum(parts[4].astype(jnp.bfloat16), "grp").astype(jnp.float32),
        lax.psum(parts[5].astype(jnp.bfloat16), "grp").astype(jnp.float32),
        lax.psum(parts[6].astype(jnp.bfloat16), "grp").astype(jnp.float32),
        lax.psum(parts[7].astype(jnp.bfloat16), "grp").astype(jnp.float32),
        lax.psum(parts[8].astype(jnp.bfloat16), "grp").astype(jnp.float32),
        lax.psum(parts[9].astype(jnp.bfloat16), "grp").astype(jnp.float32),
        lax.psum(parts[10].astype(jnp.bfloat16), "grp").astype(jnp.float32),
        lax.psum(parts[11].astype(jnp.bfloat16), "grp").astype(jnp.float32),
        lax.psum(parts[12].astype(jnp.bfloat16), "grp").astype(jnp.float32),
        lax.psum(parts[13].astype(jnp.bfloat16), "grp").astype(jnp.float32),
        lax.psum(parts[14].astype(jnp.bfloat16), "grp").astype(jnp.float32),
    )
    return (
        jnp.stack(latent_outs)[None],
        jnp.stack(latent_grads)[None],
        jnp.stack(token_grads)[None],
    ) + tuple(summed)


TOK = 8
ROWS = L // TOK
FF = 2048
GR = L // LGROUPS
LOG2E = 1.4426950408889634
LN2 = 0.6931471805599453
F32 = jnp.float32
BF16 = jnp.bfloat16
MIB = 1024 * 1024


def nn(left, right):
    return lax.dot_general(left, right, (((1,), (0,)), ((), ())), preferred_element_type=F32)


def nt(left, right):
    return lax.dot_general(left, right, (((1,), (1,)), ((), ())), preferred_element_type=F32)


def tn(left, right):
    return lax.dot_general(left, right, (((0,), (0,)), ((), ())), preferred_element_type=F32)


def norm_parts(values):
    centre = values - jnp.mean(values, axis=-1, keepdims=True)
    inverse = lax.rsqrt(jnp.mean(centre * centre, axis=-1, keepdims=True) + EPS)
    return centre * inverse, inverse


def norm_pull(hat, inverse, gain, upstream):
    scaled = upstream * gain
    inner = jnp.mean(scaled * hat, axis=-1, keepdims=True)
    grad = (scaled - jnp.mean(scaled, axis=-1, keepdims=True) - hat * inner) * inverse
    return grad, upstream * hat


def places():
    me = lax.axis_index("tok")
    core = lax.rem(me, 2)
    chip = lax.div(me, 2)
    mate = me + 1 - 2 * core
    flip_x = chip + 1 - 2 * lax.rem(chip, 2)
    flip_y = lax.rem(chip + 2, 4)
    far = 3 - chip
    return me, core, chip, mate, (far, flip_x, flip_y)


def remote(src, dst, send_sem, recv_sem, peer):
    return pltpu.make_async_remote_copy(
        src_ref=src,
        dst_ref=dst,
        send_sem=send_sem,
        recv_sem=recv_sem,
        device_id={"tok": peer},
        device_id_type=pl.DeviceIdType.MESH,
    )


def greet(devices):
    barrier = pltpu.get_barrier_semaphore()
    for device in devices:
        pl.semaphore_signal(
            barrier, inc=1, device_id={"tok": device}, device_id_type=pl.DeviceIdType.MESH
        )
    pl.semaphore_wait(barrier, len(devices))


def chip_at(chip, flip):
    high, low = divmod(flip, 2) if isinstance(flip, int) else (lax.div(flip, 2), lax.rem(flip, 2))
    across = lax.rem(lax.rem(chip, 2) + low, 2)
    along = lax.rem(lax.div(chip, 2) + high, 2)
    return 2 * along + across


def mask_loads(seg_ref, mask_ref, seg_buf, mask_buf, sem):
    return (
        pltpu.make_async_copy(seg_ref.at[0], seg_buf, sem.at[0]),
        pltpu.make_async_copy(mask_ref.at[0], mask_buf, sem.at[1]),
    )


def mask_rows(seg_buf, mask_buf, count_ref, bias_ref):
    for member in range(MB):
        scene = lax.broadcasted_iota(jnp.int32, (SCENES, TOK_DEV), 0)
        place = lax.broadcasted_iota(jnp.int32, (SCENES, TOK_DEV), 1)
        hot = jnp.where((seg_buf[member:member + 1] == scene) & (place < count_ref[0, member, 0]), 1.0, 0.0)
        seen = tn(jnp.where(mask_buf[member] > 0, 1.0, 0.0).astype(BF16), hot.astype(BF16))
        bias_ref[member] = jnp.where(seen > 0.5, 0.0, NEG)


def to_rows(first, second):
    rows = first.shape[0]
    lane = lax.broadcasted_iota(jnp.int32, (rows, 128), 1)
    return jnp.where(lane == 0, first, second).T[0:8]


def cross_forward_kernel(
    tok_ref, lat_ref, tgain_ref, qgain_ref, qw_ref, kw_ref, vw_ref, seg_ref, mask_ref, count_ref,
    k_out, v_out, q_out, att_ref, lse_ref,
    tok_buf, lat_buf, keys, values, queries, bias, part, part_s, got, got_s, stage, stage_s,
    arrive, arrive_s, total, seg_buf, mask_buf,
    mask_sem, tok_sem, lat_sem, k_sem, v_sem, q_sem,
    core_send, core_recv, core_send_s, core_recv_s, chip_send, chip_recv, chip_send_s, chip_recv_s,
):
    me, core, chip, mate, others = places()
    span = 2 * ROWS

    def unpack(step):
        if isinstance(step, int):
            return (step // 3, 3 - step % 3) if step < 3 * MB else (step - 3 * MB, 0)
        late = step >= 3 * MB
        return (
            jnp.where(late, step - 3 * MB, lax.div(step, 3)),
            jnp.where(late, 0, 3 - lax.rem(step, 3)),
        )

    def lat_copy(step):
        member, flip = unpack(step)
        start = pl.multiple_of(chip_at(chip, flip) * span, span)
        return pltpu.make_async_copy(lat_ref.at[0, member, pl.ds(start, span)], lat_buf.at[step], lat_sem.at[step])

    def q_copy(step):
        member, flip = unpack(step)
        start = pl.multiple_of(chip_at(chip, flip) * span, span)
        return pltpu.make_async_copy(queries.at[step], q_out.at[member, pl.ds(start, span)], q_sem.at[step])

    def tok_copy(member):
        return pltpu.make_async_copy(tok_ref.at[0, member], tok_buf.at[member], tok_sem.at[member])

    def kv_copies(member):
        return (
            pltpu.make_async_copy(keys.at[member], k_out.at[member], k_sem.at[member]),
            pltpu.make_async_copy(values.at[member], v_out.at[member], v_sem.at[member]),
        )

    def core_copies(step):
        return (
            remote(part.at[step, 1 - core], got.at[step], core_send.at[step], core_recv.at[step], mate),
            remote(part_s.at[step, 1 - core], got_s.at[step], core_send_s.at[step], core_recv_s.at[step], mate),
        )

    def chip_copies(step):
        member, flip = unpack(step)
        peer = 2 * chip_at(chip, flip) + core
        place = 3 * member + flip - 1
        return (
            remote(stage.at[step], arrive.at[place], chip_send.at[place], chip_recv.at[place], peer),
            remote(stage_s.at[step], arrive_s.at[place], chip_send_s.at[place], chip_recv_s.at[place], peer),
        )

    tok_copy(0).start()
    masks = mask_loads(seg_ref, mask_ref, seg_buf, mask_buf, mask_sem)
    for copy in masks:
        copy.start()
    for step in range(4):
        lat_copy(step).start()
    tok_copy(1).start()
    for step in range(4, 2 * 4):
        lat_copy(step).start()
    greet([mate] + [2 * other + core for other in others])
    for copy in masks:
        copy.wait()
    mask_rows(seg_buf, mask_buf, count_ref, bias)

    def project(member):
        tok_copy(member).wait()
        hat, inverse = norm_parts(tok_buf[member].astype(F32))
        normed = (hat * tgain_ref[...]).astype(BF16)
        keys[member] = nn(normed, kw_ref[...]).astype(BF16)
        values[member] = nn(normed, vw_ref[...]).astype(BF16)
        for copy in kv_copies(member):
            copy.start()

    def ask(step):
        hat, inverse = norm_parts(lat_buf[step])
        normed = (hat * qgain_ref[...]).astype(BF16)
        queries[step] = (nn(normed, qw_ref[...]) * (D ** (-0.5) * LOG2E)).astype(BF16)

    def compute(step, ahead):
        member, flip = unpack(step)

        @pl.when(flip == 3)
        def _():
            project(member)

        if ahead:
            lat_copy(step + 1).wait()
        scores = nt(queries[step], keys[member])
        if ahead:
            ask(step + 1)
        raised = []
        for half in range(2):
            seen = bias[member, pl.ds(2 * chip_at(chip, flip) + half, 1), :]
            own = scores[half * ROWS:(half + 1) * ROWS] + seen
            top = jnp.max(own, axis=1, keepdims=True)
            own = jnp.exp2(own - top)
            part_s[step, half] = to_rows(top, jnp.sum(own, axis=1, keepdims=True))
            raised.append(own.astype(BF16))

        @pl.when(step > 0)
        def _():
            combine(step - 1)

        sums = nn(jnp.concatenate(raised, axis=0), values[member]).astype(BF16)
        for half in range(2):
            part[step, half] = sums[half * ROWS:(half + 1) * ROWS]
        for copy in core_copies(step):
            copy.start()
        if ahead:
            q_copy(step + 1).start()

    def merge(one, one_s, two, two_s):
        top = jnp.maximum(one_s[0:1], two_s[0:1])
        one_w, two_w = jnp.exp2(one_s[0:1] - top), jnp.exp2(two_s[0:1] - top)
        sums = one_s[1:2] * one_w + two_s[1:2] * two_w
        spare = jnp.zeros((6, ROWS), F32)
        weights = jnp.concatenate([one_w, two_w, spare], axis=0).T
        return one * weights[:, 0:1] + two * weights[:, 1:2], jnp.concatenate([top, sums, spare], axis=0)

    def combine(step):
        member, flip = unpack(step)
        for copy in core_copies(step):
            copy.wait_recv()
        added, figures = merge(
            part[step, core].astype(F32), part_s[step, core], got[step].astype(F32), got_s[step]
        )
        stage_s[step] = figures

        @pl.when(flip > 0)
        def _():
            stage[step] = added.astype(BF16)
            for copy in chip_copies(step):
                copy.start()

        @pl.when(flip == 0)
        def _():
            total[member] = added

    def finish(member):
        added, figures = total[member], stage_s[3 * MB + member]
        for flip in (1, 2, 3):
            for copy in chip_copies(3 * member + 3 - flip):
                copy.wait_recv()
            place = 3 * member + flip - 1
            added, figures = merge(added, figures, arrive[place].astype(F32), arrive_s[place])
        spare = jnp.zeros((7, ROWS), F32)
        inverse = jnp.concatenate([1.0 / figures[1:2], spare], axis=0).T
        att_ref[member] = added * inverse[:, 0:1]
        lse_ref[member] = jnp.concatenate([figures[0:1] + jnp.log2(figures[1:2]), spare], axis=0)

    def step_body(step, carry):
        @pl.when(step < 4 * MB - 1)
        def _():
            compute(step, True)

        @pl.when(step == 4 * MB - 1)
        def _():
            compute(step, False)
            combine(step)

        return carry

    lat_copy(0).wait()
    ask(0)
    q_copy(0).start()
    lax.fori_loop(0, 4 * MB, step_body, 0)
    for member in range(MB):
        finish(member)
    for member in range(MB):
        for copy in kv_copies(member):
            copy.wait()
    for step in range(4 * MB):
        q_copy(step).wait()
        for copy in core_copies(step):
            copy.wait_send()
        if step < 3 * MB:
            for copy in chip_copies(step):
                copy.wait_send()


def cross_forward(collective_id, *args):
    dma = pltpu.SemaphoreType.DMA
    span = 2 * ROWS
    steps = 4 * MB
    vmem = pl.BlockSpec(memory_space=pltpu.VMEM)
    hbm = pl.BlockSpec(memory_space=pl.ANY)
    return pl.pallas_call(
        cross_forward_kernel,
        in_specs=[hbm, hbm] + [vmem] * 5 + [hbm, hbm, pl.BlockSpec(memory_space=pltpu.SMEM)],
        out_specs=[hbm, hbm, hbm, vmem, vmem],
        out_shape=[
            jax.ShapeDtypeStruct((MB, TOK_DEV, D), BF16),
            jax.ShapeDtypeStruct((MB, TOK_DEV, D), BF16),
            jax.ShapeDtypeStruct((MB, L, D), BF16),
            jax.ShapeDtypeStruct((MB, ROWS, D), F32),
            jax.ShapeDtypeStruct((MB, 8, ROWS), F32),
        ],
        scratch_shapes=[
            pltpu.VMEM((MB, TOK_DEV, D), BF16),
            pltpu.VMEM((steps, span, D), F32),
            pltpu.VMEM((MB, TOK_DEV, D), BF16),
            pltpu.VMEM((MB, TOK_DEV, D), BF16),
            pltpu.VMEM((steps, span, D), BF16),
            pltpu.VMEM((MB, LGROUPS, TOK_DEV), F32),
            pltpu.VMEM((steps, 2, ROWS, D), BF16),
            pltpu.VMEM((steps, 2, 8, ROWS), F32),
            pltpu.VMEM((steps, ROWS, D), BF16),
            pltpu.VMEM((steps, 8, ROWS), F32),
            pltpu.VMEM((steps, ROWS, D), BF16),
            pltpu.VMEM((steps, 8, ROWS), F32),
            pltpu.VMEM((3 * MB, ROWS, D), BF16),
            pltpu.VMEM((3 * MB, 8, ROWS), F32),
            pltpu.VMEM((MB, ROWS, D), F32),
            pltpu.VMEM((MB, TOK_DEV), jnp.int32),
            pltpu.VMEM((MB, SCENES, LGROUPS), jnp.int32),
            dma((2,)), dma((MB,)), dma((steps,)), dma((MB,)), dma((MB,)), dma((steps,)),
        ] + [dma((steps,))] * 4 + [dma((3 * MB,))] * 4,
        compiler_params=pltpu.CompilerParams(
            collective_id=collective_id, has_side_effects=True, vmem_limit_bytes=56 * MIB
        ),
        cost_estimate=pl.CostEstimate(
            flops=14 * 10**9, bytes_accessed=22 * 10**6, transcendentals=4 * 10**6
        ),
        name="cross_forward",
    )(*args)


def cross_backward_kernel(
    items, grad_items,
    tok_ref, tgain_ref, kw_ref, vw_ref, seg_ref, mask_ref, count_ref, k_ref, v_ref, q_ref, up_ref, fig_ref,
    lat_ref, lup_ref, qgain_ref, qw_ref, fgain_ref, mgain_ref, sgain_ref, *refs,
):
    count, more = len(items), len(grad_items)
    parts, sources = refs[:count], refs[count:count + more]
    refs = refs[count + more:]
    dlat_ref, dtok_ref, dkw_ref, dvw_ref, dqw_ref, gains_ref = refs[:6]
    sums, helds = refs[6:6 + count], refs[6 + count:6 + count + more]
    rest = refs[6 + count + more:]
    cut = CROSS_SCRATCH + 3 * count + 2
    grp, grp_devices = grp_steps(items, parts, (), rest[CROSS_SCRATCH:cut], sums)
    tok, near_devices = tok_steps(grad_items, sources, rest[cut:])
    (tok_buf, keys, values, queries, ups, figs, bias, part, got, stage, arrive, far_in, total, dk, dv, dkw, dvw,
     dgain_ref, lat, lup, seg_buf, mask_buf, mask_sem, tail_sem,
     tok_sem, k_sem, v_sem, q_sem, out_sem, near_send, near_recv, far_send, far_recv, on_send, on_recv, own_sem,
     fig_send, fig_recv, core_send, core_recv, chip_send, chip_recv, half_send, half_recv) = rest[:CROSS_SCRATCH]
    me, core, chip, mate, others = places()
    span = 2 * ROWS

    def slot_of(step):
        late = lax.div(step + 3, 8)
        member = jnp.where(step == 1, 1, late)
        flip = jnp.where(step < 2, 0, jnp.where(late == 0, step - 1, 8 - step))
        return member, flip

    def loads(step):
        member, flip = slot_of(step)
        start = pl.multiple_of(chip_at(chip, flip) * span, span)
        ring = lax.rem(step, 4)
        return pltpu.make_async_copy(q_ref.at[member, pl.ds(start, span)], queries.at[ring], q_sem.at[ring])

    def tok_copies(member):
        return (
            pltpu.make_async_copy(k_ref.at[member], keys.at[member], k_sem.at[member]),
            pltpu.make_async_copy(v_ref.at[member], values.at[member], v_sem.at[member]),
            pltpu.make_async_copy(tok_ref.at[0, member], tok_buf.at[member], tok_sem.at[member]),
        )

    def out_copy(member):
        return pltpu.make_async_copy(dk.at[member], dtok_ref.at[0, member], out_sem.at[member])

    def own_copies(member):
        slot = 4 * member
        return (
            pltpu.make_async_copy(up_ref.at[member], ups.at[slot, core], own_sem.at[member, 0]),
            pltpu.make_async_copy(fig_ref.at[member], figs.at[slot, core], own_sem.at[member, 1]),
        )

    def near_copies(member):
        slot = 4 * member
        return [
            remote(up_ref.at[member], ups.at[slot, core], near_send.at[member, 0], near_recv.at[member, 0], mate),
            remote(fig_ref.at[member], figs.at[slot, core], near_send.at[member, 1], near_recv.at[member, 1], mate),
        ]

    half_rows = (pl.ds(0, ROWS // 2), pl.ds(ROWS // 2, ROWS // 2))

    def far_copies(slot):
        member, flip = slot // 4, slot % 4
        peer = 2 * chip_at(chip, flip) + core
        if flip < 3:
            return [
                remote(up_ref.at[member], ups.at[slot, core], far_send.at[slot, 0], far_recv.at[slot, 0], peer),
                remote(fig_ref.at[member], figs.at[slot, core], far_send.at[slot, 1], far_recv.at[slot, 1], peer),
            ]
        copies = []
        for half, (held, toward) in enumerate(((1, 2), (2, 1))):
            copies.append(remote(
                ups.at[4 * member + held, core, half_rows[half]], ups.at[slot, core, half_rows[half]],
                far_send.at[slot, half], far_recv.at[slot, half], 2 * chip_at(chip, toward) + core,
            ))
        copies.append(remote(
            figs.at[4 * member + 1, core], figs.at[slot, core], fig_send.at[member], fig_recv.at[member],
            2 * chip_at(chip, 2) + core,
        ))
        return copies

    def on_copies(slot):
        return (
            remote(ups.at[slot, core], ups.at[slot, core], on_send.at[slot, 0], on_recv.at[slot, 0], mate),
            remote(figs.at[slot, core], figs.at[slot, core], on_send.at[slot, 1], on_recv.at[slot, 1], mate),
        )

    def pass_on(slot):
        for copy in far_copies(slot):
            copy.wait_recv()
        for copy in on_copies(slot):
            copy.start()

    def pass_near(member):
        pass_on(4 * member + 1)
        pass_on(4 * member + 2)
        for copy in far_copies(4 * member + 3):
            copy.start()

    def half_copy(member, half):
        return remote(
            stage.at[4 * member + 3, half_rows[half]], far_in.at[member, half], half_send.at[member, half],
            half_recv.at[member, half], 2 * chip_at(chip, half + 1) + core,
        )

    def half_copies(member):
        return [half_copy(member, half) for half in range(2)]

    def core_copy(step):
        member, flip = slot_of(step)
        slot, ring = 4 * member + flip, lax.rem(step, 4)
        return remote(part.at[ring, 1 - core], got.at[slot], core_send.at[slot], core_recv.at[slot], mate)

    def chip_copy(slot):
        member, flip = slot // 4, slot % 4
        peer = 2 * chip_at(chip, flip) + core
        place = 2 * member + flip - 1
        return remote(stage.at[slot], arrive.at[place], chip_send.at[place], chip_recv.at[place], peer)

    def relay(member):
        for half in range(2):
            half_copy(member, half).wait_recv()
            slot = 4 * member + 2 - half
            joined = stage.at[slot, half_rows[half]]
            add(joined, joined, far_in.at[member, half])
            chip_copy(slot).start()

    masks = mask_loads(seg_ref, mask_ref, seg_buf, mask_buf, mask_sem)
    for copy in masks:
        copy.start()
    own_rows = pl.ds(pl.multiple_of(me * ROWS, ROWS), ROWS)
    tails = (
        pltpu.make_async_copy(lat_ref.at[0, :, own_rows], lat, tail_sem.at[0]),
        pltpu.make_async_copy(lup_ref, lup, tail_sem.at[1]),
    )
    for copy in own_copies(0):
        copy.start()
    for copy in tok_copies(0):
        copy.start()
    for step in range(3):
        loads(jnp.int32(step)).start()
    for copy in own_copies(1):
        copy.start()
    for copy in tok_copies(1):
        copy.start()
    for copy in tails:
        copy.start()
    greet_all([mate] + [2 * other + core for other in others], grp_devices)
    for member in range(MB):
        for copy in near_copies(member):
            copy.start()
    for flip in (1, 2):
        for copy in far_copies(flip):
            copy.start()
    tok[0](0)
    for item in range(count):
        grp[0](item)
    for copy in masks:
        copy.wait()
    mask_rows(seg_buf, mask_buf, count_ref, bias)

    def compute(step):
        member, flip = slot_of(step)
        slot = 4 * member + flip

        @pl.when(step < 2)
        def _():
            for copy in tok_copies(member):
                copy.wait()
            dk[member] = jnp.zeros((TOK_DEV, D), F32)
            dv[member] = jnp.zeros((TOK_DEV, D), F32)

        loads(step).wait()

        @pl.when(step + 3 < 4 * MB)
        def _():
            loads(step + 3).start()

        @pl.when(flip == 0)
        def _():
            for copy in own_copies(member):
                copy.wait()
            for copy in near_copies(member):
                copy.wait_recv()

        @pl.when(flip > 0)
        def _():
            for copy in on_copies(slot):
                copy.wait_recv()

        asked = queries[lax.rem(step, 4)]
        upstream = ups[slot].reshape(span, D)
        scores = nt(asked, keys[member])
        soft = nt(upstream, values[member])
        weights, grads = [], []
        for half in range(2):
            seen = bias[member, pl.ds(2 * chip_at(chip, flip) + half, 1), :]
            figures = figs[slot, half].T
            rows = slice(half * ROWS, (half + 1) * ROWS)
            weight = jnp.exp2(scores[rows] + seen - figures[:, 0:1])
            grads.append((weight * (soft[rows] - figures[:, 1:2])).astype(BF16))
            weights.append(weight.astype(BF16))
        weight = jnp.concatenate(weights, axis=0)
        grad = jnp.concatenate(grads, axis=0)
        middle(step)
        dv[member] += tn(weight, upstream)
        dk[member] += tn(grad, asked)
        asked_grad = (nn(grad, keys[member]) * D ** (-0.5)).astype(BF16)

        @pl.when(step >= 4)
        def _():
            core_copy(step - 4).wait_send()

        for half in range(2):
            part[lax.rem(step, 4), half] = asked_grad[half * ROWS:(half + 1) * ROWS]
        core_copy(step).start()

    def combine(step):
        member, flip = slot_of(step)
        slot = 4 * member + flip
        core_copy(step).wait_recv()
        added = part[lax.rem(step, 4), core].astype(F32) + got[slot].astype(F32)

        @pl.when(flip > 0)
        def _():
            stage[slot] = added.astype(BF16)

        @pl.when(flip == 0)
        def _():
            total[member] = added

    def tokens_back(member, half):
        gain = tgain_ref[...]
        rows = pl.ds(pl.multiple_of(half * span, span), span)
        hat, inverse = norm_parts(tok_buf[member, rows].astype(F32))
        normed = (hat * gain).astype(BF16)
        key_grad = (dk[member, rows] * LN2).astype(BF16)
        value_grad = dv[member, rows].astype(BF16)
        dkw[...] += tn(normed, key_grad)
        dvw[...] += tn(normed, value_grad)
        normed_grad = nt(key_grad, kw_ref[...]) + nt(value_grad, vw_ref[...])
        source_grad, gain_rows = norm_pull(hat, inverse, gain, normed_grad)
        dk[member, rows] = source_grad
        dgain_ref[...] += jnp.sum(gain_rows, axis=0, keepdims=True)

    def hold(item):
        helds[item][...] = tok[4](item).astype(helds[item].dtype)

    def middle(step):
        @pl.when(step > 0)
        def _():
            combine(step - 1)

        @pl.when(step == 1)
        def _():
            pass_near(0)

        @pl.when(step == 3)
        def _():
            pass_on(3)
            pass_near(1)

        @pl.when(step == 5)
        def _():
            for copy in half_copies(0):
                copy.start()

        @pl.when(step == 6)
        def _():
            for copy in half_copies(1):
                copy.start()
            relay(0)

    def step_body(step, carry):
        compute(step)

        @pl.when(step == 0)
        def _():
            for flip in (1, 2):
                for copy in far_copies(4 + flip):
                    copy.start()
            tok[1](0)
            tok[0](1)

        @pl.when(step == 1)
        def _():
            tok[0](2)

        @pl.when(step == 2)
        def _():
            tok[1](1)

        @pl.when(step == 4)
        def _():
            pass_on(7)
            for item in range(count):
                grp[4](item)
            tok[2](0)
            tok[1](2)

        @pl.when(step == 6)
        def _():
            tok[3](0)

        @pl.when(step == 4 * MB - 1)
        def _():
            combine(step)
            relay(1)

        return carry

    lax.fori_loop(0, 4 * MB, step_body, 0)

    def tokens_body(member, carry):
        for half in range(TOK_DEV // span):
            tokens_back(member, half)
        out_copy(member).start()

        @pl.when(member == 0)
        def _():
            helds[1][...] = tok[6](1)

        return carry

    dkw[...] = jnp.zeros_like(dkw)
    dvw[...] = jnp.zeros_like(dvw)
    dgain_ref[...] = jnp.zeros_like(dgain_ref)
    lax.fori_loop(0, MB, tokens_body, 0)
    dkw_ref[...] = dkw[...].astype(BF16)
    dvw_ref[...] = dvw[...].astype(BF16)
    hold(0)
    helds[2][...] = tok[6](2)
    for copy in tails:
        copy.wait()
    gain = qgain_ref[...]
    hat, inverse = norm_parts(lat[...].reshape(MB * ROWS, D))
    normed = (hat * gain).astype(BF16)
    asked_grads = []
    for member in range(MB):
        added = total[member]
        for flip in (1, 2):
            chip_copy(4 * member + flip).wait_recv()
            added = added + arrive[2 * member + flip - 1].astype(F32)
        asked_grads.append(added.astype(BF16))
    asked_grad = jnp.concatenate(asked_grads, axis=0)
    dqw_ref[...] = tn(normed, asked_grad).astype(BF16)
    source_grad, gain_rows = norm_pull(hat, inverse, gain, nt(asked_grad, qw_ref[...]))
    lup[...] += source_grad
    last = pltpu.make_async_copy(lup, dlat_ref, tail_sem.at[2])
    last.start()
    query_gain = jnp.sum(gain_rows, axis=0, keepdims=True)
    rows = jnp.concatenate(
        [dgain_ref[...], query_gain, fgain_ref[...], mgain_ref[...], sgain_ref[...], jnp.zeros((3, D), F32)], axis=0
    )
    gains_ref[...] = jnp.zeros_like(gains_ref)
    width = D // TOK
    for device in range(TOK):
        gains_ref[16 * device:16 * device + 8, 0:width] = rows[:, device * width:(device + 1) * width]
    grp[3]((0,))
    tok[5]((1, 2))
    last.wait()
    for step in range(4, 4 * MB):
        core_copy(jnp.int32(step)).wait_send()
    for member in range(MB):
        out_copy(member).wait()
        for copy in near_copies(member) + half_copies(member):
            copy.wait_send()
        for flip in range(4):
            slot = 4 * member + flip
            if flip > 0:
                for copy in far_copies(slot):
                    copy.wait_send()
                for copy in on_copies(slot):
                    copy.wait_send()
            if flip in (1, 2):
                chip_copy(slot).wait_send()


CROSS_SCRATCH = 44


def cross_backward(collective_id, arrays, grads, *args):
    dma = pltpu.SemaphoreType.DMA
    span = 2 * ROWS
    steps = 4 * MB
    vmem = pl.BlockSpec(memory_space=pltpu.VMEM)
    hbm = pl.BlockSpec(memory_space=pl.ANY)
    smem = pl.BlockSpec(memory_space=pltpu.SMEM)
    items, kinds = held_plan(arrays)
    sources, grad_items, grad_kinds, shapes = reduce_plan(grads)
    scratch = [
        pltpu.VMEM((MB, TOK_DEV, D), BF16),
        pltpu.VMEM((MB, TOK_DEV, D), BF16),
        pltpu.VMEM((MB, TOK_DEV, D), BF16),
        pltpu.VMEM((4, span, D), BF16),
        pltpu.VMEM((steps, 2, ROWS, D), BF16),
        pltpu.VMEM((steps, 2, 8, ROWS), F32),
        pltpu.VMEM((MB, LGROUPS, TOK_DEV), F32),
        pltpu.VMEM((4, 2, ROWS, D), BF16),
        pltpu.VMEM((steps, ROWS, D), BF16),
        pltpu.VMEM((steps, ROWS, D), BF16),
        pltpu.VMEM((2 * MB, ROWS, D), BF16),
        pltpu.VMEM((MB, 2, ROWS // 2, D), BF16),
        pltpu.VMEM((MB, ROWS, D), F32),
        pltpu.VMEM((MB, TOK_DEV, D), F32),
        pltpu.VMEM((MB, TOK_DEV, D), F32),
        pltpu.VMEM((D, D), F32),
        pltpu.VMEM((D, D), F32),
        pltpu.VMEM((1, D), F32),
        pltpu.VMEM((MB, ROWS, D), F32),
        pltpu.VMEM((MB * ROWS, D), F32),
        pltpu.VMEM((MB, TOK_DEV), jnp.int32),
        pltpu.VMEM((MB, SCENES, LGROUPS), jnp.int32),
        dma((2,)), dma((3,)),
        dma((MB,)), dma((MB,)), dma((MB,)), dma((4,)), dma((MB,)),
        dma((MB, 2)), dma((MB, 2)), dma((steps, 2)), dma((steps, 2)), dma((steps, 2)), dma((steps, 2)), dma((MB, 2)),
        dma((MB,)), dma((MB,)),
        dma((steps,)), dma((steps,)), dma((2 * MB,)), dma((2 * MB,)), dma((MB, 2)), dma((MB, 2)),
    ]
    return pl.pallas_call(
        functools.partial(cross_backward_kernel, items, grad_items),
        in_specs=[hbm] + [vmem] * 3 + [hbm, hbm, smem] + [hbm] * 7 + [vmem] * 5 + [vmem] * len(arrays) + [hbm] * len(grads),
        out_specs=[hbm, hbm] + [vmem] * (4 + len(arrays) + len(grads)),
        out_shape=[
            jax.ShapeDtypeStruct((MB * ROWS, D), F32),
            jax.ShapeDtypeStruct((1, MB, TOK_DEV, D), F32),
            jax.ShapeDtypeStruct((D, D), BF16),
            jax.ShapeDtypeStruct((D, D), BF16),
            jax.ShapeDtypeStruct((D, D), BF16),
            jax.ShapeDtypeStruct((16 * TOK, 128), F32),
        ] + [jax.ShapeDtypeStruct(array.shape, array.dtype) for array in arrays]
        + [
            jax.ShapeDtypeStruct((() if i == 0 else (2, 2)) + (high // 2, wide), kind)
            for i, ((high, wide), kind) in enumerate(zip(shapes, grad_kinds))
        ],
        scratch_shapes=scratch + grp_scratch(items, kinds) + tok_scratch(grad_items, grad_kinds),
        compiler_params=pltpu.CompilerParams(
            collective_id=collective_id, has_side_effects=True, vmem_limit_bytes=60 * MIB
        ),
        cost_estimate=pl.CostEstimate(
            flops=26 * 10**9, bytes_accessed=24 * 10**6, transcendentals=4 * 10**6
        ),
        name="cross_backward",
    )(*args, *arrays, *sources)


GELU_A = 0.7978845608028654
GELU_B = 0.044715


def gelu_parts(hidden):
    square = hidden * hidden
    bent = jnp.tanh(GELU_A * hidden * (1.0 + GELU_B * square))
    half = 0.5 * (1.0 + bent)
    slope = half + 0.5 * hidden * (1.0 - bent * bent) * (GELU_A * (1.0 + 3.0 * GELU_B * square))
    return hidden * half, slope


def greet_all(tok_devices, grp_devices=()):
    barrier = pltpu.get_barrier_semaphore()
    for axis, devices in (("tok", tok_devices), ("grp", grp_devices)):
        for device in devices:
            pl.semaphore_signal(
                barrier, inc=1, device_id={axis: device}, device_id_type=pl.DeviceIdType.MESH
            )
    pl.semaphore_wait(barrier, len(tok_devices) + len(grp_devices))


def all_peers():
    me, core, chip, mate, others = places()
    peers = []
    for other in others:
        peers += [2 * other + core, 2 * other + 1 - core]
    return me, peers + [mate]


def head_copies(row_side, head_side, to_heads, member, me, peers, send, recv, local):
    lanes = pl.ds(member * ROWS, ROWS)
    row_at = lambda device: row_side.at[:, device, :, lanes]
    head_at = lambda device: head_side.at[:, member, :, pl.ds(pl.multiple_of(device * ROWS, ROWS), ROWS)]
    source, target = (row_at, head_at) if to_heads else (head_at, row_at)
    copies = [
        remote(source(peer), target(me), send.at[slot, member], recv.at[slot, member], peer)
        for slot, peer in enumerate(peers)
    ]
    return copies, pltpu.make_async_copy(source(me), target(me), local.at[member])


QB = 1024
QB_BACK = 256


def latents_forward_kernel(
    lat_ref, att_ref, cot_ref, ow_ref, fgain_ref, fup_ref, fdown_ref, mgain_ref, proj_ref, mow_ref, sgain_ref,
    sup_ref, sdown_ref,
    out_ref, fmid_ref, mmid_ref, packed_ref, exact_ref, lse_ref, up_ref, mgrad_ref, ddown_ref, dup_ref, dmo_ref,
    dgain_ref,
    lat, att, cot, ow, fup, fdown, proj, mow, sup, sdown,
    out, fmid, mmid, heads, exact, up, mgrad, ddown, dup, dmo,
    rows_out, keys, values, mixed, mixed_rows, active, hidden_low, normed_low,
    load_sem, store_sem, send_a, recv_a, local_a, send_b, recv_b, local_b,
):
    me, peers = all_peers()
    own = pl.ds(pl.multiple_of(me * ROWS, ROWS), ROWS)
    names = ("lat", "att", "ow", "fup", "fdown", "proj", "mow", "sup", "sdown", "cot")
    loads = {}
    for i, (source, target) in enumerate((
        (lat_ref.at[0, :, own], lat), (att_ref, att), (ow_ref, ow), (fup_ref, fup), (fdown_ref, fdown),
        (proj_ref, proj), (mow_ref, mow), (sup_ref, sup), (sdown_ref, sdown), (cot_ref.at[0], cot),
    )):
        loads[names[i]] = pltpu.make_async_copy(source, target, load_sem.at[i])
        loads[names[i]].start()
    stores = []

    def store(source, target):
        stores.append(pltpu.make_async_copy(source, target, store_sem.at[len(stores)]))
        stores[-1].start()

    greet_all(peers)
    flat = (MB * ROWS, D)
    for name in ("lat", "att", "ow"):
        loads[name].wait()
    outward = [head_copies(rows_out, heads, True, member, me, peers, send_a, recv_a, local_a) for member in range(MB)]
    backward = [
        head_copies(mixed_rows, mixed, False, member, me, peers, send_b, recv_b, local_b) for member in range(MB)
    ]
    for member in range(MB):
        rows = slice(member * ROWS, (member + 1) * ROWS)
        first = lat[member] + nn(att[member].astype(BF16), ow[...])
        fmid[rows] = first
        normed = (norm_parts(first)[0] * fgain_ref[...]).astype(BF16)
        if member == 0:
            loads["fup"].wait()
            loads["fdown"].wait()
        mid = first
        for part in range(2):
            cut = slice(part * FF // 2, (part + 1) * FF // 2)
            mid = mid + nn(jax.nn.gelu(nn(normed, fup[:, cut])).astype(BF16), fdown[cut])
        mmid[rows] = mid
        normed = (norm_parts(mid)[0] * mgain_ref[...]).astype(BF16).T
        if member == 0:
            loads["proj"].wait()
        for kind, scale in enumerate((HD ** (-0.5) * LOG2E, 1.0, 1.0)):
            packed = tn(proj[:, kind * D:(kind + 1) * D], normed) * scale
            rows_out[kind, :, :, rows] = packed.astype(BF16).reshape(H, HD, ROWS)
        copies, here = outward[member]
        for copy in copies:
            copy.start()
        here.start()
    store(fmid, fmid_ref)
    store(mmid, mmid_ref)
    for member in range(MB):
        copies, here = outward[member]
        for copy in copies:
            copy.wait_recv()
        here.wait()
        store(heads.at[:, member], packed_ref.at[:, member])
        keys[...] = heads[1, member].T
        values[0:HD] = heads[2, member]
        values[HD:] = jnp.ones((16, L), BF16)

        def attend(step, carry, member=member):
            at = pl.ds(pl.multiple_of(step * QB, QB), QB)
            logits = nn(keys[...], heads[0, member, :, at])
            top = jnp.max(logits, axis=0, keepdims=True)
            both = nn(values[...], jnp.exp2(logits - top).astype(BF16))
            total = both[HD:HD + 1]
            result = both[0:HD] / total
            exact[member, :, at] = result
            mixed[0, member, :, at] = result.astype(BF16)
            lse_ref[member, :, at] = jnp.broadcast_to(top + jnp.log2(total), (8, QB))
            return carry

        lax.fori_loop(0, L // QB, attend, 0)
        for copy in backward[member][0] + [backward[member][1]]:
            copy.start()
    store(exact, exact_ref)
    loads["mow"].wait()
    loads["sup"].wait()
    loads["sdown"].wait()
    loads["cot"].wait()
    gains = []
    for member in range(MB):
        copies, here = backward[member]
        for copy in copies:
            copy.wait_recv()
        here.wait()
        rows = slice(member * ROWS, (member + 1) * ROWS)
        second = mmid[rows] + tn(mixed_rows[0, :, :, rows].reshape(D, ROWS), mow[...])
        hat, inverse = norm_parts(second)
        normed = (hat * sgain_ref[...]).astype(BF16)
        normed_low[rows] = normed
        upstream = cot[member]
        grad = upstream.astype(BF16)
        final = second
        normed_grad = jnp.zeros((ROWS, D), F32)
        for part in range(2):
            cut = slice(part * FF // 2, (part + 1) * FF // 2)
            act, slope = gelu_parts(nn(normed, sup[:, cut]))
            act = act.astype(BF16)
            active[rows, cut] = act
            final = final + nn(act, sdown[cut])
            hidden_grad = (slope * nt(grad, sdown[cut])).astype(BF16)
            hidden_low[rows, cut] = hidden_grad
            normed_grad = normed_grad + nt(hidden_grad, sup[:, cut])
        out[member] = final
        residual, gain_rows = norm_pull(hat, inverse, sgain_ref[...], normed_grad)
        gains.append(jnp.sum(gain_rows, axis=0, keepdims=True))
        upstream = upstream + residual
        up[rows] = upstream
        mgrad[0, :, :, rows] = nt(mow[...], upstream.astype(BF16)).astype(BF16).reshape(H, HD, ROWS)
    store(out, out_ref.at[0])
    store(up, up_ref)
    store(mgrad, mgrad_ref)
    dgain_ref[...] = gains[0] + gains[1]
    ddown[...] = tn(active[...], cot[...].reshape(flat).astype(BF16)).astype(BF16)
    store(ddown, ddown_ref)
    dup[...] = tn(normed_low[...], hidden_low[...]).astype(BF16)
    store(dup, dup_ref)
    dmo[...] = nn(mixed_rows[0].reshape(D, MB * ROWS), up[...].astype(BF16)).astype(BF16)
    store(dmo, dmo_ref)
    for copy in stores:
        copy.wait()
    for copies, here in outward + backward:
        for copy in copies:
            copy.wait_send()


def latents_forward(collective_id, *args):
    dma = pltpu.SemaphoreType.DMA
    vmem = pl.BlockSpec(memory_space=pltpu.VMEM)
    hbm = pl.BlockSpec(memory_space=pl.ANY)
    rows = MB * ROWS
    stored = [
        ((1, MB, ROWS, D), F32), ((rows, D), F32), ((rows, D), F32), ((3, MB, HD, L), BF16), ((MB, HD, L), F32),
        ((MB, 8, L), F32), ((rows, D), F32), ((1, H, HD, rows), BF16), ((FF, D), BF16), ((D, FF), BF16), ((D, D), BF16),
        ((1, D), F32),
    ]
    return pl.pallas_call(
        latents_forward_kernel,
        in_specs=[hbm, hbm, hbm, hbm, vmem, hbm, hbm, vmem, hbm, hbm, vmem, hbm, hbm],
        out_specs=[hbm] * 5 + [vmem] + [hbm] * 5 + [vmem],
        out_shape=[jax.ShapeDtypeStruct(shape, kind) for shape, kind in stored],
        scratch_shapes=[
            pltpu.VMEM((MB, ROWS, D), F32), pltpu.VMEM((MB, ROWS, D), F32), pltpu.VMEM((MB, ROWS, D), F32),
            pltpu.VMEM((D, D), BF16), pltpu.VMEM((D, FF), BF16), pltpu.VMEM((FF, D), BF16),
            pltpu.VMEM((D, 3 * D), BF16), pltpu.VMEM((D, D), BF16), pltpu.VMEM((D, FF), BF16),
            pltpu.VMEM((FF, D), BF16),
            pltpu.VMEM((MB, ROWS, D), F32), pltpu.VMEM((rows, D), F32), pltpu.VMEM((rows, D), F32),
            pltpu.VMEM((3, MB, HD, L), BF16), pltpu.VMEM((MB, HD, L), F32), pltpu.VMEM((rows, D), F32),
            pltpu.VMEM((1, H, HD, rows), BF16), pltpu.VMEM((FF, D), BF16), pltpu.VMEM((D, FF), BF16),
            pltpu.VMEM((D, D), BF16),
            pltpu.VMEM((3, H, HD, rows), BF16), pltpu.VMEM((L, HD), BF16), pltpu.VMEM((HD + 16, L), BF16),
            pltpu.VMEM((1, MB, HD, L), BF16), pltpu.VMEM((1, H, HD, rows), BF16),
            pltpu.VMEM((rows, FF), BF16), pltpu.VMEM((rows, FF), BF16), pltpu.VMEM((rows, D), BF16),
            dma((10,)), dma((11,)), dma((7, MB)), dma((7, MB)), dma((MB,)), dma((7, MB)), dma((7, MB)), dma((MB,)),
        ],
        compiler_params=pltpu.CompilerParams(
            collective_id=collective_id, has_side_effects=True, vmem_limit_bytes=60 * MIB
        ),
        cost_estimate=pl.CostEstimate(
            flops=20 * 10**9, bytes_accessed=30 * 10**6, transcendentals=10 * 10**6
        ),
        name="latents_forward",
    )(*args)


def levels():
    level = lax.axis_index("grp")
    odd = lax.rem(level, 2)
    return odd, level + 1 - 2 * odd, lax.rem(level + 2, 4)


def half_slices(rows, odd):
    half = rows // 2
    keep = pl.ds(pl.multiple_of(odd * half, half), half)
    away = pl.ds(pl.multiple_of((1 - odd) * half, half), half)
    return keep, away


def tok_steps(items, sources, scratch):
    n = len(items)
    mine, got, near_in, first_in, second_in = [scratch[i * n:(i + 1) * n] for i in range(5)]
    (local_sem, core_send, core_recv, near_send, near_recv, one_send, one_recv, two_send, two_recv) = scratch[5 * n:]
    me, core, chip, mate, (far, flip_x, flip_y) = places()
    x, y = lax.rem(chip, 2), lax.div(chip, 2)
    odd, level_near, level_far = levels()

    def core_copies(i):
        source, rows, row_at, columns, column_at, x_first = items[i]
        part = (pl.ds(row_at, rows), pl.ds(column_at, columns))
        return (
            remote(sources[source].at[:, :, 1 - core, *part], got[i], core_send.at[i], core_recv.at[i], mate),
            pltpu.make_async_copy(sources[source].at[:, :, core, *part], mine[i], local_sem.at[i]),
        )

    def near_copy(i):
        keep, away = half_slices(items[i][1], odd)
        return pltpu.make_async_remote_copy(
            src_ref=mine[i].at[:, :, away], dst_ref=near_in[i], send_sem=near_send.at[i], recv_sem=near_recv.at[i],
            device_id={"grp": level_near}, device_id_type=pl.DeviceIdType.MESH,
        )

    def first_copy(i):
        keep, away = half_slices(items[i][1], odd)
        x_first = items[i][-1]
        source = mine[i].at[:, 1 - x, keep] if x_first else mine[i].at[1 - y, :, keep]
        peer = 2 * (flip_x if x_first else flip_y) + core
        return remote(source, first_in[i], one_send.at[i], one_recv.at[i], peer)

    def second_copy(i):
        keep, away = half_slices(items[i][1], odd)
        x_first = items[i][-1]
        source = mine[i].at[1 - y, x, keep] if x_first else mine[i].at[y, 1 - x, keep]
        peer = 2 * (flip_y if x_first else flip_x) + core
        return remote(source, second_in[i], two_send.at[i], two_recv.at[i], peer)

    def core_sends(i):
        for copy in core_copies(i):
            copy.start()

    def core_sums(i):
        there, here = core_copies(i)
        there.wait_recv()
        here.wait()
        add(mine[i], mine[i], got[i])
        near_copy(i).start()

    def near_sums(i):
        keep, away = half_slices(items[i][1], odd)
        near_copy(i).wait_recv()
        held = mine[i].at[:, :, keep]
        add(held, held, near_in[i])
        first_copy(i).start()

    def first_sums(i):
        keep, away = half_slices(items[i][1], odd)
        first_copy(i).wait_recv()
        held = mine[i].at[:, x, keep] if items[i][-1] else mine[i].at[y, :, keep]
        add(held, held, first_in[i])
        second_copy(i).start()

    def second_sums(i):
        keep, away = half_slices(items[i][1], odd)
        second_copy(i).wait_recv()
        return mine[i][y, x, keep].astype(F32) + second_in[i][...].astype(F32)

    def near_hold(i):
        keep, away = half_slices(items[i][1], odd)
        near_copy(i).wait_recv()
        return mine[i][:, :, keep] + near_in[i][...]

    def finish(near_only=()):
        for i in range(n):
            core_copies(i)[0].wait_send()
            near_copy(i).wait_send()
            if i not in near_only:
                for copy in (first_copy(i), second_copy(i)):
                    copy.wait_send()

    return (core_sends, core_sums, near_sums, first_sums, second_sums, finish, near_hold), (
        mate, 2 * flip_x + core, 2 * flip_y + core)


def quad_steps(items, quads, results, scratch):
    n = len(items)
    first_in, joined, second_in = [scratch[i * n:(i + 1) * n] for i in range(3)]
    one_send, one_recv, two_send, two_recv = scratch[3 * n:]
    me, core, chip, mate, (far, flip_x, flip_y) = places()
    x, y = lax.rem(chip, 2), lax.div(chip, 2)

    def first_copy(i):
        x_first = items[i][-1]
        source = quads[i].at[:, 1 - x] if x_first else quads[i].at[1 - y]
        peer = 2 * (flip_x if x_first else flip_y) + core
        return remote(source, first_in[i], one_send.at[i], one_recv.at[i], peer)

    def second_copy(i):
        x_first = items[i][-1]
        source = joined[i].at[1 - y] if x_first else joined[i].at[1 - x]
        peer = 2 * (flip_y if x_first else flip_x) + core
        return remote(source, second_in[i], two_send.at[i], two_recv.at[i], peer)

    def first_start(i):
        first_copy(i).start()

    def first_sums(i):
        first_copy(i).wait_recv()
        add(joined[i], quads[i].at[:, x] if items[i][-1] else quads[i].at[y], first_in[i])
        second_copy(i).start()

    def second_sums(i):
        second_copy(i).wait_recv()
        add(results[i], joined[i].at[y] if items[i][-1] else joined[i].at[x], second_in[i])

    def finish():
        for i in range(n):
            for copy in (first_copy(i), second_copy(i)):
                copy.wait_send()

    return first_start, first_sums, second_sums, finish


def plain_steps(items, sources, scratch):
    n = len(items)
    mine, got, near_in, first_in, second_in = [scratch[i * n:(i + 1) * n] for i in range(5)]
    (local_sem, core_send, core_recv, near_send, near_recv, one_send, one_recv, two_send, two_recv) = scratch[5 * n:]
    me, core, chip, mate, (far, flip_x, flip_y) = places()
    x, y = lax.rem(chip, 2), lax.div(chip, 2)
    odd, level_near, level_far = levels()

    def core_copy(i):
        return remote(sources[i].at[:, :, 1 - core], got[i], core_send.at[i], core_recv.at[i], mate)

    def local_copy(i):
        return pltpu.make_async_copy(sources[i].at[:, :, core], mine[i], local_sem.at[i])

    def first_copy(i):
        x_first = items[i][-1]
        source = mine[i].at[:, 1 - x] if x_first else mine[i].at[1 - y]
        peer = 2 * (flip_x if x_first else flip_y) + core
        return remote(source, first_in[i], one_send.at[i], one_recv.at[i], peer)

    def second_copy(i):
        x_first = items[i][-1]
        source = mine[i].at[1 - y, x] if x_first else mine[i].at[y, 1 - x]
        peer = 2 * (flip_y if x_first else flip_x) + core
        return remote(source, second_in[i], two_send.at[i], two_recv.at[i], peer)

    def near_copy(i):
        keep, away = half_slices(items[i][1], odd)
        return pltpu.make_async_remote_copy(
            src_ref=mine[i].at[y, x, away], dst_ref=near_in[i], send_sem=near_send.at[i], recv_sem=near_recv.at[i],
            device_id={"grp": level_near}, device_id_type=pl.DeviceIdType.MESH,
        )

    def core_sends(i):
        core_copy(i).start()
        local_copy(i).start()

    def core_sums(i):
        core_copy(i).wait_recv()
        local_copy(i).wait()
        add(mine[i], mine[i], got[i])
        first_copy(i).start()

    def first_sums(i):
        first_copy(i).wait_recv()
        held = mine[i].at[:, x] if items[i][-1] else mine[i].at[y]
        add(held, held, first_in[i])
        second_copy(i).start()

    def second_sums(i):
        second_copy(i).wait_recv()
        held = mine[i].at[y, x]
        add(held, held, second_in[i])
        near_copy(i).start()

    def near_sums(i):
        keep, away = half_slices(items[i][1], odd)
        near_copy(i).wait_recv()
        return mine[i][y, x, keep].astype(F32) + near_in[i][...].astype(F32)

    def finish():
        for i in range(n):
            for copy in (core_copy(i), near_copy(i), first_copy(i), second_copy(i)):
                copy.wait_send()

    return (core_sends, core_sums, first_sums, second_sums, near_sums, finish), (
        mate, 2 * flip_x + core, 2 * flip_y + core)


def grp_steps(items, held, outs, scratch, joined=None):
    n = len(items)
    far_in, own_joined, near_in = [scratch[i * n:(i + 1) * n] for i in range(3)]
    z_send, z_recv = scratch[3 * n:]
    joined = own_joined if joined is None else joined
    odd, level_near, level_far = levels()

    def along(i, step):
        source, target, other = (
            (held[i], far_in[i], level_far),
            (joined[i], near_in[i], level_near),
        )[step]
        return pltpu.make_async_remote_copy(
            src_ref=source, dst_ref=target, send_sem=z_send.at[i, step], recv_sem=z_recv.at[i, step],
            device_id={"grp": other}, device_id_type=pl.DeviceIdType.MESH,
        )

    def store(i, odd_half, value):
        source, rows, row_at, columns, column_at, x_first = items[i]
        half = rows // 2
        start = pl.multiple_of(row_at + odd_half * half, half)
        outs[source][pl.ds(start, half), pl.ds(column_at, columns)] = value.astype(F32)

    def far_start(i):
        along(i, 0).start()

    def far_join(i):
        along(i, 0).wait_recv()
        add(joined[i], held[i], far_in[i])

    def near_start(i):
        along(i, 1).start()
        store(i, odd, joined[i][...])

    def far_sum(i):
        far_join(i)
        near_start(i)

    def near_store(i):
        along(i, 1).wait_recv()
        store(i, 1 - odd, near_in[i][...])

    def finish(steps=(0, 1)):
        for i in range(n):
            for step in steps:
                along(i, step).wait_send()

    return (far_start, far_sum, near_store, finish, far_join, near_start), (level_near, level_far)


def add(target, one, two):
    target[...] = one[...] + two[...]


def reduce_kernel(items, whole, square, joined, count, *refs):
    n, m, q, k = len(items), len(whole), len(square), len(joined)

    def take(length):
        nonlocal refs
        head, refs = refs[:length], refs[length:]
        return head

    sources, held, quads, done = take(count), take(m), take(q), take(k)
    outs, whole_outs, quad_outs, joined_outs = take(count), take(m), take(q), take(k)
    tok, near_devices = plain_steps(items, sources, take(5 * n + 9))
    own_held = take(n)
    late, grp_devices = grp_steps(items, own_held, outs, take(3 * n + 2))
    early, unused = grp_steps(whole, held, whole_outs, take(3 * m + 2))
    quad_held = take(q)
    sums = quad_steps(square, quads, quad_held, take(3 * q + 4))
    mid, unused = grp_steps(square, quad_held, quad_outs, take(3 * q + 2))
    first, unused = grp_steps(joined, done, joined_outs, refs, done)
    greet_all(near_devices, grp_devices)
    for i in range(n):
        tok[0](i)
    for i in range(m):
        early[0](i)
    for i in range(q):
        sums[0](i)
    for i in range(n):
        tok[1](i)
    for i in range(k):
        first[5](i)
    for i in range(q):
        sums[1](i)
    for i in range(n):
        tok[2](i)
    for i in range(q):
        sums[2](i)
        mid[0](i)
    for i in range(n):
        tok[3](i)
    for i in range(n):
        own_held[i][...] = tok[4](i).astype(own_held[i].dtype)
        late[0](i)
    for i in range(m):
        early[1](i)
    for i in range(k):
        first[2](i)
    for i in range(q):
        mid[1](i)
    for i in range(n):
        late[1](i)
    for i in range(m):
        early[2](i)
    for i in range(q):
        mid[2](i)
    for i in range(n):
        late[2](i)
    tok[-1]()
    sums[-1]()
    late[3]()
    early[3]()
    mid[3]()
    first[3]((1,))


def reduce_plan(arrays):
    sources, items = [], []
    for source, array in enumerate(arrays):
        rows, columns = array.shape[0] // TOK, array.shape[1]
        sources.append(array.reshape(2, 2, 2, rows, columns))
        items.append((source, rows, 0, columns, 0, source % 2 == 0))
    kinds = [array.dtype for array in arrays]
    shapes = [(array.shape[0] // TOK, array.shape[1]) for array in arrays]
    return sources, tuple(items), kinds, shapes


def held_plan(arrays):
    items = tuple((i, 2 * array.shape[0], 0, array.shape[1], 0, True) for i, array in enumerate(arrays))
    return items, [array.dtype for array in arrays]


def item_blocks(items, kinds, lead, part):
    return [pltpu.VMEM(lead + (item[1] // part, item[3]), kind) for item, kind in zip(items, kinds)]


def quad_plan(arrays, x_firsts):
    items = tuple(
        (i, 2 * array.shape[2], 0, array.shape[3], 0, x_first) for i, (array, x_first) in enumerate(zip(arrays, x_firsts))
    )
    return items, [array.dtype for array in arrays]


def quad_scratch(items, kinds):
    blocks = functools.partial(item_blocks, items, kinds)
    return blocks((2,), 2) + blocks((2,), 2) + blocks((), 2) + [pltpu.SemaphoreType.DMA((len(items),))] * 4


def plain_scratch(items, kinds):
    blocks = functools.partial(item_blocks, items, kinds)
    return (blocks((2, 2), 1) + blocks((2, 2), 1) + blocks((), 2) + blocks((2,), 1) + blocks((), 1)
            + [pltpu.SemaphoreType.DMA((len(items),))] * 9)


def tok_scratch(items, kinds):
    blocks = functools.partial(item_blocks, items, kinds)
    return (blocks((2, 2), 1) + blocks((2, 2), 1) + blocks((2, 2), 2) + blocks((2,), 2) + blocks((), 2)
            + [pltpu.SemaphoreType.DMA((len(items),))] * 9)


def grp_scratch(items, kinds):
    blocks = functools.partial(item_blocks, items, kinds)
    return blocks((), 2) * 3 + [pltpu.SemaphoreType.DMA((len(items), 2))] * 2


def reduce_grads(collective_id, arrays, held, quads, x_firsts, done):
    sources, items, kinds, shapes = reduce_plan(arrays)
    whole, whole_kinds = held_plan(held)
    square, square_kinds = quad_plan(quads, x_firsts)
    joined, joined_kinds = held_plan(done)
    vmem = pl.BlockSpec(memory_space=pltpu.VMEM)
    hbm = pl.BlockSpec(memory_space=pl.ANY)
    rest = len(held) + len(quads) + len(done)
    return pl.pallas_call(
        functools.partial(reduce_kernel, items, whole, square, joined, len(arrays)),
        in_specs=[hbm] * len(arrays) + [vmem] * rest,
        out_specs=[vmem] * (len(arrays) + rest),
        out_shape=[jax.ShapeDtypeStruct(shape, F32) for shape in shapes]
        + [jax.ShapeDtypeStruct((item[1], item[3]), F32) for item in whole + square + joined],
        scratch_shapes=plain_scratch(items, kinds) + item_blocks(items, kinds, (), 2) + grp_scratch(items, kinds)
        + grp_scratch(whole, whole_kinds) + item_blocks(square, square_kinds, (), 2)
        + quad_scratch(square, square_kinds) + grp_scratch(square, square_kinds) + grp_scratch(joined, joined_kinds),
        compiler_params=pltpu.CompilerParams(
            collective_id=collective_id, has_side_effects=True, vmem_limit_bytes=56 * MIB
        ),
        name="reduce_grads",
    )(*sources, *held, *quads, *done)


def write_parts(shape):
    if len(shape) < 4:
        return [()]
    half = shape[2] // 2
    return [(0, member, pl.ds(part * half, half)) for member in range(shape[1]) for part in range(2)]


def write_kernel(count, *refs):
    sources, gain_ref, outs = refs[:count], refs[count], refs[count + 1:2 * count + 1]
    gain_outs, buffers = refs[2 * count + 1:-count - 2], refs[-count - 2:-2]
    in_sem, out_sem = refs[-2:]
    ins, backs = [], []
    for source, buffer, out in zip(sources, buffers, outs):
        for part in write_parts(source.shape):
            view = lambda ref: ref.at[part] if part else ref
            at = len(ins)
            ins.append(pltpu.make_async_copy(view(source), view(buffer), in_sem.at[at]))
            backs.append(pltpu.make_async_copy(view(buffer), view(out), out_sem.at[at]))
            ins[-1].start()
    for i, out in enumerate(gain_outs):
        out[...] = gain_ref[i:i + 1, 0:D // TOK]
    for inward, outward in zip(ins, backs):
        inward.wait()
        outward.start()
    for copy in backs:
        copy.wait()


def write_results(results, gains, gain_count):
    n = len(results)
    parts = sum(len(write_parts(result.shape)) for result in results)
    hbm, vmem = pl.BlockSpec(memory_space=pl.ANY), pl.BlockSpec(memory_space=pltpu.VMEM)
    return pl.pallas_call(
        functools.partial(write_kernel, n),
        in_specs=[hbm] * n + [vmem],
        out_specs=[hbm] * n + [vmem] * gain_count,
        out_shape=[jax.ShapeDtypeStruct(result.shape, result.dtype) for result in results]
        + [jax.ShapeDtypeStruct((1, D // TOK), F32)] * gain_count,
        scratch_shapes=[pltpu.VMEM(result.shape, result.dtype) for result in results]
        + [pltpu.SemaphoreType.DMA((parts,)), pltpu.SemaphoreType.DMA((parts,))],
        compiler_params=pltpu.CompilerParams(vmem_limit_bytes=60 * MIB),
        name="write_results",
    )(*results, gains)


def latents_backward_kernel(items, *refs):
    (mgrad_ref, packed_ref, exact_ref, lse_ref, up_ref, mmid_ref, fmid_ref, att_ref, clse_ref, ow_ref, fgain_ref,
     fup_ref, fdown_ref, mgain_ref, proj_ref) = refs[:15]
    count = max(item[0] for item in items) + 1
    sources = refs[15:15 + count]
    (agrad_ref, fig_ref, lup_ref, dup_ref, ddown_ref, dproj_ref, dout_ref, dmgain_ref, dfgain_ref) = refs[
        15 + count:24 + count]
    reduced = refs[24 + count:24 + 2 * count]
    rest = refs[24 + 2 * count:]
    (heads, exact, ups, mmid, fmid, att, ow, fup, fdown, proj, keys, values, upstream_heads, key_acc, value_acc,
     grads, back, agrad, lup, dup, ddown, dproj, dout, hidden, active, hidden_low, grad_low,
     load_sem, store_sem, send_a, recv_a, local_a, send_b, recv_b, local_b) = rest[:35]
    me, peers = all_peers()
    reducer, near_devices = tok_steps(items, sources, rest[35:])
    core_sends, core_sums, near_sums, first_sums, second_sums, finish = reducer[:6]
    odd, level_near, level_far = levels()

    def hold(item):
        reduced[item][...] = second_sums(item).astype(reduced[item].dtype)

    names = ("heads", "exact", "fmid", "fup", "up", "mmid", "proj", "fdown", "att", "ow")
    loads = {}
    for i, (source, target) in enumerate((
        (packed_ref, heads), (exact_ref, exact), (fmid_ref, fmid), (fup_ref, fup), (up_ref, ups), (mmid_ref, mmid),
        (proj_ref, proj), (fdown_ref, fdown), (att_ref, att), (ow_ref, ow),
    )):
        loads[names[i]] = pltpu.make_async_copy(source, target, load_sem.at[i])
        loads[names[i]].start()
    stores = []

    def store(source, target):
        stores.append(pltpu.make_async_copy(source, target, store_sem.at[len(stores)]))
        stores[-1].start()

    greet_all(peers, (level_near,))
    outward = [
        head_copies(mgrad_ref, upstream_heads, True, member, me, peers, send_a, recv_a, local_a) for member in range(MB)
    ]
    backward = [head_copies(back, grads, False, member, me, peers, send_b, recv_b, local_b) for member in range(MB)]
    for copies, here in outward:
        for copy in copies:
            copy.start()
        here.start()
    core_sends(0)
    loads["fmid"].wait()
    loads["fup"].wait()
    first_hat, first_inverse = norm_parts(fmid[...])
    first_normed = (first_hat * fgain_ref[...]).astype(BF16)
    hidden[...] = nn(first_normed, fup[...])
    core_sums(0)
    loads["heads"].wait()
    loads["exact"].wait()
    for member in range(MB):
        keys[...] = heads[1, member].T
        values[...] = heads[2, member].T
        key_acc[...] = jnp.zeros_like(key_acc)
        value_acc[...] = jnp.zeros_like(value_acc)
        copies, here = outward[member]
        for copy in copies:
            copy.wait_recv()
        here.wait()
        if member == 0:
            core_sends(1)
            core_sends(2)

        def attend_back(step, carry, member=member):
            at = pl.ds(pl.multiple_of(step * QB_BACK, QB_BACK), QB_BACK)
            queries = heads[0, member, :, at]
            upstream = upstream_heads[0, member, :, at]
            inner = jnp.sum(upstream.astype(F32) * exact[member, :, at], axis=0, keepdims=True)
            softened = jnp.exp2(nn(keys[...], queries) - lse_ref[member, 0:1, at])
            logit_grad = (softened * (nn(values[...], upstream) - inner)).astype(BF16)
            value_acc[...] += nt(upstream, softened.astype(BF16))
            key_acc[...] += nt(queries, logit_grad)
            grads[0, member, :, at] = (nn(heads[1, member], logit_grad) * HD ** (-0.5)).astype(BF16)
            return carry

        steps = L // QB_BACK
        lax.fori_loop(0, steps, attend_back, 0)
        grads[1, member] = (key_acc[...] * LN2).astype(BF16)
        grads[2, member] = value_acc[...].astype(BF16)
        for copy in backward[member][0] + [backward[member][1]]:
            copy.start()
        if member == 0:
            near_sums(0)
            core_sums(1)
            core_sums(2)
    loads["up"].wait()
    loads["mmid"].wait()
    loads["proj"].wait()
    loads["fdown"].wait()
    mixer_hat, mixer_inverse = norm_parts(mmid[...])
    mixer_normed = (mixer_hat * mgain_ref[...]).astype(BF16).T
    loads["att"].wait()
    loads["ow"].wait()
    mixer_gains, first_gains = [], []

    def rows_back(member):
        copies, here = backward[member]
        for copy in copies:
            copy.wait_recv()
        here.wait()
        rows = slice(member * ROWS, (member + 1) * ROWS)
        normed_grad = nn(proj[...], back[:, :, :, rows].reshape(3 * D, ROWS)).T
        residual, gain_rows = norm_pull(mixer_hat[rows], mixer_inverse[rows], mgain_ref[...], normed_grad)
        mixer_gains.append(jnp.sum(gain_rows, axis=0, keepdims=True))
        upstream = ups[rows] + residual
        grad = upstream.astype(BF16)
        grad_low[rows] = grad
        normed_grad = jnp.zeros((ROWS, D), F32)
        for part in range(2):
            cut = slice(part * FF // 2, (part + 1) * FF // 2)
            act, slope = gelu_parts(hidden[rows, cut])
            active[rows, cut] = act.astype(BF16)
            hidden_grad = (slope * nt(grad, fdown[cut])).astype(BF16)
            hidden_low[rows, cut] = hidden_grad
            normed_grad = normed_grad + nt(hidden_grad, fup[:, cut])
        residual, gain_rows = norm_pull(first_hat[rows], first_inverse[rows], fgain_ref[...], normed_grad)
        first_gains.append(jnp.sum(gain_rows, axis=0, keepdims=True))
        upstream = upstream + residual
        lup[rows] = upstream
        attended_grad = nt(upstream.astype(BF16), ow[...]).astype(BF16)
        agrad[member] = attended_grad
        inner = jnp.sum(attended_grad.astype(F32) * att[member], axis=1, keepdims=True)
        fig_ref[member] = jnp.concatenate(
            [clse_ref[member, 0:1], to_rows(inner, inner)[0:1], jnp.zeros((6, ROWS), F32)], axis=0
        )

    rows_back(0)
    first_sums(0)
    near_sums(1)
    near_sums(2)
    rows_back(1)
    hold(0)
    first_sums(1)
    first_sums(2)
    store(lup, lup_ref)
    store(agrad, agrad_ref)
    dmgain_ref[...] = mixer_gains[0] + mixer_gains[1]
    dfgain_ref[...] = first_gains[0] + first_gains[1]
    grad = grad_low[...]
    ddown[...] = tn(active[...], grad).astype(BF16)
    store(ddown, ddown_ref)
    dup[...] = tn(first_normed, hidden_low[...]).astype(BF16)
    store(dup, dup_ref)
    dproj[...] = nt(mixer_normed, back[...].reshape(3 * D, MB * ROWS)).astype(BF16)
    store(dproj, dproj_ref)
    dout[...] = tn(att[...].reshape(MB * ROWS, D).astype(BF16), lup[...].astype(BF16)).astype(BF16)
    store(dout, dout_ref)
    hold(1)
    hold(2)
    finish()
    for copy in stores:
        copy.wait()
    for copies, here in outward + backward:
        for copy in copies:
            copy.wait_send()


def latents_backward(collective_id, arrays, *args):
    dma = pltpu.SemaphoreType.DMA
    vmem = pl.BlockSpec(memory_space=pltpu.VMEM)
    hbm = pl.BlockSpec(memory_space=pl.ANY)
    rows = MB * ROWS
    sources, items, kinds, shapes = reduce_plan(arrays)
    reduced = [jax.ShapeDtypeStruct((rows_ // 2, columns), kind) for (rows_, columns), kind in zip(shapes, kinds)]
    stored = [
        ((MB, ROWS, D), BF16), ((MB, 8, ROWS), F32), ((rows, D), F32), ((D, FF), BF16), ((FF, D), BF16),
        ((D, 3 * D), BF16), ((D, D), BF16), ((1, D), F32), ((1, D), F32),
    ]
    return pl.pallas_call(
        functools.partial(latents_backward_kernel, items),
        in_specs=[hbm, hbm, hbm, vmem, hbm, hbm, hbm, hbm, vmem, hbm, vmem, hbm, hbm, vmem, hbm] + [hbm] * len(arrays),
        out_specs=[hbm, vmem] + [hbm] * 5 + [vmem] * (2 + len(arrays)),
        out_shape=[jax.ShapeDtypeStruct(shape, kind) for shape, kind in stored] + reduced,
        scratch_shapes=[
            pltpu.VMEM((3, MB, HD, L), BF16), pltpu.VMEM((MB, HD, L), F32), pltpu.VMEM((rows, D), F32),
            pltpu.VMEM((rows, D), F32), pltpu.VMEM((rows, D), F32), pltpu.VMEM((MB, ROWS, D), F32),
            pltpu.VMEM((D, D), BF16), pltpu.VMEM((D, FF), BF16), pltpu.VMEM((FF, D), BF16),
            pltpu.VMEM((D, 3 * D), BF16), pltpu.VMEM((L, HD), BF16), pltpu.VMEM((L, HD), BF16),
            pltpu.VMEM((1, MB, HD, L), BF16), pltpu.VMEM((HD, L), F32), pltpu.VMEM((HD, L), F32),
            pltpu.VMEM((3, MB, HD, L), BF16), pltpu.VMEM((3, H, HD, rows), BF16),
            pltpu.VMEM((MB, ROWS, D), BF16), pltpu.VMEM((rows, D), F32), pltpu.VMEM((D, FF), BF16),
            pltpu.VMEM((FF, D), BF16), pltpu.VMEM((D, 3 * D), BF16), pltpu.VMEM((D, D), BF16),
            pltpu.VMEM((rows, FF), F32), pltpu.VMEM((rows, FF), BF16), pltpu.VMEM((rows, FF), BF16),
            pltpu.VMEM((rows, D), BF16),
            dma((10,)), dma((6,)), dma((7, MB)), dma((7, MB)), dma((MB,)), dma((7, MB)), dma((7, MB)), dma((MB,)),
        ] + tok_scratch(items, kinds),
        compiler_params=pltpu.CompilerParams(
            collective_id=collective_id, has_side_effects=True, vmem_limit_bytes=61 * MIB
        ),
        cost_estimate=pl.CostEstimate(
            flops=35 * 10**9, bytes_accessed=36 * 10**6, transcendentals=10 * 10**6
        ),
        name="latents_backward",
    )(*args, *sources)


def fast_body(
    tokens,
    latents,
    segments,
    scene_mask,
    counts,
    token_gain,
    query_gain,
    query_weight,
    key_weight,
    value_weight,
    output_weight,
    first_gain,
    first_up,
    first_down,
    mixer_gain,
    mixer_project,
    mixer_output,
    second_gain,
    second_up,
    second_down,
    cotangent,
):
    scenes = (segments, scene_mask, counts)
    keys, values, queries, attended, lse = cross_forward(
        0, tokens, latents, token_gain[None], query_gain[None], query_weight, key_weight, value_weight, *scenes
    )
    (latents_out, first_mid, mixer_mid, packed, exact, head_lse, upstream, mixed_grad, d_second_down, d_second_up,
     d_mixer_output, d_second_gain) = latents_forward(
        1, latents, attended, cotangent, output_weight, first_gain[None], first_up, first_down, mixer_gain[None],
        mixer_project, mixer_output, second_gain[None], second_up, second_down,
    )
    (attended_grad, figures, upstream, d_first_up, d_first_down, d_project, d_output, d_mixer_gain, d_first_gain,
     *early) = latents_backward(
        2, [d_second_up, d_second_down, d_mixer_output], mixed_grad, packed, exact, head_lse, upstream, mixer_mid,
        first_mid, attended, lse, output_weight, first_gain[None], first_up, first_down, mixer_gain[None], mixer_project,
    )
    latents_grad, tokens_grad, d_key, d_value, d_query, gains, *rest = cross_backward(
        5, early, [d_first_up, d_first_down, d_project], tokens, token_gain[None], key_weight, value_weight,
        *scenes, keys, values, queries, attended_grad, figures, latents, upstream, query_gain[None], query_weight,
        d_first_gain, d_mixer_gain, d_second_gain,
    )
    early, held, quads = rest[:len(early)], rest[len(early):len(early) + 1], rest[len(early) + 1:]
    o_output, o_key, o_value, o_query, gains, *late = reduce_grads(
        7, [d_output, d_key, d_value, d_query, gains], held, quads, (False, True), early
    )
    late, early = late[:3], late[3:]
    (latents_out, latents_grad, tokens_grad, o_second_up, o_second_down, o_mixer_output, o_first_up, o_first_down,
     o_project, o_output, o_key, o_value, o_query, *o_gains) = write_results(
        [latents_out, latents_grad.reshape(latents_out.shape), tokens_grad, *early, *late, o_output, o_key, o_value, o_query], gains, 5
    )
    o_gains = [gain.reshape(D // TOK) for gain in o_gains]
    return (
        latents_out,
        latents_grad,
        tokens_grad,
        o_gains[0],
        o_gains[1],
        o_query,
        o_key,
        o_value,
        o_output,
        o_gains[2],
        o_first_up,
        o_first_down,
        o_gains[3],
        o_project,
        o_mixer_output,
        o_gains[4],
        o_second_up,
        o_second_down,
    )


IN_SPECS = (
    P("grp", None, "tok", None),
    P("grp", None, None, None),
    P("grp", None, "tok"),
    P("grp", None, None, None),
    P("grp", None, "tok"),
    P(),
    P(),
    P(),
    P(),
    P(),
    P(),
    P(),
    P(),
    P(),
    P(),
    P(),
    P(),
    P(),
    P(),
    P(),
    P("grp", None, "tok", None),
)
OUT_SPECS = (
    P("grp", None, "tok", None),
    P("grp", None, "tok", None),
    P("grp", None, "tok", None),
    P("tok"),
    P("tok"),
    P("tok", None),
    P("tok", None),
    P("tok", None),
    P("tok", None),
    P("tok"),
    P("tok", None),
    P("tok", None),
    P("tok"),
    P("tok", None),
    P("tok", None),
    P("tok"),
    P("tok", None),
    P("tok", None),
)


def solution(mesh):
    return jax.shard_map(
        fast_body if mesh.shape["tok"] == TOK else general_body,
        mesh=mesh,
        in_specs=IN_SPECS,
        out_specs=OUT_SPECS,
        check_vma=False,
    )
```

```python
import functools

import jax
import jax.numpy as jnp
from jax import lax
from jax.experimental import pallas as pl
from jax.experimental.pallas import tpu as pltpu
from jax.sharding import PartitionSpec as P

D = 512
L = 2048
H = 8
HD = 64
TOK_DEV = 1024
MB = 2
SCENES = 8
LGROUPS = 8


EPS = 1e-05
NEG = -1e30


def norm_rows(values, gain):
    centre = values - jnp.mean(values, axis=-1, keepdims=True)
    spread = jnp.mean(centre * centre, axis=-1, keepdims=True)
    return centre * lax.rsqrt(spread + EPS) * gain


def norm_back(values, gain, upstream):
    unused, pull = jax.vjp(norm_rows, values, gain)
    return pull(upstream)


def gelu_back(hidden, upstream):
    unused, pull = jax.vjp(jax.nn.gelu, hidden)
    return pull(upstream)[0]


def product_plain(left, right):
    return jnp.dot(left, right, preferred_element_type=jnp.float32)


def product_rows(left, right):
    return lax.dot_general(
        left, right, (((0,), (0,)), ((), ())), preferred_element_type=jnp.float32
    )


def product_cols(left, right):
    return lax.dot_general(
        left, right, (((1,), (1,)), ((), ())), preferred_element_type=jnp.float32
    )


def add_term(store, name, value):
    if name in store:
        store[name] = store[name] + value
    else:
        store[name] = value


def project_tokens(tokens, member, token_gain, key_weight, value_weight):
    source = tokens[0, member].astype(jnp.float32)
    normed = norm_rows(source, token_gain).astype(jnp.bfloat16)
    key_rows = product_plain(normed, key_weight).astype(jnp.bfloat16)
    value_rows = product_plain(normed, value_weight).astype(jnp.bfloat16)
    return (source, normed, key_rows, value_rows)


def mlp_forward(residual, gain, up_weight, down_weight):
    normed = norm_rows(residual, gain).astype(jnp.bfloat16)
    hidden = product_plain(normed, up_weight)
    active = jax.nn.gelu(hidden).astype(jnp.bfloat16)
    return (residual + product_plain(active, down_weight), (normed, hidden, active))


def mlp_backward(residual, gain, up_weight, down_weight, saved, upstream):
    normed, hidden, active = saved
    grad_low = upstream.astype(jnp.bfloat16)
    grad_down = product_rows(active, grad_low)
    hidden_grad = gelu_back(hidden, product_cols(grad_low, down_weight)).astype(jnp.bfloat16)
    grad_up = product_rows(normed, hidden_grad)
    residual_grad, grad_gain = norm_back(residual, gain, product_cols(hidden_grad, up_weight))
    return (upstream + residual_grad, grad_gain, grad_up, grad_down)


def mixer_forward(residual, gain, project, output):
    own_rows = residual.shape[0]
    normed = norm_rows(residual, gain).astype(jnp.bfloat16)
    packed = product_plain(normed, project).astype(jnp.bfloat16)
    pair_rows = lax.all_gather(packed[:, D:], "tok", axis=0, tiled=True)
    every = pair_rows.shape[0]
    own_queries = packed[:, :D].reshape(own_rows, H, HD)
    keys = pair_rows[:, :D].reshape(every, H, HD)
    values = pair_rows[:, D:].reshape(every, H, HD)
    logits = jnp.einsum(
        "qhd,khd->hqk", own_queries, keys, preferred_element_type=jnp.float32
    ) * HD ** (-0.5)
    peak_row = jnp.max(logits, axis=-1, keepdims=True)
    raised = jnp.exp(logits - peak_row)
    softened = raised / jnp.sum(raised, axis=-1, keepdims=True)
    softened_low = softened.astype(jnp.bfloat16)
    mixed_rows = jnp.einsum(
        "hqk,khd->qhd", softened_low, values, preferred_element_type=jnp.float32
    )
    mixed_rows = mixed_rows.reshape(own_rows, D).astype(jnp.bfloat16)
    return (
        residual + product_plain(mixed_rows, output),
        (normed, own_queries, keys, values, softened, softened_low, mixed_rows),
    )


def mixer_backward(residual, gain, project, output, saved, upstream):
    normed, own_queries, keys, values, softened, softened_low, mixed_rows = saved
    own_rows = upstream.shape[0]
    every = keys.shape[0]
    grad_low = upstream.astype(jnp.bfloat16)
    grad_output = product_rows(mixed_rows, grad_low)
    mixed_grad = product_cols(grad_low, output).astype(jnp.bfloat16).reshape(own_rows, H, HD)
    value_grad = jnp.einsum(
        "hqk,qhd->khd", softened_low, mixed_grad, preferred_element_type=jnp.float32
    )
    soft_grad = jnp.einsum("qhd,khd->hqk", mixed_grad, values, preferred_element_type=jnp.float32)
    logit_grad = softened * (soft_grad - jnp.sum(soft_grad * softened, axis=-1, keepdims=True))
    logit_grad = logit_grad.astype(jnp.bfloat16)
    query_grad = jnp.einsum(
        "hqk,khd->qhd", logit_grad, keys, preferred_element_type=jnp.float32
    ) * HD ** (-0.5)
    key_grad = jnp.einsum(
        "hqk,qhd->khd", logit_grad, own_queries, preferred_element_type=jnp.float32
    ) * HD ** (-0.5)
    pair_terms = jnp.concatenate([key_grad.reshape(every, D), value_grad.reshape(every, D)], axis=1)
    pair_grad = lax.psum_scatter(
        pair_terms.astype(jnp.bfloat16), "tok", scatter_dimension=0, tiled=True
    ).astype(jnp.float32)
    packed_grad = jnp.concatenate([query_grad.reshape(own_rows, D), pair_grad], axis=1).astype(
        jnp.bfloat16
    )
    grad_project = product_rows(normed, packed_grad)
    residual_grad, grad_gain = norm_back(residual, gain, product_cols(packed_grad, project))
    return (upstream + residual_grad, grad_gain, grad_project, grad_output)


def general_body(
    tokens,
    latents,
    segments,
    scene_mask,
    counts,
    token_gain,
    query_gain,
    query_weight,
    key_weight,
    value_weight,
    output_weight,
    first_gain,
    first_up,
    first_down,
    mixer_gain,
    mixer_project,
    mixer_output,
    second_gain,
    second_up,
    second_down,
    cotangent,
):
    scale = D ** (-0.5)
    shards = lax.axis_size("tok")
    own_rows = L // shards
    row_start = lax.axis_index("tok") * own_rows
    latent_group = jnp.arange(L) // (L // LGROUPS)
    latent_onehot = (latent_group[:, None] == jnp.arange(LGROUPS)[None, :]).astype(jnp.float32)
    token_place = jnp.arange(TOK_DEV)
    records = []
    latent_outs = []
    for member in range(MB):
        record = {}
        source, normed, key_rows, value_rows = project_tokens(
            tokens, member, token_gain, key_weight, value_weight
        )
        record["token_side"] = (source, normed, key_rows, value_rows)
        scene_onehot = (segments[0, member][:, None] == jnp.arange(SCENES)[None, :]).astype(
            jnp.float32
        )
        token_seen = jnp.dot(scene_onehot, scene_mask[0, member].astype(jnp.float32))
        visible = product_cols(latent_onehot, token_seen)
        alive = token_place < counts[0, member, 0]
        allowed = (visible > 0.5) & alive[None, :]
        latent_every = latents[0, member]
        normed_every = norm_rows(latent_every, query_gain).astype(jnp.bfloat16)
        queries = product_plain(normed_every, query_weight).astype(jnp.bfloat16)
        scores = jnp.where(allowed, product_cols(queries, key_rows) * scale, NEG)
        row_top = lax.pmax(jnp.max(scores, axis=1), "tok")
        unnormed = jnp.exp(scores - row_top[:, None])
        row_total, weighted = (
            lax.psum_scatter(
                jnp.sum(unnormed, axis=1).astype(jnp.bfloat16),
                "tok",
                scatter_dimension=0,
                tiled=True,
            ).astype(jnp.float32),
            lax.psum_scatter(
                product_plain(unnormed.astype(jnp.bfloat16), value_rows).astype(jnp.bfloat16),
                "tok",
                scatter_dimension=0,
                tiled=True,
            ).astype(jnp.float32),
        )
        latent_in = lax.dynamic_slice_in_dim(latent_every, row_start, own_rows, 0)
        latent_normed = lax.dynamic_slice_in_dim(normed_every, row_start, own_rows, 0)
        attended = weighted / row_total[:, None]
        attended_low = attended.astype(jnp.bfloat16)
        first_mid = latent_in + product_plain(attended_low, output_weight)
        mixer_mid, first_saved = mlp_forward(first_mid, first_gain, first_up, first_down)
        second_mid, mixer_saved = mixer_forward(mixer_mid, mixer_gain, mixer_project, mixer_output)
        final_rows, second_saved = mlp_forward(second_mid, second_gain, second_up, second_down)
        latent_outs.append(final_rows)
        record["latent_side"] = (
            allowed,
            latent_in,
            latent_normed,
            queries,
            row_top,
            row_total,
            attended,
            attended_low,
            first_mid,
            mixer_mid,
            second_mid,
            first_saved,
            mixer_saved,
            second_saved,
        )
        records.append(record)
    grads = {}
    latent_grads = []
    token_grads = []
    for member in range(MB):
        record = records[member]
        source, normed, key_rows, value_rows = record["token_side"]
        (
            allowed,
            latent_in,
            latent_normed,
            queries,
            row_top,
            row_total,
            attended,
            attended_low,
            first_mid,
            mixer_mid,
            second_mid,
            first_saved,
            mixer_saved,
            second_saved,
        ) = record["latent_side"]
        second_back = mlp_backward(
            second_mid, second_gain, second_up, second_down, second_saved, cotangent[0, member]
        )
        add_term(grads, "second_gain", second_back[1])
        add_term(grads, "second_up", second_back[2])
        add_term(grads, "second_down", second_back[3])
        mixer_back = mixer_backward(
            mixer_mid, mixer_gain, mixer_project, mixer_output, mixer_saved, second_back[0]
        )
        add_term(grads, "mixer_gain", mixer_back[1])
        add_term(grads, "mixer_project", mixer_back[2])
        add_term(grads, "mixer_output", mixer_back[3])
        first_back = mlp_backward(
            first_mid, first_gain, first_up, first_down, first_saved, mixer_back[0]
        )
        add_term(grads, "first_gain", first_back[1])
        add_term(grads, "first_up", first_back[2])
        add_term(grads, "first_down", first_back[3])
        latent_upstream = first_back[0]
        grad_low = latent_upstream.astype(jnp.bfloat16)
        add_term(grads, "output_weight", product_rows(attended_low, grad_low))
        attended_grad = lax.optimization_barrier(
            product_cols(grad_low, output_weight).astype(jnp.bfloat16)
        ).astype(jnp.float32)
        weighted_grad = (attended_grad / row_total[:, None]).astype(jnp.bfloat16)
        total_grad = -jnp.sum(attended_grad * attended, axis=1) / row_total
        weighted_every, total_every = (
            lax.all_gather(
                weighted_grad.astype(jnp.float32).astype(jnp.bfloat16), "tok", axis=0, tiled=True
            ).astype(jnp.float32),
            lax.all_gather(total_grad.astype(jnp.bfloat16), "tok", axis=0, tiled=True).astype(
                total_grad.dtype
            ),
        )
        weighted_every = weighted_every.astype(jnp.bfloat16)
        scores = jnp.where(allowed, product_cols(queries, key_rows) * scale, NEG)
        unnormed = jnp.exp(scores - row_top[:, None])
        unnormed_grad = product_cols(weighted_every, value_rows) + total_every[:, None]
        score_grad = (unnormed * unnormed_grad).astype(jnp.bfloat16)
        value_grad = product_rows(unnormed.astype(jnp.bfloat16), weighted_every).astype(
            jnp.bfloat16
        )
        key_grad = (product_rows(score_grad, queries) * scale).astype(jnp.bfloat16)
        query_grad = lax.psum_scatter(
            (product_plain(score_grad, key_rows) * scale).astype(jnp.bfloat16),
            "tok",
            scatter_dimension=0,
            tiled=True,
        )
        add_term(grads, "key_weight", product_rows(normed, key_grad))
        add_term(grads, "value_weight", product_rows(normed, value_grad))
        normed_grad = product_cols(key_grad, key_weight) + product_cols(value_grad, value_weight)
        source_grad, gain_grad = norm_back(source, token_gain, normed_grad)
        add_term(grads, "token_gain", gain_grad)
        token_grads.append(source_grad)
        add_term(grads, "query_weight", product_rows(latent_normed, query_grad))
        latent_grad, gain_grad = norm_back(
            latent_in, query_gain, product_cols(query_grad, query_weight)
        )
        add_term(grads, "query_gain", gain_grad)
        latent_grads.append(latent_upstream + latent_grad)
    parts = (
        lax.psum_scatter(
            grads["token_gain"].astype(jnp.bfloat16), "tok", scatter_dimension=0, tiled=True
        ).astype(jnp.float32),
        lax.psum_scatter(
            grads["query_gain"].astype(jnp.bfloat16), "tok", scatter_dimension=0, tiled=True
        ).astype(jnp.float32),
        lax.psum_scatter(
            grads["query_weight"].astype(jnp.bfloat16), "tok", scatter_dimension=0, tiled=True
        ).astype(jnp.float32),
        lax.psum_scatter(
            grads["key_weight"].astype(jnp.bfloat16), "tok", scatter_dimension=0, tiled=True
        ).astype(jnp.float32),
        lax.psum_scatter(
            grads["value_weight"].astype(jnp.bfloat16), "tok", scatter_dimension=0, tiled=True
        ).astype(jnp.float32),
        lax.psum_scatter(
            grads["output_weight"].astype(jnp.bfloat16), "tok", scatter_dimension=0, tiled=True
        ).astype(jnp.float32),
        lax.psum_scatter(
            grads["first_gain"].astype(jnp.bfloat16), "tok", scatter_dimension=0, tiled=True
        ).astype(jnp.float32),
        lax.psum_scatter(
            grads["first_up"].astype(jnp.bfloat16), "tok", scatter_dimension=0, tiled=True
        ).astype(jnp.float32),
        lax.psum_scatter(
            grads["first_down"].astype(jnp.bfloat16), "tok", scatter_dimension=0, tiled=True
        ).astype(jnp.float32),
        lax.psum_scatter(
            grads["mixer_gain"].astype(jnp.bfloat16), "tok", scatter_dimension=0, tiled=True
        ).astype(jnp.float32),
        lax.psum_scatter(
            grads["mixer_project"].astype(jnp.bfloat16), "tok", scatter_dimension=0, tiled=True
        ).astype(jnp.float32),
        lax.psum_scatter(
            grads["mixer_output"].astype(jnp.bfloat16), "tok", scatter_dimension=0, tiled=True
        ).astype(jnp.float32),
        lax.psum_scatter(
            grads["second_gain"].astype(jnp.bfloat16), "tok", scatter_dimension=0, tiled=True
        ).astype(jnp.float32),
        lax.psum_scatter(
            grads["second_up"].astype(jnp.bfloat16), "tok", scatter_dimension=0, tiled=True
        ).astype(jnp.float32),
        lax.psum_scatter(
            grads["second_down"].astype(jnp.bfloat16), "tok", scatter_dimension=0, tiled=True
        ).astype(jnp.float32),
    )
    summed = (
        lax.psum(parts[0].astype(jnp.bfloat16), "grp").astype(jnp.float32),
        lax.psum(parts[1].astype(jnp.bfloat16), "grp").astype(jnp.float32),
        lax.psum(parts[2].astype(jnp.bfloat16), "grp").astype(jnp.float32),
        lax.psum(parts[3].astype(jnp.bfloat16), "grp").astype(jnp.float32),
        lax.psum(parts[4].astype(jnp.bfloat16), "grp").astype(jnp.float32),
        lax.psum(parts[5].astype(jnp.bfloat16), "grp").astype(jnp.float32),
        lax.psum(parts[6].astype(jnp.bfloat16), "grp").astype(jnp.float32),
        lax.psum(parts[7].astype(jnp.bfloat16), "grp").astype(jnp.float32),
        lax.psum(parts[8].astype(jnp.bfloat16), "grp").astype(jnp.float32),
        lax.psum(parts[9].astype(jnp.bfloat16), "grp").astype(jnp.float32),
        lax.psum(parts[10].astype(jnp.bfloat16), "grp").astype(jnp.float32),
        lax.psum(parts[11].astype(jnp.bfloat16), "grp").astype(jnp.float32),
        lax.psum(parts[12].astype(jnp.bfloat16), "grp").astype(jnp.float32),
        lax.psum(parts[13].astype(jnp.bfloat16), "grp").astype(jnp.float32),
        lax.psum(parts[14].astype(jnp.bfloat16), "grp").astype(jnp.float32),
    )
    return (
        jnp.stack(latent_outs)[None],
        jnp.stack(latent_grads)[None],
        jnp.stack(token_grads)[None],
    ) + tuple(summed)


TOK = 8
ROWS = L // TOK
FF = 2048
GR = L // LGROUPS
LOG2E = 1.4426950408889634
LN2 = 0.6931471805599453
F32 = jnp.float32
BF16 = jnp.bfloat16
MIB = 1024 * 1024


def nn(left, right):
    return lax.dot_general(left, right, (((1,), (0,)), ((), ())), preferred_element_type=F32)


def nt(left, right):
    return lax.dot_general(left, right, (((1,), (1,)), ((), ())), preferred_element_type=F32)


def tn(left, right):
    return lax.dot_general(left, right, (((0,), (0,)), ((), ())), preferred_element_type=F32)


def norm_parts(values):
    centre = values - jnp.mean(values, axis=-1, keepdims=True)
    inverse = lax.rsqrt(jnp.mean(centre * centre, axis=-1, keepdims=True) + EPS)
    return centre * inverse, inverse


def norm_pull(hat, inverse, gain, upstream):
    scaled = upstream * gain
    inner = jnp.mean(scaled * hat, axis=-1, keepdims=True)
    grad = (scaled - jnp.mean(scaled, axis=-1, keepdims=True) - hat * inner) * inverse
    return grad, upstream * hat


def places():
    me = lax.axis_index("tok")
    core = lax.rem(me, 2)
    chip = lax.div(me, 2)
    mate = me + 1 - 2 * core
    flip_x = chip + 1 - 2 * lax.rem(chip, 2)
    flip_y = lax.rem(chip + 2, 4)
    far = 3 - chip
    return me, core, chip, mate, (far, flip_x, flip_y)


def remote(src, dst, send_sem, recv_sem, peer):
    return pltpu.make_async_remote_copy(
        src_ref=src,
        dst_ref=dst,
        send_sem=send_sem,
        recv_sem=recv_sem,
        device_id={"tok": peer},
        device_id_type=pl.DeviceIdType.MESH,
    )


def greet(devices):
    barrier = pltpu.get_barrier_semaphore()
    for device in devices:
        pl.semaphore_signal(
            barrier, inc=1, device_id={"tok": device}, device_id_type=pl.DeviceIdType.MESH
        )
    pl.semaphore_wait(barrier, len(devices))


def chip_at(chip, flip):
    high, low = divmod(flip, 2) if isinstance(flip, int) else (lax.div(flip, 2), lax.rem(flip, 2))
    across = lax.rem(lax.rem(chip, 2) + low, 2)
    along = lax.rem(lax.div(chip, 2) + high, 2)
    return 2 * along + across


def mask_loads(seg_ref, mask_ref, seg_buf, mask_buf, sem):
    return (
        pltpu.make_async_copy(seg_ref.at[0], seg_buf, sem.at[0]),
        pltpu.make_async_copy(mask_ref.at[0], mask_buf, sem.at[1]),
    )


def mask_rows(seg_buf, mask_buf, count_ref, bias_ref):
    for member in range(MB):
        scene = lax.broadcasted_iota(jnp.int32, (SCENES, TOK_DEV), 0)
        place = lax.broadcasted_iota(jnp.int32, (SCENES, TOK_DEV), 1)
        hot = jnp.where((seg_buf[member:member + 1] == scene) & (place < count_ref[member]), 1.0, 0.0)
        seen = tn(jnp.where(mask_buf[member] > 0, 1.0, 0.0).astype(BF16), hot.astype(BF16))
        bias_ref[member] = jnp.where(seen > 0.5, 0.0, NEG)


def to_rows(first, second):
    rows = first.shape[0]
    lane = lax.broadcasted_iota(jnp.int32, (rows, 128), 1)
    return jnp.where(lane == 0, first, second).T[0:8]


def cross_forward_kernel(
    tok_ref, lat_ref, tgain_ref, qgain_ref, qw_ref, kw_ref, vw_ref, seg_ref, mask_ref, count_ref,
    k_out, v_out, q_out, att_ref, lse_ref,
    tok_buf, lat_buf, keys, values, queries, bias, part, part_s, got, got_s, stage, stage_s,
    arrive, arrive_s, total, seg_buf, mask_buf,
    mask_sem, tok_sem, lat_sem, k_sem, v_sem, q_sem,
    core_send, core_recv, core_send_s, core_recv_s, chip_send, chip_recv, chip_send_s, chip_recv_s,
):
    me, core, chip, mate, others = places()
    span = 2 * ROWS

    def unpack(step):
        return lax.div(step, 4), 3 - lax.rem(step, 4)

    def lat_copy(step):
        member, flip = unpack(step)
        start = pl.multiple_of(chip_at(chip, flip) * span, span)
        return pltpu.make_async_copy(lat_ref.at[0, member, pl.ds(start, span)], lat_buf.at[step], lat_sem.at[step])

    def q_copy(step):
        member, flip = unpack(step)
        start = pl.multiple_of(chip_at(chip, flip) * span, span)
        return pltpu.make_async_copy(queries.at[step], q_out.at[member, pl.ds(start, span)], q_sem.at[step])

    def tok_copy(member):
        return pltpu.make_async_copy(tok_ref.at[0, member], tok_buf.at[member], tok_sem.at[member])

    def kv_copies(member):
        return (
            pltpu.make_async_copy(keys.at[member], k_out.at[member], k_sem.at[member]),
            pltpu.make_async_copy(values.at[member], v_out.at[member], v_sem.at[member]),
        )

    def core_copies(step):
        return (
            remote(part.at[step, 1 - core], got.at[step], core_send.at[step], core_recv.at[step], mate),
            remote(part_s.at[step, 1 - core], got_s.at[step], core_send_s.at[step], core_recv_s.at[step], mate),
        )

    def chip_copies(step):
        member, flip = unpack(step)
        peer = 2 * chip_at(chip, flip) + core
        place = 3 * member + flip - 1
        return (
            remote(stage.at[step], arrive.at[place], chip_send.at[place], chip_recv.at[place], peer),
            remote(stage_s.at[step], arrive_s.at[place], chip_send_s.at[place], chip_recv_s.at[place], peer),
        )

    tok_copy(0).start()
    masks = mask_loads(seg_ref, mask_ref, seg_buf, mask_buf, mask_sem)
    for copy in masks:
        copy.start()
    for step in range(4):
        lat_copy(step).start()
    tok_copy(1).start()
    for step in range(4, 2 * 4):
        lat_copy(step).start()
    greet([mate] + [2 * other + core for other in others])
    for copy in masks:
        copy.wait()
    mask_rows(seg_buf, mask_buf, count_ref, bias)

    def project(member):
        tok_copy(member).wait()
        hat, inverse = norm_parts(tok_buf[member].astype(F32))
        normed = (hat * tgain_ref[...]).astype(BF16)
        keys[member] = nn(normed, kw_ref[...]).astype(BF16)
        values[member] = nn(normed, vw_ref[...]).astype(BF16)
        for copy in kv_copies(member):
            copy.start()

    def ask(step):
        hat, inverse = norm_parts(lat_buf[step])
        normed = (hat * qgain_ref[...]).astype(BF16)
        queries[step] = (nn(normed, qw_ref[...]) * (D ** (-0.5) * LOG2E)).astype(BF16)

    def compute(step, ahead):
        member, flip = unpack(step)

        @pl.when(flip == 3)
        def _():
            project(member)

        if ahead:
            lat_copy(step + 1).wait()
        scores = nt(queries[step], keys[member])
        if ahead:
            ask(step + 1)
        raised = []
        for half in range(2):
            seen = bias[member, pl.ds(2 * chip_at(chip, flip) + half, 1), :]
            own = scores[half * ROWS:(half + 1) * ROWS] + seen
            top = jnp.max(own, axis=1, keepdims=True)
            own = jnp.exp2(own - top)
            part_s[step, half] = to_rows(top, jnp.sum(own, axis=1, keepdims=True))
            raised.append(own.astype(BF16))
        sums = nn(jnp.concatenate(raised, axis=0), values[member]).astype(BF16)
        for half in range(2):
            part[step, half] = sums[half * ROWS:(half + 1) * ROWS]
        for copy in core_copies(step):
            copy.start()
        if ahead:
            q_copy(step + 1).start()

    def merge(one, one_s, two, two_s):
        top = jnp.maximum(one_s[0:1], two_s[0:1])
        one_w, two_w = jnp.exp2(one_s[0:1] - top), jnp.exp2(two_s[0:1] - top)
        sums = one_s[1:2] * one_w + two_s[1:2] * two_w
        spare = jnp.zeros((6, ROWS), F32)
        weights = jnp.concatenate([one_w, two_w, spare], axis=0).T
        return one * weights[:, 0:1] + two * weights[:, 1:2], jnp.concatenate([top, sums, spare], axis=0)

    def combine(step):
        member, flip = unpack(step)
        for copy in core_copies(step):
            copy.wait_recv()
        added, figures = merge(
            part[step, core].astype(F32), part_s[step, core], got[step].astype(F32), got_s[step]
        )
        stage_s[step] = figures

        @pl.when(flip > 0)
        def _():
            stage[step] = added.astype(BF16)
            for copy in chip_copies(step):
                copy.start()

        @pl.when(flip == 0)
        def _():
            total[member] = added

    def finish(member):
        added, figures = total[member], stage_s[4 * member + 3]
        for flip in (1, 2, 3):
            for copy in chip_copies(4 * member + 3 - flip):
                copy.wait_recv()
            place = 3 * member + flip - 1
            added, figures = merge(added, figures, arrive[place].astype(F32), arrive_s[place])
        spare = jnp.zeros((7, ROWS), F32)
        inverse = jnp.concatenate([1.0 / figures[1:2], spare], axis=0).T
        att_ref[member] = added * inverse[:, 0:1]
        lse_ref[member] = jnp.concatenate([figures[0:1] + jnp.log2(figures[1:2]), spare], axis=0)

    def step_body(step, carry):
        compute(step, True)

        @pl.when(step > 0)
        def _():
            combine(step - 1)

        return carry

    last = jnp.int32(4 * MB - 1)
    lat_copy(jnp.int32(0)).wait()
    ask(0)
    q_copy(jnp.int32(0)).start()
    lax.fori_loop(0, 4 * MB - 1, step_body, 0)
    compute(last, False)
    combine(last - 1)
    combine(last)
    for member in range(MB):
        finish(member)
    for member in range(MB):
        for copy in kv_copies(member):
            copy.wait()
        for slot in range(4):
            step = 4 * member + slot
            q_copy(step).wait()
            for copy in core_copies(step):
                copy.wait_send()
            if slot < 3:
                for copy in chip_copies(step):
                    copy.wait_send()


def cross_forward(collective_id, *args):
    dma = pltpu.SemaphoreType.DMA
    span = 2 * ROWS
    steps = 4 * MB
    vmem = pl.BlockSpec(memory_space=pltpu.VMEM)
    hbm = pl.BlockSpec(memory_space=pl.ANY)
    return pl.pallas_call(
        cross_forward_kernel,
        in_specs=[hbm, hbm] + [vmem] * 5 + [hbm, hbm, pl.BlockSpec(memory_space=pltpu.SMEM)],
        out_specs=[hbm, hbm, hbm, vmem, vmem],
        out_shape=[
            jax.ShapeDtypeStruct((MB, TOK_DEV, D), BF16),
            jax.ShapeDtypeStruct((MB, TOK_DEV, D), BF16),
            jax.ShapeDtypeStruct((MB, L, D), BF16),
            jax.ShapeDtypeStruct((MB, ROWS, D), F32),
            jax.ShapeDtypeStruct((MB, 8, ROWS), F32),
        ],
        scratch_shapes=[
            pltpu.VMEM((MB, TOK_DEV, D), BF16),
            pltpu.VMEM((steps, span, D), F32),
            pltpu.VMEM((MB, TOK_DEV, D), BF16),
            pltpu.VMEM((MB, TOK_DEV, D), BF16),
            pltpu.VMEM((steps, span, D), BF16),
            pltpu.VMEM((MB, LGROUPS, TOK_DEV), F32),
            pltpu.VMEM((steps, 2, ROWS, D), BF16),
            pltpu.VMEM((steps, 2, 8, ROWS), F32),
            pltpu.VMEM((steps, ROWS, D), BF16),
            pltpu.VMEM((steps, 8, ROWS), F32),
            pltpu.VMEM((steps, ROWS, D), BF16),
            pltpu.VMEM((steps, 8, ROWS), F32),
            pltpu.VMEM((3 * MB, ROWS, D), BF16),
            pltpu.VMEM((3 * MB, 8, ROWS), F32),
            pltpu.VMEM((MB, ROWS, D), F32),
            pltpu.VMEM((MB, TOK_DEV), jnp.int32),
            pltpu.VMEM((MB, SCENES, LGROUPS), jnp.int32),
            dma((2,)), dma((MB,)), dma((steps,)), dma((MB,)), dma((MB,)), dma((steps,)),
        ] + [dma((steps,))] * 4 + [dma((3 * MB,))] * 4,
        compiler_params=pltpu.CompilerParams(
            collective_id=collective_id, has_side_effects=True, vmem_limit_bytes=56 * MIB
        ),
        cost_estimate=pl.CostEstimate(
            flops=14 * 10**9, bytes_accessed=22 * 10**6, transcendentals=4 * 10**6
        ),
        name="cross_forward",
    )(*args)


def cross_backward_kernel(
    items, grad_items,
    tok_ref, tgain_ref, kw_ref, vw_ref, seg_ref, mask_ref, count_ref, k_ref, v_ref, q_ref, up_ref, fig_ref,
    lat_ref, lup_ref, qgain_ref, qw_ref, fgain_ref, mgain_ref, sgain_ref, *refs,
):
    count, more = len(items), len(grad_items)
    parts, sources = refs[:count], refs[count:count + more]
    refs = refs[count + more:]
    dlat_ref, dtok_ref, dkw_ref, dvw_ref, dqw_ref, gains_ref = refs[:6]
    sums, helds = refs[6:6 + count], refs[6 + count:6 + count + more]
    rest = refs[6 + count + more:]
    cut = CROSS_SCRATCH + 3 * count + 2
    grp, grp_devices = grp_steps(items, parts, (), rest[CROSS_SCRATCH:cut], sums)
    tok, near_devices = tok_steps(grad_items, sources, rest[cut:])
    (tok_buf, keys, values, queries, ups, figs, bias, part, got, stage, arrive, far_in, total, dk, dv, dkw, dvw,
     dgain_ref, lat, lup, seg_buf, mask_buf, mask_sem, tail_sem,
     tok_sem, k_sem, v_sem, q_sem, out_sem, near_send, near_recv, far_send, far_recv, on_send, on_recv, own_sem,
     fig_send, fig_recv, core_send, core_recv, chip_send, chip_recv, half_send, half_recv) = rest[:CROSS_SCRATCH]
    me, core, chip, mate, others = places()
    span = 2 * ROWS

    def slot_of(step):
        late = lax.div(step + 3, 8)
        member = jnp.where(step == 1, 1, late)
        flip = jnp.where(step < 2, 0, jnp.where(late == 0, step - 1, 8 - step))
        return member, flip

    def loads(step):
        member, flip = slot_of(step)
        start = pl.multiple_of(chip_at(chip, flip) * span, span)
        ring = lax.rem(step, 4)
        return pltpu.make_async_copy(q_ref.at[member, pl.ds(start, span)], queries.at[ring], q_sem.at[ring])

    def tok_copies(member):
        return (
            pltpu.make_async_copy(k_ref.at[member], keys.at[member], k_sem.at[member]),
            pltpu.make_async_copy(v_ref.at[member], values.at[member], v_sem.at[member]),
            pltpu.make_async_copy(tok_ref.at[0, member], tok_buf.at[member], tok_sem.at[member]),
        )

    def out_copy(member):
        return pltpu.make_async_copy(dk.at[member], dtok_ref.at[0, member], out_sem.at[member])

    def own_copies(member):
        slot = 4 * member
        return (
            pltpu.make_async_copy(up_ref.at[member], ups.at[slot, core], own_sem.at[member, 0]),
            pltpu.make_async_copy(fig_ref.at[member], figs.at[slot, core], own_sem.at[member, 1]),
        )

    def near_copies(member):
        slot = 4 * member
        return [
            remote(up_ref.at[member], ups.at[slot, core], near_send.at[member, 0], near_recv.at[member, 0], mate),
            remote(fig_ref.at[member], figs.at[slot, core], near_send.at[member, 1], near_recv.at[member, 1], mate),
        ]

    half_rows = (pl.ds(0, ROWS // 2), pl.ds(ROWS // 2, ROWS // 2))

    def far_copies(slot):
        member, flip = slot // 4, slot % 4
        peer = 2 * chip_at(chip, flip) + core
        if flip < 3:
            return [
                remote(up_ref.at[member], ups.at[slot, core], far_send.at[slot, 0], far_recv.at[slot, 0], peer),
                remote(fig_ref.at[member], figs.at[slot, core], far_send.at[slot, 1], far_recv.at[slot, 1], peer),
            ]
        copies = []
        for half, (held, toward) in enumerate(((1, 2), (2, 1))):
            copies.append(remote(
                ups.at[4 * member + held, core, half_rows[half]], ups.at[slot, core, half_rows[half]],
                far_send.at[slot, half], far_recv.at[slot, half], 2 * chip_at(chip, toward) + core,
            ))
        copies.append(remote(
            figs.at[4 * member + 1, core], figs.at[slot, core], fig_send.at[member], fig_recv.at[member],
            2 * chip_at(chip, 2) + core,
        ))
        return copies

    def on_copies(slot):
        return (
            remote(ups.at[slot, core], ups.at[slot, core], on_send.at[slot, 0], on_recv.at[slot, 0], mate),
            remote(figs.at[slot, core], figs.at[slot, core], on_send.at[slot, 1], on_recv.at[slot, 1], mate),
        )

    def pass_on(slot):
        for copy in far_copies(slot):
            copy.wait_recv()
        for copy in on_copies(slot):
            copy.start()

    def pass_near(member):
        pass_on(4 * member + 1)
        pass_on(4 * member + 2)
        for copy in far_copies(4 * member + 3):
            copy.start()

    def half_copy(member, half):
        return remote(
            stage.at[4 * member + 3, half_rows[half]], far_in.at[member, half], half_send.at[member, half],
            half_recv.at[member, half], 2 * chip_at(chip, half + 1) + core,
        )

    def half_copies(member):
        return [half_copy(member, half) for half in range(2)]

    def core_copy(step):
        member, flip = slot_of(step)
        slot, ring = 4 * member + flip, lax.rem(step, 4)
        return remote(part.at[ring, 1 - core], got.at[slot], core_send.at[slot], core_recv.at[slot], mate)

    def chip_copy(slot):
        member, flip = slot // 4, slot % 4
        peer = 2 * chip_at(chip, flip) + core
        place = 2 * member + flip - 1
        return remote(stage.at[slot], arrive.at[place], chip_send.at[place], chip_recv.at[place], peer)

    def relay(member):
        for half in range(2):
            half_copy(member, half).wait_recv()
            slot = 4 * member + 2 - half
            joined = stage.at[slot, half_rows[half]]
            add(joined, joined, far_in.at[member, half])
            chip_copy(slot).start()

    masks = mask_loads(seg_ref, mask_ref, seg_buf, mask_buf, mask_sem)
    for copy in masks:
        copy.start()
    own_rows = pl.ds(pl.multiple_of(me * ROWS, ROWS), ROWS)
    tails = (
        pltpu.make_async_copy(lat_ref.at[0, :, own_rows], lat, tail_sem.at[0]),
        pltpu.make_async_copy(lup_ref, lup, tail_sem.at[1]),
    )
    for copy in own_copies(0):
        copy.start()
    for copy in tok_copies(0):
        copy.start()
    for step in range(3):
        loads(jnp.int32(step)).start()
    for copy in own_copies(1):
        copy.start()
    for copy in tok_copies(1):
        copy.start()
    for copy in tails:
        copy.start()
    greet_all([mate] + [2 * other + core for other in others], grp_devices)
    for member in range(MB):
        for copy in near_copies(member):
            copy.start()
    for flip in (1, 2):
        for copy in far_copies(flip):
            copy.start()
    tok[0](0)
    for item in range(count):
        grp[0](item)
    for copy in masks:
        copy.wait()
    mask_rows(seg_buf, mask_buf, count_ref, bias)

    def compute(step):
        member, flip = slot_of(step)
        slot = 4 * member + flip

        @pl.when(step < 2)
        def _():
            for copy in tok_copies(member):
                copy.wait()
            dk[member] = jnp.zeros((TOK_DEV, D), F32)
            dv[member] = jnp.zeros((TOK_DEV, D), F32)

        loads(step).wait()

        @pl.when(step + 3 < 4 * MB)
        def _():
            loads(step + 3).start()

        @pl.when(flip == 0)
        def _():
            for copy in own_copies(member):
                copy.wait()
            for copy in near_copies(member):
                copy.wait_recv()

        @pl.when(flip > 0)
        def _():
            for copy in on_copies(slot):
                copy.wait_recv()

        asked = queries[lax.rem(step, 4)]
        upstream = ups[slot].reshape(span, D)
        scores = nt(asked, keys[member])
        soft = nt(upstream, values[member])
        weights, grads = [], []
        for half in range(2):
            seen = bias[member, pl.ds(2 * chip_at(chip, flip) + half, 1), :]
            figures = figs[slot, half].T
            rows = slice(half * ROWS, (half + 1) * ROWS)
            weight = jnp.exp2(scores[rows] + seen - figures[:, 0:1])
            grads.append((weight * (soft[rows] - figures[:, 1:2])).astype(BF16))
            weights.append(weight.astype(BF16))
        weight = jnp.concatenate(weights, axis=0)
        grad = jnp.concatenate(grads, axis=0)
        middle(step)
        dv[member] += tn(weight, upstream)
        dk[member] += tn(grad, asked)
        asked_grad = (nn(grad, keys[member]) * D ** (-0.5)).astype(BF16)

        @pl.when(step >= 4)
        def _():
            core_copy(step - 4).wait_send()

        for half in range(2):
            part[lax.rem(step, 4), half] = asked_grad[half * ROWS:(half + 1) * ROWS]
        core_copy(step).start()

    def combine(step):
        member, flip = slot_of(step)
        slot = 4 * member + flip
        core_copy(step).wait_recv()
        added = part[lax.rem(step, 4), core].astype(F32) + got[slot].astype(F32)

        @pl.when(flip > 0)
        def _():
            stage[slot] = added.astype(BF16)

        @pl.when(flip == 0)
        def _():
            total[member] = added

    def tokens_back(member, half):
        gain = tgain_ref[...]
        rows = pl.ds(pl.multiple_of(half * span, span), span)
        hat, inverse = norm_parts(tok_buf[member, rows].astype(F32))
        normed = (hat * gain).astype(BF16)
        key_grad = (dk[member, rows] * LN2).astype(BF16)
        value_grad = dv[member, rows].astype(BF16)
        dkw[...] += tn(normed, key_grad)
        dvw[...] += tn(normed, value_grad)
        normed_grad = nt(key_grad, kw_ref[...]) + nt(value_grad, vw_ref[...])
        source_grad, gain_rows = norm_pull(hat, inverse, gain, normed_grad)
        dk[member, rows] = source_grad
        dgain_ref[...] += jnp.sum(gain_rows, axis=0, keepdims=True)

    def hold(item):
        helds[item][...] = tok[4](item).astype(helds[item].dtype)

    def middle(step):
        @pl.when(step > 0)
        def _():
            combine(step - 1)

        @pl.when(step == 1)
        def _():
            pass_near(0)

        @pl.when(step == 3)
        def _():
            pass_on(3)
            pass_near(1)

        @pl.when(step == 5)
        def _():
            for copy in half_copies(0):
                copy.start()

        @pl.when(step == 6)
        def _():
            for copy in half_copies(1):
                copy.start()
            relay(0)

    def step_body(step, carry):
        compute(step)

        @pl.when(step == 0)
        def _():
            for flip in (1, 2):
                for copy in far_copies(4 + flip):
                    copy.start()
            tok[1](0)
            tok[0](1)

        @pl.when(step == 1)
        def _():
            tok[0](2)

        @pl.when(step == 2)
        def _():
            tok[1](1)

        @pl.when(step == 4)
        def _():
            pass_on(7)
            for item in range(count):
                grp[4](item)
            tok[2](0)
            tok[1](2)

        @pl.when(step == 6)
        def _():
            tok[3](0)

        @pl.when(step == 4 * MB - 1)
        def _():
            combine(step)
            relay(1)

        return carry

    lax.fori_loop(0, 4 * MB, step_body, 0)

    def tokens_body(member, carry):
        for half in range(TOK_DEV // span):
            tokens_back(member, half)
        out_copy(member).start()

        @pl.when(member == 0)
        def _():
            helds[1][...] = tok[6](1)

        return carry

    dkw[...] = jnp.zeros_like(dkw)
    dvw[...] = jnp.zeros_like(dvw)
    dgain_ref[...] = jnp.zeros_like(dgain_ref)
    lax.fori_loop(0, MB, tokens_body, 0)
    dkw_ref[...] = dkw[...].astype(BF16)
    dvw_ref[...] = dvw[...].astype(BF16)
    hold(0)
    helds[2][...] = tok[6](2)
    for copy in tails:
        copy.wait()
    gain = qgain_ref[...]
    hat, inverse = norm_parts(lat[...].reshape(MB * ROWS, D))
    normed = (hat * gain).astype(BF16)
    asked_grads = []
    for member in range(MB):
        added = total[member]
        for flip in (1, 2):
            chip_copy(4 * member + flip).wait_recv()
            added = added + arrive[2 * member + flip - 1].astype(F32)
        asked_grads.append(added.astype(BF16))
    asked_grad = jnp.concatenate(asked_grads, axis=0)
    dqw_ref[...] = tn(normed, asked_grad).astype(BF16)
    source_grad, gain_rows = norm_pull(hat, inverse, gain, nt(asked_grad, qw_ref[...]))
    lup[...] += source_grad
    last = pltpu.make_async_copy(lup, dlat_ref, tail_sem.at[2])
    last.start()
    query_gain = jnp.sum(gain_rows, axis=0, keepdims=True)
    rows = jnp.concatenate(
        [dgain_ref[...], query_gain, fgain_ref[...], mgain_ref[...], sgain_ref[...], jnp.zeros((3, D), F32)], axis=0
    )
    gains_ref[...] = jnp.zeros_like(gains_ref)
    width = D // TOK
    for device in range(TOK):
        gains_ref[16 * device:16 * device + 8, 0:width] = rows[:, device * width:(device + 1) * width]
    grp[3]((0,))
    tok[5]((1, 2))
    last.wait()
    for step in range(4, 4 * MB):
        core_copy(jnp.int32(step)).wait_send()
    for member in range(MB):
        out_copy(member).wait()
        for copy in near_copies(member) + half_copies(member):
            copy.wait_send()
        for flip in range(4):
            slot = 4 * member + flip
            if flip > 0:
                for copy in far_copies(slot):
                    copy.wait_send()
                for copy in on_copies(slot):
                    copy.wait_send()
            if flip in (1, 2):
                chip_copy(slot).wait_send()


CROSS_SCRATCH = 44


def cross_backward(collective_id, arrays, grads, *args):
    dma = pltpu.SemaphoreType.DMA
    span = 2 * ROWS
    steps = 4 * MB
    vmem = pl.BlockSpec(memory_space=pltpu.VMEM)
    hbm = pl.BlockSpec(memory_space=pl.ANY)
    smem = pl.BlockSpec(memory_space=pltpu.SMEM)
    items, kinds = held_plan(arrays)
    sources, grad_items, grad_kinds, shapes = reduce_plan(grads)
    scratch = [
        pltpu.VMEM((MB, TOK_DEV, D), BF16),
        pltpu.VMEM((MB, TOK_DEV, D), BF16),
        pltpu.VMEM((MB, TOK_DEV, D), BF16),
        pltpu.VMEM((4, span, D), BF16),
        pltpu.VMEM((steps, 2, ROWS, D), BF16),
        pltpu.VMEM((steps, 2, 8, ROWS), F32),
        pltpu.VMEM((MB, LGROUPS, TOK_DEV), F32),
        pltpu.VMEM((4, 2, ROWS, D), BF16),
        pltpu.VMEM((steps, ROWS, D), BF16),
        pltpu.VMEM((steps, ROWS, D), BF16),
        pltpu.VMEM((2 * MB, ROWS, D), BF16),
        pltpu.VMEM((MB, 2, ROWS // 2, D), BF16),
        pltpu.VMEM((MB, ROWS, D), F32),
        pltpu.VMEM((MB, TOK_DEV, D), F32),
        pltpu.VMEM((MB, TOK_DEV, D), F32),
        pltpu.VMEM((D, D), F32),
        pltpu.VMEM((D, D), F32),
        pltpu.VMEM((1, D), F32),
        pltpu.VMEM((MB, ROWS, D), F32),
        pltpu.VMEM((MB * ROWS, D), F32),
        pltpu.VMEM((MB, TOK_DEV), jnp.int32),
        pltpu.VMEM((MB, SCENES, LGROUPS), jnp.int32),
        dma((2,)), dma((3,)),
        dma((MB,)), dma((MB,)), dma((MB,)), dma((4,)), dma((MB,)),
        dma((MB, 2)), dma((MB, 2)), dma((steps, 2)), dma((steps, 2)), dma((steps, 2)), dma((steps, 2)), dma((MB, 2)),
        dma((MB,)), dma((MB,)),
        dma((steps,)), dma((steps,)), dma((2 * MB,)), dma((2 * MB,)), dma((MB, 2)), dma((MB, 2)),
    ]
    return pl.pallas_call(
        functools.partial(cross_backward_kernel, items, grad_items),
        in_specs=[hbm] + [vmem] * 3 + [hbm, hbm, smem] + [hbm] * 7 + [vmem] * 5 + [vmem] * len(arrays) + [hbm] * len(grads),
        out_specs=[hbm, hbm] + [vmem] * (4 + len(arrays) + len(grads)),
        out_shape=[
            jax.ShapeDtypeStruct((MB * ROWS, D), F32),
            jax.ShapeDtypeStruct((1, MB, TOK_DEV, D), F32),
            jax.ShapeDtypeStruct((D, D), BF16),
            jax.ShapeDtypeStruct((D, D), BF16),
            jax.ShapeDtypeStruct((D, D), BF16),
            jax.ShapeDtypeStruct((16 * TOK, 128), F32),
        ] + [jax.ShapeDtypeStruct(array.shape, array.dtype) for array in arrays]
        + [
            jax.ShapeDtypeStruct((() if i == 0 else (2, 2)) + (high // 2, wide), kind)
            for i, ((high, wide), kind) in enumerate(zip(shapes, grad_kinds))
        ],
        scratch_shapes=scratch + grp_scratch(items, kinds) + tok_scratch(grad_items, grad_kinds),
        compiler_params=pltpu.CompilerParams(
            collective_id=collective_id, has_side_effects=True, vmem_limit_bytes=60 * MIB
        ),
        cost_estimate=pl.CostEstimate(
            flops=26 * 10**9, bytes_accessed=24 * 10**6, transcendentals=4 * 10**6
        ),
        name="cross_backward",
    )(*args, *arrays, *sources)


GELU_A = 0.7978845608028654
GELU_B = 0.044715


def gelu_parts(hidden):
    square = hidden * hidden
    bent = jnp.tanh(GELU_A * hidden * (1.0 + GELU_B * square))
    half = 0.5 * (1.0 + bent)
    slope = half + 0.5 * hidden * (1.0 - bent * bent) * (GELU_A * (1.0 + 3.0 * GELU_B * square))
    return hidden * half, slope


def greet_all(tok_devices, grp_devices=()):
    barrier = pltpu.get_barrier_semaphore()
    for axis, devices in (("tok", tok_devices), ("grp", grp_devices)):
        for device in devices:
            pl.semaphore_signal(
                barrier, inc=1, device_id={axis: device}, device_id_type=pl.DeviceIdType.MESH
            )
    pl.semaphore_wait(barrier, len(tok_devices) + len(grp_devices))


def all_peers():
    me, core, chip, mate, others = places()
    peers = []
    for other in others:
        peers += [2 * other + core, 2 * other + 1 - core]
    return me, peers + [mate]


def head_copies(row_side, head_side, to_heads, member, me, peers, send, recv, local):
    lanes = pl.ds(member * ROWS, ROWS)
    row_at = lambda device: row_side.at[:, device, :, lanes]
    head_at = lambda device: head_side.at[:, member, :, pl.ds(pl.multiple_of(device * ROWS, ROWS), ROWS)]
    source, target = (row_at, head_at) if to_heads else (head_at, row_at)
    copies = [
        remote(source(peer), target(me), send.at[slot, member], recv.at[slot, member], peer)
        for slot, peer in enumerate(peers)
    ]
    return copies, pltpu.make_async_copy(source(me), target(me), local.at[member])


QB = 1024
QB_BACK = 256


def latents_forward_kernel(
    lat_ref, att_ref, cot_ref, ow_ref, fgain_ref, fup_ref, fdown_ref, mgain_ref, proj_ref, mow_ref, sgain_ref,
    sup_ref, sdown_ref,
    out_ref, fmid_ref, mmid_ref, packed_ref, exact_ref, lse_ref, up_ref, mgrad_ref, ddown_ref, dup_ref, dmo_ref,
    dgain_ref,
    lat, att, cot, ow, fup, fdown, proj, mow, sup, sdown,
    out, fmid, mmid, heads, exact, up, mgrad, ddown, dup, dmo,
    rows_out, keys, values, mixed, mixed_rows, active, hidden_low, normed_low,
    load_sem, store_sem, send_a, recv_a, local_a, send_b, recv_b, local_b,
):
    me, peers = all_peers()
    own = pl.ds(pl.multiple_of(me * ROWS, ROWS), ROWS)
    names = ("lat", "att", "ow", "fup", "fdown", "proj", "mow", "sup", "sdown", "cot")
    loads = {}
    for i, (source, target) in enumerate((
        (lat_ref.at[0, :, own], lat), (att_ref, att), (ow_ref, ow), (fup_ref, fup), (fdown_ref, fdown),
        (proj_ref, proj), (mow_ref, mow), (sup_ref, sup), (sdown_ref, sdown), (cot_ref.at[0], cot),
    )):
        loads[names[i]] = pltpu.make_async_copy(source, target, load_sem.at[i])
        loads[names[i]].start()
    stores = []

    def store(source, target):
        stores.append(pltpu.make_async_copy(source, target, store_sem.at[len(stores)]))
        stores[-1].start()

    greet_all(peers)
    flat = (MB * ROWS, D)
    for name in ("lat", "att", "ow"):
        loads[name].wait()
    outward = [head_copies(rows_out, heads, True, member, me, peers, send_a, recv_a, local_a) for member in range(MB)]
    backward = [
        head_copies(mixed_rows, mixed, False, member, me, peers, send_b, recv_b, local_b) for member in range(MB)
    ]
    for member in range(MB):
        rows = slice(member * ROWS, (member + 1) * ROWS)
        first = lat[member] + nn(att[member].astype(BF16), ow[...])
        fmid[rows] = first
        normed = (norm_parts(first)[0] * fgain_ref[...]).astype(BF16)
        if member == 0:
            loads["fup"].wait()
            loads["fdown"].wait()
        mid = first
        for part in range(2):
            cut = slice(part * FF // 2, (part + 1) * FF // 2)
            mid = mid + nn(jax.nn.gelu(nn(normed, fup[:, cut])).astype(BF16), fdown[cut])
        mmid[rows] = mid
        normed = (norm_parts(mid)[0] * mgain_ref[...]).astype(BF16).T
        if member == 0:
            loads["proj"].wait()
        for kind, scale in enumerate((HD ** (-0.5) * LOG2E, 1.0, 1.0)):
            packed = tn(proj[:, kind * D:(kind + 1) * D], normed) * scale
            rows_out[kind, :, :, rows] = packed.astype(BF16).reshape(H, HD, ROWS)
        copies, here = outward[member]
        for copy in copies:
            copy.start()
        here.start()
    store(fmid, fmid_ref)
    store(mmid, mmid_ref)
    for member in range(MB):
        copies, here = outward[member]
        for copy in copies:
            copy.wait_recv()
        here.wait()
        store(heads.at[:, member], packed_ref.at[:, member])
        keys[...] = heads[1, member].T
        values[0:HD] = heads[2, member]
        values[HD:] = jnp.ones((16, L), BF16)

        def attend(step, carry, member=member):
            at = pl.ds(pl.multiple_of(step * QB, QB), QB)
            logits = nn(keys[...], heads[0, member, :, at])
            top = jnp.max(logits, axis=0, keepdims=True)
            both = nn(values[...], jnp.exp2(logits - top).astype(BF16))
            total = both[HD:HD + 1]
            result = both[0:HD] / total
            exact[member, :, at] = result
            mixed[0, member, :, at] = result.astype(BF16)
            lse_ref[member, :, at] = jnp.broadcast_to(top + jnp.log2(total), (8, QB))
            return carry

        lax.fori_loop(0, L // QB, attend, 0)
        for copy in backward[member][0] + [backward[member][1]]:
            copy.start()
    store(exact, exact_ref)
    loads["mow"].wait()
    loads["sup"].wait()
    loads["sdown"].wait()
    loads["cot"].wait()
    gains = []
    for member in range(MB):
        copies, here = backward[member]
        for copy in copies:
            copy.wait_recv()
        here.wait()
        rows = slice(member * ROWS, (member + 1) * ROWS)
        second = mmid[rows] + tn(mixed_rows[0, :, :, rows].reshape(D, ROWS), mow[...])
        hat, inverse = norm_parts(second)
        normed = (hat * sgain_ref[...]).astype(BF16)
        normed_low[rows] = normed
        upstream = cot[member]
        grad = upstream.astype(BF16)
        final = second
        normed_grad = jnp.zeros((ROWS, D), F32)
        for part in range(2):
            cut = slice(part * FF // 2, (part + 1) * FF // 2)
            act, slope = gelu_parts(nn(normed, sup[:, cut]))
            act = act.astype(BF16)
            active[rows, cut] = act
            final = final + nn(act, sdown[cut])
            hidden_grad = (slope * nt(grad, sdown[cut])).astype(BF16)
            hidden_low[rows, cut] = hidden_grad
            normed_grad = normed_grad + nt(hidden_grad, sup[:, cut])
        out[member] = final
        residual, gain_rows = norm_pull(hat, inverse, sgain_ref[...], normed_grad)
        gains.append(jnp.sum(gain_rows, axis=0, keepdims=True))
        upstream = upstream + residual
        up[rows] = upstream
        mgrad[0, :, :, rows] = nt(mow[...], upstream.astype(BF16)).astype(BF16).reshape(H, HD, ROWS)
    store(out, out_ref.at[0])
    store(up, up_ref)
    store(mgrad, mgrad_ref)
    dgain_ref[...] = gains[0] + gains[1]
    ddown[...] = tn(active[...], cot[...].reshape(flat).astype(BF16)).astype(BF16)
    store(ddown, ddown_ref)
    dup[...] = tn(normed_low[...], hidden_low[...]).astype(BF16)
    store(dup, dup_ref)
    dmo[...] = nn(mixed_rows[0].reshape(D, MB * ROWS), up[...].astype(BF16)).astype(BF16)
    store(dmo, dmo_ref)
    for copy in stores:
        copy.wait()
    for copies, here in outward + backward:
        for copy in copies:
            copy.wait_send()


def latents_forward(collective_id, *args):
    dma = pltpu.SemaphoreType.DMA
    vmem = pl.BlockSpec(memory_space=pltpu.VMEM)
    hbm = pl.BlockSpec(memory_space=pl.ANY)
    rows = MB * ROWS
    stored = [
        ((1, MB, ROWS, D), F32), ((rows, D), F32), ((rows, D), F32), ((3, MB, HD, L), BF16), ((MB, HD, L), F32),
        ((MB, 8, L), F32), ((rows, D), F32), ((1, H, HD, rows), BF16), ((FF, D), BF16), ((D, FF), BF16), ((D, D), BF16),
        ((1, D), F32),
    ]
    return pl.pallas_call(
        latents_forward_kernel,
        in_specs=[hbm, hbm, hbm, hbm, vmem, hbm, hbm, vmem, hbm, hbm, vmem, hbm, hbm],
        out_specs=[hbm] * 5 + [vmem] + [hbm] * 5 + [vmem],
        out_shape=[jax.ShapeDtypeStruct(shape, kind) for shape, kind in stored],
        scratch_shapes=[
            pltpu.VMEM((MB, ROWS, D), F32), pltpu.VMEM((MB, ROWS, D), F32), pltpu.VMEM((MB, ROWS, D), F32),
            pltpu.VMEM((D, D), BF16), pltpu.VMEM((D, FF), BF16), pltpu.VMEM((FF, D), BF16),
            pltpu.VMEM((D, 3 * D), BF16), pltpu.VMEM((D, D), BF16), pltpu.VMEM((D, FF), BF16),
            pltpu.VMEM((FF, D), BF16),
            pltpu.VMEM((MB, ROWS, D), F32), pltpu.VMEM((rows, D), F32), pltpu.VMEM((rows, D), F32),
            pltpu.VMEM((3, MB, HD, L), BF16), pltpu.VMEM((MB, HD, L), F32), pltpu.VMEM((rows, D), F32),
            pltpu.VMEM((1, H, HD, rows), BF16), pltpu.VMEM((FF, D), BF16), pltpu.VMEM((D, FF), BF16),
            pltpu.VMEM((D, D), BF16),
            pltpu.VMEM((3, H, HD, rows), BF16), pltpu.VMEM((L, HD), BF16), pltpu.VMEM((HD + 16, L), BF16),
            pltpu.VMEM((1, MB, HD, L), BF16), pltpu.VMEM((1, H, HD, rows), BF16),
            pltpu.VMEM((rows, FF), BF16), pltpu.VMEM((rows, FF), BF16), pltpu.VMEM((rows, D), BF16),
            dma((10,)), dma((11,)), dma((7, MB)), dma((7, MB)), dma((MB,)), dma((7, MB)), dma((7, MB)), dma((MB,)),
        ],
        compiler_params=pltpu.CompilerParams(
            collective_id=collective_id, has_side_effects=True, vmem_limit_bytes=60 * MIB
        ),
        cost_estimate=pl.CostEstimate(
            flops=20 * 10**9, bytes_accessed=30 * 10**6, transcendentals=10 * 10**6
        ),
        name="latents_forward",
    )(*args)


def levels():
    level = lax.axis_index("grp")
    odd = lax.rem(level, 2)
    return odd, level + 1 - 2 * odd, lax.rem(level + 2, 4)


def half_slices(rows, odd):
    half = rows // 2
    keep = pl.ds(pl.multiple_of(odd * half, half), half)
    away = pl.ds(pl.multiple_of((1 - odd) * half, half), half)
    return keep, away


def tok_steps(items, sources, scratch):
    n = len(items)
    mine, got, near_in, first_in, second_in = [scratch[i * n:(i + 1) * n] for i in range(5)]
    (local_sem, core_send, core_recv, near_send, near_recv, one_send, one_recv, two_send, two_recv) = scratch[5 * n:]
    me, core, chip, mate, (far, flip_x, flip_y) = places()
    x, y = lax.rem(chip, 2), lax.div(chip, 2)
    odd, level_near, level_far = levels()

    def core_copies(i):
        source, rows, row_at, columns, column_at, x_first = items[i]
        part = (pl.ds(row_at, rows), pl.ds(column_at, columns))
        return (
            remote(sources[source].at[:, :, 1 - core, *part], got[i], core_send.at[i], core_recv.at[i], mate),
            pltpu.make_async_copy(sources[source].at[:, :, core, *part], mine[i], local_sem.at[i]),
        )

    def near_copy(i):
        keep, away = half_slices(items[i][1], odd)
        return pltpu.make_async_remote_copy(
            src_ref=mine[i].at[:, :, away], dst_ref=near_in[i], send_sem=near_send.at[i], recv_sem=near_recv.at[i],
            device_id={"grp": level_near}, device_id_type=pl.DeviceIdType.MESH,
        )

    def first_copy(i):
        keep, away = half_slices(items[i][1], odd)
        x_first = items[i][-1]
        source = mine[i].at[:, 1 - x, keep] if x_first else mine[i].at[1 - y, :, keep]
        peer = 2 * (flip_x if x_first else flip_y) + core
        return remote(source, first_in[i], one_send.at[i], one_recv.at[i], peer)

    def second_copy(i):
        keep, away = half_slices(items[i][1], odd)
        x_first = items[i][-1]
        source = mine[i].at[1 - y, x, keep] if x_first else mine[i].at[y, 1 - x, keep]
        peer = 2 * (flip_y if x_first else flip_x) + core
        return remote(source, second_in[i], two_send.at[i], two_recv.at[i], peer)

    def core_sends(i):
        for copy in core_copies(i):
            copy.start()

    def core_sums(i):
        there, here = core_copies(i)
        there.wait_recv()
        here.wait()
        add(mine[i], mine[i], got[i])
        near_copy(i).start()

    def near_sums(i):
        keep, away = half_slices(items[i][1], odd)
        near_copy(i).wait_recv()
        held = mine[i].at[:, :, keep]
        add(held, held, near_in[i])
        first_copy(i).start()

    def first_sums(i):
        keep, away = half_slices(items[i][1], odd)
        first_copy(i).wait_recv()
        held = mine[i].at[:, x, keep] if items[i][-1] else mine[i].at[y, :, keep]
        add(held, held, first_in[i])
        second_copy(i).start()

    def second_sums(i):
        keep, away = half_slices(items[i][1], odd)
        second_copy(i).wait_recv()
        return mine[i][y, x, keep].astype(F32) + second_in[i][...].astype(F32)

    def near_hold(i):
        keep, away = half_slices(items[i][1], odd)
        near_copy(i).wait_recv()
        return mine[i][:, :, keep] + near_in[i][...]

    def finish(near_only=()):
        for i in range(n):
            core_copies(i)[0].wait_send()
            near_copy(i).wait_send()
            if i not in near_only:
                for copy in (first_copy(i), second_copy(i)):
                    copy.wait_send()

    return (core_sends, core_sums, near_sums, first_sums, second_sums, finish, near_hold), (
        mate, 2 * flip_x + core, 2 * flip_y + core)


def quad_steps(items, quads, results, scratch):
    n = len(items)
    first_in, joined, second_in = [scratch[i * n:(i + 1) * n] for i in range(3)]
    one_send, one_recv, two_send, two_recv = scratch[3 * n:]
    me, core, chip, mate, (far, flip_x, flip_y) = places()
    x, y = lax.rem(chip, 2), lax.div(chip, 2)

    def first_copy(i):
        x_first = items[i][-1]
        source = quads[i].at[:, 1 - x] if x_first else quads[i].at[1 - y]
        peer = 2 * (flip_x if x_first else flip_y) + core
        return remote(source, first_in[i], one_send.at[i], one_recv.at[i], peer)

    def second_copy(i):
        x_first = items[i][-1]
        source = joined[i].at[1 - y] if x_first else joined[i].at[1 - x]
        peer = 2 * (flip_y if x_first else flip_x) + core
        return remote(source, second_in[i], two_send.at[i], two_recv.at[i], peer)

    def first_start(i):
        first_copy(i).start()

    def first_sums(i):
        first_copy(i).wait_recv()
        add(joined[i], quads[i].at[:, x] if items[i][-1] else quads[i].at[y], first_in[i])
        second_copy(i).start()

    def second_sums(i):
        second_copy(i).wait_recv()
        add(results[i], joined[i].at[y] if items[i][-1] else joined[i].at[x], second_in[i])

    def finish():
        for i in range(n):
            for copy in (first_copy(i), second_copy(i)):
                copy.wait_send()

    return first_start, first_sums, second_sums, finish


def plain_steps(items, sources, scratch):
    n = len(items)
    mine, got, near_in, first_in, second_in = [scratch[i * n:(i + 1) * n] for i in range(5)]
    (local_sem, core_send, core_recv, near_send, near_recv, one_send, one_recv, two_send, two_recv) = scratch[5 * n:]
    me, core, chip, mate, (far, flip_x, flip_y) = places()
    x, y = lax.rem(chip, 2), lax.div(chip, 2)
    odd, level_near, level_far = levels()

    def core_copy(i):
        return remote(sources[i].at[:, :, 1 - core], got[i], core_send.at[i], core_recv.at[i], mate)

    def local_copy(i):
        return pltpu.make_async_copy(sources[i].at[:, :, core], mine[i], local_sem.at[i])

    def first_copy(i):
        x_first = items[i][-1]
        source = mine[i].at[:, 1 - x] if x_first else mine[i].at[1 - y]
        peer = 2 * (flip_x if x_first else flip_y) + core
        return remote(source, first_in[i], one_send.at[i], one_recv.at[i], peer)

    def second_copy(i):
        x_first = items[i][-1]
        source = mine[i].at[1 - y, x] if x_first else mine[i].at[y, 1 - x]
        peer = 2 * (flip_y if x_first else flip_x) + core
        return remote(source, second_in[i], two_send.at[i], two_recv.at[i], peer)

    def near_copy(i):
        keep, away = half_slices(items[i][1], odd)
        return pltpu.make_async_remote_copy(
            src_ref=mine[i].at[y, x, away], dst_ref=near_in[i], send_sem=near_send.at[i], recv_sem=near_recv.at[i],
            device_id={"grp": level_near}, device_id_type=pl.DeviceIdType.MESH,
        )

    def core_sends(i):
        core_copy(i).start()
        local_copy(i).start()

    def core_sums(i):
        core_copy(i).wait_recv()
        local_copy(i).wait()
        add(mine[i], mine[i], got[i])
        first_copy(i).start()

    def first_sums(i):
        first_copy(i).wait_recv()
        held = mine[i].at[:, x] if items[i][-1] else mine[i].at[y]
        add(held, held, first_in[i])
        second_copy(i).start()

    def second_sums(i):
        second_copy(i).wait_recv()
        held = mine[i].at[y, x]
        add(held, held, second_in[i])
        near_copy(i).start()

    def near_sums(i):
        keep, away = half_slices(items[i][1], odd)
        near_copy(i).wait_recv()
        return mine[i][y, x, keep].astype(F32) + near_in[i][...].astype(F32)

    def finish():
        for i in range(n):
            for copy in (core_copy(i), near_copy(i), first_copy(i), second_copy(i)):
                copy.wait_send()

    return (core_sends, core_sums, first_sums, second_sums, near_sums, finish), (
        mate, 2 * flip_x + core, 2 * flip_y + core)


def grp_steps(items, held, outs, scratch, joined=None):
    n = len(items)
    far_in, own_joined, near_in = [scratch[i * n:(i + 1) * n] for i in range(3)]
    z_send, z_recv = scratch[3 * n:]
    joined = own_joined if joined is None else joined
    odd, level_near, level_far = levels()

    def along(i, step):
        source, target, other = (
            (held[i], far_in[i], level_far),
            (joined[i], near_in[i], level_near),
        )[step]
        return pltpu.make_async_remote_copy(
            src_ref=source, dst_ref=target, send_sem=z_send.at[i, step], recv_sem=z_recv.at[i, step],
            device_id={"grp": other}, device_id_type=pl.DeviceIdType.MESH,
        )

    def store(i, odd_half, value):
        source, rows, row_at, columns, column_at, x_first = items[i]
        half = rows // 2
        start = pl.multiple_of(row_at + odd_half * half, half)
        outs[source][pl.ds(start, half), pl.ds(column_at, columns)] = value.astype(F32)

    def far_start(i):
        along(i, 0).start()

    def far_join(i):
        along(i, 0).wait_recv()
        add(joined[i], held[i], far_in[i])

    def near_start(i):
        along(i, 1).start()
        store(i, odd, joined[i][...])

    def far_sum(i):
        far_join(i)
        near_start(i)

    def near_store(i):
        along(i, 1).wait_recv()
        store(i, 1 - odd, near_in[i][...])

    def finish(steps=(0, 1)):
        for i in range(n):
            for step in steps:
                along(i, step).wait_send()

    return (far_start, far_sum, near_store, finish, far_join, near_start), (level_near, level_far)


def add(target, one, two):
    target[...] = one[...] + two[...]


def reduce_kernel(items, whole, square, joined, count, *refs):
    n, m, q, k = len(items), len(whole), len(square), len(joined)

    def take(length):
        nonlocal refs
        head, refs = refs[:length], refs[length:]
        return head

    sources, held, quads, done = take(count), take(m), take(q), take(k)
    outs, whole_outs, quad_outs, joined_outs = take(count), take(m), take(q), take(k)
    tok, near_devices = plain_steps(items, sources, take(5 * n + 9))
    own_held = take(n)
    late, grp_devices = grp_steps(items, own_held, outs, take(3 * n + 2))
    early, unused = grp_steps(whole, held, whole_outs, take(3 * m + 2))
    quad_held = take(q)
    sums = quad_steps(square, quads, quad_held, take(3 * q + 4))
    mid, unused = grp_steps(square, quad_held, quad_outs, take(3 * q + 2))
    first, unused = grp_steps(joined, done, joined_outs, refs, done)
    greet_all(near_devices, grp_devices)
    for i in range(n):
        tok[0](i)
    for i in range(m):
        early[0](i)
    for i in range(q):
        sums[0](i)
    for i in range(n):
        tok[1](i)
    for i in range(k):
        first[5](i)
    for i in range(q):
        sums[1](i)
    for i in range(n):
        tok[2](i)
    for i in range(q):
        sums[2](i)
        mid[0](i)
    for i in range(n):
        tok[3](i)
    for i in range(n):
        own_held[i][...] = tok[4](i).astype(own_held[i].dtype)
        late[0](i)
    for i in range(m):
        early[1](i)
    for i in range(k):
        first[2](i)
    for i in range(q):
        mid[1](i)
    for i in range(n):
        late[1](i)
    for i in range(m):
        early[2](i)
    for i in range(q):
        mid[2](i)
    for i in range(n):
        late[2](i)
    tok[-1]()
    sums[-1]()
    late[3]()
    early[3]()
    mid[3]()
    first[3]((1,))


def reduce_plan(arrays):
    sources, items = [], []
    for source, array in enumerate(arrays):
        rows, columns = array.shape[0] // TOK, array.shape[1]
        sources.append(array.reshape(2, 2, 2, rows, columns))
        items.append((source, rows, 0, columns, 0, source % 2 == 0))
    kinds = [array.dtype for array in arrays]
    shapes = [(array.shape[0] // TOK, array.shape[1]) for array in arrays]
    return sources, tuple(items), kinds, shapes


def held_plan(arrays):
    items = tuple((i, 2 * array.shape[0], 0, array.shape[1], 0, True) for i, array in enumerate(arrays))
    return items, [array.dtype for array in arrays]


def item_blocks(items, kinds, lead, part):
    return [pltpu.VMEM(lead + (item[1] // part, item[3]), kind) for item, kind in zip(items, kinds)]


def quad_plan(arrays, x_firsts):
    items = tuple(
        (i, 2 * array.shape[2], 0, array.shape[3], 0, x_first) for i, (array, x_first) in enumerate(zip(arrays, x_firsts))
    )
    return items, [array.dtype for array in arrays]


def quad_scratch(items, kinds):
    blocks = functools.partial(item_blocks, items, kinds)
    return blocks((2,), 2) + blocks((2,), 2) + blocks((), 2) + [pltpu.SemaphoreType.DMA((len(items),))] * 4


def plain_scratch(items, kinds):
    blocks = functools.partial(item_blocks, items, kinds)
    return (blocks((2, 2), 1) + blocks((2, 2), 1) + blocks((), 2) + blocks((2,), 1) + blocks((), 1)
            + [pltpu.SemaphoreType.DMA((len(items),))] * 9)


def tok_scratch(items, kinds):
    blocks = functools.partial(item_blocks, items, kinds)
    return (blocks((2, 2), 1) + blocks((2, 2), 1) + blocks((2, 2), 2) + blocks((2,), 2) + blocks((), 2)
            + [pltpu.SemaphoreType.DMA((len(items),))] * 9)


def grp_scratch(items, kinds):
    blocks = functools.partial(item_blocks, items, kinds)
    return blocks((), 2) * 3 + [pltpu.SemaphoreType.DMA((len(items), 2))] * 2


def reduce_grads(collective_id, arrays, held, quads, x_firsts, done):
    sources, items, kinds, shapes = reduce_plan(arrays)
    whole, whole_kinds = held_plan(held)
    square, square_kinds = quad_plan(quads, x_firsts)
    joined, joined_kinds = held_plan(done)
    vmem = pl.BlockSpec(memory_space=pltpu.VMEM)
    hbm = pl.BlockSpec(memory_space=pl.ANY)
    rest = len(held) + len(quads) + len(done)
    return pl.pallas_call(
        functools.partial(reduce_kernel, items, whole, square, joined, len(arrays)),
        in_specs=[hbm] * len(arrays) + [vmem] * rest,
        out_specs=[vmem] * (len(arrays) + rest),
        out_shape=[jax.ShapeDtypeStruct(shape, F32) for shape in shapes]
        + [jax.ShapeDtypeStruct((item[1], item[3]), F32) for item in whole + square + joined],
        scratch_shapes=plain_scratch(items, kinds) + item_blocks(items, kinds, (), 2) + grp_scratch(items, kinds)
        + grp_scratch(whole, whole_kinds) + item_blocks(square, square_kinds, (), 2)
        + quad_scratch(square, square_kinds) + grp_scratch(square, square_kinds) + grp_scratch(joined, joined_kinds),
        compiler_params=pltpu.CompilerParams(
            collective_id=collective_id, has_side_effects=True, vmem_limit_bytes=56 * MIB
        ),
        name="reduce_grads",
    )(*sources, *held, *quads, *done)


def write_kernel(count, *refs):
    sources, gain_ref, outs = refs[:count], refs[count], refs[count + 1:2 * count + 1]
    gain_outs, buffers = refs[2 * count + 1:-count - 2], refs[-count - 2:-2]
    in_sem, out_sem = refs[-2:]
    ins = [pltpu.make_async_copy(sources[i], buffers[i], in_sem.at[i]) for i in range(count)]
    backs = [pltpu.make_async_copy(buffers[i], outs[i], out_sem.at[i]) for i in range(count)]
    for copy in ins:
        copy.start()
    for i, out in enumerate(gain_outs):
        out[...] = gain_ref[i:i + 1, 0:D // TOK]
    for i in range(count):
        ins[i].wait()
        backs[i].start()
    for copy in backs:
        copy.wait()


def write_results(results, gains, gain_count):
    n = len(results)
    hbm, vmem = pl.BlockSpec(memory_space=pl.ANY), pl.BlockSpec(memory_space=pltpu.VMEM)
    return pl.pallas_call(
        functools.partial(write_kernel, n),
        in_specs=[hbm] * n + [vmem],
        out_specs=[hbm] * n + [vmem] * gain_count,
        out_shape=[jax.ShapeDtypeStruct(result.shape, result.dtype) for result in results]
        + [jax.ShapeDtypeStruct((1, D // TOK), F32)] * gain_count,
        scratch_shapes=[pltpu.VMEM(result.shape, result.dtype) for result in results]
        + [pltpu.SemaphoreType.DMA((n,)), pltpu.SemaphoreType.DMA((n,))],
        compiler_params=pltpu.CompilerParams(vmem_limit_bytes=60 * MIB),
        name="write_results",
    )(*results, gains)


def latents_backward_kernel(items, *refs):
    (mgrad_ref, packed_ref, exact_ref, lse_ref, up_ref, mmid_ref, fmid_ref, att_ref, clse_ref, ow_ref, fgain_ref,
     fup_ref, fdown_ref, mgain_ref, proj_ref) = refs[:15]
    count = max(item[0] for item in items) + 1
    sources = refs[15:15 + count]
    (agrad_ref, fig_ref, lup_ref, dup_ref, ddown_ref, dproj_ref, dout_ref, dmgain_ref, dfgain_ref) = refs[
        15 + count:24 + count]
    reduced = refs[24 + count:24 + 2 * count]
    rest = refs[24 + 2 * count:]
    (heads, exact, ups, mmid, fmid, att, ow, fup, fdown, proj, keys, values, upstream_heads, key_acc, value_acc,
     grads, back, agrad, lup, dup, ddown, dproj, dout, hidden, active, hidden_low, grad_low,
     load_sem, store_sem, send_a, recv_a, local_a, send_b, recv_b, local_b) = rest[:35]
    me, peers = all_peers()
    reducer, near_devices = tok_steps(items, sources, rest[35:])
    core_sends, core_sums, near_sums, first_sums, second_sums, finish = reducer[:6]
    odd, level_near, level_far = levels()

    def hold(item):
        reduced[item][...] = second_sums(item).astype(reduced[item].dtype)

    names = ("heads", "exact", "fmid", "fup", "up", "mmid", "proj", "fdown", "att", "ow")
    loads = {}
    for i, (source, target) in enumerate((
        (packed_ref, heads), (exact_ref, exact), (fmid_ref, fmid), (fup_ref, fup), (up_ref, ups), (mmid_ref, mmid),
        (proj_ref, proj), (fdown_ref, fdown), (att_ref, att), (ow_ref, ow),
    )):
        loads[names[i]] = pltpu.make_async_copy(source, target, load_sem.at[i])
        loads[names[i]].start()
    stores = []

    def store(source, target):
        stores.append(pltpu.make_async_copy(source, target, store_sem.at[len(stores)]))
        stores[-1].start()

    greet_all(peers, (level_near,))
    outward = [
        head_copies(mgrad_ref, upstream_heads, True, member, me, peers, send_a, recv_a, local_a) for member in range(MB)
    ]
    backward = [head_copies(back, grads, False, member, me, peers, send_b, recv_b, local_b) for member in range(MB)]
    for copies, here in outward:
        for copy in copies:
            copy.start()
        here.start()
    core_sends(0)
    loads["fmid"].wait()
    loads["fup"].wait()
    first_hat, first_inverse = norm_parts(fmid[...])
    first_normed = (first_hat * fgain_ref[...]).astype(BF16)
    hidden[...] = nn(first_normed, fup[...])
    core_sums(0)
    loads["heads"].wait()
    loads["exact"].wait()
    for member in range(MB):
        keys[...] = heads[1, member].T
        values[...] = heads[2, member].T
        key_acc[...] = jnp.zeros_like(key_acc)
        value_acc[...] = jnp.zeros_like(value_acc)
        copies, here = outward[member]
        for copy in copies:
            copy.wait_recv()
        here.wait()
        if member == 0:
            core_sends(1)
            core_sends(2)

        def attend_back(step, carry, member=member):
            at = pl.ds(pl.multiple_of(step * QB_BACK, QB_BACK), QB_BACK)
            queries = heads[0, member, :, at]
            upstream = upstream_heads[0, member, :, at]
            inner = jnp.sum(upstream.astype(F32) * exact[member, :, at], axis=0, keepdims=True)
            softened = jnp.exp2(nn(keys[...], queries) - lse_ref[member, 0:1, at])
            logit_grad = (softened * (nn(values[...], upstream) - inner)).astype(BF16)
            value_acc[...] += nt(upstream, softened.astype(BF16))
            key_acc[...] += nt(queries, logit_grad)
            grads[0, member, :, at] = (nn(heads[1, member], logit_grad) * HD ** (-0.5)).astype(BF16)
            return carry

        steps = L // QB_BACK
        lax.fori_loop(0, steps, attend_back, 0)
        grads[1, member] = (key_acc[...] * LN2).astype(BF16)
        grads[2, member] = value_acc[...].astype(BF16)
        for copy in backward[member][0] + [backward[member][1]]:
            copy.start()
        if member == 0:
            near_sums(0)
            core_sums(1)
            core_sums(2)
    loads["up"].wait()
    loads["mmid"].wait()
    loads["proj"].wait()
    loads["fdown"].wait()
    mixer_hat, mixer_inverse = norm_parts(mmid[...])
    mixer_normed = (mixer_hat * mgain_ref[...]).astype(BF16).T
    loads["att"].wait()
    loads["ow"].wait()
    mixer_gains, first_gains = [], []

    def rows_back(member):
        copies, here = backward[member]
        for copy in copies:
            copy.wait_recv()
        here.wait()
        rows = slice(member * ROWS, (member + 1) * ROWS)
        normed_grad = nn(proj[...], back[:, :, :, rows].reshape(3 * D, ROWS)).T
        residual, gain_rows = norm_pull(mixer_hat[rows], mixer_inverse[rows], mgain_ref[...], normed_grad)
        mixer_gains.append(jnp.sum(gain_rows, axis=0, keepdims=True))
        upstream = ups[rows] + residual
        grad = upstream.astype(BF16)
        grad_low[rows] = grad
        normed_grad = jnp.zeros((ROWS, D), F32)
        for part in range(2):
            cut = slice(part * FF // 2, (part + 1) * FF // 2)
            act, slope = gelu_parts(hidden[rows, cut])
            active[rows, cut] = act.astype(BF16)
            hidden_grad = (slope * nt(grad, fdown[cut])).astype(BF16)
            hidden_low[rows, cut] = hidden_grad
            normed_grad = normed_grad + nt(hidden_grad, fup[:, cut])
        residual, gain_rows = norm_pull(first_hat[rows], first_inverse[rows], fgain_ref[...], normed_grad)
        first_gains.append(jnp.sum(gain_rows, axis=0, keepdims=True))
        upstream = upstream + residual
        lup[rows] = upstream
        attended_grad = nt(upstream.astype(BF16), ow[...]).astype(BF16)
        agrad[member] = attended_grad
        inner = jnp.sum(attended_grad.astype(F32) * att[member], axis=1, keepdims=True)
        fig_ref[member] = jnp.concatenate(
            [clse_ref[member, 0:1], to_rows(inner, inner)[0:1], jnp.zeros((6, ROWS), F32)], axis=0
        )

    rows_back(0)
    first_sums(0)
    near_sums(1)
    near_sums(2)
    rows_back(1)
    hold(0)
    first_sums(1)
    first_sums(2)
    store(lup, lup_ref)
    store(agrad, agrad_ref)
    dmgain_ref[...] = mixer_gains[0] + mixer_gains[1]
    dfgain_ref[...] = first_gains[0] + first_gains[1]
    grad = grad_low[...]
    ddown[...] = tn(active[...], grad).astype(BF16)
    store(ddown, ddown_ref)
    dup[...] = tn(first_normed, hidden_low[...]).astype(BF16)
    store(dup, dup_ref)
    dproj[...] = nt(mixer_normed, back[...].reshape(3 * D, MB * ROWS)).astype(BF16)
    store(dproj, dproj_ref)
    dout[...] = tn(att[...].reshape(MB * ROWS, D).astype(BF16), lup[...].astype(BF16)).astype(BF16)
    store(dout, dout_ref)
    hold(1)
    hold(2)
    finish()
    for copy in stores:
        copy.wait()
    for copies, here in outward + backward:
        for copy in copies:
            copy.wait_send()


def latents_backward(collective_id, arrays, *args):
    dma = pltpu.SemaphoreType.DMA
    vmem = pl.BlockSpec(memory_space=pltpu.VMEM)
    hbm = pl.BlockSpec(memory_space=pl.ANY)
    rows = MB * ROWS
    sources, items, kinds, shapes = reduce_plan(arrays)
    reduced = [jax.ShapeDtypeStruct((rows_ // 2, columns), kind) for (rows_, columns), kind in zip(shapes, kinds)]
    stored = [
        ((MB, ROWS, D), BF16), ((MB, 8, ROWS), F32), ((rows, D), F32), ((D, FF), BF16), ((FF, D), BF16),
        ((D, 3 * D), BF16), ((D, D), BF16), ((1, D), F32), ((1, D), F32),
    ]
    return pl.pallas_call(
        functools.partial(latents_backward_kernel, items),
        in_specs=[hbm, hbm, hbm, vmem, hbm, hbm, hbm, hbm, vmem, hbm, vmem, hbm, hbm, vmem, hbm] + [hbm] * len(arrays),
        out_specs=[hbm, vmem] + [hbm] * 5 + [vmem] * (2 + len(arrays)),
        out_shape=[jax.ShapeDtypeStruct(shape, kind) for shape, kind in stored] + reduced,
        scratch_shapes=[
            pltpu.VMEM((3, MB, HD, L), BF16), pltpu.VMEM((MB, HD, L), F32), pltpu.VMEM((rows, D), F32),
            pltpu.VMEM((rows, D), F32), pltpu.VMEM((rows, D), F32), pltpu.VMEM((MB, ROWS, D), F32),
            pltpu.VMEM((D, D), BF16), pltpu.VMEM((D, FF), BF16), pltpu.VMEM((FF, D), BF16),
            pltpu.VMEM((D, 3 * D), BF16), pltpu.VMEM((L, HD), BF16), pltpu.VMEM((L, HD), BF16),
            pltpu.VMEM((1, MB, HD, L), BF16), pltpu.VMEM((HD, L), F32), pltpu.VMEM((HD, L), F32),
            pltpu.VMEM((3, MB, HD, L), BF16), pltpu.VMEM((3, H, HD, rows), BF16),
            pltpu.VMEM((MB, ROWS, D), BF16), pltpu.VMEM((rows, D), F32), pltpu.VMEM((D, FF), BF16),
            pltpu.VMEM((FF, D), BF16), pltpu.VMEM((D, 3 * D), BF16), pltpu.VMEM((D, D), BF16),
            pltpu.VMEM((rows, FF), F32), pltpu.VMEM((rows, FF), BF16), pltpu.VMEM((rows, FF), BF16),
            pltpu.VMEM((rows, D), BF16),
            dma((10,)), dma((6,)), dma((7, MB)), dma((7, MB)), dma((MB,)), dma((7, MB)), dma((7, MB)), dma((MB,)),
        ] + tok_scratch(items, kinds),
        compiler_params=pltpu.CompilerParams(
            collective_id=collective_id, has_side_effects=True, vmem_limit_bytes=61 * MIB
        ),
        cost_estimate=pl.CostEstimate(
            flops=35 * 10**9, bytes_accessed=36 * 10**6, transcendentals=10 * 10**6
        ),
        name="latents_backward",
    )(*args, *sources)


def fast_body(
    tokens,
    latents,
    segments,
    scene_mask,
    counts,
    token_gain,
    query_gain,
    query_weight,
    key_weight,
    value_weight,
    output_weight,
    first_gain,
    first_up,
    first_down,
    mixer_gain,
    mixer_project,
    mixer_output,
    second_gain,
    second_up,
    second_down,
    cotangent,
):
    scenes = (segments, scene_mask, counts.reshape(MB))
    keys, values, queries, attended, lse = cross_forward(
        0, tokens, latents, token_gain[None], query_gain[None], query_weight, key_weight, value_weight, *scenes
    )
    (latents_out, first_mid, mixer_mid, packed, exact, head_lse, upstream, mixed_grad, d_second_down, d_second_up,
     d_mixer_output, d_second_gain) = latents_forward(
        1, latents, attended, cotangent, output_weight, first_gain[None], first_up, first_down, mixer_gain[None],
        mixer_project, mixer_output, second_gain[None], second_up, second_down,
    )
    (attended_grad, figures, upstream, d_first_up, d_first_down, d_project, d_output, d_mixer_gain, d_first_gain,
     *early) = latents_backward(
        2, [d_second_up, d_second_down, d_mixer_output], mixed_grad, packed, exact, head_lse, upstream, mixer_mid,
        first_mid, attended, lse, output_weight, first_gain[None], first_up, first_down, mixer_gain[None], mixer_project,
    )
    latents_grad, tokens_grad, d_key, d_value, d_query, gains, *rest = cross_backward(
        5, early, [d_first_up, d_first_down, d_project], tokens, token_gain[None], key_weight, value_weight,
        *scenes, keys, values, queries, attended_grad, figures, latents, upstream, query_gain[None], query_weight,
        d_first_gain, d_mixer_gain, d_second_gain,
    )
    early, held, quads = rest[:len(early)], rest[len(early):len(early) + 1], rest[len(early) + 1:]
    o_output, o_key, o_value, o_query, gains, *late = reduce_grads(
        7, [d_output, d_key, d_value, d_query, gains], held, quads, (False, True), early
    )
    late, early = late[:3], late[3:]
    (latents_out, latents_grad, tokens_grad, o_second_up, o_second_down, o_mixer_output, o_first_up, o_first_down,
     o_project, o_output, o_key, o_value, o_query, *o_gains) = write_results(
        [latents_out, latents_grad.reshape(latents_out.shape), tokens_grad, *early, *late, o_output, o_key, o_value, o_query], gains, 5
    )
    o_gains = [gain.reshape(D // TOK) for gain in o_gains]
    return (
        latents_out,
        latents_grad,
        tokens_grad,
        o_gains[0],
        o_gains[1],
        o_query,
        o_key,
        o_value,
        o_output,
        o_gains[2],
        o_first_up,
        o_first_down,
        o_gains[3],
        o_project,
        o_mixer_output,
        o_gains[4],
        o_second_up,
        o_second_down,
    )


IN_SPECS = (
    P("grp", None, "tok", None),
    P("grp", None, None, None),
    P("grp", None, "tok"),
    P("grp", None, None, None),
    P("grp", None, "tok"),
    P(),
    P(),
    P(),
    P(),
    P(),
    P(),
    P(),
    P(),
    P(),
    P(),
    P(),
    P(),
    P(),
    P(),
    P(),
    P("grp", None, "tok", None),
)
OUT_SPECS = (
    P("grp", None, "tok", None),
    P("grp", None, "tok", None),
    P("grp", None, "tok", None),
    P("tok"),
    P("tok"),
    P("tok", None),
    P("tok", None),
    P("tok", None),
    P("tok", None),
    P("tok"),
    P("tok", None),
    P("tok", None),
    P("tok"),
    P("tok", None),
    P("tok", None),
    P("tok"),
    P("tok", None),
    P("tok", None),
)


def solution(mesh):
    return jax.shard_map(
        fast_body if mesh.shape["tok"] == TOK else general_body,
        mesh=mesh,
        in_specs=IN_SPECS,
        out_specs=OUT_SPECS,
        check_vma=False,
    )
```

```python
import functools

import jax
import jax.numpy as jnp
from jax import lax
from jax.experimental import pallas as pl
from jax.experimental.pallas import tpu as pltpu
from jax.sharding import PartitionSpec as P

D = 512
L = 2048
H = 8
HD = 64
TOK_DEV = 1024
MB = 2
SCENES = 8
LGROUPS = 8


EPS = 1e-05
NEG = -1e30


def norm_rows(values, gain):
    centre = values - jnp.mean(values, axis=-1, keepdims=True)
    spread = jnp.mean(centre * centre, axis=-1, keepdims=True)
    return centre * lax.rsqrt(spread + EPS) * gain


def norm_back(values, gain, upstream):
    unused, pull = jax.vjp(norm_rows, values, gain)
    return pull(upstream)


def gelu_back(hidden, upstream):
    unused, pull = jax.vjp(jax.nn.gelu, hidden)
    return pull(upstream)[0]


def product_plain(left, right):
    return jnp.dot(left, right, preferred_element_type=jnp.float32)


def product_rows(left, right):
    return lax.dot_general(
        left, right, (((0,), (0,)), ((), ())), preferred_element_type=jnp.float32
    )


def product_cols(left, right):
    return lax.dot_general(
        left, right, (((1,), (1,)), ((), ())), preferred_element_type=jnp.float32
    )


def add_term(store, name, value):
    if name in store:
        store[name] = store[name] + value
    else:
        store[name] = value


def project_tokens(tokens, member, token_gain, key_weight, value_weight):
    source = tokens[0, member].astype(jnp.float32)
    normed = norm_rows(source, token_gain).astype(jnp.bfloat16)
    key_rows = product_plain(normed, key_weight).astype(jnp.bfloat16)
    value_rows = product_plain(normed, value_weight).astype(jnp.bfloat16)
    return (source, normed, key_rows, value_rows)


def mlp_forward(residual, gain, up_weight, down_weight):
    normed = norm_rows(residual, gain).astype(jnp.bfloat16)
    hidden = product_plain(normed, up_weight)
    active = jax.nn.gelu(hidden).astype(jnp.bfloat16)
    return (residual + product_plain(active, down_weight), (normed, hidden, active))


def mlp_backward(residual, gain, up_weight, down_weight, saved, upstream):
    normed, hidden, active = saved
    grad_low = upstream.astype(jnp.bfloat16)
    grad_down = product_rows(active, grad_low)
    hidden_grad = gelu_back(hidden, product_cols(grad_low, down_weight)).astype(jnp.bfloat16)
    grad_up = product_rows(normed, hidden_grad)
    residual_grad, grad_gain = norm_back(residual, gain, product_cols(hidden_grad, up_weight))
    return (upstream + residual_grad, grad_gain, grad_up, grad_down)


def mixer_forward(residual, gain, project, output):
    own_rows = residual.shape[0]
    normed = norm_rows(residual, gain).astype(jnp.bfloat16)
    packed = product_plain(normed, project).astype(jnp.bfloat16)
    pair_rows = lax.all_gather(packed[:, D:], "tok", axis=0, tiled=True)
    every = pair_rows.shape[0]
    own_queries = packed[:, :D].reshape(own_rows, H, HD)
    keys = pair_rows[:, :D].reshape(every, H, HD)
    values = pair_rows[:, D:].reshape(every, H, HD)
    logits = jnp.einsum(
        "qhd,khd->hqk", own_queries, keys, preferred_element_type=jnp.float32
    ) * HD ** (-0.5)
    peak_row = jnp.max(logits, axis=-1, keepdims=True)
    raised = jnp.exp(logits - peak_row)
    softened = raised / jnp.sum(raised, axis=-1, keepdims=True)
    softened_low = softened.astype(jnp.bfloat16)
    mixed_rows = jnp.einsum(
        "hqk,khd->qhd", softened_low, values, preferred_element_type=jnp.float32
    )
    mixed_rows = mixed_rows.reshape(own_rows, D).astype(jnp.bfloat16)
    return (
        residual + product_plain(mixed_rows, output),
        (normed, own_queries, keys, values, softened, softened_low, mixed_rows),
    )


def mixer_backward(residual, gain, project, output, saved, upstream):
    normed, own_queries, keys, values, softened, softened_low, mixed_rows = saved
    own_rows = upstream.shape[0]
    every = keys.shape[0]
    grad_low = upstream.astype(jnp.bfloat16)
    grad_output = product_rows(mixed_rows, grad_low)
    mixed_grad = product_cols(grad_low, output).astype(jnp.bfloat16).reshape(own_rows, H, HD)
    value_grad = jnp.einsum(
        "hqk,qhd->khd", softened_low, mixed_grad, preferred_element_type=jnp.float32
    )
    soft_grad = jnp.einsum("qhd,khd->hqk", mixed_grad, values, preferred_element_type=jnp.float32)
    logit_grad = softened * (soft_grad - jnp.sum(soft_grad * softened, axis=-1, keepdims=True))
    logit_grad = logit_grad.astype(jnp.bfloat16)
    query_grad = jnp.einsum(
        "hqk,khd->qhd", logit_grad, keys, preferred_element_type=jnp.float32
    ) * HD ** (-0.5)
    key_grad = jnp.einsum(
        "hqk,qhd->khd", logit_grad, own_queries, preferred_element_type=jnp.float32
    ) * HD ** (-0.5)
    pair_terms = jnp.concatenate([key_grad.reshape(every, D), value_grad.reshape(every, D)], axis=1)
    pair_grad = lax.psum_scatter(
        pair_terms.astype(jnp.bfloat16), "tok", scatter_dimension=0, tiled=True
    ).astype(jnp.float32)
    packed_grad = jnp.concatenate([query_grad.reshape(own_rows, D), pair_grad], axis=1).astype(
        jnp.bfloat16
    )
    grad_project = product_rows(normed, packed_grad)
    residual_grad, grad_gain = norm_back(residual, gain, product_cols(packed_grad, project))
    return (upstream + residual_grad, grad_gain, grad_project, grad_output)


def general_body(
    tokens,
    latents,
    segments,
    scene_mask,
    counts,
    token_gain,
    query_gain,
    query_weight,
    key_weight,
    value_weight,
    output_weight,
    first_gain,
    first_up,
    first_down,
    mixer_gain,
    mixer_project,
    mixer_output,
    second_gain,
    second_up,
    second_down,
    cotangent,
):
    scale = D ** (-0.5)
    shards = lax.axis_size("tok")
    own_rows = L // shards
    row_start = lax.axis_index("tok") * own_rows
    latent_group = jnp.arange(L) // (L // LGROUPS)
    latent_onehot = (latent_group[:, None] == jnp.arange(LGROUPS)[None, :]).astype(jnp.float32)
    token_place = jnp.arange(TOK_DEV)
    records = []
    latent_outs = []
    for member in range(MB):
        record = {}
        source, normed, key_rows, value_rows = project_tokens(
            tokens, member, token_gain, key_weight, value_weight
        )
        record["token_side"] = (source, normed, key_rows, value_rows)
        scene_onehot = (segments[0, member][:, None] == jnp.arange(SCENES)[None, :]).astype(
            jnp.float32
        )
        token_seen = jnp.dot(scene_onehot, scene_mask[0, member].astype(jnp.float32))
        visible = product_cols(latent_onehot, token_seen)
        alive = token_place < counts[0, member, 0]
        allowed = (visible > 0.5) & alive[None, :]
        latent_every = latents[0, member]
        normed_every = norm_rows(latent_every, query_gain).astype(jnp.bfloat16)
        queries = product_plain(normed_every, query_weight).astype(jnp.bfloat16)
        scores = jnp.where(allowed, product_cols(queries, key_rows) * scale, NEG)
        row_top = lax.pmax(jnp.max(scores, axis=1), "tok")
        unnormed = jnp.exp(scores - row_top[:, None])
        row_total, weighted = (
            lax.psum_scatter(
                jnp.sum(unnormed, axis=1).astype(jnp.bfloat16),
                "tok",
                scatter_dimension=0,
                tiled=True,
            ).astype(jnp.float32),
            lax.psum_scatter(
                product_plain(unnormed.astype(jnp.bfloat16), value_rows).astype(jnp.bfloat16),
                "tok",
                scatter_dimension=0,
                tiled=True,
            ).astype(jnp.float32),
        )
        latent_in = lax.dynamic_slice_in_dim(latent_every, row_start, own_rows, 0)
        latent_normed = lax.dynamic_slice_in_dim(normed_every, row_start, own_rows, 0)
        attended = weighted / row_total[:, None]
        attended_low = attended.astype(jnp.bfloat16)
        first_mid = latent_in + product_plain(attended_low, output_weight)
        mixer_mid, first_saved = mlp_forward(first_mid, first_gain, first_up, first_down)
        second_mid, mixer_saved = mixer_forward(mixer_mid, mixer_gain, mixer_project, mixer_output)
        final_rows, second_saved = mlp_forward(second_mid, second_gain, second_up, second_down)
        latent_outs.append(final_rows)
        record["latent_side"] = (
            allowed,
            latent_in,
            latent_normed,
            queries,
            row_top,
            row_total,
            attended,
            attended_low,
            first_mid,
            mixer_mid,
            second_mid,
            first_saved,
            mixer_saved,
            second_saved,
        )
        records.append(record)
    grads = {}
    latent_grads = []
    token_grads = []
    for member in range(MB):
        record = records[member]
        source, normed, key_rows, value_rows = record["token_side"]
        (
            allowed,
            latent_in,
            latent_normed,
            queries,
            row_top,
            row_total,
            attended,
            attended_low,
            first_mid,
            mixer_mid,
            second_mid,
            first_saved,
            mixer_saved,
            second_saved,
        ) = record["latent_side"]
        second_back = mlp_backward(
            second_mid, second_gain, second_up, second_down, second_saved, cotangent[0, member]
        )
        add_term(grads, "second_gain", second_back[1])
        add_term(grads, "second_up", second_back[2])
        add_term(grads, "second_down", second_back[3])
        mixer_back = mixer_backward(
            mixer_mid, mixer_gain, mixer_project, mixer_output, mixer_saved, second_back[0]
        )
        add_term(grads, "mixer_gain", mixer_back[1])
        add_term(grads, "mixer_project", mixer_back[2])
        add_term(grads, "mixer_output", mixer_back[3])
        first_back = mlp_backward(
            first_mid, first_gain, first_up, first_down, first_saved, mixer_back[0]
        )
        add_term(grads, "first_gain", first_back[1])
        add_term(grads, "first_up", first_back[2])
        add_term(grads, "first_down", first_back[3])
        latent_upstream = first_back[0]
        grad_low = latent_upstream.astype(jnp.bfloat16)
        add_term(grads, "output_weight", product_rows(attended_low, grad_low))
        attended_grad = lax.optimization_barrier(
            product_cols(grad_low, output_weight).astype(jnp.bfloat16)
        ).astype(jnp.float32)
        weighted_grad = (attended_grad / row_total[:, None]).astype(jnp.bfloat16)
        total_grad = -jnp.sum(attended_grad * attended, axis=1) / row_total
        weighted_every, total_every = (
            lax.all_gather(
                weighted_grad.astype(jnp.float32).astype(jnp.bfloat16), "tok", axis=0, tiled=True
            ).astype(jnp.float32),
            lax.all_gather(total_grad.astype(jnp.bfloat16), "tok", axis=0, tiled=True).astype(
                total_grad.dtype
            ),
        )
        weighted_every = weighted_every.astype(jnp.bfloat16)
        scores = jnp.where(allowed, product_cols(queries, key_rows) * scale, NEG)
        unnormed = jnp.exp(scores - row_top[:, None])
        unnormed_grad = product_cols(weighted_every, value_rows) + total_every[:, None]
        score_grad = (unnormed * unnormed_grad).astype(jnp.bfloat16)
        value_grad = product_rows(unnormed.astype(jnp.bfloat16), weighted_every).astype(
            jnp.bfloat16
        )
        key_grad = (product_rows(score_grad, queries) * scale).astype(jnp.bfloat16)
        query_grad = lax.psum_scatter(
            (product_plain(score_grad, key_rows) * scale).astype(jnp.bfloat16),
            "tok",
            scatter_dimension=0,
            tiled=True,
        )
        add_term(grads, "key_weight", product_rows(normed, key_grad))
        add_term(grads, "value_weight", product_rows(normed, value_grad))
        normed_grad = product_cols(key_grad, key_weight) + product_cols(value_grad, value_weight)
        source_grad, gain_grad = norm_back(source, token_gain, normed_grad)
        add_term(grads, "token_gain", gain_grad)
        token_grads.append(source_grad)
        add_term(grads, "query_weight", product_rows(latent_normed, query_grad))
        latent_grad, gain_grad = norm_back(
            latent_in, query_gain, product_cols(query_grad, query_weight)
        )
        add_term(grads, "query_gain", gain_grad)
        latent_grads.append(latent_upstream + latent_grad)
    parts = (
        lax.psum_scatter(
            grads["token_gain"].astype(jnp.bfloat16), "tok", scatter_dimension=0, tiled=True
        ).astype(jnp.float32),
        lax.psum_scatter(
            grads["query_gain"].astype(jnp.bfloat16), "tok", scatter_dimension=0, tiled=True
        ).astype(jnp.float32),
        lax.psum_scatter(
            grads["query_weight"].astype(jnp.bfloat16), "tok", scatter_dimension=0, tiled=True
        ).astype(jnp.float32),
        lax.psum_scatter(
            grads["key_weight"].astype(jnp.bfloat16), "tok", scatter_dimension=0, tiled=True
        ).astype(jnp.float32),
        lax.psum_scatter(
            grads["value_weight"].astype(jnp.bfloat16), "tok", scatter_dimension=0, tiled=True
        ).astype(jnp.float32),
        lax.psum_scatter(
            grads["output_weight"].astype(jnp.bfloat16), "tok", scatter_dimension=0, tiled=True
        ).astype(jnp.float32),
        lax.psum_scatter(
            grads["first_gain"].astype(jnp.bfloat16), "tok", scatter_dimension=0, tiled=True
        ).astype(jnp.float32),
        lax.psum_scatter(
            grads["first_up"].astype(jnp.bfloat16), "tok", scatter_dimension=0, tiled=True
        ).astype(jnp.float32),
        lax.psum_scatter(
            grads["first_down"].astype(jnp.bfloat16), "tok", scatter_dimension=0, tiled=True
        ).astype(jnp.float32),
        lax.psum_scatter(
            grads["mixer_gain"].astype(jnp.bfloat16), "tok", scatter_dimension=0, tiled=True
        ).astype(jnp.float32),
        lax.psum_scatter(
            grads["mixer_project"].astype(jnp.bfloat16), "tok", scatter_dimension=0, tiled=True
        ).astype(jnp.float32),
        lax.psum_scatter(
            grads["mixer_output"].astype(jnp.bfloat16), "tok", scatter_dimension=0, tiled=True
        ).astype(jnp.float32),
        lax.psum_scatter(
            grads["second_gain"].astype(jnp.bfloat16), "tok", scatter_dimension=0, tiled=True
        ).astype(jnp.float32),
        lax.psum_scatter(
            grads["second_up"].astype(jnp.bfloat16), "tok", scatter_dimension=0, tiled=True
        ).astype(jnp.float32),
        lax.psum_scatter(
            grads["second_down"].astype(jnp.bfloat16), "tok", scatter_dimension=0, tiled=True
        ).astype(jnp.float32),
    )
    summed = (
        lax.psum(parts[0].astype(jnp.bfloat16), "grp").astype(jnp.float32),
        lax.psum(parts[1].astype(jnp.bfloat16), "grp").astype(jnp.float32),
        lax.psum(parts[2].astype(jnp.bfloat16), "grp").astype(jnp.float32),
        lax.psum(parts[3].astype(jnp.bfloat16), "grp").astype(jnp.float32),
        lax.psum(parts[4].astype(jnp.bfloat16), "grp").astype(jnp.float32),
        lax.psum(parts[5].astype(jnp.bfloat16), "grp").astype(jnp.float32),
        lax.psum(parts[6].astype(jnp.bfloat16), "grp").astype(jnp.float32),
        lax.psum(parts[7].astype(jnp.bfloat16), "grp").astype(jnp.float32),
        lax.psum(parts[8].astype(jnp.bfloat16), "grp").astype(jnp.float32),
        lax.psum(parts[9].astype(jnp.bfloat16), "grp").astype(jnp.float32),
        lax.psum(parts[10].astype(jnp.bfloat16), "grp").astype(jnp.float32),
        lax.psum(parts[11].astype(jnp.bfloat16), "grp").astype(jnp.float32),
        lax.psum(parts[12].astype(jnp.bfloat16), "grp").astype(jnp.float32),
        lax.psum(parts[13].astype(jnp.bfloat16), "grp").astype(jnp.float32),
        lax.psum(parts[14].astype(jnp.bfloat16), "grp").astype(jnp.float32),
    )
    return (
        jnp.stack(latent_outs)[None],
        jnp.stack(latent_grads)[None],
        jnp.stack(token_grads)[None],
    ) + tuple(summed)


TOK = 8
ROWS = L // TOK
FF = 2048
GR = L // LGROUPS
LOG2E = 1.4426950408889634
LN2 = 0.6931471805599453
F32 = jnp.float32
BF16 = jnp.bfloat16
MIB = 1024 * 1024


def nn(left, right):
    return lax.dot_general(left, right, (((1,), (0,)), ((), ())), preferred_element_type=F32)


def nt(left, right):
    return lax.dot_general(left, right, (((1,), (1,)), ((), ())), preferred_element_type=F32)


def tn(left, right):
    return lax.dot_general(left, right, (((0,), (0,)), ((), ())), preferred_element_type=F32)


def norm_parts(values):
    centre = values - jnp.mean(values, axis=-1, keepdims=True)
    inverse = lax.rsqrt(jnp.mean(centre * centre, axis=-1, keepdims=True) + EPS)
    return centre * inverse, inverse


def norm_pull(hat, inverse, gain, upstream):
    scaled = upstream * gain
    inner = jnp.mean(scaled * hat, axis=-1, keepdims=True)
    grad = (scaled - jnp.mean(scaled, axis=-1, keepdims=True) - hat * inner) * inverse
    return grad, upstream * hat


def places():
    me = lax.axis_index("tok")
    core = lax.rem(me, 2)
    chip = lax.div(me, 2)
    mate = me + 1 - 2 * core
    flip_x = chip + 1 - 2 * lax.rem(chip, 2)
    flip_y = lax.rem(chip + 2, 4)
    far = 3 - chip
    return me, core, chip, mate, (far, flip_x, flip_y)


def remote(src, dst, send_sem, recv_sem, peer):
    return pltpu.make_async_remote_copy(
        src_ref=src,
        dst_ref=dst,
        send_sem=send_sem,
        recv_sem=recv_sem,
        device_id={"tok": peer},
        device_id_type=pl.DeviceIdType.MESH,
    )


def greet(devices):
    barrier = pltpu.get_barrier_semaphore()
    for device in devices:
        pl.semaphore_signal(
            barrier, inc=1, device_id={"tok": device}, device_id_type=pl.DeviceIdType.MESH
        )
    pl.semaphore_wait(barrier, len(devices))


def chip_at(chip, flip):
    high, low = divmod(flip, 2) if isinstance(flip, int) else (lax.div(flip, 2), lax.rem(flip, 2))
    across = lax.rem(lax.rem(chip, 2) + low, 2)
    along = lax.rem(lax.div(chip, 2) + high, 2)
    return 2 * along + across


def mask_loads(seg_ref, mask_ref, seg_buf, mask_buf, sem):
    return (
        pltpu.make_async_copy(seg_ref.at[0], seg_buf, sem.at[0]),
        pltpu.make_async_copy(mask_ref.at[0], mask_buf, sem.at[1]),
    )


def mask_rows(seg_buf, mask_buf, count_ref, bias_ref):
    for member in range(MB):
        scene = lax.broadcasted_iota(jnp.int32, (SCENES, TOK_DEV), 0)
        place = lax.broadcasted_iota(jnp.int32, (SCENES, TOK_DEV), 1)
        hot = jnp.where((seg_buf[member:member + 1] == scene) & (place < count_ref[member]), 1.0, 0.0)
        seen = tn(jnp.where(mask_buf[member] > 0, 1.0, 0.0).astype(BF16), hot.astype(BF16))
        bias_ref[member] = jnp.where(seen > 0.5, 0.0, NEG)


def to_rows(first, second):
    rows = first.shape[0]
    lane = lax.broadcasted_iota(jnp.int32, (rows, 128), 1)
    return jnp.where(lane == 0, first, second).T[0:8]


def cross_forward_kernel(
    tok_ref, lat_ref, tgain_ref, qgain_ref, qw_ref, kw_ref, vw_ref, seg_ref, mask_ref, count_ref,
    k_out, v_out, q_out, att_ref, lse_ref,
    tok_buf, lat_buf, keys, values, queries, bias, part, part_s, got, got_s, stage, stage_s,
    arrive, arrive_s, total, seg_buf, mask_buf,
    mask_sem, tok_sem, lat_sem, k_sem, v_sem, q_sem,
    core_send, core_recv, core_send_s, core_recv_s, chip_send, chip_recv, chip_send_s, chip_recv_s,
):
    me, core, chip, mate, others = places()
    span = 2 * ROWS

    def unpack(step):
        return lax.div(step, 4), 3 - lax.rem(step, 4)

    def lat_copy(step):
        member, flip = unpack(step)
        start = pl.multiple_of(chip_at(chip, flip) * span, span)
        return pltpu.make_async_copy(lat_ref.at[0, member, pl.ds(start, span)], lat_buf.at[step], lat_sem.at[step])

    def q_copy(step):
        member, flip = unpack(step)
        start = pl.multiple_of(chip_at(chip, flip) * span, span)
        return pltpu.make_async_copy(queries.at[step], q_out.at[member, pl.ds(start, span)], q_sem.at[step])

    def tok_copy(member):
        return pltpu.make_async_copy(tok_ref.at[0, member], tok_buf.at[member], tok_sem.at[member])

    def kv_copies(member):
        return (
            pltpu.make_async_copy(keys.at[member], k_out.at[member], k_sem.at[member]),
            pltpu.make_async_copy(values.at[member], v_out.at[member], v_sem.at[member]),
        )

    def core_copies(step):
        return (
            remote(part.at[step, 1 - core], got.at[step], core_send.at[step], core_recv.at[step], mate),
            remote(part_s.at[step, 1 - core], got_s.at[step], core_send_s.at[step], core_recv_s.at[step], mate),
        )

    def chip_copies(step):
        member, flip = unpack(step)
        peer = 2 * chip_at(chip, flip) + core
        place = 3 * member + flip - 1
        return (
            remote(stage.at[step], arrive.at[place], chip_send.at[place], chip_recv.at[place], peer),
            remote(stage_s.at[step], arrive_s.at[place], chip_send_s.at[place], chip_recv_s.at[place], peer),
        )

    tok_copy(0).start()
    masks = mask_loads(seg_ref, mask_ref, seg_buf, mask_buf, mask_sem)
    for copy in masks:
        copy.start()
    for step in range(4):
        lat_copy(step).start()
    tok_copy(1).start()
    for step in range(4, 2 * 4):
        lat_copy(step).start()
    greet([mate] + [2 * other + core for other in others])
    for copy in masks:
        copy.wait()
    mask_rows(seg_buf, mask_buf, count_ref, bias)

    def project(member):
        tok_copy(member).wait()
        hat, inverse = norm_parts(tok_buf[member].astype(F32))
        normed = (hat * tgain_ref[...]).astype(BF16)
        keys[member] = nn(normed, kw_ref[...]).astype(BF16)
        values[member] = nn(normed, vw_ref[...]).astype(BF16)
        for copy in kv_copies(member):
            copy.start()

    def ask(step):
        hat, inverse = norm_parts(lat_buf[step])
        normed = (hat * qgain_ref[...]).astype(BF16)
        queries[step] = (nn(normed, qw_ref[...]) * (D ** (-0.5) * LOG2E)).astype(BF16)

    def compute(step, ahead):
        member, flip = unpack(step)

        @pl.when(flip == 3)
        def _():
            project(member)

        if ahead:
            lat_copy(step + 1).wait()
        scores = nt(queries[step], keys[member])
        if ahead:
            ask(step + 1)
        raised = []
        for half in range(2):
            seen = bias[member, pl.ds(2 * chip_at(chip, flip) + half, 1), :]
            own = scores[half * ROWS:(half + 1) * ROWS] + seen
            top = jnp.max(own, axis=1, keepdims=True)
            own = jnp.exp2(own - top)
            part_s[step, half] = to_rows(top, jnp.sum(own, axis=1, keepdims=True))
            raised.append(own.astype(BF16))
        sums = nn(jnp.concatenate(raised, axis=0), values[member]).astype(BF16)
        for half in range(2):
            part[step, half] = sums[half * ROWS:(half + 1) * ROWS]
        for copy in core_copies(step):
            copy.start()
        if ahead:
            q_copy(step + 1).start()

    def merge(one, one_s, two, two_s):
        top = jnp.maximum(one_s[0:1], two_s[0:1])
        one_w, two_w = jnp.exp2(one_s[0:1] - top), jnp.exp2(two_s[0:1] - top)
        sums = one_s[1:2] * one_w + two_s[1:2] * two_w
        spare = jnp.zeros((6, ROWS), F32)
        weights = jnp.concatenate([one_w, two_w, spare], axis=0).T
        return one * weights[:, 0:1] + two * weights[:, 1:2], jnp.concatenate([top, sums, spare], axis=0)

    def combine(step):
        member, flip = unpack(step)
        for copy in core_copies(step):
            copy.wait_recv()
        added, figures = merge(
            part[step, core].astype(F32), part_s[step, core], got[step].astype(F32), got_s[step]
        )
        stage_s[step] = figures

        @pl.when(flip > 0)
        def _():
            stage[step] = added.astype(BF16)
            for copy in chip_copies(step):
                copy.start()

        @pl.when(flip == 0)
        def _():
            total[member] = added

    def finish(member):
        added, figures = total[member], stage_s[4 * member + 3]
        for flip in (1, 2, 3):
            for copy in chip_copies(4 * member + 3 - flip):
                copy.wait_recv()
            place = 3 * member + flip - 1
            added, figures = merge(added, figures, arrive[place].astype(F32), arrive_s[place])
        spare = jnp.zeros((7, ROWS), F32)
        inverse = jnp.concatenate([1.0 / figures[1:2], spare], axis=0).T
        att_ref[member] = added * inverse[:, 0:1]
        lse_ref[member] = jnp.concatenate([figures[0:1] + jnp.log2(figures[1:2]), spare], axis=0)

    def step_body(step, carry):
        compute(step, True)

        @pl.when(step > 0)
        def _():
            combine(step - 1)

        return carry

    last = jnp.int32(4 * MB - 1)
    lat_copy(jnp.int32(0)).wait()
    ask(0)
    q_copy(jnp.int32(0)).start()
    lax.fori_loop(0, 4 * MB - 1, step_body, 0)
    compute(last, False)
    combine(last - 1)
    combine(last)
    for member in range(MB):
        finish(member)
    for member in range(MB):
        for copy in kv_copies(member):
            copy.wait()
        for slot in range(4):
            step = 4 * member + slot
            q_copy(step).wait()
            for copy in core_copies(step):
                copy.wait_send()
            if slot < 3:
                for copy in chip_copies(step):
                    copy.wait_send()


def cross_forward(collective_id, *args):
    dma = pltpu.SemaphoreType.DMA
    span = 2 * ROWS
    steps = 4 * MB
    vmem = pl.BlockSpec(memory_space=pltpu.VMEM)
    hbm = pl.BlockSpec(memory_space=pl.ANY)
    return pl.pallas_call(
        cross_forward_kernel,
        in_specs=[hbm, hbm] + [vmem] * 5 + [hbm, hbm, pl.BlockSpec(memory_space=pltpu.SMEM)],
        out_specs=[hbm, hbm, hbm, vmem, vmem],
        out_shape=[
            jax.ShapeDtypeStruct((MB, TOK_DEV, D), BF16),
            jax.ShapeDtypeStruct((MB, TOK_DEV, D), BF16),
            jax.ShapeDtypeStruct((MB, L, D), BF16),
            jax.ShapeDtypeStruct((MB, ROWS, D), F32),
            jax.ShapeDtypeStruct((MB, 8, ROWS), F32),
        ],
        scratch_shapes=[
            pltpu.VMEM((MB, TOK_DEV, D), BF16),
            pltpu.VMEM((steps, span, D), F32),
            pltpu.VMEM((MB, TOK_DEV, D), BF16),
            pltpu.VMEM((MB, TOK_DEV, D), BF16),
            pltpu.VMEM((steps, span, D), BF16),
            pltpu.VMEM((MB, LGROUPS, TOK_DEV), F32),
            pltpu.VMEM((steps, 2, ROWS, D), BF16),
            pltpu.VMEM((steps, 2, 8, ROWS), F32),
            pltpu.VMEM((steps, ROWS, D), BF16),
            pltpu.VMEM((steps, 8, ROWS), F32),
            pltpu.VMEM((steps, ROWS, D), BF16),
            pltpu.VMEM((steps, 8, ROWS), F32),
            pltpu.VMEM((3 * MB, ROWS, D), BF16),
            pltpu.VMEM((3 * MB, 8, ROWS), F32),
            pltpu.VMEM((MB, ROWS, D), F32),
            pltpu.VMEM((MB, TOK_DEV), jnp.int32),
            pltpu.VMEM((MB, SCENES, LGROUPS), jnp.int32),
            dma((2,)), dma((MB,)), dma((steps,)), dma((MB,)), dma((MB,)), dma((steps,)),
        ] + [dma((steps,))] * 4 + [dma((3 * MB,))] * 4,
        compiler_params=pltpu.CompilerParams(
            collective_id=collective_id, has_side_effects=True, vmem_limit_bytes=56 * MIB
        ),
        cost_estimate=pl.CostEstimate(
            flops=14 * 10**9, bytes_accessed=22 * 10**6, transcendentals=4 * 10**6
        ),
        name="cross_forward",
    )(*args)


def cross_backward_kernel(
    items, grad_items,
    tok_ref, tgain_ref, kw_ref, vw_ref, seg_ref, mask_ref, count_ref, k_ref, v_ref, q_ref, up_ref, fig_ref,
    lat_ref, lup_ref, qgain_ref, qw_ref, fgain_ref, mgain_ref, sgain_ref, *refs,
):
    count, more = len(items), len(grad_items)
    parts, sources = refs[:count], refs[count:count + more]
    refs = refs[count + more:]
    dlat_ref, dtok_ref, dkw_ref, dvw_ref, dqw_ref, gains_ref = refs[:6]
    sums, helds = refs[6:6 + count], refs[6 + count:6 + count + more]
    rest = refs[6 + count + more:]
    cut = CROSS_SCRATCH + 3 * count + 2
    grp, grp_devices = grp_steps(items, parts, (), rest[CROSS_SCRATCH:cut], sums)
    tok, near_devices = tok_steps(grad_items, sources, rest[cut:])
    (tok_buf, keys, values, queries, ups, figs, bias, part, got, stage, arrive, far_in, total, dk, dv, dkw, dvw,
     dgain_ref, lat, lup, seg_buf, mask_buf, mask_sem, tail_sem,
     tok_sem, k_sem, v_sem, q_sem, out_sem, near_send, near_recv, far_send, far_recv, on_send, on_recv, own_sem,
     fig_send, fig_recv, core_send, core_recv, chip_send, chip_recv, half_send, half_recv) = rest[:CROSS_SCRATCH]
    me, core, chip, mate, others = places()
    span = 2 * ROWS

    def slot_of(step):
        late = lax.div(step + 3, 8)
        member = jnp.where(step == 1, 1, late)
        flip = jnp.where(step < 2, 0, jnp.where(late == 0, step - 1, 8 - step))
        return member, flip

    def loads(step):
        member, flip = slot_of(step)
        start = pl.multiple_of(chip_at(chip, flip) * span, span)
        ring = lax.rem(step, 4)
        return pltpu.make_async_copy(q_ref.at[member, pl.ds(start, span)], queries.at[ring], q_sem.at[ring])

    def tok_copies(member):
        return (
            pltpu.make_async_copy(k_ref.at[member], keys.at[member], k_sem.at[member]),
            pltpu.make_async_copy(v_ref.at[member], values.at[member], v_sem.at[member]),
            pltpu.make_async_copy(tok_ref.at[0, member], tok_buf.at[member], tok_sem.at[member]),
        )

    def out_copy(member):
        return pltpu.make_async_copy(dk.at[member], dtok_ref.at[0, member], out_sem.at[member])

    def own_copies(member):
        slot = 4 * member
        return (
            pltpu.make_async_copy(up_ref.at[member], ups.at[slot, core], own_sem.at[member, 0]),
            pltpu.make_async_copy(fig_ref.at[member], figs.at[slot, core], own_sem.at[member, 1]),
        )

    def near_copies(member):
        slot = 4 * member
        return [
            remote(up_ref.at[member], ups.at[slot, core], near_send.at[member, 0], near_recv.at[member, 0], mate),
            remote(fig_ref.at[member], figs.at[slot, core], near_send.at[member, 1], near_recv.at[member, 1], mate),
        ]

    half_rows = (pl.ds(0, ROWS // 2), pl.ds(ROWS // 2, ROWS // 2))

    def far_copies(slot):
        member, flip = slot // 4, slot % 4
        peer = 2 * chip_at(chip, flip) + core
        if flip < 3:
            return [
                remote(up_ref.at[member], ups.at[slot, core], far_send.at[slot, 0], far_recv.at[slot, 0], peer),
                remote(fig_ref.at[member], figs.at[slot, core], far_send.at[slot, 1], far_recv.at[slot, 1], peer),
            ]
        copies = []
        for half, (held, toward) in enumerate(((1, 2), (2, 1))):
            copies.append(remote(
                ups.at[4 * member + held, core, half_rows[half]], ups.at[slot, core, half_rows[half]],
                far_send.at[slot, half], far_recv.at[slot, half], 2 * chip_at(chip, toward) + core,
            ))
        copies.append(remote(
            figs.at[4 * member + 1, core], figs.at[slot, core], fig_send.at[member], fig_recv.at[member],
            2 * chip_at(chip, 2) + core,
        ))
        return copies

    def on_copies(slot):
        return (
            remote(ups.at[slot, core], ups.at[slot, core], on_send.at[slot, 0], on_recv.at[slot, 0], mate),
            remote(figs.at[slot, core], figs.at[slot, core], on_send.at[slot, 1], on_recv.at[slot, 1], mate),
        )

    def pass_on(slot):
        for copy in far_copies(slot):
            copy.wait_recv()
        for copy in on_copies(slot):
            copy.start()

    def pass_near(member):
        pass_on(4 * member + 1)
        pass_on(4 * member + 2)
        for copy in far_copies(4 * member + 3):
            copy.start()

    def half_copy(member, half):
        return remote(
            stage.at[4 * member + 3, half_rows[half]], far_in.at[member, half], half_send.at[member, half],
            half_recv.at[member, half], 2 * chip_at(chip, half + 1) + core,
        )

    def half_copies(member):
        return [half_copy(member, half) for half in range(2)]

    def core_copy(step):
        member, flip = slot_of(step)
        slot, ring = 4 * member + flip, lax.rem(step, 4)
        return remote(part.at[ring, 1 - core], got.at[slot], core_send.at[slot], core_recv.at[slot], mate)

    def chip_copy(slot):
        member, flip = slot // 4, slot % 4
        peer = 2 * chip_at(chip, flip) + core
        place = 2 * member + flip - 1
        return remote(stage.at[slot], arrive.at[place], chip_send.at[place], chip_recv.at[place], peer)

    def relay(member):
        for half in range(2):
            half_copy(member, half).wait_recv()
            slot = 4 * member + 2 - half
            joined = stage.at[slot, half_rows[half]]
            add(joined, joined, far_in.at[member, half])
            chip_copy(slot).start()

    masks = mask_loads(seg_ref, mask_ref, seg_buf, mask_buf, mask_sem)
    for copy in masks:
        copy.start()
    own_rows = pl.ds(pl.multiple_of(me * ROWS, ROWS), ROWS)
    tails = (
        pltpu.make_async_copy(lat_ref.at[0, :, own_rows], lat, tail_sem.at[0]),
        pltpu.make_async_copy(lup_ref, lup, tail_sem.at[1]),
    )
    for copy in own_copies(0):
        copy.start()
    for copy in tok_copies(0):
        copy.start()
    for step in range(3):
        loads(jnp.int32(step)).start()
    for copy in own_copies(1):
        copy.start()
    for copy in tok_copies(1):
        copy.start()
    for copy in tails:
        copy.start()
    greet_all([mate] + [2 * other + core for other in others], grp_devices)
    for member in range(MB):
        for copy in near_copies(member):
            copy.start()
    for flip in (1, 2):
        for copy in far_copies(flip):
            copy.start()
    tok[0](0)
    for item in range(count):
        grp[0](item)
    for copy in masks:
        copy.wait()
    mask_rows(seg_buf, mask_buf, count_ref, bias)

    def compute(step):
        member, flip = slot_of(step)
        slot = 4 * member + flip

        @pl.when(step < 2)
        def _():
            for copy in tok_copies(member):
                copy.wait()
            dk[member] = jnp.zeros((TOK_DEV, D), F32)
            dv[member] = jnp.zeros((TOK_DEV, D), F32)

        loads(step).wait()

        @pl.when(step + 3 < 4 * MB)
        def _():
            loads(step + 3).start()

        @pl.when(flip == 0)
        def _():
            for copy in own_copies(member):
                copy.wait()
            for copy in near_copies(member):
                copy.wait_recv()

        @pl.when(flip > 0)
        def _():
            for copy in on_copies(slot):
                copy.wait_recv()

        asked = queries[lax.rem(step, 4)]
        upstream = ups[slot].reshape(span, D)
        scores = nt(asked, keys[member])
        soft = nt(upstream, values[member])
        weights, grads = [], []
        for half in range(2):
            seen = bias[member, pl.ds(2 * chip_at(chip, flip) + half, 1), :]
            figures = figs[slot, half].T
            rows = slice(half * ROWS, (half + 1) * ROWS)
            weight = jnp.exp2(scores[rows] + seen - figures[:, 0:1])
            grads.append((weight * (soft[rows] - figures[:, 1:2])).astype(BF16))
            weights.append(weight.astype(BF16))
        weight = jnp.concatenate(weights, axis=0)
        grad = jnp.concatenate(grads, axis=0)
        middle(step)
        dv[member] += tn(weight, upstream)
        dk[member] += tn(grad, asked)
        asked_grad = (nn(grad, keys[member]) * D ** (-0.5)).astype(BF16)

        @pl.when(step >= 4)
        def _():
            core_copy(step - 4).wait_send()

        for half in range(2):
            part[lax.rem(step, 4), half] = asked_grad[half * ROWS:(half + 1) * ROWS]
        core_copy(step).start()

    def combine(step):
        member, flip = slot_of(step)
        slot = 4 * member + flip
        core_copy(step).wait_recv()
        added = part[lax.rem(step, 4), core].astype(F32) + got[slot].astype(F32)

        @pl.when(flip > 0)
        def _():
            stage[slot] = added.astype(BF16)

        @pl.when(flip == 0)
        def _():
            total[member] = added

    def tokens_back(member, half):
        gain = tgain_ref[...]
        rows = pl.ds(pl.multiple_of(half * span, span), span)
        hat, inverse = norm_parts(tok_buf[member, rows].astype(F32))
        normed = (hat * gain).astype(BF16)
        key_grad = (dk[member, rows] * LN2).astype(BF16)
        value_grad = dv[member, rows].astype(BF16)
        dkw[...] += tn(normed, key_grad)
        dvw[...] += tn(normed, value_grad)
        normed_grad = nt(key_grad, kw_ref[...]) + nt(value_grad, vw_ref[...])
        source_grad, gain_rows = norm_pull(hat, inverse, gain, normed_grad)
        dk[member, rows] = source_grad
        dgain_ref[...] += jnp.sum(gain_rows, axis=0, keepdims=True)

    def hold(item):
        helds[item][...] = tok[4](item).astype(helds[item].dtype)

    def middle(step):
        @pl.when(step > 0)
        def _():
            combine(step - 1)

        @pl.when(step == 1)
        def _():
            pass_near(0)

        @pl.when(step == 3)
        def _():
            pass_on(3)
            pass_near(1)

        @pl.when(step == 5)
        def _():
            for copy in half_copies(0):
                copy.start()

        @pl.when(step == 6)
        def _():
            for copy in half_copies(1):
                copy.start()
            relay(0)

    def step_body(step, carry):
        compute(step)

        @pl.when(step == 0)
        def _():
            for flip in (1, 2):
                for copy in far_copies(4 + flip):
                    copy.start()
            tok[1](0)
            tok[0](1)

        @pl.when(step == 1)
        def _():
            tok[0](2)

        @pl.when(step == 2)
        def _():
            tok[1](1)

        @pl.when(step == 4)
        def _():
            pass_on(7)
            for item in range(count):
                grp[4](item)
            tok[2](0)
            tok[1](2)

        @pl.when(step == 6)
        def _():
            tok[3](0)

        @pl.when(step == 4 * MB - 1)
        def _():
            combine(step)
            relay(1)

        return carry

    lax.fori_loop(0, 4 * MB, step_body, 0)

    def tokens_body(member, carry):
        for half in range(TOK_DEV // span):
            tokens_back(member, half)
        out_copy(member).start()

        @pl.when(member == 0)
        def _():
            helds[1][...] = tok[6](1)

        return carry

    dkw[...] = jnp.zeros_like(dkw)
    dvw[...] = jnp.zeros_like(dvw)
    dgain_ref[...] = jnp.zeros_like(dgain_ref)
    lax.fori_loop(0, MB, tokens_body, 0)
    dkw_ref[...] = dkw[...].astype(BF16)
    dvw_ref[...] = dvw[...].astype(BF16)
    hold(0)
    helds[2][...] = tok[6](2)
    for copy in tails:
        copy.wait()
    gain = qgain_ref[...]
    hat, inverse = norm_parts(lat[...].reshape(MB * ROWS, D))
    normed = (hat * gain).astype(BF16)
    asked_grads = []
    for member in range(MB):
        added = total[member]
        for flip in (1, 2):
            chip_copy(4 * member + flip).wait_recv()
            added = added + arrive[2 * member + flip - 1].astype(F32)
        asked_grads.append(added.astype(BF16))
    asked_grad = jnp.concatenate(asked_grads, axis=0)
    dqw_ref[...] = tn(normed, asked_grad).astype(BF16)
    source_grad, gain_rows = norm_pull(hat, inverse, gain, nt(asked_grad, qw_ref[...]))
    lup[...] += source_grad
    last = pltpu.make_async_copy(lup, dlat_ref, tail_sem.at[2])
    last.start()
    query_gain = jnp.sum(gain_rows, axis=0, keepdims=True)
    rows = jnp.concatenate(
        [dgain_ref[...], query_gain, fgain_ref[...], mgain_ref[...], sgain_ref[...], jnp.zeros((3, D), F32)], axis=0
    )
    gains_ref[...] = jnp.zeros_like(gains_ref)
    width = D // TOK
    for device in range(TOK):
        gains_ref[16 * device:16 * device + 8, 0:width] = rows[:, device * width:(device + 1) * width]
    grp[3]((0,))
    tok[5]((1, 2))
    last.wait()
    for step in range(4, 4 * MB):
        core_copy(jnp.int32(step)).wait_send()
    for member in range(MB):
        out_copy(member).wait()
        for copy in near_copies(member) + half_copies(member):
            copy.wait_send()
        for flip in range(4):
            slot = 4 * member + flip
            if flip > 0:
                for copy in far_copies(slot):
                    copy.wait_send()
                for copy in on_copies(slot):
                    copy.wait_send()
            if flip in (1, 2):
                chip_copy(slot).wait_send()


CROSS_SCRATCH = 44


def cross_backward(collective_id, arrays, grads, *args):
    dma = pltpu.SemaphoreType.DMA
    span = 2 * ROWS
    steps = 4 * MB
    vmem = pl.BlockSpec(memory_space=pltpu.VMEM)
    hbm = pl.BlockSpec(memory_space=pl.ANY)
    smem = pl.BlockSpec(memory_space=pltpu.SMEM)
    items, kinds = held_plan(arrays)
    sources, grad_items, grad_kinds, shapes = reduce_plan(grads)
    scratch = [
        pltpu.VMEM((MB, TOK_DEV, D), BF16),
        pltpu.VMEM((MB, TOK_DEV, D), BF16),
        pltpu.VMEM((MB, TOK_DEV, D), BF16),
        pltpu.VMEM((4, span, D), BF16),
        pltpu.VMEM((steps, 2, ROWS, D), BF16),
        pltpu.VMEM((steps, 2, 8, ROWS), F32),
        pltpu.VMEM((MB, LGROUPS, TOK_DEV), F32),
        pltpu.VMEM((4, 2, ROWS, D), BF16),
        pltpu.VMEM((steps, ROWS, D), BF16),
        pltpu.VMEM((steps, ROWS, D), BF16),
        pltpu.VMEM((2 * MB, ROWS, D), BF16),
        pltpu.VMEM((MB, 2, ROWS // 2, D), BF16),
        pltpu.VMEM((MB, ROWS, D), F32),
        pltpu.VMEM((MB, TOK_DEV, D), F32),
        pltpu.VMEM((MB, TOK_DEV, D), F32),
        pltpu.VMEM((D, D), F32),
        pltpu.VMEM((D, D), F32),
        pltpu.VMEM((1, D), F32),
        pltpu.VMEM((MB, ROWS, D), F32),
        pltpu.VMEM((MB * ROWS, D), F32),
        pltpu.VMEM((MB, TOK_DEV), jnp.int32),
        pltpu.VMEM((MB, SCENES, LGROUPS), jnp.int32),
        dma((2,)), dma((3,)),
        dma((MB,)), dma((MB,)), dma((MB,)), dma((4,)), dma((MB,)),
        dma((MB, 2)), dma((MB, 2)), dma((steps, 2)), dma((steps, 2)), dma((steps, 2)), dma((steps, 2)), dma((MB, 2)),
        dma((MB,)), dma((MB,)),
        dma((steps,)), dma((steps,)), dma((2 * MB,)), dma((2 * MB,)), dma((MB, 2)), dma((MB, 2)),
    ]
    return pl.pallas_call(
        functools.partial(cross_backward_kernel, items, grad_items),
        in_specs=[hbm] + [vmem] * 3 + [hbm, hbm, smem] + [hbm] * 7 + [vmem] * 5 + [vmem] * len(arrays) + [hbm] * len(grads),
        out_specs=[hbm, hbm] + [vmem] * (4 + len(arrays) + len(grads)),
        out_shape=[
            jax.ShapeDtypeStruct((MB * ROWS, D), F32),
            jax.ShapeDtypeStruct((1, MB, TOK_DEV, D), F32),
            jax.ShapeDtypeStruct((D, D), BF16),
            jax.ShapeDtypeStruct((D, D), BF16),
            jax.ShapeDtypeStruct((D, D), BF16),
            jax.ShapeDtypeStruct((16 * TOK, 128), F32),
        ] + [jax.ShapeDtypeStruct(array.shape, array.dtype) for array in arrays]
        + [
            jax.ShapeDtypeStruct((() if i == 0 else (2, 2)) + (high // 2, wide), kind)
            for i, ((high, wide), kind) in enumerate(zip(shapes, grad_kinds))
        ],
        scratch_shapes=scratch + grp_scratch(items, kinds) + tok_scratch(grad_items, grad_kinds),
        compiler_params=pltpu.CompilerParams(
            collective_id=collective_id, has_side_effects=True, vmem_limit_bytes=60 * MIB
        ),
        cost_estimate=pl.CostEstimate(
            flops=26 * 10**9, bytes_accessed=24 * 10**6, transcendentals=4 * 10**6
        ),
        name="cross_backward",
    )(*args, *arrays, *sources)


GELU_A = 0.7978845608028654
GELU_B = 0.044715


def gelu_parts(hidden):
    square = hidden * hidden
    bent = jnp.tanh(GELU_A * hidden * (1.0 + GELU_B * square))
    half = 0.5 * (1.0 + bent)
    slope = half + 0.5 * hidden * (1.0 - bent * bent) * (GELU_A * (1.0 + 3.0 * GELU_B * square))
    return hidden * half, slope


def greet_all(tok_devices, grp_devices=()):
    barrier = pltpu.get_barrier_semaphore()
    for axis, devices in (("tok", tok_devices), ("grp", grp_devices)):
        for device in devices:
            pl.semaphore_signal(
                barrier, inc=1, device_id={axis: device}, device_id_type=pl.DeviceIdType.MESH
            )
    pl.semaphore_wait(barrier, len(tok_devices) + len(grp_devices))


def all_peers():
    me, core, chip, mate, others = places()
    peers = []
    for other in others:
        peers += [2 * other + core, 2 * other + 1 - core]
    return me, peers + [mate]


def head_copies(row_side, head_side, to_heads, member, me, peers, send, recv, local):
    lanes = pl.ds(member * ROWS, ROWS)
    row_at = lambda device: row_side.at[:, device, :, lanes]
    head_at = lambda device: head_side.at[:, member, :, pl.ds(pl.multiple_of(device * ROWS, ROWS), ROWS)]
    source, target = (row_at, head_at) if to_heads else (head_at, row_at)
    copies = [
        remote(source(peer), target(me), send.at[slot, member], recv.at[slot, member], peer)
        for slot, peer in enumerate(peers)
    ]
    return copies, pltpu.make_async_copy(source(me), target(me), local.at[member])


QB = 1024
QB_BACK = 256


def latents_forward_kernel(
    lat_ref, att_ref, cot_ref, ow_ref, fgain_ref, fup_ref, fdown_ref, mgain_ref, proj_ref, mow_ref, sgain_ref,
    sup_ref, sdown_ref,
    out_ref, fmid_ref, mmid_ref, packed_ref, exact_ref, lse_ref, up_ref, mgrad_ref, ddown_ref, dup_ref, dmo_ref,
    dgain_ref,
    lat, att, cot, ow, fup, fdown, proj, mow, sup, sdown,
    out, fmid, mmid, heads, exact, up, mgrad, ddown, dup, dmo,
    rows_out, keys, values, mixed, mixed_rows, active, hidden_low, normed_low,
    load_sem, store_sem, send_a, recv_a, local_a, send_b, recv_b, local_b,
):
    me, peers = all_peers()
    own = pl.ds(pl.multiple_of(me * ROWS, ROWS), ROWS)
    names = ("lat", "att", "ow", "fup", "fdown", "proj", "mow", "sup", "sdown", "cot")
    loads = {}
    for i, (source, target) in enumerate((
        (lat_ref.at[0, :, own], lat), (att_ref, att), (ow_ref, ow), (fup_ref, fup), (fdown_ref, fdown),
        (proj_ref, proj), (mow_ref, mow), (sup_ref, sup), (sdown_ref, sdown), (cot_ref.at[0], cot),
    )):
        loads[names[i]] = pltpu.make_async_copy(source, target, load_sem.at[i])
        loads[names[i]].start()
    stores = []

    def store(source, target):
        stores.append(pltpu.make_async_copy(source, target, store_sem.at[len(stores)]))
        stores[-1].start()

    greet_all(peers)
    flat = (MB * ROWS, D)
    for name in ("lat", "att", "ow"):
        loads[name].wait()
    outward = [head_copies(rows_out, heads, True, member, me, peers, send_a, recv_a, local_a) for member in range(MB)]
    backward = [
        head_copies(mixed_rows, mixed, False, member, me, peers, send_b, recv_b, local_b) for member in range(MB)
    ]
    for member in range(MB):
        rows = slice(member * ROWS, (member + 1) * ROWS)
        first = lat[member] + nn(att[member].astype(BF16), ow[...])
        fmid[rows] = first
        normed = (norm_parts(first)[0] * fgain_ref[...]).astype(BF16)
        if member == 0:
            loads["fup"].wait()
            loads["fdown"].wait()
        mid = first
        for part in range(2):
            cut = slice(part * FF // 2, (part + 1) * FF // 2)
            mid = mid + nn(jax.nn.gelu(nn(normed, fup[:, cut])).astype(BF16), fdown[cut])
        mmid[rows] = mid
        normed = (norm_parts(mid)[0] * mgain_ref[...]).astype(BF16).T
        if member == 0:
            loads["proj"].wait()
        for kind, scale in enumerate((HD ** (-0.5) * LOG2E, 1.0, 1.0)):
            packed = tn(proj[:, kind * D:(kind + 1) * D], normed) * scale
            rows_out[kind, :, :, rows] = packed.astype(BF16).reshape(H, HD, ROWS)
        copies, here = outward[member]
        for copy in copies:
            copy.start()
        here.start()
    store(fmid, fmid_ref)
    store(mmid, mmid_ref)
    for member in range(MB):
        copies, here = outward[member]
        for copy in copies:
            copy.wait_recv()
        here.wait()
        store(heads.at[:, member], packed_ref.at[:, member])
        keys[...] = heads[1, member].T
        values[0:HD] = heads[2, member]
        values[HD:] = jnp.ones((16, L), BF16)

        def attend(step, carry, member=member):
            at = pl.ds(pl.multiple_of(step * QB, QB), QB)
            logits = nn(keys[...], heads[0, member, :, at])
            top = jnp.max(logits, axis=0, keepdims=True)
            both = nn(values[...], jnp.exp2(logits - top).astype(BF16))
            total = both[HD:HD + 1]
            result = both[0:HD] / total
            exact[member, :, at] = result
            mixed[0, member, :, at] = result.astype(BF16)
            lse_ref[member, :, at] = jnp.broadcast_to(top + jnp.log2(total), (8, QB))
            return carry

        lax.fori_loop(0, L // QB, attend, 0)
        for copy in backward[member][0] + [backward[member][1]]:
            copy.start()
    store(exact, exact_ref)
    loads["mow"].wait()
    loads["sup"].wait()
    loads["sdown"].wait()
    loads["cot"].wait()
    gains = []
    for member in range(MB):
        copies, here = backward[member]
        for copy in copies:
            copy.wait_recv()
        here.wait()
        rows = slice(member * ROWS, (member + 1) * ROWS)
        second = mmid[rows] + tn(mixed_rows[0, :, :, rows].reshape(D, ROWS), mow[...])
        hat, inverse = norm_parts(second)
        normed = (hat * sgain_ref[...]).astype(BF16)
        normed_low[rows] = normed
        upstream = cot[member]
        grad = upstream.astype(BF16)
        final = second
        normed_grad = jnp.zeros((ROWS, D), F32)
        for part in range(2):
            cut = slice(part * FF // 2, (part + 1) * FF // 2)
            act, slope = gelu_parts(nn(normed, sup[:, cut]))
            act = act.astype(BF16)
            active[rows, cut] = act
            final = final + nn(act, sdown[cut])
            hidden_grad = (slope * nt(grad, sdown[cut])).astype(BF16)
            hidden_low[rows, cut] = hidden_grad
            normed_grad = normed_grad + nt(hidden_grad, sup[:, cut])
        out[member] = final
        residual, gain_rows = norm_pull(hat, inverse, sgain_ref[...], normed_grad)
        gains.append(jnp.sum(gain_rows, axis=0, keepdims=True))
        upstream = upstream + residual
        up[rows] = upstream
        mgrad[0, :, :, rows] = nt(mow[...], upstream.astype(BF16)).astype(BF16).reshape(H, HD, ROWS)
    store(out, out_ref.at[0])
    store(up, up_ref)
    store(mgrad, mgrad_ref)
    dgain_ref[...] = gains[0] + gains[1]
    ddown[...] = tn(active[...], cot[...].reshape(flat).astype(BF16)).astype(BF16)
    store(ddown, ddown_ref)
    dup[...] = tn(normed_low[...], hidden_low[...]).astype(BF16)
    store(dup, dup_ref)
    dmo[...] = nn(mixed_rows[0].reshape(D, MB * ROWS), up[...].astype(BF16)).astype(BF16)
    store(dmo, dmo_ref)
    for copy in stores:
        copy.wait()
    for copies, here in outward + backward:
        for copy in copies:
            copy.wait_send()


def latents_forward(collective_id, *args):
    dma = pltpu.SemaphoreType.DMA
    vmem = pl.BlockSpec(memory_space=pltpu.VMEM)
    hbm = pl.BlockSpec(memory_space=pl.ANY)
    rows = MB * ROWS
    stored = [
        ((1, MB, ROWS, D), F32), ((rows, D), F32), ((rows, D), F32), ((3, MB, HD, L), BF16), ((MB, HD, L), F32),
        ((MB, 8, L), F32), ((rows, D), F32), ((1, H, HD, rows), BF16), ((FF, D), BF16), ((D, FF), BF16), ((D, D), BF16),
        ((1, D), F32),
    ]
    return pl.pallas_call(
        latents_forward_kernel,
        in_specs=[hbm, hbm, hbm, hbm, vmem, hbm, hbm, vmem, hbm, hbm, vmem, hbm, hbm],
        out_specs=[hbm] * 5 + [vmem] + [hbm] * 5 + [vmem],
        out_shape=[jax.ShapeDtypeStruct(shape, kind) for shape, kind in stored],
        scratch_shapes=[
            pltpu.VMEM((MB, ROWS, D), F32), pltpu.VMEM((MB, ROWS, D), F32), pltpu.VMEM((MB, ROWS, D), F32),
            pltpu.VMEM((D, D), BF16), pltpu.VMEM((D, FF), BF16), pltpu.VMEM((FF, D), BF16),
            pltpu.VMEM((D, 3 * D), BF16), pltpu.VMEM((D, D), BF16), pltpu.VMEM((D, FF), BF16),
            pltpu.VMEM((FF, D), BF16),
            pltpu.VMEM((MB, ROWS, D), F32), pltpu.VMEM((rows, D), F32), pltpu.VMEM((rows, D), F32),
            pltpu.VMEM((3, MB, HD, L), BF16), pltpu.VMEM((MB, HD, L), F32), pltpu.VMEM((rows, D), F32),
            pltpu.VMEM((1, H, HD, rows), BF16), pltpu.VMEM((FF, D), BF16), pltpu.VMEM((D, FF), BF16),
            pltpu.VMEM((D, D), BF16),
            pltpu.VMEM((3, H, HD, rows), BF16), pltpu.VMEM((L, HD), BF16), pltpu.VMEM((HD + 16, L), BF16),
            pltpu.VMEM((1, MB, HD, L), BF16), pltpu.VMEM((1, H, HD, rows), BF16),
            pltpu.VMEM((rows, FF), BF16), pltpu.VMEM((rows, FF), BF16), pltpu.VMEM((rows, D), BF16),
            dma((10,)), dma((11,)), dma((7, MB)), dma((7, MB)), dma((MB,)), dma((7, MB)), dma((7, MB)), dma((MB,)),
        ],
        compiler_params=pltpu.CompilerParams(
            collective_id=collective_id, has_side_effects=True, vmem_limit_bytes=60 * MIB
        ),
        cost_estimate=pl.CostEstimate(
            flops=20 * 10**9, bytes_accessed=30 * 10**6, transcendentals=10 * 10**6
        ),
        name="latents_forward",
    )(*args)


def levels():
    level = lax.axis_index("grp")
    odd = lax.rem(level, 2)
    return odd, level + 1 - 2 * odd, lax.rem(level + 2, 4)


def half_slices(rows, odd):
    half = rows // 2
    keep = pl.ds(pl.multiple_of(odd * half, half), half)
    away = pl.ds(pl.multiple_of((1 - odd) * half, half), half)
    return keep, away


def tok_steps(items, sources, scratch):
    n = len(items)
    mine, got, near_in, first_in, second_in = [scratch[i * n:(i + 1) * n] for i in range(5)]
    (local_sem, core_send, core_recv, near_send, near_recv, one_send, one_recv, two_send, two_recv) = scratch[5 * n:]
    me, core, chip, mate, (far, flip_x, flip_y) = places()
    x, y = lax.rem(chip, 2), lax.div(chip, 2)
    odd, level_near, level_far = levels()

    def core_copies(i):
        source, rows, row_at, columns, column_at, x_first = items[i]
        part = (pl.ds(row_at, rows), pl.ds(column_at, columns))
        return (
            remote(sources[source].at[:, :, 1 - core, *part], got[i], core_send.at[i], core_recv.at[i], mate),
            pltpu.make_async_copy(sources[source].at[:, :, core, *part], mine[i], local_sem.at[i]),
        )

    def near_copy(i):
        keep, away = half_slices(items[i][1], odd)
        return pltpu.make_async_remote_copy(
            src_ref=mine[i].at[:, :, away], dst_ref=near_in[i], send_sem=near_send.at[i], recv_sem=near_recv.at[i],
            device_id={"grp": level_near}, device_id_type=pl.DeviceIdType.MESH,
        )

    def first_copy(i):
        keep, away = half_slices(items[i][1], odd)
        x_first = items[i][-1]
        source = mine[i].at[:, 1 - x, keep] if x_first else mine[i].at[1 - y, :, keep]
        peer = 2 * (flip_x if x_first else flip_y) + core
        return remote(source, first_in[i], one_send.at[i], one_recv.at[i], peer)

    def second_copy(i):
        keep, away = half_slices(items[i][1], odd)
        x_first = items[i][-1]
        source = mine[i].at[1 - y, x, keep] if x_first else mine[i].at[y, 1 - x, keep]
        peer = 2 * (flip_y if x_first else flip_x) + core
        return remote(source, second_in[i], two_send.at[i], two_recv.at[i], peer)

    def core_sends(i):
        for copy in core_copies(i):
            copy.start()

    def core_sums(i):
        there, here = core_copies(i)
        there.wait_recv()
        here.wait()
        add(mine[i], mine[i], got[i])
        near_copy(i).start()

    def near_sums(i):
        keep, away = half_slices(items[i][1], odd)
        near_copy(i).wait_recv()
        held = mine[i].at[:, :, keep]
        add(held, held, near_in[i])
        first_copy(i).start()

    def first_sums(i):
        keep, away = half_slices(items[i][1], odd)
        first_copy(i).wait_recv()
        held = mine[i].at[:, x, keep] if items[i][-1] else mine[i].at[y, :, keep]
        add(held, held, first_in[i])
        second_copy(i).start()

    def second_sums(i):
        keep, away = half_slices(items[i][1], odd)
        second_copy(i).wait_recv()
        return mine[i][y, x, keep].astype(F32) + second_in[i][...].astype(F32)

    def near_hold(i):
        keep, away = half_slices(items[i][1], odd)
        near_copy(i).wait_recv()
        return mine[i][:, :, keep] + near_in[i][...]

    def finish(near_only=()):
        for i in range(n):
            core_copies(i)[0].wait_send()
            near_copy(i).wait_send()
            if i not in near_only:
                for copy in (first_copy(i), second_copy(i)):
                    copy.wait_send()

    return (core_sends, core_sums, near_sums, first_sums, second_sums, finish, near_hold), (
        mate, 2 * flip_x + core, 2 * flip_y + core)


def quad_steps(items, quads, results, scratch):
    n = len(items)
    first_in, joined, second_in = [scratch[i * n:(i + 1) * n] for i in range(3)]
    one_send, one_recv, two_send, two_recv = scratch[3 * n:]
    me, core, chip, mate, (far, flip_x, flip_y) = places()
    x, y = lax.rem(chip, 2), lax.div(chip, 2)

    def first_copy(i):
        x_first = items[i][-1]
        source = quads[i].at[:, 1 - x] if x_first else quads[i].at[1 - y]
        peer = 2 * (flip_x if x_first else flip_y) + core
        return remote(source, first_in[i], one_send.at[i], one_recv.at[i], peer)

    def second_copy(i):
        x_first = items[i][-1]
        source = joined[i].at[1 - y] if x_first else joined[i].at[1 - x]
        peer = 2 * (flip_y if x_first else flip_x) + core
        return remote(source, second_in[i], two_send.at[i], two_recv.at[i], peer)

    def first_start(i):
        first_copy(i).start()

    def first_sums(i):
        first_copy(i).wait_recv()
        add(joined[i], quads[i].at[:, x] if items[i][-1] else quads[i].at[y], first_in[i])
        second_copy(i).start()

    def second_sums(i):
        second_copy(i).wait_recv()
        add(results[i], joined[i].at[y] if items[i][-1] else joined[i].at[x], second_in[i])

    def finish():
        for i in range(n):
            for copy in (first_copy(i), second_copy(i)):
                copy.wait_send()

    return first_start, first_sums, second_sums, finish


def plain_steps(items, sources, scratch):
    n = len(items)
    mine, got, near_in, first_in, second_in = [scratch[i * n:(i + 1) * n] for i in range(5)]
    (local_sem, core_send, core_recv, near_send, near_recv, one_send, one_recv, two_send, two_recv) = scratch[5 * n:]
    me, core, chip, mate, (far, flip_x, flip_y) = places()
    x, y = lax.rem(chip, 2), lax.div(chip, 2)
    odd, level_near, level_far = levels()

    def core_copy(i):
        return remote(sources[i].at[:, :, 1 - core], got[i], core_send.at[i], core_recv.at[i], mate)

    def local_copy(i):
        return pltpu.make_async_copy(sources[i].at[:, :, core], mine[i], local_sem.at[i])

    def first_copy(i):
        x_first = items[i][-1]
        source = mine[i].at[:, 1 - x] if x_first else mine[i].at[1 - y]
        peer = 2 * (flip_x if x_first else flip_y) + core
        return remote(source, first_in[i], one_send.at[i], one_recv.at[i], peer)

    def second_copy(i):
        x_first = items[i][-1]
        source = mine[i].at[1 - y, x] if x_first else mine[i].at[y, 1 - x]
        peer = 2 * (flip_y if x_first else flip_x) + core
        return remote(source, second_in[i], two_send.at[i], two_recv.at[i], peer)

    def near_copy(i):
        keep, away = half_slices(items[i][1], odd)
        return pltpu.make_async_remote_copy(
            src_ref=mine[i].at[y, x, away], dst_ref=near_in[i], send_sem=near_send.at[i], recv_sem=near_recv.at[i],
            device_id={"grp": level_near}, device_id_type=pl.DeviceIdType.MESH,
        )

    def core_sends(i):
        core_copy(i).start()
        local_copy(i).start()

    def core_sums(i):
        core_copy(i).wait_recv()
        local_copy(i).wait()
        add(mine[i], mine[i], got[i])
        first_copy(i).start()

    def first_sums(i):
        first_copy(i).wait_recv()
        held = mine[i].at[:, x] if items[i][-1] else mine[i].at[y]
        add(held, held, first_in[i])
        second_copy(i).start()

    def second_sums(i):
        second_copy(i).wait_recv()
        held = mine[i].at[y, x]
        add(held, held, second_in[i])
        near_copy(i).start()

    def near_sums(i):
        keep, away = half_slices(items[i][1], odd)
        near_copy(i).wait_recv()
        return mine[i][y, x, keep].astype(F32) + near_in[i][...].astype(F32)

    def finish():
        for i in range(n):
            for copy in (core_copy(i), near_copy(i), first_copy(i), second_copy(i)):
                copy.wait_send()

    return (core_sends, core_sums, first_sums, second_sums, near_sums, finish), (
        mate, 2 * flip_x + core, 2 * flip_y + core)


def grp_steps(items, held, outs, scratch, joined=None):
    n = len(items)
    far_in, own_joined, near_in = [scratch[i * n:(i + 1) * n] for i in range(3)]
    z_send, z_recv = scratch[3 * n:]
    joined = own_joined if joined is None else joined
    odd, level_near, level_far = levels()

    def along(i, step):
        source, target, other = (
            (held[i], far_in[i], level_far),
            (joined[i], near_in[i], level_near),
        )[step]
        return pltpu.make_async_remote_copy(
            src_ref=source, dst_ref=target, send_sem=z_send.at[i, step], recv_sem=z_recv.at[i, step],
            device_id={"grp": other}, device_id_type=pl.DeviceIdType.MESH,
        )

    def store(i, odd_half, value):
        source, rows, row_at, columns, column_at, x_first = items[i]
        half = rows // 2
        start = pl.multiple_of(row_at + odd_half * half, half)
        outs[source][pl.ds(start, half), pl.ds(column_at, columns)] = value.astype(F32)

    def far_start(i):
        along(i, 0).start()

    def far_join(i):
        along(i, 0).wait_recv()
        add(joined[i], held[i], far_in[i])

    def near_start(i):
        along(i, 1).start()
        store(i, odd, joined[i][...])

    def far_sum(i):
        far_join(i)
        near_start(i)

    def near_store(i):
        along(i, 1).wait_recv()
        store(i, 1 - odd, near_in[i][...])

    def finish(steps=(0, 1)):
        for i in range(n):
            for step in steps:
                along(i, step).wait_send()

    return (far_start, far_sum, near_store, finish, far_join, near_start), (level_near, level_far)


def add(target, one, two):
    target[...] = one[...] + two[...]


def reduce_kernel(items, whole, square, joined, count, *refs):
    n, m, q, k = len(items), len(whole), len(square), len(joined)

    def take(length):
        nonlocal refs
        head, refs = refs[:length], refs[length:]
        return head

    sources, held, quads, done = take(count), take(m), take(q), take(k)
    outs, whole_outs, quad_outs, joined_outs = take(count), take(m), take(q), take(k)
    tok, near_devices = plain_steps(items, sources, take(5 * n + 9))
    own_held = take(n)
    late, grp_devices = grp_steps(items, own_held, outs, take(3 * n + 2))
    early, unused = grp_steps(whole, held, whole_outs, take(3 * m + 2))
    quad_held = take(q)
    sums = quad_steps(square, quads, quad_held, take(3 * q + 4))
    mid, unused = grp_steps(square, quad_held, quad_outs, take(3 * q + 2))
    first, unused = grp_steps(joined, done, joined_outs, refs, done)
    greet_all(near_devices, grp_devices)
    for i in range(n):
        tok[0](i)
    for i in range(m):
        early[0](i)
    for i in range(q):
        sums[0](i)
    for i in range(n):
        tok[1](i)
    for i in range(k):
        first[5](i)
    for i in range(q):
        sums[1](i)
    for i in range(n):
        tok[2](i)
    for i in range(q):
        sums[2](i)
        mid[0](i)
    for i in range(n):
        tok[3](i)
    for i in range(n):
        own_held[i][...] = tok[4](i).astype(own_held[i].dtype)
        late[0](i)
    for i in range(m):
        early[1](i)
    for i in range(k):
        first[2](i)
    for i in range(q):
        mid[1](i)
    for i in range(n):
        late[1](i)
    for i in range(m):
        early[2](i)
    for i in range(q):
        mid[2](i)
    for i in range(n):
        late[2](i)
    tok[-1]()
    sums[-1]()
    late[3]()
    early[3]()
    mid[3]()
    first[3]((1,))


def reduce_plan(arrays):
    sources, items = [], []
    for source, array in enumerate(arrays):
        rows, columns = array.shape[0] // TOK, array.shape[1]
        sources.append(array.reshape(2, 2, 2, rows, columns))
        items.append((source, rows, 0, columns, 0, source % 2 == 0))
    kinds = [array.dtype for array in arrays]
    shapes = [(array.shape[0] // TOK, array.shape[1]) for array in arrays]
    return sources, tuple(items), kinds, shapes


def held_plan(arrays):
    items = tuple((i, 2 * array.shape[0], 0, array.shape[1], 0, True) for i, array in enumerate(arrays))
    return items, [array.dtype for array in arrays]


def item_blocks(items, kinds, lead, part):
    return [pltpu.VMEM(lead + (item[1] // part, item[3]), kind) for item, kind in zip(items, kinds)]


def quad_plan(arrays, x_firsts):
    items = tuple(
        (i, 2 * array.shape[2], 0, array.shape[3], 0, x_first) for i, (array, x_first) in enumerate(zip(arrays, x_firsts))
    )
    return items, [array.dtype for array in arrays]


def quad_scratch(items, kinds):
    blocks = functools.partial(item_blocks, items, kinds)
    return blocks((2,), 2) + blocks((2,), 2) + blocks((), 2) + [pltpu.SemaphoreType.DMA((len(items),))] * 4


def plain_scratch(items, kinds):
    blocks = functools.partial(item_blocks, items, kinds)
    return (blocks((2, 2), 1) + blocks((2, 2), 1) + blocks((), 2) + blocks((2,), 1) + blocks((), 1)
            + [pltpu.SemaphoreType.DMA((len(items),))] * 9)


def tok_scratch(items, kinds):
    blocks = functools.partial(item_blocks, items, kinds)
    return (blocks((2, 2), 1) + blocks((2, 2), 1) + blocks((2, 2), 2) + blocks((2,), 2) + blocks((), 2)
            + [pltpu.SemaphoreType.DMA((len(items),))] * 9)


def grp_scratch(items, kinds):
    blocks = functools.partial(item_blocks, items, kinds)
    return blocks((), 2) * 3 + [pltpu.SemaphoreType.DMA((len(items), 2))] * 2


def reduce_grads(collective_id, arrays, held, quads, x_firsts, done):
    sources, items, kinds, shapes = reduce_plan(arrays)
    whole, whole_kinds = held_plan(held)
    square, square_kinds = quad_plan(quads, x_firsts)
    joined, joined_kinds = held_plan(done)
    vmem = pl.BlockSpec(memory_space=pltpu.VMEM)
    hbm = pl.BlockSpec(memory_space=pl.ANY)
    rest = len(held) + len(quads) + len(done)
    return pl.pallas_call(
        functools.partial(reduce_kernel, items, whole, square, joined, len(arrays)),
        in_specs=[hbm] * len(arrays) + [vmem] * rest,
        out_specs=[vmem] * (len(arrays) + rest),
        out_shape=[jax.ShapeDtypeStruct(shape, F32) for shape in shapes]
        + [jax.ShapeDtypeStruct((item[1], item[3]), F32) for item in whole + square + joined],
        scratch_shapes=plain_scratch(items, kinds) + item_blocks(items, kinds, (), 2) + grp_scratch(items, kinds)
        + grp_scratch(whole, whole_kinds) + item_blocks(square, square_kinds, (), 2)
        + quad_scratch(square, square_kinds) + grp_scratch(square, square_kinds) + grp_scratch(joined, joined_kinds),
        compiler_params=pltpu.CompilerParams(
            collective_id=collective_id, has_side_effects=True, vmem_limit_bytes=48 * MIB
        ),
        name="reduce_grads",
    )(*sources, *held, *quads, *done)


def write_kernel(count, large, *refs):
    sources, gain_ref, outs = refs[:count], refs[count], refs[count + 1:2 * count + 1]
    gain_outs, buffers = refs[2 * count + 1:-large - 2], refs[-large - 2:-2]
    in_sem, out_sem = refs[-2:]
    ins = [pltpu.make_async_copy(sources[i], buffers[i], in_sem.at[i]) for i in range(large)]
    held = buffers + sources[large:]
    backs = [pltpu.make_async_copy(held[i], outs[i], out_sem.at[i]) for i in range(count)]
    for copy in ins + backs[large:]:
        copy.start()
    for i, out in enumerate(gain_outs):
        out[...] = gain_ref[i:i + 1, 0:D // TOK]
    for i in range(large):
        ins[i].wait()
        backs[i].start()
    for copy in backs:
        copy.wait()


def write_results(results, gains, gain_count):
    n = len(results)
    large = sum(result.ndim == 4 for result in results)
    hbm, vmem = pl.BlockSpec(memory_space=pl.ANY), pl.BlockSpec(memory_space=pltpu.VMEM)
    return pl.pallas_call(
        functools.partial(write_kernel, n, large),
        in_specs=[hbm] * large + [vmem] * (n - large + 1),
        out_specs=[hbm] * n + [vmem] * gain_count,
        out_shape=[jax.ShapeDtypeStruct(result.shape, result.dtype) for result in results]
        + [jax.ShapeDtypeStruct((1, D // TOK), F32)] * gain_count,
        scratch_shapes=[pltpu.VMEM(result.shape, result.dtype) for result in results[:large]]
        + [pltpu.SemaphoreType.DMA((large,)), pltpu.SemaphoreType.DMA((n,))],
        compiler_params=pltpu.CompilerParams(vmem_limit_bytes=56 * MIB),
        name="write_results",
    )(*results, gains)


def latents_backward_kernel(items, *refs):
    (mgrad_ref, packed_ref, exact_ref, lse_ref, up_ref, mmid_ref, fmid_ref, att_ref, clse_ref, ow_ref, fgain_ref,
     fup_ref, fdown_ref, mgain_ref, proj_ref) = refs[:15]
    count = max(item[0] for item in items) + 1
    sources = refs[15:15 + count]
    (agrad_ref, fig_ref, lup_ref, dup_ref, ddown_ref, dproj_ref, dout_ref, dmgain_ref, dfgain_ref) = refs[
        15 + count:24 + count]
    reduced = refs[24 + count:24 + 2 * count]
    rest = refs[24 + 2 * count:]
    (heads, exact, ups, mmid, fmid, att, ow, fup, fdown, proj, keys, values, upstream_heads, key_acc, value_acc,
     grads, back, agrad, lup, dup, ddown, dproj, dout, hidden, active, hidden_low, grad_low,
     load_sem, store_sem, send_a, recv_a, local_a, send_b, recv_b, local_b) = rest[:35]
    me, peers = all_peers()
    reducer, near_devices = tok_steps(items, sources, rest[35:])
    core_sends, core_sums, near_sums, first_sums, second_sums, finish = reducer[:6]
    odd, level_near, level_far = levels()

    def hold(item):
        reduced[item][...] = second_sums(item).astype(reduced[item].dtype)

    names = ("heads", "exact", "fmid", "fup", "up", "mmid", "proj", "fdown", "att", "ow")
    loads = {}
    for i, (source, target) in enumerate((
        (packed_ref, heads), (exact_ref, exact), (fmid_ref, fmid), (fup_ref, fup), (up_ref, ups), (mmid_ref, mmid),
        (proj_ref, proj), (fdown_ref, fdown), (att_ref, att), (ow_ref, ow),
    )):
        loads[names[i]] = pltpu.make_async_copy(source, target, load_sem.at[i])
        loads[names[i]].start()
    stores = []

    def store(source, target):
        stores.append(pltpu.make_async_copy(source, target, store_sem.at[len(stores)]))
        stores[-1].start()

    greet_all(peers, (level_near,))
    outward = [
        head_copies(mgrad_ref, upstream_heads, True, member, me, peers, send_a, recv_a, local_a) for member in range(MB)
    ]
    backward = [head_copies(back, grads, False, member, me, peers, send_b, recv_b, local_b) for member in range(MB)]
    for copies, here in outward:
        for copy in copies:
            copy.start()
        here.start()
    core_sends(0)
    loads["fmid"].wait()
    loads["fup"].wait()
    first_hat, first_inverse = norm_parts(fmid[...])
    first_normed = (first_hat * fgain_ref[...]).astype(BF16)
    hidden[...] = nn(first_normed, fup[...])
    core_sums(0)
    loads["heads"].wait()
    loads["exact"].wait()
    for member in range(MB):
        keys[...] = heads[1, member].T
        values[...] = heads[2, member].T
        key_acc[...] = jnp.zeros_like(key_acc)
        value_acc[...] = jnp.zeros_like(value_acc)
        copies, here = outward[member]
        for copy in copies:
            copy.wait_recv()
        here.wait()
        if member == 0:
            core_sends(1)
            core_sends(2)

        def attend_back(step, carry, member=member):
            at = pl.ds(pl.multiple_of(step * QB_BACK, QB_BACK), QB_BACK)
            queries = heads[0, member, :, at]
            upstream = upstream_heads[0, member, :, at]
            inner = jnp.sum(upstream.astype(F32) * exact[member, :, at], axis=0, keepdims=True)
            softened = jnp.exp2(nn(keys[...], queries) - lse_ref[member, 0:1, at])
            logit_grad = (softened * (nn(values[...], upstream) - inner)).astype(BF16)
            value_acc[...] += nt(upstream, softened.astype(BF16))
            key_acc[...] += nt(queries, logit_grad)
            grads[0, member, :, at] = (nn(heads[1, member], logit_grad) * HD ** (-0.5)).astype(BF16)
            return carry

        steps = L // QB_BACK
        lax.fori_loop(0, steps, attend_back, 0)
        grads[1, member] = (key_acc[...] * LN2).astype(BF16)
        grads[2, member] = value_acc[...].astype(BF16)
        for copy in backward[member][0] + [backward[member][1]]:
            copy.start()
        if member == 0:
            near_sums(0)
            core_sums(1)
            core_sums(2)
    loads["up"].wait()
    loads["mmid"].wait()
    loads["proj"].wait()
    loads["fdown"].wait()
    mixer_hat, mixer_inverse = norm_parts(mmid[...])
    mixer_normed = (mixer_hat * mgain_ref[...]).astype(BF16).T
    loads["att"].wait()
    loads["ow"].wait()
    mixer_gains, first_gains = [], []

    def rows_back(member):
        copies, here = backward[member]
        for copy in copies:
            copy.wait_recv()
        here.wait()
        rows = slice(member * ROWS, (member + 1) * ROWS)
        normed_grad = nn(proj[...], back[:, :, :, rows].reshape(3 * D, ROWS)).T
        residual, gain_rows = norm_pull(mixer_hat[rows], mixer_inverse[rows], mgain_ref[...], normed_grad)
        mixer_gains.append(jnp.sum(gain_rows, axis=0, keepdims=True))
        upstream = ups[rows] + residual
        grad = upstream.astype(BF16)
        grad_low[rows] = grad
        normed_grad = jnp.zeros((ROWS, D), F32)
        for part in range(2):
            cut = slice(part * FF // 2, (part + 1) * FF // 2)
            act, slope = gelu_parts(hidden[rows, cut])
            active[rows, cut] = act.astype(BF16)
            hidden_grad = (slope * nt(grad, fdown[cut])).astype(BF16)
            hidden_low[rows, cut] = hidden_grad
            normed_grad = normed_grad + nt(hidden_grad, fup[:, cut])
        residual, gain_rows = norm_pull(first_hat[rows], first_inverse[rows], fgain_ref[...], normed_grad)
        first_gains.append(jnp.sum(gain_rows, axis=0, keepdims=True))
        upstream = upstream + residual
        lup[rows] = upstream
        attended_grad = nt(upstream.astype(BF16), ow[...]).astype(BF16)
        agrad[member] = attended_grad
        inner = jnp.sum(attended_grad.astype(F32) * att[member], axis=1, keepdims=True)
        fig_ref[member] = jnp.concatenate(
            [clse_ref[member, 0:1], to_rows(inner, inner)[0:1], jnp.zeros((6, ROWS), F32)], axis=0
        )

    rows_back(0)
    first_sums(0)
    near_sums(1)
    near_sums(2)
    rows_back(1)
    hold(0)
    first_sums(1)
    first_sums(2)
    store(lup, lup_ref)
    store(agrad, agrad_ref)
    dmgain_ref[...] = mixer_gains[0] + mixer_gains[1]
    dfgain_ref[...] = first_gains[0] + first_gains[1]
    grad = grad_low[...]
    ddown[...] = tn(active[...], grad).astype(BF16)
    store(ddown, ddown_ref)
    dup[...] = tn(first_normed, hidden_low[...]).astype(BF16)
    store(dup, dup_ref)
    dproj[...] = nt(mixer_normed, back[...].reshape(3 * D, MB * ROWS)).astype(BF16)
    store(dproj, dproj_ref)
    dout[...] = tn(att[...].reshape(MB * ROWS, D).astype(BF16), lup[...].astype(BF16)).astype(BF16)
    store(dout, dout_ref)
    hold(1)
    hold(2)
    finish()
    for copy in stores:
        copy.wait()
    for copies, here in outward + backward:
        for copy in copies:
            copy.wait_send()


def latents_backward(collective_id, arrays, *args):
    dma = pltpu.SemaphoreType.DMA
    vmem = pl.BlockSpec(memory_space=pltpu.VMEM)
    hbm = pl.BlockSpec(memory_space=pl.ANY)
    rows = MB * ROWS
    sources, items, kinds, shapes = reduce_plan(arrays)
    reduced = [jax.ShapeDtypeStruct((rows_ // 2, columns), kind) for (rows_, columns), kind in zip(shapes, kinds)]
    stored = [
        ((MB, ROWS, D), BF16), ((MB, 8, ROWS), F32), ((rows, D), F32), ((D, FF), BF16), ((FF, D), BF16),
        ((D, 3 * D), BF16), ((D, D), BF16), ((1, D), F32), ((1, D), F32),
    ]
    return pl.pallas_call(
        functools.partial(latents_backward_kernel, items),
        in_specs=[hbm, hbm, hbm, vmem, hbm, hbm, hbm, hbm, vmem, hbm, vmem, hbm, hbm, vmem, hbm] + [hbm] * len(arrays),
        out_specs=[hbm, vmem] + [hbm] * 5 + [vmem] * (2 + len(arrays)),
        out_shape=[jax.ShapeDtypeStruct(shape, kind) for shape, kind in stored] + reduced,
        scratch_shapes=[
            pltpu.VMEM((3, MB, HD, L), BF16), pltpu.VMEM((MB, HD, L), F32), pltpu.VMEM((rows, D), F32),
            pltpu.VMEM((rows, D), F32), pltpu.VMEM((rows, D), F32), pltpu.VMEM((MB, ROWS, D), F32),
            pltpu.VMEM((D, D), BF16), pltpu.VMEM((D, FF), BF16), pltpu.VMEM((FF, D), BF16),
            pltpu.VMEM((D, 3 * D), BF16), pltpu.VMEM((L, HD), BF16), pltpu.VMEM((L, HD), BF16),
            pltpu.VMEM((1, MB, HD, L), BF16), pltpu.VMEM((HD, L), F32), pltpu.VMEM((HD, L), F32),
            pltpu.VMEM((3, MB, HD, L), BF16), pltpu.VMEM((3, H, HD, rows), BF16),
            pltpu.VMEM((MB, ROWS, D), BF16), pltpu.VMEM((rows, D), F32), pltpu.VMEM((D, FF), BF16),
            pltpu.VMEM((FF, D), BF16), pltpu.VMEM((D, 3 * D), BF16), pltpu.VMEM((D, D), BF16),
            pltpu.VMEM((rows, FF), F32), pltpu.VMEM((rows, FF), BF16), pltpu.VMEM((rows, FF), BF16),
            pltpu.VMEM((rows, D), BF16),
            dma((10,)), dma((6,)), dma((7, MB)), dma((7, MB)), dma((MB,)), dma((7, MB)), dma((7, MB)), dma((MB,)),
        ] + tok_scratch(items, kinds),
        compiler_params=pltpu.CompilerParams(
            collective_id=collective_id, has_side_effects=True, vmem_limit_bytes=61 * MIB
        ),
        cost_estimate=pl.CostEstimate(
            flops=35 * 10**9, bytes_accessed=36 * 10**6, transcendentals=10 * 10**6
        ),
        name="latents_backward",
    )(*args, *sources)


def fast_body(
    tokens,
    latents,
    segments,
    scene_mask,
    counts,
    token_gain,
    query_gain,
    query_weight,
    key_weight,
    value_weight,
    output_weight,
    first_gain,
    first_up,
    first_down,
    mixer_gain,
    mixer_project,
    mixer_output,
    second_gain,
    second_up,
    second_down,
    cotangent,
):
    scenes = (segments, scene_mask, counts.reshape(MB))
    keys, values, queries, attended, lse = cross_forward(
        0, tokens, latents, token_gain[None], query_gain[None], query_weight, key_weight, value_weight, *scenes
    )
    (latents_out, first_mid, mixer_mid, packed, exact, head_lse, upstream, mixed_grad, d_second_down, d_second_up,
     d_mixer_output, d_second_gain) = latents_forward(
        1, latents, attended, cotangent, output_weight, first_gain[None], first_up, first_down, mixer_gain[None],
        mixer_project, mixer_output, second_gain[None], second_up, second_down,
    )
    (attended_grad, figures, upstream, d_first_up, d_first_down, d_project, d_output, d_mixer_gain, d_first_gain,
     *early) = latents_backward(
        2, [d_second_up, d_second_down, d_mixer_output], mixed_grad, packed, exact, head_lse, upstream, mixer_mid,
        first_mid, attended, lse, output_weight, first_gain[None], first_up, first_down, mixer_gain[None], mixer_project,
    )
    latents_grad, tokens_grad, d_key, d_value, d_query, gains, *rest = cross_backward(
        5, early, [d_first_up, d_first_down, d_project], tokens, token_gain[None], key_weight, value_weight,
        *scenes, keys, values, queries, attended_grad, figures, latents, upstream, query_gain[None], query_weight,
        d_first_gain, d_mixer_gain, d_second_gain,
    )
    early, held, quads = rest[:len(early)], rest[len(early):len(early) + 1], rest[len(early) + 1:]
    o_output, o_key, o_value, o_query, gains, *late = reduce_grads(
        7, [d_output, d_key, d_value, d_query, gains], held, quads, (False, True), early
    )
    late, early = late[:3], late[3:]
    (latents_out, latents_grad, tokens_grad, o_second_up, o_second_down, o_mixer_output, o_first_up, o_first_down,
     o_project, o_output, o_key, o_value, o_query, *o_gains) = write_results(
        [latents_out, latents_grad.reshape(latents_out.shape), tokens_grad, *early, *late, o_output, o_key, o_value, o_query], gains, 5
    )
    o_gains = [gain.reshape(D // TOK) for gain in o_gains]
    return (
        latents_out,
        latents_grad,
        tokens_grad,
        o_gains[0],
        o_gains[1],
        o_query,
        o_key,
        o_value,
        o_output,
        o_gains[2],
        o_first_up,
        o_first_down,
        o_gains[3],
        o_project,
        o_mixer_output,
        o_gains[4],
        o_second_up,
        o_second_down,
    )


IN_SPECS = (
    P("grp", None, "tok", None),
    P("grp", None, None, None),
    P("grp", None, "tok"),
    P("grp", None, None, None),
    P("grp", None, "tok"),
    P(),
    P(),
    P(),
    P(),
    P(),
    P(),
    P(),
    P(),
    P(),
    P(),
    P(),
    P(),
    P(),
    P(),
    P(),
    P("grp", None, "tok", None),
)
OUT_SPECS = (
    P("grp", None, "tok", None),
    P("grp", None, "tok", None),
    P("grp", None, "tok", None),
    P("tok"),
    P("tok"),
    P("tok", None),
    P("tok", None),
    P("tok", None),
    P("tok", None),
    P("tok"),
    P("tok", None),
    P("tok", None),
    P("tok"),
    P("tok", None),
    P("tok", None),
    P("tok"),
    P("tok", None),
    P("tok", None),
)


def solution(mesh):
    return jax.shard_map(
        fast_body if mesh.shape["tok"] == TOK else general_body,
        mesh=mesh,
        in_specs=IN_SPECS,
        out_specs=OUT_SPECS,
        check_vma=False,
    )
```
